32 devices in a mesh: chan: 4 (over z), space: 8 (over y, x, core).
Axes of the slice: x: 2, y: 2, z: 4, core: 2. Of those that a mesh axis runs over, the one named last changes fastest.
Arguments:
- blocks: bfloat16 [512, 8192], P('space', 'chan'), may hold values from -10 to 10
- weight_one: bfloat16 [9, 512, 512], P(None, 'chan'), may hold values from -0.09375 to 0.09375
- weight_two: bfloat16 [9, 512, 512], P(None, 'chan'), may hold values from -0.09375 to 0.09375
- gain_one: float32 [512], P('chan'), may hold values from 0.5 to 1.5
- shift_one: float32 [512], P('chan'), may hold values from -3 to 3
- gain_two: float32 [512], P('chan'), may hold values from 0.5 to 1.5
- shift_two: float32 [512], P('chan'), may hold values from -3 to 3
- cell_live: int32 [512, 16], P('space'), may hold values from 0 to 1, as said below
- cotangent: bfloat16 [512, 8192], P('space', 'chan'), may hold values from -6 to 6
Outputs:
- block_out: bfloat16 [512, 8192], P('space', 'chan')
- input_grad: float32 [512, 8192], P('space', 'chan')
- weight_one_grad: float32 [9, 512, 512], P(None, 'chan')
- weight_two_grad: float32 [9, 512, 512], P(None, 'chan')
- gain_one_grad: float32 [512], P('chan')
- shift_one_grad: float32 [512], P('chan')
- gain_two_grad: float32 [512], P('chan')
- shift_two_grad: float32 [512], P('chan')
The draws below stay inside these ranges and needn't reach their ends.
Inputs may be any that keep to these rules, and one draw needn't show every extreme that they name: `cell_live`: 1 marks a pixel of an image, 0 an empty cell; images are 7 x 7 or 3 x 3 crops (cut at the strip's two ends), and any two images are parted by empty rows and columns.
All inputs are finite; a program needn't handle non-finite values.
Results may differ from the reference program's by a relative error of at most 0.0059.
Values may be sent and summed in bfloat16 or wider, within the bound.
A program may use at most 128 MiB of HBM per device.

```python
from functools import partial
import jax
import jax.numpy as jnp
from jax import lax

C = 512
WID = 16
ROWS_DEV = 64
ROWS = 512


def draw_blocks(key, part):
    key = jax.random.fold_in(key, 11)
    first_key = jax.random.fold_in(key, 0)
    positions = jnp.arange(ROWS, dtype=jnp.float32)
    rising = jnp.exp(jnp.log(0.6) + jnp.log(3.0) * positions / ROWS)[:, None]
    values = jax.random.normal(first_key, (ROWS, C * WID), jnp.float32)
    return jnp.clip(values * rising, -10.0, 10.0).astype(jnp.bfloat16)


def draw_cell_live(key, part):
    key = jax.random.fold_in(key, 23)
    slots = ROWS // 8 + 1
    picked = jax.random.randint(key, (slots,), 0, 100)
    number = jnp.arange(slots)
    empty_cut = 65 * (ROWS - 8 * number) // ROWS
    kinds = jnp.where(picked < empty_cut, 0, jnp.where(picked < empty_cut + (100 - empty_cut) // 2, 1, 2))
    kinds = jnp.where(number % (ROWS_DEV // 8) == 0, 2, kinds)
    positions = jnp.arange(ROWS)
    owner = (positions + 4) // 8
    within = (positions + 4) % 8
    columns = jnp.arange(WID)
    large_cell = (within[:, None] < 7) & (columns[None, :] % 8 < 7)
    small_cell = (within[:, None] % 4 < 3) & (columns[None, :] % 4 < 3)
    chosen = kinds[owner][:, None]
    live = jnp.where(chosen == 2, large_cell, jnp.where(chosen == 1, small_cell, False))
    return live.astype(jnp.int32)


def block_scale(own_key, dims, shards, smallest, largest):
    factor_of = 1.0
    for axis_at, parts in shards:
        heights = jax.random.uniform(jax.random.fold_in(jax.random.fold_in(own_key, 6), axis_at), (parts,), jnp.float32, smallest / len(shards), largest / len(shards))
        factor_of = factor_of * jnp.repeat(jnp.exp(heights), dims[axis_at] // parts).reshape((-1,) + (1,) * (len(dims) - 1 - axis_at))
    return factor_of


def normal_values(rng, shape, scale, limit, cuts=(), kind=jnp.bfloat16):
    drawn = scale * jax.random.normal(rng, shape, jnp.float32)
    if cuts:
        drawn = drawn * block_scale(rng, shape, cuts, -0.22, 0.18)
    return jnp.clip(drawn, -limit, limit).astype(kind)


def setup_inputs(seed: int = 0) -> dict:
    keys = jax.random.split(jax.random.key(seed), 10)
    return {
        "blocks": draw_blocks(jax.random.fold_in(keys[9], 71), 0),
        "weight_one": normal_values(keys[1], (9, C, C), (9 * C) ** -0.5, 0.09375, ((1, 4),)),
        "weight_two": normal_values(keys[2], (9, C, C), (9 * C) ** -0.5, 0.09375, ((1, 4),)),
        "gain_one": jnp.clip(1.0 + 0.1 * jax.random.normal(keys[3], (C,), jnp.float32), 0.5, 1.5),
        "shift_one": normal_values(keys[4], (C,), 0.5, 3.0, ((0, 4),), jnp.float32),
        "gain_two": jnp.clip(1.0 + 0.1 * jax.random.normal(keys[5], (C,), jnp.float32), 0.5, 1.5),
        "shift_two": normal_values(keys[6], (C,), 0.5, 3.0, ((0, 4),), jnp.float32),
        "cell_live": draw_cell_live(jax.random.fold_in(keys[9], 71), 0),
        "cotangent": normal_values(keys[8], (ROWS, C * WID), 1.0, 6.0, ((0, 8), (1, 4))),
    }


EPSILON = 1e-05

@jax.custom_vjp
def low(v):
    return lax.optimization_barrier(v.astype(jnp.bfloat16)).astype(jnp.float32)

@jax.custom_vjp
def low_back(v):
    return v

def low_keep(v):
    return (low(v), None)

def low_pass(kept, grad):
    return (grad,)

def back_keep(v):
    return (v, None)

def back_low(kept, grad):
    return (low(grad),)
low.defvjp(low_keep, low_pass)
low_back.defvjp(back_keep, back_low)

def to_grid(flat):
    return flat.reshape(flat.shape[0], -1, WID).transpose(0, 2, 1)

def to_flat(grid):
    return grid.transpose(0, 2, 1).reshape(grid.shape[0], -1)

def convolve(field, weight):
    kernel = weight.reshape(3, 3, weight.shape[1], weight.shape[2])
    result = lax.conv_general_dilated(field[None], kernel, (1, 1), 'SAME', dimension_numbers=('NHWC', 'HWIO', 'NHWC'), precision=lax.Precision.HIGHEST)
    return result[0]

def normalize(value, living, count, gain, shift):
    mean = lax.optimization_barrier(jnp.sum(value * living, axis=(0, 1))) / count
    centred = value - mean
    variance = lax.optimization_barrier(jnp.sum(centred * centred * living, axis=(0, 1))) / count
    return centred * lax.rsqrt(variance + EPSILON) * gain + shift

def forward(blocks, weight_one, weight_two, gain_one, shift_one, gain_two, shift_two, living, count):
    masked = low(blocks * living)
    first = low_back(convolve(masked, weight_one))
    hidden = low(jax.nn.gelu(normalize(first, living, count, gain_one, shift_one), approximate=False) * living)
    second = low_back(convolve(hidden, weight_two))
    summed = normalize(second, living, count, gain_two, shift_two) + masked
    return jax.nn.gelu(summed, approximate=False) * living

def reference(blocks, weight_one, weight_two, gain_one, shift_one, gain_two, shift_two, cell_live, cotangent):
    living = cell_live.astype(jnp.float32)[:, :, None]
    count = jnp.sum(cell_live.astype(jnp.float32))
    field = to_grid(blocks).astype(jnp.float32)
    upstream = to_grid(cotangent).astype(jnp.float32)
    output, pullback = jax.vjp(partial(forward, living=living, count=count), field, weight_one.astype(jnp.float32), weight_two.astype(jnp.float32), gain_one, shift_one, gain_two, shift_two)
    grads = pullback(upstream)
    return (to_flat(output.astype(jnp.bfloat16)), to_flat(grads[0]), grads[1], grads[2], grads[3], grads[4], grads[5], grads[6])
```

```python
import functools

import jax
import jax.numpy as jnp
from jax import lax
from jax.experimental import pallas as pl
from jax.experimental.pallas import tpu as pltpu
from jax.sharding import PartitionSpec as P

EPSILON = 1e-05
MESH = pl.DeviceIdType.MESH
F32 = jnp.float32
BF16 = jnp.bfloat16
ROOT_HALF = 0.7071067811865476
ROOT_TWO_PI = 0.3989422804014327
CHUNK = 128


def dot(a, b):
    return jnp.dot(a, b, preferred_element_type=F32)


def gelu_parts(v):
    upper = 0.5 * (1.0 + lax.erf(v * ROOT_HALF))
    slope = upper + v * (ROOT_TWO_PI * jnp.exp(-0.5 * v * v))
    return v * upper, slope


def block_kernel(n, s_count, rows, wide, ch, aligned, *refs):
    (x_in, cot_in, live_in, params, w1_hbm, w2_hbm) = refs[:6]
    (out_block, out_input, out_wg1, out_wg2, out_sums) = refs[6:11]
    (wv, wt, cat, x_t, rs_send, rs_recv, edge_send, edge_recv, cotm, mask, masked,
     normed1, normed2, through, slope1, hid, pad, acc, hold, gcat,
     part, psend, crecv, hsend, qrecv, wout, st_send, st_recv, row_send, row_recv,
     w_sem, rs_ssem, rs_rsem, e_ssem, e_rsem, ag_ssem, ag_rsem,
     st_ssem, st_rsem, row_ssem, row_rsem, c_ssem, c_rsem, q_ssem, q_rsem,
     f_ssem, f_rsem, h_ssem, h_rsem, o_sem) = refs[11:]

    z = lax.axis_index("chan")
    s = lax.axis_index("space")
    cells = rows * wide
    main = cells
    total = main + 2 * wide
    core, chip, chips = s % 2, s // 2, s_count // 2
    before, after = (s + s_count - 1) % s_count, (s + 1) % s_count
    half_rows = n * 9 * ch // 2
    piece = half_rows // chips

    barrier = pltpu.get_barrier_semaphore()

    @pl.loop(1, s_count)
    def _(k):
        pl.semaphore_signal(barrier, inc=1, device_id=(z, (s + k) % s_count), device_id_type=MESH)

    @pl.when(z > 0)
    def _():
        pl.semaphore_signal(barrier, inc=1, device_id=(z - 1, s), device_id_type=MESH)

    @pl.when(z < n - 1)
    def _():
        pl.semaphore_signal(barrier, inc=1, device_id=(z + 1, s), device_id_type=MESH)

    w_copies = []
    for which, source in enumerate((w1_hbm, w2_hbm)):
        if aligned:
            for d in range(n):
                w_copies.append(pltpu.make_async_copy(
                    source.at[:, :, d * ch:(d + 1) * ch], wv.at[which, d], w_sem.at[which, d]))
        else:
            for d in range(n):
                w_copies.append(pltpu.make_async_copy(
                    source.at[d], wv.at[which, d], w_sem.at[which, d]))
    for copy in w_copies:
        copy.start()

    def chunked(fn, init):
        def step(i, carry):
            return fn(pl.multiple_of(i * CHUNK, CHUNK), CHUNK, carry)
        return lax.fori_loop(0, main // CHUNK, step, init)

    def load_main(start, size, carry):
        at = pl.ds(start, size)
        lv = live_in[at, :].astype(F32)
        mask[at, :] = lv
        masked[at, :] = x_in[at, :].astype(F32) * lv
        cotm[at, :] = cot_in[at, :].astype(F32) * lv
        return carry

    chunked(load_main, 0)
    for side, start in ((0, 0), (1, cells - wide)):
        edge_send[side, 0] = masked[start:start + wide, :].astype(BF16)
        edge_send[side, 1] = cotm[start:start + wide, :].astype(BF16)
        edge_send[side, 2] = mask[start:start + wide, :].astype(BF16)
    acc[...] = jnp.zeros_like(acc)
    st_send[...] = jnp.zeros_like(st_send)

    neighbours = jnp.where(z > 0, 1, 0) + jnp.where(z < n - 1, 1, 0)
    pl.semaphore_wait(barrier, s_count - 1 + neighbours)

    def edge_copy(side):
        return pltpu.make_async_remote_copy(
            src_ref=edge_send.at[side], dst_ref=edge_recv.at[1 - side],
            send_sem=e_ssem.at[side], recv_sem=e_rsem.at[1 - side],
            device_id=(z, before if side == 0 else after), device_id_type=MESH)

    for side in range(2):
        edge_copy(side).start()

    def row_copy(slot, side):
        return pltpu.make_async_remote_copy(
            src_ref=row_send.at[slot, side], dst_ref=row_recv.at[slot, 1 - side],
            send_sem=row_ssem.at[slot, side], recv_sem=row_rsem.at[slot, 1 - side],
            device_id=(z, before if side == 0 else after), device_id_type=MESH)

    def send_rows(slot, ref):
        for side, start in ((0, 0), (1, cells - wide)):
            row_send[slot, side] = ref[start:start + wide, :]
            row_copy(slot, side).start()

    def take_rows(slot, ref):
        for side in range(2):
            row_copy(slot, 1 - side).wait_recv()
            ref[main + side * wide:main + (side + 1) * wide, :] = row_recv[slot, side]

    def st_copy(slot, k):
        return pltpu.make_async_remote_copy(
            src_ref=st_send.at[slot], dst_ref=st_recv.at[slot, s],
            send_sem=st_ssem.at[slot, k], recv_sem=st_rsem.at[slot, s],
            device_id=(z, (s + k) % s_count), device_id_type=MESH)

    def send_stats(slot, values):
        for i, v in enumerate(values):
            st_send[slot, i:i + 1, :] = v
        st_recv[slot, s] = st_send[slot]

        @pl.loop(1, s_count)
        def _(k):
            st_copy(slot, k).start()

    def take_stats(slot):
        @pl.loop(1, s_count)
        def _(k):
            peer = (s + k) % s_count
            pltpu.make_async_remote_copy(
                src_ref=st_send.at[slot], dst_ref=st_recv.at[slot, peer],
                send_sem=st_ssem.at[slot, k], recv_sem=st_rsem.at[slot, peer],
                device_id=(z, peer), device_id_type=MESH).wait_recv()

    def lay_out(value_of, target):
        pad[8:8 + wide, :] = value_of(main, wide)
        pad[8 + wide + cells:8 + 2 * wide + cells, :] = value_of(main + wide, wide)

        def fill(start, size, carry):
            pad[pl.ds(8 + wide + start, size), :] = value_of(start, size)
            return carry

        chunked(fill, 0)
        strip = CHUNK // wide
        column = lax.broadcasted_iota(jnp.int32, (CHUNK, ch), 0) % wide

        def shift(first, count):
            size = count * wide
            where = column[:size]
            here = pad[pl.ds(8 + first * wide, size), :]
            left = pad[pl.ds(7 + first * wide, size), :]
            right = pad[pl.ds(9 + first * wide, size), :]
            left = jnp.where(where == 0, 0.0, left)
            right = jnp.where(where == wide - 1, 0.0, right)
            for b, v in enumerate((left, here, right)):
                target[pl.ds(first, count), :, b * ch:(b + 1) * ch] = (
                    v.astype(BF16).reshape(count, wide, ch))

        @pl.loop(0, rows // strip)
        def _(i):
            shift(i * strip, strip)
        shift(rows, 2)

    def conv_rows(which, field, d, row, count):
        result = None
        for a in range(3):
            lhs = field[pl.ds(row + a, count), :, :].reshape(count * wide, 3 * ch)
            rhs = wv[which, d, 3 * a:3 * a + 3].reshape(3 * ch, ch)
            term = dot(lhs, rhs)
            result = term if result is None else result + term
        return result

    sub_rows = 16
    sub = sub_rows * wide
    halves = 2
    half = main // halves

    def rs_copy(ph, way, d, q, peer):
        at = pl.ds(q * half, half)
        return pltpu.make_async_remote_copy(
            src_ref=rs_send.at[ph, way, d, at, :], dst_ref=rs_recv.at[ph, way, d, at, :],
            send_sem=rs_ssem.at[ph, way, d, q], recv_sem=rs_rsem.at[ph, way, d, q],
            device_id=(z + peer, s), device_id_type=MESH)

    def way_of(j):
        way, k = j % 2, j // 2
        sign = 1 - 2 * way
        d = (1 - way) * (n - 1 - k) + way * k
        return way, sign, d

    def reduce_conv(ph, target, idle):
        field = cat.at[ph]

        @pl.loop(0, 2 * (n - 1))
        def _(j):
            way, sign, d = way_of(j)
            fed = (z - sign >= 0) & (z - sign < n)

            @pl.when((d - z) * sign > 0)
            def _():
                for q in range(halves):
                    @pl.when(fed)
                    def _():
                        rs_copy(ph, way, d, q, sign).wait_recv()

                    @pl.loop(0, half // sub)
                    def _(i):
                        row = q * (half // wide) + i * sub_rows
                        v = conv_rows(ph, field, d, row, sub_rows)
                        at = pl.ds(pl.multiple_of(row * wide, sub), sub)
                        got = rs_recv[ph, way, d, at, :].astype(F32)
                        v = v + jnp.where(fed, got, 0.0)
                        rs_send[ph, way, d, at, :] = v.astype(BF16)
                    rs_copy(ph, way, d, q, sign).start()

        @pl.loop(0, main // sub)
        def _(i):
            row = i * sub_rows
            at = pl.ds(pl.multiple_of(row * wide, sub), sub)
            target[at, :] = conv_rows(ph, field, z, row, sub_rows)
        idle()
        for way in range(2):
            @pl.when(z > 0 if way == 0 else z < n - 1)
            def _():
                for q in range(halves):
                    rs_copy(ph, way, z, q, 1 - 2 * way).wait_recv()

                    @pl.loop(0, half // sub)
                    def _(i):
                        at = pl.ds(pl.multiple_of(q * half + i * sub, sub), sub)
                        target[at, :] = target[at, :] + rs_recv[ph, way, z, at, :].astype(F32)

    def prepare(ph):
        for t in range(9):
            a, b = t // 3, t % 3

            @pl.loop(0, main // sub)
            def _(i):
                v = cat[ph, pl.ds(a + i * sub_rows, sub_rows), :, b * ch:(b + 1) * ch]
                x_t[ph, t * ch:(t + 1) * ch, pl.ds(pl.multiple_of(i * sub, sub), sub)] = (
                    v.reshape(sub, ch).T)

        @pl.loop(0, n)
        def _(d):
            for t in range(9):
                a, b = 2 - t // 3, 2 - t % 3
                wt[ph, d, a, b * ch:(b + 1) * ch, :] = wv[ph, d, t].T

    def local_moments(ref):
        def sums(start, size, carry):
            at = pl.ds(start, size)
            m = mask[at, :]
            return (carry[0] + jnp.sum(ref[at, :] * m, axis=0, keepdims=True),
                    carry[1] + jnp.sum(m, axis=0, keepdims=True))
        zero = jnp.zeros((1, ch), F32)
        added, number = chunked(sums, (zero, zero))
        middle = added / jnp.maximum(number, 1.0)

        def spread(start, size, carry):
            at = pl.ds(start, size)
            c = (ref[at, :] - middle) * mask[at, :]
            return carry + jnp.sum(c * c, axis=0, keepdims=True)
        return added, number, chunked(spread, zero)

    def moments(slot):
        take_stats(slot)
        got = [st_recv[slot, k] for k in range(s_count)]
        added = sum(g[0:1] for g in got)
        number = sum(g[1:2] for g in got)
        mean = added / number
        spread = 0.0
        for g in got:
            off = g[0:1] / jnp.maximum(g[1:2], 1.0) - mean
            spread = spread + (g[2:3] + g[1:2] * off * off)
        return mean, lax.rsqrt(spread / number + EPSILON), number

    def everywhere(fn, carry):
        chunked(fn, 0)
        fn(main, 2 * wide, 0)
        return carry

    gain1, shift1, gain2, shift2 = (params[i:i + 1, :] for i in range(4))

    for side in range(2):
        edge_copy(1 - side).wait_recv()
        inside = jnp.where(s > 0, 1.0, 0.0) if side == 0 else jnp.where(s < s_count - 1, 1.0, 0.0)
        at = slice(main + side * wide, main + (side + 1) * wide)
        masked[at, :] = edge_recv[side, 0].astype(F32) * inside
        cotm[at, :] = edge_recv[side, 1].astype(F32) * inside
        mask[at, :] = edge_recv[side, 2].astype(F32) * inside
    lay_out(lambda start, size: masked[pl.ds(start, size), :], cat.at[0])
    for copy in w_copies:
        copy.wait()

    reduce_conv(0, normed1, lambda: prepare(0))
    send_rows(0, normed1)
    send_stats(0, local_moments(normed1))
    mean1, scale1, count = moments(0)
    take_rows(0, normed1)

    def activate_one(start, size, carry):
        at = pl.ds(start, size)
        nv = (normed1[at, :] - mean1) * scale1
        normed1[at, :] = nv
        value, slope = gelu_parts(nv * gain1 + shift1)
        m = mask[at, :]
        hid[at, :] = value * m
        slope1[at, :] = slope * m
        return carry

    everywhere(activate_one, 0)
    lay_out(lambda start, size: hid[pl.ds(start, size), :], cat.at[1])

    reduce_conv(1, normed2, lambda: prepare(1))
    send_rows(1, normed2)
    send_stats(1, local_moments(normed2))
    mean2, scale2, _ = moments(1)
    take_rows(1, normed2)

    def activate_two(start, size, carry):
        at = pl.ds(start, size)
        nv = (normed2[at, :] - mean2) * scale2
        normed2[at, :] = nv
        value, slope = gelu_parts(nv * gain2 + shift2 + masked[at, :])
        t = cotm[at, :] * slope
        through[at, :] = t
        return value, nv, t

    def activate_main(start, size, carry):
        value, nv, t = activate_two(start, size, carry)
        at = pl.ds(start, size)
        out_block[at, :] = (value * mask[at, :]).astype(BF16)
        return (carry[0] + jnp.sum(t * nv, axis=0, keepdims=True),
                carry[1] + jnp.sum(t, axis=0, keepdims=True))

    zero = jnp.zeros((1, ch), F32)
    send_stats(2, chunked(activate_main, (zero, zero)))
    activate_two(main, 2 * wide, 0)

    def gradient_sums(slot):
        take_stats(slot)
        got = [st_recv[slot, k] for k in range(s_count)]
        return sum(g[0:1] for g in got), sum(g[1:2] for g in got)

    def norm_back(ph, upstream, normed, gain, scale, sums):
        gain_grad, shift_grad = sums
        factor = gain * scale
        level, tilt = shift_grad / count, gain_grad / count

        def step(start, size, carry):
            at = pl.ds(start, size)
            v = upstream[at, :] - mask[at, :] * (level + normed[at, :] * tilt)
            hold[ph, z, at, :] = (factor * v).astype(BF16)
            return carry
        everywhere(step, 0)

    ag_rows = ((0, total // 32 * 16), (total // 32 * 16, total - total // 32 * 16))

    def ag_copy(ph, block, q, sign):
        at = pl.ds(*ag_rows[q])
        return pltpu.make_async_remote_copy(
            src_ref=hold.at[ph, block, at, :], dst_ref=hold.at[ph, block, at, :],
            send_sem=ag_ssem.at[ph, (1 - sign) // 2, block, q], recv_sem=ag_rsem.at[ph, block, q],
            device_id=(z + sign, s), device_id_type=MESH)

    def ag_sends(ph, block, q, sign):
        @pl.when((z + sign >= 0) & (z + sign < n))
        def _():
            ag_copy(ph, block, q, sign).start()

    def process(ph, block):
        lay_out(lambda start, size: hold[ph, block, pl.ds(start, size), :].astype(F32), gcat)

        @pl.loop(0, main // sub)
        def _(i):
            row = i * sub_rows
            result = None
            for a in range(3):
                lhs = gcat[pl.ds(row + a, sub_rows), :, :].reshape(sub, 3 * ch)
                term = dot(lhs, wt[ph, block, a])
                result = term if result is None else result + term
            at = pl.ds(pl.multiple_of(row * wide, sub), sub)
            acc[at, :] = acc[at, :] + result

        @pl.loop(0, 9)
        def _(t):
            at = pl.ds(pl.multiple_of(t * ch, ch), ch)
            grad = dot(x_t[ph, at, :], hold[ph, block, 0:main, :])
            part[ph, pl.ds(pl.multiple_of((block * 9 + t) * ch, ch), ch), :] = grad

    def gather_back(ph):
        for q in range(2):
            for sign in (1, -1):
                ag_sends(ph, z, q, sign)
        process(ph, z)

        @pl.loop(1, n)
        def _(k):
            for q in range(2):
                for sign in (1, -1):
                    block = z - k * sign
                    @pl.when((block >= 0) & (block < n))
                    def _():
                        ag_copy(ph, block, q, sign).wait_recv()
                        ag_sends(ph, block, q, sign)

            @pl.loop(0, 2)
            def _(way):
                block = z - k * (1 - 2 * way)
                @pl.when((block >= 0) & (block < n))
                def _():
                    process(ph, block)

    def c_copy(ph):
        return pltpu.make_async_remote_copy(
            src_ref=psend.at[ph], dst_ref=crecv.at[ph], send_sem=c_ssem.at[ph], recv_sem=c_rsem.at[ph],
            device_id=(z, chip * 2 + 1 - core), device_id_type=MESH)

    def q_copy(ph, e, other):
        return pltpu.make_async_remote_copy(
            src_ref=hsend.at[ph, (chip + e) % chips], dst_ref=qrecv.at[ph, other],
            send_sem=q_ssem.at[ph, e], recv_sem=q_rsem.at[ph, other],
            device_id=(z, ((chip + e) % chips) * 2 + core), device_id_type=MESH)

    def f_copy(ph, e, other):
        at = pl.ds(core * half_rows + other * piece, piece)
        return pltpu.make_async_remote_copy(
            src_ref=wout.at[ph, at, :], dst_ref=wout.at[ph, at, :],
            send_sem=f_ssem.at[ph, e], recv_sem=f_rsem.at[ph, other],
            device_id=(z, ((chip + e) % chips) * 2 + core), device_id_type=MESH)

    def h_copy(ph, whose):
        at = pl.ds(whose * half_rows, half_rows)
        return pltpu.make_async_remote_copy(
            src_ref=wout.at[ph, at, :], dst_ref=wout.at[ph, at, :],
            send_sem=h_ssem.at[ph], recv_sem=h_rsem.at[ph],
            device_id=(z, chip * 2 + 1 - core), device_id_type=MESH)

    step_rows = 16 * 9

    def wide_loop(length, fn):
        @pl.loop(0, length // step_rows)
        def _(i):
            fn(pl.multiple_of(i * step_rows, step_rows))

    def sum_cores(ph):
        def convert(at):
            psend[ph, pl.ds(at, step_rows), :] = (
                part[ph, pl.ds((1 - core) * half_rows + at, step_rows), :].astype(BF16))
        wide_loop(half_rows, convert)
        c_copy(ph).start()

    def sum_chips(ph):
        c_copy(ph).wait_recv()

        def add(at):
            mine = pl.ds(core * half_rows + at, step_rows)
            v = part[ph, mine, :] + crecv[ph, pl.ds(at, step_rows), :].astype(F32)
            part[ph, mine, :] = v
            hsend[ph, at // piece, pl.ds(at % piece, step_rows), :] = v.astype(BF16)
        wide_loop(half_rows, add)

        @pl.loop(1, chips)
        def _(e):
            q_copy(ph, e, chip).start()

    def spread_chips(ph):
        @pl.loop(1, chips)
        def _(e):
            q_copy(ph, e, (chip + e) % chips).wait_recv()

        def add(at):
            mine = pl.ds(core * half_rows + chip * piece + at, step_rows)

            def one(e, v):
                return v + qrecv[ph, (chip + e) % chips, pl.ds(at, step_rows), :].astype(F32)
            wout[ph, mine, :] = lax.fori_loop(1, chips, one, part[ph, mine, :]).astype(BF16)
        wide_loop(piece, add)

        @pl.loop(1, chips)
        def _(e):
            f_copy(ph, e, chip).start()

    def spread_cores(ph):
        @pl.loop(1, chips)
        def _(e):
            f_copy(ph, e, (chip + e) % chips).wait_recv()
        h_copy(ph, core).start()

    def finish(ph, target):
        h_copy(ph, 1 - core).wait_recv()
        copies = []
        for d in range(n):
            source = wout.at[ph, d * 9 * ch:(d + 1) * 9 * ch, :]
            dest = target.at[:, d * ch:(d + 1) * ch] if aligned else target.at[d]
            copies.append(pltpu.make_async_copy(source, dest, o_sem.at[ph, d]))
        for copy in copies:
            copy.start()
        return copies

    sums2 = gradient_sums(2)
    norm_back(1, through, normed2, gain2, scale2, sums2)
    gather_back(1)
    sum_cores(1)

    send_rows(2, acc)

    def inner_main(start, size, carry):
        at = pl.ds(start, size)
        v = acc[at, :] * slope1[at, :]
        slope1[at, :] = v
        acc[at, :] = jnp.zeros((size, ch), F32)
        return (carry[0] + jnp.sum(v * normed1[at, :], axis=0, keepdims=True),
                carry[1] + jnp.sum(v, axis=0, keepdims=True))

    send_stats(3, chunked(inner_main, (zero, zero)))
    for side in range(2):
        row_copy(2, 1 - side).wait_recv()
        at = slice(main + side * wide, main + (side + 1) * wide)
        slope1[at, :] = row_recv[2, side] * slope1[at, :]
    sum_chips(1)
    sums1 = gradient_sums(3)
    norm_back(0, slope1, normed1, gain1, scale1, sums1)
    spread_chips(1)
    gather_back(0)
    sum_cores(0)
    spread_cores(1)

    def finish_input(start, size, carry):
        at = pl.ds(start, size)
        out_input[at, :] = (acc[at, :] + through[at, :]) * mask[at, :]
        return carry

    chunked(finish_input, 0)
    out_sums[0:1, :], out_sums[1:2, :] = sums1
    out_sums[2:3, :], out_sums[3:4, :] = sums2
    out_sums[4:8, :] = jnp.zeros((4, ch), F32)
    sum_chips(0)
    spread_chips(0)
    outs = finish(1, out_wg2)
    spread_cores(0)
    outs += finish(0, out_wg1)

    for side in range(2):
        edge_copy(side).wait_send()
        for slot in range(3):
            row_copy(slot, side).wait_send()
    for slot in range(4):
        @pl.loop(1, s_count)
        def _(k):
            st_copy(slot, k).wait_send()
    for ph in range(2):
        @pl.loop(0, 2 * (n - 1))
        def _(j):
            way, sign, d = way_of(j)

            @pl.when((d - z) * sign > 0)
            def _():
                for q in range(halves):
                    rs_copy(ph, way, d, q, sign).wait_send()

        @pl.loop(0, n)
        def _(k):
            for sign in (1, -1):
                block = z - k * sign

                @pl.when((block >= 0) & (block < n) & (z + sign >= 0) & (z + sign < n))
                def _():
                    for q in range(2):
                        ag_copy(ph, block, q, sign).wait_send()
        c_copy(ph).wait_send()

        @pl.loop(1, chips)
        def _(e):
            q_copy(ph, e, chip).wait_send()
            f_copy(ph, e, chip).wait_send()
        h_copy(ph, core).wait_send()
    for copy in outs:
        copy.wait()


def per_device(n, s_count, blocks, weight_one, weight_two, gain_one, shift_one, gain_two, shift_two, cell_live, cotangent):
    rows, wide = cell_live.shape
    ch = blocks.shape[1] // wide
    cells = rows * wide
    main = cells
    total = main + 2 * wide
    aligned = ch % 128 == 0
    chips = s_count // 2
    half_rows = n * 9 * ch // 2
    piece = half_rows // chips

    def cells_first(flat):
        return flat.reshape(rows, ch, wide).transpose(0, 2, 1).reshape(cells, ch)

    live = jnp.broadcast_to(cell_live.astype(BF16)[:, :, None], (rows, wide, ch)).reshape(cells, ch)
    params = jnp.stack([gain_one, shift_one, gain_two, shift_two] + [jnp.zeros_like(gain_one)] * 4)
    if not aligned:
        weight_one, weight_two = (
            w.reshape(9, ch, n, ch).transpose(2, 0, 1, 3) for w in (weight_one, weight_two))
    grad_shape = (9 * ch, n * ch) if aligned else (n, 9 * ch, ch)
    vmem = pl.BlockSpec(memory_space=pltpu.VMEM)
    hbm = pl.BlockSpec(memory_space=pl.ANY)
    sem = pltpu.SemaphoreType.DMA
    scratch = [
        pltpu.VMEM((2, n, 9, ch, ch), BF16),
        pltpu.VMEM((2, n, 3, 3 * ch, ch), BF16),
        pltpu.VMEM((2, rows + 2, wide, 3 * ch), BF16),
        pltpu.VMEM((2, 9 * ch, main), BF16),
        pltpu.VMEM((2, 2, n, main, ch), BF16),
        pltpu.VMEM((2, 2, n, main, ch), BF16),
        pltpu.VMEM((2, 3, wide, ch), BF16),
        pltpu.VMEM((2, 3, wide, ch), BF16),
        pltpu.VMEM((total, ch), F32),
        pltpu.VMEM((total, ch), F32),
        pltpu.VMEM((total, ch), F32),
        pltpu.VMEM((total, ch), F32),
        pltpu.VMEM((total, ch), F32),
        pltpu.VMEM((total, ch), F32),
        pltpu.VMEM((total, ch), F32),
        pltpu.VMEM((total, ch), F32),
        pltpu.VMEM((cells + 2 * wide + 16, ch), F32),
        pltpu.VMEM((cells, ch), F32),
        pltpu.VMEM((2, n, total, ch), BF16),
        pltpu.VMEM((rows + 2, wide, 3 * ch), BF16),
        pltpu.VMEM((2, 2 * half_rows, ch), F32),
        pltpu.VMEM((2, half_rows, ch), BF16),
        pltpu.VMEM((2, half_rows, ch), BF16),
        pltpu.VMEM((2, chips, piece, ch), BF16),
        pltpu.VMEM((2, chips, piece, ch), BF16),
        pltpu.VMEM((2, 2 * half_rows, ch), BF16),
        pltpu.VMEM((4, 8, ch), F32),
        pltpu.VMEM((4, s_count, 8, ch), F32),
        pltpu.VMEM((3, 2, wide, ch), F32),
        pltpu.VMEM((3, 2, wide, ch), F32),
        sem((2, n)),
        sem((2, 2, n, 2)), sem((2, 2, n, 2)),
        sem((2,)), sem((2,)),
        sem((2, 2, n, 2)), sem((2, n, 2)),
        sem((4, s_count)), sem((4, s_count)),
        sem((3, 2)), sem((3, 2)),
        sem((2,)), sem((2,)),
        sem((2, chips)), sem((2, chips)),
        sem((2, chips)), sem((2, chips)),
        sem((2,)), sem((2,)),
        sem((2, n)),
    ]
    block_out, input_grad, wg1, wg2, sums = pl.pallas_call(
        functools.partial(block_kernel, n, s_count, rows, wide, ch, aligned),
        out_shape=(
            jax.ShapeDtypeStruct((cells, ch), BF16),
            jax.ShapeDtypeStruct((cells, ch), F32),
            jax.ShapeDtypeStruct(grad_shape, BF16),
            jax.ShapeDtypeStruct(grad_shape, BF16),
            jax.ShapeDtypeStruct((8, ch), F32),
        ),
        in_specs=[vmem] * 4 + [hbm] * 2,
        out_specs=(vmem, vmem, hbm, hbm, vmem),
        scratch_shapes=scratch,
        compiler_params=pltpu.CompilerParams(
            collective_id=0, has_side_effects=True, vmem_limit_bytes=60 * 1024 * 1024),
    )(cells_first(blocks), cells_first(cotangent), live, params, weight_one, weight_two)

    def flat(grid):
        return grid.reshape(rows, wide, ch).transpose(0, 2, 1).reshape(rows, wide * ch)

    def whole(grad):
        if not aligned:
            grad = grad.transpose(1, 0, 2)
        return grad.astype(F32).reshape(9, ch, n * ch)

    return (flat(block_out), flat(input_grad), whole(wg1), whole(wg2), sums[0], sums[1], sums[2], sums[3])


def solution(mesh):
    return jax.shard_map(
        functools.partial(per_device, mesh.shape["chan"], mesh.shape["space"]),
        mesh=mesh,
        in_specs=(
            P("space", "chan"),
            P(None, "chan", None),
            P(None, "chan", None),
            P("chan"),
            P("chan"),
            P("chan"),
            P("chan"),
            P("space", None),
            P("space", "chan"),
        ),
        out_specs=(
            P("space", "chan"),
            P("space", "chan"),
            P(None, "chan", None),
            P(None, "chan", None),
            P("chan"),
            P("chan"),
            P("chan"),
            P("chan"),
        ),
        check_vma=False,
    )
```

```python
import functools
import math

import jax
import jax.numpy as jnp
from jax import lax
from jax.experimental import pallas as pl
from jax.experimental.pallas import tpu as pltpu
from jax.sharding import PartitionSpec as P

EPSILON = 1e-05
MESH = pl.DeviceIdType.MESH
F32 = jnp.float32
BF16 = jnp.bfloat16
ROOT_HALF = 0.7071067811865476
ROOT_TWO_PI = 0.3989422804014327
CHUNK = 128
HALVES = 2
LARGE, SMALL = 7, 3


def dot(a, b):
    return jnp.dot(a, b, preferred_element_type=F32)


def gelu_parts(v):
    upper = 0.5 * (1.0 + lax.erf(v * ROOT_HALF))
    slope = upper + v * (ROOT_TWO_PI * jnp.exp(-0.5 * v * v))
    return v * upper, slope


def most_live(rows, wide):
    units = (wide + 1) // (SMALL + 1)
    live_rows = rows - rows // (LARGE + 1)
    return min(rows * wide, math.ceil(units * live_rows * LARGE / 2))


def block_kernel(n, s_count, rows, wide, ch, aligned, packed, *refs):
    (x_in, cot_in, live_in, gain1_in, shift1_in, gain2_in, shift2_in, w1_hbm, w2_hbm) = refs[:9]
    (out_block, out_input, out_wg1, out_wg2, out_sums) = refs[9:14]
    (wv, wf, wt, cat, x_t, pack, unpack, edge_send, edge_recv, cotm, mask, masked,
     normed1, normed2, through, slope1, hid, pad, acc, hold, gcat,
     part, psend, crecv, hsend, qrecv, wout, st_send, st_recv, row_send, row_recv,
     w_sem, wz_ssem, wz_rsem, wp_ssem, wp_rsem, e_ssem, e_rsem, ag_ssem, ag_rsem,
     st_ssem, st_rsem, row_ssem, row_rsem, c_ssem, c_rsem, q_ssem, q_rsem,
     f_ssem, f_rsem, h_ssem, h_rsem, o_sem) = refs[14:]

    z = lax.axis_index("chan")
    s = lax.axis_index("space")
    cells = rows * wide
    total = cells + 2 * wide
    band = cells // HALVES
    core, chip, chips = s % 2, s // 2, s_count // 2
    before, after = (s + s_count - 1) % s_count, (s + 1) % s_count
    tap_rows = 9 * ch

    barrier = pltpu.get_barrier_semaphore()

    @pl.loop(1, s_count)
    def _(k):
        pl.semaphore_signal(barrier, inc=1, device_id=(z, (s + k) % s_count), device_id_type=MESH)

    @pl.loop(1, n)
    def _(k):
        pl.semaphore_signal(barrier, inc=1, device_id=((z + k) % n, s), device_id_type=MESH)

    w_copies = []
    for which, source in enumerate((w1_hbm, w2_hbm)):
        for d in range(n):
            block = source.at[:, d * ch:(d + 1) * ch] if aligned else source.at[d]
            w_copies.append(pltpu.make_async_copy(block, wv.at[which, d], w_sem.at[which, d]))
    for copy in w_copies:
        copy.start()

    def chunked(fn, init, first=0, count=cells):
        def step(i, carry):
            return fn(pl.multiple_of(first + i * CHUNK, CHUNK), CHUNK, carry)
        return lax.fori_loop(0, count // CHUNK, step, init)

    live = live_in[...].astype(BF16)
    ones = jnp.ones((wide, ch), BF16)

    def spread_mask(start, size, carry):
        cell = start + lax.broadcasted_iota(jnp.int32, (size, rows), 0)
        pick = (cell // wide == lax.broadcasted_iota(jnp.int32, (size, rows), 1)).astype(F32).astype(BF16)
        column = lax.broadcasted_iota(jnp.int32, (size, wide), 0) % wide
        value = jnp.where(column == lax.broadcasted_iota(jnp.int32, (size, wide), 1), dot(pick, live), 0.0)
        lv = dot(value.astype(BF16), ones)
        at = pl.ds(start, size)
        mask[at, :] = lv
        masked[at, :] = x_in[at, :].astype(F32) * lv
        cotm[at, :] = cot_in[at, :].astype(F32) * lv
        return carry

    chunked(spread_mask, 0)
    for side, start in ((0, 0), (1, cells - wide)):
        edge_send[side, 0] = masked[start:start + wide, :].astype(BF16)
        edge_send[side, 1] = cotm[start:start + wide, :].astype(BF16)
        edge_send[side, 2] = mask[start:start + wide, :].astype(BF16)

    below = lax.broadcasted_iota(jnp.int32, (band, band), 1) < lax.broadcasted_iota(jnp.int32, (band, band), 0)
    below = below.astype(F32).astype(BF16)
    for h in range(HALVES):
        lv = mask[h * band:(h + 1) * band, :]
        place = jnp.where(lv > 0.0, dot(below, lv.astype(BF16)), -1.0)
        across = place.T[0:1, :]
        spot = lax.broadcasted_iota(jnp.int32, (packed, band), 0).astype(F32)
        pack[h] = jnp.where(spot == across, 1.0, 0.0).astype(BF16)
        for start in range(0, packed, ch):
            size = min(ch, packed - start)
            spot = start + lax.broadcasted_iota(jnp.int32, (band, size), 1)
            unpack[h, :, start:start + size] = jnp.where(
                place[:, :size] == spot.astype(F32), 1.0, 0.0).astype(BF16)
    acc[...] = jnp.zeros_like(acc)
    st_send[...] = jnp.zeros_like(st_send)

    pl.semaphore_wait(barrier, s_count - 1 + n - 1)

    def edge_copy(side):
        return pltpu.make_async_remote_copy(
            src_ref=edge_send.at[side], dst_ref=edge_recv.at[1 - side],
            send_sem=e_ssem.at[side], recv_sem=e_rsem.at[1 - side],
            device_id=(z, before if side == 0 else after), device_id_type=MESH)

    for side in range(2):
        edge_copy(side).start()

    w_parts = math.gcd(tap_rows // 16, s_count)
    w_rows = tap_rows // w_parts
    w_mine = s % w_parts
    w_group = s - w_mine

    def wz_copy(which, k):
        at = pl.ds(w_mine * w_rows, w_rows)
        slot = n - k - 1
        return pltpu.make_async_remote_copy(
            src_ref=wv.at[which, (z + k) % n, at, :], dst_ref=wf.at[which, slot, at, :],
            send_sem=wz_ssem.at[which, slot], recv_sem=wz_rsem.at[which, slot],
            device_id=((z + k) % n, s), device_id_type=MESH)

    def wp_copy(which, k, whose):
        at = pl.ds(whose * w_rows, w_rows)
        return pltpu.make_async_remote_copy(
            src_ref=wf.at[which, :, at, :], dst_ref=wf.at[which, :, at, :],
            send_sem=wp_ssem.at[which, k], recv_sem=wp_rsem.at[which, whose],
            device_id=(z, w_group + (w_mine + k) % w_parts), device_id_type=MESH)

    def weights_over_z(which):
        for copy in w_copies[which * n:(which + 1) * n]:
            copy.wait()

        @pl.loop(1, n)
        def _(k):
            wz_copy(which, k).start()

    def weights_round(which):
        @pl.loop(1, n)
        def _(k):
            wz_copy(which, k).wait_recv()

        @pl.loop(1, w_parts)
        def _(k):
            wp_copy(which, k, w_mine).start()

    def weights_arrived(which):
        @pl.loop(1, w_parts)
        def _(k):
            wp_copy(which, k, (w_mine + k) % w_parts).wait_recv()

    def row_copy(slot, side):
        return pltpu.make_async_remote_copy(
            src_ref=row_send.at[slot, side], dst_ref=row_recv.at[slot, 1 - side],
            send_sem=row_ssem.at[slot, side], recv_sem=row_rsem.at[slot, 1 - side],
            device_id=(z, before if side == 0 else after), device_id_type=MESH)

    def send_rows(slot, ref):
        for side, start in ((0, 0), (1, cells - wide)):
            row_send[slot, side] = ref[start:start + wide, :]
            row_copy(slot, side).start()

    def take_rows(slot, ref):
        for side in range(2):
            row_copy(slot, 1 - side).wait_recv()
            ref[cells + side * wide:cells + (side + 1) * wide, :] = row_recv[slot, side]

    def st_copy(slot, k, whose):
        return pltpu.make_async_remote_copy(
            src_ref=st_send.at[slot], dst_ref=st_recv.at[slot, whose],
            send_sem=st_ssem.at[slot, k], recv_sem=st_rsem.at[slot, whose],
            device_id=(z, (s + k) % s_count), device_id_type=MESH)

    def send_stats(slot, values):
        for i, v in enumerate(values):
            st_send[slot, i:i + 1, :] = v
        st_recv[slot, s] = st_send[slot]

        @pl.loop(1, s_count)
        def _(k):
            st_copy(slot, k, s).start()

    def take_stats(slot):
        @pl.loop(1, s_count)
        def _(k):
            st_copy(slot, k, (s + k) % s_count).wait_recv()

    strip = CHUNK // wide
    column = lax.broadcasted_iota(jnp.int32, (CHUNK, ch), 0) % wide

    def shift(target, first, count):
        size = count * wide
        where = column[:size]
        here = pad[pl.ds(8 + first * wide, size), :]
        left = jnp.where(where == 0, 0.0, pad[pl.ds(7 + first * wide, size), :])
        right = jnp.where(where == wide - 1, 0.0, pad[pl.ds(9 + first * wide, size), :])
        for b, v in enumerate((left, here, right)):
            target[pl.ds(first, count), :, b * ch:(b + 1) * ch] = v.astype(BF16).reshape(count, wide, ch)

    edge = 2 * wide
    ag_rows = ((0, edge + packed), (edge + packed, packed))
    band_rows = rows // HALVES

    def unpack_half(ph, block, q, target):
        if q == 0:
            pad[8:8 + wide, :] = hold[ph, block, 0:wide, :].astype(F32)
            pad[8 + wide + cells:8 + 2 * wide + cells, :] = hold[ph, block, wide:edge, :].astype(F32)
            shift(target, 0, 1)
            shift(target, rows + 1, 1)
        pad[8 + wide + q * band:8 + wide + (q + 1) * band, :] = dot(
            unpack[q], hold[ph, block, edge + q * packed:edge + (q + 1) * packed, :])

        @pl.loop(0, band_rows // strip)
        def _(i):
            shift(target, 1 + q * band_rows + i * strip, strip)

    def add_conv(q, field, taps):
        first, last = (0, band_rows - 1) if q == 0 else (band_rows - 1, rows)
        count = last - first
        result = None
        for a in range(3):
            lhs = field[first + a:last + a, :, :].reshape(count * wide, 3 * ch)
            term = dot(lhs, taps(a))
            result = term if result is None else result + term
        at = pl.ds(first * wide, count * wide)
        acc[at, :] = acc[at, :] + result

    def ag_copy(ph, block, q, sign):
        at = pl.ds(*ag_rows[q])
        return pltpu.make_async_remote_copy(
            src_ref=hold.at[ph, block, at, :], dst_ref=hold.at[ph, block, at, :],
            send_sem=ag_ssem.at[ph, (1 - sign) // 2, block, q], recv_sem=ag_rsem.at[ph, block, q],
            device_id=(z + sign, s), device_id_type=MESH)

    def pack_field(ph, value):
        hold[ph, z, 0:edge, :] = value(cells, edge)
        for q in range(HALVES):
            hold[ph, z, edge + q * packed:edge + (q + 1) * packed, :] = dot(
                pack[q], value(q * band, band)).astype(BF16)
            for sign in (1, -1):
                @pl.when((z + sign >= 0) & (z + sign < n))
                def _():
                    ag_copy(ph, z, q, sign).start()

    def gather(ph, consume, each=None):
        @pl.loop(0, n)
        def _(k):
            for q in range(HALVES):
                for sign in (1, -1):
                    block = z - k * sign

                    @pl.when((k > 0) & (block >= 0) & (block < n))
                    def _():
                        ag_copy(ph, block, q, sign).wait_recv()

                        @pl.when((z + sign >= 0) & (z + sign < n))
                        def _():
                            ag_copy(ph, block, q, sign).start()

                @pl.loop(0, 2)
                def _(way):
                    block = z - k * (1 - 2 * way)

                    @pl.when((block >= 0) & (block < n) & ((k > 0) | (way == 0)))
                    def _():
                        consume(k, block, q, gcat.at[way])
            if each is not None:
                each(k)

    def forward(ph):
        def consume(k, block, q, taken):
            unpack_half(ph, block, q, taken)

            @pl.when(k == 0)
            def _():
                add_conv(q, taken, lambda a: wv[ph, z, 3 * a * ch:3 * (a + 1) * ch, :])
                cat[ph, q * band_rows:(q + 1) * band_rows + 2] = taken[q * band_rows:(q + 1) * band_rows + 2]

            @pl.when(k > 0)
            def _():
                slot = (block - z + n - 1) % n
                add_conv(q, taken, lambda a: wf[ph, slot, 3 * a * ch:3 * (a + 1) * ch, :])

        def each(k):
            @pl.when(k == 0)
            def _():
                weights_arrived(ph) if ph else weights_round(0)
                turn_weights(ph)
                if ph == 0:
                    weights_arrived(0)

            @pl.when(k == n - 2)
            def _():
                turn_field(ph)
                if ph == 0:
                    weights_round(1)
        gather(ph, consume, each)

    sub_rows = 16
    sub = sub_rows * wide

    def turn_field(ph):
        for t in range(9):
            a, b = t // 3, t % 3

            @pl.loop(0, cells // sub)
            def _(i):
                v = cat[ph, pl.ds(a + i * sub_rows, sub_rows), :, b * ch:(b + 1) * ch]
                x_t[ph, t * ch:(t + 1) * ch, pl.ds(pl.multiple_of(i * sub, sub), sub)] = (
                    v.reshape(sub, ch).T)

    def turn_weights(ph):
        @pl.loop(0, n)
        def _(d):
            for t in range(9):
                a, b = 2 - t // 3, 2 - t % 3
                wt[ph, d, a, b * ch:(b + 1) * ch, :] = wv[ph, d, t * ch:(t + 1) * ch, :].T

    half_rows = tap_rows // 2
    owners = math.gcd(half_rows // 16, chips)
    piece = half_rows // owners

    def c_copy(ph, j):
        return pltpu.make_async_remote_copy(
            src_ref=psend.at[ph, j], dst_ref=crecv.at[ph, j],
            send_sem=c_ssem.at[ph, j], recv_sem=c_rsem.at[ph, j],
            device_id=(z, chip * 2 + 1 - core), device_id_type=MESH)

    def q_copy(ph, j, e, whose, owner):
        return pltpu.make_async_remote_copy(
            src_ref=hsend.at[ph, j, pl.ds(owner * piece, piece), :], dst_ref=qrecv.at[ph, j, whose],
            send_sem=q_ssem.at[ph, j, e], recv_sem=q_rsem.at[ph, j, whose],
            device_id=(z, ((chip + e) % chips) * 2 + core), device_id_type=MESH)

    def f_copy(ph, j, e, owner):
        at = pl.ds(core * half_rows + owner * piece, piece)
        return pltpu.make_async_remote_copy(
            src_ref=wout.at[ph, j, at, :], dst_ref=wout.at[ph, j, at, :],
            send_sem=f_ssem.at[ph, j, e], recv_sem=f_rsem.at[ph, j, owner],
            device_id=(z, ((chip + e) % chips) * 2 + core), device_id_type=MESH)

    def h_copy(ph, j, whose):
        at = pl.ds(whose * half_rows, half_rows)
        return pltpu.make_async_remote_copy(
            src_ref=wout.at[ph, j, at, :], dst_ref=wout.at[ph, j, at, :],
            send_sem=h_ssem.at[ph, j], recv_sem=h_rsem.at[ph, j],
            device_id=(z, chip * 2 + 1 - core), device_id_type=MESH)

    def o_copy(ph, j):
        target = (out_wg1, out_wg2)[ph]
        if aligned:
            target = target.at[:, pl.ds(pl.multiple_of(j * ch, ch), ch)]
        else:
            target = target.at[j]
        return pltpu.make_async_copy(wout.at[ph, j], target, o_sem.at[ph, j])

    def sum_cores(ph, j):
        psend[ph, j] = part[ph, j, pl.ds((1 - core) * half_rows, half_rows), :].astype(BF16)
        c_copy(ph, j).start()

    def sum_chips(ph, j):
        c_copy(ph, j).wait_recv()
        mine = pl.ds(core * half_rows, half_rows)
        v = part[ph, j, mine, :] + crecv[ph, j].astype(F32)
        part[ph, j, mine, :] = v
        hsend[ph, j] = v.astype(BF16)

        @pl.loop(1, chips)
        def _(e):
            peer = (chip + e) % chips

            @pl.when(peer < owners)
            def _():
                q_copy(ph, j, e, chip, peer).start()

    def spread_chips(ph, j):
        @pl.when(chip < owners)
        def _():
            @pl.loop(1, chips)
            def _(e):
                q_copy(ph, j, e, (chip + e) % chips, chip).wait_recv()
            mine = pl.ds(core * half_rows + chip * piece, piece)

            def one(e, v):
                return v + qrecv[ph, j, (chip + e) % chips].astype(F32)
            wout[ph, j, mine, :] = lax.fori_loop(1, chips, one, part[ph, j, mine, :]).astype(BF16)

            @pl.loop(1, chips)
            def _(e):
                f_copy(ph, j, e, chip).start()

    def spread_cores(ph, j):
        @pl.loop(1, chips)
        def _(e):
            peer = (chip + e) % chips

            @pl.when(peer < owners)
            def _():
                f_copy(ph, j, e, peer).wait_recv()
        h_copy(ph, j, core).start()

    def finish(ph, j):
        h_copy(ph, j, 1 - core).wait_recv()
        o_copy(ph, j).start()

    stages = (sum_cores, sum_chips, spread_chips, spread_cores, finish)

    def advance(ph, k, first=0):
        for age, stage in enumerate(stages):
            if age < first:
                continue

            @pl.loop(0, 2)
            def _(way):
                back = k - age
                block = z - back * (1 - 2 * way)

                @pl.when((back >= 0) & (back < n) & (block >= 0) & (block < n) & ((back > 0) | (way == 0)))
                def _():
                    stage(ph, block)

    def backward(ph):
        def consume(k, block, q, taken):
            unpack_half(2 + ph, block, q, taken)
            add_conv(q, taken, lambda a: wt[ph, block, a])
            if q == HALVES - 1:
                grad = taken[1:rows + 1, :, ch:2 * ch].reshape(cells, ch)

                @pl.loop(0, 3)
                def _(t):
                    at = pl.ds(pl.multiple_of(t * 3 * ch, ch), 3 * ch)
                    part[ph, block, at, :] = dot(x_t[ph, at, :], grad)
        gather(2 + ph, consume, lambda k: advance(ph, k))

    def local_moments(ref):
        def sums(start, size, carry):
            at = pl.ds(start, size)
            m = mask[at, :]
            return (carry[0] + jnp.sum(ref[at, :] * m, axis=0, keepdims=True),
                    carry[1] + jnp.sum(m, axis=0, keepdims=True))
        zero = jnp.zeros((1, ch), F32)
        added, number = chunked(sums, (zero, zero))
        middle = added / jnp.maximum(number, 1.0)

        def spread(start, size, carry):
            at = pl.ds(start, size)
            c = (ref[at, :] - middle) * mask[at, :]
            return carry + jnp.sum(c * c, axis=0, keepdims=True)
        return added, number, chunked(spread, zero)

    def moments(slot):
        take_stats(slot)
        got = [st_recv[slot, k] for k in range(s_count)]
        added = sum(g[0:1] for g in got)
        number = sum(g[1:2] for g in got)
        mean = added / number
        spread = 0.0
        for g in got:
            off = g[0:1] / jnp.maximum(g[1:2], 1.0) - mean
            spread = spread + (g[2:3] + g[1:2] * off * off)
        return mean, lax.rsqrt(spread / number + EPSILON), number

    def everywhere(fn):
        chunked(fn, 0)
        fn(cells, 2 * wide, 0)

    gain1, shift1, gain2, shift2 = (r[...] for r in (gain1_in, shift1_in, gain2_in, shift2_in))

    weights_over_z(0)
    for side in range(2):
        edge_copy(1 - side).wait_recv()
        inside = jnp.where(s > 0, 1.0, 0.0) if side == 0 else jnp.where(s < s_count - 1, 1.0, 0.0)
        at = slice(cells + side * wide, cells + (side + 1) * wide)
        masked[at, :] = edge_recv[side, 0].astype(F32) * inside
        cotm[at, :] = edge_recv[side, 1].astype(F32) * inside
        mask[at, :] = edge_recv[side, 2].astype(F32) * inside

    pack_field(0, lambda start, size: masked[start:start + size, :].astype(BF16))
    weights_over_z(1)
    forward(0)
    send_rows(0, acc)
    send_stats(0, local_moments(acc))
    mean1, scale1, count = moments(0)

    def activate_one(source):
        def step(start, size, carry):
            at = pl.ds(start, size)
            nv = (source[at, :] - mean1) * scale1
            normed1[at, :] = nv
            value, slope = gelu_parts(nv * gain1 + shift1)
            m = mask[at, :]
            hid[at, :] = value * m
            slope1[at, :] = slope * m
            if start is not cells:
                acc[at, :] = jnp.zeros((size, ch), F32)
            return carry
        return step

    chunked(activate_one(acc), 0)
    take_rows(0, normed1)
    activate_one(normed1)(cells, edge, 0)

    pack_field(1, lambda start, size: hid[start:start + size, :].astype(BF16))
    forward(1)
    send_rows(1, acc)
    send_stats(1, local_moments(acc))
    mean2, scale2, _ = moments(1)

    def activate_two(source, start, size):
        at = pl.ds(start, size)
        nv = (source[at, :] - mean2) * scale2
        normed2[at, :] = nv
        value, slope = gelu_parts(nv * gain2 + shift2 + masked[at, :])
        t = cotm[at, :] * slope
        through[at, :] = t
        return value, nv, t

    def activate_main(start, size, carry):
        value, nv, t = activate_two(acc, start, size)
        at = pl.ds(start, size)
        out_block[at, :] = (value * mask[at, :]).astype(BF16)
        acc[at, :] = jnp.zeros((size, ch), F32)
        return (carry[0] + jnp.sum(t * nv, axis=0, keepdims=True),
                carry[1] + jnp.sum(t, axis=0, keepdims=True))

    zero = jnp.zeros((1, ch), F32)
    send_stats(2, chunked(activate_main, (zero, zero)))
    take_rows(1, normed2)
    activate_two(normed2, cells, edge)

    def gradient_sums(slot):
        take_stats(slot)
        got = [st_recv[slot, k] for k in range(s_count)]
        return sum(g[0:1] for g in got), sum(g[1:2] for g in got)

    def norm_back(upstream, normed, gain, scale, sums):
        gain_grad, shift_grad = sums
        factor = gain * scale
        level, tilt = shift_grad / count, gain_grad / count

        def step(start, size, carry):
            at = pl.ds(start, size)
            v = upstream[at, :] - mask[at, :] * (level + normed[at, :] * tilt)
            hid[at, :] = factor * v
            return carry
        everywhere(step)

    sums2 = gradient_sums(2)
    norm_back(through, normed2, gain2, scale2, sums2)
    pack_field(3, lambda start, size: hid[start:start + size, :].astype(BF16))
    backward(1)

    send_rows(2, acc)

    def inner_main(start, size, carry):
        at = pl.ds(start, size)
        v = acc[at, :] * slope1[at, :]
        slope1[at, :] = v
        acc[at, :] = jnp.zeros((size, ch), F32)
        return (carry[0] + jnp.sum(v * normed1[at, :], axis=0, keepdims=True),
                carry[1] + jnp.sum(v, axis=0, keepdims=True))

    send_stats(3, chunked(inner_main, (zero, zero)))
    advance(1, n, 1)
    for side in range(2):
        row_copy(2, 1 - side).wait_recv()
        at = slice(cells + side * wide, cells + (side + 1) * wide)
        slope1[at, :] = row_recv[2, side] * slope1[at, :]
    sums1 = gradient_sums(3)
    norm_back(slope1, normed1, gain1, scale1, sums1)
    pack_field(2, lambda start, size: hid[start:start + size, :].astype(BF16))
    for extra in range(1, len(stages) - 1):
        advance(1, n + extra, 1 + extra)
    backward(0)
    advance(0, n, 1)

    def finish_input(start, size, carry):
        at = pl.ds(start, size)
        out_input[at, :] = (acc[at, :] + through[at, :]) * mask[at, :]
        return carry

    chunked(finish_input, 0)
    out_sums[0:1, :], out_sums[1:2, :] = sums1
    out_sums[2:3, :], out_sums[3:4, :] = sums2
    out_sums[4:8, :] = jnp.zeros((4, ch), F32)
    for extra in range(1, len(stages) - 1):
        advance(0, n + extra, 1 + extra)

    for side in range(2):
        edge_copy(side).wait_send()
        for slot in range(3):
            row_copy(slot, side).wait_send()

    @pl.loop(1, s_count)
    def _(k):
        for slot in range(4):
            st_copy(slot, k, s).wait_send()

    @pl.loop(1, n)
    def _(k):
        for which in range(2):
            wz_copy(which, k).wait_send()

    @pl.loop(1, w_parts)
    def _(k):
        for which in range(2):
            wp_copy(which, k, w_mine).wait_send()

    @pl.loop(0, n)
    def _(k):
        for sign in (1, -1):
            block = z - k * sign

            @pl.when((block >= 0) & (block < n) & (z + sign >= 0) & (z + sign < n))
            def _():
                for ph in range(4):
                    for q in range(HALVES):
                        ag_copy(ph, block, q, sign).wait_send()

    @pl.loop(0, n)
    def _(j):
        for ph in range(2):
            c_copy(ph, j).wait_send()
            h_copy(ph, j, core).wait_send()
            o_copy(ph, j).wait()

            @pl.loop(1, chips)
            def _(e):
                peer = (chip + e) % chips

                @pl.when(peer < owners)
                def _():
                    q_copy(ph, j, e, chip, peer).wait_send()

                @pl.when(chip < owners)
                def _():
                    f_copy(ph, j, e, chip).wait_send()


def per_device(n, s_count, blocks, weight_one, weight_two, gain_one, shift_one, gain_two, shift_two, cell_live, cotangent):
    rows, wide = cell_live.shape
    ch = blocks.shape[1] // wide
    cells = rows * wide
    total = cells + 2 * wide
    packed = -(-most_live(rows // HALVES, wide) // 16) * 16
    aligned = ch % 128 == 0
    chips = s_count // 2
    tap_rows = 9 * ch
    half_rows = tap_rows // 2
    piece = half_rows // math.gcd(half_rows // 16, chips)

    def cells_first(flat):
        return flat.reshape(rows, ch, wide).transpose(0, 2, 1).reshape(cells, ch)

    if aligned:
        weight_one, weight_two = (w.reshape(tap_rows, n * ch) for w in (weight_one, weight_two))
    else:
        weight_one, weight_two = (
            w.reshape(tap_rows, n, ch).transpose(1, 0, 2) for w in (weight_one, weight_two))
    grad_shape = (tap_rows, n * ch) if aligned else (n, tap_rows, ch)
    vmem = pl.BlockSpec(memory_space=pltpu.VMEM)
    hbm = pl.BlockSpec(memory_space=pl.ANY)
    sem = pltpu.SemaphoreType.DMA
    field = pltpu.VMEM((total, ch), F32)
    scratch = [
        pltpu.VMEM((2, n, tap_rows, ch), BF16),
        pltpu.VMEM((2, n - 1, tap_rows, ch), BF16),
        pltpu.VMEM((2, n, 3, 3 * ch, ch), BF16),
        pltpu.VMEM((2, rows + 2, wide, 3 * ch), BF16),
        pltpu.VMEM((2, tap_rows, cells), BF16),
        pltpu.VMEM((HALVES, packed, cells // HALVES), BF16),
        pltpu.VMEM((HALVES, cells // HALVES, packed), BF16),
        pltpu.VMEM((2, 3, wide, ch), BF16),
        pltpu.VMEM((2, 3, wide, ch), BF16),
        field, field, field, field, field, field, field, field,
        pltpu.VMEM((total + 16, ch), F32),
        pltpu.VMEM((cells, ch), F32),
        pltpu.VMEM((4, n, 2 * wide + HALVES * packed, ch), BF16),
        pltpu.VMEM((2, rows + 2, wide, 3 * ch), BF16),
        pltpu.VMEM((2, n, tap_rows, ch), F32),
        pltpu.VMEM((2, n, half_rows, ch), BF16),
        pltpu.VMEM((2, n, half_rows, ch), BF16),
        pltpu.VMEM((2, n, half_rows, ch), BF16),
        pltpu.VMEM((2, n, chips, piece, ch), BF16),
        pltpu.VMEM((2, n, tap_rows, ch), BF16),
        pltpu.VMEM((4, 8, ch), F32),
        pltpu.VMEM((4, s_count, 8, ch), F32),
        pltpu.VMEM((3, 2, wide, ch), F32),
        pltpu.VMEM((3, 2, wide, ch), F32),
        sem((2, n)),
        sem((2, n)), sem((2, n)),
        sem((2, s_count)), sem((2, s_count)),
        sem((2,)), sem((2,)),
        sem((4, 2, n, HALVES)), sem((4, n, HALVES)),
        sem((4, s_count)), sem((4, s_count)),
        sem((3, 2)), sem((3, 2)),
        sem((2, n)), sem((2, n)),
        sem((2, n, chips)), sem((2, n, chips)),
        sem((2, n, chips)), sem((2, n, chips)),
        sem((2, n)), sem((2, n)),
        sem((2, n)),
    ]
    block_out, input_grad, wg1, wg2, sums = pl.pallas_call(
        functools.partial(block_kernel, n, s_count, rows, wide, ch, aligned, packed),
        out_shape=(
            jax.ShapeDtypeStruct((cells, ch), BF16),
            jax.ShapeDtypeStruct((cells, ch), F32),
            jax.ShapeDtypeStruct(grad_shape, BF16),
            jax.ShapeDtypeStruct(grad_shape, BF16),
            jax.ShapeDtypeStruct((8, ch), F32),
        ),
        in_specs=[vmem] * 7 + [hbm] * 2,
        out_specs=(vmem, vmem, hbm, hbm, vmem),
        scratch_shapes=scratch,
        compiler_params=pltpu.CompilerParams(
            collective_id=0, has_side_effects=True, vmem_limit_bytes=60 * 1024 * 1024),
    )(cells_first(blocks), cells_first(cotangent), cell_live,
      *(v.reshape(1, ch) for v in (gain_one, shift_one, gain_two, shift_two)), weight_one, weight_two)

    def flat(grid):
        return grid.reshape(rows, wide, ch).transpose(0, 2, 1).reshape(rows, wide * ch)

    def whole(grad):
        if not aligned:
            grad = grad.transpose(1, 0, 2)
        return grad.astype(F32).reshape(9, ch, n * ch)

    return (flat(block_out), flat(input_grad), whole(wg1), whole(wg2), sums[0], sums[1], sums[2], sums[3])


def solution(mesh):
    return jax.shard_map(
        functools.partial(per_device, mesh.shape["chan"], mesh.shape["space"]),
        mesh=mesh,
        in_specs=(
            P("space", "chan"),
            P(None, "chan", None),
            P(None, "chan", None),
            P("chan"),
            P("chan"),
            P("chan"),
            P("chan"),
            P("space", None),
            P("space", "chan"),
        ),
        out_specs=(
            P("space", "chan"),
            P("space", "chan"),
            P(None, "chan", None),
            P(None, "chan", None),
            P("chan"),
            P("chan"),
            P("chan"),
            P("chan"),
        ),
        check_vma=False,
    )
```

```python
import functools
import math

import jax
import jax.numpy as jnp
from jax import lax
from jax.experimental import pallas as pl
from jax.experimental.pallas import tpu as pltpu
from jax.sharding import PartitionSpec as P

EPSILON = 1e-05
MESH = pl.DeviceIdType.MESH
F32 = jnp.float32
BF16 = jnp.bfloat16
ROOT_HALF = 0.7071067811865476
ROOT_TWO_PI = 0.3989422804014327
CHUNK = 64
UNROLL = 2
HALVES = 2
LARGE, SMALL = 7, 3


def dot(a, b):
    return jnp.dot(a, b, preferred_element_type=F32)


def gelu_parts(v):
    upper = 0.5 * (1.0 + lax.erf(v * ROOT_HALF))
    slope = upper + v * (ROOT_TWO_PI * jnp.exp(-0.5 * v * v))
    return v * upper, slope


def most_live(rows, wide):
    units = (wide + 1) // (SMALL + 1)
    live_rows = rows - rows // (LARGE + 1)
    return min(rows * wide, math.ceil(units * live_rows * LARGE / 2))


def block_kernel(n, s_count, rows, wide, ch, aligned, packed, *refs):
    (x_in, cot_in, live_in, gain1_in, shift1_in, gain2_in, shift2_in, w1_hbm, w2_hbm) = refs[:9]
    (out_block, out_input, out_wg1, out_wg2, out_sums) = refs[9:14]
    (wv, wf, wt, x_t, pack, unpack, edge_send, edge_recv, cotm, mask, masked,
     normed1, normed2, through, slope1, hid, pad, acc, hold, taken,
     part, psend, crecv, hsend, qrecv, wout, st_send, st_recv, row_send, row_recv,
     w_sem, wz_ssem, wz_rsem, wp_ssem, wp_rsem, e_ssem, e_rsem, ag_ssem, ag_rsem,
     st_ssem, st_rsem, row_ssem, row_rsem, c_ssem, c_rsem, q_ssem, q_rsem,
     f_ssem, f_rsem, h_ssem, h_rsem, o_sem) = refs[14:]

    z = lax.axis_index("chan")
    s = lax.axis_index("space")
    cells = rows * wide
    total = cells + 2 * wide
    band = cells // HALVES
    core, chip, chips = s % 2, s // 2, s_count // 2
    before, after = (s + s_count - 1) % s_count, (s + 1) % s_count
    tap_rows = 9 * ch

    barrier = pltpu.get_barrier_semaphore()

    @pl.loop(1, s_count)
    def _(k):
        pl.semaphore_signal(barrier, inc=1, device_id=(z, (s + k) % s_count), device_id_type=MESH)

    @pl.loop(1, n)
    def _(k):
        pl.semaphore_signal(barrier, inc=1, device_id=((z + k) % n, s), device_id_type=MESH)

    w_copies = []
    for which, source in enumerate((w1_hbm, w2_hbm)):
        for d in range(n):
            block = source.at[:, d * ch:(d + 1) * ch] if aligned else source.at[d]
            w_copies.append(pltpu.make_async_copy(block, wv.at[which, d], w_sem.at[which, d]))
    for copy in w_copies:
        copy.start()

    def chunked(fn, init, first=0, count=cells):
        def step(i, carry):
            return fn(pl.multiple_of(first + i * CHUNK, CHUNK), CHUNK, carry)
        return lax.fori_loop(0, count // CHUNK, step, init, unroll=UNROLL)

    cell = lax.broadcasted_iota(jnp.int32, (cells, rows), 0)
    pick = (cell // wide == lax.broadcasted_iota(jnp.int32, (cells, rows), 1)).astype(F32).astype(BF16)
    column_of = lax.broadcasted_iota(jnp.int32, (cells, wide), 0) % wide
    picked = dot(pick, live_in[...].astype(BF16))
    picked = jnp.where(column_of == lax.broadcasted_iota(jnp.int32, (cells, wide), 1), picked, 0.0)
    mask[0:cells, :] = dot(picked.astype(BF16), jnp.ones((wide, ch), BF16))

    def load_main(start, size, carry):
        at = pl.ds(start, size)
        lv = mask[at, :]
        masked[at, :] = x_in[at, :].astype(F32) * lv
        cotm[at, :] = cot_in[at, :].astype(F32) * lv
        return carry

    chunked(load_main, 0)
    for side, start in ((0, 0), (1, cells - wide)):
        edge_send[side, 0] = masked[start:start + wide, :].astype(BF16)
        edge_send[side, 1] = cotm[start:start + wide, :].astype(BF16)
        edge_send[side, 2] = mask[start:start + wide, :].astype(BF16)

    acc[...] = jnp.zeros_like(acc)
    st_send[...] = jnp.zeros_like(st_send)

    pl.semaphore_wait(barrier, s_count - 1 + n - 1)

    def edge_copy(side):
        return pltpu.make_async_remote_copy(
            src_ref=edge_send.at[side], dst_ref=edge_recv.at[1 - side],
            send_sem=e_ssem.at[side], recv_sem=e_rsem.at[1 - side],
            device_id=(z, before if side == 0 else after), device_id_type=MESH)

    for side in range(2):
        edge_copy(side).start()

    w_parts = math.gcd(tap_rows // 16, s_count)
    w_rows = tap_rows // w_parts
    w_mine = s % w_parts
    w_group = s - w_mine

    def wz_copy(which, k):
        at = pl.ds(w_mine * w_rows, w_rows)
        slot = n - k - 1
        return pltpu.make_async_remote_copy(
            src_ref=wv.at[which, (z + k) % n, at, :], dst_ref=wf.at[which, slot, at, :],
            send_sem=wz_ssem.at[which, slot], recv_sem=wz_rsem.at[which, slot],
            device_id=((z + k) % n, s), device_id_type=MESH)

    def wp_copy(which, slot, k, whose):
        at = pl.ds(whose * w_rows, w_rows)
        return pltpu.make_async_remote_copy(
            src_ref=wf.at[which, slot, at, :], dst_ref=wf.at[which, slot, at, :],
            send_sem=wp_ssem.at[which, slot, k], recv_sem=wp_rsem.at[which, slot, whose],
            device_id=(z, w_group + (w_mine + k) % w_parts), device_id_type=MESH)

    def weights_over_z(which):
        for copy in w_copies[which * n:(which + 1) * n]:
            copy.wait()

        @pl.loop(1, n)
        def _(k):
            wz_copy(which, k).start()

    def slot_of(block):
        return (block - z + n - 1) % n

    def weights_round(which):
        @pl.loop(1, n)
        def _(distance):
            for sign in (1, -1):
                block = z - distance * sign

                @pl.when((block >= 0) & (block < n))
                def _():
                    slot = slot_of(block)
                    wz_copy(which, n - 1 - slot).wait_recv()

                    @pl.loop(1, w_parts)
                    def _(k):
                        wp_copy(which, slot, k, w_mine).start()

    def weights_arrived(which, slot):
        @pl.loop(1, w_parts)
        def _(k):
            wp_copy(which, slot, k, (w_mine + k) % w_parts).wait_recv()

    def row_copy(slot, side):
        return pltpu.make_async_remote_copy(
            src_ref=row_send.at[slot, side], dst_ref=row_recv.at[slot, 1 - side],
            send_sem=row_ssem.at[slot, side], recv_sem=row_rsem.at[slot, 1 - side],
            device_id=(z, before if side == 0 else after), device_id_type=MESH)

    def send_rows(slot, ref):
        for side, start in ((0, 0), (1, cells - wide)):
            row_send[slot, side] = ref[start:start + wide, :]
            row_copy(slot, side).start()

    def take_rows(slot, ref):
        for side in range(2):
            row_copy(slot, 1 - side).wait_recv()
            ref[cells + side * wide:cells + (side + 1) * wide, :] = row_recv[slot, side]

    def st_copy(slot, k, whose):
        return pltpu.make_async_remote_copy(
            src_ref=st_send.at[slot], dst_ref=st_recv.at[slot, whose],
            send_sem=st_ssem.at[slot, k], recv_sem=st_rsem.at[slot, whose],
            device_id=(z, (s + k) % s_count), device_id_type=MESH)

    def send_stats(slot, values):
        for i, v in enumerate(values):
            st_send[slot, i:i + 1, :] = v
        st_recv[slot, s] = st_send[slot]

        @pl.loop(1, s_count)
        def _(k):
            st_copy(slot, k, s).start()

    def take_stats(slot):
        @pl.loop(1, s_count)
        def _(k):
            st_copy(slot, k, (s + k) % s_count).wait_recv()

    strip = 8
    column = lax.broadcasted_iota(jnp.int32, (strip * wide, ch), 0) % wide

    def shift(target, first, count):
        size = count * wide
        where = column[:size]
        here = pad[pl.ds(8 + first * wide, size), :]
        left = jnp.where(where == 0, 0.0, pad[pl.ds(7 + first * wide, size), :])
        right = jnp.where(where == wide - 1, 0.0, pad[pl.ds(9 + first * wide, size), :])
        for b, v in enumerate((left, here, right)):
            target[pl.ds(first, count), :, b * ch:(b + 1) * ch] = v.astype(BF16).reshape(count, wide, ch)

    edge = 2 * wide
    ag_rows = ((0, edge + packed), (edge + packed, packed))
    band_rows = rows // HALVES

    def unpack_half(ph, block, q, target):
        if q == 0:
            pad[8:8 + wide, :] = hold[ph, block, 0:wide, :].astype(F32)
            pad[8 + wide + cells:8 + 2 * wide + cells, :] = hold[ph, block, wide:edge, :].astype(F32)
            shift(target, 0, 1)
            shift(target, rows + 1, 1)
        pad[8 + wide + q * band:8 + wide + (q + 1) * band, :] = dot(
            unpack[q], hold[ph, block, edge + q * packed:edge + (q + 1) * packed, :])

        for i in range(band_rows // strip):
            shift(target, 1 + q * band_rows + i * strip, strip)

    def add_conv(q, field, taps):
        first, last = (0, band_rows - 1) if q == 0 else (band_rows - 1, rows)
        count = last - first
        result = None
        for a in range(3):
            lhs = field[first + a:last + a, :, :].reshape(count * wide, 3 * ch)
            term = dot(lhs, taps(a))
            result = term if result is None else result + term
        at = pl.ds(first * wide, count * wide)
        acc[at, :] = acc[at, :] + result

    def ag_copy(ph, block, q, sign):
        at = pl.ds(*ag_rows[q])
        return pltpu.make_async_remote_copy(
            src_ref=hold.at[ph, block, at, :], dst_ref=hold.at[ph, block, at, :],
            send_sem=ag_ssem.at[ph, (1 - sign) // 2, block, q], recv_sem=ag_rsem.at[ph, block, q],
            device_id=(z + sign, s), device_id_type=MESH)

    def pack_field(ph, value):
        hold[ph, z, 0:edge, :] = value(cells, edge)
        for q in range(HALVES):
            hold[ph, z, edge + q * packed:edge + (q + 1) * packed, :] = dot(
                pack[q], value(q * band, band)).astype(BF16)
            for sign in (1, -1):
                @pl.when((z + sign >= 0) & (z + sign < n))
                def _():
                    ag_copy(ph, z, q, sign).start()

    def inside(slice_at):
        return (slice_at >= 0) & (slice_at < n)

    def take_and_pass(ph, k, q, sign, passes=True, takes=True):
        block = z - k * sign

        @pl.when((k > 0) & inside(block))
        def _():
            if passes and takes:
                ag_copy(ph, block, q, sign).wait_recv()

            @pl.when(inside(z + sign))
            def _():
                if passes:
                    if not takes:
                        ag_copy(ph, block, q, sign).wait_recv()
                    ag_copy(ph, block, q, sign).start()

            if not passes:
                @pl.when(jnp.logical_not(inside(z + sign)))
                def _():
                    ag_copy(ph, block, q, sign).wait_recv()

    def consume_both(k, q, consume):
        @pl.loop(0, 2)
        def _(way):
            block = z - k * (1 - 2 * way)

            @pl.when(inside(block) & ((k > 0) | (way == 0)))
            def _():
                consume(k, block, q, taken.at[way])

    def gather(ph, consume, each):
        @pl.loop(0, n)
        def _(k):
            for q in range(HALVES):
                for sign in (1, -1):
                    take_and_pass(ph, k, q, sign)
                consume_both(k, q, consume)
            each(k)

    def gather_passing_first(ph, consume, each):
        @pl.loop(0, n)
        def _(k):
            @pl.when(k == 1)
            def _():
                @pl.loop(1, n)
                def _(ahead):
                    for q in range(HALVES):
                        for sign in (1, -1):
                            take_and_pass(ph, ahead, q, sign, takes=False)
            for q in range(HALVES):
                for sign in (1, -1):
                    take_and_pass(ph, k, q, sign, passes=False)
                consume_both(k, q, consume)
            each(k)

    last_pass = jnp.maximum(jnp.where(z < n - 1, z, 0), jnp.where(z > 0, n - 1 - z, 0))

    def forward(ph, field):
        def consume(k, block, q, into):
            unpack_half(ph, block, q, into)

            @pl.when(k == 0)
            def _():
                add_conv(q, into, lambda a: wv[ph, z, 3 * a * ch:3 * (a + 1) * ch, :])

            @pl.when(k > 0)
            def _():
                slot = slot_of(block)
                if q == 0:
                    weights_arrived(ph, slot)
                add_conv(q, into, lambda a: wf[ph, slot, 3 * a * ch:3 * (a + 1) * ch, :])

        def each(k):
            if ph == 0:
                @pl.when(k == 0)
                def _():
                    weights_round(0)

            @pl.when(k == last_pass)
            def _():
                turn_weights(ph)
                for i in range(cells // ch):
                    x_t[ph, :, i * ch:(i + 1) * ch] = field[i * ch:(i + 1) * ch, :].T.astype(BF16)
        (gather if ph else gather_passing_first)(ph, consume, each)

    def turn_weights(ph):
        @pl.loop(0, n)
        def _(d):
            for t in range(9):
                a, b = 2 - t // 3, 2 - t % 3
                wt[ph, d, a, b * ch:(b + 1) * ch, :] = wv[ph, d, t * ch:(t + 1) * ch, :].T

    half_rows = tap_rows // 2
    owners = math.gcd(half_rows // 16, chips)
    piece = half_rows // owners

    def c_copy(ph, j):
        return pltpu.make_async_remote_copy(
            src_ref=psend.at[ph, j], dst_ref=crecv.at[ph, j],
            send_sem=c_ssem.at[ph, j], recv_sem=c_rsem.at[ph, j],
            device_id=(z, chip * 2 + 1 - core), device_id_type=MESH)

    def q_copy(ph, j, e, whose, owner):
        return pltpu.make_async_remote_copy(
            src_ref=hsend.at[ph, j, owner], dst_ref=qrecv.at[ph, j, whose],
            send_sem=q_ssem.at[ph, j, e], recv_sem=q_rsem.at[ph, j, whose],
            device_id=(z, ((chip + e) % chips) * 2 + core), device_id_type=MESH)

    def f_copy(ph, j, e, owner):
        return pltpu.make_async_remote_copy(
            src_ref=wout.at[ph, j, core, owner], dst_ref=wout.at[ph, j, core, owner],
            send_sem=f_ssem.at[ph, j, e], recv_sem=f_rsem.at[ph, j, owner],
            device_id=(z, ((chip + e) % chips) * 2 + core), device_id_type=MESH)

    def h_copy(ph, j, whose):
        return pltpu.make_async_remote_copy(
            src_ref=wout.at[ph, j, whose], dst_ref=wout.at[ph, j, whose],
            send_sem=h_ssem.at[ph, j], recv_sem=h_rsem.at[ph, j],
            device_id=(z, chip * 2 + 1 - core), device_id_type=MESH)

    def o_copy(ph, j):
        target = (out_wg1, out_wg2)[ph]
        if aligned:
            target = target.at[:, :, :, pl.ds(pl.multiple_of(j * ch, ch), ch)]
        else:
            target = target.at[j]
        return pltpu.make_async_copy(wout.at[ph, j], target, o_sem.at[ph, j])

    def sum_cores(ph, j):
        for o in range(owners):
            psend[ph, j, o] = part[ph, j, 1 - core, o].astype(BF16)
        c_copy(ph, j).start()

    def sum_chips(ph, j):
        c_copy(ph, j).wait_recv()
        for o in range(owners):
            v = part[ph, j, core, o] + crecv[ph, j, o].astype(F32)
            part[ph, j, core, o] = v
            hsend[ph, j, o] = v.astype(BF16)

        @pl.loop(1, chips)
        def _(e):
            peer = (chip + e) % chips

            @pl.when(peer < owners)
            def _():
                q_copy(ph, j, e, chip, peer).start()

    def spread_chips(ph, j):
        @pl.when(chip < owners)
        def _():
            @pl.loop(1, chips)
            def _(e):
                q_copy(ph, j, e, (chip + e) % chips, chip).wait_recv()
            v = part[ph, j, core, chip]
            for e in range(1, chips):
                v = v + qrecv[ph, j, (chip + e) % chips].astype(F32)
            wout[ph, j, core, chip] = v.astype(BF16)

            @pl.loop(1, chips)
            def _(e):
                f_copy(ph, j, e, chip).start()

    def spread_cores(ph, j):
        @pl.loop(1, chips)
        def _(e):
            peer = (chip + e) % chips

            @pl.when(peer < owners)
            def _():
                f_copy(ph, j, e, peer).wait_recv()
        h_copy(ph, j, core).start()

    def finish(ph, j):
        h_copy(ph, j, 1 - core).wait_recv()
        o_copy(ph, j).start()

    def put_part(ph, j, tap, value):
        start = tap * ch
        done = 0
        while done < ch:
            row = start + done
            side, o, at = row // half_rows, row % half_rows // piece, row % piece
            size = min(ch - done, piece - at)
            part[ph, j, side, o, at:at + size, :] = value[done:done + size, :]
            done += size

    stages = (sum_cores, sum_chips, spread_chips, spread_cores, finish)

    def advance(ph, k, first=0):
        for age, stage in enumerate(stages):
            if age < first:
                continue

            @pl.loop(0, 2)
            def _(way):
                back = k - age
                block = z - back * (1 - 2 * way)

                @pl.when((back >= 0) & (back < n) & (block >= 0) & (block < n) & ((back > 0) | (way == 0)))
                def _():
                    stage(ph, block)

    def backward(ph):
        def consume(k, block, q, into):
            unpack_half(2 + ph, block, q, into)
            add_conv(q, into, lambda a: wt[ph, block, a])
            if q == HALVES - 1:
                for a in range(3):
                    grad = into[a:a + rows, :, :].reshape(cells, 3 * ch)
                    value = dot(x_t[ph], grad)
                    for b in range(3):
                        put_part(ph, block, 3 * (2 - a) + 2 - b, value[:, b * ch:(b + 1) * ch])
        gather(2 + ph, consume, lambda k: advance(ph, k))

    def fold(v):
        return jnp.sum(v.reshape(v.shape[0] // 8, 8, ch), axis=0)

    def flatten(v):
        return jnp.sum(v, axis=0, keepdims=True)

    zero = jnp.zeros((8, ch), F32)

    def local_moments(ref):
        def sums(start, size, carry):
            at = pl.ds(start, size)
            m = mask[at, :]
            return carry[0] + fold(ref[at, :] * m), carry[1] + fold(m)
        added, number = (flatten(v) for v in chunked(sums, (zero, zero)))
        middle = added / jnp.maximum(number, 1.0)

        def spread(start, size, carry):
            at = pl.ds(start, size)
            c = (ref[at, :] - middle) * mask[at, :]
            return carry + fold(c * c)
        return added, number, flatten(chunked(spread, zero))

    def moments(slot):
        take_stats(slot)
        got = [st_recv[slot, k] for k in range(s_count)]
        added = sum(g[0:1] for g in got)
        number = sum(g[1:2] for g in got)
        mean = added / number
        spread = 0.0
        for g in got:
            off = g[0:1] / jnp.maximum(g[1:2], 1.0) - mean
            spread = spread + (g[2:3] + g[1:2] * off * off)
        return mean, lax.rsqrt(spread / number + EPSILON), number

    def everywhere(fn):
        chunked(fn, 0)
        fn(cells, 2 * wide, 0)

    gain1, shift1, gain2, shift2 = (r[...] for r in (gain1_in, shift1_in, gain2_in, shift2_in))

    weights_over_z(0)

    below = lax.broadcasted_iota(jnp.int32, (band, band), 1) < lax.broadcasted_iota(jnp.int32, (band, band), 0)
    below = below.astype(F32).astype(BF16)
    for h in range(HALVES):
        lv = mask[h * band:(h + 1) * band, :]
        place = jnp.where(lv > 0.0, dot(below, lv.astype(BF16)), -1.0)
        across = place.T[0:1, :]
        spot = lax.broadcasted_iota(jnp.int32, (packed, band), 0).astype(F32)
        pack[h] = jnp.where(spot == across, 1.0, 0.0).astype(BF16)
        for start in range(0, packed, ch):
            size = min(ch, packed - start)
            spot = start + lax.broadcasted_iota(jnp.int32, (band, size), 1)
            unpack[h, :, start:start + size] = jnp.where(
                place[:, :size] == spot.astype(F32), 1.0, 0.0).astype(BF16)

    for side in range(2):
        edge_copy(1 - side).wait_recv()
        there = jnp.where(s > 0, 1.0, 0.0) if side == 0 else jnp.where(s < s_count - 1, 1.0, 0.0)
        at = slice(cells + side * wide, cells + (side + 1) * wide)
        masked[at, :] = edge_recv[side, 0].astype(F32) * there
        cotm[at, :] = edge_recv[side, 1].astype(F32) * there
        mask[at, :] = edge_recv[side, 2].astype(F32) * there

    pack_field(0, lambda start, size: masked[start:start + size, :].astype(BF16))
    forward(0, masked)
    weights_over_z(1)
    send_rows(0, acc)
    send_stats(0, local_moments(acc))
    mean1, scale1, count = moments(0)
    weights_round(1)

    def activate_one(source):
        def step(start, size, carry):
            at = pl.ds(start, size)
            nv = (source[at, :] - mean1) * scale1
            normed1[at, :] = nv
            value, slope = gelu_parts(nv * gain1 + shift1)
            m = mask[at, :]
            hid[at, :] = value * m
            slope1[at, :] = slope * m
            if start is not cells:
                acc[at, :] = jnp.zeros((size, ch), F32)
            return carry
        return step

    chunked(activate_one(acc), 0)
    take_rows(0, normed1)
    activate_one(normed1)(cells, edge, 0)

    pack_field(1, lambda start, size: hid[start:start + size, :].astype(BF16))
    forward(1, hid)
    send_rows(1, acc)
    send_stats(1, local_moments(acc))
    mean2, scale2, _ = moments(1)

    def activate_two(source, start, size):
        at = pl.ds(start, size)
        nv = (source[at, :] - mean2) * scale2
        normed2[at, :] = nv
        value, slope = gelu_parts(nv * gain2 + shift2 + masked[at, :])
        t = cotm[at, :] * slope
        through[at, :] = t
        return value, nv, t

    def activate_main(start, size, carry):
        value, nv, t = activate_two(acc, start, size)
        at = pl.ds(start, size)
        out_block[at, :] = (value * mask[at, :]).astype(BF16)
        acc[at, :] = jnp.zeros((size, ch), F32)
        return (carry[0] + fold(t * nv),
                carry[1] + fold(t))

    send_stats(2, [flatten(v) for v in chunked(activate_main, (zero, zero))])
    take_rows(1, normed2)
    activate_two(normed2, cells, edge)

    def gradient_sums(slot):
        take_stats(slot)
        got = [st_recv[slot, k] for k in range(s_count)]
        return sum(g[0:1] for g in got), sum(g[1:2] for g in got)

    def norm_back(upstream, normed, gain, scale, sums):
        gain_grad, shift_grad = sums
        factor = gain * scale
        level, tilt = shift_grad / count, gain_grad / count

        def step(start, size, carry):
            at = pl.ds(start, size)
            v = upstream[at, :] - mask[at, :] * (level + normed[at, :] * tilt)
            hid[at, :] = factor * v
            return carry
        everywhere(step)

    sums2 = gradient_sums(2)
    norm_back(through, normed2, gain2, scale2, sums2)
    pack_field(3, lambda start, size: hid[start:start + size, :].astype(BF16))
    backward(1)

    send_rows(2, acc)

    def inner_main(start, size, carry):
        at = pl.ds(start, size)
        v = acc[at, :] * slope1[at, :]
        slope1[at, :] = v
        acc[at, :] = jnp.zeros((size, ch), F32)
        return (carry[0] + fold(v * normed1[at, :]),
                carry[1] + fold(v))

    send_stats(3, [flatten(v) for v in chunked(inner_main, (zero, zero))])
    advance(1, n, 1)
    for side in range(2):
        row_copy(2, 1 - side).wait_recv()
        at = slice(cells + side * wide, cells + (side + 1) * wide)
        slope1[at, :] = row_recv[2, side] * slope1[at, :]
    sums1 = gradient_sums(3)
    norm_back(slope1, normed1, gain1, scale1, sums1)
    pack_field(2, lambda start, size: hid[start:start + size, :].astype(BF16))
    for extra in range(1, len(stages) - 1):
        advance(1, n + extra, 1 + extra)
    backward(0)
    advance(0, n, 1)

    def finish_input(start, size, carry):
        at = pl.ds(start, size)
        out_input[at, :] = (acc[at, :] + through[at, :]) * mask[at, :]
        return carry

    chunked(finish_input, 0)
    out_sums[0:1, :], out_sums[1:2, :] = sums1
    out_sums[2:3, :], out_sums[3:4, :] = sums2
    out_sums[4:8, :] = jnp.zeros((4, ch), F32)
    for extra in range(1, len(stages) - 1):
        advance(0, n + extra, 1 + extra)

    for side in range(2):
        edge_copy(side).wait_send()
        for slot in range(3):
            row_copy(slot, side).wait_send()

    @pl.loop(1, s_count)
    def _(k):
        for slot in range(4):
            st_copy(slot, k, s).wait_send()

    @pl.loop(1, n)
    def _(k):
        for which in range(2):
            wz_copy(which, k).wait_send()

    @pl.loop(1, w_parts)
    def _(k):
        for which in range(2):
            for slot in range(n - 1):
                wp_copy(which, slot, k, w_mine).wait_send()

    @pl.loop(0, n)
    def _(k):
        for sign in (1, -1):
            block = z - k * sign

            @pl.when((block >= 0) & (block < n) & (z + sign >= 0) & (z + sign < n))
            def _():
                for ph in range(4):
                    for q in range(HALVES):
                        ag_copy(ph, block, q, sign).wait_send()

    @pl.loop(0, n)
    def _(j):
        for ph in range(2):
            c_copy(ph, j).wait_send()
            h_copy(ph, j, core).wait_send()
            o_copy(ph, j).wait()

            @pl.loop(1, chips)
            def _(e):
                peer = (chip + e) % chips

                @pl.when(peer < owners)
                def _():
                    q_copy(ph, j, e, chip, peer).wait_send()

                @pl.when(chip < owners)
                def _():
                    f_copy(ph, j, e, chip).wait_send()


def per_device(n, s_count, blocks, weight_one, weight_two, gain_one, shift_one, gain_two, shift_two, cell_live, cotangent):
    rows, wide = cell_live.shape
    ch = blocks.shape[1] // wide
    cells = rows * wide
    total = cells + 2 * wide
    packed = -(-most_live(rows // HALVES, wide) // 16) * 16
    aligned = ch % 128 == 0
    chips = s_count // 2
    tap_rows = 9 * ch
    half_rows = tap_rows // 2
    owners = math.gcd(half_rows // 16, chips)
    piece = half_rows // owners

    def cells_first(flat):
        return flat.reshape(rows, ch, wide).transpose(0, 2, 1).reshape(cells, ch)

    if aligned:
        weight_one, weight_two = (w.reshape(tap_rows, n * ch) for w in (weight_one, weight_two))
    else:
        weight_one, weight_two = (
            w.reshape(tap_rows, n, ch).transpose(1, 0, 2) for w in (weight_one, weight_two))
    grad_shape = (2, owners, piece, n * ch) if aligned else (n, 2, owners, piece, ch)
    vmem = pl.BlockSpec(memory_space=pltpu.VMEM)
    hbm = pl.BlockSpec(memory_space=pl.ANY)
    sem = pltpu.SemaphoreType.DMA
    field = pltpu.VMEM((total, ch), F32)
    scratch = [
        pltpu.VMEM((2, n, tap_rows, ch), BF16),
        pltpu.VMEM((2, n - 1, tap_rows, ch), BF16),
        pltpu.VMEM((2, n, 3, 3 * ch, ch), BF16),
        pltpu.VMEM((2, ch, cells), BF16),
        pltpu.VMEM((HALVES, packed, cells // HALVES), BF16),
        pltpu.VMEM((HALVES, cells // HALVES, packed), BF16),
        pltpu.VMEM((2, 3, wide, ch), BF16),
        pltpu.VMEM((2, 3, wide, ch), BF16),
        field, field, field, field, field, field, field, field,
        pltpu.VMEM((total + 16, ch), F32),
        pltpu.VMEM((cells, ch), F32),
        pltpu.VMEM((4, n, 2 * wide + HALVES * packed, ch), BF16),
        pltpu.VMEM((2, rows + 2, wide, 3 * ch), BF16),
        pltpu.VMEM((2, n, 2, owners, piece, ch), F32),
        pltpu.VMEM((2, n, owners, piece, ch), BF16),
        pltpu.VMEM((2, n, owners, piece, ch), BF16),
        pltpu.VMEM((2, n, owners, piece, ch), BF16),
        pltpu.VMEM((2, n, chips, piece, ch), BF16),
        pltpu.VMEM((2, n, 2, owners, piece, ch), BF16),
        pltpu.VMEM((4, 8, ch), F32),
        pltpu.VMEM((4, s_count, 8, ch), F32),
        pltpu.VMEM((3, 2, wide, ch), F32),
        pltpu.VMEM((3, 2, wide, ch), F32),
        sem((2, n)),
        sem((2, n)), sem((2, n)),
        sem((2, n - 1, s_count)), sem((2, n - 1, s_count)),
        sem((2,)), sem((2,)),
        sem((4, 2, n, HALVES)), sem((4, n, HALVES)),
        sem((4, s_count)), sem((4, s_count)),
        sem((3, 2)), sem((3, 2)),
        sem((2, n)), sem((2, n)),
        sem((2, n, chips)), sem((2, n, chips)),
        sem((2, n, chips)), sem((2, n, chips)),
        sem((2, n)), sem((2, n)),
        sem((2, n)),
    ]
    block_out, input_grad, wg1, wg2, sums = pl.pallas_call(
        functools.partial(block_kernel, n, s_count, rows, wide, ch, aligned, packed),
        out_shape=(
            jax.ShapeDtypeStruct((cells, ch), BF16),
            jax.ShapeDtypeStruct((cells, ch), F32),
            jax.ShapeDtypeStruct(grad_shape, BF16),
            jax.ShapeDtypeStruct(grad_shape, BF16),
            jax.ShapeDtypeStruct((8, ch), F32),
        ),
        in_specs=[vmem] * 7 + [hbm] * 2,
        out_specs=(vmem, vmem, hbm, hbm, vmem),
        scratch_shapes=scratch,
        compiler_params=pltpu.CompilerParams(
            collective_id=0, has_side_effects=True, vmem_limit_bytes=60 * 1024 * 1024),
    )(cells_first(blocks), cells_first(cotangent), cell_live,
      *(v.reshape(1, ch) for v in (gain_one, shift_one, gain_two, shift_two)), weight_one, weight_two)

    def flat(grid):
        return grid.reshape(rows, wide, ch).transpose(0, 2, 1).reshape(rows, wide * ch)

    def whole(grad):
        if not aligned:
            grad = grad.reshape(n, tap_rows, ch).transpose(1, 0, 2)
        return grad.astype(F32).reshape(9, ch, n * ch)

    return (flat(block_out), flat(input_grad), whole(wg1), whole(wg2), sums[0], sums[1], sums[2], sums[3])


def solution(mesh):
    return jax.shard_map(
        functools.partial(per_device, mesh.shape["chan"], mesh.shape["space"]),
        mesh=mesh,
        in_specs=(
            P("space", "chan"),
            P(None, "chan", None),
            P(None, "chan", None),
            P("chan"),
            P("chan"),
            P("chan"),
            P("chan"),
            P("space", None),
            P("space", "chan"),
        ),
        out_specs=(
            P("space", "chan"),
            P("space", "chan"),
            P(None, "chan", None),
            P(None, "chan", None),
            P("chan"),
            P("chan"),
            P("chan"),
            P("chan"),
        ),
        check_vma=False,
    )
```

```python
import functools
import math

import jax
import jax.numpy as jnp
from jax import lax
from jax.experimental import pallas as pl
from jax.experimental.pallas import tpu as pltpu
from jax.sharding import PartitionSpec as P

EPSILON = 1e-05
MESH = pl.DeviceIdType.MESH
F32 = jnp.float32
BF16 = jnp.bfloat16
ROOT_HALF = 0.7071067811865476
ROOT_TWO_PI = 0.3989422804014327
CHUNK = 64
UNROLL = 2
HALVES = 2
LARGE, SMALL = 7, 3


def dot(a, b):
    return jnp.dot(a, b, preferred_element_type=F32)


def gelu_parts(v):
    upper = 0.5 * (1.0 + lax.erf(v * ROOT_HALF))
    slope = upper + v * (ROOT_TWO_PI * jnp.exp(-0.5 * v * v))
    return v * upper, slope


def most_live(rows, wide):
    units = (wide + 1) // (SMALL + 1)
    live_rows = rows - rows // (LARGE + 1)
    return min(rows * wide, math.ceil(units * live_rows * LARGE / 2))


def block_kernel(n, s_count, rows, wide, ch, aligned, packed, *refs):
    (x_in, cot_in, live_in, gain1_in, shift1_in, gain2_in, shift2_in, w1_hbm, w2_hbm) = refs[:9]
    (out_block, out_input, out_wg1, out_wg2, out_sums) = refs[9:14]
    (wv, wf, wt, x_t, pack, unpack, places, edge_send, edge_recv, cotm, mask, masked,
     normed1, normed2, through, slope1, hid, pad, acc, hold, taken,
     part, psend, crecv, hsend, qrecv, wout, st_send, st_recv, row_send, row_recv,
     w_sem, wz_ssem, wz_rsem, wp_ssem, wp_rsem, e_ssem, e_rsem, ag_ssem, ag_rsem,
     st_ssem, st_rsem, row_ssem, row_rsem, c_ssem, c_rsem, q_ssem, q_rsem,
     f_ssem, f_rsem, h_ssem, h_rsem, o_sem) = refs[14:]

    z = lax.axis_index("chan")
    s = lax.axis_index("space")
    cells = rows * wide
    total = cells + 2 * wide
    band = cells // HALVES
    core, chip, chips = s % 2, s // 2, s_count // 2
    before, after = (s + s_count - 1) % s_count, (s + 1) % s_count
    tap_rows = 9 * ch

    barrier = pltpu.get_barrier_semaphore()

    @pl.loop(1, s_count)
    def _(k):
        pl.semaphore_signal(barrier, inc=1, device_id=(z, (s + k) % s_count), device_id_type=MESH)

    @pl.loop(1, n)
    def _(k):
        pl.semaphore_signal(barrier, inc=1, device_id=((z + k) % n, s), device_id_type=MESH)

    w_copies = []
    for which, source in enumerate((w1_hbm, w2_hbm)):
        for d in range(n):
            block = source.at[:, d * ch:(d + 1) * ch] if aligned else source.at[d]
            w_copies.append(pltpu.make_async_copy(block, wv.at[which, d], w_sem.at[which, d]))
    for copy in w_copies:
        copy.start()

    def chunked(fn, init, first=0, count=cells):
        def step(i, carry):
            return fn(pl.multiple_of(first + i * CHUNK, CHUNK), CHUNK, carry)
        return lax.fori_loop(0, count // CHUNK, step, init, unroll=UNROLL)

    cell = lax.broadcasted_iota(jnp.int32, (cells, rows), 0)
    pick = (cell // wide == lax.broadcasted_iota(jnp.int32, (cells, rows), 1)).astype(F32).astype(BF16)
    column_of = lax.broadcasted_iota(jnp.int32, (cells, wide), 0) % wide
    picked = dot(pick, live_in[...].astype(BF16))
    picked = jnp.where(column_of == lax.broadcasted_iota(jnp.int32, (cells, wide), 1), picked, 0.0)
    mask[0:cells, :] = dot(picked.astype(BF16), jnp.ones((wide, ch), BF16))

    def load_main(start, size, carry):
        at = pl.ds(start, size)
        lv = mask[at, :]
        masked[at, :] = x_in[at, :].astype(F32) * lv
        cotm[at, :] = cot_in[at, :].astype(F32) * lv
        return carry

    chunked(load_main, 0)
    for side, start in ((0, 0), (1, cells - wide)):
        edge_send[side, 0] = masked[start:start + wide, :].astype(BF16)
        edge_send[side, 1] = cotm[start:start + wide, :].astype(BF16)
        edge_send[side, 2] = mask[start:start + wide, :].astype(BF16)

    acc[...] = jnp.zeros_like(acc)
    st_send[...] = jnp.zeros_like(st_send)

    pl.semaphore_wait(barrier, s_count - 1 + n - 1)

    def edge_copy(side):
        return pltpu.make_async_remote_copy(
            src_ref=edge_send.at[side], dst_ref=edge_recv.at[1 - side],
            send_sem=e_ssem.at[side], recv_sem=e_rsem.at[1 - side],
            device_id=(z, before if side == 0 else after), device_id_type=MESH)

    for side in range(2):
        edge_copy(side).start()

    w_parts = math.gcd(tap_rows // 16, s_count)
    w_rows = tap_rows // w_parts
    w_mine = s % w_parts
    w_group = s - w_mine

    def wz_copy(which, k):
        at = pl.ds(w_mine * w_rows, w_rows)
        slot = n - k - 1
        return pltpu.make_async_remote_copy(
            src_ref=wv.at[which, (z + k) % n, at, :], dst_ref=wf.at[which, slot, at, :],
            send_sem=wz_ssem.at[which, slot], recv_sem=wz_rsem.at[which, slot],
            device_id=((z + k) % n, s), device_id_type=MESH)

    def wp_copy(which, slot, k, whose):
        at = pl.ds(whose * w_rows, w_rows)
        return pltpu.make_async_remote_copy(
            src_ref=wf.at[which, slot, at, :], dst_ref=wf.at[which, slot, at, :],
            send_sem=wp_ssem.at[which, slot, k], recv_sem=wp_rsem.at[which, slot, whose],
            device_id=(z, w_group + (w_mine + k) % w_parts), device_id_type=MESH)

    def weights_over_z(which):
        for copy in w_copies[which * n:(which + 1) * n]:
            copy.wait()

        @pl.loop(1, n)
        def _(k):
            wz_copy(which, k).start()

    def slot_of(block):
        return (block - z + n - 1) % n

    def weights_round(which):
        @pl.loop(1, n)
        def _(distance):
            for sign in (1, -1):
                block = z - distance * sign

                @pl.when((block >= 0) & (block < n))
                def _():
                    slot = slot_of(block)
                    wz_copy(which, n - 1 - slot).wait_recv()

                    @pl.loop(1, w_parts)
                    def _(k):
                        wp_copy(which, slot, k, w_mine).start()

    def weights_arrived(which, slot):
        @pl.loop(1, w_parts)
        def _(k):
            wp_copy(which, slot, k, (w_mine + k) % w_parts).wait_recv()

    def row_copy(slot, side):
        return pltpu.make_async_remote_copy(
            src_ref=row_send.at[slot, side], dst_ref=row_recv.at[slot, 1 - side],
            send_sem=row_ssem.at[slot, side], recv_sem=row_rsem.at[slot, 1 - side],
            device_id=(z, before if side == 0 else after), device_id_type=MESH)

    def send_rows(slot, ref):
        for side, start in ((0, 0), (1, cells - wide)):
            row_send[slot, side] = ref[start:start + wide, :]
            row_copy(slot, side).start()

    def take_rows(slot, ref):
        for side in range(2):
            row_copy(slot, 1 - side).wait_recv()
            ref[cells + side * wide:cells + (side + 1) * wide, :] = row_recv[slot, side]

    def st_copy(slot, k, whose):
        return pltpu.make_async_remote_copy(
            src_ref=st_send.at[slot], dst_ref=st_recv.at[slot, whose],
            send_sem=st_ssem.at[slot, k], recv_sem=st_rsem.at[slot, whose],
            device_id=(z, (s + k) % s_count), device_id_type=MESH)

    def send_stats(slot, values):
        for i, v in enumerate(values):
            st_send[slot, i:i + 1, :] = v
        for k in range(1, s_count):
            st_copy(slot, k, s).start()
        st_recv[slot, s] = st_send[slot]

    def take_stats(slot):
        for k in range(1, s_count):
            st_copy(slot, k, (s + k) % s_count).wait_recv()

    strip = 8
    column = lax.broadcasted_iota(jnp.int32, (strip * wide, ch), 0) % wide

    def shift(target, first, count):
        size = count * wide
        where = column[:size]
        here = pad[pl.ds(8 + first * wide, size), :]
        left = jnp.where(where == 0, 0.0, pad[pl.ds(7 + first * wide, size), :])
        right = jnp.where(where == wide - 1, 0.0, pad[pl.ds(9 + first * wide, size), :])
        for b, v in enumerate((left, here, right)):
            target[pl.ds(first, count), :, b * ch:(b + 1) * ch] = v.astype(BF16).reshape(count, wide, ch)

    edge = 2 * wide
    ag_rows = ((0, edge + packed), (edge + packed, packed))
    band_rows = rows // HALVES

    def unpack_half(ph, block, q, target):
        if q == 0:
            pad[8:8 + wide, :] = hold[ph, block, 0:wide, :].astype(F32)
            pad[8 + wide + cells:8 + 2 * wide + cells, :] = hold[ph, block, wide:edge, :].astype(F32)
            shift(target, 0, 1)
            shift(target, rows + 1, 1)
        pad[8 + wide + q * band:8 + wide + (q + 1) * band, :] = dot(
            unpack[q], hold[ph, block, edge + q * packed:edge + (q + 1) * packed, :])

        for i in range(band_rows // strip):
            shift(target, 1 + q * band_rows + i * strip, strip)

    def add_conv(q, field, taps):
        first, last = (0, band_rows - 1) if q == 0 else (band_rows - 1, rows)
        count = last - first
        lhs = field[first:last + 2, :, :].reshape((count + 2) * wide, 3 * ch)
        value = dot(lhs, jnp.concatenate([taps(a) for a in range(3)], axis=1))
        at = pl.ds(first * wide, count * wide)
        acc[at, :] = acc[at, :] + sum(
            value[a * wide:(a + count) * wide, a * ch:(a + 1) * ch] for a in range(3))

    def ag_copy(ph, block, q, sign):
        at = pl.ds(*ag_rows[q])
        return pltpu.make_async_remote_copy(
            src_ref=hold.at[ph, block, at, :], dst_ref=hold.at[ph, block, at, :],
            send_sem=ag_ssem.at[ph, (1 - sign) // 2, block, q], recv_sem=ag_rsem.at[ph, block, q],
            device_id=(z + sign, s), device_id_type=MESH)

    def pack_field(ph, source, fill=None, first=None):
        if fill is not None:
            fill(cells, edge, 0)
        hold[ph, z, 0:edge, :] = source[cells:cells + edge, :].astype(BF16)
        for q in range(HALVES):
            if first is not None:
                first(q)
            if fill is not None:
                chunked(fill, 0, q * band, band)
            hold[ph, z, edge + q * packed:edge + (q + 1) * packed, :] = dot(
                pack[q], source[q * band:(q + 1) * band, :].astype(BF16)).astype(BF16)
            for sign in (1, -1):
                @pl.when((z + sign >= 0) & (z + sign < n))
                def _():
                    ag_copy(ph, z, q, sign).start()

    def inside(slice_at):
        return (slice_at >= 0) & (slice_at < n)

    def take_and_pass(ph, k, q, sign, passes=True, takes=True):
        block = z - k * sign

        @pl.when((k > 0) & inside(block))
        def _():
            if passes and takes:
                ag_copy(ph, block, q, sign).wait_recv()

            @pl.when(inside(z + sign))
            def _():
                if passes:
                    if not takes:
                        ag_copy(ph, block, q, sign).wait_recv()
                    ag_copy(ph, block, q, sign).start()

            if not passes:
                @pl.when(jnp.logical_not(inside(z + sign)))
                def _():
                    ag_copy(ph, block, q, sign).wait_recv()

    def consume_both(k, q, consume):
        @pl.loop(0, 2)
        def _(way):
            block = z - k * (1 - 2 * way)

            @pl.when(inside(block) & ((k > 0) | (way == 0)))
            def _():
                consume(k, block, q)

    def gather(ph, consume, each):
        @pl.loop(0, n)
        def _(k):
            for q in range(HALVES):
                for sign in (1, -1):
                    take_and_pass(ph, k, q, sign)
                consume_both(k, q, consume)
            each(k)

    def gather_passing_first(ph, consume, each):
        @pl.loop(0, n)
        def _(k):
            @pl.when(k == 1)
            def _():
                @pl.loop(1, n)
                def _(ahead):
                    for q in range(HALVES):
                        for sign in (1, -1):
                            take_and_pass(ph, ahead, q, sign, takes=False)
            for q in range(HALVES):
                for sign in (1, -1):
                    take_and_pass(ph, k, q, sign, passes=False)
                consume_both(k, q, consume)
            each(k)

    last_pass = jnp.maximum(jnp.where(z < n - 1, z, 0), jnp.where(z > 0, n - 1 - z, 0))

    def forward(ph, field):
        def consume(k, block, q):
            into = taken.at[block]
            unpack_half(ph, block, q, into)

            @pl.when(k == 0)
            def _():
                add_conv(q, into, lambda a: wv[ph, z, 3 * a * ch:3 * (a + 1) * ch, :])

            @pl.when(k > 0)
            def _():
                slot = slot_of(block)
                if q == 0:
                    weights_arrived(ph, slot)
                add_conv(q, into, lambda a: wf[ph, slot, 3 * a * ch:3 * (a + 1) * ch, :])

        def each(k):
            if ph == 0:
                @pl.when(k == 0)
                def _():
                    weights_round(0)

            @pl.when(k == last_pass)
            def _():
                turn_weights(ph)
                turn_field(ph, field)
        (gather if ph else gather_passing_first)(ph, consume, each)

    def turn_field(ph, field):
        for a in range(3):
            for start in range(0, cells, ch):
                first = start + (a - 1) * wide
                if first < 0:
                    v = jnp.concatenate([field[cells:cells + wide, :], field[0:first + ch, :]], axis=0)
                elif first + ch > cells:
                    v = jnp.concatenate([field[first:cells, :], field[cells + wide:total, :]], axis=0)
                else:
                    v = field[first:first + ch, :]
                x_t[ph, a * ch:(a + 1) * ch, start:start + ch] = v.T.astype(BF16)

    def turn_weights(ph):
        @pl.loop(0, n)
        def _(d):
            for t in range(9):
                a, b = 2 - t // 3, 2 - t % 3
                wt[ph, d, a, b * ch:(b + 1) * ch, :] = wv[ph, d, t * ch:(t + 1) * ch, :].T

    half_rows = tap_rows // 2
    owners = math.gcd(half_rows // 16, chips)
    piece = half_rows // owners

    def c_copy(ph, j):
        return pltpu.make_async_remote_copy(
            src_ref=psend.at[ph, j], dst_ref=crecv.at[ph, j],
            send_sem=c_ssem.at[ph, j], recv_sem=c_rsem.at[ph, j],
            device_id=(z, chip * 2 + 1 - core), device_id_type=MESH)

    def q_copy(ph, j, e, whose, owner):
        return pltpu.make_async_remote_copy(
            src_ref=hsend.at[ph, j, owner], dst_ref=qrecv.at[ph, j, whose],
            send_sem=q_ssem.at[ph, j, e], recv_sem=q_rsem.at[ph, j, whose],
            device_id=(z, ((chip + e) % chips) * 2 + core), device_id_type=MESH)

    def f_copy(ph, j, e, owner):
        return pltpu.make_async_remote_copy(
            src_ref=wout.at[ph, j, core, owner], dst_ref=wout.at[ph, j, core, owner],
            send_sem=f_ssem.at[ph, j, e], recv_sem=f_rsem.at[ph, j, owner],
            device_id=(z, ((chip + e) % chips) * 2 + core), device_id_type=MESH)

    def h_copy(ph, j, whose):
        return pltpu.make_async_remote_copy(
            src_ref=wout.at[ph, j, whose], dst_ref=wout.at[ph, j, whose],
            send_sem=h_ssem.at[ph, j], recv_sem=h_rsem.at[ph, j],
            device_id=(z, chip * 2 + 1 - core), device_id_type=MESH)

    def o_copy(ph, j):
        target = (out_wg1, out_wg2)[ph]
        if aligned:
            target = target.at[:, :, :, pl.ds(pl.multiple_of(j * ch, ch), ch)]
        else:
            target = target.at[j]
        return pltpu.make_async_copy(wout.at[ph, j], target, o_sem.at[ph, j])

    def sum_cores(ph, j):
        for o in range(owners):
            psend[ph, j, o] = part[ph, j, 1 - core, o].astype(BF16)
        c_copy(ph, j).start()

    def sum_chips(ph, j):
        c_copy(ph, j).wait_recv()
        for o in range(owners):
            v = part[ph, j, core, o] + crecv[ph, j, o].astype(F32)
            part[ph, j, core, o] = v
            hsend[ph, j, o] = v.astype(BF16)

        @pl.loop(1, chips)
        def _(e):
            peer = (chip + e) % chips

            @pl.when(peer < owners)
            def _():
                q_copy(ph, j, e, chip, peer).start()

    def spread_chips(ph, j):
        @pl.when(chip < owners)
        def _():
            @pl.loop(1, chips)
            def _(e):
                q_copy(ph, j, e, (chip + e) % chips, chip).wait_recv()
            v = part[ph, j, core, chip]
            for e in range(1, chips):
                v = v + qrecv[ph, j, (chip + e) % chips].astype(F32)
            wout[ph, j, core, chip] = v.astype(BF16)

            @pl.loop(1, chips)
            def _(e):
                f_copy(ph, j, e, chip).start()

    def spread_cores(ph, j):
        @pl.loop(1, chips)
        def _(e):
            peer = (chip + e) % chips

            @pl.when(peer < owners)
            def _():
                f_copy(ph, j, e, peer).wait_recv()
        h_copy(ph, j, core).start()

    def finish(ph, j):
        h_copy(ph, j, 1 - core).wait_recv()
        o_copy(ph, j).start()

    def put_part(ph, j, tap, value):
        start = tap * ch
        done = 0
        while done < ch:
            row = start + done
            side, o, at = row // half_rows, row % half_rows // piece, row % piece
            size = min(ch - done, piece - at)
            part[ph, j, side, o, at:at + size, :] = value[done:done + size, :]
            done += size

    stages = (sum_cores, sum_chips, spread_chips, spread_cores, finish)

    def of_step(k, fn):
        @pl.loop(0, 2)
        def _(way):
            block = z - k * (1 - 2 * way)

            @pl.when((k >= 0) & (k < n) & inside(block) & ((k > 0) | (way == 0)))
            def _():
                fn(block)

    passing = last_pass > 0

    def made_at(step):
        first = jnp.where(passing & (step > 0), jnp.where(step == last_pass, 1, step + 1), step)
        return first, step + 1

    def advance(ph, k):
        for age in range(1, len(stages)):
            step = k - age

            @pl.when((step >= 0) & (step < n))
            def _():
                @pl.loop(*made_at(step))
                def _(made):
                    of_step(made, functools.partial(stages[age], ph))

    def advance_all(ph, age):
        @pl.loop(0, n)
        def _(j):
            stages[age](ph, j)

    def field_grad(ph, block):
        grad = taken[block, 1:rows + 1, :, :].reshape(cells, 3 * ch)
        value = dot(x_t[ph], grad)
        for a in range(3):
            for b in range(3):
                put_part(ph, block, 3 * a + b, value[a * ch:(a + 1) * ch, (2 - b) * ch:(3 - b) * ch])

    def make_grad(ph, block):
        field_grad(ph, block)
        sum_cores(ph, block)

    def backward(ph):
        last = ph == 0

        def consume(k, block, q):
            into = taken.at[block]
            unpack_half(2 + ph, block, q, into)
            if last and q == HALVES - 1:
                @pl.when((k == 0) | (k >= last_pass))
                def _():
                    make_grad(ph, block)
            add_conv(q, into, lambda a: wt[ph, block, a])

        def each(k):
            first, end = made_at(k)
            if last:
                @pl.loop(first, end - 1)
                def _(step):
                    of_step(step, functools.partial(make_grad, ph))
                advance(ph, k)
                for age in range(2, len(stages)):
                    @pl.when(k == age - 2)
                    def _():
                        advance_all(1, age)
            else:
                @pl.loop(first, jnp.where(passing | (k < n - 1), end, first))
                def _(step):
                    of_step(step, functools.partial(make_grad, ph))
        gather(2 + ph, consume, each)

    def fold(v):
        return jnp.sum(v.reshape(v.shape[0] // 8, 8, ch), axis=0)

    def flatten(v):
        return jnp.sum(v, axis=0, keepdims=True)

    zero = jnp.zeros((8, ch), F32)

    def local_moments(ref):
        def sums(start, size, carry):
            at = pl.ds(start, size)
            m = mask[at, :]
            return carry[0] + fold(ref[at, :] * m), carry[1] + fold(m)
        added, number = (flatten(v) for v in chunked(sums, (zero, zero)))
        middle = added / jnp.maximum(number, 1.0)

        def spread(start, size, carry):
            at = pl.ds(start, size)
            c = (ref[at, :] - middle) * mask[at, :]
            return carry + fold(c * c)
        return added, number, flatten(chunked(spread, zero))

    def moments(slot):
        take_stats(slot)
        got = [st_recv[slot, k] for k in range(s_count)]
        added = sum(g[0:1] for g in got)
        number = sum(g[1:2] for g in got)
        mean = added / number
        spread = 0.0
        for g in got:
            off = g[0:1] / jnp.maximum(g[1:2], 1.0) - mean
            spread = spread + (g[2:3] + g[1:2] * off * off)
        return mean, lax.rsqrt(spread / number + EPSILON), number

    def everywhere(fn):
        chunked(fn, 0)
        fn(cells, 2 * wide, 0)

    gain1, shift1, gain2, shift2 = (r[...] for r in (gain1_in, shift1_in, gain2_in, shift2_in))

    weights_over_z(0)

    below = lax.broadcasted_iota(jnp.int32, (band, band), 1) < lax.broadcasted_iota(jnp.int32, (band, band), 0)
    below = below.astype(F32).astype(BF16)

    def make_pack(h):
        lv = mask[h * band:(h + 1) * band, :]
        place = jnp.where(lv > 0.0, dot(below, lv.astype(BF16)), -1.0)
        places[h] = place
        across = place.T[0:1, :]
        spot = lax.broadcasted_iota(jnp.int32, (packed, band), 0).astype(F32)
        pack[h] = jnp.where(spot == across, 1.0, 0.0).astype(BF16)

    def make_unpack(h):
        for start in range(0, packed, ch):
            size = min(ch, packed - start)
            spot = start + lax.broadcasted_iota(jnp.int32, (band, size), 1)
            unpack[h, :, start:start + size] = jnp.where(
                places[h, :, :size] == spot.astype(F32), 1.0, 0.0).astype(BF16)

    for side in range(2):
        edge_copy(1 - side).wait_recv()
        there = jnp.where(s > 0, 1.0, 0.0) if side == 0 else jnp.where(s < s_count - 1, 1.0, 0.0)
        at = slice(cells + side * wide, cells + (side + 1) * wide)
        masked[at, :] = edge_recv[side, 0].astype(F32) * there
        cotm[at, :] = edge_recv[side, 1].astype(F32) * there
        mask[at, :] = edge_recv[side, 2].astype(F32) * there

    pack_field(0, masked, first=make_pack)
    for h in range(HALVES):
        make_unpack(h)
    forward(0, masked)
    weights_over_z(1)
    send_rows(0, acc)
    send_stats(0, local_moments(acc))
    mean1, scale1, count = moments(0)
    weights_round(1)

    def activate_one(start, size, carry):
        at = pl.ds(start, size)
        main = start is not cells
        nv = ((acc if main else normed1)[at, :] - mean1) * scale1
        normed1[at, :] = nv
        hid[at, :] = gelu_parts(nv * gain1 + shift1)[0] * mask[at, :]
        if main:
            acc[at, :] = jnp.zeros((size, ch), F32)
        return carry

    def slope_one(start, size, carry):
        at = pl.ds(start, size)
        slope1[at, :] = gelu_parts(normed1[at, :] * gain1 + shift1)[1] * mask[at, :]
        return carry

    take_rows(0, normed1)
    pack_field(1, hid, activate_one)
    everywhere(slope_one)
    forward(1, hid)
    send_rows(1, acc)
    send_stats(1, local_moments(acc))
    mean2, scale2, _ = moments(1)

    def activate_two(source, start, size):
        at = pl.ds(start, size)
        nv = (source[at, :] - mean2) * scale2
        normed2[at, :] = nv
        value, slope = gelu_parts(nv * gain2 + shift2 + masked[at, :])
        t = cotm[at, :] * slope
        through[at, :] = t
        return value, nv, t

    def activate_main(start, size, carry):
        value, nv, t = activate_two(acc, start, size)
        at = pl.ds(start, size)
        out_block[at, :] = (value * mask[at, :]).astype(BF16)
        acc[at, :] = jnp.zeros((size, ch), F32)
        return carry[0] + fold(t * nv), carry[1] + fold(t)

    send_stats(2, [flatten(v) for v in chunked(activate_main, (zero, zero))])
    take_rows(1, normed2)
    activate_two(normed2, cells, edge)

    def gradient_sums(slot):
        take_stats(slot)
        got = [st_recv[slot, k] for k in range(s_count)]
        return sum(g[0:1] for g in got), sum(g[1:2] for g in got)

    def norm_back(upstream, normed, gain, scale, sums):
        gain_grad, shift_grad = sums
        factor = gain * scale
        level, tilt = shift_grad / count, gain_grad / count

        def fill(start, size, carry):
            at = pl.ds(start, size)
            v = upstream[at, :] - mask[at, :] * (level + normed[at, :] * tilt)
            hid[at, :] = factor * v
            return carry
        return fill

    sums2 = gradient_sums(2)
    pack_field(3, hid, norm_back(through, normed2, gain2, scale2, sums2))
    backward(1)

    send_rows(2, acc)

    def inner_main(start, size, carry):
        at = pl.ds(start, size)
        v = acc[at, :] * slope1[at, :]
        slope1[at, :] = v
        acc[at, :] = jnp.zeros((size, ch), F32)
        return carry[0] + fold(v * normed1[at, :]), carry[1] + fold(v)

    send_stats(3, [flatten(v) for v in chunked(inner_main, (zero, zero))])

    @pl.when(jnp.logical_not(passing))
    def _():
        of_step(n - 1, functools.partial(make_grad, 1))
    for side in range(2):
        row_copy(2, 1 - side).wait_recv()
        at = slice(cells + side * wide, cells + (side + 1) * wide)
        slope1[at, :] = row_recv[2, side] * slope1[at, :]
    sums1 = gradient_sums(3)
    pack_field(2, hid, norm_back(slope1, normed1, gain1, scale1, sums1))
    advance_all(1, 1)
    backward(0)
    advance(0, n)

    def finish_input(start, size, carry):
        at = pl.ds(start, size)
        out_input[at, :] = (acc[at, :] + through[at, :]) * mask[at, :]
        return carry

    chunked(finish_input, 0)
    out_sums[0:1, :], out_sums[1:2, :] = sums1
    out_sums[2:3, :], out_sums[3:4, :] = sums2
    out_sums[4:8, :] = jnp.zeros((4, ch), F32)
    for extra in range(1, len(stages) - 1):
        advance(0, n + extra)

    for side in range(2):
        edge_copy(side).wait_send()
        for slot in range(3):
            row_copy(slot, side).wait_send()

    @pl.loop(1, s_count)
    def _(k):
        for slot in range(4):
            st_copy(slot, k, s).wait_send()

    @pl.loop(1, n)
    def _(k):
        for which in range(2):
            wz_copy(which, k).wait_send()

    @pl.loop(1, w_parts)
    def _(k):
        for which in range(2):
            for slot in range(n - 1):
                wp_copy(which, slot, k, w_mine).wait_send()

    @pl.loop(0, n)
    def _(k):
        for sign in (1, -1):
            block = z - k * sign

            @pl.when((block >= 0) & (block < n) & (z + sign >= 0) & (z + sign < n))
            def _():
                for ph in range(4):
                    for q in range(HALVES):
                        ag_copy(ph, block, q, sign).wait_send()

    @pl.loop(0, n)
    def _(j):
        for ph in range(2):
            c_copy(ph, j).wait_send()
            h_copy(ph, j, core).wait_send()
            o_copy(ph, j).wait()

            @pl.loop(1, chips)
            def _(e):
                peer = (chip + e) % chips

                @pl.when(peer < owners)
                def _():
                    q_copy(ph, j, e, chip, peer).wait_send()

                @pl.when(chip < owners)
                def _():
                    f_copy(ph, j, e, chip).wait_send()


def per_device(n, s_count, blocks, weight_one, weight_two, gain_one, shift_one, gain_two, shift_two, cell_live, cotangent):
    rows, wide = cell_live.shape
    ch = blocks.shape[1] // wide
    cells = rows * wide
    total = cells + 2 * wide
    packed = -(-most_live(rows // HALVES, wide) // 16) * 16
    aligned = ch % 128 == 0
    chips = s_count // 2
    tap_rows = 9 * ch
    half_rows = tap_rows // 2
    owners = math.gcd(half_rows // 16, chips)
    piece = half_rows // owners

    def cells_first(flat):
        return flat.reshape(rows, ch, wide).transpose(0, 2, 1).reshape(cells, ch)

    if aligned:
        weight_one, weight_two = (w.reshape(tap_rows, n * ch) for w in (weight_one, weight_two))
    else:
        weight_one, weight_two = (
            w.reshape(tap_rows, n, ch).transpose(1, 0, 2) for w in (weight_one, weight_two))
    grad_shape = (2, owners, piece, n * ch) if aligned else (n, 2, owners, piece, ch)
    vmem = pl.BlockSpec(memory_space=pltpu.VMEM)
    hbm = pl.BlockSpec(memory_space=pl.ANY)
    sem = pltpu.SemaphoreType.DMA
    field = pltpu.VMEM((total, ch), F32)
    scratch = [
        pltpu.VMEM((2, n, tap_rows, ch), BF16),
        pltpu.VMEM((2, n - 1, tap_rows, ch), BF16),
        pltpu.VMEM((2, n, 3, 3 * ch, ch), BF16),
        pltpu.VMEM((2, 3 * ch, cells), BF16),
        pltpu.VMEM((HALVES, packed, cells // HALVES), BF16),
        pltpu.VMEM((HALVES, cells // HALVES, packed), BF16),
        pltpu.VMEM((HALVES, cells // HALVES, ch), F32),
        pltpu.VMEM((2, 3, wide, ch), BF16),
        pltpu.VMEM((2, 3, wide, ch), BF16),
        field, field, field, field, field, field, field, field,
        pltpu.VMEM((total + 16, ch), F32),
        pltpu.VMEM((cells, ch), F32),
        pltpu.VMEM((4, n, 2 * wide + HALVES * packed, ch), BF16),
        pltpu.VMEM((n, rows + 2, wide, 3 * ch), BF16),
        pltpu.VMEM((2, n, 2, owners, piece, ch), F32),
        pltpu.VMEM((2, n, owners, piece, ch), BF16),
        pltpu.VMEM((2, n, owners, piece, ch), BF16),
        pltpu.VMEM((2, n, owners, piece, ch), BF16),
        pltpu.VMEM((2, n, chips, piece, ch), BF16),
        pltpu.VMEM((2, n, 2, owners, piece, ch), BF16),
        pltpu.VMEM((4, 8, ch), F32),
        pltpu.VMEM((4, s_count, 8, ch), F32),
        pltpu.VMEM((3, 2, wide, ch), F32),
        pltpu.VMEM((3, 2, wide, ch), F32),
        sem((2, n)),
        sem((2, n)), sem((2, n)),
        sem((2, n - 1, s_count)), sem((2, n - 1, s_count)),
        sem((2,)), sem((2,)),
        sem((4, 2, n, HALVES)), sem((4, n, HALVES)),
        sem((4, s_count)), sem((4, s_count)),
        sem((3, 2)), sem((3, 2)),
        sem((2, n)), sem((2, n)),
        sem((2, n, chips)), sem((2, n, chips)),
        sem((2, n, chips)), sem((2, n, chips)),
        sem((2, n)), sem((2, n)),
        sem((2, n)),
    ]
    block_out, input_grad, wg1, wg2, sums = pl.pallas_call(
        functools.partial(block_kernel, n, s_count, rows, wide, ch, aligned, packed),
        out_shape=(
            jax.ShapeDtypeStruct((cells, ch), BF16),
            jax.ShapeDtypeStruct((cells, ch), F32),
            jax.ShapeDtypeStruct(grad_shape, BF16),
            jax.ShapeDtypeStruct(grad_shape, BF16),
            jax.ShapeDtypeStruct((8, ch), F32),
        ),
        in_specs=[vmem] * 7 + [hbm] * 2,
        out_specs=(vmem, vmem, hbm, hbm, vmem),
        scratch_shapes=scratch,
        compiler_params=pltpu.CompilerParams(
            collective_id=0, has_side_effects=True, vmem_limit_bytes=60 * 1024 * 1024),
    )(cells_first(blocks), cells_first(cotangent), cell_live,
      *(v.reshape(1, ch) for v in (gain_one, shift_one, gain_two, shift_two)), weight_one, weight_two)

    def flat(grid):
        return grid.reshape(rows, wide, ch).transpose(0, 2, 1).reshape(rows, wide * ch)

    def whole(grad):
        if not aligned:
            grad = grad.reshape(n, tap_rows, ch).transpose(1, 0, 2)
        return grad.astype(F32).reshape(9, ch, n * ch)

    return (flat(block_out), flat(input_grad), whole(wg1), whole(wg2), sums[0], sums[1], sums[2], sums[3])


def solution(mesh):
    return jax.shard_map(
        functools.partial(per_device, mesh.shape["chan"], mesh.shape["space"]),
        mesh=mesh,
        in_specs=(
            P("space", "chan"),
            P(None, "chan", None),
            P(None, "chan", None),
            P("chan"),
            P("chan"),
            P("chan"),
            P("chan"),
            P("space", None),
            P("space", "chan"),
        ),
        out_specs=(
            P("space", "chan"),
            P("space", "chan"),
            P(None, "chan", None),
            P(None, "chan", None),
            P("chan"),
            P("chan"),
            P("chan"),
            P("chan"),
        ),
        check_vma=False,
    )
```

```python
import functools
import math

import jax
import jax.numpy as jnp
from jax import lax
from jax.experimental import pallas as pl
from jax.experimental.pallas import tpu as pltpu
from jax.sharding import PartitionSpec as P

EPSILON = 1e-05
MESH = pl.DeviceIdType.MESH
F32 = jnp.float32
BF16 = jnp.bfloat16
ROOT_HALF = 0.7071067811865476
ROOT_TWO_PI = 0.3989422804014327
CHUNK = 64
UNROLL = 2
HALVES = 2
STREAMS = 4
LARGE, SMALL = 7, 3


def dot(a, b):
    return jnp.dot(a, b, preferred_element_type=F32)


def gelu_parts(v):
    upper = 0.5 * (1.0 + lax.erf(v * ROOT_HALF))
    slope = upper + v * (ROOT_TWO_PI * jnp.exp(-0.5 * v * v))
    return v * upper, slope


def most_live(rows, wide):
    units = (wide + 1) // (SMALL + 1)
    live_rows = rows - rows // (LARGE + 1)
    return min(rows * wide, math.ceil(units * live_rows * LARGE / 2))


def block_kernel(n, s_count, rows, wide, ch, aligned, packed, *refs):
    (x_in, cot_in, live_in, gain1_in, shift1_in, gain2_in, shift2_in, w1_hbm, w2_hbm) = refs[:9]
    (out_block, out_input, out_wg1, out_wg2, out_sums) = refs[9:14]
    (wv, wf, wt, x_t, pack, unpack, places, edge_send, edge_recv, cotm, mask, masked,
     normed1, normed2, through, slope1, hid, pad, acc, hold, taken,
     part, psend, crecv, hsend, qrecv, wout, st_send, st_recv, row_send, row_recv,
     w_sem, wz_ssem, wz_rsem, wp_ssem, wp_rsem, e_ssem, e_rsem, ag_ssem, ag_rsem,
     st_ssem, st_rsem, row_ssem, row_rsem, c_ssem, c_rsem, q_ssem, q_rsem,
     f_ssem, f_rsem, h_ssem, h_rsem, o_sem) = refs[14:]

    z = lax.axis_index("chan")
    s = lax.axis_index("space")
    cells = rows * wide
    total = cells + 2 * wide
    band = cells // HALVES
    core, chip, chips = s % 2, s // 2, s_count // 2
    before, after = (s + s_count - 1) % s_count, (s + 1) % s_count
    tap_rows = 9 * ch

    barrier = pltpu.get_barrier_semaphore()

    @pl.loop(1, s_count)
    def _(k):
        pl.semaphore_signal(barrier, inc=1, device_id=(z, (s + k) % s_count), device_id_type=MESH)

    @pl.loop(1, n)
    def _(k):
        pl.semaphore_signal(barrier, inc=1, device_id=((z + k) % n, s), device_id_type=MESH)

    w_copies = []
    for which, source in enumerate((w1_hbm, w2_hbm)):
        for d in range(n):
            block = source.at[:, d * ch:(d + 1) * ch] if aligned else source.at[d]
            w_copies.append(pltpu.make_async_copy(block, wv.at[which, d], w_sem.at[which, d]))
    for copy in w_copies:
        copy.start()

    def chunked(fn, init, first=0, count=cells):
        def step(i, carry):
            return fn(pl.multiple_of(first + i * CHUNK, CHUNK), CHUNK, carry)
        return lax.fori_loop(0, count // CHUNK, step, init, unroll=UNROLL)

    cell = lax.broadcasted_iota(jnp.int32, (cells, rows), 0)
    pick = (cell // wide == lax.broadcasted_iota(jnp.int32, (cells, rows), 1)).astype(F32).astype(BF16)
    column_of = lax.broadcasted_iota(jnp.int32, (cells, wide), 0) % wide
    picked = dot(pick, live_in[...].astype(BF16))
    picked = jnp.where(column_of == lax.broadcasted_iota(jnp.int32, (cells, wide), 1), picked, 0.0)
    mask[0:cells, :] = dot(picked.astype(BF16), jnp.ones((wide, ch), BF16))

    def load_main(start, size, carry):
        at = pl.ds(start, size)
        lv = mask[at, :]
        masked[at, :] = x_in[at, :].astype(F32) * lv
        cotm[at, :] = cot_in[at, :].astype(F32) * lv
        return carry

    chunked(load_main, 0)
    for side, start in ((0, 0), (1, cells - wide)):
        edge_send[side, 0] = masked[start:start + wide, :].astype(BF16)
        edge_send[side, 1] = cotm[start:start + wide, :].astype(BF16)
        edge_send[side, 2] = mask[start:start + wide, :].astype(BF16)

    acc[...] = jnp.zeros_like(acc)
    st_send[...] = jnp.zeros_like(st_send)

    pl.semaphore_wait(barrier, s_count - 1 + n - 1)

    def edge_copy(side):
        return pltpu.make_async_remote_copy(
            src_ref=edge_send.at[side], dst_ref=edge_recv.at[1 - side],
            send_sem=e_ssem.at[side], recv_sem=e_rsem.at[1 - side],
            device_id=(z, before if side == 0 else after), device_id_type=MESH)

    for side in range(2):
        edge_copy(side).start()

    w_parts = math.gcd(tap_rows // 16, s_count)
    w_rows = tap_rows // w_parts
    w_mine = s % w_parts
    w_group = s - w_mine

    def wz_copy(which, k):
        at = pl.ds(w_mine * w_rows, w_rows)
        slot = n - k - 1
        return pltpu.make_async_remote_copy(
            src_ref=wv.at[which, (z + k) % n, at, :], dst_ref=wf.at[which, slot, at, :],
            send_sem=wz_ssem.at[which, slot], recv_sem=wz_rsem.at[which, slot],
            device_id=((z + k) % n, s), device_id_type=MESH)

    def wp_copy(which, slot, k, whose):
        at = pl.ds(whose * w_rows, w_rows)
        return pltpu.make_async_remote_copy(
            src_ref=wf.at[which, slot, at, :], dst_ref=wf.at[which, slot, at, :],
            send_sem=wp_ssem.at[which, slot, k], recv_sem=wp_rsem.at[which, slot, whose],
            device_id=(z, w_group + (w_mine + k) % w_parts), device_id_type=MESH)

    def weights_over_z(which):
        for copy in w_copies[which * n:(which + 1) * n]:
            copy.wait()

        @pl.loop(1, n)
        def _(k):
            wz_copy(which, k).start()

    def slot_of(block):
        return (block - z + n - 1) % n

    def weights_round(which):
        @pl.loop(1, n)
        def _(distance):
            for sign in (1, -1):
                block = z - distance * sign

                @pl.when((block >= 0) & (block < n))
                def _():
                    slot = slot_of(block)
                    wz_copy(which, n - 1 - slot).wait_recv()

                    @pl.loop(1, w_parts)
                    def _(k):
                        wp_copy(which, slot, k, w_mine).start()

    def weights_arrived(which, slot):
        @pl.loop(1, w_parts)
        def _(k):
            wp_copy(which, slot, k, (w_mine + k) % w_parts).wait_recv()

    def row_copy(slot, side):
        return pltpu.make_async_remote_copy(
            src_ref=row_send.at[slot, side], dst_ref=row_recv.at[slot, 1 - side],
            send_sem=row_ssem.at[slot, side], recv_sem=row_rsem.at[slot, 1 - side],
            device_id=(z, before if side == 0 else after), device_id_type=MESH)

    def send_rows(slot, ref):
        for side, start in ((0, 0), (1, cells - wide)):
            row_send[slot, side] = ref[start:start + wide, :]
            row_copy(slot, side).start()

    def take_rows(slot, ref):
        for side in range(2):
            row_copy(slot, 1 - side).wait_recv()
            ref[cells + side * wide:cells + (side + 1) * wide, :] = row_recv[slot, side]

    def st_copy(slot, k, whose):
        return pltpu.make_async_remote_copy(
            src_ref=st_send.at[slot], dst_ref=st_recv.at[slot, whose],
            send_sem=st_ssem.at[slot, k], recv_sem=st_rsem.at[slot, whose],
            device_id=(z, (s + k) % s_count), device_id_type=MESH)

    def send_stats(slot, values):
        for i, v in enumerate(values):
            st_send[slot, i:i + 1, :] = v
        for k in range(1, s_count):
            st_copy(slot, k, s).start()
        st_recv[slot, s] = st_send[slot]

    def take_stats(slot):
        for k in range(1, s_count):
            st_copy(slot, k, (s + k) % s_count).wait_recv()

    strip = 8
    column = lax.broadcasted_iota(jnp.int32, (strip * wide, ch), 0) % wide

    def shift(target, first, count):
        size = count * wide
        where = column[:size]
        here = pad[pl.ds(8 + first * wide, size), :]
        left = jnp.where(where == 0, 0.0, pad[pl.ds(7 + first * wide, size), :])
        right = jnp.where(where == wide - 1, 0.0, pad[pl.ds(9 + first * wide, size), :])
        for b, v in enumerate((left, here, right)):
            target[pl.ds(first, count), :, b * ch:(b + 1) * ch] = v.astype(BF16).reshape(count, wide, ch)

    edge = 2 * wide
    ag_rows = ((0, edge + packed), (edge + packed, packed))
    band_rows = rows // HALVES

    def unpack_half(ph, block, q, target):
        if q == 0:
            pad[8:8 + wide, :] = hold[ph, block, 0:wide, :].astype(F32)
            pad[8 + wide + cells:8 + 2 * wide + cells, :] = hold[ph, block, wide:edge, :].astype(F32)
            shift(target, 0, 1)
            shift(target, rows + 1, 1)
        pad[8 + wide + q * band:8 + wide + (q + 1) * band, :] = dot(
            unpack[q], hold[ph, block, edge + q * packed:edge + (q + 1) * packed, :])

        for i in range(band_rows // strip):
            shift(target, 1 + q * band_rows + i * strip, strip)

    def add_conv(q, field, taps):
        first, last = (0, band_rows - 1) if q == 0 else (band_rows - 1, rows)
        count = last - first
        lhs = field[first:last + 2, :, :].reshape((count + 2) * wide, 3 * ch)
        value = dot(lhs, jnp.concatenate([taps(a) for a in range(3)], axis=1))
        at = pl.ds(first * wide, count * wide)
        acc[at, :] = acc[at, :] + sum(
            value[a * wide:(a + count) * wide, a * ch:(a + 1) * ch] for a in range(3))

    def ag_start(ph, block, q, sign):
        first, count = ag_rows[q]
        tiles = count // 16
        for i in range(STREAMS):
            low, high = (16 * (tiles * j // STREAMS) for j in (i, i + 1))
            ag_copy(ph, block, q, sign, pl.ds(first + low, high - low)).start()

    def ag_copy(ph, block, q, sign, at=None):
        at = pl.ds(*ag_rows[q]) if at is None else at
        return pltpu.make_async_remote_copy(
            src_ref=hold.at[ph, block, at, :], dst_ref=hold.at[ph, block, at, :],
            send_sem=ag_ssem.at[ph, (1 - sign) // 2, block, q], recv_sem=ag_rsem.at[ph, block, q],
            device_id=(z + sign, s), device_id_type=MESH)

    def pack_field(ph, source, fill=None, first=None):
        if fill is not None:
            fill(cells, edge, 0)
        hold[ph, z, 0:edge, :] = source[cells:cells + edge, :].astype(BF16)
        for q in range(HALVES):
            if first is not None:
                first(q)
            if fill is not None:
                chunked(fill, 0, q * band, band)
            hold[ph, z, edge + q * packed:edge + (q + 1) * packed, :] = dot(
                pack[q], source[q * band:(q + 1) * band, :].astype(BF16)).astype(BF16)
            for sign in (1, -1):
                @pl.when((z + sign >= 0) & (z + sign < n))
                def _():
                    ag_start(ph, z, q, sign)

    def inside(slice_at):
        return (slice_at >= 0) & (slice_at < n)

    def take_and_pass(ph, k, q, sign, passes=True, takes=True):
        block = z - k * sign

        @pl.when((k > 0) & inside(block))
        def _():
            if passes and takes:
                ag_copy(ph, block, q, sign).wait_recv()

            @pl.when(inside(z + sign))
            def _():
                if passes:
                    if not takes:
                        ag_copy(ph, block, q, sign).wait_recv()
                    ag_start(ph, block, q, sign)

            if not passes:
                @pl.when(jnp.logical_not(inside(z + sign)))
                def _():
                    ag_copy(ph, block, q, sign).wait_recv()

    def consume_both(k, q, consume):
        @pl.loop(0, 2)
        def _(way):
            block = z - k * (1 - 2 * way)

            @pl.when(inside(block) & ((k > 0) | (way == 0)))
            def _():
                consume(k, block, q)

    def gather(ph, consume, each):
        @pl.loop(0, n)
        def _(k):
            for q in range(HALVES):
                for sign in (1, -1):
                    take_and_pass(ph, k, q, sign)
                consume_both(k, q, consume)
            each(k)

    def gather_passing_first(ph, consume, each):
        @pl.loop(0, n)
        def _(k):
            @pl.when(k == 1)
            def _():
                @pl.loop(1, n)
                def _(ahead):
                    for q in range(HALVES):
                        for sign in (1, -1):
                            take_and_pass(ph, ahead, q, sign, takes=False)
            for q in range(HALVES):
                for sign in (1, -1):
                    take_and_pass(ph, k, q, sign, passes=False)
                consume_both(k, q, consume)
            each(k)

    last_pass = jnp.maximum(jnp.where(z < n - 1, z, 0), jnp.where(z > 0, n - 1 - z, 0))

    def forward(ph, field):
        def consume(k, block, q):
            into = taken.at[block]
            unpack_half(ph, block, q, into)

            @pl.when(k == 0)
            def _():
                add_conv(q, into, lambda a: wv[ph, z, 3 * a * ch:3 * (a + 1) * ch, :])

            @pl.when(k > 0)
            def _():
                slot = slot_of(block)
                if q == 0:
                    weights_arrived(ph, slot)
                add_conv(q, into, lambda a: wf[ph, slot, 3 * a * ch:3 * (a + 1) * ch, :])

        def each(k):
            if ph == 0:
                @pl.when(k == 0)
                def _():
                    weights_round(0)

            @pl.when(k == last_pass)
            def _():
                turn_weights(ph)
                turn_field(ph, field)
        (gather if ph else gather_passing_first)(ph, consume, each)

    def turn_field(ph, field):
        for a in range(3):
            for start in range(0, cells, ch):
                first = start + (a - 1) * wide
                if first < 0:
                    v = jnp.concatenate([field[cells:cells + wide, :], field[0:first + ch, :]], axis=0)
                elif first + ch > cells:
                    v = jnp.concatenate([field[first:cells, :], field[cells + wide:total, :]], axis=0)
                else:
                    v = field[first:first + ch, :]
                x_t[ph, a * ch:(a + 1) * ch, start:start + ch] = v.T.astype(BF16)

    def turn_weights(ph):
        @pl.loop(0, n)
        def _(d):
            for t in range(9):
                a, b = 2 - t // 3, 2 - t % 3
                wt[ph, d, a, b * ch:(b + 1) * ch, :] = wv[ph, d, t * ch:(t + 1) * ch, :].T

    half_rows = tap_rows // 2
    owners = math.gcd(half_rows // 16, chips)
    piece = half_rows // owners

    def c_copy(ph, j):
        return pltpu.make_async_remote_copy(
            src_ref=psend.at[ph, j], dst_ref=crecv.at[ph, j],
            send_sem=c_ssem.at[ph, j], recv_sem=c_rsem.at[ph, j],
            device_id=(z, chip * 2 + 1 - core), device_id_type=MESH)

    def q_copy(ph, j, e, whose, owner):
        return pltpu.make_async_remote_copy(
            src_ref=hsend.at[ph, j, owner], dst_ref=qrecv.at[ph, j, whose],
            send_sem=q_ssem.at[ph, j, e], recv_sem=q_rsem.at[ph, j, whose],
            device_id=(z, ((chip + e) % chips) * 2 + core), device_id_type=MESH)

    def f_copy(ph, j, e, owner):
        return pltpu.make_async_remote_copy(
            src_ref=wout.at[ph, j, core, owner], dst_ref=wout.at[ph, j, core, owner],
            send_sem=f_ssem.at[ph, j, e], recv_sem=f_rsem.at[ph, j, owner],
            device_id=(z, ((chip + e) % chips) * 2 + core), device_id_type=MESH)

    def h_copy(ph, j, whose):
        return pltpu.make_async_remote_copy(
            src_ref=wout.at[ph, j, whose], dst_ref=wout.at[ph, j, whose],
            send_sem=h_ssem.at[ph, j], recv_sem=h_rsem.at[ph, j],
            device_id=(z, chip * 2 + 1 - core), device_id_type=MESH)

    def o_copy(ph, j):
        target = (out_wg1, out_wg2)[ph]
        if aligned:
            target = target.at[:, :, :, pl.ds(pl.multiple_of(j * ch, ch), ch)]
        else:
            target = target.at[j]
        return pltpu.make_async_copy(wout.at[ph, j], target, o_sem.at[ph, j])

    def sum_cores(ph, j):
        for o in range(owners):
            psend[ph, j, o] = part[ph, j, 1 - core, o].astype(BF16)
        c_copy(ph, j).start()

    def sum_chips(ph, j):
        c_copy(ph, j).wait_recv()
        for o in range(owners):
            v = part[ph, j, core, o] + crecv[ph, j, o].astype(F32)
            part[ph, j, core, o] = v
            hsend[ph, j, o] = v.astype(BF16)

        @pl.loop(1, chips)
        def _(e):
            peer = (chip + e) % chips

            @pl.when(peer < owners)
            def _():
                q_copy(ph, j, e, chip, peer).start()

    def spread_chips(ph, j):
        @pl.when(chip < owners)
        def _():
            @pl.loop(1, chips)
            def _(e):
                q_copy(ph, j, e, (chip + e) % chips, chip).wait_recv()
            v = part[ph, j, core, chip]
            for e in range(1, chips):
                v = v + qrecv[ph, j, (chip + e) % chips].astype(F32)
            wout[ph, j, core, chip] = v.astype(BF16)

            @pl.loop(1, chips)
            def _(e):
                f_copy(ph, j, e, chip).start()

    def spread_cores(ph, j):
        @pl.loop(1, chips)
        def _(e):
            peer = (chip + e) % chips

            @pl.when(peer < owners)
            def _():
                f_copy(ph, j, e, peer).wait_recv()
        h_copy(ph, j, core).start()

    def finish(ph, j):
        h_copy(ph, j, 1 - core).wait_recv()
        o_copy(ph, j).start()

    def put_part(ph, j, tap, value):
        start = tap * ch
        done = 0
        while done < ch:
            row = start + done
            side, o, at = row // half_rows, row % half_rows // piece, row % piece
            size = min(ch - done, piece - at)
            part[ph, j, side, o, at:at + size, :] = value[done:done + size, :]
            done += size

    stages = (sum_cores, sum_chips, spread_chips, spread_cores, finish)

    def of_step(k, fn):
        @pl.loop(0, 2)
        def _(way):
            block = z - k * (1 - 2 * way)

            @pl.when((k >= 0) & (k < n) & inside(block) & ((k > 0) | (way == 0)))
            def _():
                fn(block)

    passing = last_pass > 0

    def made_at(step):
        first = jnp.where(passing & (step > 0), jnp.where(step == last_pass, 1, step + 1), step)
        return first, step + 1

    def advance(ph, k):
        for age in range(1, len(stages)):
            step = k - age

            @pl.when((step >= 0) & (step < n))
            def _():
                @pl.loop(*made_at(step))
                def _(made):
                    of_step(made, functools.partial(stages[age], ph))

    def advance_all(ph, age):
        @pl.loop(0, n)
        def _(j):
            stages[age](ph, j)

    def field_grad(ph, block):
        grad = taken[block, 1:rows + 1, :, :].reshape(cells, 3 * ch)
        value = dot(x_t[ph], grad)
        for a in range(3):
            for b in range(3):
                put_part(ph, block, 3 * a + b, value[a * ch:(a + 1) * ch, (2 - b) * ch:(3 - b) * ch])

    def make_grad(ph, block):
        field_grad(ph, block)
        sum_cores(ph, block)

    def backward(ph):
        last = ph == 0

        def consume(k, block, q):
            into = taken.at[block]
            unpack_half(2 + ph, block, q, into)
            if last and q == HALVES - 1:
                @pl.when((k == 0) | (k >= last_pass))
                def _():
                    make_grad(ph, block)
            add_conv(q, into, lambda a: wt[ph, block, a])

        def each(k):
            first, end = made_at(k)
            if last:
                @pl.loop(first, end - 1)
                def _(step):
                    of_step(step, functools.partial(make_grad, ph))
                advance(ph, k)
                for age in range(2, len(stages)):
                    @pl.when(k == age - 2)
                    def _():
                        advance_all(1, age)
            else:
                @pl.loop(first, jnp.where(passing | (k < n - 1), end, first))
                def _(step):
                    of_step(step, functools.partial(make_grad, ph))
        gather(2 + ph, consume, each)

    def fold(v):
        return jnp.sum(v.reshape(v.shape[0] // 8, 8, ch), axis=0)

    def flatten(v):
        return jnp.sum(v, axis=0, keepdims=True)

    zero = jnp.zeros((8, ch), F32)

    def local_moments(ref):
        def sums(start, size, carry):
            at = pl.ds(start, size)
            m = mask[at, :]
            return carry[0] + fold(ref[at, :] * m), carry[1] + fold(m)
        added, number = (flatten(v) for v in chunked(sums, (zero, zero)))
        middle = added / jnp.maximum(number, 1.0)

        def spread(start, size, carry):
            at = pl.ds(start, size)
            c = (ref[at, :] - middle) * mask[at, :]
            return carry + fold(c * c)
        return added, number, flatten(chunked(spread, zero))

    def moments(slot):
        take_stats(slot)
        got = [st_recv[slot, k] for k in range(s_count)]
        added = sum(g[0:1] for g in got)
        number = sum(g[1:2] for g in got)
        mean = added / number
        spread = 0.0
        for g in got:
            off = g[0:1] / jnp.maximum(g[1:2], 1.0) - mean
            spread = spread + (g[2:3] + g[1:2] * off * off)
        return mean, lax.rsqrt(spread / number + EPSILON), number

    def everywhere(fn):
        chunked(fn, 0)
        fn(cells, 2 * wide, 0)

    gain1, shift1, gain2, shift2 = (r[...] for r in (gain1_in, shift1_in, gain2_in, shift2_in))

    weights_over_z(0)

    below = lax.broadcasted_iota(jnp.int32, (band, band), 1) < lax.broadcasted_iota(jnp.int32, (band, band), 0)
    below = below.astype(F32).astype(BF16)

    def make_pack(h):
        lv = mask[h * band:(h + 1) * band, :]
        place = jnp.where(lv > 0.0, dot(below, lv.astype(BF16)), -1.0)
        places[h] = place
        across = place.T[0:1, :]
        spot = lax.broadcasted_iota(jnp.int32, (packed, band), 0).astype(F32)
        pack[h] = jnp.where(spot == across, 1.0, 0.0).astype(BF16)

    def make_unpack(h):
        for start in range(0, packed, ch):
            size = min(ch, packed - start)
            spot = start + lax.broadcasted_iota(jnp.int32, (band, size), 1)
            unpack[h, :, start:start + size] = jnp.where(
                places[h, :, :size] == spot.astype(F32), 1.0, 0.0).astype(BF16)

    for side in range(2):
        edge_copy(1 - side).wait_recv()
        there = jnp.where(s > 0, 1.0, 0.0) if side == 0 else jnp.where(s < s_count - 1, 1.0, 0.0)
        at = slice(cells + side * wide, cells + (side + 1) * wide)
        masked[at, :] = edge_recv[side, 0].astype(F32) * there
        cotm[at, :] = edge_recv[side, 1].astype(F32) * there
        mask[at, :] = edge_recv[side, 2].astype(F32) * there

    pack_field(0, masked, first=make_pack)
    for h in range(HALVES):
        make_unpack(h)
    forward(0, masked)
    weights_over_z(1)
    send_rows(0, acc)
    send_stats(0, local_moments(acc))
    mean1, scale1, count = moments(0)
    weights_round(1)

    def activate_one(start, size, carry):
        at = pl.ds(start, size)
        main = start is not cells
        nv = ((acc if main else normed1)[at, :] - mean1) * scale1
        normed1[at, :] = nv
        hid[at, :] = gelu_parts(nv * gain1 + shift1)[0] * mask[at, :]
        if main:
            acc[at, :] = jnp.zeros((size, ch), F32)
        return carry

    def slope_one(start, size, carry):
        at = pl.ds(start, size)
        slope1[at, :] = gelu_parts(normed1[at, :] * gain1 + shift1)[1] * mask[at, :]
        return carry

    take_rows(0, normed1)
    pack_field(1, hid, activate_one)
    everywhere(slope_one)
    forward(1, hid)
    send_rows(1, acc)
    send_stats(1, local_moments(acc))
    mean2, scale2, _ = moments(1)

    def activate_two(source, start, size):
        at = pl.ds(start, size)
        nv = (source[at, :] - mean2) * scale2
        normed2[at, :] = nv
        value, slope = gelu_parts(nv * gain2 + shift2 + masked[at, :])
        t = cotm[at, :] * slope
        through[at, :] = t
        return value, nv, t

    def activate_main(start, size, carry):
        value, nv, t = activate_two(acc, start, size)
        at = pl.ds(start, size)
        out_block[at, :] = (value * mask[at, :]).astype(BF16)
        acc[at, :] = jnp.zeros((size, ch), F32)
        return carry[0] + fold(t * nv), carry[1] + fold(t)

    send_stats(2, [flatten(v) for v in chunked(activate_main, (zero, zero))])
    take_rows(1, normed2)
    activate_two(normed2, cells, edge)

    def gradient_sums(slot):
        take_stats(slot)
        got = [st_recv[slot, k] for k in range(s_count)]
        return sum(g[0:1] for g in got), sum(g[1:2] for g in got)

    def norm_back(upstream, normed, gain, scale, sums):
        gain_grad, shift_grad = sums
        factor = gain * scale
        level, tilt = shift_grad / count, gain_grad / count

        def fill(start, size, carry):
            at = pl.ds(start, size)
            v = upstream[at, :] - mask[at, :] * (level + normed[at, :] * tilt)
            hid[at, :] = factor * v
            return carry
        return fill

    sums2 = gradient_sums(2)
    pack_field(3, hid, norm_back(through, normed2, gain2, scale2, sums2))
    backward(1)

    send_rows(2, acc)

    def inner_main(start, size, carry):
        at = pl.ds(start, size)
        v = acc[at, :] * slope1[at, :]
        slope1[at, :] = v
        acc[at, :] = jnp.zeros((size, ch), F32)
        return carry[0] + fold(v * normed1[at, :]), carry[1] + fold(v)

    send_stats(3, [flatten(v) for v in chunked(inner_main, (zero, zero))])

    @pl.when(jnp.logical_not(passing))
    def _():
        of_step(n - 1, functools.partial(make_grad, 1))
    for side in range(2):
        row_copy(2, 1 - side).wait_recv()
        at = slice(cells + side * wide, cells + (side + 1) * wide)
        slope1[at, :] = row_recv[2, side] * slope1[at, :]
    sums1 = gradient_sums(3)
    pack_field(2, hid, norm_back(slope1, normed1, gain1, scale1, sums1))
    advance_all(1, 1)
    backward(0)
    advance(0, n)

    def finish_input(start, size, carry):
        at = pl.ds(start, size)
        out_input[at, :] = (acc[at, :] + through[at, :]) * mask[at, :]
        return carry

    chunked(finish_input, 0)
    out_sums[0:1, :], out_sums[1:2, :] = sums1
    out_sums[2:3, :], out_sums[3:4, :] = sums2
    out_sums[4:8, :] = jnp.zeros((4, ch), F32)
    for extra in range(1, len(stages) - 1):
        advance(0, n + extra)

    for side in range(2):
        edge_copy(side).wait_send()
        for slot in range(3):
            row_copy(slot, side).wait_send()

    @pl.loop(1, s_count)
    def _(k):
        for slot in range(4):
            st_copy(slot, k, s).wait_send()

    @pl.loop(1, n)
    def _(k):
        for which in range(2):
            wz_copy(which, k).wait_send()

    @pl.loop(1, w_parts)
    def _(k):
        for which in range(2):
            for slot in range(n - 1):
                wp_copy(which, slot, k, w_mine).wait_send()

    @pl.loop(0, n)
    def _(k):
        for sign in (1, -1):
            block = z - k * sign

            @pl.when((block >= 0) & (block < n) & (z + sign >= 0) & (z + sign < n))
            def _():
                for ph in range(4):
                    for q in range(HALVES):
                        ag_copy(ph, block, q, sign).wait_send()

    @pl.loop(0, n)
    def _(j):
        for ph in range(2):
            c_copy(ph, j).wait_send()
            h_copy(ph, j, core).wait_send()
            o_copy(ph, j).wait()

            @pl.loop(1, chips)
            def _(e):
                peer = (chip + e) % chips

                @pl.when(peer < owners)
                def _():
                    q_copy(ph, j, e, chip, peer).wait_send()

                @pl.when(chip < owners)
                def _():
                    f_copy(ph, j, e, chip).wait_send()


def per_device(n, s_count, blocks, weight_one, weight_two, gain_one, shift_one, gain_two, shift_two, cell_live, cotangent):
    rows, wide = cell_live.shape
    ch = blocks.shape[1] // wide
    cells = rows * wide
    total = cells + 2 * wide
    packed = -(-most_live(rows // HALVES, wide) // 16) * 16
    aligned = ch % 128 == 0
    chips = s_count // 2
    tap_rows = 9 * ch
    half_rows = tap_rows // 2
    owners = math.gcd(half_rows // 16, chips)
    piece = half_rows // owners

    def cells_first(flat):
        return flat.reshape(rows, ch, wide).transpose(0, 2, 1).reshape(cells, ch)

    if aligned:
        weight_one, weight_two = (w.reshape(tap_rows, n * ch) for w in (weight_one, weight_two))
    else:
        weight_one, weight_two = (
            w.reshape(tap_rows, n, ch).transpose(1, 0, 2) for w in (weight_one, weight_two))
    grad_shape = (2, owners, piece, n * ch) if aligned else (n, 2, owners, piece, ch)
    vmem = pl.BlockSpec(memory_space=pltpu.VMEM)
    hbm = pl.BlockSpec(memory_space=pl.ANY)
    sem = pltpu.SemaphoreType.DMA
    field = pltpu.VMEM((total, ch), F32)
    scratch = [
        pltpu.VMEM((2, n, tap_rows, ch), BF16),
        pltpu.VMEM((2, n - 1, tap_rows, ch), BF16),
        pltpu.VMEM((2, n, 3, 3 * ch, ch), BF16),
        pltpu.VMEM((2, 3 * ch, cells), BF16),
        pltpu.VMEM((HALVES, packed, cells // HALVES), BF16),
        pltpu.VMEM((HALVES, cells // HALVES, packed), BF16),
        pltpu.VMEM((HALVES, cells // HALVES, ch), F32),
        pltpu.VMEM((2, 3, wide, ch), BF16),
        pltpu.VMEM((2, 3, wide, ch), BF16),
        field, field, field, field, field, field, field, field,
        pltpu.VMEM((total + 16, ch), F32),
        pltpu.VMEM((cells, ch), F32),
        pltpu.VMEM((4, n, 2 * wide + HALVES * packed, ch), BF16),
        pltpu.VMEM((n, rows + 2, wide, 3 * ch), BF16),
        pltpu.VMEM((2, n, 2, owners, piece, ch), F32),
        pltpu.VMEM((2, n, owners, piece, ch), BF16),
        pltpu.VMEM((2, n, owners, piece, ch), BF16),
        pltpu.VMEM((2, n, owners, piece, ch), BF16),
        pltpu.VMEM((2, n, chips, piece, ch), BF16),
        pltpu.VMEM((2, n, 2, owners, piece, ch), BF16),
        pltpu.VMEM((4, 8, ch), F32),
        pltpu.VMEM((4, s_count, 8, ch), F32),
        pltpu.VMEM((3, 2, wide, ch), F32),
        pltpu.VMEM((3, 2, wide, ch), F32),
        sem((2, n)),
        sem((2, n)), sem((2, n)),
        sem((2, n - 1, s_count)), sem((2, n - 1, s_count)),
        sem((2,)), sem((2,)),
        sem((4, 2, n, HALVES)), sem((4, n, HALVES)),
        sem((4, s_count)), sem((4, s_count)),
        sem((3, 2)), sem((3, 2)),
        sem((2, n)), sem((2, n)),
        sem((2, n, chips)), sem((2, n, chips)),
        sem((2, n, chips)), sem((2, n, chips)),
        sem((2, n)), sem((2, n)),
        sem((2, n)),
    ]
    block_out, input_grad, wg1, wg2, sums = pl.pallas_call(
        functools.partial(block_kernel, n, s_count, rows, wide, ch, aligned, packed),
        out_shape=(
            jax.ShapeDtypeStruct((cells, ch), BF16),
            jax.ShapeDtypeStruct((cells, ch), F32),
            jax.ShapeDtypeStruct(grad_shape, BF16),
            jax.ShapeDtypeStruct(grad_shape, BF16),
            jax.ShapeDtypeStruct((8, ch), F32),
        ),
        in_specs=[vmem] * 7 + [hbm] * 2,
        out_specs=(vmem, vmem, hbm, hbm, vmem),
        scratch_shapes=scratch,
        compiler_params=pltpu.CompilerParams(
            collective_id=0, has_side_effects=True, vmem_limit_bytes=60 * 1024 * 1024),
    )(cells_first(blocks), cells_first(cotangent), cell_live,
      *(v.reshape(1, ch) for v in (gain_one, shift_one, gain_two, shift_two)), weight_one, weight_two)

    def flat(grid):
        return grid.reshape(rows, wide, ch).transpose(0, 2, 1).reshape(rows, wide * ch)

    def whole(grad):
        if not aligned:
            grad = grad.reshape(n, tap_rows, ch).transpose(1, 0, 2)
        return grad.astype(F32).reshape(9, ch, n * ch)

    return (flat(block_out), flat(input_grad), whole(wg1), whole(wg2), sums[0], sums[1], sums[2], sums[3])


def solution(mesh):
    return jax.shard_map(
        functools.partial(per_device, mesh.shape["chan"], mesh.shape["space"]),
        mesh=mesh,
        in_specs=(
            P("space", "chan"),
            P(None, "chan", None),
            P(None, "chan", None),
            P("chan"),
            P("chan"),
            P("chan"),
            P("chan"),
            P("space", None),
            P("space", "chan"),
        ),
        out_specs=(
            P("space", "chan"),
            P("space", "chan"),
            P(None, "chan", None),
            P(None, "chan", None),
            P("chan"),
            P("chan"),
            P("chan"),
            P("chan"),
        ),
        check_vma=False,
    )
```

```python
import functools
import math

import jax
import jax.numpy as jnp
from jax import lax
from jax.experimental import pallas as pl
from jax.experimental.pallas import tpu as pltpu
from jax.sharding import PartitionSpec as P

EPSILON = 1e-05
MESH = pl.DeviceIdType.MESH
F32 = jnp.float32
BF16 = jnp.bfloat16
ROOT_HALF = 0.7071067811865476
ROOT_TWO_PI = 0.3989422804014327
CHUNK = 64
UNROLL = 2
HALVES = 2
LARGE, SMALL = 7, 3


def dot(a, b):
    return jnp.dot(a, b, preferred_element_type=F32)


def gelu_parts(v):
    upper = 0.5 * (1.0 + lax.erf(v * ROOT_HALF))
    slope = upper + v * (ROOT_TWO_PI * jnp.exp(-0.5 * v * v))
    return v * upper, slope


def most_live(rows, wide):
    units = (wide + 1) // (SMALL + 1)
    live_rows = rows - rows // (LARGE + 1)
    return min(rows * wide, math.ceil(units * live_rows * LARGE / 2))


def block_kernel(n, s_count, rows, wide, ch, aligned, packed, *refs):
    (x_in, cot_in, live_in, gain1_in, shift1_in, gain2_in, shift2_in, w1_hbm, w2_hbm) = refs[:9]
    (out_block, out_input, out_wg1, out_wg2, out_gain1, out_shift1, out_gain2, out_shift2) = refs[9:17]
    (turned, wv, wf, wt, x_t, pack, unpack, places, edge_send, edge_recv, cot_send, cot_recv, cotm, mask, masked,
     normed1, normed2, through, slope1, hid, hid2, pad, acc, hold, taken,
     part, psend, crecv, hsend, qrecv, wout, st_send, st_recv, row_send, row_recv,
     w_sem, wz_ssem, wz_rsem, wp_ssem, wp_rsem, e_ssem, e_rsem, ce_ssem, ce_rsem, ag_ssem, ag_rsem,
     st_ssem, st_rsem, row_ssem, row_rsem, c_ssem, c_rsem, q_ssem, q_rsem,
     f_ssem, f_rsem, h_ssem, h_rsem, o_sem) = refs[17:]

    z = lax.axis_index("chan")
    s = lax.axis_index("space")
    cells = rows * wide
    total = cells + 2 * wide
    band = cells // HALVES
    core, chip, chips = s % 2, s // 2, s_count // 2
    before, after = (s + s_count - 1) % s_count, (s + 1) % s_count
    tap_rows = 9 * ch

    barrier = pltpu.get_barrier_semaphore()

    @pl.loop(1, s_count)
    def _(k):
        pl.semaphore_signal(barrier, inc=1, device_id=(z, (s + k) % s_count), device_id_type=MESH)

    @pl.loop(1, n)
    def _(k):
        pl.semaphore_signal(barrier, inc=1, device_id=((z + k) % n, s), device_id_type=MESH)

    w_copies = []
    for which, source in enumerate((w1_hbm, w2_hbm)):
        for d in range(n):
            block = source.at[:, d * ch:(d + 1) * ch] if aligned else source.at[d]
            w_copies.append(pltpu.make_async_copy(block, wv.at[which, d], w_sem.at[which, d]))
    for copy in w_copies:
        copy.start()

    def chunked(fn, init, first=0, count=cells):
        def step(i, carry):
            return fn(pl.multiple_of(first + i * CHUNK, CHUNK), CHUNK, carry)
        return lax.fori_loop(0, count // CHUNK, step, init, unroll=UNROLL)

    lanes = 128
    tiles = ch * wide // lanes

    def from_flat(flat, put):
        for i in range(tiles):
            turned[i * lanes:(i + 1) * lanes, 0:rows] = flat[:, i * lanes:(i + 1) * lanes].astype(F32).T
        for w in range(wide):
            put(pl.ds(w, rows, stride=wide), turned[pl.ds(w, ch, stride=wide), 0:rows].T)

    def to_flat(source, flat):
        for w in range(wide):
            turned[pl.ds(w, ch, stride=wide), 0:rows] = source[pl.ds(w, rows, stride=wide), :].T
        for i in range(tiles):
            flat[:, i * lanes:(i + 1) * lanes] = turned[i * lanes:(i + 1) * lanes, 0:rows].T.astype(flat.dtype)

    def put_masked(at, value):
        masked[at, :] = value

    from_flat(x_in, put_masked)

    cell = lax.broadcasted_iota(jnp.int32, (cells, rows), 0)
    pick = (cell // wide == lax.broadcasted_iota(jnp.int32, (cells, rows), 1)).astype(F32).astype(BF16)
    column_of = lax.broadcasted_iota(jnp.int32, (cells, wide), 0) % wide
    picked = dot(pick, live_in[...].astype(BF16))
    picked = jnp.where(column_of == lax.broadcasted_iota(jnp.int32, (cells, wide), 1), picked, 0.0)
    mask[0:cells, :] = dot(picked.astype(BF16), jnp.ones((wide, ch), BF16))

    def load_main(start, size, carry):
        at = pl.ds(start, size)
        lv = mask[at, :]
        masked[at, :] = masked[at, :] * lv
        return carry

    chunked(load_main, 0)
    for side, start in ((0, 0), (1, cells - wide)):
        edge_send[side, 0] = masked[start:start + wide, :].astype(BF16)
        edge_send[side, 1] = mask[start:start + wide, :].astype(BF16)

    acc[...] = jnp.zeros_like(acc)
    st_send[...] = jnp.zeros_like(st_send)

    pl.semaphore_wait(barrier, s_count - 1 + n - 1)

    def edge_copy(side):
        return pltpu.make_async_remote_copy(
            src_ref=edge_send.at[side], dst_ref=edge_recv.at[1 - side],
            send_sem=e_ssem.at[side], recv_sem=e_rsem.at[1 - side],
            device_id=(z, before if side == 0 else after), device_id_type=MESH)

    for side in range(2):
        edge_copy(side).start()

    def cot_copy(side):
        return pltpu.make_async_remote_copy(
            src_ref=cot_send.at[side], dst_ref=cot_recv.at[1 - side],
            send_sem=ce_ssem.at[side], recv_sem=ce_rsem.at[1 - side],
            device_id=(z, before if side == 0 else after), device_id_type=MESH)

    def load_cotangent():
        def put(at, value):
            cotm[at, :] = value
        from_flat(cot_in, put)

        def live_only(start, size, carry):
            at = pl.ds(start, size)
            cotm[at, :] = cotm[at, :] * mask[at, :]
            return carry
        chunked(live_only, 0)
        for side, start in ((0, 0), (1, cells - wide)):
            cot_send[side] = cotm[start:start + wide, :].astype(BF16)
            cot_copy(side).start()

    def take_cotangent():
        for side in range(2):
            cot_copy(1 - side).wait_recv()
            at = slice(cells + side * wide, cells + (side + 1) * wide)
            cotm[at, :] = cot_recv[side].astype(F32) * mask[at, :]

    w_parts = math.gcd(tap_rows // 16, s_count)
    w_rows = tap_rows // w_parts
    w_mine = s % w_parts
    w_group = s - w_mine

    def wz_copy(which, k):
        at = pl.ds(w_mine * w_rows, w_rows)
        slot = n - k - 1
        return pltpu.make_async_remote_copy(
            src_ref=wv.at[which, (z + k) % n, at, :], dst_ref=wf.at[which, slot, at, :],
            send_sem=wz_ssem.at[which, slot], recv_sem=wz_rsem.at[which, slot],
            device_id=((z + k) % n, s), device_id_type=MESH)

    def wp_copy(which, slot, k, whose):
        at = pl.ds(whose * w_rows, w_rows)
        return pltpu.make_async_remote_copy(
            src_ref=wf.at[which, slot, at, :], dst_ref=wf.at[which, slot, at, :],
            send_sem=wp_ssem.at[which, slot, k], recv_sem=wp_rsem.at[which, slot, whose],
            device_id=(z, w_group + (w_mine + k) % w_parts), device_id_type=MESH)

    def weights_over_z(which):
        for copy in w_copies[which * n:(which + 1) * n]:
            copy.wait()

        @pl.loop(1, n)
        def _(k):
            wz_copy(which, k).start()

    def slot_of(block):
        return (block - z + n - 1) % n

    def weights_round(which):
        @pl.loop(1, n)
        def _(distance):
            for sign in (1, -1):
                block = z - distance * sign

                @pl.when((block >= 0) & (block < n))
                def _():
                    slot = slot_of(block)
                    wz_copy(which, n - 1 - slot).wait_recv()

                    @pl.loop(1, w_parts)
                    def _(k):
                        wp_copy(which, slot, k, w_mine).start()

    def weights_arrived(which, slot):
        @pl.loop(1, w_parts)
        def _(k):
            wp_copy(which, slot, k, (w_mine + k) % w_parts).wait_recv()

    def row_copy(slot, side):
        return pltpu.make_async_remote_copy(
            src_ref=row_send.at[slot, side], dst_ref=row_recv.at[slot, 1 - side],
            send_sem=row_ssem.at[slot, side], recv_sem=row_rsem.at[slot, 1 - side],
            device_id=(z, before if side == 0 else after), device_id_type=MESH)

    def send_rows(slot, ref):
        for side, start in ((0, 0), (1, cells - wide)):
            row_send[slot, side] = ref[start:start + wide, :]
            row_copy(slot, side).start()

    def take_rows(slot, ref):
        for side in range(2):
            row_copy(slot, 1 - side).wait_recv()
            ref[cells + side * wide:cells + (side + 1) * wide, :] = row_recv[slot, side]

    def st_copy(slot, k, whose):
        return pltpu.make_async_remote_copy(
            src_ref=st_send.at[slot], dst_ref=st_recv.at[slot, whose],
            send_sem=st_ssem.at[slot, k], recv_sem=st_rsem.at[slot, whose],
            device_id=(z, (s + k) % s_count), device_id_type=MESH)

    def send_stats(slot, values):
        for i, v in enumerate(values):
            st_send[slot, i:i + 1, :] = v
        for k in range(1, s_count):
            st_copy(slot, k, s).start()
        st_recv[slot, s] = st_send[slot]

    def take_stats(slot):
        for k in range(1, s_count):
            st_copy(slot, k, (s + k) % s_count).wait_recv()

    strip = 8
    column = lax.broadcasted_iota(jnp.int32, (strip * wide, ch), 0) % wide

    def shift(target, first, count):
        size = count * wide
        where = column[:size]
        here = pad[pl.ds(8 + first * wide, size), :]
        left = jnp.where(where == 0, 0.0, pad[pl.ds(7 + first * wide, size), :])
        right = jnp.where(where == wide - 1, 0.0, pad[pl.ds(9 + first * wide, size), :])
        for b, v in enumerate((left, here, right)):
            target[pl.ds(first, count), :, b * ch:(b + 1) * ch] = v.astype(BF16).reshape(count, wide, ch)

    edge = 2 * wide
    ag_rows = ((0, edge + packed), (edge + packed, packed))
    band_rows = rows // HALVES

    def unpack_half(ph, block, q, target):
        if q == 0:
            pad[8:8 + wide, :] = hold[ph, block, 0:wide, :].astype(F32)
            pad[8 + wide + cells:8 + 2 * wide + cells, :] = hold[ph, block, wide:edge, :].astype(F32)
            shift(target, 0, 1)
            shift(target, rows + 1, 1)
        pad[8 + wide + q * band:8 + wide + (q + 1) * band, :] = dot(
            unpack[q], hold[ph, block, edge + q * packed:edge + (q + 1) * packed, :])

        for i in range(band_rows // strip):
            shift(target, 1 + q * band_rows + i * strip, strip)

    def add_conv(q, field, taps):
        first, last = (0, band_rows - 1) if q == 0 else (band_rows - 1, rows)
        count = last - first
        lhs = field[first:last + 2, :, :].reshape((count + 2) * wide, 3 * ch)
        value = dot(lhs, jnp.concatenate([taps(a) for a in range(3)], axis=1))
        at = pl.ds(first * wide, count * wide)
        acc[at, :] = acc[at, :] + sum(
            value[a * wide:(a + count) * wide, a * ch:(a + 1) * ch] for a in range(3))

    def ag_copy(ph, block, q, sign):
        at = pl.ds(*ag_rows[q])
        return pltpu.make_async_remote_copy(
            src_ref=hold.at[ph, block, at, :], dst_ref=hold.at[ph, block, at, :],
            send_sem=ag_ssem.at[ph, (1 - sign) // 2, block, q], recv_sem=ag_rsem.at[ph, block, q],
            device_id=(z + sign, s), device_id_type=MESH)

    def pack_field(ph, source, fill=None, first=None):
        if fill is not None:
            fill(cells, edge, 0)
        hold[ph, z, 0:edge, :] = source[cells:cells + edge, :].astype(BF16)
        for q in range(HALVES):
            if first is not None:
                first(q)
            if fill is not None:
                chunked(fill, 0, q * band, band)
            hold[ph, z, edge + q * packed:edge + (q + 1) * packed, :] = dot(
                pack[q], source[q * band:(q + 1) * band, :].astype(BF16)).astype(BF16)
            for sign in (1, -1):
                @pl.when((z + sign >= 0) & (z + sign < n))
                def _():
                    ag_copy(ph, z, q, sign).start()

    def inside(slice_at):
        return (slice_at >= 0) & (slice_at < n)

    def take_and_pass(ph, k, q, sign, passes=True, takes=True):
        block = z - k * sign

        @pl.when((k > 0) & inside(block))
        def _():
            if passes and takes:
                ag_copy(ph, block, q, sign).wait_recv()

            @pl.when(inside(z + sign))
            def _():
                if passes:
                    if not takes:
                        ag_copy(ph, block, q, sign).wait_recv()
                    ag_copy(ph, block, q, sign).start()

            if not passes:
                @pl.when(jnp.logical_not(inside(z + sign)))
                def _():
                    ag_copy(ph, block, q, sign).wait_recv()

    near = jnp.where(z < n - n // 2, 1, 0)

    def consume_way(k, q, way, consume):
        block = z - k * (1 - 2 * way)

        @pl.when((k >= 0) & (k < n) & inside(block) & ((k > 0) | (way == near)))
        def _():
            consume(k, block, q)

    def take_both(ph, k, q, **how):
        @pl.loop(0, 2)
        def _(i):
            way = (near + i) % 2
            take_and_pass(ph, k, q, 1 - 2 * way, **how)

    def gather(ph, consume, each):
        @pl.loop(0, n)
        def _(k):
            for q in range(HALVES):
                take_both(ph, k, q)
                if q:
                    consume_way(k, q - 1, 1 - near, consume)
                else:
                    consume_way(k - 1, HALVES - 1, 1 - near, consume)
                consume_way(k, q, near, consume)
            each(k)

    def gather_passing_first(ph, consume, each):
        @pl.loop(0, n)
        def _(k):
            @pl.when(k == 1)
            def _():
                @pl.loop(1, n)
                def _(ahead):
                    for q in range(HALVES):
                        take_both(ph, ahead, q, takes=False)
            for q in range(HALVES):
                take_both(ph, k, q, passes=False)

                @pl.loop(0, 2)
                def _(i):
                    consume_way(k, q, (near + i) % 2, consume)
            each(k)

    last_pass = jnp.maximum(jnp.where(z < n - 1, z, 0), jnp.where(z > 0, n - 1 - z, 0))

    def forward(ph, field):
        def consume(k, block, q):
            into = taken.at[block]
            unpack_half(ph, block, q, into)

            @pl.when(k == 0)
            def _():
                add_conv(q, into, lambda a: wv[ph, z, 3 * a * ch:3 * (a + 1) * ch, :])

            @pl.when(k > 0)
            def _():
                slot = slot_of(block)
                if q == 0:
                    weights_arrived(ph, slot)
                add_conv(q, into, lambda a: wf[ph, slot, 3 * a * ch:3 * (a + 1) * ch, :])

        def each(k):
            if ph == 0:
                @pl.when(k == 0)
                def _():
                    weights_round(0)

            @pl.when(k == last_pass)
            def _():
                turn_weights(ph)
                turn_field(ph, field)
                if ph == 0:
                    load_cotangent()
        (gather if ph else gather_passing_first)(ph, consume, each)

    def turn_field(ph, field):
        for a in range(3):
            for start in range(0, cells, ch):
                first = start + (a - 1) * wide
                if first < 0:
                    v = jnp.concatenate([field[cells:cells + wide, :], field[0:first + ch, :]], axis=0)
                elif first + ch > cells:
                    v = jnp.concatenate([field[first:cells, :], field[cells + wide:total, :]], axis=0)
                else:
                    v = field[first:first + ch, :]
                x_t[ph, a * ch:(a + 1) * ch, start:start + ch] = v.T.astype(BF16)

    def turn_weights(ph):
        @pl.loop(0, n)
        def _(d):
            for t in range(9):
                a, b = 2 - t // 3, 2 - t % 3
                wt[ph, d, a, b * ch:(b + 1) * ch, :] = wv[ph, d, t * ch:(t + 1) * ch, :].T

    half_rows = tap_rows // 2
    owners = math.gcd(half_rows // 16, chips)
    piece = half_rows // owners

    def c_copy(ph, j):
        return pltpu.make_async_remote_copy(
            src_ref=psend.at[ph, j], dst_ref=crecv.at[ph, j],
            send_sem=c_ssem.at[ph, j], recv_sem=c_rsem.at[ph, j],
            device_id=(z, chip * 2 + 1 - core), device_id_type=MESH)

    def q_copy(ph, j, e, whose, owner):
        return pltpu.make_async_remote_copy(
            src_ref=hsend.at[ph, j, owner], dst_ref=qrecv.at[ph, j, whose],
            send_sem=q_ssem.at[ph, j, e], recv_sem=q_rsem.at[ph, j, whose],
            device_id=(z, ((chip + e) % chips) * 2 + core), device_id_type=MESH)

    def f_copy(ph, j, e, owner):
        return pltpu.make_async_remote_copy(
            src_ref=wout.at[ph, j, core, owner], dst_ref=wout.at[ph, j, core, owner],
            send_sem=f_ssem.at[ph, j, e], recv_sem=f_rsem.at[ph, j, owner],
            device_id=(z, ((chip + e) % chips) * 2 + core), device_id_type=MESH)

    def h_copy(ph, j, whose):
        return pltpu.make_async_remote_copy(
            src_ref=wout.at[ph, j, whose], dst_ref=wout.at[ph, j, whose],
            send_sem=h_ssem.at[ph, j], recv_sem=h_rsem.at[ph, j],
            device_id=(z, chip * 2 + 1 - core), device_id_type=MESH)

    def o_copy(ph, j):
        target = (out_wg1, out_wg2)[ph]
        if aligned:
            target = target.at[:, :, :, pl.ds(pl.multiple_of(j * ch, ch), ch)]
        else:
            target = target.at[j]
        return pltpu.make_async_copy(wout.at[ph, j], target, o_sem.at[ph, j])

    def sum_cores(ph, j):
        for o in range(owners):
            psend[ph, j, o] = part[ph, j, 1 - core, o].astype(BF16)
        c_copy(ph, j).start()

    def sum_chips(ph, j):
        c_copy(ph, j).wait_recv()
        for o in range(owners):
            v = part[ph, j, core, o] + crecv[ph, j, o].astype(F32)
            part[ph, j, core, o] = v
            hsend[ph, j, o] = v.astype(BF16)

        @pl.loop(1, chips)
        def _(e):
            peer = (chip + e) % chips

            @pl.when(peer < owners)
            def _():
                q_copy(ph, j, e, chip, peer).start()

    def spread_chips(ph, j):
        @pl.when(chip < owners)
        def _():
            @pl.loop(1, chips)
            def _(e):
                q_copy(ph, j, e, (chip + e) % chips, chip).wait_recv()
            v = part[ph, j, core, chip]
            for e in range(1, chips):
                v = v + qrecv[ph, j, (chip + e) % chips].astype(F32)
            wout[ph, j, core, chip] = v.astype(BF16)

            @pl.loop(1, chips)
            def _(e):
                f_copy(ph, j, e, chip).start()

    def spread_cores(ph, j):
        @pl.loop(1, chips)
        def _(e):
            peer = (chip + e) % chips

            @pl.when(peer < owners)
            def _():
                f_copy(ph, j, e, peer).wait_recv()
        h_copy(ph, j, core).start()

    def finish(ph, j):
        h_copy(ph, j, 1 - core).wait_recv()
        o_copy(ph, j).start()

    def put_part(ph, j, tap, value):
        start = tap * ch
        done = 0
        while done < ch:
            row = start + done
            side, o, at = row // half_rows, row % half_rows // piece, row % piece
            size = min(ch - done, piece - at)
            part[ph, j, side, o, at:at + size, :] = value[done:done + size, :]
            done += size

    stages = (sum_cores, sum_chips, spread_chips, spread_cores, finish)

    def of_step(k, fn):
        @pl.loop(0, 2)
        def _(way):
            block = z - k * (1 - 2 * way)

            @pl.when((k >= 0) & (k < n) & inside(block) & ((k > 0) | (way == 0)))
            def _():
                fn(block)

    passing = last_pass > 0

    def made_at(step):
        first = jnp.where(passing & (step > 0), jnp.where(step == last_pass, 1, step + 1), step)
        return first, step + 1

    def advance(ph, k):
        for age in range(1, len(stages)):
            step = k - age

            @pl.when((step >= 0) & (step < n))
            def _():
                @pl.loop(*made_at(step))
                def _(made):
                    of_step(made, functools.partial(stages[age], ph))

    def advance_all(ph, age):
        @pl.loop(0, n)
        def _(j):
            stages[age](ph, j)

    def field_grad(ph, block):
        grad = taken[block, 1:rows + 1, :, :].reshape(cells, 3 * ch)
        value = dot(x_t[ph], grad)
        for a in range(3):
            for b in range(3):
                put_part(ph, block, 3 * a + b, value[a * ch:(a + 1) * ch, (2 - b) * ch:(3 - b) * ch])

    def make_grad(ph, block):
        field_grad(ph, block)
        sum_cores(ph, block)

    def backward(ph):
        last = ph == 0

        def consume(k, block, q):
            into = taken.at[block]
            unpack_half(2 + ph, block, q, into)
            if last and q == HALVES - 1:
                @pl.when((k == 0) | (k >= last_pass))
                def _():
                    make_grad(ph, block)
            add_conv(q, into, lambda a: wt[ph, block, a])

        def each(k):
            first, end = made_at(k)
            if last:
                @pl.loop(first, end - 1)
                def _(step):
                    of_step(step, functools.partial(make_grad, ph))
                advance(ph, k)
                for age in range(2, len(stages)):
                    @pl.when(k == age - 2)
                    def _():
                        advance_all(1, age)
            else:
                @pl.loop(first, jnp.where(passing | (k < n - 1), end, first))
                def _(step):
                    of_step(step, functools.partial(make_grad, ph))

                @pl.when(k == last_pass)
                def _():
                    to_flat(hid2, out_block)
        gather(2 + ph, consume, each)

    def fold(v):
        return jnp.sum(v.reshape(v.shape[0] // 8, 8, ch), axis=0)

    def flatten(v):
        return jnp.sum(v, axis=0, keepdims=True)

    zero = jnp.zeros((8, ch), F32)

    def local_moments(ref):
        def sums(start, size, carry):
            at = pl.ds(start, size)
            m = mask[at, :]
            return carry[0] + fold(ref[at, :] * m), carry[1] + fold(m)
        added, number = (flatten(v) for v in chunked(sums, (zero, zero)))
        middle = added / jnp.maximum(number, 1.0)

        def spread(start, size, carry):
            at = pl.ds(start, size)
            c = (ref[at, :] - middle) * mask[at, :]
            return carry + fold(c * c)
        return added, number, flatten(chunked(spread, zero))

    def moments(slot):
        take_stats(slot)
        got = [st_recv[slot, k] for k in range(s_count)]
        added = sum(g[0:1] for g in got)
        number = sum(g[1:2] for g in got)
        mean = added / number
        spread = 0.0
        for g in got:
            off = g[0:1] / jnp.maximum(g[1:2], 1.0) - mean
            spread = spread + (g[2:3] + g[1:2] * off * off)
        return mean, lax.rsqrt(spread / number + EPSILON), number

    def everywhere(fn):
        chunked(fn, 0)
        fn(cells, 2 * wide, 0)

    gain1, shift1, gain2, shift2 = (r[...] for r in (gain1_in, shift1_in, gain2_in, shift2_in))

    weights_over_z(0)

    below = lax.broadcasted_iota(jnp.int32, (band, band), 1) < lax.broadcasted_iota(jnp.int32, (band, band), 0)
    below = below.astype(F32).astype(BF16)

    def make_pack(h):
        lv = mask[h * band:(h + 1) * band, :]
        place = jnp.where(lv > 0.0, dot(below, lv.astype(BF16)), -1.0)
        places[h] = place
        across = place.T[0:1, :]
        spot = lax.broadcasted_iota(jnp.int32, (packed, band), 0).astype(F32)
        pack[h] = jnp.where(spot == across, 1.0, 0.0).astype(BF16)

    def make_unpack(h):
        for start in range(0, packed, ch):
            size = min(ch, packed - start)
            spot = start + lax.broadcasted_iota(jnp.int32, (band, size), 1)
            unpack[h, :, start:start + size] = jnp.where(
                places[h, :, :size] == spot.astype(F32), 1.0, 0.0).astype(BF16)

    for side in range(2):
        edge_copy(1 - side).wait_recv()
        there = jnp.where(s > 0, 1.0, 0.0) if side == 0 else jnp.where(s < s_count - 1, 1.0, 0.0)
        at = slice(cells + side * wide, cells + (side + 1) * wide)
        masked[at, :] = edge_recv[side, 0].astype(F32) * there
        mask[at, :] = edge_recv[side, 1].astype(F32) * there

    pack_field(0, masked, first=make_pack)
    for h in range(HALVES):
        make_unpack(h)
    forward(0, masked)
    weights_over_z(1)
    send_rows(0, acc)
    send_stats(0, local_moments(acc))
    mean1, scale1, count = moments(0)
    weights_round(1)

    def activate_one(start, size, carry):
        at = pl.ds(start, size)
        main = start is not cells
        nv = ((acc if main else normed1)[at, :] - mean1) * scale1
        normed1[at, :] = nv
        hid[at, :] = gelu_parts(nv * gain1 + shift1)[0] * mask[at, :]
        if main:
            acc[at, :] = jnp.zeros((size, ch), F32)
        return carry

    def slope_one(start, size, carry):
        at = pl.ds(start, size)
        slope1[at, :] = gelu_parts(normed1[at, :] * gain1 + shift1)[1] * mask[at, :]
        return carry

    take_rows(0, normed1)
    pack_field(1, hid, activate_one)
    everywhere(slope_one)
    forward(1, hid)
    send_rows(1, acc)
    send_stats(1, local_moments(acc))
    mean2, scale2, _ = moments(1)

    def activate_two(source, start, size):
        at = pl.ds(start, size)
        nv = (source[at, :] - mean2) * scale2
        normed2[at, :] = nv
        value, slope = gelu_parts(nv * gain2 + shift2 + masked[at, :])
        t = cotm[at, :] * slope
        through[at, :] = t
        return value, nv, t

    def activate_main(start, size, carry):
        value, nv, t = activate_two(acc, start, size)
        at = pl.ds(start, size)
        hid2[at, :] = value * mask[at, :]
        acc[at, :] = jnp.zeros((size, ch), F32)
        return carry[0] + fold(t * nv), carry[1] + fold(t)

    send_stats(2, [flatten(v) for v in chunked(activate_main, (zero, zero))])
    take_rows(1, normed2)
    take_cotangent()
    activate_two(normed2, cells, edge)

    def gradient_sums(slot):
        take_stats(slot)
        got = [st_recv[slot, k] for k in range(s_count)]
        return sum(g[0:1] for g in got), sum(g[1:2] for g in got)

    def norm_back(upstream, normed, gain, scale, sums):
        gain_grad, shift_grad = sums
        factor = gain * scale
        level, tilt = shift_grad / count, gain_grad / count

        def fill(start, size, carry):
            at = pl.ds(start, size)
            v = upstream[at, :] - mask[at, :] * (level + normed[at, :] * tilt)
            hid[at, :] = factor * v
            return carry
        return fill

    sums2 = gradient_sums(2)
    pack_field(3, hid, norm_back(through, normed2, gain2, scale2, sums2))
    backward(1)

    send_rows(2, acc)

    def inner_main(start, size, carry):
        at = pl.ds(start, size)
        v = acc[at, :] * slope1[at, :]
        slope1[at, :] = v
        acc[at, :] = jnp.zeros((size, ch), F32)
        return carry[0] + fold(v * normed1[at, :]), carry[1] + fold(v)

    send_stats(3, [flatten(v) for v in chunked(inner_main, (zero, zero))])

    @pl.when(jnp.logical_not(passing))
    def _():
        of_step(n - 1, functools.partial(make_grad, 1))
    for side in range(2):
        row_copy(2, 1 - side).wait_recv()
        at = slice(cells + side * wide, cells + (side + 1) * wide)
        slope1[at, :] = row_recv[2, side] * slope1[at, :]
    sums1 = gradient_sums(3)
    pack_field(2, hid, norm_back(slope1, normed1, gain1, scale1, sums1))
    advance_all(1, 1)
    backward(0)
    advance(0, n)

    def finish_input(start, size, carry):
        at = pl.ds(start, size)
        acc[at, :] = (acc[at, :] + through[at, :]) * mask[at, :]
        return carry

    chunked(finish_input, 0)
    to_flat(acc, out_input)
    out_gain1[...], out_shift1[...] = sums1
    out_gain2[...], out_shift2[...] = sums2
    for extra in range(1, len(stages) - 1):
        advance(0, n + extra)

    for side in range(2):
        edge_copy(side).wait_send()
        cot_copy(side).wait_send()
        for slot in range(3):
            row_copy(slot, side).wait_send()

    @pl.loop(1, s_count)
    def _(k):
        for slot in range(4):
            st_copy(slot, k, s).wait_send()

    @pl.loop(1, n)
    def _(k):
        for which in range(2):
            wz_copy(which, k).wait_send()

    @pl.loop(1, w_parts)
    def _(k):
        for which in range(2):
            for slot in range(n - 1):
                wp_copy(which, slot, k, w_mine).wait_send()

    @pl.loop(0, n)
    def _(k):
        for sign in (1, -1):
            block = z - k * sign

            @pl.when((block >= 0) & (block < n) & (z + sign >= 0) & (z + sign < n))
            def _():
                for ph in range(4):
                    for q in range(HALVES):
                        ag_copy(ph, block, q, sign).wait_send()

    @pl.loop(0, n)
    def _(j):
        for ph in range(2):
            c_copy(ph, j).wait_send()
            h_copy(ph, j, core).wait_send()
            o_copy(ph, j).wait()

            @pl.loop(1, chips)
            def _(e):
                peer = (chip + e) % chips

                @pl.when(peer < owners)
                def _():
                    q_copy(ph, j, e, chip, peer).wait_send()

                @pl.when(chip < owners)
                def _():
                    f_copy(ph, j, e, chip).wait_send()


def per_device(n, s_count, blocks, weight_one, weight_two, gain_one, shift_one, gain_two, shift_two, cell_live, cotangent):
    rows, wide = cell_live.shape
    ch = blocks.shape[1] // wide
    cells = rows * wide
    total = cells + 2 * wide
    packed = -(-most_live(rows // HALVES, wide) // 16) * 16
    aligned = ch % 128 == 0
    chips = s_count // 2
    tap_rows = 9 * ch
    half_rows = tap_rows // 2
    owners = math.gcd(half_rows // 16, chips)
    piece = half_rows // owners

    if aligned:
        weight_one, weight_two = (w.reshape(tap_rows, n * ch) for w in (weight_one, weight_two))
    else:
        weight_one, weight_two = (
            w.reshape(tap_rows, n, ch).transpose(1, 0, 2) for w in (weight_one, weight_two))
    grad_shape = (2, owners, piece, n * ch) if aligned else (n, 2, owners, piece, ch)
    vmem = pl.BlockSpec(memory_space=pltpu.VMEM)
    hbm = pl.BlockSpec(memory_space=pl.ANY)
    sem = pltpu.SemaphoreType.DMA
    field = pltpu.VMEM((total, ch), F32)
    scratch = [
        pltpu.VMEM((ch * wide, 128), F32),
        pltpu.VMEM((2, n, tap_rows, ch), BF16),
        pltpu.VMEM((2, n - 1, tap_rows, ch), BF16),
        pltpu.VMEM((2, n, 3, 3 * ch, ch), BF16),
        pltpu.VMEM((2, 3 * ch, cells), BF16),
        pltpu.VMEM((HALVES, packed, cells // HALVES), BF16),
        pltpu.VMEM((HALVES, cells // HALVES, packed), BF16),
        pltpu.VMEM((HALVES, cells // HALVES, ch), F32),
        pltpu.VMEM((2, 2, wide, ch), BF16),
        pltpu.VMEM((2, 2, wide, ch), BF16),
        pltpu.VMEM((2, wide, ch), BF16),
        pltpu.VMEM((2, wide, ch), BF16),
        field, field, field, field, field, field, field, field, field,
        pltpu.VMEM((total + 16, ch), F32),
        pltpu.VMEM((cells, ch), F32),
        pltpu.VMEM((4, n, 2 * wide + HALVES * packed, ch), BF16),
        pltpu.VMEM((n, rows + 2, wide, 3 * ch), BF16),
        pltpu.VMEM((2, n, 2, owners, piece, ch), F32),
        pltpu.VMEM((2, n, owners, piece, ch), BF16),
        pltpu.VMEM((2, n, owners, piece, ch), BF16),
        pltpu.VMEM((2, n, owners, piece, ch), BF16),
        pltpu.VMEM((2, n, chips, piece, ch), BF16),
        pltpu.VMEM((2, n, 2, owners, piece, ch), BF16),
        pltpu.VMEM((4, 8, ch), F32),
        pltpu.VMEM((4, s_count, 8, ch), F32),
        pltpu.VMEM((3, 2, wide, ch), F32),
        pltpu.VMEM((3, 2, wide, ch), F32),
        sem((2, n)),
        sem((2, n)), sem((2, n)),
        sem((2, n - 1, s_count)), sem((2, n - 1, s_count)),
        sem((2,)), sem((2,)),
        sem((2,)), sem((2,)),
        sem((4, 2, n, HALVES)), sem((4, n, HALVES)),
        sem((4, s_count)), sem((4, s_count)),
        sem((3, 2)), sem((3, 2)),
        sem((2, n)), sem((2, n)),
        sem((2, n, chips)), sem((2, n, chips)),
        sem((2, n, chips)), sem((2, n, chips)),
        sem((2, n)), sem((2, n)),
        sem((2, n)),
    ]
    block_out, input_grad, wg1, wg2, *sums = pl.pallas_call(
        functools.partial(block_kernel, n, s_count, rows, wide, ch, aligned, packed),
        out_shape=(
            jax.ShapeDtypeStruct((rows, ch * wide), BF16),
            jax.ShapeDtypeStruct((rows, ch * wide), F32),
            jax.ShapeDtypeStruct(grad_shape, BF16),
            jax.ShapeDtypeStruct(grad_shape, BF16),
            *[jax.ShapeDtypeStruct((1, ch), F32)] * 4,
        ),
        in_specs=[vmem] * 7 + [hbm] * 2,
        out_specs=(vmem, vmem, hbm, hbm, vmem, vmem, vmem, vmem),
        scratch_shapes=scratch,
        compiler_params=pltpu.CompilerParams(
            collective_id=0, has_side_effects=True, vmem_limit_bytes=60 * 1024 * 1024),
    )(blocks, cotangent, cell_live,
      *(v.reshape(1, ch) for v in (gain_one, shift_one, gain_two, shift_two)), weight_one, weight_two)

    def whole(grad):
        if not aligned:
            grad = grad.reshape(n, tap_rows, ch).transpose(1, 0, 2)
        return grad.astype(F32).reshape(9, ch, n * ch)

    return (block_out, input_grad, whole(wg1), whole(wg2), *(v.reshape(ch) for v in sums))


def solution(mesh):
    return jax.shard_map(
        functools.partial(per_device, mesh.shape["chan"], mesh.shape["space"]),
        mesh=mesh,
        in_specs=(
            P("space", "chan"),
            P(None, "chan", None),
            P(None, "chan", None),
            P("chan"),
            P("chan"),
            P("chan"),
            P("chan"),
            P("space", None),
            P("space", "chan"),
        ),
        out_specs=(
            P("space", "chan"),
            P("space", "chan"),
            P(None, "chan", None),
            P(None, "chan", None),
            P("chan"),
            P("chan"),
            P("chan"),
            P("chan"),
        ),
        check_vma=False,
    )
```

```python
import functools
import math

import jax
import jax.numpy as jnp
from jax import lax
from jax.experimental import pallas as pl
from jax.experimental.pallas import tpu as pltpu
from jax.sharding import PartitionSpec as P

EPSILON = 1e-05
MESH = pl.DeviceIdType.MESH
F32 = jnp.float32
BF16 = jnp.bfloat16
ROOT_HALF = 0.7071067811865476
ROOT_TWO_PI = 0.3989422804014327
CHUNK = 64
FINISH_PARTS = 4
UNROLL = 2
HALVES = 2
LARGE, SMALL = 7, 3


def dot(a, b):
    return jnp.dot(a, b, preferred_element_type=F32)


def gelu_parts(v):
    upper = 0.5 * (1.0 + lax.erf(v * ROOT_HALF))
    slope = upper + v * (ROOT_TWO_PI * jnp.exp(-0.5 * v * v))
    return v * upper, slope


def most_live(rows, wide):
    units = (wide + 1) // (SMALL + 1)
    live_rows = rows - rows // (LARGE + 1)
    return min(rows * wide, math.ceil(units * live_rows * LARGE / 2))


def block_kernel(n, s_count, rows, wide, ch, aligned, packed, *refs):
    (x_in, cot_in, live_in, gain1_in, shift1_in, gain2_in, shift2_in, w1_hbm, w2_hbm) = refs[:9]
    (out_block, out_input, out_wg1, out_wg2, out_gain1, out_shift1, out_gain2, out_shift2) = refs[9:17]
    (turned, wv, wf, wt, x_t, pack, unpack, places, edge_send, edge_recv, cot_send, cot_recv, cotm, mask, masked,
     normed1, normed2, through, slope1, hid, hid2, pad, acc, hold, taken,
     part, psend, crecv, hsend, qrecv, wout, st_send, st_recv, row_send, row_recv,
     w_sem, wz_ssem, wz_rsem, wp_ssem, wp_rsem, e_ssem, e_rsem, ce_ssem, ce_rsem, ag_ssem, ag_rsem,
     st_ssem, st_rsem, row_ssem, row_rsem, c_ssem, c_rsem, q_ssem, q_rsem,
     f_ssem, f_rsem, h_ssem, h_rsem, o_sem) = refs[17:]

    z = lax.axis_index("chan")
    s = lax.axis_index("space")
    cells = rows * wide
    total = cells + 2 * wide
    band = cells // HALVES
    core, chip, chips = s % 2, s // 2, s_count // 2
    before, after = (s + s_count - 1) % s_count, (s + 1) % s_count
    tap_rows = 9 * ch

    barrier = pltpu.get_barrier_semaphore()

    @pl.loop(1, s_count)
    def _(k):
        pl.semaphore_signal(barrier, inc=1, device_id=(z, (s + k) % s_count), device_id_type=MESH)

    @pl.loop(1, n)
    def _(k):
        pl.semaphore_signal(barrier, inc=1, device_id=((z + k) % n, s), device_id_type=MESH)

    w_copies = []
    for which, source in enumerate((w1_hbm, w2_hbm)):
        for d in range(n):
            block = source.at[:, d * ch:(d + 1) * ch] if aligned else source.at[d]
            w_copies.append(pltpu.make_async_copy(block, wv.at[which, d], w_sem.at[which, d]))
    for copy in w_copies:
        copy.start()

    def chunked(fn, init, first=0, count=cells):
        def step(i, carry):
            return fn(pl.multiple_of(first + i * CHUNK, CHUNK), CHUNK, carry)
        return lax.fori_loop(0, count // CHUNK, step, init, unroll=UNROLL)

    lanes = 128
    tiles = ch * wide // lanes

    def from_flat(flat, put):
        for i in range(tiles):
            turned[i * lanes:(i + 1) * lanes, 0:rows] = flat[:, i * lanes:(i + 1) * lanes].astype(F32).T
        for w in range(wide):
            put(pl.ds(w, rows, stride=wide), turned[pl.ds(w, ch, stride=wide), 0:rows].T)

    def to_flat(source, flat):
        for w in range(wide):
            turned[pl.ds(w, ch, stride=wide), 0:rows] = source[pl.ds(w, rows, stride=wide), :].T
        for i in range(tiles):
            flat[:, i * lanes:(i + 1) * lanes] = turned[i * lanes:(i + 1) * lanes, 0:rows].T.astype(flat.dtype)

    def put_masked(at, value):
        masked[at, :] = value

    from_flat(x_in, put_masked)

    cell = lax.broadcasted_iota(jnp.int32, (cells, rows), 0)
    pick = (cell // wide == lax.broadcasted_iota(jnp.int32, (cells, rows), 1)).astype(F32).astype(BF16)
    column_of = lax.broadcasted_iota(jnp.int32, (cells, wide), 0) % wide
    picked = lax.dot_general(pick, live_in[...].astype(BF16), (((1,), (1,)), ((), ())), preferred_element_type=F32)
    picked = jnp.where(column_of == lax.broadcasted_iota(jnp.int32, (cells, wide), 1), picked, 0.0)
    mask[0:cells, :] = dot(picked.astype(BF16), jnp.ones((wide, ch), BF16))

    def load_main(start, size, carry):
        at = pl.ds(start, size)
        lv = mask[at, :]
        masked[at, :] = masked[at, :] * lv
        return carry

    chunked(load_main, 0)
    for side, start in ((0, 0), (1, cells - wide)):
        edge_send[side, 0] = masked[start:start + wide, :].astype(BF16)
        edge_send[side, 1] = mask[start:start + wide, :].astype(BF16)

    acc[...] = jnp.zeros_like(acc)
    st_send[...] = jnp.zeros_like(st_send)

    pl.semaphore_wait(barrier, s_count - 1 + n - 1)

    def edge_copy(side):
        return pltpu.make_async_remote_copy(
            src_ref=edge_send.at[side], dst_ref=edge_recv.at[1 - side],
            send_sem=e_ssem.at[side], recv_sem=e_rsem.at[1 - side],
            device_id=(z, before if side == 0 else after), device_id_type=MESH)

    for side in range(2):
        edge_copy(side).start()

    def cot_copy(side):
        return pltpu.make_async_remote_copy(
            src_ref=cot_send.at[side], dst_ref=cot_recv.at[1 - side],
            send_sem=ce_ssem.at[side], recv_sem=ce_rsem.at[1 - side],
            device_id=(z, before if side == 0 else after), device_id_type=MESH)

    def load_cotangent():
        def put(at, value):
            cotm[at, :] = value
        from_flat(cot_in, put)

        def live_only(start, size, carry):
            at = pl.ds(start, size)
            cotm[at, :] = cotm[at, :] * mask[at, :]
            return carry
        chunked(live_only, 0)
        for side, start in ((0, 0), (1, cells - wide)):
            cot_send[side] = cotm[start:start + wide, :].astype(BF16)
            cot_copy(side).start()

    def take_cotangent():
        for side in range(2):
            cot_copy(1 - side).wait_recv()
            at = slice(cells + side * wide, cells + (side + 1) * wide)
            cotm[at, :] = cot_recv[side].astype(F32) * mask[at, :]

    w_parts = math.gcd(tap_rows // 16, s_count)
    w_rows = tap_rows // w_parts
    w_mine = s % w_parts
    w_group = s - w_mine

    def wz_copy(which, k):
        at = pl.ds(w_mine * w_rows, w_rows)
        slot = n - k - 1
        return pltpu.make_async_remote_copy(
            src_ref=wv.at[which, (z + k) % n, at, :], dst_ref=wf.at[which, slot, at, :],
            send_sem=wz_ssem.at[which, slot], recv_sem=wz_rsem.at[which, slot],
            device_id=((z + k) % n, s), device_id_type=MESH)

    def wp_copy(which, slot, k, whose):
        at = pl.ds(whose * w_rows, w_rows)
        return pltpu.make_async_remote_copy(
            src_ref=wf.at[which, slot, at, :], dst_ref=wf.at[which, slot, at, :],
            send_sem=wp_ssem.at[which, slot, k], recv_sem=wp_rsem.at[which, slot, whose],
            device_id=(z, w_group + (w_mine + k) % w_parts), device_id_type=MESH)

    def weights_over_z(which):
        for copy in w_copies[which * n:(which + 1) * n]:
            copy.wait()

        @pl.loop(1, n)
        def _(k):
            wz_copy(which, k).start()

    def slot_of(block):
        return (block - z + n - 1) % n

    def weights_round(which):
        @pl.loop(1, n)
        def _(distance):
            for sign in (1, -1):
                block = z - distance * sign

                @pl.when((block >= 0) & (block < n))
                def _():
                    slot = slot_of(block)
                    wz_copy(which, n - 1 - slot).wait_recv()

                    @pl.loop(1, w_parts)
                    def _(k):
                        wp_copy(which, slot, k, w_mine).start()

    def weights_arrived(which, slot):
        @pl.loop(1, w_parts)
        def _(k):
            wp_copy(which, slot, k, (w_mine + k) % w_parts).wait_recv()

    def row_copy(slot, side):
        return pltpu.make_async_remote_copy(
            src_ref=row_send.at[slot, side], dst_ref=row_recv.at[slot, 1 - side],
            send_sem=row_ssem.at[slot, side], recv_sem=row_rsem.at[slot, 1 - side],
            device_id=(z, before if side == 0 else after), device_id_type=MESH)

    def send_rows(slot, ref):
        for side, start in ((0, 0), (1, cells - wide)):
            row_send[slot, side] = ref[start:start + wide, :]
            row_copy(slot, side).start()

    def take_rows(slot, ref):
        for side in range(2):
            row_copy(slot, 1 - side).wait_recv()
            ref[cells + side * wide:cells + (side + 1) * wide, :] = row_recv[slot, side]

    def st_copy(slot, k, whose):
        return pltpu.make_async_remote_copy(
            src_ref=st_send.at[slot], dst_ref=st_recv.at[slot, whose],
            send_sem=st_ssem.at[slot, k], recv_sem=st_rsem.at[slot, whose],
            device_id=(z, (s + k) % s_count), device_id_type=MESH)

    def send_stats(slot, values):
        for i, v in enumerate(values):
            st_send[slot, i:i + 1, :] = v
        for k in range(1, s_count):
            st_copy(slot, k, s).start()
        st_recv[slot, s] = st_send[slot]

    def take_stats(slot):
        for k in range(1, s_count):
            st_copy(slot, k, (s + k) % s_count).wait_recv()

    strip = 8
    column = lax.broadcasted_iota(jnp.int32, (strip * wide, ch), 0) % wide

    def shift(target, first, count):
        size = count * wide
        where = column[:size]
        here = pad[pl.ds(8 + first * wide, size), :]
        left = jnp.where(where == 0, 0.0, pad[pl.ds(7 + first * wide, size), :])
        right = jnp.where(where == wide - 1, 0.0, pad[pl.ds(9 + first * wide, size), :])
        for b, v in enumerate((left, here, right)):
            target[pl.ds(first, count), :, b * ch:(b + 1) * ch] = v.astype(BF16).reshape(count, wide, ch)

    edge = 2 * wide
    ag_rows = ((0, edge + packed), (edge + packed, packed))
    band_rows = rows // HALVES

    def unpack_half(ph, block, q, target):
        if q == 0:
            pad[8:8 + wide, :] = hold[ph, block, 0:wide, :].astype(F32)
            pad[8 + wide + cells:8 + 2 * wide + cells, :] = hold[ph, block, wide:edge, :].astype(F32)
            shift(target, 0, 1)
            shift(target, rows + 1, 1)
        pad[8 + wide + q * band:8 + wide + (q + 1) * band, :] = dot(
            unpack[q], hold[ph, block, edge + q * packed:edge + (q + 1) * packed, :])

        for i in range(band_rows // strip):
            shift(target, 1 + q * band_rows + i * strip, strip)

    def add_conv(q, field, taps):
        first, last = (0, band_rows - 1) if q == 0 else (band_rows - 1, rows)
        count = last - first
        lhs = field[first:last + 2, :, :].reshape((count + 2) * wide, 3 * ch)
        value = dot(lhs, jnp.concatenate([taps(a) for a in range(3)], axis=1))
        at = pl.ds(first * wide, count * wide)
        acc[at, :] = acc[at, :] + sum(
            value[a * wide:(a + count) * wide, a * ch:(a + 1) * ch] for a in range(3))

    def ag_copy(ph, block, q, sign):
        at = pl.ds(*ag_rows[q])
        return pltpu.make_async_remote_copy(
            src_ref=hold.at[ph, block, at, :], dst_ref=hold.at[ph, block, at, :],
            send_sem=ag_ssem.at[ph, (1 - sign) // 2, block, q], recv_sem=ag_rsem.at[ph, block, q],
            device_id=(z + sign, s), device_id_type=MESH)

    def pack_field(ph, source, fill=None, first=None):
        if fill is not None:
            fill(cells, edge, 0)
        hold[ph, z, 0:edge, :] = source[cells:cells + edge, :].astype(BF16)
        for q in range(HALVES):
            if first is not None:
                first(q)
            if fill is not None:
                chunked(fill, 0, q * band, band)
            hold[ph, z, edge + q * packed:edge + (q + 1) * packed, :] = dot(
                pack[q], source[q * band:(q + 1) * band, :].astype(BF16)).astype(BF16)
            for sign in (1, -1):
                @pl.when((z + sign >= 0) & (z + sign < n))
                def _():
                    ag_copy(ph, z, q, sign).start()

    def inside(slice_at):
        return (slice_at >= 0) & (slice_at < n)

    def take_and_pass(ph, k, q, sign, passes=True, takes=True):
        block = z - k * sign

        @pl.when((k > 0) & inside(block))
        def _():
            if passes and takes:
                ag_copy(ph, block, q, sign).wait_recv()

            @pl.when(inside(z + sign))
            def _():
                if passes:
                    if not takes:
                        ag_copy(ph, block, q, sign).wait_recv()
                    ag_copy(ph, block, q, sign).start()

            if not passes:
                @pl.when(jnp.logical_not(inside(z + sign)))
                def _():
                    ag_copy(ph, block, q, sign).wait_recv()

    near = jnp.where(z < n - n // 2, 1, 0)

    def consume_way(k, q, way, consume):
        block = z - k * (1 - 2 * way)

        @pl.when((k >= 0) & (k < n) & inside(block) & ((k > 0) | (way == near)))
        def _():
            consume(k, block, q)

    def take_both(ph, k, q, **how):
        @pl.loop(0, 2)
        def _(i):
            way = (near + i) % 2
            take_and_pass(ph, k, q, 1 - 2 * way, **how)

    def gather(ph, consume, each):
        @pl.loop(0, n)
        def _(k):
            for q in range(HALVES):
                take_both(ph, k, q)
                if q:
                    consume_way(k, q - 1, 1 - near, consume)
                else:
                    consume_way(k - 1, HALVES - 1, 1 - near, consume)
                consume_way(k, q, near, consume)
            each(k)

    def gather_passing_first(ph, consume, each):
        @pl.loop(0, n)
        def _(k):
            @pl.when(k == 1)
            def _():
                @pl.loop(1, n)
                def _(ahead):
                    for q in range(HALVES):
                        take_both(ph, ahead, q, takes=False)
            for q in range(HALVES):
                take_both(ph, k, q, passes=False)

                @pl.loop(0, 2)
                def _(i):
                    consume_way(k, q, (near + i) % 2, consume)
            each(k)

    last_pass = jnp.maximum(jnp.where(z < n - 1, z, 0), jnp.where(z > 0, n - 1 - z, 0))

    def forward(ph, field):
        def consume(k, block, q):
            into = taken.at[block]
            unpack_half(ph, block, q, into)

            @pl.when(k == 0)
            def _():
                add_conv(q, into, lambda a: wv[ph, z, 3 * a * ch:3 * (a + 1) * ch, :])

            @pl.when(k > 0)
            def _():
                slot = slot_of(block)
                if q == 0:
                    weights_arrived(ph, slot)
                add_conv(q, into, lambda a: wf[ph, slot, 3 * a * ch:3 * (a + 1) * ch, :])

        def each(k):
            if ph == 0:
                @pl.when(k == 0)
                def _():
                    weights_round(0)

            @pl.when(k == last_pass)
            def _():
                turn_weights(ph)
                turn_field(ph, field)
                if ph == 0:
                    load_cotangent()
        (gather if ph else gather_passing_first)(ph, consume, each)

    def turn_field(ph, field):
        for a in range(3):
            for start in range(0, cells, ch):
                first = start + (a - 1) * wide
                if first < 0:
                    v = jnp.concatenate([field[cells:cells + wide, :], field[0:first + ch, :]], axis=0)
                elif first + ch > cells:
                    v = jnp.concatenate([field[first:cells, :], field[cells + wide:total, :]], axis=0)
                else:
                    v = field[first:first + ch, :]
                x_t[ph, a * ch:(a + 1) * ch, start:start + ch] = v.T.astype(BF16)

    def turn_weights(ph):
        @pl.loop(0, n)
        def _(d):
            for t in range(9):
                a, b = 2 - t // 3, 2 - t % 3
                wt[ph, d, a, b * ch:(b + 1) * ch, :] = wv[ph, d, t * ch:(t + 1) * ch, :].T

    half_rows = tap_rows // 2
    owners = math.gcd(half_rows // 16, chips)
    piece = half_rows // owners

    def c_copy(ph, j):
        return pltpu.make_async_remote_copy(
            src_ref=psend.at[ph, j], dst_ref=crecv.at[ph, j],
            send_sem=c_ssem.at[ph, j], recv_sem=c_rsem.at[ph, j],
            device_id=(z, chip * 2 + 1 - core), device_id_type=MESH)

    def q_copy(ph, j, e, whose, owner):
        return pltpu.make_async_remote_copy(
            src_ref=hsend.at[ph, j, owner], dst_ref=qrecv.at[ph, j, whose],
            send_sem=q_ssem.at[ph, j, e], recv_sem=q_rsem.at[ph, j, whose],
            device_id=(z, ((chip + e) % chips) * 2 + core), device_id_type=MESH)

    def f_copy(ph, j, e, owner):
        return pltpu.make_async_remote_copy(
            src_ref=wout.at[ph, j, core, owner], dst_ref=wout.at[ph, j, core, owner],
            send_sem=f_ssem.at[ph, j, e], recv_sem=f_rsem.at[ph, j, owner],
            device_id=(z, ((chip + e) % chips) * 2 + core), device_id_type=MESH)

    def h_copy(ph, j, whose):
        return pltpu.make_async_remote_copy(
            src_ref=wout.at[ph, j, whose], dst_ref=wout.at[ph, j, whose],
            send_sem=h_ssem.at[ph, j], recv_sem=h_rsem.at[ph, j],
            device_id=(z, chip * 2 + 1 - core), device_id_type=MESH)

    def o_copy(ph, j):
        target = (out_wg1, out_wg2)[ph]
        if aligned:
            target = target.at[:, :, :, pl.ds(pl.multiple_of(j * ch, ch), ch)]
        else:
            target = target.at[j]
        return pltpu.make_async_copy(wout.at[ph, j], target, o_sem.at[ph, j])

    def sum_cores(ph, j):
        for o in range(owners):
            psend[ph, j, o] = part[ph, j, 1 - core, o].astype(BF16)
        c_copy(ph, j).start()

    def sum_chips(ph, j):
        c_copy(ph, j).wait_recv()
        for o in range(owners):
            v = part[ph, j, core, o] + crecv[ph, j, o].astype(F32)
            part[ph, j, core, o] = v
            hsend[ph, j, o] = v.astype(BF16)

        @pl.loop(1, chips)
        def _(e):
            peer = (chip + e) % chips

            @pl.when(peer < owners)
            def _():
                q_copy(ph, j, e, chip, peer).start()

    def spread_chips(ph, j):
        @pl.when(chip < owners)
        def _():
            @pl.loop(1, chips)
            def _(e):
                q_copy(ph, j, e, (chip + e) % chips, chip).wait_recv()
            v = part[ph, j, core, chip]
            for e in range(1, chips):
                v = v + qrecv[ph, j, (chip + e) % chips].astype(F32)
            wout[ph, j, core, chip] = v.astype(BF16)

            @pl.loop(1, chips)
            def _(e):
                f_copy(ph, j, e, chip).start()

    def spread_cores(ph, j):
        @pl.loop(1, chips)
        def _(e):
            peer = (chip + e) % chips

            @pl.when(peer < owners)
            def _():
                f_copy(ph, j, e, peer).wait_recv()
        h_copy(ph, j, core).start()

    def finish(ph, j):
        h_copy(ph, j, 1 - core).wait_recv()
        o_copy(ph, j).start()

    def put_part(ph, j, tap, value):
        start = tap * ch
        done = 0
        while done < ch:
            row = start + done
            side, o, at = row // half_rows, row % half_rows // piece, row % piece
            size = min(ch - done, piece - at)
            part[ph, j, side, o, at:at + size, :] = value[done:done + size, :]
            done += size

    stages = (sum_cores, sum_chips, spread_chips, spread_cores, finish)

    def of_step(k, fn):
        @pl.loop(0, 2)
        def _(way):
            block = z - k * (1 - 2 * way)

            @pl.when((k >= 0) & (k < n) & inside(block) & ((k > 0) | (way == 0)))
            def _():
                fn(block)

    passing = last_pass > 0

    def made_at(step):
        first = jnp.where(passing & (step > 0), jnp.where(step == last_pass, 1, step + 1), step)
        return first, step + 1

    def advance(ph, k):
        for age in range(1, len(stages)):
            step = k - age

            @pl.when((step >= 0) & (step < n))
            def _():
                @pl.loop(*made_at(step))
                def _(made):
                    of_step(made, functools.partial(stages[age], ph))

    def advance_all(ph, age):
        @pl.loop(0, n)
        def _(j):
            stages[age](ph, j)

    def field_grad(ph, block):
        grad = taken[block, 1:rows + 1, :, :].reshape(cells, 3 * ch)
        value = dot(x_t[ph], grad)
        for a in range(3):
            for b in range(3):
                put_part(ph, block, 3 * a + b, value[a * ch:(a + 1) * ch, (2 - b) * ch:(3 - b) * ch])

    def make_grad(ph, block):
        field_grad(ph, block)
        sum_cores(ph, block)

    def backward(ph):
        last = ph == 0

        def consume(k, block, q):
            into = taken.at[block]
            unpack_half(2 + ph, block, q, into)
            if last and q == HALVES - 1:
                @pl.when((k == 0) | (k >= last_pass))
                def _():
                    make_grad(ph, block)
            add_conv(q, into, lambda a: wt[ph, block, a])

        def each(k):
            first, end = made_at(k)
            if last:
                @pl.loop(first, end - 1)
                def _(step):
                    of_step(step, functools.partial(make_grad, ph))
                advance(ph, k)
                for age in range(2, len(stages)):
                    @pl.when(k == age - 2)
                    def _():
                        advance_all(1, age)
            else:
                @pl.loop(first, jnp.where(passing | (k < n - 1), end, first))
                def _(step):
                    of_step(step, functools.partial(make_grad, ph))

                @pl.when(k == last_pass)
                def _():
                    to_flat(hid2, out_block)
        gather(2 + ph, consume, each)

    def fold(v):
        return jnp.sum(v.reshape(v.shape[0] // 8, 8, ch), axis=0)

    def flatten(v):
        return jnp.sum(v, axis=0, keepdims=True)

    zero = jnp.zeros((8, ch), F32)

    def local_moments(ref):
        def sums(start, size, carry):
            at = pl.ds(start, size)
            m = mask[at, :]
            return carry[0] + fold(ref[at, :] * m), carry[1] + fold(m)
        added, number = (flatten(v) for v in chunked(sums, (zero, zero)))
        middle = added / jnp.maximum(number, 1.0)

        def spread(start, size, carry):
            at = pl.ds(start, size)
            c = (ref[at, :] - middle) * mask[at, :]
            return carry + fold(c * c)
        return added, number, flatten(chunked(spread, zero))

    def moments(slot):
        take_stats(slot)
        got = [st_recv[slot, k] for k in range(s_count)]
        added = sum(g[0:1] for g in got)
        number = sum(g[1:2] for g in got)
        mean = added / number
        spread = 0.0
        for g in got:
            off = g[0:1] / jnp.maximum(g[1:2], 1.0) - mean
            spread = spread + (g[2:3] + g[1:2] * off * off)
        return mean, lax.rsqrt(spread / number + EPSILON), number

    def everywhere(fn):
        chunked(fn, 0)
        fn(cells, 2 * wide, 0)

    gain1, shift1, gain2, shift2 = (r[...] for r in (gain1_in, shift1_in, gain2_in, shift2_in))

    weights_over_z(0)

    below = lax.broadcasted_iota(jnp.int32, (band, band), 1) < lax.broadcasted_iota(jnp.int32, (band, band), 0)
    below = below.astype(F32).astype(BF16)

    def make_pack(h):
        lv = mask[h * band:(h + 1) * band, :]
        place = jnp.where(lv > 0.0, dot(below, lv.astype(BF16)), -1.0)
        places[h] = place
        across = place.T[0:1, :]
        spot = lax.broadcasted_iota(jnp.int32, (packed, band), 0).astype(F32)
        pack[h] = jnp.where(spot == across, 1.0, 0.0).astype(BF16)

    def make_unpack(h):
        for start in range(0, packed, ch):
            size = min(ch, packed - start)
            spot = start + lax.broadcasted_iota(jnp.int32, (band, size), 1)
            unpack[h, :, start:start + size] = jnp.where(
                places[h, :, :size] == spot.astype(F32), 1.0, 0.0).astype(BF16)

    for side in range(2):
        edge_copy(1 - side).wait_recv()
        there = jnp.where(s > 0, 1.0, 0.0) if side == 0 else jnp.where(s < s_count - 1, 1.0, 0.0)
        at = slice(cells + side * wide, cells + (side + 1) * wide)
        masked[at, :] = edge_recv[side, 0].astype(F32) * there
        mask[at, :] = edge_recv[side, 1].astype(F32) * there

    with jax.named_scope("pack_input"):
        pack_field(0, masked, first=make_pack)
        for h in range(HALVES):
            make_unpack(h)
    with jax.named_scope("first_conv"):
        forward(0, masked)
    weights_over_z(1)
    with jax.named_scope("first_moments"):
        send_rows(0, acc)
        send_stats(0, local_moments(acc))
        mean1, scale1, count = moments(0)
    weights_round(1)

    def activate_one(start, size, carry):
        at = pl.ds(start, size)
        main = start is not cells
        nv = ((acc if main else normed1)[at, :] - mean1) * scale1
        normed1[at, :] = nv
        hid[at, :] = gelu_parts(nv * gain1 + shift1)[0] * mask[at, :]
        if main:
            acc[at, :] = jnp.zeros((size, ch), F32)
        return carry

    def slope_one(start, size, carry):
        at = pl.ds(start, size)
        slope1[at, :] = gelu_parts(normed1[at, :] * gain1 + shift1)[1] * mask[at, :]
        return carry

    with jax.named_scope("activate"):
        take_rows(0, normed1)
        pack_field(1, hid, activate_one)
        everywhere(slope_one)
    with jax.named_scope("second_conv"):
        forward(1, hid)
    with jax.named_scope("second_moments"):
        send_rows(1, acc)
        send_stats(1, local_moments(acc))
        mean2, scale2, _ = moments(1)

    def activate_two(source, start, size):
        at = pl.ds(start, size)
        nv = (source[at, :] - mean2) * scale2
        normed2[at, :] = nv
        value, slope = gelu_parts(nv * gain2 + shift2 + masked[at, :])
        t = cotm[at, :] * slope
        through[at, :] = t
        return value, nv, t

    def activate_main(start, size, carry):
        value, nv, t = activate_two(acc, start, size)
        at = pl.ds(start, size)
        hid2[at, :] = value * mask[at, :]
        acc[at, :] = jnp.zeros((size, ch), F32)
        return carry[0] + fold(t * nv), carry[1] + fold(t)

    with jax.named_scope("activate_output"):
        send_stats(2, [flatten(v) for v in chunked(activate_main, (zero, zero))])
        take_rows(1, normed2)
        take_cotangent()
        activate_two(normed2, cells, edge)

    def gradient_sums(slot):
        take_stats(slot)
        got = [st_recv[slot, k] for k in range(s_count)]
        return sum(g[0:1] for g in got), sum(g[1:2] for g in got)

    def norm_back(upstream, normed, gain, scale, sums):
        gain_grad, shift_grad = sums
        factor = gain * scale
        level, tilt = shift_grad / count, gain_grad / count

        def fill(start, size, carry):
            at = pl.ds(start, size)
            v = upstream[at, :] - mask[at, :] * (level + normed[at, :] * tilt)
            hid[at, :] = factor * v
            return carry
        return fill

    with jax.named_scope("second_sums"):
        sums2 = gradient_sums(2)
    with jax.named_scope("second_norm_back"):
        pack_field(3, hid, norm_back(through, normed2, gain2, scale2, sums2))
    with jax.named_scope("second_conv_back"):
        backward(1)

    send_rows(2, acc)

    def inner_main(start, size, carry):
        at = pl.ds(start, size)
        v = acc[at, :] * slope1[at, :]
        slope1[at, :] = v
        acc[at, :] = jnp.zeros((size, ch), F32)
        return carry[0] + fold(v * normed1[at, :]), carry[1] + fold(v)

    send_stats(3, [flatten(v) for v in chunked(inner_main, (zero, zero))])

    @pl.when(jnp.logical_not(passing))
    def _():
        of_step(n - 1, functools.partial(make_grad, 1))
    for side in range(2):
        row_copy(2, 1 - side).wait_recv()
        at = slice(cells + side * wide, cells + (side + 1) * wide)
        slope1[at, :] = row_recv[2, side] * slope1[at, :]
    with jax.named_scope("first_sums"):
        sums1 = gradient_sums(3)
    with jax.named_scope("first_norm_back"):
        pack_field(2, hid, norm_back(slope1, normed1, gain1, scale1, sums1))
    advance_all(1, 1)
    with jax.named_scope("first_conv_back"):
        backward(0)
    advance(0, n)

    def finish_input(start, size, carry):
        at = pl.ds(start, size)
        acc[at, :] = (acc[at, :] + through[at, :]) * mask[at, :]
        return carry

    chunked(finish_input, 0)
    to_flat(acc, out_input)
    out_gain1[...], out_shift1[...] = sums1
    out_gain2[...], out_shift2[...] = sums2
    for extra in range(1, len(stages) - 1):
        advance(0, n + extra)

    for side in range(2):
        edge_copy(side).wait_send()
        cot_copy(side).wait_send()
        for slot in range(3):
            row_copy(slot, side).wait_send()

    @pl.loop(1, s_count)
    def _(k):
        for slot in range(4):
            st_copy(slot, k, s).wait_send()

    @pl.loop(1, n)
    def _(k):
        for which in range(2):
            wz_copy(which, k).wait_send()

    @pl.loop(1, w_parts)
    def _(k):
        for which in range(2):
            for slot in range(n - 1):
                wp_copy(which, slot, k, w_mine).wait_send()

    @pl.loop(0, n)
    def _(k):
        for sign in (1, -1):
            block = z - k * sign

            @pl.when((block >= 0) & (block < n) & (z + sign >= 0) & (z + sign < n))
            def _():
                for ph in range(4):
                    for q in range(HALVES):
                        ag_copy(ph, block, q, sign).wait_send()

    @pl.loop(0, n)
    def _(j):
        for ph in range(2):
            c_copy(ph, j).wait_send()
            h_copy(ph, j, core).wait_send()
            o_copy(ph, j).wait()

            @pl.loop(1, chips)
            def _(e):
                peer = (chip + e) % chips

                @pl.when(peer < owners)
                def _():
                    q_copy(ph, j, e, chip, peer).wait_send()

                @pl.when(chip < owners)
                def _():
                    f_copy(ph, j, e, chip).wait_send()


def finish_kernel(*refs):
    count = (len(refs) - 5) // 2
    ins, outs = refs[:count], refs[count:2 * count]
    narrow, wide, in_sem, out_sem, move_sem = refs[2 * count:]
    rows = narrow.shape[1] // FINISH_PARTS
    parts = [(w, i, pl.ds(i * rows, rows)) for i in range(FINISH_PARTS) for w in range(2)]
    loads = [pltpu.make_async_copy(ins[w].at[at, :], narrow.at[w, at, :], in_sem.at[w, i]) for w, i, at in parts]
    stores = [pltpu.make_async_copy(wide.at[w, at, :], outs[w].at[at, :], out_sem.at[w, i]) for w, i, at in parts]
    moves = [pltpu.make_async_copy(ins[2 + k], outs[2 + k], move_sem.at[k]) for k in range(count - 2)]
    for copy in loads + moves:
        copy.start()
    for load, store, (w, i, at) in zip(loads, stores, parts):
        load.wait()
        wide[w, at, :] = narrow[w, at, :].astype(F32)
        store.start()
    for copy in stores + moves:
        copy.wait()


def per_device(n, s_count, blocks, weight_one, weight_two, gain_one, shift_one, gain_two, shift_two, cell_live, cotangent):
    rows, wide = cell_live.shape
    ch = blocks.shape[1] // wide
    cells = rows * wide
    total = cells + 2 * wide
    packed = -(-most_live(rows // HALVES, wide) // 16) * 16
    aligned = ch % 128 == 0
    chips = s_count // 2
    tap_rows = 9 * ch
    half_rows = tap_rows // 2
    owners = math.gcd(half_rows // 16, chips)
    piece = half_rows // owners

    if aligned:
        weight_one, weight_two = (w.reshape(tap_rows, n * ch) for w in (weight_one, weight_two))
    else:
        weight_one, weight_two = (
            w.reshape(tap_rows, n, ch).transpose(1, 0, 2) for w in (weight_one, weight_two))
    grad_shape = (2, owners, piece, n * ch) if aligned else (n, 2, owners, piece, ch)
    vmem = pl.BlockSpec(memory_space=pltpu.VMEM)
    hbm = pl.BlockSpec(memory_space=pl.ANY)
    sem = pltpu.SemaphoreType.DMA
    field = pltpu.VMEM((total, ch), F32)
    scratch = [
        pltpu.VMEM((ch * wide, 128), F32),
        pltpu.VMEM((2, n, tap_rows, ch), BF16),
        pltpu.VMEM((2, n - 1, tap_rows, ch), BF16),
        pltpu.VMEM((2, n, 3, 3 * ch, ch), BF16),
        pltpu.VMEM((2, 3 * ch, cells), BF16),
        pltpu.VMEM((HALVES, packed, cells // HALVES), BF16),
        pltpu.VMEM((HALVES, cells // HALVES, packed), BF16),
        pltpu.VMEM((HALVES, cells // HALVES, ch), F32),
        pltpu.VMEM((2, 2, wide, ch), BF16),
        pltpu.VMEM((2, 2, wide, ch), BF16),
        pltpu.VMEM((2, wide, ch), BF16),
        pltpu.VMEM((2, wide, ch), BF16),
        field, field, field, field, field, field, field, field, field,
        pltpu.VMEM((total + 16, ch), F32),
        pltpu.VMEM((cells, ch), F32),
        pltpu.VMEM((4, n, 2 * wide + HALVES * packed, ch), BF16),
        pltpu.VMEM((n, rows + 2, wide, 3 * ch), BF16),
        pltpu.VMEM((2, n, 2, owners, piece, ch), F32),
        pltpu.VMEM((2, n, owners, piece, ch), BF16),
        pltpu.VMEM((2, n, owners, piece, ch), BF16),
        pltpu.VMEM((2, n, owners, piece, ch), BF16),
        pltpu.VMEM((2, n, chips, piece, ch), BF16),
        pltpu.VMEM((2, n, 2, owners, piece, ch), BF16),
        pltpu.VMEM((4, 8, ch), F32),
        pltpu.VMEM((4, s_count, 8, ch), F32),
        pltpu.VMEM((3, 2, wide, ch), F32),
        pltpu.VMEM((3, 2, wide, ch), F32),
        sem((2, n)),
        sem((2, n)), sem((2, n)),
        sem((2, n - 1, s_count)), sem((2, n - 1, s_count)),
        sem((2,)), sem((2,)),
        sem((2,)), sem((2,)),
        sem((4, 2, n, HALVES)), sem((4, n, HALVES)),
        sem((4, s_count)), sem((4, s_count)),
        sem((3, 2)), sem((3, 2)),
        sem((2, n)), sem((2, n)),
        sem((2, n, chips)), sem((2, n, chips)),
        sem((2, n, chips)), sem((2, n, chips)),
        sem((2, n)), sem((2, n)),
        sem((2, n)),
    ]
    block_out, input_grad, wg1, wg2, *sums = pl.pallas_call(
        functools.partial(block_kernel, n, s_count, rows, wide, ch, aligned, packed),
        out_shape=(
            jax.ShapeDtypeStruct((rows, ch * wide), BF16),
            jax.ShapeDtypeStruct((rows, ch * wide), F32),
            jax.ShapeDtypeStruct(grad_shape, BF16),
            jax.ShapeDtypeStruct(grad_shape, BF16),
            *[jax.ShapeDtypeStruct((1, ch), F32)] * 4,
        ),
        in_specs=[vmem] * 7 + [hbm] * 2,
        out_specs=(vmem, vmem, hbm, hbm, vmem, vmem, vmem, vmem),
        scratch_shapes=scratch,
        compiler_params=pltpu.CompilerParams(
            collective_id=0, has_side_effects=True, vmem_limit_bytes=60 * 1024 * 1024),
    )(blocks, cotangent, cell_live.T,
      *(v.reshape(1, ch) for v in (gain_one, shift_one, gain_two, shift_two)), weight_one, weight_two)

    if not aligned:
        def whole(grad):
            grad = grad.reshape(n, tap_rows, ch).transpose(1, 0, 2)
            return grad.astype(F32).reshape(9, ch, n * ch)
        return (block_out, input_grad, whole(wg1), whole(wg2), *(v.reshape(ch) for v in sums))

    wg1, wg2 = (w.reshape(tap_rows, n * ch) for w in (wg1, wg2))
    wide_grad = jax.ShapeDtypeStruct((tap_rows, n * ch), F32)
    moved = (block_out, input_grad, *sums)
    grad1, grad2, *moved = pl.pallas_call(
        finish_kernel,
        out_shape=(wide_grad, wide_grad, *(jax.ShapeDtypeStruct(v.shape, v.dtype) for v in moved)),
        in_specs=[hbm] * (2 + len(moved)),
        out_specs=[hbm] * (2 + len(moved)),
        scratch_shapes=[
            pltpu.VMEM((2, tap_rows, n * ch), BF16), pltpu.VMEM((2, tap_rows, n * ch), F32),
            sem((2, FINISH_PARTS)), sem((2, FINISH_PARTS)), sem((len(moved),)),
        ],
        compiler_params=pltpu.CompilerParams(vmem_limit_bytes=32 * 1024 * 1024),
    )(wg1, wg2, *moved)
    block_out, input_grad, *sums = moved
    grads = (g.reshape(9, ch, n * ch) for g in (grad1, grad2))
    return (block_out, input_grad, *grads, *(v.reshape(ch) for v in sums))


def solution(mesh):
    return jax.shard_map(
        functools.partial(per_device, mesh.shape["chan"], mesh.shape["space"]),
        mesh=mesh,
        in_specs=(
            P("space", "chan"),
            P(None, "chan", None),
            P(None, "chan", None),
            P("chan"),
            P("chan"),
            P("chan"),
            P("chan"),
            P("space", None),
            P("space", "chan"),
        ),
        out_specs=(
            P("space", "chan"),
            P("space", "chan"),
            P(None, "chan", None),
            P(None, "chan", None),
            P("chan"),
            P("chan"),
            P("chan"),
            P("chan"),
        ),
        check_vma=False,
    )
```

```python
import functools
import math

import jax
import jax.numpy as jnp
from jax import lax
from jax.experimental import pallas as pl
from jax.experimental.pallas import tpu as pltpu
from jax.sharding import PartitionSpec as P

EPSILON = 1e-05
MESH = pl.DeviceIdType.MESH
F32 = jnp.float32
BF16 = jnp.bfloat16
ROOT_HALF = 0.7071067811865476
ROOT_TWO_PI = 0.3989422804014327
CHUNK = 64
FINISH_PARTS = 4
UNROLL = 2
HALVES = 2
LARGE, SMALL = 7, 3


def dot(a, b):
    return jnp.dot(a, b, preferred_element_type=F32)


def gelu_parts(v):
    upper = 0.5 * (1.0 + lax.erf(v * ROOT_HALF))
    slope = upper + v * (ROOT_TWO_PI * jnp.exp(-0.5 * v * v))
    return v * upper, slope


def most_live(rows, wide):
    units = (wide + 1) // (SMALL + 1)
    live_rows = rows - rows // (LARGE + 1)
    return min(rows * wide, math.ceil(units * live_rows * LARGE / 2))


def block_kernel(n, s_count, rows, wide, ch, aligned, packed, *refs):
    (x_in, cot_in, live_in, gain1_in, shift1_in, gain2_in, shift2_in, w1_hbm, w2_hbm) = refs[:9]
    (out_block, out_input, out_wg1, out_wg2, out_gain1, out_shift1, out_gain2, out_shift2) = refs[9:17]
    (turned, wv, wf, wt, x_t, pack, unpack, places, edge_send, edge_recv, cot_send, cot_recv, cotm, mask, masked,
     normed1, normed2, through, slope1, hid, hid2, pad, acc, hold, taken,
     part, psend, crecv, hsend, qrecv, wout, st_send, st_recv, row_send, row_recv,
     w_sem, wz_ssem, wz_rsem, wp_ssem, wp_rsem, e_ssem, e_rsem, ce_ssem, ce_rsem, ag_ssem, ag_rsem,
     st_ssem, st_rsem, row_ssem, row_rsem, c_ssem, c_rsem, q_ssem, q_rsem,
     f_ssem, f_rsem, h_ssem, h_rsem, o_sem) = refs[17:]

    z = lax.axis_index("chan")
    s = lax.axis_index("space")
    cells = rows * wide
    total = cells + 2 * wide
    band = cells // HALVES
    core, chip, chips = s % 2, s // 2, s_count // 2
    before, after = (s + s_count - 1) % s_count, (s + 1) % s_count
    tap_rows = 9 * ch

    barrier = pltpu.get_barrier_semaphore()

    @pl.loop(1, s_count)
    def _(k):
        pl.semaphore_signal(barrier, inc=1, device_id=(z, (s + k) % s_count), device_id_type=MESH)

    @pl.loop(1, n)
    def _(k):
        pl.semaphore_signal(barrier, inc=1, device_id=((z + k) % n, s), device_id_type=MESH)

    w_copies = []
    for which, source in enumerate((w1_hbm, w2_hbm)):
        for d in range(n):
            block = source.at[:, d * ch:(d + 1) * ch] if aligned else source.at[d]
            w_copies.append(pltpu.make_async_copy(block, wv.at[which, d], w_sem.at[which, d]))
    for copy in w_copies:
        copy.start()

    def chunked(fn, init, first=0, count=cells):
        def step(i, carry):
            return fn(pl.multiple_of(first + i * CHUNK, CHUNK), CHUNK, carry)
        return lax.fori_loop(0, count // CHUNK, step, init, unroll=UNROLL)

    lanes = 128
    tiles = ch * wide // lanes

    def from_flat(flat, put):
        for i in range(tiles):
            turned[i * lanes:(i + 1) * lanes, 0:rows] = flat[:, i * lanes:(i + 1) * lanes].astype(F32).T
        for w in range(wide):
            put(pl.ds(w, rows, stride=wide), turned[pl.ds(w, ch, stride=wide), 0:rows].T)

    def to_flat(source, flat):
        for w in range(wide):
            turned[pl.ds(w, ch, stride=wide), 0:rows] = source[pl.ds(w, rows, stride=wide), :].T
        for i in range(tiles):
            flat[:, i * lanes:(i + 1) * lanes] = turned[i * lanes:(i + 1) * lanes, 0:rows].T.astype(flat.dtype)

    def put_masked(at, value):
        masked[at, :] = value

    from_flat(x_in, put_masked)

    cell = lax.broadcasted_iota(jnp.int32, (cells, rows), 0)
    pick = (cell // wide == lax.broadcasted_iota(jnp.int32, (cells, rows), 1)).astype(F32).astype(BF16)
    column_of = lax.broadcasted_iota(jnp.int32, (cells, wide), 0) % wide
    picked = lax.dot_general(pick, live_in[...].astype(BF16), (((1,), (1,)), ((), ())), preferred_element_type=F32)
    picked = jnp.where(column_of == lax.broadcasted_iota(jnp.int32, (cells, wide), 1), picked, 0.0)
    mask[0:cells, :] = dot(picked.astype(BF16), jnp.ones((wide, ch), BF16))

    def load_main(start, size, carry):
        at = pl.ds(start, size)
        lv = mask[at, :]
        masked[at, :] = masked[at, :] * lv
        return carry

    chunked(load_main, 0)
    for side, start in ((0, 0), (1, cells - wide)):
        edge_send[side, 0] = masked[start:start + wide, :].astype(BF16)
        edge_send[side, 1] = mask[start:start + wide, :].astype(BF16)

    acc[...] = jnp.zeros_like(acc)
    st_send[...] = jnp.zeros_like(st_send)

    pl.semaphore_wait(barrier, s_count - 1 + n - 1)

    def edge_copy(side):
        return pltpu.make_async_remote_copy(
            src_ref=edge_send.at[side], dst_ref=edge_recv.at[1 - side],
            send_sem=e_ssem.at[side], recv_sem=e_rsem.at[1 - side],
            device_id=(z, before if side == 0 else after), device_id_type=MESH)

    for side in range(2):
        edge_copy(side).start()

    def cot_copy(side):
        return pltpu.make_async_remote_copy(
            src_ref=cot_send.at[side], dst_ref=cot_recv.at[1 - side],
            send_sem=ce_ssem.at[side], recv_sem=ce_rsem.at[1 - side],
            device_id=(z, before if side == 0 else after), device_id_type=MESH)

    def load_cotangent():
        def put(at, value):
            cotm[at, :] = value
        from_flat(cot_in, put)

        def live_only(start, size, carry):
            at = pl.ds(start, size)
            cotm[at, :] = cotm[at, :] * mask[at, :]
            return carry
        chunked(live_only, 0)
        for side, start in ((0, 0), (1, cells - wide)):
            cot_send[side] = cotm[start:start + wide, :].astype(BF16)
            cot_copy(side).start()

    def take_cotangent():
        for side in range(2):
            cot_copy(1 - side).wait_recv()
            at = slice(cells + side * wide, cells + (side + 1) * wide)
            cotm[at, :] = cot_recv[side].astype(F32) * mask[at, :]

    w_parts = math.gcd(tap_rows // 16, s_count)
    w_rows = tap_rows // w_parts
    w_mine = s % w_parts
    w_group = s - w_mine

    def wz_copy(which, k):
        at = pl.ds(w_mine * w_rows, w_rows)
        slot = n - k - 1
        return pltpu.make_async_remote_copy(
            src_ref=wv.at[which, (z + k) % n, at, :], dst_ref=wf.at[which, slot, at, :],
            send_sem=wz_ssem.at[which, slot], recv_sem=wz_rsem.at[which, slot],
            device_id=((z + k) % n, s), device_id_type=MESH)

    def wp_copy(which, slot, k, whose):
        at = pl.ds(whose * w_rows, w_rows)
        return pltpu.make_async_remote_copy(
            src_ref=wf.at[which, slot, at, :], dst_ref=wf.at[which, slot, at, :],
            send_sem=wp_ssem.at[which, slot, k], recv_sem=wp_rsem.at[which, slot, whose],
            device_id=(z, w_group + (w_mine + k) % w_parts), device_id_type=MESH)

    def weights_over_z(which):
        for copy in w_copies[which * n:(which + 1) * n]:
            copy.wait()

        @pl.loop(1, n)
        def _(k):
            wz_copy(which, k).start()

    def slot_of(block):
        return (block - z + n - 1) % n

    def weights_round(which):
        @pl.loop(1, n)
        def _(distance):
            for sign in (1, -1):
                block = z - distance * sign

                @pl.when((block >= 0) & (block < n))
                def _():
                    slot = slot_of(block)
                    wz_copy(which, n - 1 - slot).wait_recv()

                    @pl.loop(1, w_parts)
                    def _(k):
                        wp_copy(which, slot, k, w_mine).start()

    def weights_arrived(which, slot):
        @pl.loop(1, w_parts)
        def _(k):
            wp_copy(which, slot, k, (w_mine + k) % w_parts).wait_recv()

    def row_copy(slot, side):
        return pltpu.make_async_remote_copy(
            src_ref=row_send.at[slot, side], dst_ref=row_recv.at[slot, 1 - side],
            send_sem=row_ssem.at[slot, side], recv_sem=row_rsem.at[slot, 1 - side],
            device_id=(z, before if side == 0 else after), device_id_type=MESH)

    def send_rows(slot, ref):
        for side, start in ((0, 0), (1, cells - wide)):
            row_send[slot, side] = ref[start:start + wide, :]
            row_copy(slot, side).start()

    def take_rows(slot, ref):
        for side in range(2):
            row_copy(slot, 1 - side).wait_recv()
            ref[cells + side * wide:cells + (side + 1) * wide, :] = row_recv[slot, side]

    def st_copy(slot, k, whose):
        return pltpu.make_async_remote_copy(
            src_ref=st_send.at[slot], dst_ref=st_recv.at[slot, whose],
            send_sem=st_ssem.at[slot, k], recv_sem=st_rsem.at[slot, whose],
            device_id=(z, (s + k) % s_count), device_id_type=MESH)

    def send_stats(slot, values):
        for i, v in enumerate(values):
            st_send[slot, i:i + 1, :] = v
        for k in range(1, s_count):
            st_copy(slot, k, s).start()
        st_recv[slot, s] = st_send[slot]

    def take_stats(slot):
        for k in range(1, s_count):
            st_copy(slot, k, (s + k) % s_count).wait_recv()

    strip = 8
    column = lax.broadcasted_iota(jnp.int32, (strip * wide, ch), 0) % wide

    def shift(target, first, count):
        size = count * wide
        where = column[:size]
        here = pad[pl.ds(8 + first * wide, size), :]
        left = jnp.where(where == 0, 0.0, pad[pl.ds(7 + first * wide, size), :])
        right = jnp.where(where == wide - 1, 0.0, pad[pl.ds(9 + first * wide, size), :])
        for b, v in enumerate((left, here, right)):
            target[pl.ds(first, count), :, b * ch:(b + 1) * ch] = v.astype(BF16).reshape(count, wide, ch)

    edge = 2 * wide
    ag_rows = ((0, edge + packed), (edge + packed, packed))
    band_rows = rows // HALVES

    def unpack_half(ph, block, q, target):
        if q == 0:
            pad[8:8 + wide, :] = hold[ph, block, 0:wide, :].astype(F32)
            pad[8 + wide + cells:8 + 2 * wide + cells, :] = hold[ph, block, wide:edge, :].astype(F32)
            shift(target, 0, 1)
            shift(target, rows + 1, 1)
        pad[8 + wide + q * band:8 + wide + (q + 1) * band, :] = dot(
            unpack[q], hold[ph, block, edge + q * packed:edge + (q + 1) * packed, :])

        for i in range(band_rows // strip):
            shift(target, 1 + q * band_rows + i * strip, strip)

    def add_conv(q, field, taps):
        first, last = (0, band_rows - 1) if q == 0 else (band_rows - 1, rows)
        count = last - first
        lhs = field[first:last + 2, :, :].reshape((count + 2) * wide, 3 * ch)
        value = dot(lhs, jnp.concatenate([taps(a) for a in range(3)], axis=1))
        at = pl.ds(first * wide, count * wide)
        acc[at, :] = acc[at, :] + sum(
            value[a * wide:(a + count) * wide, a * ch:(a + 1) * ch] for a in range(3))

    def ag_copy(ph, block, q, sign):
        at = pl.ds(*ag_rows[q])
        return pltpu.make_async_remote_copy(
            src_ref=hold.at[ph, block, at, :], dst_ref=hold.at[ph, block, at, :],
            send_sem=ag_ssem.at[ph, (1 - sign) // 2, block, q], recv_sem=ag_rsem.at[ph, block, q],
            device_id=(z + sign, s), device_id_type=MESH)

    def pack_field(ph, source, fill=None, first=None):
        if fill is not None:
            fill(cells, edge, 0)
        hold[ph, z, 0:edge, :] = source[cells:cells + edge, :].astype(BF16)
        for q in range(HALVES):
            if first is not None:
                first(q)
            if fill is not None:
                chunked(fill, 0, q * band, band)
            hold[ph, z, edge + q * packed:edge + (q + 1) * packed, :] = dot(
                pack[q], source[q * band:(q + 1) * band, :].astype(BF16)).astype(BF16)
            for sign in (1, -1):
                @pl.when((z + sign >= 0) & (z + sign < n))
                def _():
                    ag_copy(ph, z, q, sign).start()

    def inside(slice_at):
        return (slice_at >= 0) & (slice_at < n)

    def take_and_pass(ph, k, q, sign, passes=True, takes=True):
        block = z - k * sign

        @pl.when((k > 0) & inside(block))
        def _():
            if passes and takes:
                ag_copy(ph, block, q, sign).wait_recv()

            @pl.when(inside(z + sign))
            def _():
                if passes:
                    if not takes:
                        ag_copy(ph, block, q, sign).wait_recv()
                    ag_copy(ph, block, q, sign).start()

            if not passes:
                @pl.when(jnp.logical_not(inside(z + sign)))
                def _():
                    ag_copy(ph, block, q, sign).wait_recv()

    near = jnp.where(z < n - n // 2, 1, 0)

    def consume_way(k, q, way, consume):
        block = z - k * (1 - 2 * way)

        @pl.when((k >= 0) & (k < n) & inside(block) & ((k > 0) | (way == near)))
        def _():
            consume(k, block, q)

    def take_both(ph, k, q, **how):
        @pl.loop(0, 2)
        def _(i):
            way = (near + i) % 2
            take_and_pass(ph, k, q, 1 - 2 * way, **how)

    def gather(ph, consume, each):
        @pl.loop(0, n)
        def _(k):
            for q in range(HALVES):
                take_both(ph, k, q)
                if q:
                    consume_way(k, q - 1, 1 - near, consume)
                else:
                    consume_way(k - 1, HALVES - 1, 1 - near, consume)
                consume_way(k, q, near, consume)
            each(k)

    def gather_passing_first(ph, consume, each):
        @pl.loop(0, n)
        def _(k):
            @pl.when(k == 1)
            def _():
                @pl.loop(1, n)
                def _(ahead):
                    for q in range(HALVES):
                        take_both(ph, ahead, q, takes=False)
            for q in range(HALVES):
                take_both(ph, k, q, passes=False)

                @pl.loop(0, 2)
                def _(i):
                    consume_way(k, q, (near + i) % 2, consume)
            each(k)

    last_pass = jnp.maximum(jnp.where(z < n - 1, z, 0), jnp.where(z > 0, n - 1 - z, 0))

    def forward(ph, field):
        def consume(k, block, q):
            into = taken.at[block]
            unpack_half(ph, block, q, into)

            @pl.when(k == 0)
            def _():
                add_conv(q, into, lambda a: wv[ph, z, 3 * a * ch:3 * (a + 1) * ch, :])

            @pl.when(k > 0)
            def _():
                slot = slot_of(block)
                if q == 0:
                    weights_arrived(ph, slot)
                add_conv(q, into, lambda a: wf[ph, slot, 3 * a * ch:3 * (a + 1) * ch, :])

        def each(k):
            if ph == 0:
                @pl.when(k == 0)
                def _():
                    weights_round(0)

            @pl.when(k == last_pass)
            def _():
                turn_weights(ph)
                turn_field(ph, field)
                if ph == 0:
                    load_cotangent()
        (gather if ph else gather_passing_first)(ph, consume, each)

    def turn_field(ph, field):
        for a in range(3):
            for start in range(0, cells, ch):
                first = start + (a - 1) * wide
                if first < 0:
                    v = jnp.concatenate([field[cells:cells + wide, :], field[0:first + ch, :]], axis=0)
                elif first + ch > cells:
                    v = jnp.concatenate([field[first:cells, :], field[cells + wide:total, :]], axis=0)
                else:
                    v = field[first:first + ch, :]
                x_t[ph, a * ch:(a + 1) * ch, start:start + ch] = v.T.astype(BF16)

    def turn_weights(ph):
        @pl.loop(0, n)
        def _(d):
            for t in range(9):
                a, b = 2 - t // 3, 2 - t % 3
                wt[ph, d, a, b * ch:(b + 1) * ch, :] = wv[ph, d, t * ch:(t + 1) * ch, :].T

    half_rows = tap_rows // 2
    owners = math.gcd(half_rows // 16, chips)
    piece = half_rows // owners

    def c_copy(ph, j):
        return pltpu.make_async_remote_copy(
            src_ref=psend.at[ph, j], dst_ref=crecv.at[ph, j],
            send_sem=c_ssem.at[ph, j], recv_sem=c_rsem.at[ph, j],
            device_id=(z, chip * 2 + 1 - core), device_id_type=MESH)

    def q_copy(ph, j, e, whose, owner):
        return pltpu.make_async_remote_copy(
            src_ref=hsend.at[ph, j, owner], dst_ref=qrecv.at[ph, j, whose],
            send_sem=q_ssem.at[ph, j, e], recv_sem=q_rsem.at[ph, j, whose],
            device_id=(z, ((chip + e) % chips) * 2 + core), device_id_type=MESH)

    def f_copy(ph, j, e, owner):
        return pltpu.make_async_remote_copy(
            src_ref=wout.at[ph, j, core, owner], dst_ref=wout.at[ph, j, core, owner],
            send_sem=f_ssem.at[ph, j, e], recv_sem=f_rsem.at[ph, j, owner],
            device_id=(z, ((chip + e) % chips) * 2 + core), device_id_type=MESH)

    def h_copy(ph, j, whose):
        return pltpu.make_async_remote_copy(
            src_ref=wout.at[ph, j, whose], dst_ref=wout.at[ph, j, whose],
            send_sem=h_ssem.at[ph, j], recv_sem=h_rsem.at[ph, j],
            device_id=(z, chip * 2 + 1 - core), device_id_type=MESH)

    def o_copy(ph, j):
        target = (out_wg1, out_wg2)[ph]
        if aligned:
            target = target.at[:, :, :, pl.ds(pl.multiple_of(j * ch, ch), ch)]
        else:
            target = target.at[j]
        return pltpu.make_async_copy(wout.at[ph, j], target, o_sem.at[ph, j])

    def sum_cores(ph, j):
        for o in range(owners):
            psend[ph, j, o] = part[ph, j, 1 - core, o].astype(BF16)
        c_copy(ph, j).start()

    def sum_chips(ph, j):
        c_copy(ph, j).wait_recv()
        for o in range(owners):
            v = part[ph, j, core, o] + crecv[ph, j, o].astype(F32)
            part[ph, j, core, o] = v
            hsend[ph, j, o] = v.astype(BF16)

        @pl.loop(1, chips)
        def _(e):
            peer = (chip + e) % chips

            @pl.when(peer < owners)
            def _():
                q_copy(ph, j, e, chip, peer).start()

    def spread_chips(ph, j):
        @pl.when(chip < owners)
        def _():
            @pl.loop(1, chips)
            def _(e):
                q_copy(ph, j, e, (chip + e) % chips, chip).wait_recv()
            v = part[ph, j, core, chip]
            for e in range(1, chips):
                v = v + qrecv[ph, j, (chip + e) % chips].astype(F32)
            wout[ph, j, core, chip] = v.astype(BF16)

            @pl.loop(1, chips)
            def _(e):
                f_copy(ph, j, e, chip).start()

    def spread_cores(ph, j):
        @pl.loop(1, chips)
        def _(e):
            peer = (chip + e) % chips

            @pl.when(peer < owners)
            def _():
                f_copy(ph, j, e, peer).wait_recv()
        h_copy(ph, j, core).start()

    def finish(ph, j):
        h_copy(ph, j, 1 - core).wait_recv()
        o_copy(ph, j).start()

    def put_part(ph, j, tap, value):
        start = tap * ch
        done = 0
        while done < ch:
            row = start + done
            side, o, at = row // half_rows, row % half_rows // piece, row % piece
            size = min(ch - done, piece - at)
            part[ph, j, side, o, at:at + size, :] = value[done:done + size, :]
            done += size

    stages = (sum_cores, sum_chips, spread_chips, spread_cores, finish)

    def of_step(k, fn):
        @pl.loop(0, 2)
        def _(way):
            block = z - k * (1 - 2 * way)

            @pl.when((k >= 0) & (k < n) & inside(block) & ((k > 0) | (way == 0)))
            def _():
                fn(block)

    passing = last_pass > 0

    def made_at(step):
        first = jnp.where(passing & (step > 0), jnp.where(step == last_pass, 1, step + 1), step)
        return first, step + 1

    def advance(ph, k):
        for age in range(1, len(stages)):
            step = k - age

            @pl.when((step >= 0) & (step < n))
            def _():
                @pl.loop(*made_at(step))
                def _(made):
                    of_step(made, functools.partial(stages[age], ph))

    def advance_all(ph, age):
        @pl.loop(0, n)
        def _(j):
            stages[age](ph, j)

    def field_grad(ph, block):
        grad = taken[block, 1:rows + 1, :, :].reshape(cells, 3 * ch)
        value = dot(x_t[ph], grad)
        for a in range(3):
            for b in range(3):
                put_part(ph, block, 3 * a + b, value[a * ch:(a + 1) * ch, (2 - b) * ch:(3 - b) * ch])

    def make_grad(ph, block):
        field_grad(ph, block)
        sum_cores(ph, block)

    def backward(ph):
        last = ph == 0

        def consume(k, block, q):
            into = taken.at[block]
            unpack_half(2 + ph, block, q, into)
            if last and q == HALVES - 1:
                @pl.when((k == 0) | (k >= last_pass))
                def _():
                    make_grad(ph, block)
            add_conv(q, into, lambda a: wt[ph, block, a])

        def each(k):
            first, end = made_at(k)
            if last:
                @pl.loop(first, end - 1)
                def _(step):
                    of_step(step, functools.partial(make_grad, ph))
                advance(ph, k)
                for age in range(2, len(stages)):
                    @pl.when(k == age - 2)
                    def _():
                        advance_all(1, age)
            else:
                @pl.loop(first, jnp.where(passing | (k < n - 1), end, first))
                def _(step):
                    of_step(step, functools.partial(make_grad, ph))

                @pl.when(k == last_pass)
                def _():
                    to_flat(hid2, out_block)
        gather(2 + ph, consume, each)

    def fold(v):
        return jnp.sum(v.reshape(v.shape[0] // 8, 8, ch), axis=0)

    def flatten(v):
        return jnp.sum(v, axis=0, keepdims=True)

    zero = jnp.zeros((8, ch), F32)

    def local_moments(ref):
        def sums(start, size, carry):
            at = pl.ds(start, size)
            m = mask[at, :]
            return carry[0] + fold(ref[at, :] * m), carry[1] + fold(m)
        added, number = (flatten(v) for v in chunked(sums, (zero, zero)))
        middle = added / jnp.maximum(number, 1.0)

        def spread(start, size, carry):
            at = pl.ds(start, size)
            c = (ref[at, :] - middle) * mask[at, :]
            return carry + fold(c * c)
        return added, number, flatten(chunked(spread, zero))

    def moments(slot):
        take_stats(slot)
        got = [st_recv[slot, k] for k in range(s_count)]
        added = sum(g[0:1] for g in got)
        number = sum(g[1:2] for g in got)
        mean = added / number
        spread = 0.0
        for g in got:
            off = g[0:1] / jnp.maximum(g[1:2], 1.0) - mean
            spread = spread + (g[2:3] + g[1:2] * off * off)
        return mean, lax.rsqrt(spread / number + EPSILON), number

    def everywhere(fn):
        chunked(fn, 0)
        fn(cells, 2 * wide, 0)

    gain1, shift1, gain2, shift2 = (r[...] for r in (gain1_in, shift1_in, gain2_in, shift2_in))

    weights_over_z(0)

    below = lax.broadcasted_iota(jnp.int32, (band, band), 1) < lax.broadcasted_iota(jnp.int32, (band, band), 0)
    below = below.astype(F32).astype(BF16)

    def make_pack(h):
        lv = mask[h * band:(h + 1) * band, :]
        place = jnp.where(lv > 0.0, dot(below, lv.astype(BF16)), -1.0)
        places[h] = place
        across = place.T[0:1, :]
        spot = lax.broadcasted_iota(jnp.int32, (packed, band), 0).astype(F32)
        pack[h] = jnp.where(spot == across, 1.0, 0.0).astype(BF16)

    def make_unpack(h):
        for start in range(0, packed, ch):
            size = min(ch, packed - start)
            spot = start + lax.broadcasted_iota(jnp.int32, (band, size), 1)
            unpack[h, :, start:start + size] = jnp.where(
                places[h, :, :size] == spot.astype(F32), 1.0, 0.0).astype(BF16)

    for side in range(2):
        edge_copy(1 - side).wait_recv()
        there = jnp.where(s > 0, 1.0, 0.0) if side == 0 else jnp.where(s < s_count - 1, 1.0, 0.0)
        at = slice(cells + side * wide, cells + (side + 1) * wide)
        masked[at, :] = edge_recv[side, 0].astype(F32) * there
        mask[at, :] = edge_recv[side, 1].astype(F32) * there

    pack_field(0, masked, first=make_pack)
    for h in range(HALVES):
        make_unpack(h)
    forward(0, masked)
    weights_over_z(1)
    send_rows(0, acc)
    send_stats(0, local_moments(acc))
    mean1, scale1, count = moments(0)
    weights_round(1)

    def activate_one(start, size, carry):
        at = pl.ds(start, size)
        main = start is not cells
        nv = ((acc if main else normed1)[at, :] - mean1) * scale1
        normed1[at, :] = nv
        hid[at, :] = gelu_parts(nv * gain1 + shift1)[0] * mask[at, :]
        if main:
            acc[at, :] = jnp.zeros((size, ch), F32)
        return carry

    def slope_one(start, size, carry):
        at = pl.ds(start, size)
        slope1[at, :] = gelu_parts(normed1[at, :] * gain1 + shift1)[1] * mask[at, :]
        return carry

    take_rows(0, normed1)
    pack_field(1, hid, activate_one)
    everywhere(slope_one)
    forward(1, hid)
    send_rows(1, acc)
    send_stats(1, local_moments(acc))
    mean2, scale2, _ = moments(1)

    def activate_two(source, start, size):
        at = pl.ds(start, size)
        nv = (source[at, :] - mean2) * scale2
        normed2[at, :] = nv
        value, slope = gelu_parts(nv * gain2 + shift2 + masked[at, :])
        t = cotm[at, :] * slope
        through[at, :] = t
        return value, nv, t

    def activate_main(start, size, carry):
        value, nv, t = activate_two(acc, start, size)
        at = pl.ds(start, size)
        hid2[at, :] = value * mask[at, :]
        acc[at, :] = jnp.zeros((size, ch), F32)
        return carry[0] + fold(t * nv), carry[1] + fold(t)

    send_stats(2, [flatten(v) for v in chunked(activate_main, (zero, zero))])
    take_rows(1, normed2)
    take_cotangent()
    activate_two(normed2, cells, edge)

    def gradient_sums(slot):
        take_stats(slot)
        got = [st_recv[slot, k] for k in range(s_count)]
        return sum(g[0:1] for g in got), sum(g[1:2] for g in got)

    def norm_back(upstream, normed, gain, scale, sums):
        gain_grad, shift_grad = sums
        factor = gain * scale
        level, tilt = shift_grad / count, gain_grad / count

        def fill(start, size, carry):
            at = pl.ds(start, size)
            v = upstream[at, :] - mask[at, :] * (level + normed[at, :] * tilt)
            hid[at, :] = factor * v
            return carry
        return fill

    sums2 = gradient_sums(2)
    pack_field(3, hid, norm_back(through, normed2, gain2, scale2, sums2))
    backward(1)

    send_rows(2, acc)

    def inner_main(start, size, carry):
        at = pl.ds(start, size)
        v = acc[at, :] * slope1[at, :]
        slope1[at, :] = v
        acc[at, :] = jnp.zeros((size, ch), F32)
        return carry[0] + fold(v * normed1[at, :]), carry[1] + fold(v)

    send_stats(3, [flatten(v) for v in chunked(inner_main, (zero, zero))])

    @pl.when(jnp.logical_not(passing))
    def _():
        of_step(n - 1, functools.partial(make_grad, 1))
    for side in range(2):
        row_copy(2, 1 - side).wait_recv()
        at = slice(cells + side * wide, cells + (side + 1) * wide)
        slope1[at, :] = row_recv[2, side] * slope1[at, :]
    sums1 = gradient_sums(3)
    pack_field(2, hid, norm_back(slope1, normed1, gain1, scale1, sums1))
    advance_all(1, 1)
    backward(0)
    advance(0, n)

    def finish_input(start, size, carry):
        at = pl.ds(start, size)
        acc[at, :] = (acc[at, :] + through[at, :]) * mask[at, :]
        return carry

    chunked(finish_input, 0)
    to_flat(acc, out_input)
    out_gain1[...], out_shift1[...] = sums1
    out_gain2[...], out_shift2[...] = sums2
    for extra in range(1, len(stages) - 1):
        advance(0, n + extra)

    for side in range(2):
        edge_copy(side).wait_send()
        cot_copy(side).wait_send()
        for slot in range(3):
            row_copy(slot, side).wait_send()

    @pl.loop(1, s_count)
    def _(k):
        for slot in range(4):
            st_copy(slot, k, s).wait_send()

    @pl.loop(1, n)
    def _(k):
        for which in range(2):
            wz_copy(which, k).wait_send()

    @pl.loop(1, w_parts)
    def _(k):
        for which in range(2):
            for slot in range(n - 1):
                wp_copy(which, slot, k, w_mine).wait_send()

    @pl.loop(0, n)
    def _(k):
        for sign in (1, -1):
            block = z - k * sign

            @pl.when((block >= 0) & (block < n) & (z + sign >= 0) & (z + sign < n))
            def _():
                for ph in range(4):
                    for q in range(HALVES):
                        ag_copy(ph, block, q, sign).wait_send()

    @pl.loop(0, n)
    def _(j):
        for ph in range(2):
            c_copy(ph, j).wait_send()
            h_copy(ph, j, core).wait_send()
            o_copy(ph, j).wait()

            @pl.loop(1, chips)
            def _(e):
                peer = (chip + e) % chips

                @pl.when(peer < owners)
                def _():
                    q_copy(ph, j, e, chip, peer).wait_send()

                @pl.when(chip < owners)
                def _():
                    f_copy(ph, j, e, chip).wait_send()


def finish_kernel(*refs):
    count = (len(refs) - 5) // 2
    ins, outs = refs[:count], refs[count:2 * count]
    narrow, wide, in_sem, out_sem, move_sem = refs[2 * count:]
    rows = narrow.shape[1] // FINISH_PARTS
    parts = [(w, i, pl.ds(i * rows, rows)) for i in range(FINISH_PARTS) for w in range(2)]
    loads = [pltpu.make_async_copy(ins[w].at[at, :], narrow.at[w, at, :], in_sem.at[w, i]) for w, i, at in parts]
    stores = [pltpu.make_async_copy(wide.at[w, at, :], outs[w].at[at, :], out_sem.at[w, i]) for w, i, at in parts]
    moves = [pltpu.make_async_copy(ins[2 + k], outs[2 + k], move_sem.at[k]) for k in range(count - 2)]
    for copy in loads + moves:
        copy.start()
    for load, store, (w, i, at) in zip(loads, stores, parts):
        load.wait()
        wide[w, at, :] = narrow[w, at, :].astype(F32)
        store.start()
    for copy in stores + moves:
        copy.wait()


def per_device(n, s_count, blocks, weight_one, weight_two, gain_one, shift_one, gain_two, shift_two, cell_live, cotangent):
    rows, wide = cell_live.shape
    ch = blocks.shape[1] // wide
    cells = rows * wide
    total = cells + 2 * wide
    packed = -(-most_live(rows // HALVES, wide) // 16) * 16
    aligned = ch % 128 == 0
    chips = s_count // 2
    tap_rows = 9 * ch
    half_rows = tap_rows // 2
    owners = math.gcd(half_rows // 16, chips)
    piece = half_rows // owners

    if aligned:
        weight_one, weight_two = (w.reshape(tap_rows, n * ch) for w in (weight_one, weight_two))
    else:
        weight_one, weight_two = (
            w.reshape(tap_rows, n, ch).transpose(1, 0, 2) for w in (weight_one, weight_two))
    grad_shape = (2, owners, piece, n * ch) if aligned else (n, 2, owners, piece, ch)
    vmem = pl.BlockSpec(memory_space=pltpu.VMEM)
    hbm = pl.BlockSpec(memory_space=pl.ANY)
    sem = pltpu.SemaphoreType.DMA
    field = pltpu.VMEM((total, ch), F32)
    scratch = [
        pltpu.VMEM((ch * wide, 128), F32),
        pltpu.VMEM((2, n, tap_rows, ch), BF16),
        pltpu.VMEM((2, n - 1, tap_rows, ch), BF16),
        pltpu.VMEM((2, n, 3, 3 * ch, ch), BF16),
        pltpu.VMEM((2, 3 * ch, cells), BF16),
        pltpu.VMEM((HALVES, packed, cells // HALVES), BF16),
        pltpu.VMEM((HALVES, cells // HALVES, packed), BF16),
        pltpu.VMEM((HALVES, cells // HALVES, ch), F32),
        pltpu.VMEM((2, 2, wide, ch), BF16),
        pltpu.VMEM((2, 2, wide, ch), BF16),
        pltpu.VMEM((2, wide, ch), BF16),
        pltpu.VMEM((2, wide, ch), BF16),
        field, field, field, field, field, field, field, field, field,
        pltpu.VMEM((total + 16, ch), F32),
        pltpu.VMEM((cells, ch), F32),
        pltpu.VMEM((4, n, 2 * wide + HALVES * packed, ch), BF16),
        pltpu.VMEM((n, rows + 2, wide, 3 * ch), BF16),
        pltpu.VMEM((2, n, 2, owners, piece, ch), F32),
        pltpu.VMEM((2, n, owners, piece, ch), BF16),
        pltpu.VMEM((2, n, owners, piece, ch), BF16),
        pltpu.VMEM((2, n, owners, piece, ch), BF16),
        pltpu.VMEM((2, n, chips, piece, ch), BF16),
        pltpu.VMEM((2, n, 2, owners, piece, ch), BF16),
        pltpu.VMEM((4, 8, ch), F32),
        pltpu.VMEM((4, s_count, 8, ch), F32),
        pltpu.VMEM((3, 2, wide, ch), F32),
        pltpu.VMEM((3, 2, wide, ch), F32),
        sem((2, n)),
        sem((2, n)), sem((2, n)),
        sem((2, n - 1, s_count)), sem((2, n - 1, s_count)),
        sem((2,)), sem((2,)),
        sem((2,)), sem((2,)),
        sem((4, 2, n, HALVES)), sem((4, n, HALVES)),
        sem((4, s_count)), sem((4, s_count)),
        sem((3, 2)), sem((3, 2)),
        sem((2, n)), sem((2, n)),
        sem((2, n, chips)), sem((2, n, chips)),
        sem((2, n, chips)), sem((2, n, chips)),
        sem((2, n)), sem((2, n)),
        sem((2, n)),
    ]
    block_out, input_grad, wg1, wg2, *sums = pl.pallas_call(
        functools.partial(block_kernel, n, s_count, rows, wide, ch, aligned, packed),
        out_shape=(
            jax.ShapeDtypeStruct((rows, ch * wide), BF16),
            jax.ShapeDtypeStruct((rows, ch * wide), F32),
            jax.ShapeDtypeStruct(grad_shape, BF16),
            jax.ShapeDtypeStruct(grad_shape, BF16),
            *[jax.ShapeDtypeStruct((1, ch), F32)] * 4,
        ),
        in_specs=[vmem] * 7 + [hbm] * 2,
        out_specs=(vmem, vmem, hbm, hbm, vmem, vmem, vmem, vmem),
        scratch_shapes=scratch,
        compiler_params=pltpu.CompilerParams(
            collective_id=0, has_side_effects=True, vmem_limit_bytes=60 * 1024 * 1024),
    )(blocks, cotangent, cell_live.T,
      *(v.reshape(1, ch) for v in (gain_one, shift_one, gain_two, shift_two)), weight_one, weight_two)

    if not aligned:
        def whole(grad):
            grad = grad.reshape(n, tap_rows, ch).transpose(1, 0, 2)
            return grad.astype(F32).reshape(9, ch, n * ch)
        return (block_out, input_grad, whole(wg1), whole(wg2), *(v.reshape(ch) for v in sums))

    wg1, wg2 = (w.reshape(tap_rows, n * ch) for w in (wg1, wg2))
    wide_grad = jax.ShapeDtypeStruct((tap_rows, n * ch), F32)
    moved = (block_out, input_grad, *sums)
    grad1, grad2, *moved = pl.pallas_call(
        finish_kernel,
        out_shape=(wide_grad, wide_grad, *(jax.ShapeDtypeStruct(v.shape, v.dtype) for v in moved)),
        in_specs=[pl.BlockSpec(memory_space=pl.ANY)] * (2 + len(moved)),
        out_specs=[pl.BlockSpec(memory_space=pl.ANY)] * (2 + len(moved)),
        scratch_shapes=[
            pltpu.VMEM((2, tap_rows, n * ch), BF16), pltpu.VMEM((2, tap_rows, n * ch), F32),
            sem((2, FINISH_PARTS)), sem((2, FINISH_PARTS)), sem((len(moved),)),
        ],
        compiler_params=pltpu.CompilerParams(vmem_limit_bytes=64 * 1024 * 1024),
    )(wg1, wg2, *moved)
    block_out, input_grad, *sums = moved
    grads = (g.reshape(9, ch, n * ch) for g in (grad1, grad2))
    return (block_out, input_grad, *grads, *(v.reshape(ch) for v in sums))


def solution(mesh):
    return jax.shard_map(
        functools.partial(per_device, mesh.shape["chan"], mesh.shape["space"]),
        mesh=mesh,
        in_specs=(
            P("space", "chan"),
            P(None, "chan", None),
            P(None, "chan", None),
            P("chan"),
            P("chan"),
            P("chan"),
            P("chan"),
            P("space", None),
            P("space", "chan"),
        ),
        out_specs=(
            P("space", "chan"),
            P("space", "chan"),
            P(None, "chan", None),
            P(None, "chan", None),
            P("chan"),
            P("chan"),
            P("chan"),
            P("chan"),
        ),
        check_vma=False,
    )
```

```python
import functools
import math

import jax
import jax.numpy as jnp
from jax import lax
from jax.experimental import pallas as pl
from jax.experimental.pallas import tpu as pltpu
from jax.sharding import PartitionSpec as P

EPSILON = 1e-05
MESH = pl.DeviceIdType.MESH
F32 = jnp.float32
BF16 = jnp.bfloat16
ROOT_HALF = 0.7071067811865476
ROOT_TWO_PI = 0.3989422804014327
CHUNK = 64
FINISH_PARTS = 4
UNROLL = 2
HALVES = 2
LARGE, SMALL = 7, 3


def dot(a, b):
    return jnp.dot(a, b, preferred_element_type=F32)


def gelu_parts(v):
    upper = 0.5 * (1.0 + lax.erf(v * ROOT_HALF))
    slope = upper + v * (ROOT_TWO_PI * jnp.exp(-0.5 * v * v))
    return v * upper, slope


def most_live(rows, wide):
    units = (wide + 1) // (SMALL + 1)
    live_rows = rows - rows // (LARGE + 1)
    return min(rows * wide, math.ceil(units * live_rows * LARGE / 2))


def block_kernel(n, s_count, rows, wide, ch, aligned, packed, *refs):
    (x_in, cot_in, live_in, gain1_in, shift1_in, gain2_in, shift2_in, w1_hbm, w2_hbm) = refs[:9]
    (out_block, out_input, out_wg1, out_wg2, out_gain1, out_shift1, out_gain2, out_shift2) = refs[9:17]
    (turned, wv, wf, wt, x_t, pack, unpack, places, edge_send, edge_recv, cot_send, cot_recv, cotm, mask, masked,
     normed1, normed2, through, slope1, hid, hid2, pad, acc, hold, taken,
     part, psend, crecv, hsend, qrecv, wout, st_send, st_recv, row_send, row_recv,
     w_sem, wz_ssem, wz_rsem, wp_ssem, wp_rsem, e_ssem, e_rsem, ce_ssem, ce_rsem, ag_ssem, ag_rsem,
     st_ssem, st_rsem, row_ssem, row_rsem, c_ssem, c_rsem, q_ssem, q_rsem,
     f_ssem, f_rsem, h_ssem, h_rsem, o_sem) = refs[17:]

    z = lax.axis_index("chan")
    s = lax.axis_index("space")
    cells = rows * wide
    total = cells + 2 * wide
    band = cells // HALVES
    core, chip, chips = s % 2, s // 2, s_count // 2
    before, after = (s + s_count - 1) % s_count, (s + 1) % s_count
    tap_rows = 9 * ch

    barrier = pltpu.get_barrier_semaphore()

    @pl.loop(1, s_count)
    def _(k):
        pl.semaphore_signal(barrier, inc=1, device_id=(z, (s + k) % s_count), device_id_type=MESH)

    @pl.loop(1, n)
    def _(k):
        pl.semaphore_signal(barrier, inc=1, device_id=((z + k) % n, s), device_id_type=MESH)

    w_copies = []
    for which, source in enumerate((w1_hbm, w2_hbm)):
        for d in range(n):
            block = source.at[:, d * ch:(d + 1) * ch] if aligned else source.at[d]
            w_copies.append(pltpu.make_async_copy(block, wv.at[which, d], w_sem.at[which, d]))
    for copy in w_copies:
        copy.start()

    def chunked(fn, init, first=0, count=cells):
        def step(i, carry):
            return fn(pl.multiple_of(first + i * CHUNK, CHUNK), CHUNK, carry)
        return lax.fori_loop(0, count // CHUNK, step, init, unroll=UNROLL)

    lanes = 128
    tiles = ch * wide // lanes

    def from_flat(flat, put):
        for i in range(tiles):
            turned[i * lanes:(i + 1) * lanes, 0:rows] = flat[:, i * lanes:(i + 1) * lanes].astype(F32).T
        for w in range(wide):
            put(pl.ds(w, rows, stride=wide), turned[pl.ds(w, ch, stride=wide), 0:rows].T)

    def to_flat(source, flat):
        for w in range(wide):
            turned[pl.ds(w, ch, stride=wide), 0:rows] = source[pl.ds(w, rows, stride=wide), :].T
        for i in range(tiles):
            flat[:, i * lanes:(i + 1) * lanes] = turned[i * lanes:(i + 1) * lanes, 0:rows].T.astype(flat.dtype)

    def put_masked(at, value):
        masked[at, :] = value

    from_flat(x_in, put_masked)

    cell = lax.broadcasted_iota(jnp.int32, (cells, rows), 0)
    pick = (cell // wide == lax.broadcasted_iota(jnp.int32, (cells, rows), 1)).astype(F32).astype(BF16)
    column_of = lax.broadcasted_iota(jnp.int32, (cells, wide), 0) % wide
    picked = lax.dot_general(pick, live_in[...].astype(BF16), (((1,), (1,)), ((), ())), preferred_element_type=F32)
    picked = jnp.where(column_of == lax.broadcasted_iota(jnp.int32, (cells, wide), 1), picked, 0.0)
    mask[0:cells, :] = dot(picked.astype(BF16), jnp.ones((wide, ch), BF16))

    def load_main(start, size, carry):
        at = pl.ds(start, size)
        lv = mask[at, :]
        masked[at, :] = masked[at, :] * lv
        return carry

    chunked(load_main, 0)
    for side, start in ((0, 0), (1, cells - wide)):
        edge_send[side, 0] = masked[start:start + wide, :].astype(BF16)
        edge_send[side, 1] = mask[start:start + wide, :].astype(BF16)

    acc[...] = jnp.zeros_like(acc)
    st_send[...] = jnp.zeros_like(st_send)

    pl.semaphore_wait(barrier, s_count - 1 + n - 1)

    def edge_copy(side):
        return pltpu.make_async_remote_copy(
            src_ref=edge_send.at[side], dst_ref=edge_recv.at[1 - side],
            send_sem=e_ssem.at[side], recv_sem=e_rsem.at[1 - side],
            device_id=(z, before if side == 0 else after), device_id_type=MESH)

    for side in range(2):
        edge_copy(side).start()

    def cot_copy(side):
        return pltpu.make_async_remote_copy(
            src_ref=cot_send.at[side], dst_ref=cot_recv.at[1 - side],
            send_sem=ce_ssem.at[side], recv_sem=ce_rsem.at[1 - side],
            device_id=(z, before if side == 0 else after), device_id_type=MESH)

    def load_cotangent():
        def put(at, value):
            cotm[at, :] = value
        from_flat(cot_in, put)

        def live_only(start, size, carry):
            at = pl.ds(start, size)
            cotm[at, :] = cotm[at, :] * mask[at, :]
            return carry
        chunked(live_only, 0)
        for side, start in ((0, 0), (1, cells - wide)):
            cot_send[side] = cotm[start:start + wide, :].astype(BF16)
            cot_copy(side).start()

    def take_cotangent():
        for side in range(2):
            cot_copy(1 - side).wait_recv()
            at = slice(cells + side * wide, cells + (side + 1) * wide)
            cotm[at, :] = cot_recv[side].astype(F32) * mask[at, :]

    w_parts = math.gcd(tap_rows // 16, s_count)
    w_rows = tap_rows // w_parts
    w_mine = s % w_parts
    w_group = s - w_mine

    def wz_copy(which, k):
        at = pl.ds(w_mine * w_rows, w_rows)
        slot = n - k - 1
        return pltpu.make_async_remote_copy(
            src_ref=wv.at[which, (z + k) % n, at, :], dst_ref=wf.at[which, slot, at, :],
            send_sem=wz_ssem.at[which, slot], recv_sem=wz_rsem.at[which, slot],
            device_id=((z + k) % n, s), device_id_type=MESH)

    def wp_copy(which, slot, k, whose):
        at = pl.ds(whose * w_rows, w_rows)
        return pltpu.make_async_remote_copy(
            src_ref=wf.at[which, slot, at, :], dst_ref=wf.at[which, slot, at, :],
            send_sem=wp_ssem.at[which, slot, k], recv_sem=wp_rsem.at[which, slot, whose],
            device_id=(z, w_group + (w_mine + k) % w_parts), device_id_type=MESH)

    def weights_over_z(which):
        for copy in w_copies[which * n:(which + 1) * n]:
            copy.wait()

        @pl.loop(1, n)
        def _(k):
            wz_copy(which, k).start()

    def slot_of(block):
        return (block - z + n - 1) % n

    def weights_round(which):
        @pl.loop(1, n)
        def _(distance):
            for sign in (1, -1):
                block = z - distance * sign

                @pl.when((block >= 0) & (block < n))
                def _():
                    slot = slot_of(block)
                    wz_copy(which, n - 1 - slot).wait_recv()

                    @pl.loop(1, w_parts)
                    def _(k):
                        wp_copy(which, slot, k, w_mine).start()

    def weights_arrived(which, slot):
        @pl.loop(1, w_parts)
        def _(k):
            wp_copy(which, slot, k, (w_mine + k) % w_parts).wait_recv()

    def row_copy(slot, side):
        return pltpu.make_async_remote_copy(
            src_ref=row_send.at[slot, side], dst_ref=row_recv.at[slot, 1 - side],
            send_sem=row_ssem.at[slot, side], recv_sem=row_rsem.at[slot, 1 - side],
            device_id=(z, before if side == 0 else after), device_id_type=MESH)

    def send_rows(slot, ref):
        for side, start in ((0, 0), (1, cells - wide)):
            row_send[slot, side] = ref[start:start + wide, :]
            row_copy(slot, side).start()

    def take_rows(slot, ref):
        for side in range(2):
            row_copy(slot, 1 - side).wait_recv()
            ref[cells + side * wide:cells + (side + 1) * wide, :] = row_recv[slot, side]

    def st_copy(slot, k, whose):
        return pltpu.make_async_remote_copy(
            src_ref=st_send.at[slot], dst_ref=st_recv.at[slot, whose],
            send_sem=st_ssem.at[slot, k], recv_sem=st_rsem.at[slot, whose],
            device_id=(z, (s + k) % s_count), device_id_type=MESH)

    def send_stats(slot, values):
        for i, v in enumerate(values):
            st_send[slot, i:i + 1, :] = v
        for k in range(1, s_count):
            st_copy(slot, k, s).start()
        st_recv[slot, s] = st_send[slot]

    def take_stats(slot):
        for k in range(1, s_count):
            st_copy(slot, k, (s + k) % s_count).wait_recv()

    strip = 8
    column = lax.broadcasted_iota(jnp.int32, (strip * wide, ch), 0) % wide

    def shift(target, first, count):
        size = count * wide
        where = column[:size]
        here = pad[pl.ds(8 + first * wide, size), :]
        left = jnp.where(where == 0, 0.0, pad[pl.ds(7 + first * wide, size), :])
        right = jnp.where(where == wide - 1, 0.0, pad[pl.ds(9 + first * wide, size), :])
        for b, v in enumerate((left, here, right)):
            target[pl.ds(first, count), :, b * ch:(b + 1) * ch] = v.astype(BF16).reshape(count, wide, ch)

    edge = 2 * wide
    ag_rows = ((0, edge + packed), (edge + packed, packed))
    band_rows = rows // HALVES

    def unpack_half(ph, block, q, target):
        if q == 0:
            pad[8:8 + wide, :] = hold[ph, block, 0:wide, :].astype(F32)
            pad[8 + wide + cells:8 + 2 * wide + cells, :] = hold[ph, block, wide:edge, :].astype(F32)
            shift(target, 0, 1)
            shift(target, rows + 1, 1)
        pad[8 + wide + q * band:8 + wide + (q + 1) * band, :] = dot(
            unpack[q], hold[ph, block, edge + q * packed:edge + (q + 1) * packed, :])

        for i in range(band_rows // strip):
            shift(target, 1 + q * band_rows + i * strip, strip)

    def add_conv(q, field, taps):
        first, last = (0, band_rows - 1) if q == 0 else (band_rows - 1, rows)
        count = last - first
        lhs = field[first:last + 2, :, :].reshape((count + 2) * wide, 3 * ch)
        value = dot(lhs, jnp.concatenate([taps(a) for a in range(3)], axis=1))
        at = pl.ds(first * wide, count * wide)
        acc[at, :] = acc[at, :] + sum(
            value[a * wide:(a + count) * wide, a * ch:(a + 1) * ch] for a in range(3))

    def ag_copy(ph, block, q, sign):
        at = pl.ds(*ag_rows[q])
        return pltpu.make_async_remote_copy(
            src_ref=hold.at[ph, block, at, :], dst_ref=hold.at[ph, block, at, :],
            send_sem=ag_ssem.at[ph, (1 - sign) // 2, block, q], recv_sem=ag_rsem.at[ph, block, q],
            device_id=(z + sign, s), device_id_type=MESH)

    def pack_field(ph, source, fill=None, first=None):
        if fill is not None:
            fill(cells, edge, 0)
        hold[ph, z, 0:edge, :] = source[cells:cells + edge, :].astype(BF16)
        for q in range(HALVES):
            if first is not None:
                first(q)
            if fill is not None:
                chunked(fill, 0, q * band, band)
            hold[ph, z, edge + q * packed:edge + (q + 1) * packed, :] = dot(
                pack[q], source[q * band:(q + 1) * band, :].astype(BF16)).astype(BF16)
            for sign in (1, -1):
                @pl.when((z + sign >= 0) & (z + sign < n))
                def _():
                    ag_copy(ph, z, q, sign).start()

    def inside(slice_at):
        return (slice_at >= 0) & (slice_at < n)

    def take_and_pass(ph, k, q, sign, passes=True, takes=True):
        block = z - k * sign

        @pl.when((k > 0) & inside(block))
        def _():
            if passes and takes:
                ag_copy(ph, block, q, sign).wait_recv()

            @pl.when(inside(z + sign))
            def _():
                if passes:
                    if not takes:
                        ag_copy(ph, block, q, sign).wait_recv()
                    ag_copy(ph, block, q, sign).start()

            if not passes:
                @pl.when(jnp.logical_not(inside(z + sign)))
                def _():
                    ag_copy(ph, block, q, sign).wait_recv()

    near = jnp.where(z < n - n // 2, 1, 0)

    def consume_way(k, q, way, consume):
        block = z - k * (1 - 2 * way)

        @pl.when((k >= 0) & (k < n) & inside(block) & ((k > 0) | (way == near)))
        def _():
            consume(k, block, q)

    def take_both(ph, k, q, **how):
        @pl.loop(0, 2)
        def _(i):
            way = (near + i) % 2
            take_and_pass(ph, k, q, 1 - 2 * way, **how)

    def gather(ph, consume, each):
        @pl.loop(0, n)
        def _(k):
            for q in range(HALVES):
                take_both(ph, k, q)
                if q:
                    consume_way(k, q - 1, 1 - near, consume)
                else:
                    consume_way(k - 1, HALVES - 1, 1 - near, consume)
                consume_way(k, q, near, consume)
            each(k)

    def gather_passing_first(ph, consume, each):
        @pl.loop(0, n)
        def _(k):
            @pl.when(k == 1)
            def _():
                @pl.loop(1, n)
                def _(ahead):
                    for q in range(HALVES):
                        take_both(ph, ahead, q, takes=False)
            for q in range(HALVES):
                take_both(ph, k, q, passes=False)

                @pl.loop(0, 2)
                def _(i):
                    consume_way(k, q, (near + i) % 2, consume)
            each(k)

    last_pass = jnp.maximum(jnp.where(z < n - 1, z, 0), jnp.where(z > 0, n - 1 - z, 0))

    def forward(ph, field):
        def consume(k, block, q):
            into = taken.at[block]
            unpack_half(ph, block, q, into)

            @pl.when(k == 0)
            def _():
                add_conv(q, into, lambda a: wv[ph, z, 3 * a * ch:3 * (a + 1) * ch, :])

            @pl.when(k > 0)
            def _():
                slot = slot_of(block)
                if q == 0:
                    weights_arrived(ph, slot)
                add_conv(q, into, lambda a: wf[ph, slot, 3 * a * ch:3 * (a + 1) * ch, :])

        def each(k):
            if ph == 0:
                @pl.when(k == 0)
                def _():
                    weights_round(0)

            @pl.when(k == last_pass)
            def _():
                turn_weights(ph)
                turn_field(ph, field)
                if ph == 0:
                    load_cotangent()
        (gather if ph else gather_passing_first)(ph, consume, each)

    def turn_field(ph, field):
        for a in range(3):
            for start in range(0, cells, ch):
                first = start + (a - 1) * wide
                if first < 0:
                    v = jnp.concatenate([field[cells:cells + wide, :], field[0:first + ch, :]], axis=0)
                elif first + ch > cells:
                    v = jnp.concatenate([field[first:cells, :], field[cells + wide:total, :]], axis=0)
                else:
                    v = field[first:first + ch, :]
                x_t[ph, a * ch:(a + 1) * ch, start:start + ch] = v.T.astype(BF16)

    def turn_weights(ph):
        @pl.loop(0, n)
        def _(d):
            for t in range(9):
                a, b = 2 - t // 3, 2 - t % 3
                wt[ph, d, a, b * ch:(b + 1) * ch, :] = wv[ph, d, t * ch:(t + 1) * ch, :].T

    half_rows = tap_rows // 2
    owners = math.gcd(half_rows // 16, chips)
    piece = half_rows // owners

    def c_copy(ph, j):
        return pltpu.make_async_remote_copy(
            src_ref=psend.at[ph, j], dst_ref=crecv.at[ph, j],
            send_sem=c_ssem.at[ph, j], recv_sem=c_rsem.at[ph, j],
            device_id=(z, chip * 2 + 1 - core), device_id_type=MESH)

    def q_copy(ph, j, e, whose, owner):
        return pltpu.make_async_remote_copy(
            src_ref=hsend.at[ph, j, owner], dst_ref=qrecv.at[ph, j, whose],
            send_sem=q_ssem.at[ph, j, e], recv_sem=q_rsem.at[ph, j, whose],
            device_id=(z, ((chip + e) % chips) * 2 + core), device_id_type=MESH)

    def f_copy(ph, j, e, owner):
        return pltpu.make_async_remote_copy(
            src_ref=wout.at[ph, j, core, owner], dst_ref=wout.at[ph, j, core, owner],
            send_sem=f_ssem.at[ph, j, e], recv_sem=f_rsem.at[ph, j, owner],
            device_id=(z, ((chip + e) % chips) * 2 + core), device_id_type=MESH)

    def h_copy(ph, j, whose):
        return pltpu.make_async_remote_copy(
            src_ref=wout.at[ph, j, whose], dst_ref=wout.at[ph, j, whose],
            send_sem=h_ssem.at[ph, j], recv_sem=h_rsem.at[ph, j],
            device_id=(z, chip * 2 + 1 - core), device_id_type=MESH)

    def o_copy(ph, j):
        target = (out_wg1, out_wg2)[ph]
        if aligned:
            target = target.at[:, :, :, pl.ds(pl.multiple_of(j * ch, ch), ch)]
        else:
            target = target.at[j]
        return pltpu.make_async_copy(wout.at[ph, j], target, o_sem.at[ph, j])

    def sum_cores(ph, j):
        for o in range(owners):
            psend[ph, j, o] = part[ph, j, 1 - core, o].astype(BF16)
        c_copy(ph, j).start()

    def sum_chips(ph, j):
        c_copy(ph, j).wait_recv()
        for o in range(owners):
            v = part[ph, j, core, o] + crecv[ph, j, o].astype(F32)
            part[ph, j, core, o] = v
            hsend[ph, j, o] = v.astype(BF16)

        @pl.loop(1, chips)
        def _(e):
            peer = (chip + e) % chips

            @pl.when(peer < owners)
            def _():
                q_copy(ph, j, e, chip, peer).start()

    def spread_chips(ph, j):
        @pl.when(chip < owners)
        def _():
            @pl.loop(1, chips)
            def _(e):
                q_copy(ph, j, e, (chip + e) % chips, chip).wait_recv()
            v = part[ph, j, core, chip]
            for e in range(1, chips):
                v = v + qrecv[ph, j, (chip + e) % chips].astype(F32)
            wout[ph, j, core, chip] = v.astype(BF16)

            @pl.loop(1, chips)
            def _(e):
                f_copy(ph, j, e, chip).start()

    def spread_cores(ph, j):
        @pl.loop(1, chips)
        def _(e):
            peer = (chip + e) % chips

            @pl.when(peer < owners)
            def _():
                f_copy(ph, j, e, peer).wait_recv()
        h_copy(ph, j, core).start()

    def finish(ph, j):
        h_copy(ph, j, 1 - core).wait_recv()
        o_copy(ph, j).start()

    def put_part(ph, j, tap, value):
        start = tap * ch
        done = 0
        while done < ch:
            row = start + done
            side, o, at = row // half_rows, row % half_rows // piece, row % piece
            size = min(ch - done, piece - at)
            part[ph, j, side, o, at:at + size, :] = value[done:done + size, :]
            done += size

    stages = (sum_cores, sum_chips, spread_chips, spread_cores, finish)

    def of_step(k, fn):
        @pl.loop(0, 2)
        def _(way):
            block = z - k * (1 - 2 * way)

            @pl.when((k >= 0) & (k < n) & inside(block) & ((k > 0) | (way == 0)))
            def _():
                fn(block)

    passing = last_pass > 0

    def made_at(step):
        first = jnp.where(passing & (step > 0), jnp.where(step == last_pass, 1, step + 1), step)
        return first, step + 1

    def advance(ph, k):
        for age in range(1, len(stages)):
            step = k - age

            @pl.when((step >= 0) & (step < n))
            def _():
                @pl.loop(*made_at(step))
                def _(made):
                    of_step(made, functools.partial(stages[age], ph))

    def advance_all(ph, age):
        @pl.loop(0, n)
        def _(j):
            stages[age](ph, j)

    def field_grad(ph, block):
        grad = taken[block, 1:rows + 1, :, :].reshape(cells, 3 * ch)
        value = dot(x_t[ph], grad)
        for a in range(3):
            for b in range(3):
                put_part(ph, block, 3 * a + b, value[a * ch:(a + 1) * ch, (2 - b) * ch:(3 - b) * ch])

    def make_grad(ph, block):
        field_grad(ph, block)
        sum_cores(ph, block)

    def backward(ph):
        last = ph == 0

        def consume(k, block, q):
            into = taken.at[block]
            unpack_half(2 + ph, block, q, into)
            if last and q == HALVES - 1:
                @pl.when((k == 0) | (k >= last_pass))
                def _():
                    make_grad(ph, block)
            add_conv(q, into, lambda a: wt[ph, block, a])

        def each(k):
            first, end = made_at(k)
            if last:
                @pl.loop(first, end - 1)
                def _(step):
                    of_step(step, functools.partial(make_grad, ph))
                advance(ph, k)
                for age in range(2, len(stages)):
                    @pl.when(k == age - 2)
                    def _():
                        advance_all(1, age)
            else:
                @pl.loop(first, jnp.where(passing | (k < n - 1), end, first))
                def _(step):
                    of_step(step, functools.partial(make_grad, ph))

                @pl.when(k == last_pass)
                def _():
                    to_flat(hid2, out_block)
        gather(2 + ph, consume, each)

    def fold(v):
        return jnp.sum(v.reshape(v.shape[0] // 8, 8, ch), axis=0)

    def flatten(v):
        return jnp.sum(v, axis=0, keepdims=True)

    zero = jnp.zeros((8, ch), F32)

    def local_moments(ref):
        def sums(start, size, carry):
            at = pl.ds(start, size)
            m = mask[at, :]
            return carry[0] + fold(ref[at, :] * m), carry[1] + fold(m)
        added, number = (flatten(v) for v in chunked(sums, (zero, zero)))
        middle = added / jnp.maximum(number, 1.0)

        def spread(start, size, carry):
            at = pl.ds(start, size)
            c = (ref[at, :] - middle) * mask[at, :]
            return carry + fold(c * c)
        return added, number, flatten(chunked(spread, zero))

    def moments(slot):
        take_stats(slot)
        got = [st_recv[slot, k] for k in range(s_count)]
        added = sum(g[0:1] for g in got)
        number = sum(g[1:2] for g in got)
        mean = added / number
        spread = 0.0
        for g in got:
            off = g[0:1] / jnp.maximum(g[1:2], 1.0) - mean
            spread = spread + (g[2:3] + g[1:2] * off * off)
        return mean, lax.rsqrt(spread / number + EPSILON), number

    def everywhere(fn):
        chunked(fn, 0)
        fn(cells, 2 * wide, 0)

    gain1, shift1, gain2, shift2 = (r[...] for r in (gain1_in, shift1_in, gain2_in, shift2_in))

    weights_over_z(0)

    below = lax.broadcasted_iota(jnp.int32, (band, band), 1) < lax.broadcasted_iota(jnp.int32, (band, band), 0)
    below = below.astype(F32).astype(BF16)

    def make_pack(h):
        lv = mask[h * band:(h + 1) * band, :]
        place = jnp.where(lv > 0.0, dot(below, lv.astype(BF16)), -1.0)
        places[h] = place
        across = place.T[0:1, :]
        spot = lax.broadcasted_iota(jnp.int32, (packed, band), 0).astype(F32)
        pack[h] = jnp.where(spot == across, 1.0, 0.0).astype(BF16)

    def make_unpack(h):
        for start in range(0, packed, ch):
            size = min(ch, packed - start)
            spot = start + lax.broadcasted_iota(jnp.int32, (band, size), 1)
            unpack[h, :, start:start + size] = jnp.where(
                places[h, :, :size] == spot.astype(F32), 1.0, 0.0).astype(BF16)

    for side in range(2):
        edge_copy(1 - side).wait_recv()
        there = jnp.where(s > 0, 1.0, 0.0) if side == 0 else jnp.where(s < s_count - 1, 1.0, 0.0)
        at = slice(cells + side * wide, cells + (side + 1) * wide)
        masked[at, :] = edge_recv[side, 0].astype(F32) * there
        mask[at, :] = edge_recv[side, 1].astype(F32) * there

    pack_field(0, masked, first=make_pack)
    for h in range(HALVES):
        make_unpack(h)
    forward(0, masked)
    weights_over_z(1)
    send_rows(0, acc)
    send_stats(0, local_moments(acc))
    mean1, scale1, count = moments(0)
    weights_round(1)

    def activate_one(start, size, carry):
        at = pl.ds(start, size)
        main = start is not cells
        nv = ((acc if main else normed1)[at, :] - mean1) * scale1
        normed1[at, :] = nv
        hid[at, :] = gelu_parts(nv * gain1 + shift1)[0] * mask[at, :]
        if main:
            acc[at, :] = jnp.zeros((size, ch), F32)
        return carry

    def slope_one(start, size, carry):
        at = pl.ds(start, size)
        slope1[at, :] = gelu_parts(normed1[at, :] * gain1 + shift1)[1] * mask[at, :]
        return carry

    take_rows(0, normed1)
    pack_field(1, hid, activate_one)
    everywhere(slope_one)
    forward(1, hid)
    send_rows(1, acc)
    send_stats(1, local_moments(acc))
    mean2, scale2, _ = moments(1)

    def activate_two(source, start, size):
        at = pl.ds(start, size)
        nv = (source[at, :] - mean2) * scale2
        normed2[at, :] = nv
        value, slope = gelu_parts(nv * gain2 + shift2 + masked[at, :])
        t = cotm[at, :] * slope
        through[at, :] = t
        return value, nv, t

    def activate_main(start, size, carry):
        value, nv, t = activate_two(acc, start, size)
        at = pl.ds(start, size)
        hid2[at, :] = value * mask[at, :]
        acc[at, :] = jnp.zeros((size, ch), F32)
        return carry[0] + fold(t * nv), carry[1] + fold(t)

    send_stats(2, [flatten(v) for v in chunked(activate_main, (zero, zero))])
    take_rows(1, normed2)
    take_cotangent()
    activate_two(normed2, cells, edge)

    def gradient_sums(slot):
        take_stats(slot)
        got = [st_recv[slot, k] for k in range(s_count)]
        return sum(g[0:1] for g in got), sum(g[1:2] for g in got)

    def norm_back(upstream, normed, gain, scale, sums):
        gain_grad, shift_grad = sums
        factor = gain * scale
        level, tilt = shift_grad / count, gain_grad / count

        def fill(start, size, carry):
            at = pl.ds(start, size)
            v = upstream[at, :] - mask[at, :] * (level + normed[at, :] * tilt)
            hid[at, :] = factor * v
            return carry
        return fill

    sums2 = gradient_sums(2)
    pack_field(3, hid, norm_back(through, normed2, gain2, scale2, sums2))
    backward(1)

    send_rows(2, acc)

    def inner_main(start, size, carry):
        at = pl.ds(start, size)
        v = acc[at, :] * slope1[at, :]
        slope1[at, :] = v
        acc[at, :] = jnp.zeros((size, ch), F32)
        return carry[0] + fold(v * normed1[at, :]), carry[1] + fold(v)

    send_stats(3, [flatten(v) for v in chunked(inner_main, (zero, zero))])

    @pl.when(jnp.logical_not(passing))
    def _():
        of_step(n - 1, functools.partial(make_grad, 1))
    for side in range(2):
        row_copy(2, 1 - side).wait_recv()
        at = slice(cells + side * wide, cells + (side + 1) * wide)
        slope1[at, :] = row_recv[2, side] * slope1[at, :]
    sums1 = gradient_sums(3)
    pack_field(2, hid, norm_back(slope1, normed1, gain1, scale1, sums1))
    advance_all(1, 1)
    backward(0)
    advance(0, n)

    def finish_input(start, size, carry):
        at = pl.ds(start, size)
        acc[at, :] = (acc[at, :] + through[at, :]) * mask[at, :]
        return carry

    chunked(finish_input, 0)
    to_flat(acc, out_input)
    out_gain1[...], out_shift1[...] = sums1
    out_gain2[...], out_shift2[...] = sums2
    for extra in range(1, len(stages) - 1):
        advance(0, n + extra)

    for side in range(2):
        edge_copy(side).wait_send()
        cot_copy(side).wait_send()
        for slot in range(3):
            row_copy(slot, side).wait_send()

    @pl.loop(1, s_count)
    def _(k):
        for slot in range(4):
            st_copy(slot, k, s).wait_send()

    @pl.loop(1, n)
    def _(k):
        for which in range(2):
            wz_copy(which, k).wait_send()

    @pl.loop(1, w_parts)
    def _(k):
        for which in range(2):
            for slot in range(n - 1):
                wp_copy(which, slot, k, w_mine).wait_send()

    @pl.loop(0, n)
    def _(k):
        for sign in (1, -1):
            block = z - k * sign

            @pl.when((block >= 0) & (block < n) & (z + sign >= 0) & (z + sign < n))
            def _():
                for ph in range(4):
                    for q in range(HALVES):
                        ag_copy(ph, block, q, sign).wait_send()

    @pl.loop(0, n)
    def _(j):
        for ph in range(2):
            c_copy(ph, j).wait_send()
            h_copy(ph, j, core).wait_send()
            o_copy(ph, j).wait()

            @pl.loop(1, chips)
            def _(e):
                peer = (chip + e) % chips

                @pl.when(peer < owners)
                def _():
                    q_copy(ph, j, e, chip, peer).wait_send()

                @pl.when(chip < owners)
                def _():
                    f_copy(ph, j, e, chip).wait_send()


def finish_kernel(count, *refs):
    ins, outs = refs[:count], refs[count:2 * count]
    narrow, wide, in_sem, out_sem, take_sem, give_sem = refs[2 * count:2 * count + 6]
    held = refs[2 * count + 6:]
    rows = narrow.shape[1] // FINISH_PARTS
    parts = [(w, i, pl.ds(i * rows, rows)) for i in range(FINISH_PARTS) for w in range(2)]
    loads = [pltpu.make_async_copy(ins[w].at[at, :], narrow.at[w, at, :], in_sem.at[w, i]) for w, i, at in parts]
    stores = [pltpu.make_async_copy(wide.at[w, at, :], outs[w].at[at, :], out_sem.at[w, i]) for w, i, at in parts]
    takes = [pltpu.make_async_copy(ins[2 + k], v, take_sem.at[k]) for k, v in enumerate(held)]
    gives = [pltpu.make_async_copy(v, outs[2 + k], give_sem.at[k]) for k, v in enumerate(held)]
    for copy in loads + takes:
        copy.start()
    for load, store, (w, i, at) in zip(loads, stores, parts):
        load.wait()
        wide[w, at, :] = narrow[w, at, :].astype(F32)
        store.start()
    for take, give in zip(takes, gives):
        take.wait()
        give.start()
    for copy in stores + gives:
        copy.wait()


def per_device(n, s_count, blocks, weight_one, weight_two, gain_one, shift_one, gain_two, shift_two, cell_live, cotangent):
    rows, wide = cell_live.shape
    ch = blocks.shape[1] // wide
    cells = rows * wide
    total = cells + 2 * wide
    packed = -(-most_live(rows // HALVES, wide) // 16) * 16
    aligned = ch % 128 == 0
    chips = s_count // 2
    tap_rows = 9 * ch
    half_rows = tap_rows // 2
    owners = math.gcd(half_rows // 16, chips)
    piece = half_rows // owners

    if aligned:
        weight_one, weight_two = (w.reshape(tap_rows, n * ch) for w in (weight_one, weight_two))
    else:
        weight_one, weight_two = (
            w.reshape(tap_rows, n, ch).transpose(1, 0, 2) for w in (weight_one, weight_two))
    grad_shape = (2, owners, piece, n * ch) if aligned else (n, 2, owners, piece, ch)
    vmem = pl.BlockSpec(memory_space=pltpu.VMEM)
    hbm = pl.BlockSpec(memory_space=pl.ANY)
    sem = pltpu.SemaphoreType.DMA
    field = pltpu.VMEM((total, ch), F32)
    scratch = [
        pltpu.VMEM((ch * wide, 128), F32),
        pltpu.VMEM((2, n, tap_rows, ch), BF16),
        pltpu.VMEM((2, n - 1, tap_rows, ch), BF16),
        pltpu.VMEM((2, n, 3, 3 * ch, ch), BF16),
        pltpu.VMEM((2, 3 * ch, cells), BF16),
        pltpu.VMEM((HALVES, packed, cells // HALVES), BF16),
        pltpu.VMEM((HALVES, cells // HALVES, packed), BF16),
        pltpu.VMEM((HALVES, cells // HALVES, ch), F32),
        pltpu.VMEM((2, 2, wide, ch), BF16),
        pltpu.VMEM((2, 2, wide, ch), BF16),
        pltpu.VMEM((2, wide, ch), BF16),
        pltpu.VMEM((2, wide, ch), BF16),
        field, field, field, field, field, field, field, field, field,
        pltpu.VMEM((total + 16, ch), F32),
        pltpu.VMEM((cells, ch), F32),
        pltpu.VMEM((4, n, 2 * wide + HALVES * packed, ch), BF16),
        pltpu.VMEM((n, rows + 2, wide, 3 * ch), BF16),
        pltpu.VMEM((2, n, 2, owners, piece, ch), F32),
        pltpu.VMEM((2, n, owners, piece, ch), BF16),
        pltpu.VMEM((2, n, owners, piece, ch), BF16),
        pltpu.VMEM((2, n, owners, piece, ch), BF16),
        pltpu.VMEM((2, n, chips, piece, ch), BF16),
        pltpu.VMEM((2, n, 2, owners, piece, ch), BF16),
        pltpu.VMEM((4, 8, ch), F32),
        pltpu.VMEM((4, s_count, 8, ch), F32),
        pltpu.VMEM((3, 2, wide, ch), F32),
        pltpu.VMEM((3, 2, wide, ch), F32),
        sem((2, n)),
        sem((2, n)), sem((2, n)),
        sem((2, n - 1, s_count)), sem((2, n - 1, s_count)),
        sem((2,)), sem((2,)),
        sem((2,)), sem((2,)),
        sem((4, 2, n, HALVES)), sem((4, n, HALVES)),
        sem((4, s_count)), sem((4, s_count)),
        sem((3, 2)), sem((3, 2)),
        sem((2, n)), sem((2, n)),
        sem((2, n, chips)), sem((2, n, chips)),
        sem((2, n, chips)), sem((2, n, chips)),
        sem((2, n)), sem((2, n)),
        sem((2, n)),
    ]
    block_out, input_grad, wg1, wg2, *sums = pl.pallas_call(
        functools.partial(block_kernel, n, s_count, rows, wide, ch, aligned, packed),
        out_shape=(
            jax.ShapeDtypeStruct((rows, ch * wide), BF16),
            jax.ShapeDtypeStruct((rows, ch * wide), F32),
            jax.ShapeDtypeStruct(grad_shape, BF16),
            jax.ShapeDtypeStruct(grad_shape, BF16),
            *[jax.ShapeDtypeStruct((1, ch), F32)] * 4,
        ),
        in_specs=[vmem] * 7 + [hbm] * 2,
        out_specs=(vmem, vmem, hbm, hbm, vmem, vmem, vmem, vmem),
        scratch_shapes=scratch,
        compiler_params=pltpu.CompilerParams(
            collective_id=0, has_side_effects=True, vmem_limit_bytes=60 * 1024 * 1024),
    )(blocks, cotangent, cell_live.T,
      *(v.reshape(1, ch) for v in (gain_one, shift_one, gain_two, shift_two)), weight_one, weight_two)

    if not aligned:
        def whole(grad):
            grad = grad.reshape(n, tap_rows, ch).transpose(1, 0, 2)
            return grad.astype(F32).reshape(9, ch, n * ch)
        return (block_out, input_grad, whole(wg1), whole(wg2), *(v.reshape(ch) for v in sums))

    wg1, wg2 = (w.reshape(tap_rows, n * ch) for w in (wg1, wg2))
    wide_grad = jax.ShapeDtypeStruct((tap_rows, n * ch), F32)
    moved = (block_out, input_grad, *sums)
    grad1, grad2, *moved = pl.pallas_call(
        functools.partial(finish_kernel, 2 + len(moved)),
        out_shape=(wide_grad, wide_grad, *(jax.ShapeDtypeStruct(v.shape, v.dtype) for v in moved)),
        in_specs=[pl.BlockSpec(memory_space=pl.ANY)] * (2 + len(moved)),
        out_specs=[pl.BlockSpec(memory_space=pl.ANY)] * (2 + len(moved)),
        scratch_shapes=[
            pltpu.VMEM((2, tap_rows, n * ch), BF16), pltpu.VMEM((2, tap_rows, n * ch), F32),
            sem((2, FINISH_PARTS)), sem((2, FINISH_PARTS)), sem((len(moved),)), sem((len(moved),)),
            *(pltpu.VMEM(v.shape, v.dtype) for v in moved),
        ],
        compiler_params=pltpu.CompilerParams(vmem_limit_bytes=64 * 1024 * 1024),
    )(wg1, wg2, *moved)
    block_out, input_grad, *sums = moved
    grads = (g.reshape(9, ch, n * ch) for g in (grad1, grad2))
    return (block_out, input_grad, *grads, *(v.reshape(ch) for v in sums))


def solution(mesh):
    return jax.shard_map(
        functools.partial(per_device, mesh.shape["chan"], mesh.shape["space"]),
        mesh=mesh,
        in_specs=(
            P("space", "chan"),
            P(None, "chan", None),
            P(None, "chan", None),
            P("chan"),
            P("chan"),
            P("chan"),
            P("chan"),
            P("space", None),
            P("space", "chan"),
        ),
        out_specs=(
            P("space", "chan"),
            P("space", "chan"),
            P(None, "chan", None),
            P(None, "chan", None),
            P("chan"),
            P("chan"),
            P("chan"),
            P("chan"),
        ),
        check_vma=False,
    )
```

```python
import functools
import math

import jax
import jax.numpy as jnp
from jax import lax
from jax.experimental import pallas as pl
from jax.experimental.pallas import tpu as pltpu
from jax.sharding import PartitionSpec as P

EPSILON = 1e-05
MESH = pl.DeviceIdType.MESH
F32 = jnp.float32
BF16 = jnp.bfloat16
ROOT_HALF = 0.7071067811865476
ROOT_TWO_PI = 0.3989422804014327
CHUNK = 64
FINISH_PARTS = 4
UNROLL = 2
PLAIN_HALVES = 2
SCRATCH_LIMIT = 56 * 1024 * 1024
LARGE, SMALL = 7, 3


def dot(a, b):
    return jnp.dot(a, b, preferred_element_type=F32)


def gelu_parts(v):
    upper = 0.5 * (1.0 + lax.erf(v * ROOT_HALF))
    slope = upper + v * (ROOT_TWO_PI * jnp.exp(-0.5 * v * v))
    return v * upper, slope


def most_live(rows, wide):
    units = (wide + 1) // (SMALL + 1)
    live_rows = rows - rows // (LARGE + 1)
    return min(rows * wide, math.ceil(units * live_rows * LARGE / 2))


def packed_rows(rows, wide):
    return -(-most_live(rows, wide) // 16) * 16


def block_kernel(n, s_count, rows, wide, ch, aligned, packed, *refs):
    (x_in, cot_in, live_in, gain1_in, shift1_in, gain2_in, shift2_in, w1_hbm, w2_hbm) = refs[:9]
    (out_block, out_input, out_wg1, out_wg2, out_gain1, out_shift1, out_gain2, out_shift2) = refs[9:17]
    (turned, wv, wf, wvb, wt1, wt2, x_t1, x_t2, pack, unpack, places,
     masked, cot, mask, edge_send, edge_recv, cedge_send, cedge_recv, par_send, par_recv,
     mask_c, masked_c, cot_c, normed1, normed2, through, slope1, hid, block_c, pad, acc,
     hold0, hold1, hold3, taken, cot_send, cot_recv, ret_send, ret_recv, thr_n, blk_n,
     part, psend, crecv, hsend, qrecv, zz_send, zz_recv, wout, st_send, st_recv, row_send, row_recv, norm, scales,
     w_sem, wz_ssem, wz_rsem, wp_ssem, wp_rsem, wh_ssem, wh_rsem, e_ssem, e_rsem, ce_ssem, ce_rsem,
     par_ssem, par_rsem, a_ssem, a_rsem, b_ssem, b_rsem, ag_ssem, ag_rsem, cx_ssem, cx_rsem, ret_ssem, ret_rsem,
     st_ssem, st_rsem, row_ssem, row_rsem, c_ssem, c_rsem, q_ssem, q_rsem,
     f_ssem, f_rsem, h_ssem, h_rsem, zz_ssem, zz_rsem, o_sem) = refs[17:]

    parts = n // 2
    z = lax.axis_index("chan")
    s = lax.axis_index("space")
    m, p = z % 2, z // 2
    twin = z + 1 - 2 * m
    cells = rows * wide
    part_rows = rows // parts
    pc = part_rows * wide
    edge = 2 * wide
    pt = pc + edge
    core, chip, chips = s % 2, s // 2, s_count // 2
    before, after = (s + s_count - 1) % s_count, (s + 1) % s_count
    tap_rows = 9 * ch
    half_rows = tap_rows // 2
    owners = math.gcd(half_rows // 16, chips)
    piece = half_rows // owners

    def remote(src, dst, send, recv, at_z, at_s):
        return pltpu.make_async_remote_copy(
            src_ref=src, dst_ref=dst, send_sem=send, recv_sem=recv,
            device_id=(at_z, at_s), device_id_type=MESH)

    def inside(at):
        return (at >= 0) & (at < n)

    barrier = pltpu.get_barrier_semaphore()
    family = parts * s_count

    @pl.loop(1, family)
    def _(k):
        to = (2 * ((p + k // s_count) % parts) + m, (s + k % s_count) % s_count)
        pl.semaphore_signal(barrier, inc=1, device_id=to, device_id_type=MESH)

    @pl.loop(0, parts)
    def _(q):
        pl.semaphore_signal(barrier, inc=1, device_id=(2 * q + 1 - m, s), device_id_type=MESH)

    def place_of(block):
        return block % 2 * parts + block // 2

    w_copies = []
    for which, source in enumerate((w1_hbm, w2_hbm)):
        for d in range(n):
            block = source.at[:, d * ch:(d + 1) * ch] if aligned else source.at[d]
            w_copies.append(pltpu.make_async_copy(block, wv.at[which, place_of(d)], w_sem.at[which, d]))
    for copy in w_copies:
        copy.start()

    def chunked(fn, init, count=pc):
        def step(i, carry):
            return fn(pl.multiple_of(i * CHUNK, CHUNK), CHUNK, carry)
        return lax.fori_loop(0, count // CHUNK, step, init, unroll=UNROLL)

    lanes = 128
    tiles = ch * wide // lanes

    def from_flat(flat, put):
        for i in range(tiles):
            turned[i * lanes:(i + 1) * lanes, 0:rows] = flat[:, i * lanes:(i + 1) * lanes].astype(F32).T
        for w in range(wide):
            put(pl.ds(w, rows, stride=wide), turned[pl.ds(w, ch, stride=wide), 0:rows].T)

    def to_flat(source, flat):
        for w in range(wide):
            turned[pl.ds(w, ch, stride=wide), 0:rows] = source[pl.ds(w, rows, stride=wide), :].T
        for i in range(tiles):
            flat[:, i * lanes:(i + 1) * lanes] = turned[i * lanes:(i + 1) * lanes, 0:rows].T.astype(flat.dtype)

    def put_masked(at, value):
        masked[at, :] = value

    from_flat(x_in, put_masked)

    cell = lax.broadcasted_iota(jnp.int32, (cells, rows), 0)
    pick = (cell // wide == lax.broadcasted_iota(jnp.int32, (cells, rows), 1)).astype(F32).astype(BF16)
    column_of = lax.broadcasted_iota(jnp.int32, (cells, wide), 0) % wide
    picked = lax.dot_general(pick, live_in[...].astype(BF16), (((1,), (1,)), ((), ())), preferred_element_type=F32)
    picked = jnp.where(column_of == lax.broadcasted_iota(jnp.int32, (cells, wide), 1), picked, 0.0)
    mask[0:cells, :] = dot(picked.astype(BF16), jnp.ones((wide, ch), BF16))

    def load_main(start, size, carry):
        at = pl.ds(start, size)
        masked[at, :] = masked[at, :] * mask[at, :]
        return carry

    chunked(load_main, 0, cells)
    for side, start in ((0, 0), (1, cells - wide)):
        edge_send[side, 0] = masked[start:start + wide, :].astype(BF16)
        edge_send[side, 1] = mask[start:start + wide, :].astype(BF16)
    acc[...] = jnp.zeros_like(acc)
    st_send[...] = jnp.zeros_like(st_send)
    par_send[...] = jnp.zeros_like(par_send)
    for i, given in enumerate((gain1_in, shift1_in, gain2_in, shift2_in)):
        par_send[i:i + 1, :] = given[...]
    par_recv[p] = par_send[...]

    pl.semaphore_wait(barrier, family - 1 + parts)

    def edge_copy(side):
        return remote(edge_send.at[side], edge_recv.at[1 - side], e_ssem.at[side], e_rsem.at[1 - side],
                      z, before if side == 0 else after)

    def cedge_copy(side):
        return remote(cedge_send.at[side], cedge_recv.at[1 - side], ce_ssem.at[side], ce_rsem.at[1 - side],
                      z, before if side == 0 else after)

    for side in range(2):
        edge_copy(side).start()

    def others(fn):
        @pl.loop(1, parts)
        def _(k):
            fn((p + k) % parts)

    def par_copy(other, whose):
        return remote(par_send, par_recv.at[whose], par_ssem.at[other], par_rsem.at[whose], 2 * other + m, s)

    group = chip - chip % owners
    my_rows = pl.ds(core * half_rows + (chip % owners) * piece, piece)

    def slot_of(block):
        return (block - z + n - 1) % n

    def wz_copy(which, k):
        to = (z + k) % n
        slot = n - k - 1
        return remote(wv.at[which, pl.ds(to % 2 * parts, parts), my_rows, :], wf.at[which, slot, :, my_rows, :],
                      wz_ssem.at[which * (n - 1) + slot], wz_rsem.at[which * (n - 1) + slot], to, s)

    def wb_copy(other, whose):
        base = 2 * (n - 1)
        return remote(wv.at[1, :, my_rows, :], wvb.at[whose, :, my_rows, :],
                      wz_ssem.at[base + other], wz_rsem.at[base + whose], 2 * other + m, s)

    def forward_weights(which, slot):
        return wf.at[which, slot], which * (n - 1) + slot

    def backward_weights(other):
        return wvb.at[other], 2 * (n - 1) + other

    def wp_copy(view, index, k, whose):
        at = pl.ds(core * half_rows + whose * piece, piece)
        to = group + (chip + k) % owners
        return remote(view.at[:, at, :], view.at[:, at, :], wp_ssem.at[index, k], wp_rsem.at[index, whose], z, to * 2 + core)

    def wh_copy(view, index, whose):
        at = pl.ds(whose * half_rows, half_rows)
        return remote(view.at[:, at, :], view.at[:, at, :], wh_ssem.at[index], wh_rsem.at[index], z, chip * 2 + 1 - core)

    def round_chips(view, index):
        @pl.loop(1, owners)
        def _(k):
            wp_copy(view, index, k, chip % owners).start()

    def round_cores(view, index):
        @pl.loop(1, owners)
        def _(k):
            wp_copy(view, index, k, (chip + k) % owners).wait_recv()
        wh_copy(view, index, core).start()

    def round_done(view, index):
        wh_copy(view, index, 1 - core).wait_recv()

    def weights_over_z(which):
        @pl.loop(1, n)
        def _(k):
            wz_copy(which, k).start()

    def nth_block(i):
        low = jnp.minimum(z, n - 1 - z)
        turn = i % 2 * 2 - 1
        return jnp.where(i <= 2 * low, z + turn * ((i + 1) // 2), z + jnp.where(z < parts, 1, -1) * (i - low))

    def weights_round(which):
        @pl.loop(1, n)
        def _(i):
            slot = slot_of(nth_block(i))
            wz_copy(which, n - 1 - slot).wait_recv()
            round_chips(*forward_weights(which, slot))

    def row_copy(slot, side):
        if side == 0:
            to_p, to_s = jnp.where(p == 0, parts - 1, p - 1), jnp.where(p == 0, before, s)
        else:
            to_p, to_s = jnp.where(p == parts - 1, 0, p + 1), jnp.where(p == parts - 1, after, s)
        return remote(row_send.at[slot, side], row_recv.at[slot, 1 - side], row_ssem.at[slot, side],
                      row_rsem.at[slot, 1 - side], 2 * to_p + m, to_s)

    def send_rows(slot, ref):
        for side, start in ((0, 0), (1, pc - wide)):
            row_send[slot, side] = ref[:, start:start + wide, :]
            row_copy(slot, side).start()

    def take_rows(slot, ref):
        for side in range(2):
            row_copy(slot, 1 - side).wait_recv()
            ref[:, pc + side * wide:pc + (side + 1) * wide, :] = row_recv[slot, side]

    def st_copy(slot, k, whose):
        to_p, to_s = (p + k // s_count) % parts, (s + k % s_count) % s_count
        return remote(st_send.at[slot], st_recv.at[slot, whose], st_ssem.at[slot, k], st_rsem.at[slot, whose],
                      2 * to_p + m, to_s)

    me = p * s_count + s

    def send_stats(slot, values):
        for i, v in enumerate(values):
            st_send[slot, i:i + 1, :] = v

        @pl.loop(1, family)
        def _(k):
            st_copy(slot, k, me).start()
        st_recv[slot, me] = st_send[slot]

    def take_stats(slot):
        @pl.loop(1, family)
        def _(k):
            st_copy(slot, k, (p + k // s_count) % parts * s_count + (s + k % s_count) % s_count).wait_recv()
        return [st_recv[slot, k] for k in range(family)]

    strip = 8
    column = lax.broadcasted_iota(jnp.int32, (strip * wide, ch), 0) % wide

    def shift(target, first, count):
        size = count * wide
        where = column[:size]
        here = pad[pl.ds(8 + first * wide, size), :]
        left = jnp.where(where == 0, 0.0, pad[pl.ds(7 + first * wide, size), :])
        right = jnp.where(where == wide - 1, 0.0, pad[pl.ds(9 + first * wide, size), :])
        for b, v in enumerate((left, here, right)):
            target[pl.ds(first, count), :, b * ch:(b + 1) * ch] = v.astype(BF16).reshape(count, wide, ch)

    def unpack_chunk(chunk, q):
        pad[8:8 + wide, :] = chunk[0:wide, :].astype(F32)
        pad[8 + wide + pc:8 + edge + pc, :] = chunk[wide:edge, :].astype(F32)
        pad[8 + wide:8 + wide + pc, :] = dot(unpack[q], chunk[edge:edge + packed, :])

    def make_taps(chunk, q, target):
        unpack_chunk(chunk, q)
        shift(target, 0, 1)
        for i in range(part_rows // strip):
            shift(target, 1 + i * strip, strip)
        shift(target, part_rows + 1, 1)

    def from_pad(ref):
        ref[0:pc, :] = pad[8 + wide:8 + wide + pc, :]
        ref[pc:pc + wide, :] = pad[8:8 + wide, :]
        ref[pc + wide:pt, :] = pad[8 + wide + pc:8 + edge + pc, :]

    def rows_of(q):
        return pl.ds(pl.multiple_of(q * pc, pc), pc)

    def rows_around(q):
        above = jnp.where(q == 0, cells, q * pc - wide)
        below = jnp.where(q == parts - 1, cells + wide, (q + 1) * pc)
        return tuple(pl.ds(pl.multiple_of(at, wide), wide) for at in (above, below))

    def make_chunk(q, source, chunk):
        above, below = rows_around(q)
        chunk[0:wide, :] = source[above, :].astype(BF16)
        chunk[wide:edge, :] = source[below, :].astype(BF16)
        chunk[edge:edge + packed, :] = dot(pack[q], source[rows_of(q), :].astype(BF16)).astype(BF16)

    def own_part(source, target):
        above, below = rows_around(p)
        target[0:pc, :] = source[rows_of(p), :]
        target[pc:pc + wide, :] = source[above, :]
        target[pc + wide:pt, :] = source[below, :]

    def add_conv(target, field, taps):
        lhs = field[...].reshape((part_rows + 2) * wide, 3 * ch)
        value = dot(lhs, jnp.concatenate([taps(a) for a in range(3)], axis=1))
        target[...] = target[...] + sum(
            value[a * wide:a * wide + pc, a * ch:(a + 1) * ch] for a in range(3))

    def tap_rows_of(view):
        return lambda a: view[3 * a * ch:3 * (a + 1) * ch, :]

    def a_copy(j, q, sign):
        return remote(hold0.at[j, q], hold0.at[j, q], a_ssem.at[(1 - sign) // 2, j, q], a_rsem.at[j, q], z + sign, s)

    def wanted(q, sign, at):
        return inside(at) & ((2 * q + 1 >= at) if sign > 0 else (2 * q <= at))

    def pass_on(k):
        for sign in (1, -1):
            block = z - k * sign
            for q in range(parts):
                @pl.when(inside(block) & wanted(q, sign, z + sign))
                def _():
                    a_copy(block, q, sign).wait_recv()
                    a_copy(block, q, sign).start()

    def first_taps(block):
        into = taken.at[block % 2, block // 2]
        make_taps(hold0.at[block, p], p, into)

        @pl.when(block % 2 == m)
        def _():
            from_pad(masked_c.at[block // 2])
        return into

    def b_copy(ph, mm, u):
        return remote(hold1.at[ph, mm, u], hold1.at[ph, mm, u], b_ssem.at[ph, u], b_rsem.at[ph, u], twin, s)

    def pack_own(ph, fill):
        for k in range(parts):
            u = (p + k) % parts
            fill(u)
            chunk = hold1.at[ph, m, u]
            chunk[0:edge, :] = hid[u, pc:pt, :].astype(BF16)
            chunk[edge:edge + packed, :] = dot(pack[p], hid[u, 0:pc, :].astype(BF16)).astype(BF16)
            b_copy(ph, m, u).start()

    def everywhere(fn, u):
        chunked(functools.partial(fn, u), 0)
        fn(u, pc, edge, 0)

    def turn_weights(source, target):
        @pl.loop(0, n)
        def _(d):
            for t in range(9):
                a, b = 2 - t // 3, 2 - t % 3
                target[d, a, b * ch:(b + 1) * ch, :] = source[place_of(d), t * ch:(t + 1) * ch, :].T

    def turn_field(main, above, below, target):
        for a in range(3):
            for start in range(0, pc, ch):
                first = start + (a - 1) * wide
                if first < 0:
                    v = jnp.concatenate([above(), main(0, first + ch)], axis=0)
                elif first + ch > pc:
                    v = jnp.concatenate([main(first, pc), below()], axis=0)
                else:
                    v = main(first, first + ch)
                target[a * ch:(a + 1) * ch, start:start + ch] = v.T.astype(BF16)

    def turn_input():
        @pl.loop(0, parts)
        def _(q):
            above, below = rows_around(q)
            turn_field(lambda i, j: masked[pl.ds(pl.multiple_of(q * pc + i, wide), j - i), :],
                       lambda: masked[above, :], lambda: masked[below, :], x_t1.at[q])

    def turn_hidden():
        for u in range(parts):
            turn_field(lambda i, j: hid[u, i:j, :], lambda: hid[u, pc:pc + wide, :],
                       lambda: hid[u, pc + wide:pt, :], x_t2.at[u])

    def load_cotangent():
        def put(at, value):
            cot[at, :] = value
        from_flat(cot_in, put)

        def live_only(start, size, carry):
            at = pl.ds(start, size)
            cot[at, :] = cot[at, :] * mask[at, :]
            return carry
        chunked(live_only, 0, cells)
        for side, start in ((0, 0), (1, cells - wide)):
            cedge_send[side] = cot[start:start + wide, :].astype(BF16)
            cedge_copy(side).start()

    def cx_copy(other, whose):
        return remote(cot_send.at[other], cot_recv.at[whose], cx_ssem.at[other], cx_rsem.at[whose], 2 * other + m, s)

    def exchange_cotangent():
        for side in range(2):
            cedge_copy(1 - side).wait_recv()
            at = slice(cells + side * wide, cells + (side + 1) * wide)
            cot[at, :] = cedge_recv[side].astype(F32) * mask[at, :]

        def send(other):
            make_chunk(other, cot, cot_send.at[other])
            cx_copy(other, p).start()
        others(send)
        own_part(cot, cot_c.at[p])

    def take_cotangent():
        def take(other):
            cx_copy(other, other).wait_recv()
            unpack_chunk(cot_recv.at[other], p)
            from_pad(cot_c.at[other])
        others(take)

    def ret_copy(kind, other, whose):
        return remote(ret_send.at[kind, other], ret_recv.at[kind, whose],
                      ret_ssem.at[kind, other], ret_rsem.at[kind, whose], 2 * other + m, s)

    def give_back():
        def send(other):
            for kind, source in enumerate((block_c, through)):
                ret_send[kind, other] = dot(pack[p], source[other, 0:pc, :].astype(BF16)).astype(BF16)
                ret_copy(kind, other, p).start()
        others(send)
        for source, target in ((block_c, blk_n), (through, thr_n)):
            target[rows_of(p), :] = source[p, 0:pc, :]

    def take_back():
        def take(other):
            for kind, target in enumerate((blk_n, thr_n)):
                ret_copy(kind, other, other).wait_recv()
                target[rows_of(other), :] = dot(unpack[other], ret_recv[kind, other])
        others(take)
        to_flat(blk_n, out_block)

    def c_copy(unit):
        return remote(psend.at[unit], crecv.at[unit], c_ssem.at[unit], c_rsem.at[unit], z, chip * 2 + 1 - core)

    def q_copy(unit, e, whose, owner):
        return remote(hsend.at[unit, owner], qrecv.at[unit, whose], q_ssem.at[unit, e], q_rsem.at[unit, whose],
                      z, ((chip + e) % chips) * 2 + core)

    def zz_copy(u, j, whose):
        return remote(zz_send.at[u, j], zz_recv.at[whose, j], zz_ssem.at[u, j], zz_rsem.at[whose, j], 2 * u + m, s)

    def f_copy(which, j, e, owner):
        return remote(wout.at[which, j, core, owner], wout.at[which, j, core, owner],
                      f_ssem.at[which, j, e], f_rsem.at[which, j, owner], z, ((chip + e) % chips) * 2 + core)

    def h_copy(which, j, whose):
        return remote(wout.at[which, j, whose], wout.at[which, j, whose],
                      h_ssem.at[which, j], h_rsem.at[which, j], z, chip * 2 + 1 - core)

    def o_copy(which, j):
        target = (out_wg1, out_wg2)[which]
        if aligned:
            target = target.at[:, :, :, pl.ds(pl.multiple_of(j * ch, ch), ch)]
        else:
            target = target.at[j]
        return pltpu.make_async_copy(wout.at[which, j], target, o_sem.at[which, j])

    def put_part(unit, tap, value):
        start = tap * ch
        done = 0
        while done < ch:
            row = start + done
            side, o, at = row // half_rows, row % half_rows // piece, row % piece
            size = min(ch - done, piece - at)
            part[unit, side, o, at:at + size, :] = value[done:done + size, :]
            done += size

    def put_grad(unit, value):
        for a in range(3):
            for b in range(3):
                put_part(unit, 3 * a + b, value[a * ch:(a + 1) * ch, (2 - b) * ch:(3 - b) * ch])

    def centre(mm, u):
        return taken[mm, u, 1:part_rows + 1, :, :].reshape(pc, 3 * ch)

    def sum_cores(unit):
        for o in range(owners):
            psend[unit, o] = part[unit, 1 - core, o].astype(BF16)
        c_copy(unit).start()

    def sum_chips(unit):
        c_copy(unit).wait_recv()
        for o in range(owners):
            v = part[unit, core, o] + crecv[unit, o].astype(F32)
            part[unit, core, o] = v
            hsend[unit, o] = v.astype(BF16)

        @pl.loop(1, chips)
        def _(e):
            peer = (chip + e) % chips

            @pl.when(peer < owners)
            def _():
                q_copy(unit, e, chip, peer).start()

    def plane_sum(unit):
        @pl.loop(1, chips)
        def _(e):
            q_copy(unit, e, (chip + e) % chips, chip).wait_recv()
        v = part[unit, core, chip]
        for e in range(1, chips):
            v = v + qrecv[unit, (chip + e) % chips].astype(F32)
        return v

    def spread_chips(which, j, v):
        wout[which, j, core, chip] = v.astype(BF16)

        @pl.loop(1, chips)
        def _(e):
            f_copy(which, j, e, chip).start()

    def if_owner(fn):
        pl.when(chip < owners)(fn)

    def spread_first(j):
        @if_owner
        def _():
            spread_chips(0, j, plane_sum(j))

    def unit_of(u, j):
        return n + u * n + j

    def sum_planes(u, j):
        @if_owner
        def _():
            v = plane_sum(unit_of(u, j))

            @pl.when(u == p)
            def _():
                part[unit_of(u, j), core, chip] = v

            @pl.when(u != p)
            def _():
                zz_send[u, j] = v.astype(BF16)
                zz_copy(u, j, p).start()

    def spread_second(j):
        @if_owner
        def _():
            @pl.loop(1, parts)
            def _(k):
                other = (p + k) % parts
                zz_copy(other, j, other).wait_recv()
            v = part[unit_of(p, j), core, chip]
            for k in range(1, parts):
                v = v + zz_recv[(p + k) % parts, j].astype(F32)
            spread_chips(1, j, v)

    def spread_cores(which, j):
        @pl.loop(1, chips)
        def _(e):
            peer = (chip + e) % chips

            @pl.when(peer < owners)
            def _():
                f_copy(which, j, e, peer).wait_recv()
        h_copy(which, j, core).start()

    def finish(which, j):
        h_copy(which, j, 1 - core).wait_recv()
        o_copy(which, j).start()

    def fold(v):
        return jnp.sum(v.reshape(v.shape[0] // 8, 8, ch), axis=0)

    def flatten(v):
        return jnp.sum(v, axis=0, keepdims=True)

    zero = jnp.zeros((8, ch), F32)

    def local_moments():
        def count(start, size, carry):
            return carry + fold(mask_c[pl.ds(start, size), :])
        number = flatten(chunked(count, zero))
        values = [number]
        for u in range(parts):
            def sums(start, size, carry):
                at = pl.ds(start, size)
                return carry + fold(acc[u, at, :] * mask_c[at, :])
            added = flatten(chunked(sums, zero))
            middle = added / jnp.maximum(number, 1.0)

            def spread(start, size, carry):
                at = pl.ds(start, size)
                c = (acc[u, at, :] - middle) * mask_c[at, :]
                return carry + fold(c * c)
            values += [added, flatten(chunked(spread, zero))]
        return values

    def moments(got):
        number = sum(g[0:1] for g in got)
        for u in range(parts):
            mean = sum(g[1 + 2 * u:2 + 2 * u] for g in got) / number
            spread = 0.0
            for g in got:
                off = g[1 + 2 * u:2 + 2 * u] / jnp.maximum(g[0:1], 1.0) - mean
                spread = spread + (g[2 + 2 * u:3 + 2 * u] + g[0:1] * off * off)
            norm[0, u] = mean
            norm[1, u] = lax.rsqrt(spread / number + EPSILON)
        return number

    def gradient_sums(got):
        for i in range(2 * parts):
            norm[2 + i % 2, i // 2] = sum(g[i:i + 1] for g in got)

    weight_waits = [lambda which=which: [c.wait() for c in w_copies[which * n:(which + 1) * n]] for which in range(2)]
    weight_waits[0]()
    weights_over_z(0)
    others(lambda other: par_copy(other, p).start())

    below = lax.broadcasted_iota(jnp.int32, (pc, pc), 1) < lax.broadcasted_iota(jnp.int32, (pc, pc), 0)
    below = below.astype(F32).astype(BF16)

    @pl.loop(0, parts)
    def _(q):
        lv = mask[rows_of(q), :]
        place = jnp.where(lv > 0.0, dot(below, lv.astype(BF16)), -1.0)
        places[q] = place
        across = place.T[0:1, :]
        spot = lax.broadcasted_iota(jnp.int32, (packed, pc), 0).astype(F32)
        pack[q] = jnp.where(spot == across, 1.0, 0.0).astype(BF16)

    for side in range(2):
        edge_copy(1 - side).wait_recv()
        there = jnp.where(s > 0, 1.0, 0.0) if side == 0 else jnp.where(s < s_count - 1, 1.0, 0.0)
        at = slice(cells + side * wide, cells + (side + 1) * wide)
        masked[at, :] = edge_recv[side, 0].astype(F32) * there
        mask[at, :] = edge_recv[side, 1].astype(F32) * there

    @pl.loop(0, parts)
    def _(i):
        q = jnp.where(z < parts, parts - 1 - i, i)
        make_chunk(q, masked, hold0.at[z, q])
        for sign in (1, -1):
            @pl.when(inside(z + sign) & ((2 * q + 1 >= z + sign) if sign > 0 else (2 * q <= z + sign)))
            def _():
                a_copy(z, q, sign).start()

    @pl.loop(0, parts)
    def _(q):
        for start in range(0, packed, ch):
            size = min(ch, packed - start)
            spot = start + lax.broadcasted_iota(jnp.int32, (pc, size), 1)
            unpack[q, :, start:start + size] = jnp.where(
                places[q, :, :size] == spot.astype(F32), 1.0, 0.0).astype(BF16)
    own_part(mask, mask_c)

    into = first_taps(z)
    for u in range(parts):
        add_conv(acc.at[u], into, tap_rows_of(wv.at[0, m * parts + u]))
    weights_round(0)
    pass_on(1)
    turn_weights(wv.at[0], wt1)
    for k in range(2, n):
        pass_on(k)

    @pl.loop(1, n)
    def _(i):
        block = nth_block(i)
        view, index = forward_weights(0, slot_of(block))
        round_cores(view, index)

        @pl.when(i == 1)
        def _():
            turn_input()

        @pl.when(i == 2)
        def _():
            load_cotangent()
        passed = jnp.where(block < z, jnp.where(wanted(p, 1, z + 1), 1, 0), jnp.where(wanted(p, -1, z - 1), 1, 0))

        @pl.when(passed == 0)
        def _():
            a_copy(block, p, 1).wait_recv()
        taps = first_taps(block)
        round_done(view, index)
        for u in range(parts):
            add_conv(acc.at[u], taps, tap_rows_of(wf.at[0, slot_of(block), u]))

    send_rows(0, acc)
    send_stats(0, local_moments())
    weight_waits[1]()
    weights_over_z(1)
    exchange_cotangent()
    others(lambda other: par_copy(other, other).wait_recv())
    got = take_stats(0)
    count = moments(got)
    weights_round(1)
    others(lambda other: wb_copy(other, p).start())

    def params(u):
        return [par_recv[u, i:i + 1, :] for i in range(4)]

    def activate_one(u, start, size, carry):
        at = pl.ds(start, size)
        main = start is not pc
        gain, shift_by = params(u)[:2]
        nv = ((acc if main else normed1)[u, at, :] - norm[0, u]) * norm[1, u]
        normed1[u, at, :] = nv
        hid[u, at, :] = gelu_parts(nv * gain + shift_by)[0] * mask_c[at, :]
        if main:
            acc[u, at, :] = jnp.zeros((size, ch), F32)
        return carry

    def slope_one(u, start, size, carry):
        at = pl.ds(start, size)
        gain, shift_by = params(u)[:2]
        slope1[u, at, :] = gelu_parts(normed1[u, at, :] * gain + shift_by)[1] * mask_c[at, :]
        return carry

    norm1_scale = [None] * parts
    for u in range(parts):
        norm1_scale[u] = norm[1, u]

    take_rows(0, normed1)
    pack_own(0, functools.partial(everywhere, activate_one))

    @pl.loop(0, 2 * parts)
    def _(i):
        mm = jnp.where(i < parts, m, 1 - m)
        u = (p + i % parts) % parts
        into = taken.at[mm, u]

        @pl.when(i >= parts)
        def _():
            b_copy(0, mm, u).wait_recv()
        make_taps(hold1.at[0, mm, u], p, into)

        @pl.when(i == 0)
        def _():
            for v in range(parts):
                add_conv(acc.at[v], into, tap_rows_of(wv.at[1, m * parts + v]))
            everywhere(slope_one, 0)
            for v in range(1, parts):
                everywhere(slope_one, v)

        @pl.when(i > 0)
        def _():
            slot = slot_of(2 * u + mm)
            view, index = forward_weights(1, slot)
            round_cores(view, index)
            round_done(view, index)
            for v in range(parts):
                add_conv(acc.at[v], into, tap_rows_of(wf.at[1, slot, v]))

    send_rows(1, acc)
    send_stats(1, local_moments())

    def wb_round(other):
        wb_copy(other, other).wait_recv()
        round_chips(*backward_weights(other))
    others(wb_round)
    take_cotangent()
    turn_hidden()
    moments(take_stats(1))

    def activate_two(u, start, size, source):
        at = pl.ds(start, size)
        gain, shift_by = params(u)[2:]
        nv = (source[u, at, :] - norm[0, u]) * norm[1, u]
        normed2[u, at, :] = nv
        value, slope = gelu_parts(nv * gain + shift_by + masked_c[u, at, :])
        t = cot_c[u, at, :] * slope
        through[u, at, :] = t
        return value, nv, t

    def activate_main(u, start, size, carry):
        value, nv, t = activate_two(u, start, size, acc)
        at = pl.ds(start, size)
        block_c[u, at, :] = value * mask_c[at, :]
        acc[u, at, :] = jnp.zeros((size, ch), F32)
        return carry[0] + fold(t * nv), carry[1] + fold(t)

    sums = []
    for u in range(parts):
        sums += [flatten(v) for v in chunked(functools.partial(activate_main, u), (zero, zero))]
    send_stats(2, sums)
    take_rows(1, normed2)
    for u in range(parts):
        activate_two(u, pc, edge, normed2)
    others(lambda other: round_cores(*backward_weights(other)))

    @pl.loop(0, parts)
    def _(u):
        @pl.when(u == p)
        def _():
            turn_weights(wv.at[1], wt2.at[u])

    def norm_back(upstream, normed, gain_at, scale):
        def fill(u, start, size, carry):
            at = pl.ds(start, size)
            factor = params(u)[gain_at] * scale[u]
            v = upstream[u, at, :] - mask_c[at, :] * (
                norm[3, u] / count + normed[u, at, :] * (norm[2, u] / count))
            hid[u, at, :] = factor * v
            return carry
        return fill

    gradient_sums(take_stats(2))
    for u in range(parts):
        scales[0, u] = norm1_scale[u]
        scales[1, u] = norm[1, u]
    out_gain2[...], out_shift2[...] = norm[2, p], norm[3, p]

    pack_own(1, functools.partial(everywhere, norm_back(through, normed2, 2, scales.at[1])))
    give_back()

    def turn_other(other):
        round_done(*backward_weights(other))
        turn_weights(wvb.at[other], wt2.at[other])

    def second_grads(mm, u):
        j = 2 * u + mm
        for v in range(parts):
            unit = unit_of(v, j)
            put_grad(unit, dot(x_t2[v], centre(mm, u)))
            sum_cores(unit)

    @pl.loop(0, 2 * parts)
    def _(i):
        mm = jnp.where(i < parts, m, 1 - m)
        u = (p + i % parts) % parts

        @pl.when(i >= parts)
        def _():
            b_copy(1, mm, u).wait_recv()
        into = taken.at[mm, u]
        make_taps(hold1.at[1, mm, u], p, into)

        @pl.when(i == 0)
        def _():
            others(turn_other)
        for v in range(parts):
            add_conv(acc.at[v], into, lambda a: wt2[v, 2 * u + mm, a])

        @pl.when(i < parts)
        def _():
            second_grads(mm, u)

    send_rows(2, acc)

    def inner_main(u, start, size, carry):
        at = pl.ds(start, size)
        v = acc[u, at, :] * slope1[u, at, :]
        slope1[u, at, :] = v
        acc[u, at, :] = jnp.zeros((size, ch), F32)
        return carry[0] + fold(v * normed1[u, at, :]), carry[1] + fold(v)

    sums = []
    for u in range(parts):
        sums += [flatten(v) for v in chunked(functools.partial(inner_main, u), (zero, zero))]
    send_stats(3, sums)
    for u in range(parts):
        second_grads(1 - m, u)

    def by_parity(mm, fn):
        for v in range(1, parts + 1):
            for u in range(parts):
                fn((p + v) % parts, 2 * u + mm)

    by_parity(m, lambda v, j: sum_chips(unit_of(v, j)))
    for side in range(2):
        row_copy(2, 1 - side).wait_recv()
        at = slice(pc + side * wide, pc + (side + 1) * wide)
        slope1[:, at, :] = row_recv[2, side] * slope1[:, at, :]
    gradient_sums(take_stats(3))
    out_gain1[...], out_shift1[...] = norm[2, p], norm[3, p]

    def ag_copy(block, q, sign):
        return remote(hold3.at[block, q], hold3.at[block, q], ag_ssem.at[(1 - sign) // 2, block, q],
                      ag_rsem.at[block, q], z + sign, s)

    fill = norm_back(slope1, normed1, 0, scales.at[0])
    for u in range(parts):
        everywhere(fill, u)
        chunk = hold3.at[z, u]
        chunk[0:edge, :] = hid[u, pc:pt, :].astype(BF16)
        chunk[edge:edge + packed, :] = dot(pack[p], hid[u, 0:pc, :].astype(BF16)).astype(BF16)
        for sign in (1, -1):
            @pl.when(inside(z + sign))
            def _():
                ag_copy(z, u, sign).start()
    by_parity(1 - m, lambda v, j: sum_chips(unit_of(v, j)))

    last_pass = jnp.maximum(jnp.where(z < n - 1, z, 0), jnp.where(z > 0, n - 1 - z, 0))

    def made_at(mm):
        return jnp.maximum(jnp.maximum(jnp.abs(mm - z), jnp.abs(2 * (parts - 1) + mm - z)), last_pass)

    def first_grad(mm, u):
        j = 2 * u + mm
        put_grad(j, sum(dot(x_t1[q], centre(2 * q + mm, u)) for q in range(parts)))
        sum_cores(j)

    first_stages = (sum_chips, spread_first, functools.partial(spread_cores, 0), functools.partial(finish, 0))

    def advance(k):
        @pl.loop(0, 2)
        def _(mm):
            made = made_at(mm)
            for age, stage in enumerate(first_stages):
                @pl.when(made + age + 1 == k)
                def _():
                    @pl.loop(0, parts)
                    def _(u):
                        stage(2 * u + mm)

    @pl.loop(0, n)
    def _(k):
        for q in range(parts):
            for sign in (1, -1):
                block = z - k * sign

                @pl.when((k > 0) & inside(block))
                def _():
                    ag_copy(block, q, sign).wait_recv()

                    @pl.when(inside(z + sign))
                    def _():
                        ag_copy(block, q, sign).start()

            @pl.loop(0, 2)
            def _(way):
                block = z - k * (1 - 2 * way)

                @pl.when(inside(block) & ((k > 0) | (way == 0)))
                def _():
                    into = taken.at[block, q]
                    make_taps(hold3.at[block, q], block // 2, into)
                    add_conv(acc.at[block // 2], into, lambda a: wt1[2 * q + block % 2, a])

        @pl.loop(0, 2)
        def _(mm):
            @pl.when(made_at(mm) == k)
            def _():
                @pl.loop(0, parts)
                def _(u):
                    first_grad(mm, u)
        advance(k)

        @pl.when(k == jnp.maximum(last_pass, 1))
        def _():
            for mm in range(2):
                by_parity(jnp.abs(m - mm), sum_planes)

        @pl.when(k == last_pass)
        def _():
            take_back()

        @pl.when(k == n - 1)
        def _():
            @pl.loop(0, n)
            def _(j):
                spread_second(j)

    advance(n)

    def finish_input(start, size, carry):
        at = pl.ds(start, size)
        thr_n[at, :] = (acc[start // pc, pl.ds(pl.multiple_of(start % pc, CHUNK), size), :] + thr_n[at, :]) * mask[at, :]
        return carry

    chunked(finish_input, 0, cells)
    to_flat(thr_n, out_input)

    @pl.loop(0, n)
    def _(j):
        spread_cores(1, j)
    advance(n + 1)

    @pl.loop(0, n)
    def _(j):
        finish(1, j)
    for extra in range(2, len(first_stages)):
        advance(n + extra)

    for side in range(2):
        edge_copy(side).wait_send()
        cedge_copy(side).wait_send()
        for slot in range(3):
            row_copy(slot, side).wait_send()

    def sent_to(other):
        par_copy(other, p).wait_send()
        cx_copy(other, p).wait_send()
        wb_copy(other, p).wait_send()
        for kind in range(2):
            ret_copy(kind, other, p).wait_send()

        @if_owner
        def _():
            @pl.loop(0, n)
            def _(j):
                zz_copy(other, j, p).wait_send()
    others(sent_to)

    @pl.loop(1, family)
    def _(k):
        for slot in range(4):
            st_copy(slot, k, me).wait_send()

    @pl.loop(0, parts)
    def _(u):
        for ph in range(2):
            b_copy(ph, m, u).wait_send()

    def weights_sent(view, index):
        @pl.loop(1, owners)
        def _(k):
            wp_copy(view, index, k, chip % owners).wait_send()
        wh_copy(view, index, core).wait_send()

    @pl.loop(1, n)
    def _(k):
        for which in range(2):
            wz_copy(which, k).wait_send()
            weights_sent(*forward_weights(which, n - k - 1))
    others(lambda other: weights_sent(*backward_weights(other)))

    @pl.loop(0, n)
    def _(k):
        for sign in (1, -1):
            block = z - k * sign

            @pl.when(inside(block) & inside(z + sign))
            def _():
                for q in range(parts):
                    ag_copy(block, q, sign).wait_send()

                    @pl.when(wanted(q, sign, z + sign))
                    def _():
                        a_copy(block, q, sign).wait_send()

    @pl.loop(0, n + parts * n)
    def _(unit):
        c_copy(unit).wait_send()

        @pl.loop(1, chips)
        def _(e):
            peer = (chip + e) % chips

            @pl.when(peer < owners)
            def _():
                q_copy(unit, e, chip, peer).wait_send()

    @pl.loop(0, n)
    def _(j):
        for which in range(2):
            h_copy(which, j, core).wait_send()
            o_copy(which, j).wait()

            @if_owner
            def _():
                @pl.loop(1, chips)
                def _(e):
                    f_copy(which, j, e, chip).wait_send()


def plain_kernel(n, s_count, rows, wide, ch, aligned, packed, *refs):
    (x_in, cot_in, live_in, gain1_in, shift1_in, gain2_in, shift2_in, w1_hbm, w2_hbm) = refs[:9]
    (out_block, out_input, out_wg1, out_wg2, out_gain1, out_shift1, out_gain2, out_shift2) = refs[9:17]
    (turned, wv, wf, wt, x_t, pack, unpack, places, edge_send, edge_recv, cot_send, cot_recv, cotm, mask, masked,
     normed1, normed2, through, slope1, hid, hid2, pad, acc, hold, taken,
     part, psend, crecv, hsend, qrecv, wout, st_send, st_recv, row_send, row_recv,
     w_sem, wz_ssem, wz_rsem, wp_ssem, wp_rsem, e_ssem, e_rsem, ce_ssem, ce_rsem, ag_ssem, ag_rsem,
     st_ssem, st_rsem, row_ssem, row_rsem, c_ssem, c_rsem, q_ssem, q_rsem,
     f_ssem, f_rsem, h_ssem, h_rsem, o_sem) = refs[17:]

    z = lax.axis_index("chan")
    s = lax.axis_index("space")
    cells = rows * wide
    total = cells + 2 * wide
    band = cells // PLAIN_HALVES
    core, chip, chips = s % 2, s // 2, s_count // 2
    before, after = (s + s_count - 1) % s_count, (s + 1) % s_count
    tap_rows = 9 * ch

    barrier = pltpu.get_barrier_semaphore()

    @pl.loop(1, s_count)
    def _(k):
        pl.semaphore_signal(barrier, inc=1, device_id=(z, (s + k) % s_count), device_id_type=MESH)

    @pl.loop(1, n)
    def _(k):
        pl.semaphore_signal(barrier, inc=1, device_id=((z + k) % n, s), device_id_type=MESH)

    w_copies = []
    for which, source in enumerate((w1_hbm, w2_hbm)):
        for d in range(n):
            block = source.at[:, d * ch:(d + 1) * ch] if aligned else source.at[d]
            w_copies.append(pltpu.make_async_copy(block, wv.at[which, d], w_sem.at[which, d]))
    for copy in w_copies:
        copy.start()

    def chunked(fn, init, first=0, count=cells):
        def step(i, carry):
            return fn(pl.multiple_of(first + i * CHUNK, CHUNK), CHUNK, carry)
        return lax.fori_loop(0, count // CHUNK, step, init, unroll=UNROLL)

    lanes = 128
    tiles = ch * wide // lanes

    def from_flat(flat, put):
        for i in range(tiles):
            turned[i * lanes:(i + 1) * lanes, 0:rows] = flat[:, i * lanes:(i + 1) * lanes].astype(F32).T
        for w in range(wide):
            put(pl.ds(w, rows, stride=wide), turned[pl.ds(w, ch, stride=wide), 0:rows].T)

    def to_flat(source, flat):
        for w in range(wide):
            turned[pl.ds(w, ch, stride=wide), 0:rows] = source[pl.ds(w, rows, stride=wide), :].T
        for i in range(tiles):
            flat[:, i * lanes:(i + 1) * lanes] = turned[i * lanes:(i + 1) * lanes, 0:rows].T.astype(flat.dtype)

    def put_masked(at, value):
        masked[at, :] = value

    from_flat(x_in, put_masked)

    cell = lax.broadcasted_iota(jnp.int32, (cells, rows), 0)
    pick = (cell // wide == lax.broadcasted_iota(jnp.int32, (cells, rows), 1)).astype(F32).astype(BF16)
    column_of = lax.broadcasted_iota(jnp.int32, (cells, wide), 0) % wide
    picked = lax.dot_general(pick, live_in[...].astype(BF16), (((1,), (1,)), ((), ())), preferred_element_type=F32)
    picked = jnp.where(column_of == lax.broadcasted_iota(jnp.int32, (cells, wide), 1), picked, 0.0)
    mask[0:cells, :] = dot(picked.astype(BF16), jnp.ones((wide, ch), BF16))

    def load_main(start, size, carry):
        at = pl.ds(start, size)
        lv = mask[at, :]
        masked[at, :] = masked[at, :] * lv
        return carry

    chunked(load_main, 0)
    for side, start in ((0, 0), (1, cells - wide)):
        edge_send[side, 0] = masked[start:start + wide, :].astype(BF16)
        edge_send[side, 1] = mask[start:start + wide, :].astype(BF16)

    acc[...] = jnp.zeros_like(acc)
    st_send[...] = jnp.zeros_like(st_send)

    pl.semaphore_wait(barrier, s_count - 1 + n - 1)

    def edge_copy(side):
        return pltpu.make_async_remote_copy(
            src_ref=edge_send.at[side], dst_ref=edge_recv.at[1 - side],
            send_sem=e_ssem.at[side], recv_sem=e_rsem.at[1 - side],
            device_id=(z, before if side == 0 else after), device_id_type=MESH)

    for side in range(2):
        edge_copy(side).start()

    def cot_copy(side):
        return pltpu.make_async_remote_copy(
            src_ref=cot_send.at[side], dst_ref=cot_recv.at[1 - side],
            send_sem=ce_ssem.at[side], recv_sem=ce_rsem.at[1 - side],
            device_id=(z, before if side == 0 else after), device_id_type=MESH)

    def load_cotangent():
        def put(at, value):
            cotm[at, :] = value
        from_flat(cot_in, put)

        def live_only(start, size, carry):
            at = pl.ds(start, size)
            cotm[at, :] = cotm[at, :] * mask[at, :]
            return carry
        chunked(live_only, 0)
        for side, start in ((0, 0), (1, cells - wide)):
            cot_send[side] = cotm[start:start + wide, :].astype(BF16)
            cot_copy(side).start()

    def take_cotangent():
        for side in range(2):
            cot_copy(1 - side).wait_recv()
            at = slice(cells + side * wide, cells + (side + 1) * wide)
            cotm[at, :] = cot_recv[side].astype(F32) * mask[at, :]

    w_parts = math.gcd(tap_rows // 16, s_count)
    w_rows = tap_rows // w_parts
    w_mine = s % w_parts
    w_group = s - w_mine

    def wz_copy(which, k):
        at = pl.ds(w_mine * w_rows, w_rows)
        slot = n - k - 1
        return pltpu.make_async_remote_copy(
            src_ref=wv.at[which, (z + k) % n, at, :], dst_ref=wf.at[which, slot, at, :],
            send_sem=wz_ssem.at[which, slot], recv_sem=wz_rsem.at[which, slot],
            device_id=((z + k) % n, s), device_id_type=MESH)

    def wp_copy(which, slot, k, whose):
        at = pl.ds(whose * w_rows, w_rows)
        return pltpu.make_async_remote_copy(
            src_ref=wf.at[which, slot, at, :], dst_ref=wf.at[which, slot, at, :],
            send_sem=wp_ssem.at[which, slot, k], recv_sem=wp_rsem.at[which, slot, whose],
            device_id=(z, w_group + (w_mine + k) % w_parts), device_id_type=MESH)

    def weights_over_z(which):
        for copy in w_copies[which * n:(which + 1) * n]:
            copy.wait()

        @pl.loop(1, n)
        def _(k):
            wz_copy(which, k).start()

    def slot_of(block):
        return (block - z + n - 1) % n

    def weights_round(which):
        @pl.loop(1, n)
        def _(distance):
            for sign in (1, -1):
                block = z - distance * sign

                @pl.when((block >= 0) & (block < n))
                def _():
                    slot = slot_of(block)
                    wz_copy(which, n - 1 - slot).wait_recv()

                    @pl.loop(1, w_parts)
                    def _(k):
                        wp_copy(which, slot, k, w_mine).start()

    def weights_arrived(which, slot):
        @pl.loop(1, w_parts)
        def _(k):
            wp_copy(which, slot, k, (w_mine + k) % w_parts).wait_recv()

    def row_copy(slot, side):
        return pltpu.make_async_remote_copy(
            src_ref=row_send.at[slot, side], dst_ref=row_recv.at[slot, 1 - side],
            send_sem=row_ssem.at[slot, side], recv_sem=row_rsem.at[slot, 1 - side],
            device_id=(z, before if side == 0 else after), device_id_type=MESH)

    def send_rows(slot, ref):
        for side, start in ((0, 0), (1, cells - wide)):
            row_send[slot, side] = ref[start:start + wide, :]
            row_copy(slot, side).start()

    def take_rows(slot, ref):
        for side in range(2):
            row_copy(slot, 1 - side).wait_recv()
            ref[cells + side * wide:cells + (side + 1) * wide, :] = row_recv[slot, side]

    def st_copy(slot, k, whose):
        return pltpu.make_async_remote_copy(
            src_ref=st_send.at[slot], dst_ref=st_recv.at[slot, whose],
            send_sem=st_ssem.at[slot, k], recv_sem=st_rsem.at[slot, whose],
            device_id=(z, (s + k) % s_count), device_id_type=MESH)

    def send_stats(slot, values):
        for i, v in enumerate(values):
            st_send[slot, i:i + 1, :] = v
        for k in range(1, s_count):
            st_copy(slot, k, s).start()
        st_recv[slot, s] = st_send[slot]

    def take_stats(slot):
        for k in range(1, s_count):
            st_copy(slot, k, (s + k) % s_count).wait_recv()

    strip = 8
    column = lax.broadcasted_iota(jnp.int32, (strip * wide, ch), 0) % wide

    def shift(target, first, count):
        size = count * wide
        where = column[:size]
        here = pad[pl.ds(8 + first * wide, size), :]
        left = jnp.where(where == 0, 0.0, pad[pl.ds(7 + first * wide, size), :])
        right = jnp.where(where == wide - 1, 0.0, pad[pl.ds(9 + first * wide, size), :])
        for b, v in enumerate((left, here, right)):
            target[pl.ds(first, count), :, b * ch:(b + 1) * ch] = v.astype(BF16).reshape(count, wide, ch)

    edge = 2 * wide
    ag_rows = ((0, edge + packed), (edge + packed, packed))
    band_rows = rows // PLAIN_HALVES

    def unpack_half(ph, block, q, target):
        if q == 0:
            pad[8:8 + wide, :] = hold[ph, block, 0:wide, :].astype(F32)
            pad[8 + wide + cells:8 + 2 * wide + cells, :] = hold[ph, block, wide:edge, :].astype(F32)
            shift(target, 0, 1)
            shift(target, rows + 1, 1)
        pad[8 + wide + q * band:8 + wide + (q + 1) * band, :] = dot(
            unpack[q], hold[ph, block, edge + q * packed:edge + (q + 1) * packed, :])

        for i in range(band_rows // strip):
            shift(target, 1 + q * band_rows + i * strip, strip)

    def add_conv(q, field, taps):
        first, last = (0, band_rows - 1) if q == 0 else (band_rows - 1, rows)
        count = last - first
        lhs = field[first:last + 2, :, :].reshape((count + 2) * wide, 3 * ch)
        value = dot(lhs, jnp.concatenate([taps(a) for a in range(3)], axis=1))
        at = pl.ds(first * wide, count * wide)
        acc[at, :] = acc[at, :] + sum(
            value[a * wide:(a + count) * wide, a * ch:(a + 1) * ch] for a in range(3))

    def ag_copy(ph, block, q, sign):
        at = pl.ds(*ag_rows[q])
        return pltpu.make_async_remote_copy(
            src_ref=hold.at[ph, block, at, :], dst_ref=hold.at[ph, block, at, :],
            send_sem=ag_ssem.at[ph, (1 - sign) // 2, block, q], recv_sem=ag_rsem.at[ph, block, q],
            device_id=(z + sign, s), device_id_type=MESH)

    def pack_field(ph, source, fill=None, first=None):
        if fill is not None:
            fill(cells, edge, 0)
        hold[ph, z, 0:edge, :] = source[cells:cells + edge, :].astype(BF16)
        for q in range(PLAIN_HALVES):
            if first is not None:
                first(q)
            if fill is not None:
                chunked(fill, 0, q * band, band)
            hold[ph, z, edge + q * packed:edge + (q + 1) * packed, :] = dot(
                pack[q], source[q * band:(q + 1) * band, :].astype(BF16)).astype(BF16)
            for sign in (1, -1):
                @pl.when((z + sign >= 0) & (z + sign < n))
                def _():
                    ag_copy(ph, z, q, sign).start()

    def inside(slice_at):
        return (slice_at >= 0) & (slice_at < n)

    def take_and_pass(ph, k, q, sign, passes=True, takes=True):
        block = z - k * sign

        @pl.when((k > 0) & inside(block))
        def _():
            if passes and takes:
                ag_copy(ph, block, q, sign).wait_recv()

            @pl.when(inside(z + sign))
            def _():
                if passes:
                    if not takes:
                        ag_copy(ph, block, q, sign).wait_recv()
                    ag_copy(ph, block, q, sign).start()

            if not passes:
                @pl.when(jnp.logical_not(inside(z + sign)))
                def _():
                    ag_copy(ph, block, q, sign).wait_recv()

    near = jnp.where(z < n - n // 2, 1, 0)

    def consume_way(k, q, way, consume):
        block = z - k * (1 - 2 * way)

        @pl.when((k >= 0) & (k < n) & inside(block) & ((k > 0) | (way == near)))
        def _():
            consume(k, block, q)

    def take_both(ph, k, q, **how):
        @pl.loop(0, 2)
        def _(i):
            way = (near + i) % 2
            take_and_pass(ph, k, q, 1 - 2 * way, **how)

    def gather(ph, consume, each):
        @pl.loop(0, n)
        def _(k):
            for q in range(PLAIN_HALVES):
                take_both(ph, k, q)
                if q:
                    consume_way(k, q - 1, 1 - near, consume)
                else:
                    consume_way(k - 1, PLAIN_HALVES - 1, 1 - near, consume)
                consume_way(k, q, near, consume)
            each(k)

    def gather_passing_first(ph, consume, each):
        @pl.loop(0, n)
        def _(k):
            @pl.when(k == 1)
            def _():
                @pl.loop(1, n)
                def _(ahead):
                    for q in range(PLAIN_HALVES):
                        take_both(ph, ahead, q, takes=False)
            for q in range(PLAIN_HALVES):
                take_both(ph, k, q, passes=False)

                @pl.loop(0, 2)
                def _(i):
                    consume_way(k, q, (near + i) % 2, consume)
            each(k)

    last_pass = jnp.maximum(jnp.where(z < n - 1, z, 0), jnp.where(z > 0, n - 1 - z, 0))

    def forward(ph, field):
        def consume(k, block, q):
            into = taken.at[block]
            unpack_half(ph, block, q, into)

            @pl.when(k == 0)
            def _():
                add_conv(q, into, lambda a: wv[ph, z, 3 * a * ch:3 * (a + 1) * ch, :])

            @pl.when(k > 0)
            def _():
                slot = slot_of(block)
                if q == 0:
                    weights_arrived(ph, slot)
                add_conv(q, into, lambda a: wf[ph, slot, 3 * a * ch:3 * (a + 1) * ch, :])

        def each(k):
            if ph == 0:
                @pl.when(k == 0)
                def _():
                    weights_round(0)

            @pl.when(k == last_pass)
            def _():
                turn_weights(ph)
                turn_field(ph, field)
                if ph == 0:
                    load_cotangent()
        (gather if ph else gather_passing_first)(ph, consume, each)

    def turn_field(ph, field):
        for a in range(3):
            for start in range(0, cells, ch):
                first = start + (a - 1) * wide
                if first < 0:
                    v = jnp.concatenate([field[cells:cells + wide, :], field[0:first + ch, :]], axis=0)
                elif first + ch > cells:
                    v = jnp.concatenate([field[first:cells, :], field[cells + wide:total, :]], axis=0)
                else:
                    v = field[first:first + ch, :]
                x_t[ph, a * ch:(a + 1) * ch, start:start + ch] = v.T.astype(BF16)

    def turn_weights(ph):
        @pl.loop(0, n)
        def _(d):
            for t in range(9):
                a, b = 2 - t // 3, 2 - t % 3
                wt[ph, d, a, b * ch:(b + 1) * ch, :] = wv[ph, d, t * ch:(t + 1) * ch, :].T

    half_rows = tap_rows // 2
    owners = math.gcd(half_rows // 16, chips)
    piece = half_rows // owners

    def c_copy(ph, j):
        return pltpu.make_async_remote_copy(
            src_ref=psend.at[ph, j], dst_ref=crecv.at[ph, j],
            send_sem=c_ssem.at[ph, j], recv_sem=c_rsem.at[ph, j],
            device_id=(z, chip * 2 + 1 - core), device_id_type=MESH)

    def q_copy(ph, j, e, whose, owner):
        return pltpu.make_async_remote_copy(
            src_ref=hsend.at[ph, j, owner], dst_ref=qrecv.at[ph, j, whose],
            send_sem=q_ssem.at[ph, j, e], recv_sem=q_rsem.at[ph, j, whose],
            device_id=(z, ((chip + e) % chips) * 2 + core), device_id_type=MESH)

    def f_copy(ph, j, e, owner):
        return pltpu.make_async_remote_copy(
            src_ref=wout.at[ph, j, core, owner], dst_ref=wout.at[ph, j, core, owner],
            send_sem=f_ssem.at[ph, j, e], recv_sem=f_rsem.at[ph, j, owner],
            device_id=(z, ((chip + e) % chips) * 2 + core), device_id_type=MESH)

    def h_copy(ph, j, whose):
        return pltpu.make_async_remote_copy(
            src_ref=wout.at[ph, j, whose], dst_ref=wout.at[ph, j, whose],
            send_sem=h_ssem.at[ph, j], recv_sem=h_rsem.at[ph, j],
            device_id=(z, chip * 2 + 1 - core), device_id_type=MESH)

    def o_copy(ph, j):
        target = (out_wg1, out_wg2)[ph]
        if aligned:
            target = target.at[:, :, :, pl.ds(pl.multiple_of(j * ch, ch), ch)]
        else:
            target = target.at[j]
        return pltpu.make_async_copy(wout.at[ph, j], target, o_sem.at[ph, j])

    def sum_cores(ph, j):
        for o in range(owners):
            psend[ph, j, o] = part[ph, j, 1 - core, o].astype(BF16)
        c_copy(ph, j).start()

    def sum_chips(ph, j):
        c_copy(ph, j).wait_recv()
        for o in range(owners):
            v = part[ph, j, core, o] + crecv[ph, j, o].astype(F32)
            part[ph, j, core, o] = v
            hsend[ph, j, o] = v.astype(BF16)

        @pl.loop(1, chips)
        def _(e):
            peer = (chip + e) % chips

            @pl.when(peer < owners)
            def _():
                q_copy(ph, j, e, chip, peer).start()

    def spread_chips(ph, j):
        @pl.when(chip < owners)
        def _():
            @pl.loop(1, chips)
            def _(e):
                q_copy(ph, j, e, (chip + e) % chips, chip).wait_recv()
            v = part[ph, j, core, chip]
            for e in range(1, chips):
                v = v + qrecv[ph, j, (chip + e) % chips].astype(F32)
            wout[ph, j, core, chip] = v.astype(BF16)

            @pl.loop(1, chips)
            def _(e):
                f_copy(ph, j, e, chip).start()

    def spread_cores(ph, j):
        @pl.loop(1, chips)
        def _(e):
            peer = (chip + e) % chips

            @pl.when(peer < owners)
            def _():
                f_copy(ph, j, e, peer).wait_recv()
        h_copy(ph, j, core).start()

    def finish(ph, j):
        h_copy(ph, j, 1 - core).wait_recv()
        o_copy(ph, j).start()

    def put_part(ph, j, tap, value):
        start = tap * ch
        done = 0
        while done < ch:
            row = start + done
            side, o, at = row // half_rows, row % half_rows // piece, row % piece
            size = min(ch - done, piece - at)
            part[ph, j, side, o, at:at + size, :] = value[done:done + size, :]
            done += size

    stages = (sum_cores, sum_chips, spread_chips, spread_cores, finish)

    def of_step(k, fn):
        @pl.loop(0, 2)
        def _(way):
            block = z - k * (1 - 2 * way)

            @pl.when((k >= 0) & (k < n) & inside(block) & ((k > 0) | (way == 0)))
            def _():
                fn(block)

    passing = last_pass > 0

    def made_at(step):
        first = jnp.where(passing & (step > 0), jnp.where(step == last_pass, 1, step + 1), step)
        return first, step + 1

    def advance(ph, k):
        for age in range(1, len(stages)):
            step = k - age

            @pl.when((step >= 0) & (step < n))
            def _():
                @pl.loop(*made_at(step))
                def _(made):
                    of_step(made, functools.partial(stages[age], ph))

    def advance_all(ph, age):
        @pl.loop(0, n)
        def _(j):
            stages[age](ph, j)

    def field_grad(ph, block):
        grad = taken[block, 1:rows + 1, :, :].reshape(cells, 3 * ch)
        value = dot(x_t[ph], grad)
        for a in range(3):
            for b in range(3):
                put_part(ph, block, 3 * a + b, value[a * ch:(a + 1) * ch, (2 - b) * ch:(3 - b) * ch])

    def make_grad(ph, block):
        field_grad(ph, block)
        sum_cores(ph, block)

    def backward(ph):
        last = ph == 0

        def consume(k, block, q):
            into = taken.at[block]
            unpack_half(2 + ph, block, q, into)
            if last and q == PLAIN_HALVES - 1:
                @pl.when((k == 0) | (k >= last_pass))
                def _():
                    make_grad(ph, block)
            add_conv(q, into, lambda a: wt[ph, block, a])

        def each(k):
            first, end = made_at(k)
            if last:
                @pl.loop(first, end - 1)
                def _(step):
                    of_step(step, functools.partial(make_grad, ph))
                advance(ph, k)
                for age in range(2, len(stages)):
                    @pl.when(k == age - 2)
                    def _():
                        advance_all(1, age)
            else:
                @pl.loop(first, jnp.where(passing | (k < n - 1), end, first))
                def _(step):
                    of_step(step, functools.partial(make_grad, ph))

                @pl.when(k == last_pass)
                def _():
                    to_flat(hid2, out_block)
        gather(2 + ph, consume, each)

    def fold(v):
        return jnp.sum(v.reshape(v.shape[0] // 8, 8, ch), axis=0)

    def flatten(v):
        return jnp.sum(v, axis=0, keepdims=True)

    zero = jnp.zeros((8, ch), F32)

    def local_moments(ref):
        def sums(start, size, carry):
            at = pl.ds(start, size)
            m = mask[at, :]
            return carry[0] + fold(ref[at, :] * m), carry[1] + fold(m)
        added, number = (flatten(v) for v in chunked(sums, (zero, zero)))
        middle = added / jnp.maximum(number, 1.0)

        def spread(start, size, carry):
            at = pl.ds(start, size)
            c = (ref[at, :] - middle) * mask[at, :]
            return carry + fold(c * c)
        return added, number, flatten(chunked(spread, zero))

    def moments(slot):
        take_stats(slot)
        got = [st_recv[slot, k] for k in range(s_count)]
        added = sum(g[0:1] for g in got)
        number = sum(g[1:2] for g in got)
        mean = added / number
        spread = 0.0
        for g in got:
            off = g[0:1] / jnp.maximum(g[1:2], 1.0) - mean
            spread = spread + (g[2:3] + g[1:2] * off * off)
        return mean, lax.rsqrt(spread / number + EPSILON), number

    def everywhere(fn):
        chunked(fn, 0)
        fn(cells, 2 * wide, 0)

    gain1, shift1, gain2, shift2 = (r[...] for r in (gain1_in, shift1_in, gain2_in, shift2_in))

    weights_over_z(0)

    below = lax.broadcasted_iota(jnp.int32, (band, band), 1) < lax.broadcasted_iota(jnp.int32, (band, band), 0)
    below = below.astype(F32).astype(BF16)

    def make_pack(h):
        lv = mask[h * band:(h + 1) * band, :]
        place = jnp.where(lv > 0.0, dot(below, lv.astype(BF16)), -1.0)
        places[h] = place
        across = place.T[0:1, :]
        spot = lax.broadcasted_iota(jnp.int32, (packed, band), 0).astype(F32)
        pack[h] = jnp.where(spot == across, 1.0, 0.0).astype(BF16)

    def make_unpack(h):
        for start in range(0, packed, ch):
            size = min(ch, packed - start)
            spot = start + lax.broadcasted_iota(jnp.int32, (band, size), 1)
            unpack[h, :, start:start + size] = jnp.where(
                places[h, :, :size] == spot.astype(F32), 1.0, 0.0).astype(BF16)

    for side in range(2):
        edge_copy(1 - side).wait_recv()
        there = jnp.where(s > 0, 1.0, 0.0) if side == 0 else jnp.where(s < s_count - 1, 1.0, 0.0)
        at = slice(cells + side * wide, cells + (side + 1) * wide)
        masked[at, :] = edge_recv[side, 0].astype(F32) * there
        mask[at, :] = edge_recv[side, 1].astype(F32) * there

    pack_field(0, masked, first=make_pack)
    for h in range(PLAIN_HALVES):
        make_unpack(h)
    forward(0, masked)
    weights_over_z(1)
    send_rows(0, acc)
    send_stats(0, local_moments(acc))
    mean1, scale1, count = moments(0)
    weights_round(1)

    def activate_one(start, size, carry):
        at = pl.ds(start, size)
        main = start is not cells
        nv = ((acc if main else normed1)[at, :] - mean1) * scale1
        normed1[at, :] = nv
        hid[at, :] = gelu_parts(nv * gain1 + shift1)[0] * mask[at, :]
        if main:
            acc[at, :] = jnp.zeros((size, ch), F32)
        return carry

    def slope_one(start, size, carry):
        at = pl.ds(start, size)
        slope1[at, :] = gelu_parts(normed1[at, :] * gain1 + shift1)[1] * mask[at, :]
        return carry

    take_rows(0, normed1)
    pack_field(1, hid, activate_one)
    everywhere(slope_one)
    forward(1, hid)
    send_rows(1, acc)
    send_stats(1, local_moments(acc))
    mean2, scale2, _ = moments(1)

    def activate_two(source, start, size):
        at = pl.ds(start, size)
        nv = (source[at, :] - mean2) * scale2
        normed2[at, :] = nv
        value, slope = gelu_parts(nv * gain2 + shift2 + masked[at, :])
        t = cotm[at, :] * slope
        through[at, :] = t
        return value, nv, t

    def activate_main(start, size, carry):
        value, nv, t = activate_two(acc, start, size)
        at = pl.ds(start, size)
        hid2[at, :] = value * mask[at, :]
        acc[at, :] = jnp.zeros((size, ch), F32)
        return carry[0] + fold(t * nv), carry[1] + fold(t)

    send_stats(2, [flatten(v) for v in chunked(activate_main, (zero, zero))])
    take_rows(1, normed2)
    take_cotangent()
    activate_two(normed2, cells, edge)

    def gradient_sums(slot):
        take_stats(slot)
        got = [st_recv[slot, k] for k in range(s_count)]
        return sum(g[0:1] for g in got), sum(g[1:2] for g in got)

    def norm_back(upstream, normed, gain, scale, sums):
        gain_grad, shift_grad = sums
        factor = gain * scale
        level, tilt = shift_grad / count, gain_grad / count

        def fill(start, size, carry):
            at = pl.ds(start, size)
            v = upstream[at, :] - mask[at, :] * (level + normed[at, :] * tilt)
            hid[at, :] = factor * v
            return carry
        return fill

    sums2 = gradient_sums(2)
    pack_field(3, hid, norm_back(through, normed2, gain2, scale2, sums2))
    backward(1)

    send_rows(2, acc)

    def inner_main(start, size, carry):
        at = pl.ds(start, size)
        v = acc[at, :] * slope1[at, :]
        slope1[at, :] = v
        acc[at, :] = jnp.zeros((size, ch), F32)
        return carry[0] + fold(v * normed1[at, :]), carry[1] + fold(v)

    send_stats(3, [flatten(v) for v in chunked(inner_main, (zero, zero))])

    @pl.when(jnp.logical_not(passing))
    def _():
        of_step(n - 1, functools.partial(make_grad, 1))
    for side in range(2):
        row_copy(2, 1 - side).wait_recv()
        at = slice(cells + side * wide, cells + (side + 1) * wide)
        slope1[at, :] = row_recv[2, side] * slope1[at, :]
    sums1 = gradient_sums(3)
    pack_field(2, hid, norm_back(slope1, normed1, gain1, scale1, sums1))
    advance_all(1, 1)
    backward(0)
    advance(0, n)

    def finish_input(start, size, carry):
        at = pl.ds(start, size)
        acc[at, :] = (acc[at, :] + through[at, :]) * mask[at, :]
        return carry

    chunked(finish_input, 0)
    to_flat(acc, out_input)
    out_gain1[...], out_shift1[...] = sums1
    out_gain2[...], out_shift2[...] = sums2
    for extra in range(1, len(stages) - 1):
        advance(0, n + extra)

    for side in range(2):
        edge_copy(side).wait_send()
        cot_copy(side).wait_send()
        for slot in range(3):
            row_copy(slot, side).wait_send()

    @pl.loop(1, s_count)
    def _(k):
        for slot in range(4):
            st_copy(slot, k, s).wait_send()

    @pl.loop(1, n)
    def _(k):
        for which in range(2):
            wz_copy(which, k).wait_send()

    @pl.loop(1, w_parts)
    def _(k):
        for which in range(2):
            for slot in range(n - 1):
                wp_copy(which, slot, k, w_mine).wait_send()

    @pl.loop(0, n)
    def _(k):
        for sign in (1, -1):
            block = z - k * sign

            @pl.when((block >= 0) & (block < n) & (z + sign >= 0) & (z + sign < n))
            def _():
                for ph in range(4):
                    for q in range(PLAIN_HALVES):
                        ag_copy(ph, block, q, sign).wait_send()

    @pl.loop(0, n)
    def _(j):
        for ph in range(2):
            c_copy(ph, j).wait_send()
            h_copy(ph, j, core).wait_send()
            o_copy(ph, j).wait()

            @pl.loop(1, chips)
            def _(e):
                peer = (chip + e) % chips

                @pl.when(peer < owners)
                def _():
                    q_copy(ph, j, e, chip, peer).wait_send()

                @pl.when(chip < owners)
                def _():
                    f_copy(ph, j, e, chip).wait_send()


def finish_kernel(count, *refs):
    ins, outs = refs[:count], refs[count:2 * count]
    narrow, wide, in_sem, out_sem, take_sem, give_sem = refs[2 * count:2 * count + 6]
    held = refs[2 * count + 6:]
    rows = narrow.shape[1] // FINISH_PARTS
    parts = [(w, i, pl.ds(i * rows, rows)) for i in range(FINISH_PARTS) for w in range(2)]
    loads = [pltpu.make_async_copy(ins[w].at[at, :], narrow.at[w, at, :], in_sem.at[w, i]) for w, i, at in parts]
    stores = [pltpu.make_async_copy(wide.at[w, at, :], outs[w].at[at, :], out_sem.at[w, i]) for w, i, at in parts]
    takes = [pltpu.make_async_copy(ins[2 + k], v, take_sem.at[k]) for k, v in enumerate(held)]
    gives = [pltpu.make_async_copy(v, outs[2 + k], give_sem.at[k]) for k, v in enumerate(held)]
    for copy in loads + takes:
        copy.start()
    for load, store, (w, i, at) in zip(loads, stores, parts):
        load.wait()
        wide[w, at, :] = narrow[w, at, :].astype(F32)
        store.start()
    for take, give in zip(takes, gives):
        take.wait()
        give.start()
    for copy in stores + gives:
        copy.wait()


def block_scratch(n, s_count, rows, wide, ch):
    cells = rows * wide
    total = cells + 2 * wide
    parts = n // 2
    part_rows = rows // parts
    pc = part_rows * wide
    pt = pc + 2 * wide
    packed = packed_rows(part_rows, wide)
    chunk = 2 * wide + packed
    chips = s_count // 2
    tap_rows = 9 * ch
    half_rows = tap_rows // 2
    owners = math.gcd(half_rows // 16, chips)
    piece = half_rows // owners
    units = n + parts * n
    family = parts * s_count
    st_rows = -(-(1 + 2 * parts) // 8) * 8

    sem = pltpu.SemaphoreType.DMA
    field = pltpu.VMEM((parts, pt, ch), F32)
    whole_field = pltpu.VMEM((total, ch), F32)
    weight_sets = 2 * (n - 1) + parts
    return [
        pltpu.VMEM((ch * wide, 128), F32),
        pltpu.VMEM((2, n, tap_rows, ch), BF16),
        pltpu.VMEM((2, n - 1, parts, tap_rows, ch), BF16),
        pltpu.VMEM((parts, n, tap_rows, ch), BF16),
        pltpu.VMEM((n, 3, 3 * ch, ch), BF16),
        pltpu.VMEM((parts, n, 3, 3 * ch, ch), BF16),
        pltpu.VMEM((parts, 3 * ch, pc), BF16),
        pltpu.VMEM((parts, 3 * ch, pc), BF16),
        pltpu.VMEM((parts, packed, pc), BF16),
        pltpu.VMEM((parts, pc, packed), BF16),
        pltpu.VMEM((parts, pc, ch), F32),
        whole_field, whole_field, whole_field,
        pltpu.VMEM((2, 2, wide, ch), BF16),
        pltpu.VMEM((2, 2, wide, ch), BF16),
        pltpu.VMEM((2, wide, ch), BF16),
        pltpu.VMEM((2, wide, ch), BF16),
        pltpu.VMEM((8, ch), F32),
        pltpu.VMEM((parts, 8, ch), F32),
        pltpu.VMEM((pt, ch), F32),
        field, field, field, field, field, field, field, field,
        pltpu.VMEM((pt + 16, ch), F32),
        pltpu.VMEM((parts, pc, ch), F32),
        pltpu.VMEM((n, parts, chunk, ch), BF16),
        pltpu.VMEM((2, 2, parts, chunk, ch), BF16),
        pltpu.VMEM((n, parts, chunk, ch), BF16),
        pltpu.VMEM((n, parts, part_rows + 2, wide, 3 * ch), BF16),
        pltpu.VMEM((parts, chunk, ch), BF16),
        pltpu.VMEM((parts, chunk, ch), BF16),
        pltpu.VMEM((2, parts, packed, ch), BF16),
        pltpu.VMEM((2, parts, packed, ch), BF16),
        pltpu.VMEM((cells, ch), F32),
        pltpu.VMEM((cells, ch), F32),
        pltpu.VMEM((units, 2, owners, piece, ch), F32),
        pltpu.VMEM((units, owners, piece, ch), BF16),
        pltpu.VMEM((units, owners, piece, ch), BF16),
        pltpu.VMEM((units, owners, piece, ch), BF16),
        pltpu.VMEM((units, chips, piece, ch), BF16),
        pltpu.VMEM((parts, n, piece, ch), BF16),
        pltpu.VMEM((parts, n, piece, ch), BF16),
        pltpu.VMEM((2, n, 2, owners, piece, ch), BF16),
        pltpu.VMEM((4, st_rows, ch), F32),
        pltpu.VMEM((4, family, st_rows, ch), F32),
        pltpu.VMEM((3, 2, parts, wide, ch), F32),
        pltpu.VMEM((3, 2, parts, wide, ch), F32),
        pltpu.VMEM((4, parts, 1, ch), F32),
        pltpu.VMEM((2, parts, 1, ch), F32),
        sem((2, n)),
        sem((weight_sets,)), sem((weight_sets,)),
        sem((weight_sets, owners)), sem((weight_sets, owners)),
        sem((weight_sets,)), sem((weight_sets,)),
        sem((2,)), sem((2,)),
        sem((2,)), sem((2,)),
        sem((parts,)), sem((parts,)),
        sem((2, n, parts)), sem((n, parts)),
        sem((2, parts)), sem((2, parts)),
        sem((2, n, parts)), sem((n, parts)),
        sem((parts,)), sem((parts,)),
        sem((2, parts)), sem((2, parts)),
        sem((4, family)), sem((4, family)),
        sem((3, 2)), sem((3, 2)),
        sem((units,)), sem((units,)),
        sem((units, chips)), sem((units, chips)),
        sem((2, n, chips)), sem((2, n, chips)),
        sem((2, n)), sem((2, n)),
        sem((parts, n)), sem((parts, n)),
        sem((2, n)),
    ]


def plain_scratch(n, s_count, rows, wide, ch):
    cells = rows * wide
    total = cells + 2 * wide
    packed = packed_rows(rows // PLAIN_HALVES, wide)
    chips = s_count // 2
    tap_rows = 9 * ch
    half_rows = tap_rows // 2
    owners = math.gcd(half_rows // 16, chips)
    piece = half_rows // owners
    sem = pltpu.SemaphoreType.DMA
    field = pltpu.VMEM((total, ch), F32)
    return [
        pltpu.VMEM((ch * wide, 128), F32),
        pltpu.VMEM((2, n, tap_rows, ch), BF16),
        pltpu.VMEM((2, n - 1, tap_rows, ch), BF16),
        pltpu.VMEM((2, n, 3, 3 * ch, ch), BF16),
        pltpu.VMEM((2, 3 * ch, cells), BF16),
        pltpu.VMEM((PLAIN_HALVES, packed, cells // PLAIN_HALVES), BF16),
        pltpu.VMEM((PLAIN_HALVES, cells // PLAIN_HALVES, packed), BF16),
        pltpu.VMEM((PLAIN_HALVES, cells // PLAIN_HALVES, ch), F32),
        pltpu.VMEM((2, 2, wide, ch), BF16),
        pltpu.VMEM((2, 2, wide, ch), BF16),
        pltpu.VMEM((2, wide, ch), BF16),
        pltpu.VMEM((2, wide, ch), BF16),
        field, field, field, field, field, field, field, field, field,
        pltpu.VMEM((total + 16, ch), F32),
        pltpu.VMEM((cells, ch), F32),
        pltpu.VMEM((4, n, 2 * wide + PLAIN_HALVES * packed, ch), BF16),
        pltpu.VMEM((n, rows + 2, wide, 3 * ch), BF16),
        pltpu.VMEM((2, n, 2, owners, piece, ch), F32),
        pltpu.VMEM((2, n, owners, piece, ch), BF16),
        pltpu.VMEM((2, n, owners, piece, ch), BF16),
        pltpu.VMEM((2, n, owners, piece, ch), BF16),
        pltpu.VMEM((2, n, chips, piece, ch), BF16),
        pltpu.VMEM((2, n, 2, owners, piece, ch), BF16),
        pltpu.VMEM((4, 8, ch), F32),
        pltpu.VMEM((4, s_count, 8, ch), F32),
        pltpu.VMEM((3, 2, wide, ch), F32),
        pltpu.VMEM((3, 2, wide, ch), F32),
        sem((2, n)),
        sem((2, n)), sem((2, n)),
        sem((2, n - 1, s_count)), sem((2, n - 1, s_count)),
        sem((2,)), sem((2,)),
        sem((2,)), sem((2,)),
        sem((4, 2, n, PLAIN_HALVES)), sem((4, n, PLAIN_HALVES)),
        sem((4, s_count)), sem((4, s_count)),
        sem((3, 2)), sem((3, 2)),
        sem((2, n)), sem((2, n)),
        sem((2, n, chips)), sem((2, n, chips)),
        sem((2, n, chips)), sem((2, n, chips)),
        sem((2, n)), sem((2, n)),
        sem((2, n)),
    ]


def scratch_bytes(scratch):
    held = [v for v in scratch if hasattr(v, "dtype") and v.dtype in (F32, BF16)]
    return sum(math.prod(v.shape[:-1]) * -(-v.shape[-1] // 128) * 128 * v.dtype.itemsize for v in held)


def per_device(n, s_count, blocks, weight_one, weight_two, gain_one, shift_one, gain_two, shift_two, cell_live, cotangent):
    rows, wide = cell_live.shape
    ch = blocks.shape[1] // wide
    aligned = ch % 128 == 0
    tap_rows = 9 * ch
    half_rows = tap_rows // 2
    owners = math.gcd(half_rows // 16, s_count // 2)
    piece = half_rows // owners

    sizes = (n, s_count, rows, wide, ch)
    kernel, packed, scratch = block_kernel, packed_rows(rows // (n // 2), wide), block_scratch(*sizes)
    if scratch_bytes(scratch) > SCRATCH_LIMIT:
        kernel, packed, scratch = plain_kernel, packed_rows(rows // PLAIN_HALVES, wide), plain_scratch(*sizes)

    if aligned:
        weight_one, weight_two = (w.reshape(tap_rows, n * ch) for w in (weight_one, weight_two))
    else:
        weight_one, weight_two = (
            w.reshape(tap_rows, n, ch).transpose(1, 0, 2) for w in (weight_one, weight_two))
    grad_shape = (2, owners, piece, n * ch) if aligned else (n, 2, owners, piece, ch)
    vmem = pl.BlockSpec(memory_space=pltpu.VMEM)
    hbm = pl.BlockSpec(memory_space=pl.ANY)
    sem = pltpu.SemaphoreType.DMA
    block_out, input_grad, wg1, wg2, *sums = pl.pallas_call(
        functools.partial(kernel, n, s_count, rows, wide, ch, aligned, packed),
        out_shape=(
            jax.ShapeDtypeStruct((rows, ch * wide), BF16),
            jax.ShapeDtypeStruct((rows, ch * wide), F32),
            jax.ShapeDtypeStruct(grad_shape, BF16),
            jax.ShapeDtypeStruct(grad_shape, BF16),
            *[jax.ShapeDtypeStruct((1, ch), F32)] * 4,
        ),
        in_specs=[vmem] * 7 + [hbm] * 2,
        out_specs=(vmem, vmem, hbm, hbm, vmem, vmem, vmem, vmem),
        scratch_shapes=scratch,
        compiler_params=pltpu.CompilerParams(
            collective_id=0, has_side_effects=True, vmem_limit_bytes=60 * 1024 * 1024),
    )(blocks, cotangent, cell_live.T,
      *(v.reshape(1, ch) for v in (gain_one, shift_one, gain_two, shift_two)), weight_one, weight_two)

    if not aligned:
        def whole(grad):
            grad = grad.reshape(n, tap_rows, ch).transpose(1, 0, 2)
            return grad.astype(F32).reshape(9, ch, n * ch)
        return (block_out, input_grad, whole(wg1), whole(wg2), *(v.reshape(ch) for v in sums))

    wg1, wg2 = (w.reshape(tap_rows, n * ch) for w in (wg1, wg2))
    wide_grad = jax.ShapeDtypeStruct((tap_rows, n * ch), F32)
    moved = (block_out, input_grad, *sums)
    grad1, grad2, *moved = pl.pallas_call(
        functools.partial(finish_kernel, 2 + len(moved)),
        out_shape=(wide_grad, wide_grad, *(jax.ShapeDtypeStruct(v.shape, v.dtype) for v in moved)),
        in_specs=[pl.BlockSpec(memory_space=pl.ANY)] * (2 + len(moved)),
        out_specs=[pl.BlockSpec(memory_space=pl.ANY)] * (2 + len(moved)),
        scratch_shapes=[
            pltpu.VMEM((2, tap_rows, n * ch), BF16), pltpu.VMEM((2, tap_rows, n * ch), F32),
            sem((2, FINISH_PARTS)), sem((2, FINISH_PARTS)), sem((len(moved),)), sem((len(moved),)),
            *(pltpu.VMEM(v.shape, v.dtype) for v in moved),
        ],
        compiler_params=pltpu.CompilerParams(vmem_limit_bytes=64 * 1024 * 1024),
    )(wg1, wg2, *moved)
    block_out, input_grad, *sums = moved
    grads = (g.reshape(9, ch, n * ch) for g in (grad1, grad2))
    return (block_out, input_grad, *grads, *(v.reshape(ch) for v in sums))


def solution(mesh):
    return jax.shard_map(
        functools.partial(per_device, mesh.shape["chan"], mesh.shape["space"]),
        mesh=mesh,
        in_specs=(
            P("space", "chan"),
            P(None, "chan", None),
            P(None, "chan", None),
            P("chan"),
            P("chan"),
            P("chan"),
            P("chan"),
            P("space", None),
            P("space", "chan"),
        ),
        out_specs=(
            P("space", "chan"),
            P("space", "chan"),
            P(None, "chan", None),
            P(None, "chan", None),
            P("chan"),
            P("chan"),
            P("chan"),
            P("chan"),
        ),
        check_vma=False,
    )
```

```python
import functools
import math

import jax
import jax.numpy as jnp
from jax import lax
from jax.experimental import pallas as pl
from jax.experimental.pallas import tpu as pltpu
from jax.sharding import PartitionSpec as P

EPSILON = 1e-05
MESH = pl.DeviceIdType.MESH
F32 = jnp.float32
BF16 = jnp.bfloat16
ROOT_HALF = 0.7071067811865476
ROOT_TWO_PI = 0.3989422804014327
CHUNK = 64
FINISH_PARTS = 4
UNROLL = 2
HALVES = 2
LARGE, SMALL = 7, 3


def dot(a, b):
    return jnp.dot(a, b, preferred_element_type=F32)


def gelu_parts(v):
    upper = 0.5 * (1.0 + lax.erf(v * ROOT_HALF))
    slope = upper + v * (ROOT_TWO_PI * jnp.exp(-0.5 * v * v))
    return v * upper, slope


def most_live(rows, wide):
    units = (wide + 1) // (SMALL + 1)
    live_rows = rows - rows // (LARGE + 1)
    return min(rows * wide, math.ceil(units * live_rows * LARGE / 2))


def block_kernel(n, s_count, rows, wide, ch, aligned, packed, *refs):
    (x_in, cot_in, live_in, gain1_in, shift1_in, gain2_in, shift2_in, w1_hbm, w2_hbm) = refs[:9]
    (out_block, out_input, out_wg1, out_wg2, out_gain1, out_shift1, out_gain2, out_shift2) = refs[9:17]
    (turned, wv, wf, x_t, pack, unpack, places, edge_send, edge_recv, cot_send, cot_recv, cotm, mask, masked,
     normed1, normed2, through, slope1, hid, hid2, pad, acc, hold, taken,
     part, psend, crecv, hsend, qrecv, wout, st_send, st_recv, row_send, row_recv,
     w_sem, wz_ssem, wz_rsem, wp_ssem, wp_rsem, e_ssem, e_rsem, ce_ssem, ce_rsem, ag_ssem, ag_rsem,
     st_ssem, st_rsem, row_ssem, row_rsem, c_ssem, c_rsem, q_ssem, q_rsem,
     f_ssem, f_rsem, h_ssem, h_rsem, o_sem) = refs[17:]

    z = lax.axis_index("chan")
    s = lax.axis_index("space")
    cells = rows * wide
    total = cells + 2 * wide
    band = cells // HALVES
    core, chip, chips = s % 2, s // 2, s_count // 2
    before, after = (s + s_count - 1) % s_count, (s + 1) % s_count
    tap_rows = 9 * ch

    barrier = pltpu.get_barrier_semaphore()

    @pl.loop(1, s_count)
    def _(k):
        pl.semaphore_signal(barrier, inc=1, device_id=(z, (s + k) % s_count), device_id_type=MESH)

    @pl.loop(1, n)
    def _(k):
        pl.semaphore_signal(barrier, inc=1, device_id=((z + k) % n, s), device_id_type=MESH)

    w_copies = []
    for which, source in enumerate((w1_hbm, w2_hbm)):
        for d in range(n):
            block = source.at[:, d * ch:(d + 1) * ch] if aligned else source.at[d]
            w_copies.append(pltpu.make_async_copy(block, wv.at[which, d], w_sem.at[which, d]))
    for copy in w_copies:
        copy.start()

    def chunked(fn, init, first=0, count=cells):
        def step(i, carry):
            return fn(pl.multiple_of(first + i * CHUNK, CHUNK), CHUNK, carry)
        return lax.fori_loop(0, count // CHUNK, step, init, unroll=UNROLL)

    lanes = 128
    tiles = ch * wide // lanes

    def from_flat(flat, put):
        for i in range(tiles):
            turned[i * lanes:(i + 1) * lanes, 0:rows] = flat[:, i * lanes:(i + 1) * lanes].astype(F32).T
        for w in range(wide):
            put(pl.ds(w, rows, stride=wide), turned[pl.ds(w, ch, stride=wide), 0:rows].T)

    def to_flat(source, flat):
        for w in range(wide):
            turned[pl.ds(w, ch, stride=wide), 0:rows] = source[pl.ds(w, rows, stride=wide), :].T
        for i in range(tiles):
            flat[:, i * lanes:(i + 1) * lanes] = turned[i * lanes:(i + 1) * lanes, 0:rows].T.astype(flat.dtype)

    def put_masked(at, value):
        masked[at, :] = value

    from_flat(x_in, put_masked)

    cell = lax.broadcasted_iota(jnp.int32, (cells, rows), 0)
    pick = (cell // wide == lax.broadcasted_iota(jnp.int32, (cells, rows), 1)).astype(F32).astype(BF16)
    column_of = lax.broadcasted_iota(jnp.int32, (cells, wide), 0) % wide
    picked = lax.dot_general(pick, live_in[...].astype(BF16), (((1,), (1,)), ((), ())), preferred_element_type=F32)
    picked = jnp.where(column_of == lax.broadcasted_iota(jnp.int32, (cells, wide), 1), picked, 0.0)
    mask[0:cells, :] = dot(picked.astype(BF16), jnp.ones((wide, ch), BF16))

    def load_main(start, size, carry):
        at = pl.ds(start, size)
        lv = mask[at, :]
        masked[at, :] = masked[at, :] * lv
        return carry

    chunked(load_main, 0)
    for side, start in ((0, 0), (1, cells - wide)):
        edge_send[side, 0] = masked[start:start + wide, :].astype(BF16)
        edge_send[side, 1] = mask[start:start + wide, :].astype(BF16)

    acc[...] = jnp.zeros_like(acc)
    st_send[...] = jnp.zeros_like(st_send)

    pl.semaphore_wait(barrier, s_count - 1 + n - 1)

    def edge_copy(side):
        return pltpu.make_async_remote_copy(
            src_ref=edge_send.at[side], dst_ref=edge_recv.at[1 - side],
            send_sem=e_ssem.at[side], recv_sem=e_rsem.at[1 - side],
            device_id=(z, before if side == 0 else after), device_id_type=MESH)

    for side in range(2):
        edge_copy(side).start()

    def cot_copy(side):
        return pltpu.make_async_remote_copy(
            src_ref=cot_send.at[side], dst_ref=cot_recv.at[1 - side],
            send_sem=ce_ssem.at[side], recv_sem=ce_rsem.at[1 - side],
            device_id=(z, before if side == 0 else after), device_id_type=MESH)

    def load_cotangent():
        def put(at, value):
            cotm[at, :] = value
        from_flat(cot_in, put)

        def live_only(start, size, carry):
            at = pl.ds(start, size)
            cotm[at, :] = cotm[at, :] * mask[at, :]
            return carry
        chunked(live_only, 0)
        for side, start in ((0, 0), (1, cells - wide)):
            cot_send[side] = cotm[start:start + wide, :].astype(BF16)
            cot_copy(side).start()

    def take_cotangent():
        for side in range(2):
            cot_copy(1 - side).wait_recv()
            at = slice(cells + side * wide, cells + (side + 1) * wide)
            cotm[at, :] = cot_recv[side].astype(F32) * mask[at, :]

    w_parts = math.gcd(tap_rows // 16, s_count)
    w_rows = tap_rows // w_parts
    w_mine = s % w_parts
    w_group = s - w_mine

    def wz_copy(which, k):
        at = pl.ds(w_mine * w_rows, w_rows)
        slot = n - k - 1
        return pltpu.make_async_remote_copy(
            src_ref=wv.at[which, (z + k) % n, at, :], dst_ref=wf.at[which, slot, at, :],
            send_sem=wz_ssem.at[which, slot], recv_sem=wz_rsem.at[which, slot],
            device_id=((z + k) % n, s), device_id_type=MESH)

    def wp_copy(which, slot, k, whose):
        at = pl.ds(whose * w_rows, w_rows)
        return pltpu.make_async_remote_copy(
            src_ref=wf.at[which, slot, at, :], dst_ref=wf.at[which, slot, at, :],
            send_sem=wp_ssem.at[which, slot, k], recv_sem=wp_rsem.at[which, slot, whose],
            device_id=(z, w_group + (w_mine + k) % w_parts), device_id_type=MESH)

    def weights_over_z(which):
        for copy in w_copies[which * n:(which + 1) * n]:
            copy.wait()

        @pl.loop(1, n)
        def _(k):
            wz_copy(which, k).start()

    def slot_of(block):
        return (block - z + n - 1) % n

    def weights_round(which):
        @pl.loop(1, n)
        def _(distance):
            for sign in (1, -1):
                block = z - distance * sign

                @pl.when((block >= 0) & (block < n))
                def _():
                    slot = slot_of(block)
                    wz_copy(which, n - 1 - slot).wait_recv()

                    @pl.loop(1, w_parts)
                    def _(k):
                        wp_copy(which, slot, k, w_mine).start()

    def weights_arrived(which, slot):
        @pl.loop(1, w_parts)
        def _(k):
            wp_copy(which, slot, k, (w_mine + k) % w_parts).wait_recv()

    def row_copy(slot, side):
        return pltpu.make_async_remote_copy(
            src_ref=row_send.at[slot, side], dst_ref=row_recv.at[slot, 1 - side],
            send_sem=row_ssem.at[slot, side], recv_sem=row_rsem.at[slot, 1 - side],
            device_id=(z, before if side == 0 else after), device_id_type=MESH)

    def send_rows(slot, ref):
        for side, start in ((0, 0), (1, cells - wide)):
            row_send[slot, side] = ref[start:start + wide, :]
            row_copy(slot, side).start()

    def take_rows(slot, ref):
        for side in range(2):
            row_copy(slot, 1 - side).wait_recv()
            ref[cells + side * wide:cells + (side + 1) * wide, :] = row_recv[slot, side]

    def st_copy(slot, k, whose):
        return pltpu.make_async_remote_copy(
            src_ref=st_send.at[slot], dst_ref=st_recv.at[slot, whose],
            send_sem=st_ssem.at[slot, k], recv_sem=st_rsem.at[slot, whose],
            device_id=(z, (s + k) % s_count), device_id_type=MESH)

    def send_stats(slot, values):
        for i, v in enumerate(values):
            st_send[slot, i:i + 1, :] = v
        for k in range(1, s_count):
            st_copy(slot, k, s).start()
        st_recv[slot, s] = st_send[slot]

    def take_stats(slot):
        for k in range(1, s_count):
            st_copy(slot, k, (s + k) % s_count).wait_recv()

    strip = 8
    column = lax.broadcasted_iota(jnp.int32, (strip * wide, ch), 0) % wide

    def shift(target, first, count):
        size = count * wide
        where = column[:size]
        here = pad[pl.ds(8 + first * wide, size), :]
        left = jnp.where(where == 0, 0.0, pad[pl.ds(7 + first * wide, size), :])
        right = jnp.where(where == wide - 1, 0.0, pad[pl.ds(9 + first * wide, size), :])
        for b, v in enumerate((left, here, right)):
            target[pl.ds(first, count), :, b * ch:(b + 1) * ch] = v.astype(BF16).reshape(count, wide, ch)

    edge = 2 * wide
    ag_rows = ((0, edge + packed), (edge + packed, packed))
    band_rows = rows // HALVES

    def unpack_half(ph, block, q, target):
        if q == 0:
            pad[8:8 + wide, :] = hold[ph, block, 0:wide, :].astype(F32)
            pad[8 + wide + cells:8 + 2 * wide + cells, :] = hold[ph, block, wide:edge, :].astype(F32)
            shift(target, 0, 1)
            shift(target, rows + 1, 1)
        pad[8 + wide + q * band:8 + wide + (q + 1) * band, :] = dot(
            unpack[q], hold[ph, block, edge + q * packed:edge + (q + 1) * packed, :])

        for i in range(band_rows // strip):
            shift(target, 1 + q * band_rows + i * strip, strip)

    def add_conv(q, field, taps, turned_taps=None):
        first, last = (0, band_rows - 1) if q == 0 else (band_rows - 1, rows)
        count = last - first
        lhs = field[first:last + 2, :, :].reshape((count + 2) * wide, 3 * ch)
        if turned_taps is None:
            value = dot(lhs, jnp.concatenate([taps(a) for a in range(3)], axis=1))
        else:
            rhs = jnp.concatenate([
                jnp.concatenate([turned_taps(3 * (2 - a) + 2 - b) for b in range(3)], axis=1) for a in range(3)], axis=0)
            value = lax.dot_general(lhs, rhs, (((1,), (1,)), ((), ())), preferred_element_type=F32)
        at = pl.ds(first * wide, count * wide)
        acc[at, :] = acc[at, :] + sum(
            value[a * wide:(a + count) * wide, a * ch:(a + 1) * ch] for a in range(3))

    def ag_copy(ph, block, q, sign):
        at = pl.ds(*ag_rows[q])
        return pltpu.make_async_remote_copy(
            src_ref=hold.at[ph, block, at, :], dst_ref=hold.at[ph, block, at, :],
            send_sem=ag_ssem.at[ph, (1 - sign) // 2, block, q], recv_sem=ag_rsem.at[ph, block, q],
            device_id=(z + sign, s), device_id_type=MESH)

    def pack_field(ph, source, fill=None, first=None):
        if fill is not None:
            fill(cells, edge, 0)
        hold[ph, z, 0:edge, :] = source[cells:cells + edge, :].astype(BF16)
        for q in range(HALVES):
            if first is not None:
                first(q)
            if fill is not None:
                chunked(fill, 0, q * band, band)
            hold[ph, z, edge + q * packed:edge + (q + 1) * packed, :] = dot(
                pack[q], source[q * band:(q + 1) * band, :].astype(BF16)).astype(BF16)
            for sign in (1, -1):
                @pl.when((z + sign >= 0) & (z + sign < n))
                def _():
                    ag_copy(ph, z, q, sign).start()

    def inside(slice_at):
        return (slice_at >= 0) & (slice_at < n)

    def take_and_pass(ph, k, q, sign, passes=True, takes=True):
        block = z - k * sign

        @pl.when((k > 0) & inside(block))
        def _():
            if passes and takes:
                ag_copy(ph, block, q, sign).wait_recv()

            @pl.when(inside(z + sign))
            def _():
                if passes:
                    if not takes:
                        ag_copy(ph, block, q, sign).wait_recv()
                    ag_copy(ph, block, q, sign).start()

            if not passes:
                @pl.when(jnp.logical_not(inside(z + sign)))
                def _():
                    ag_copy(ph, block, q, sign).wait_recv()

    near = jnp.where(z < n - n // 2, 1, 0)

    def consume_way(k, q, way, consume):
        block = z - k * (1 - 2 * way)

        @pl.when((k >= 0) & (k < n) & inside(block) & ((k > 0) | (way == near)))
        def _():
            consume(k, block, q)

    def take_both(ph, k, q, **how):
        @pl.loop(0, 2)
        def _(i):
            way = (near + i) % 2
            take_and_pass(ph, k, q, 1 - 2 * way, **how)

    def gather(ph, consume, each):
        @pl.loop(0, n)
        def _(k):
            for q in range(HALVES):
                take_both(ph, k, q)
                if q:
                    consume_way(k, q - 1, 1 - near, consume)
                else:
                    consume_way(k - 1, HALVES - 1, 1 - near, consume)
                consume_way(k, q, near, consume)
            each(k)

    def gather_passing_first(ph, consume, each):
        @pl.loop(0, n)
        def _(k):
            @pl.when(k == 1)
            def _():
                @pl.loop(1, n)
                def _(ahead):
                    for q in range(HALVES):
                        take_both(ph, ahead, q, takes=False)
            for q in range(HALVES):
                take_both(ph, k, q, passes=False)

                @pl.loop(0, 2)
                def _(i):
                    consume_way(k, q, (near + i) % 2, consume)
            each(k)

    last_pass = jnp.maximum(jnp.where(z < n - 1, z, 0), jnp.where(z > 0, n - 1 - z, 0))

    def forward(ph, field):
        def consume(k, block, q):
            into = taken.at[block]
            unpack_half(ph, block, q, into)

            @pl.when(k == 0)
            def _():
                add_conv(q, into, lambda a: wv[ph, z, 3 * a * ch:3 * (a + 1) * ch, :])

            @pl.when(k > 0)
            def _():
                slot = slot_of(block)
                if q == 0:
                    weights_arrived(ph, slot)
                add_conv(q, into, lambda a: wf[ph, slot, 3 * a * ch:3 * (a + 1) * ch, :])

        def each(k):
            if ph == 0:
                @pl.when(k == 0)
                def _():
                    weights_round(0)

                @pl.when(k == 1)
                def _():
                    weights_over_z(1)

            @pl.when(k == last_pass)
            def _():
                turn_field(ph, field)
                if ph == 0:
                    load_cotangent()
        (gather if ph else gather_passing_first)(ph, consume, each)

    def turn_field(ph, field):
        main = [field[start:start + ch, :].T for start in range(0, cells, ch)]
        ends = field[cells:cells + edge, :]
        if edge < ch:
            ends = jnp.concatenate([ends, jnp.zeros((ch - edge, ch), F32)], axis=0)
        ends = ends.T
        for i, here in enumerate(main):
            left = jnp.concatenate(
                [ends[:, 0:wide] if i == 0 else main[i - 1][:, ch - wide:], here[:, 0:ch - wide]], axis=1)
            right = jnp.concatenate(
                [here[:, wide:], main[i + 1][:, 0:wide] if i + 1 < len(main) else ends[:, wide:edge]], axis=1)
            for a, v in enumerate((left, here, right)):
                x_t[ph, a * ch:(a + 1) * ch, i * ch:(i + 1) * ch] = v.astype(BF16)

    half_rows = tap_rows // 2
    owners = math.gcd(half_rows // 16, chips)
    piece = half_rows // owners

    def c_copy(ph, j):
        return pltpu.make_async_remote_copy(
            src_ref=psend.at[ph, j], dst_ref=crecv.at[ph, j],
            send_sem=c_ssem.at[ph, j], recv_sem=c_rsem.at[ph, j],
            device_id=(z, chip * 2 + 1 - core), device_id_type=MESH)

    def q_copy(ph, j, e, whose, owner):
        return pltpu.make_async_remote_copy(
            src_ref=hsend.at[ph, j, owner], dst_ref=qrecv.at[ph, j, whose],
            send_sem=q_ssem.at[ph, j, e], recv_sem=q_rsem.at[ph, j, whose],
            device_id=(z, ((chip + e) % chips) * 2 + core), device_id_type=MESH)

    def f_copy(ph, j, e, owner):
        return pltpu.make_async_remote_copy(
            src_ref=wout.at[ph, j, core, owner], dst_ref=wout.at[ph, j, core, owner],
            send_sem=f_ssem.at[ph, j, e], recv_sem=f_rsem.at[ph, j, owner],
            device_id=(z, ((chip + e) % chips) * 2 + core), device_id_type=MESH)

    def h_copy(ph, j, whose):
        return pltpu.make_async_remote_copy(
            src_ref=wout.at[ph, j, whose], dst_ref=wout.at[ph, j, whose],
            send_sem=h_ssem.at[ph, j], recv_sem=h_rsem.at[ph, j],
            device_id=(z, chip * 2 + 1 - core), device_id_type=MESH)

    def o_copy(ph, j):
        target = (out_wg1, out_wg2)[ph]
        if aligned:
            target = target.at[:, :, :, pl.ds(pl.multiple_of(j * ch, ch), ch)]
        else:
            target = target.at[j]
        return pltpu.make_async_copy(wout.at[ph, j], target, o_sem.at[ph, j])

    def sum_cores(ph, j):
        for o in range(owners):
            psend[ph, j, o] = part[ph, j, 1 - core, o].astype(BF16)
        c_copy(ph, j).start()

    def sum_chips(ph, j):
        c_copy(ph, j).wait_recv()
        for o in range(owners):
            v = part[ph, j, core, o] + crecv[ph, j, o].astype(F32)
            part[ph, j, core, o] = v
            hsend[ph, j, o] = v.astype(BF16)

        @pl.loop(1, chips)
        def _(e):
            peer = (chip + e) % chips

            @pl.when(peer < owners)
            def _():
                q_copy(ph, j, e, chip, peer).start()

    def spread_chips(ph, j):
        @pl.when(chip < owners)
        def _():
            @pl.loop(1, chips)
            def _(e):
                q_copy(ph, j, e, (chip + e) % chips, chip).wait_recv()
            v = part[ph, j, core, chip]
            for e in range(1, chips):
                v = v + qrecv[ph, j, (chip + e) % chips].astype(F32)
            wout[ph, j, core, chip] = v.astype(BF16)

            @pl.loop(1, chips)
            def _(e):
                f_copy(ph, j, e, chip).start()

    def spread_cores(ph, j):
        @pl.loop(1, chips)
        def _(e):
            peer = (chip + e) % chips

            @pl.when(peer < owners)
            def _():
                f_copy(ph, j, e, peer).wait_recv()
        h_copy(ph, j, core).start()

    def finish(ph, j):
        h_copy(ph, j, 1 - core).wait_recv()
        o_copy(ph, j).start()

    def put_part(ph, j, tap, value):
        start = tap * ch
        done = 0
        while done < ch:
            row = start + done
            side, o, at = row // half_rows, row % half_rows // piece, row % piece
            size = min(ch - done, piece - at)
            part[ph, j, side, o, at:at + size, :] = value[done:done + size, :]
            done += size

    stages = (sum_cores, sum_chips, spread_chips, spread_cores, finish)

    def of_step(k, fn):
        @pl.loop(0, 2)
        def _(way):
            block = z - k * (1 - 2 * way)

            @pl.when((k >= 0) & (k < n) & inside(block) & ((k > 0) | (way == 0)))
            def _():
                fn(block)

    passing = last_pass > 0

    def made_at(step):
        first = jnp.where(passing & (step > 0), jnp.where(step == last_pass, 1, step + 1), step)
        return first, step + 1

    def advance(ph, k):
        for age in range(1, len(stages)):
            step = k - age

            @pl.when((step >= 0) & (step < n))
            def _():
                @pl.loop(*made_at(step))
                def _(made):
                    of_step(made, functools.partial(stages[age], ph))

    def advance_all(ph, age):
        @pl.loop(0, n)
        def _(j):
            stages[age](ph, j)

    def field_grad(ph, block):
        grad = taken[block, 1:rows + 1, :, :].reshape(cells, 3 * ch)
        value = dot(x_t[ph], grad)
        for a in range(3):
            for b in range(3):
                put_part(ph, block, 3 * a + b, value[a * ch:(a + 1) * ch, (2 - b) * ch:(3 - b) * ch])

    def make_grad(ph, block):
        field_grad(ph, block)
        sum_cores(ph, block)

    def backward(ph):
        last = ph == 0

        def consume(k, block, q):
            into = taken.at[block]
            unpack_half(2 + ph, block, q, into)
            if last and q == HALVES - 1:
                @pl.when((k == 0) | (k >= last_pass))
                def _():
                    make_grad(ph, block)
            add_conv(q, into, None, lambda t: wv[ph, block, t * ch:(t + 1) * ch, :])

        def each(k):
            first, end = made_at(k)
            if last:
                @pl.loop(first, end - 1)
                def _(step):
                    of_step(step, functools.partial(make_grad, ph))
                advance(ph, k)
                for age in range(2, len(stages)):
                    @pl.when(k == age - 2)
                    def _():
                        advance_all(1, age)
            else:
                @pl.loop(first, jnp.where(passing | (k < n - 1), end, first))
                def _(step):
                    of_step(step, functools.partial(make_grad, ph))

                @pl.when(k == last_pass)
                def _():
                    to_flat(hid2, out_block)
        gather(2 + ph, consume, each)

    def fold(v):
        return jnp.sum(v.reshape(v.shape[0] // 8, 8, ch), axis=0)

    def flatten(v):
        return jnp.sum(v, axis=0, keepdims=True)

    zero = jnp.zeros((8, ch), F32)

    def local_moments(ref):
        def sums(start, size, carry):
            at = pl.ds(start, size)
            m = mask[at, :]
            return carry[0] + fold(ref[at, :] * m), carry[1] + fold(m)
        added, number = (flatten(v) for v in chunked(sums, (zero, zero)))
        middle = added / jnp.maximum(number, 1.0)

        def spread(start, size, carry):
            at = pl.ds(start, size)
            c = (ref[at, :] - middle) * mask[at, :]
            return carry + fold(c * c)
        return added, number, flatten(chunked(spread, zero))

    def moments(slot):
        take_stats(slot)
        got = [st_recv[slot, k] for k in range(s_count)]
        added = sum(g[0:1] for g in got)
        number = sum(g[1:2] for g in got)
        mean = added / number
        spread = 0.0
        for g in got:
            off = g[0:1] / jnp.maximum(g[1:2], 1.0) - mean
            spread = spread + (g[2:3] + g[1:2] * off * off)
        return mean, lax.rsqrt(spread / number + EPSILON), number

    def everywhere(fn):
        chunked(fn, 0)
        fn(cells, 2 * wide, 0)

    gain1, shift1, gain2, shift2 = (r[...] for r in (gain1_in, shift1_in, gain2_in, shift2_in))

    weights_over_z(0)

    below = lax.broadcasted_iota(jnp.int32, (band, band), 1) < lax.broadcasted_iota(jnp.int32, (band, band), 0)
    below = below.astype(F32).astype(BF16)

    def make_pack(h):
        lv = mask[h * band:(h + 1) * band, :]
        place = jnp.where(lv > 0.0, dot(below, lv.astype(BF16)), -1.0)
        places[h] = place
        across = place.T[0:1, :]
        spot = lax.broadcasted_iota(jnp.int32, (packed, band), 0).astype(F32)
        pack[h] = jnp.where(spot == across, 1.0, 0.0).astype(BF16)

    def make_unpack(h):
        for start in range(0, packed, ch):
            size = min(ch, packed - start)
            spot = start + lax.broadcasted_iota(jnp.int32, (band, size), 1)
            unpack[h, :, start:start + size] = jnp.where(
                places[h, :, :size] == spot.astype(F32), 1.0, 0.0).astype(BF16)

    for side in range(2):
        edge_copy(1 - side).wait_recv()
        there = jnp.where(s > 0, 1.0, 0.0) if side == 0 else jnp.where(s < s_count - 1, 1.0, 0.0)
        at = slice(cells + side * wide, cells + (side + 1) * wide)
        masked[at, :] = edge_recv[side, 0].astype(F32) * there
        mask[at, :] = edge_recv[side, 1].astype(F32) * there

    pack_field(0, masked, first=make_pack)
    for h in range(HALVES):
        make_unpack(h)
    forward(0, masked)
    send_rows(0, acc)
    send_stats(0, local_moments(acc))
    weights_round(1)
    mean1, scale1, count = moments(0)

    def activate_one(start, size, carry):
        at = pl.ds(start, size)
        main = start is not cells
        nv = ((acc if main else normed1)[at, :] - mean1) * scale1
        normed1[at, :] = nv
        hid[at, :] = gelu_parts(nv * gain1 + shift1)[0] * mask[at, :]
        if main:
            acc[at, :] = jnp.zeros((size, ch), F32)
        return carry

    def slope_one(start, size, carry):
        at = pl.ds(start, size)
        slope1[at, :] = gelu_parts(normed1[at, :] * gain1 + shift1)[1] * mask[at, :]
        return carry

    take_rows(0, normed1)
    pack_field(1, hid, activate_one)
    everywhere(slope_one)
    forward(1, hid)
    send_rows(1, acc)
    send_stats(1, local_moments(acc))
    mean2, scale2, _ = moments(1)

    def activate_two(source, start, size):
        at = pl.ds(start, size)
        nv = (source[at, :] - mean2) * scale2
        normed2[at, :] = nv
        value, slope = gelu_parts(nv * gain2 + shift2 + masked[at, :])
        t = cotm[at, :] * slope
        through[at, :] = t
        return value, nv, t

    def activate_main(start, size, carry):
        value, nv, t = activate_two(acc, start, size)
        at = pl.ds(start, size)
        hid2[at, :] = value * mask[at, :]
        acc[at, :] = jnp.zeros((size, ch), F32)
        return carry[0] + fold(t * nv), carry[1] + fold(t)

    send_stats(2, [flatten(v) for v in chunked(activate_main, (zero, zero))])
    take_rows(1, normed2)
    take_cotangent()
    activate_two(normed2, cells, edge)

    def gradient_sums(slot):
        take_stats(slot)
        got = [st_recv[slot, k] for k in range(s_count)]
        return sum(g[0:1] for g in got), sum(g[1:2] for g in got)

    def norm_back(upstream, normed, gain, scale, sums):
        gain_grad, shift_grad = sums
        factor = gain * scale
        level, tilt = shift_grad / count, gain_grad / count

        def fill(start, size, carry):
            at = pl.ds(start, size)
            v = upstream[at, :] - mask[at, :] * (level + normed[at, :] * tilt)
            hid[at, :] = factor * v
            return carry
        return fill

    sums2 = gradient_sums(2)
    pack_field(3, hid, norm_back(through, normed2, gain2, scale2, sums2))
    backward(1)

    send_rows(2, acc)

    def inner_main(start, size, carry):
        at = pl.ds(start, size)
        v = acc[at, :] * slope1[at, :]
        slope1[at, :] = v
        acc[at, :] = jnp.zeros((size, ch), F32)
        return carry[0] + fold(v * normed1[at, :]), carry[1] + fold(v)

    send_stats(3, [flatten(v) for v in chunked(inner_main, (zero, zero))])

    @pl.when(jnp.logical_not(passing))
    def _():
        of_step(n - 1, functools.partial(make_grad, 1))
    for side in range(2):
        row_copy(2, 1 - side).wait_recv()
        at = slice(cells + side * wide, cells + (side + 1) * wide)
        slope1[at, :] = row_recv[2, side] * slope1[at, :]
    sums1 = gradient_sums(3)
    pack_field(2, hid, norm_back(slope1, normed1, gain1, scale1, sums1))
    advance_all(1, 1)
    backward(0)
    advance(0, n)

    def finish_input(start, size, carry):
        at = pl.ds(start, size)
        acc[at, :] = (acc[at, :] + through[at, :]) * mask[at, :]
        return carry

    chunked(finish_input, 0)
    to_flat(acc, out_input)
    out_gain1[...], out_shift1[...] = sums1
    out_gain2[...], out_shift2[...] = sums2
    for extra in range(1, len(stages) - 1):
        advance(0, n + extra)

    for side in range(2):
        edge_copy(side).wait_send()
        cot_copy(side).wait_send()
        for slot in range(3):
            row_copy(slot, side).wait_send()

    @pl.loop(1, s_count)
    def _(k):
        for slot in range(4):
            st_copy(slot, k, s).wait_send()

    @pl.loop(1, n)
    def _(k):
        for which in range(2):
            wz_copy(which, k).wait_send()

    @pl.loop(1, w_parts)
    def _(k):
        for which in range(2):
            for slot in range(n - 1):
                wp_copy(which, slot, k, w_mine).wait_send()

    @pl.loop(0, n)
    def _(k):
        for sign in (1, -1):
            block = z - k * sign

            @pl.when((block >= 0) & (block < n) & (z + sign >= 0) & (z + sign < n))
            def _():
                for ph in range(4):
                    for q in range(HALVES):
                        ag_copy(ph, block, q, sign).wait_send()

    @pl.loop(0, n)
    def _(j):
        for ph in range(2):
            c_copy(ph, j).wait_send()
            h_copy(ph, j, core).wait_send()
            o_copy(ph, j).wait()

            @pl.loop(1, chips)
            def _(e):
                peer = (chip + e) % chips

                @pl.when(peer < owners)
                def _():
                    q_copy(ph, j, e, chip, peer).wait_send()

                @pl.when(chip < owners)
                def _():
                    f_copy(ph, j, e, chip).wait_send()


def finish_kernel(count, *refs):
    ins, outs = refs[:count], refs[count:2 * count]
    narrow, wide, in_sem, out_sem, take_sem, give_sem = refs[2 * count:2 * count + 6]
    held = refs[2 * count + 6:]
    rows = narrow.shape[1] // FINISH_PARTS
    parts = [(w, i, pl.ds(i * rows, rows)) for i in range(FINISH_PARTS) for w in range(2)]
    loads = [pltpu.make_async_copy(ins[w].at[at, :], narrow.at[w, at, :], in_sem.at[w, i]) for w, i, at in parts]
    stores = [pltpu.make_async_copy(wide.at[w, at, :], outs[w].at[at, :], out_sem.at[w, i]) for w, i, at in parts]
    takes = [pltpu.make_async_copy(ins[2 + k], v, take_sem.at[k]) for k, v in enumerate(held)]
    gives = [pltpu.make_async_copy(v, outs[2 + k], give_sem.at[k]) for k, v in enumerate(held)]
    for copy in loads + takes:
        copy.start()
    for load, store, (w, i, at) in zip(loads, stores, parts):
        load.wait()
        wide[w, at, :] = narrow[w, at, :].astype(F32)
        store.start()
    for take, give in zip(takes, gives):
        take.wait()
        give.start()
    for copy in stores + gives:
        copy.wait()


def per_device(n, s_count, blocks, weight_one, weight_two, gain_one, shift_one, gain_two, shift_two, cell_live, cotangent):
    rows, wide = cell_live.shape
    ch = blocks.shape[1] // wide
    cells = rows * wide
    total = cells + 2 * wide
    packed = -(-most_live(rows // HALVES, wide) // 16) * 16
    aligned = ch % 128 == 0
    chips = s_count // 2
    tap_rows = 9 * ch
    half_rows = tap_rows // 2
    owners = math.gcd(half_rows // 16, chips)
    piece = half_rows // owners

    if aligned:
        weight_one, weight_two = (w.reshape(tap_rows, n * ch) for w in (weight_one, weight_two))
    else:
        weight_one, weight_two = (
            w.reshape(tap_rows, n, ch).transpose(1, 0, 2) for w in (weight_one, weight_two))
    grad_shape = (2, owners, piece, n * ch) if aligned else (n, 2, owners, piece, ch)
    vmem = pl.BlockSpec(memory_space=pltpu.VMEM)
    hbm = pl.BlockSpec(memory_space=pl.ANY)
    sem = pltpu.SemaphoreType.DMA
    field = pltpu.VMEM((total, ch), F32)
    scratch = [
        pltpu.VMEM((ch * wide, 128), F32),
        pltpu.VMEM((2, n, tap_rows, ch), BF16),
        pltpu.VMEM((2, n - 1, tap_rows, ch), BF16),
        pltpu.VMEM((2, 3 * ch, cells), BF16),
        pltpu.VMEM((HALVES, packed, cells // HALVES), BF16),
        pltpu.VMEM((HALVES, cells // HALVES, packed), BF16),
        pltpu.VMEM((HALVES, cells // HALVES, ch), F32),
        pltpu.VMEM((2, 2, wide, ch), BF16),
        pltpu.VMEM((2, 2, wide, ch), BF16),
        pltpu.VMEM((2, wide, ch), BF16),
        pltpu.VMEM((2, wide, ch), BF16),
        field, field, field, field, field, field, field, field, field,
        pltpu.VMEM((total + 16, ch), F32),
        pltpu.VMEM((cells, ch), F32),
        pltpu.VMEM((4, n, 2 * wide + HALVES * packed, ch), BF16),
        pltpu.VMEM((n, rows + 2, wide, 3 * ch), BF16),
        pltpu.VMEM((2, n, 2, owners, piece, ch), F32),
        pltpu.VMEM((2, n, owners, piece, ch), BF16),
        pltpu.VMEM((2, n, owners, piece, ch), BF16),
        pltpu.VMEM((2, n, owners, piece, ch), BF16),
        pltpu.VMEM((2, n, chips, piece, ch), BF16),
        pltpu.VMEM((2, n, 2, owners, piece, ch), BF16),
        pltpu.VMEM((4, 8, ch), F32),
        pltpu.VMEM((4, s_count, 8, ch), F32),
        pltpu.VMEM((3, 2, wide, ch), F32),
        pltpu.VMEM((3, 2, wide, ch), F32),
        sem((2, n)),
        sem((2, n)), sem((2, n)),
        sem((2, n - 1, s_count)), sem((2, n - 1, s_count)),
        sem((2,)), sem((2,)),
        sem((2,)), sem((2,)),
        sem((4, 2, n, HALVES)), sem((4, n, HALVES)),
        sem((4, s_count)), sem((4, s_count)),
        sem((3, 2)), sem((3, 2)),
        sem((2, n)), sem((2, n)),
        sem((2, n, chips)), sem((2, n, chips)),
        sem((2, n, chips)), sem((2, n, chips)),
        sem((2, n)), sem((2, n)),
        sem((2, n)),
    ]
    block_out, input_grad, wg1, wg2, *sums = pl.pallas_call(
        functools.partial(block_kernel, n, s_count, rows, wide, ch, aligned, packed),
        out_shape=(
            jax.ShapeDtypeStruct((rows, ch * wide), BF16),
            jax.ShapeDtypeStruct((rows, ch * wide), F32),
            jax.ShapeDtypeStruct(grad_shape, BF16),
            jax.ShapeDtypeStruct(grad_shape, BF16),
            *[jax.ShapeDtypeStruct((1, ch), F32)] * 4,
        ),
        in_specs=[vmem] * 7 + [hbm] * 2,
        out_specs=(vmem, vmem, hbm, hbm, vmem, vmem, vmem, vmem),
        scratch_shapes=scratch,
        compiler_params=pltpu.CompilerParams(
            collective_id=0, has_side_effects=True, vmem_limit_bytes=60 * 1024 * 1024),
    )(blocks, cotangent, cell_live.T,
      *(v.reshape(1, ch) for v in (gain_one, shift_one, gain_two, shift_two)), weight_one, weight_two)

    if not aligned:
        def whole(grad):
            grad = grad.reshape(n, tap_rows, ch).transpose(1, 0, 2)
            return grad.astype(F32).reshape(9, ch, n * ch)
        return (block_out, input_grad, whole(wg1), whole(wg2), *(v.reshape(ch) for v in sums))

    wg1, wg2 = (w.reshape(tap_rows, n * ch) for w in (wg1, wg2))
    wide_grad = jax.ShapeDtypeStruct((tap_rows, n * ch), F32)
    moved = (block_out, input_grad, *sums)
    grad1, grad2, *moved = pl.pallas_call(
        functools.partial(finish_kernel, 2 + len(moved)),
        out_shape=(wide_grad, wide_grad, *(jax.ShapeDtypeStruct(v.shape, v.dtype) for v in moved)),
        in_specs=[pl.BlockSpec(memory_space=pl.ANY)] * (2 + len(moved)),
        out_specs=[pl.BlockSpec(memory_space=pl.ANY)] * (2 + len(moved)),
        scratch_shapes=[
            pltpu.VMEM((2, tap_rows, n * ch), BF16), pltpu.VMEM((2, tap_rows, n * ch), F32),
            sem((2, FINISH_PARTS)), sem((2, FINISH_PARTS)), sem((len(moved),)), sem((len(moved),)),
            *(pltpu.VMEM(v.shape, v.dtype) for v in moved),
        ],
        compiler_params=pltpu.CompilerParams(vmem_limit_bytes=64 * 1024 * 1024),
    )(wg1, wg2, *moved)
    block_out, input_grad, *sums = moved
    grads = (g.reshape(9, ch, n * ch) for g in (grad1, grad2))
    return (block_out, input_grad, *grads, *(v.reshape(ch) for v in sums))


def solution(mesh):
    return jax.shard_map(
        functools.partial(per_device, mesh.shape["chan"], mesh.shape["space"]),
        mesh=mesh,
        in_specs=(
            P("space", "chan"),
            P(None, "chan", None),
            P(None, "chan", None),
            P("chan"),
            P("chan"),
            P("chan"),
            P("chan"),
            P("space", None),
            P("space", "chan"),
        ),
        out_specs=(
            P("space", "chan"),
            P("space", "chan"),
            P(None, "chan", None),
            P(None, "chan", None),
            P("chan"),
            P("chan"),
            P("chan"),
            P("chan"),
        ),
        check_vma=False,
    )
```

```python
import functools
import math

import jax
import jax.numpy as jnp
from jax import lax
from jax.experimental import pallas as pl
from jax.experimental.pallas import tpu as pltpu
from jax.sharding import PartitionSpec as P

EPSILON = 1e-05
MESH = pl.DeviceIdType.MESH
F32 = jnp.float32
BF16 = jnp.bfloat16
ROOT_HALF = 0.7071067811865476
ROOT_TWO_PI = 0.3989422804014327
CHUNK = 64
FINISH_PARTS = 4
UNROLL = 2
HALVES = 2


def dot(a, b):
    return jnp.dot(a, b, preferred_element_type=F32)


def gelu_parts(v):
    upper = 0.5 * (1.0 + lax.erf(v * ROOT_HALF))
    slope = upper + v * (ROOT_TWO_PI * jnp.exp(-0.5 * v * v))
    return v * upper, slope


def block_kernel(n, s_count, rows, wide, ch, aligned, packed, *refs):
    (x_in, cot_in, live_in, gain1_in, shift1_in, gain2_in, shift2_in, w1_hbm, w2_hbm) = refs[:9]
    (out_block, out_input, out_wg1, out_wg2, out_gain1, out_shift1, out_gain2, out_shift2) = refs[9:17]
    (turned, wv, wf, x_t, edge_send, edge_recv, cot_send, cot_recv, cotm, mask, masked,
     normed1, normed2, through, slope1, hid, hid2, pad, acc, hold, taken,
     part, psend, crecv, hsend, qrecv, wout, st_send, st_recv, row_send, row_recv,
     w_sem, wz_ssem, wz_rsem, wp_ssem, wp_rsem, e_ssem, e_rsem, ce_ssem, ce_rsem, ag_ssem, ag_rsem,
     st_ssem, st_rsem, row_ssem, row_rsem, c_ssem, c_rsem, q_ssem, q_rsem,
     f_ssem, f_rsem, h_ssem, h_rsem, o_sem) = refs[17:]

    z = lax.axis_index("chan")
    s = lax.axis_index("space")
    cells = rows * wide
    total = cells + 2 * wide
    band = cells // HALVES
    core, chip, chips = s % 2, s // 2, s_count // 2
    before, after = (s + s_count - 1) % s_count, (s + 1) % s_count
    tap_rows = 9 * ch

    barrier = pltpu.get_barrier_semaphore()

    @pl.loop(1, s_count)
    def _(k):
        pl.semaphore_signal(barrier, inc=1, device_id=(z, (s + k) % s_count), device_id_type=MESH)

    @pl.loop(1, n)
    def _(k):
        pl.semaphore_signal(barrier, inc=1, device_id=((z + k) % n, s), device_id_type=MESH)

    w_copies = []
    for which, source in enumerate((w1_hbm, w2_hbm)):
        for d in range(n):
            block = source.at[:, d * ch:(d + 1) * ch] if aligned else source.at[d]
            w_copies.append(pltpu.make_async_copy(block, wv.at[which, d], w_sem.at[which, d]))
    for copy in w_copies:
        copy.start()

    def chunked(fn, init, first=0, count=cells):
        def step(i, carry):
            return fn(pl.multiple_of(first + i * CHUNK, CHUNK), CHUNK, carry)
        return lax.fori_loop(0, count // CHUNK, step, init, unroll=UNROLL)

    lanes = 128
    tiles = ch * wide // lanes

    def from_flat(flat, put):
        for i in range(tiles):
            turned[i * lanes:(i + 1) * lanes, 0:rows] = flat[:, i * lanes:(i + 1) * lanes].astype(F32).T
        for w in range(wide):
            put(pl.ds(w, rows, stride=wide), turned[pl.ds(w, ch, stride=wide), 0:rows].T)

    def to_flat(source, flat):
        for w in range(wide):
            turned[pl.ds(w, ch, stride=wide), 0:rows] = source[pl.ds(w, rows, stride=wide), :].T
        for i in range(tiles):
            flat[:, i * lanes:(i + 1) * lanes] = turned[i * lanes:(i + 1) * lanes, 0:rows].T.astype(flat.dtype)

    def put_masked(at, value):
        masked[at, :] = value

    from_flat(x_in, put_masked)

    cell = lax.broadcasted_iota(jnp.int32, (cells, rows), 0)
    pick = (cell // wide == lax.broadcasted_iota(jnp.int32, (cells, rows), 1)).astype(F32).astype(BF16)
    column_of = lax.broadcasted_iota(jnp.int32, (cells, wide), 0) % wide
    picked = lax.dot_general(pick, live_in[...].astype(BF16), (((1,), (1,)), ((), ())), preferred_element_type=F32)
    picked = jnp.where(column_of == lax.broadcasted_iota(jnp.int32, (cells, wide), 1), picked, 0.0)
    mask[0:cells, :] = dot(picked.astype(BF16), jnp.ones((wide, ch), BF16))

    def load_main(start, size, carry):
        at = pl.ds(start, size)
        lv = mask[at, :]
        masked[at, :] = masked[at, :] * lv
        return carry

    chunked(load_main, 0)
    for side, start in ((0, 0), (1, cells - wide)):
        edge_send[side, 0] = masked[start:start + wide, :].astype(BF16)
        edge_send[side, 1] = mask[start:start + wide, :].astype(BF16)

    acc[...] = jnp.zeros_like(acc)
    st_send[...] = jnp.zeros_like(st_send)

    pl.semaphore_wait(barrier, s_count - 1 + n - 1)

    def edge_copy(side):
        return pltpu.make_async_remote_copy(
            src_ref=edge_send.at[side], dst_ref=edge_recv.at[1 - side],
            send_sem=e_ssem.at[side], recv_sem=e_rsem.at[1 - side],
            device_id=(z, before if side == 0 else after), device_id_type=MESH)

    for side in range(2):
        edge_copy(side).start()

    def cot_copy(side):
        return pltpu.make_async_remote_copy(
            src_ref=cot_send.at[side], dst_ref=cot_recv.at[1 - side],
            send_sem=ce_ssem.at[side], recv_sem=ce_rsem.at[1 - side],
            device_id=(z, before if side == 0 else after), device_id_type=MESH)

    def load_cotangent():
        def put(at, value):
            cotm[at, :] = value
        from_flat(cot_in, put)

        def live_only(start, size, carry):
            at = pl.ds(start, size)
            cotm[at, :] = cotm[at, :] * mask[at, :]
            return carry
        chunked(live_only, 0)
        for side, start in ((0, 0), (1, cells - wide)):
            cot_send[side] = cotm[start:start + wide, :].astype(BF16)
            cot_copy(side).start()

    def take_cotangent():
        for side in range(2):
            cot_copy(1 - side).wait_recv()
            at = slice(cells + side * wide, cells + (side + 1) * wide)
            cotm[at, :] = cot_recv[side].astype(F32) * mask[at, :]

    w_parts = math.gcd(tap_rows // 16, s_count)
    w_rows = tap_rows // w_parts
    w_mine = s % w_parts
    w_group = s - w_mine

    def wz_copy(which, k):
        at = pl.ds(w_mine * w_rows, w_rows)
        slot = n - k - 1
        return pltpu.make_async_remote_copy(
            src_ref=wv.at[which, (z + k) % n, at, :], dst_ref=wf.at[which, slot, at, :],
            send_sem=wz_ssem.at[which, slot], recv_sem=wz_rsem.at[which, slot],
            device_id=((z + k) % n, s), device_id_type=MESH)

    def wp_copy(which, slot, k, whose):
        at = pl.ds(whose * w_rows, w_rows)
        return pltpu.make_async_remote_copy(
            src_ref=wf.at[which, slot, at, :], dst_ref=wf.at[which, slot, at, :],
            send_sem=wp_ssem.at[which, slot, k], recv_sem=wp_rsem.at[which, slot, whose],
            device_id=(z, w_group + (w_mine + k) % w_parts), device_id_type=MESH)

    def weights_over_z(which):
        for copy in w_copies[which * n:(which + 1) * n]:
            copy.wait()

        @pl.loop(1, n)
        def _(k):
            wz_copy(which, k).start()

    def slot_of(block):
        return (block - z + n - 1) % n

    def weights_round(which):
        @pl.loop(1, n)
        def _(distance):
            for sign in (1, -1):
                block = z - distance * sign

                @pl.when((block >= 0) & (block < n))
                def _():
                    slot = slot_of(block)
                    wz_copy(which, n - 1 - slot).wait_recv()

                    @pl.loop(1, w_parts)
                    def _(k):
                        wp_copy(which, slot, k, w_mine).start()

    def weights_arrived(which, slot):
        @pl.loop(1, w_parts)
        def _(k):
            wp_copy(which, slot, k, (w_mine + k) % w_parts).wait_recv()

    def row_copy(slot, side):
        return pltpu.make_async_remote_copy(
            src_ref=row_send.at[slot, side], dst_ref=row_recv.at[slot, 1 - side],
            send_sem=row_ssem.at[slot, side], recv_sem=row_rsem.at[slot, 1 - side],
            device_id=(z, before if side == 0 else after), device_id_type=MESH)

    def send_rows(slot, ref):
        for side, start in ((0, 0), (1, cells - wide)):
            row_send[slot, side] = ref[start:start + wide, :]
            row_copy(slot, side).start()

    def take_rows(slot, ref):
        for side in range(2):
            row_copy(slot, 1 - side).wait_recv()
            ref[cells + side * wide:cells + (side + 1) * wide, :] = row_recv[slot, side]

    def st_copy(slot, k, whose):
        return pltpu.make_async_remote_copy(
            src_ref=st_send.at[slot], dst_ref=st_recv.at[slot, whose],
            send_sem=st_ssem.at[slot, k], recv_sem=st_rsem.at[slot, whose],
            device_id=(z, (s + k) % s_count), device_id_type=MESH)

    def send_stats(slot, values):
        for i, v in enumerate(values):
            st_send[slot, i:i + 1, :] = v
        for k in range(1, s_count):
            st_copy(slot, k, s).start()
        st_recv[slot, s] = st_send[slot]

    def take_stats(slot):
        for k in range(1, s_count):
            st_copy(slot, k, (s + k) % s_count).wait_recv()

    strip = 8
    column = lax.broadcasted_iota(jnp.int32, (strip * wide, ch), 0) % wide

    def shift(target, first, count):
        size = count * wide
        where = column[:size]
        here = pad[pl.ds(8 + first * wide, size), :]
        left = jnp.where(where == 0, 0.0, pad[pl.ds(7 + first * wide, size), :])
        right = jnp.where(where == wide - 1, 0.0, pad[pl.ds(9 + first * wide, size), :])
        for b, v in enumerate((left, here, right)):
            target[pl.ds(first, count), :, b * ch:(b + 1) * ch] = v.astype(BF16).reshape(count, wide, ch)

    edge = 2 * wide
    ag_rows = ((0, edge + packed), (edge + packed, packed))
    band_rows = rows // HALVES

    def unpack_half(ph, block, q, target):
        if q == 0:
            pad[8:8 + wide, :] = hold[ph, block, 0:wide, :].astype(F32)
            pad[8 + wide + cells:8 + 2 * wide + cells, :] = hold[ph, block, wide:edge, :].astype(F32)
            shift(target, 0, 1)
            shift(target, rows + 1, 1)
        pad[8 + wide + q * band:8 + wide + (q + 1) * band, :] = (
            hold[ph, block, edge + q * packed:edge + (q + 1) * packed, :].astype(F32))

        for i in range(band_rows // strip):
            shift(target, 1 + q * band_rows + i * strip, strip)

    def add_conv(q, field, taps, turned_taps=None):
        first, last = (0, band_rows - 1) if q == 0 else (band_rows - 1, rows)
        count = last - first
        lhs = field[first:last + 2, :, :].reshape((count + 2) * wide, 3 * ch)
        if turned_taps is None:
            value = dot(lhs, jnp.concatenate([taps(a) for a in range(3)], axis=1))
        else:
            rhs = jnp.concatenate([
                jnp.concatenate([turned_taps(3 * (2 - a) + 2 - b) for b in range(3)], axis=1) for a in range(3)], axis=0)
            value = lax.dot_general(lhs, rhs, (((1,), (1,)), ((), ())), preferred_element_type=F32)
        at = pl.ds(first * wide, count * wide)
        acc[at, :] = acc[at, :] + sum(
            value[a * wide:(a + count) * wide, a * ch:(a + 1) * ch] for a in range(3))

    def ag_copy(ph, block, q, sign):
        at = pl.ds(*ag_rows[q])
        return pltpu.make_async_remote_copy(
            src_ref=hold.at[ph, block, at, :], dst_ref=hold.at[ph, block, at, :],
            send_sem=ag_ssem.at[ph, (1 - sign) // 2, block, q], recv_sem=ag_rsem.at[ph, block, q],
            device_id=(z + sign, s), device_id_type=MESH)

    def pack_field(ph, source, fill=None):
        if fill is not None:
            fill(cells, edge, 0)
        hold[ph, z, 0:edge, :] = source[cells:cells + edge, :].astype(BF16)
        for q in range(HALVES):
            if fill is not None:
                chunked(fill, 0, q * band, band)
            hold[ph, z, edge + q * packed:edge + (q + 1) * packed, :] = source[q * band:(q + 1) * band, :].astype(BF16)
            for sign in (1, -1):
                @pl.when((z + sign >= 0) & (z + sign < n))
                def _():
                    ag_copy(ph, z, q, sign).start()

    def inside(slice_at):
        return (slice_at >= 0) & (slice_at < n)

    def take_and_pass(ph, k, q, sign, passes=True, takes=True):
        block = z - k * sign

        @pl.when((k > 0) & inside(block))
        def _():
            if passes and takes:
                ag_copy(ph, block, q, sign).wait_recv()

            @pl.when(inside(z + sign))
            def _():
                if passes:
                    if not takes:
                        ag_copy(ph, block, q, sign).wait_recv()
                    ag_copy(ph, block, q, sign).start()

            if not passes:
                @pl.when(jnp.logical_not(inside(z + sign)))
                def _():
                    ag_copy(ph, block, q, sign).wait_recv()

    near = jnp.where(z < n - n // 2, 1, 0)

    def consume_way(k, q, way, consume):
        block = z - k * (1 - 2 * way)

        @pl.when((k >= 0) & (k < n) & inside(block) & ((k > 0) | (way == near)))
        def _():
            consume(k, block, q)

    def take_both(ph, k, q, **how):
        @pl.loop(0, 2)
        def _(i):
            way = (near + i) % 2
            take_and_pass(ph, k, q, 1 - 2 * way, **how)

    def gather(ph, consume, each):
        @pl.loop(0, n)
        def _(k):
            for q in range(HALVES):
                take_both(ph, k, q)
                if q:
                    consume_way(k, q - 1, 1 - near, consume)
                else:
                    consume_way(k - 1, HALVES - 1, 1 - near, consume)
                consume_way(k, q, near, consume)
            each(k)

    def gather_passing_first(ph, consume, each):
        @pl.loop(0, n)
        def _(k):
            @pl.when(k == 1)
            def _():
                @pl.loop(1, n)
                def _(ahead):
                    for q in range(HALVES):
                        take_both(ph, ahead, q, takes=False)
            for q in range(HALVES):
                take_both(ph, k, q, passes=False)

                @pl.loop(0, 2)
                def _(i):
                    consume_way(k, q, (near + i) % 2, consume)
            each(k)

    last_pass = jnp.maximum(jnp.where(z < n - 1, z, 0), jnp.where(z > 0, n - 1 - z, 0))

    def forward(ph, field):
        def consume(k, block, q):
            into = taken.at[block]
            unpack_half(ph, block, q, into)

            @pl.when(k == 0)
            def _():
                add_conv(q, into, lambda a: wv[ph, z, 3 * a * ch:3 * (a + 1) * ch, :])

            @pl.when(k > 0)
            def _():
                slot = slot_of(block)
                if q == 0:
                    weights_arrived(ph, slot)
                add_conv(q, into, lambda a: wf[ph, slot, 3 * a * ch:3 * (a + 1) * ch, :])

        def each(k):
            if ph == 0:
                @pl.when(k == 0)
                def _():
                    weights_round(0)

                @pl.when(k == 1)
                def _():
                    weights_over_z(1)

            @pl.when(k == last_pass)
            def _():
                turn_field(ph, field)
                if ph == 0:
                    load_cotangent()
        (gather if ph else gather_passing_first)(ph, consume, each)

    def turn_field(ph, field):
        main = [field[start:start + ch, :].T for start in range(0, cells, ch)]
        ends = field[cells:cells + edge, :]
        if edge < ch:
            ends = jnp.concatenate([ends, jnp.zeros((ch - edge, ch), F32)], axis=0)
        ends = ends.T
        for i, here in enumerate(main):
            left = jnp.concatenate(
                [ends[:, 0:wide] if i == 0 else main[i - 1][:, ch - wide:], here[:, 0:ch - wide]], axis=1)
            right = jnp.concatenate(
                [here[:, wide:], main[i + 1][:, 0:wide] if i + 1 < len(main) else ends[:, wide:edge]], axis=1)
            for a, v in enumerate((left, here, right)):
                x_t[ph, a * ch:(a + 1) * ch, i * ch:(i + 1) * ch] = v.astype(BF16)

    half_rows = tap_rows // 2
    owners = math.gcd(half_rows // 16, chips)
    piece = half_rows // owners

    def c_copy(ph, j):
        return pltpu.make_async_remote_copy(
            src_ref=psend.at[ph, j], dst_ref=crecv.at[ph, j],
            send_sem=c_ssem.at[ph, j], recv_sem=c_rsem.at[ph, j],
            device_id=(z, chip * 2 + 1 - core), device_id_type=MESH)

    def q_copy(ph, j, e, whose, owner):
        return pltpu.make_async_remote_copy(
            src_ref=hsend.at[ph, j, owner], dst_ref=qrecv.at[ph, j, whose],
            send_sem=q_ssem.at[ph, j, e], recv_sem=q_rsem.at[ph, j, whose],
            device_id=(z, ((chip + e) % chips) * 2 + core), device_id_type=MESH)

    def f_copy(ph, j, e, owner):
        return pltpu.make_async_remote_copy(
            src_ref=wout.at[ph, j, core, owner], dst_ref=wout.at[ph, j, core, owner],
            send_sem=f_ssem.at[ph, j, e], recv_sem=f_rsem.at[ph, j, owner],
            device_id=(z, ((chip + e) % chips) * 2 + core), device_id_type=MESH)

    def h_copy(ph, j, whose):
        return pltpu.make_async_remote_copy(
            src_ref=wout.at[ph, j, whose], dst_ref=wout.at[ph, j, whose],
            send_sem=h_ssem.at[ph, j], recv_sem=h_rsem.at[ph, j],
            device_id=(z, chip * 2 + 1 - core), device_id_type=MESH)

    def o_copy(ph, j):
        target = (out_wg1, out_wg2)[ph]
        if aligned:
            target = target.at[:, :, :, pl.ds(pl.multiple_of(j * ch, ch), ch)]
        else:
            target = target.at[j]
        return pltpu.make_async_copy(wout.at[ph, j], target, o_sem.at[ph, j])

    def sum_cores(ph, j):
        for o in range(owners):
            psend[ph, j, o] = part[ph, j, 1 - core, o].astype(BF16)
        c_copy(ph, j).start()

    def sum_chips(ph, j):
        c_copy(ph, j).wait_recv()
        for o in range(owners):
            v = part[ph, j, core, o] + crecv[ph, j, o].astype(F32)
            part[ph, j, core, o] = v
            hsend[ph, j, o] = v.astype(BF16)

        @pl.loop(1, chips)
        def _(e):
            peer = (chip + e) % chips

            @pl.when(peer < owners)
            def _():
                q_copy(ph, j, e, chip, peer).start()

    def spread_chips(ph, j):
        @pl.when(chip < owners)
        def _():
            @pl.loop(1, chips)
            def _(e):
                q_copy(ph, j, e, (chip + e) % chips, chip).wait_recv()
            v = part[ph, j, core, chip]
            for e in range(1, chips):
                v = v + qrecv[ph, j, (chip + e) % chips].astype(F32)
            wout[ph, j, core, chip] = v.astype(BF16)

            @pl.loop(1, chips)
            def _(e):
                f_copy(ph, j, e, chip).start()

    def spread_cores(ph, j):
        @pl.loop(1, chips)
        def _(e):
            peer = (chip + e) % chips

            @pl.when(peer < owners)
            def _():
                f_copy(ph, j, e, peer).wait_recv()
        h_copy(ph, j, core).start()

    def finish(ph, j):
        h_copy(ph, j, 1 - core).wait_recv()
        o_copy(ph, j).start()

    def put_part(ph, j, tap, value):
        start = tap * ch
        done = 0
        while done < ch:
            row = start + done
            side, o, at = row // half_rows, row % half_rows // piece, row % piece
            size = min(ch - done, piece - at)
            part[ph, j, side, o, at:at + size, :] = value[done:done + size, :]
            done += size

    stages = (sum_cores, sum_chips, spread_chips, spread_cores, finish)

    def of_step(k, fn):
        @pl.loop(0, 2)
        def _(way):
            block = z - k * (1 - 2 * way)

            @pl.when((k >= 0) & (k < n) & inside(block) & ((k > 0) | (way == 0)))
            def _():
                fn(block)

    passing = last_pass > 0

    def made_at(step):
        first = jnp.where(passing & (step > 0), jnp.where(step == last_pass, 1, step + 1), step)
        return first, step + 1

    def advance(ph, k):
        for age in range(1, len(stages)):
            step = k - age

            @pl.when((step >= 0) & (step < n))
            def _():
                @pl.loop(*made_at(step))
                def _(made):
                    of_step(made, functools.partial(stages[age], ph))

    def advance_all(ph, age):
        @pl.loop(0, n)
        def _(j):
            stages[age](ph, j)

    def field_grad(ph, block):
        grad = taken[block, 1:rows + 1, :, :].reshape(cells, 3 * ch)
        value = dot(x_t[ph], grad)
        for a in range(3):
            for b in range(3):
                put_part(ph, block, 3 * a + b, value[a * ch:(a + 1) * ch, (2 - b) * ch:(3 - b) * ch])

    def make_grad(ph, block):
        field_grad(ph, block)
        sum_cores(ph, block)

    def backward(ph):
        last = ph == 0

        def consume(k, block, q):
            into = taken.at[block]
            unpack_half(2 + ph, block, q, into)
            if last and q == HALVES - 1:
                @pl.when((k == 0) | (k >= last_pass))
                def _():
                    make_grad(ph, block)
            add_conv(q, into, None, lambda t: wv[ph, block, t * ch:(t + 1) * ch, :])

        def each(k):
            first, end = made_at(k)
            if last:
                @pl.loop(first, end - 1)
                def _(step):
                    of_step(step, functools.partial(make_grad, ph))
                advance(ph, k)
                for age in range(2, len(stages)):
                    @pl.when(k == age - 2)
                    def _():
                        advance_all(1, age)
            else:
                @pl.loop(first, jnp.where(passing | (k < n - 1), end, first))
                def _(step):
                    of_step(step, functools.partial(make_grad, ph))

                @pl.when(k == last_pass)
                def _():
                    to_flat(hid2, out_block)
        gather(2 + ph, consume, each)

    def fold(v):
        return jnp.sum(v.reshape(v.shape[0] // 8, 8, ch), axis=0)

    def flatten(v):
        return jnp.sum(v, axis=0, keepdims=True)

    zero = jnp.zeros((8, ch), F32)

    def local_moments(ref):
        def sums(start, size, carry):
            at = pl.ds(start, size)
            m = mask[at, :]
            return carry[0] + fold(ref[at, :] * m), carry[1] + fold(m)
        added, number = (flatten(v) for v in chunked(sums, (zero, zero)))
        middle = added / jnp.maximum(number, 1.0)

        def spread(start, size, carry):
            at = pl.ds(start, size)
            c = (ref[at, :] - middle) * mask[at, :]
            return carry + fold(c * c)
        return added, number, flatten(chunked(spread, zero))

    def moments(slot):
        take_stats(slot)
        got = [st_recv[slot, k] for k in range(s_count)]
        added = sum(g[0:1] for g in got)
        number = sum(g[1:2] for g in got)
        mean = added / number
        spread = 0.0
        for g in got:
            off = g[0:1] / jnp.maximum(g[1:2], 1.0) - mean
            spread = spread + (g[2:3] + g[1:2] * off * off)
        return mean, lax.rsqrt(spread / number + EPSILON), number

    def everywhere(fn):
        chunked(fn, 0)
        fn(cells, 2 * wide, 0)

    gain1, shift1, gain2, shift2 = (r[...] for r in (gain1_in, shift1_in, gain2_in, shift2_in))

    weights_over_z(0)

    for side in range(2):
        edge_copy(1 - side).wait_recv()
        there = jnp.where(s > 0, 1.0, 0.0) if side == 0 else jnp.where(s < s_count - 1, 1.0, 0.0)
        at = slice(cells + side * wide, cells + (side + 1) * wide)
        masked[at, :] = edge_recv[side, 0].astype(F32) * there
        mask[at, :] = edge_recv[side, 1].astype(F32) * there

    pack_field(0, masked)
    forward(0, masked)
    send_rows(0, acc)
    send_stats(0, local_moments(acc))
    weights_round(1)
    mean1, scale1, count = moments(0)

    def activate_one(start, size, carry):
        at = pl.ds(start, size)
        main = start is not cells
        nv = ((acc if main else normed1)[at, :] - mean1) * scale1
        normed1[at, :] = nv
        hid[at, :] = gelu_parts(nv * gain1 + shift1)[0] * mask[at, :]
        if main:
            acc[at, :] = jnp.zeros((size, ch), F32)
        return carry

    def slope_one(start, size, carry):
        at = pl.ds(start, size)
        slope1[at, :] = gelu_parts(normed1[at, :] * gain1 + shift1)[1] * mask[at, :]
        return carry

    take_rows(0, normed1)
    pack_field(1, hid, activate_one)
    everywhere(slope_one)
    forward(1, hid)
    send_rows(1, acc)
    send_stats(1, local_moments(acc))
    mean2, scale2, _ = moments(1)

    def activate_two(source, start, size):
        at = pl.ds(start, size)
        nv = (source[at, :] - mean2) * scale2
        normed2[at, :] = nv
        value, slope = gelu_parts(nv * gain2 + shift2 + masked[at, :])
        t = cotm[at, :] * slope
        through[at, :] = t
        return value, nv, t

    def activate_main(start, size, carry):
        value, nv, t = activate_two(acc, start, size)
        at = pl.ds(start, size)
        hid2[at, :] = value * mask[at, :]
        acc[at, :] = jnp.zeros((size, ch), F32)
        return carry[0] + fold(t * nv), carry[1] + fold(t)

    send_stats(2, [flatten(v) for v in chunked(activate_main, (zero, zero))])
    take_rows(1, normed2)
    take_cotangent()
    activate_two(normed2, cells, edge)

    def gradient_sums(slot):
        take_stats(slot)
        got = [st_recv[slot, k] for k in range(s_count)]
        return sum(g[0:1] for g in got), sum(g[1:2] for g in got)

    def norm_back(upstream, normed, gain, scale, sums):
        gain_grad, shift_grad = sums
        factor = gain * scale
        level, tilt = shift_grad / count, gain_grad / count

        def fill(start, size, carry):
            at = pl.ds(start, size)
            v = upstream[at, :] - mask[at, :] * (level + normed[at, :] * tilt)
            hid[at, :] = factor * v
            return carry
        return fill

    sums2 = gradient_sums(2)
    pack_field(3, hid, norm_back(through, normed2, gain2, scale2, sums2))
    backward(1)

    send_rows(2, acc)

    def inner_main(start, size, carry):
        at = pl.ds(start, size)
        v = acc[at, :] * slope1[at, :]
        slope1[at, :] = v
        acc[at, :] = jnp.zeros((size, ch), F32)
        return carry[0] + fold(v * normed1[at, :]), carry[1] + fold(v)

    send_stats(3, [flatten(v) for v in chunked(inner_main, (zero, zero))])

    @pl.when(jnp.logical_not(passing))
    def _():
        of_step(n - 1, functools.partial(make_grad, 1))
    for side in range(2):
        row_copy(2, 1 - side).wait_recv()
        at = slice(cells + side * wide, cells + (side + 1) * wide)
        slope1[at, :] = row_recv[2, side] * slope1[at, :]
    sums1 = gradient_sums(3)
    pack_field(2, hid, norm_back(slope1, normed1, gain1, scale1, sums1))
    advance_all(1, 1)
    backward(0)
    advance(0, n)

    def finish_input(start, size, carry):
        at = pl.ds(start, size)
        acc[at, :] = (acc[at, :] + through[at, :]) * mask[at, :]
        return carry

    chunked(finish_input, 0)
    to_flat(acc, out_input)
    out_gain1[...], out_shift1[...] = sums1
    out_gain2[...], out_shift2[...] = sums2
    for extra in range(1, len(stages) - 1):
        advance(0, n + extra)

    for side in range(2):
        edge_copy(side).wait_send()
        cot_copy(side).wait_send()
        for slot in range(3):
            row_copy(slot, side).wait_send()

    @pl.loop(1, s_count)
    def _(k):
        for slot in range(4):
            st_copy(slot, k, s).wait_send()

    @pl.loop(1, n)
    def _(k):
        for which in range(2):
            wz_copy(which, k).wait_send()

    @pl.loop(1, w_parts)
    def _(k):
        for which in range(2):
            for slot in range(n - 1):
                wp_copy(which, slot, k, w_mine).wait_send()

    @pl.loop(0, n)
    def _(k):
        for sign in (1, -1):
            block = z - k * sign

            @pl.when((block >= 0) & (block < n) & (z + sign >= 0) & (z + sign < n))
            def _():
                for ph in range(4):
                    for q in range(HALVES):
                        ag_copy(ph, block, q, sign).wait_send()

    @pl.loop(0, n)
    def _(j):
        for ph in range(2):
            c_copy(ph, j).wait_send()
            h_copy(ph, j, core).wait_send()
            o_copy(ph, j).wait()

            @pl.loop(1, chips)
            def _(e):
                peer = (chip + e) % chips

                @pl.when(peer < owners)
                def _():
                    q_copy(ph, j, e, chip, peer).wait_send()

                @pl.when(chip < owners)
                def _():
                    f_copy(ph, j, e, chip).wait_send()


def finish_kernel(count, *refs):
    ins, outs = refs[:count], refs[count:2 * count]
    narrow, wide, in_sem, out_sem, take_sem, give_sem = refs[2 * count:2 * count + 6]
    held = refs[2 * count + 6:]
    rows = narrow.shape[1] // FINISH_PARTS
    parts = [(w, i, pl.ds(i * rows, rows)) for i in range(FINISH_PARTS) for w in range(2)]
    loads = [pltpu.make_async_copy(ins[w].at[at, :], narrow.at[w, at, :], in_sem.at[w, i]) for w, i, at in parts]
    stores = [pltpu.make_async_copy(wide.at[w, at, :], outs[w].at[at, :], out_sem.at[w, i]) for w, i, at in parts]
    takes = [pltpu.make_async_copy(ins[2 + k], v, take_sem.at[k]) for k, v in enumerate(held)]
    gives = [pltpu.make_async_copy(v, outs[2 + k], give_sem.at[k]) for k, v in enumerate(held)]
    for copy in loads + takes:
        copy.start()
    for load, store, (w, i, at) in zip(loads, stores, parts):
        load.wait()
        wide[w, at, :] = narrow[w, at, :].astype(F32)
        store.start()
    for take, give in zip(takes, gives):
        take.wait()
        give.start()
    for copy in stores + gives:
        copy.wait()


def per_device(n, s_count, blocks, weight_one, weight_two, gain_one, shift_one, gain_two, shift_two, cell_live, cotangent):
    rows, wide = cell_live.shape
    ch = blocks.shape[1] // wide
    cells = rows * wide
    total = cells + 2 * wide
    packed = cells // HALVES
    aligned = ch % 128 == 0
    chips = s_count // 2
    tap_rows = 9 * ch
    half_rows = tap_rows // 2
    owners = math.gcd(half_rows // 16, chips)
    piece = half_rows // owners

    if aligned:
        weight_one, weight_two = (w.reshape(tap_rows, n * ch) for w in (weight_one, weight_two))
    else:
        weight_one, weight_two = (
            w.reshape(tap_rows, n, ch).transpose(1, 0, 2) for w in (weight_one, weight_two))
    grad_shape = (2, owners, piece, n * ch) if aligned else (n, 2, owners, piece, ch)
    vmem = pl.BlockSpec(memory_space=pltpu.VMEM)
    hbm = pl.BlockSpec(memory_space=pl.ANY)
    sem = pltpu.SemaphoreType.DMA
    field = pltpu.VMEM((total, ch), F32)
    scratch = [
        pltpu.VMEM((ch * wide, 128), F32),
        pltpu.VMEM((2, n, tap_rows, ch), BF16),
        pltpu.VMEM((2, n - 1, tap_rows, ch), BF16),
        pltpu.VMEM((2, 3 * ch, cells), BF16),
        pltpu.VMEM((2, 2, wide, ch), BF16),
        pltpu.VMEM((2, 2, wide, ch), BF16),
        pltpu.VMEM((2, wide, ch), BF16),
        pltpu.VMEM((2, wide, ch), BF16),
        field, field, field, field, field, field, field, field, field,
        pltpu.VMEM((total + 16, ch), F32),
        pltpu.VMEM((cells, ch), F32),
        pltpu.VMEM((4, n, 2 * wide + HALVES * packed, ch), BF16),
        pltpu.VMEM((n, rows + 2, wide, 3 * ch), BF16),
        pltpu.VMEM((2, n, 2, owners, piece, ch), F32),
        pltpu.VMEM((2, n, owners, piece, ch), BF16),
        pltpu.VMEM((2, n, owners, piece, ch), BF16),
        pltpu.VMEM((2, n, owners, piece, ch), BF16),
        pltpu.VMEM((2, n, chips, piece, ch), BF16),
        pltpu.VMEM((2, n, 2, owners, piece, ch), BF16),
        pltpu.VMEM((4, 8, ch), F32),
        pltpu.VMEM((4, s_count, 8, ch), F32),
        pltpu.VMEM((3, 2, wide, ch), F32),
        pltpu.VMEM((3, 2, wide, ch), F32),
        sem((2, n)),
        sem((2, n)), sem((2, n)),
        sem((2, n - 1, s_count)), sem((2, n - 1, s_count)),
        sem((2,)), sem((2,)),
        sem((2,)), sem((2,)),
        sem((4, 2, n, HALVES)), sem((4, n, HALVES)),
        sem((4, s_count)), sem((4, s_count)),
        sem((3, 2)), sem((3, 2)),
        sem((2, n)), sem((2, n)),
        sem((2, n, chips)), sem((2, n, chips)),
        sem((2, n, chips)), sem((2, n, chips)),
        sem((2, n)), sem((2, n)),
        sem((2, n)),
    ]
    block_out, input_grad, wg1, wg2, *sums = pl.pallas_call(
        functools.partial(block_kernel, n, s_count, rows, wide, ch, aligned, packed),
        out_shape=(
            jax.ShapeDtypeStruct((rows, ch * wide), BF16),
            jax.ShapeDtypeStruct((rows, ch * wide), F32),
            jax.ShapeDtypeStruct(grad_shape, BF16),
            jax.ShapeDtypeStruct(grad_shape, BF16),
            *[jax.ShapeDtypeStruct((1, ch), F32)] * 4,
        ),
        in_specs=[vmem] * 7 + [hbm] * 2,
        out_specs=(vmem, vmem, hbm, hbm, vmem, vmem, vmem, vmem),
        scratch_shapes=scratch,
        compiler_params=pltpu.CompilerParams(
            collective_id=0, has_side_effects=True, vmem_limit_bytes=60 * 1024 * 1024),
    )(blocks, cotangent, cell_live.T,
      *(v.reshape(1, ch) for v in (gain_one, shift_one, gain_two, shift_two)), weight_one, weight_two)

    if not aligned:
        def whole(grad):
            grad = grad.reshape(n, tap_rows, ch).transpose(1, 0, 2)
            return grad.astype(F32).reshape(9, ch, n * ch)
        return (block_out, input_grad, whole(wg1), whole(wg2), *(v.reshape(ch) for v in sums))

    wg1, wg2 = (w.reshape(tap_rows, n * ch) for w in (wg1, wg2))
    wide_grad = jax.ShapeDtypeStruct((tap_rows, n * ch), F32)
    moved = (block_out, input_grad, *sums)
    grad1, grad2, *moved = pl.pallas_call(
        functools.partial(finish_kernel, 2 + len(moved)),
        out_shape=(wide_grad, wide_grad, *(jax.ShapeDtypeStruct(v.shape, v.dtype) for v in moved)),
        in_specs=[pl.BlockSpec(memory_space=pl.ANY)] * (2 + len(moved)),
        out_specs=[pl.BlockSpec(memory_space=pl.ANY)] * (2 + len(moved)),
        scratch_shapes=[
            pltpu.VMEM((2, tap_rows, n * ch), BF16), pltpu.VMEM((2, tap_rows, n * ch), F32),
            sem((2, FINISH_PARTS)), sem((2, FINISH_PARTS)), sem((len(moved),)), sem((len(moved),)),
            *(pltpu.VMEM(v.shape, v.dtype) for v in moved),
        ],
        compiler_params=pltpu.CompilerParams(vmem_limit_bytes=64 * 1024 * 1024),
    )(wg1, wg2, *moved)
    block_out, input_grad, *sums = moved
    grads = (g.reshape(9, ch, n * ch) for g in (grad1, grad2))
    return (block_out, input_grad, *grads, *(v.reshape(ch) for v in sums))


def solution(mesh):
    return jax.shard_map(
        functools.partial(per_device, mesh.shape["chan"], mesh.shape["space"]),
        mesh=mesh,
        in_specs=(
            P("space", "chan"),
            P(None, "chan", None),
            P(None, "chan", None),
            P("chan"),
            P("chan"),
            P("chan"),
            P("chan"),
            P("space", None),
            P("space", "chan"),
        ),
        out_specs=(
            P("space", "chan"),
            P("space", "chan"),
            P(None, "chan", None),
            P(None, "chan", None),
            P("chan"),
            P("chan"),
            P("chan"),
            P("chan"),
        ),
        check_vma=False,
    )
```

```python
import functools
import math

import jax
import jax.numpy as jnp
from jax import lax
from jax.experimental import pallas as pl
from jax.experimental.pallas import tpu as pltpu
from jax.sharding import PartitionSpec as P

EPSILON = 1e-05
MESH = pl.DeviceIdType.MESH
F32 = jnp.float32
BF16 = jnp.bfloat16
ROOT_HALF = 0.7071067811865476
ROOT_TWO_PI = 0.3989422804014327
CHUNK = 64
FINISH_PARTS = 4
UNROLL = 2
HALVES = 2
LARGE, SMALL = 7, 3


def dot(a, b):
    return jnp.dot(a, b, preferred_element_type=F32)


def gelu_parts(v):
    upper = 0.5 * (1.0 + lax.erf(v * ROOT_HALF))
    slope = upper + v * (ROOT_TWO_PI * jnp.exp(-0.5 * v * v))
    return v * upper, slope


def most_live(rows, wide):
    units = (wide + 1) // (SMALL + 1)
    live_rows = rows - rows // (LARGE + 1)
    return min(rows * wide, math.ceil(units * live_rows * LARGE / 2))


def block_kernel(n, s_count, rows, wide, ch, aligned, packed, *refs):
    (x_in, cot_in, live_in, gain1_in, shift1_in, gain2_in, shift2_in, w1_hbm, w2_hbm) = refs[:9]
    (out_block, out_input, out_wg1, out_wg2, out_gain1, out_shift1, out_gain2, out_shift2) = refs[9:17]
    (turned, wv, wf, x_t, pack, unpack, places, edge_send, edge_recv, cot_send, cot_recv, cotm, mask, masked,
     normed1, normed2, through, slope1, hid, hid2, pad, acc, hold, taken,
     part, psend, crecv, hsend, qrecv, wout, st_send, st_recv, row_send, row_recv, flat_block, flat_input, cot_flat,
     w_sem, wz_ssem, wz_rsem, wp_ssem, wp_rsem, wh_ssem, wh_rsem, e_ssem, e_rsem, ce_ssem, ce_rsem, ag_ssem, ag_rsem,
     st_ssem, st_rsem, row_ssem, row_rsem, c_ssem, c_rsem, q_ssem, q_rsem,
     f_ssem, f_rsem, h_ssem, h_rsem, o_sem, r_sem) = refs[17:]

    z = lax.axis_index("chan")
    s = lax.axis_index("space")
    cells = rows * wide
    total = cells + 2 * wide
    band = cells // HALVES
    core, chip, chips = s % 2, s // 2, s_count // 2
    before, after = (s + s_count - 1) % s_count, (s + 1) % s_count
    tap_rows = 9 * ch
    half_rows = tap_rows // 2
    owners = math.gcd(half_rows // 16, chips)
    piece = half_rows // owners

    barrier = pltpu.get_barrier_semaphore()

    @pl.loop(1, s_count)
    def _(k):
        pl.semaphore_signal(barrier, inc=1, device_id=(z, (s + k) % s_count), device_id_type=MESH)

    @pl.loop(1, n)
    def _(k):
        pl.semaphore_signal(barrier, inc=1, device_id=((z + k) % n, s), device_id_type=MESH)

    w_copies = []
    for which, source in enumerate((w1_hbm, w2_hbm)):
        for d in range(n):
            block = source.at[:, d * ch:(d + 1) * ch] if aligned else source.at[d]
            w_copies.append(pltpu.make_async_copy(block, wv.at[which, d], w_sem.at[which, d]))
    for copy in w_copies:
        copy.start()

    cot_load = pltpu.make_async_copy(cot_in, cot_flat, r_sem.at[2])
    cot_load.start()

    def chunked(fn, init, first=0, count=cells):
        def step(i, carry):
            return fn(pl.multiple_of(first + i * CHUNK, CHUNK), CHUNK, carry)
        return lax.fori_loop(0, count // CHUNK, step, init, unroll=UNROLL)

    lanes = 128
    tiles = ch * wide // lanes

    def from_flat(flat, put):
        for i in range(tiles):
            turned[i * lanes:(i + 1) * lanes, 0:rows] = flat[:, i * lanes:(i + 1) * lanes].astype(F32).T
        for w in range(wide):
            put(pl.ds(w, rows, stride=wide), turned[pl.ds(w, ch, stride=wide), 0:rows].T)

    def to_flat(source, flat):
        for w in range(wide):
            turned[pl.ds(w, ch, stride=wide), 0:rows] = source[pl.ds(w, rows, stride=wide), :].T
        for i in range(tiles):
            flat[:, i * lanes:(i + 1) * lanes] = turned[i * lanes:(i + 1) * lanes, 0:rows].T.astype(flat.dtype)

    def put_masked(at, value):
        masked[at, :] = value

    from_flat(x_in, put_masked)

    cell = lax.broadcasted_iota(jnp.int32, (cells, rows), 0)
    pick = (cell // wide == lax.broadcasted_iota(jnp.int32, (cells, rows), 1)).astype(F32).astype(BF16)
    column_of = lax.broadcasted_iota(jnp.int32, (cells, wide), 0) % wide
    picked = lax.dot_general(pick, live_in[...].astype(BF16), (((1,), (1,)), ((), ())), preferred_element_type=F32)
    picked = jnp.where(column_of == lax.broadcasted_iota(jnp.int32, (cells, wide), 1), picked, 0.0)
    mask[0:cells, :] = dot(picked.astype(BF16), jnp.ones((wide, ch), BF16))

    def load_main(start, size, carry):
        at = pl.ds(start, size)
        lv = mask[at, :]
        masked[at, :] = masked[at, :] * lv
        return carry

    chunked(load_main, 0)
    for side, start in ((0, 0), (1, cells - wide)):
        edge_send[side, 0] = masked[start:start + wide, :].astype(BF16)
        edge_send[side, 1] = mask[start:start + wide, :].astype(BF16)

    acc[...] = jnp.zeros_like(acc)
    st_send[...] = jnp.zeros_like(st_send)

    pl.semaphore_wait(barrier, s_count - 1 + n - 1)

    def edge_copy(side):
        return pltpu.make_async_remote_copy(
            src_ref=edge_send.at[side], dst_ref=edge_recv.at[1 - side],
            send_sem=e_ssem.at[side], recv_sem=e_rsem.at[1 - side],
            device_id=(z, before if side == 0 else after), device_id_type=MESH)

    for side in range(2):
        edge_copy(side).start()

    def cot_copy(side):
        return pltpu.make_async_remote_copy(
            src_ref=cot_send.at[side], dst_ref=cot_recv.at[1 - side],
            send_sem=ce_ssem.at[side], recv_sem=ce_rsem.at[1 - side],
            device_id=(z, before if side == 0 else after), device_id_type=MESH)

    def load_cotangent():
        def put(at, value):
            cotm[at, :] = value
        cot_load.wait()
        from_flat(cot_flat, put)

        def live_only(start, size, carry):
            at = pl.ds(start, size)
            cotm[at, :] = cotm[at, :] * mask[at, :]
            return carry
        chunked(live_only, 0)
        for side, start in ((0, 0), (1, cells - wide)):
            cot_send[side] = cotm[start:start + wide, :].astype(BF16)
            cot_copy(side).start()

    def take_cotangent():
        for side in range(2):
            cot_copy(1 - side).wait_recv()
            at = slice(cells + side * wide, cells + (side + 1) * wide)
            cotm[at, :] = cot_recv[side].astype(F32) * mask[at, :]

    w_group = chip - chip % owners
    w_mine = pl.ds(core * half_rows + (chip % owners) * piece, piece)

    def wz_copy(which, k):
        slot = n - k - 1
        return pltpu.make_async_remote_copy(
            src_ref=wv.at[which, (z + k) % n, w_mine, :], dst_ref=wf.at[which, slot, w_mine, :],
            send_sem=wz_ssem.at[which, slot], recv_sem=wz_rsem.at[which, slot],
            device_id=((z + k) % n, s), device_id_type=MESH)

    def wp_copy(which, slot, k, whose):
        at = pl.ds(core * half_rows + whose * piece, piece)
        return pltpu.make_async_remote_copy(
            src_ref=wf.at[which, slot, at, :], dst_ref=wf.at[which, slot, at, :],
            send_sem=wp_ssem.at[which, slot, k], recv_sem=wp_rsem.at[which, slot, whose],
            device_id=(z, (w_group + (chip + k) % owners) * 2 + core), device_id_type=MESH)

    def wh_copy(which, slot, whose):
        at = pl.ds(whose * half_rows, half_rows)
        return pltpu.make_async_remote_copy(
            src_ref=wf.at[which, slot, at, :], dst_ref=wf.at[which, slot, at, :],
            send_sem=wh_ssem.at[which, slot], recv_sem=wh_rsem.at[which, slot],
            device_id=(z, chip * 2 + 1 - core), device_id_type=MESH)

    def weights_over_z(which):
        for copy in w_copies[which * n:(which + 1) * n]:
            copy.wait()
        for k in range(1, n):
            wz_copy(which, k).start()

    def slot_of(block):
        return (block - z + n - 1) % n

    def weights_round(which):
        @pl.loop(1, n)
        def _(distance):
            for sign in (1, -1):
                block = z - distance * sign

                @pl.when((block >= 0) & (block < n))
                def _():
                    slot = slot_of(block)
                    wz_copy(which, n - 1 - slot).wait_recv()
                    for k in range(1, owners):
                        wp_copy(which, slot, k, chip % owners).start()

    def weights_to_core(which, slot):
        for k in range(1, owners):
            wp_copy(which, slot, k, (chip + k) % owners).wait_recv()
        wh_copy(which, slot, core).start()

    def weights_arrived(which, slot):
        wh_copy(which, slot, 1 - core).wait_recv()

    def weights_sent(which):
        for k in range(1, n):
            wz_copy(which, k).wait_send()
        for slot in range(n - 1):
            for k in range(1, owners):
                wp_copy(which, slot, k, chip % owners).wait_send()
            wh_copy(which, slot, core).wait_send()

    def row_copy(slot, side):
        return pltpu.make_async_remote_copy(
            src_ref=row_send.at[slot, side], dst_ref=row_recv.at[slot, 1 - side],
            send_sem=row_ssem.at[slot, side], recv_sem=row_rsem.at[slot, 1 - side],
            device_id=(z, before if side == 0 else after), device_id_type=MESH)

    def send_rows(slot, ref):
        for side, start in ((0, 0), (1, cells - wide)):
            row_send[slot, side] = ref[start:start + wide, :]
            row_copy(slot, side).start()

    def take_rows(slot, ref):
        for side in range(2):
            row_copy(slot, 1 - side).wait_recv()
            ref[cells + side * wide:cells + (side + 1) * wide, :] = row_recv[slot, side]

    def st_copy(slot, k, whose):
        return pltpu.make_async_remote_copy(
            src_ref=st_send.at[slot], dst_ref=st_recv.at[slot, whose],
            send_sem=st_ssem.at[slot, k], recv_sem=st_rsem.at[slot, whose],
            device_id=(z, (s + k) % s_count), device_id_type=MESH)

    def send_stats(slot, values):
        for i, v in enumerate(values):
            st_send[slot, i:i + 1, :] = v
        for k in range(1, s_count):
            st_copy(slot, k, s).start()
        st_recv[slot, s] = st_send[slot]

    def take_stats(slot):
        for k in range(1, s_count):
            st_copy(slot, k, (s + k) % s_count).wait_recv()

    strip = 8
    column = lax.broadcasted_iota(jnp.int32, (strip * wide, ch), 0) % wide

    def shift(target, first, count):
        size = count * wide
        where = column[:size]
        here = pad[pl.ds(8 + first * wide, size), :]
        left = jnp.where(where == 0, 0.0, pad[pl.ds(7 + first * wide, size), :])
        right = jnp.where(where == wide - 1, 0.0, pad[pl.ds(9 + first * wide, size), :])
        for b, v in enumerate((left, here, right)):
            target[pl.ds(first, count), :, b * ch:(b + 1) * ch] = v.astype(BF16).reshape(count, wide, ch)

    edge = 2 * wide
    ag_rows = ((0, edge + packed), (edge + packed, packed))
    band_rows = rows // HALVES

    def unpack_half(ph, block, q, target):
        if q == 0:
            pad[8:8 + wide, :] = hold[ph, block, 0:wide, :].astype(F32)
            pad[8 + wide + cells:8 + 2 * wide + cells, :] = hold[ph, block, wide:edge, :].astype(F32)
            shift(target, 0, 1)
            shift(target, rows + 1, 1)
        pad[8 + wide + q * band:8 + wide + (q + 1) * band, :] = dot(
            unpack[q], hold[ph, block, edge + q * packed:edge + (q + 1) * packed, :])

        for i in range(band_rows // strip):
            shift(target, 1 + q * band_rows + i * strip, strip)

    def add_conv(q, field, taps, turned_taps=None):
        first, last = (0, band_rows - 1) if q == 0 else (band_rows - 1, rows)
        count = last - first
        lhs = field[first:last + 2, :, :].reshape((count + 2) * wide, 3 * ch)
        if turned_taps is None:
            value = dot(lhs, jnp.concatenate([taps(a) for a in range(3)], axis=1))
        else:
            rhs = jnp.concatenate([
                jnp.concatenate([turned_taps(3 * (2 - a) + 2 - b) for b in range(3)], axis=1) for a in range(3)], axis=0)
            value = lax.dot_general(lhs, rhs, (((1,), (1,)), ((), ())), preferred_element_type=F32)
        at = pl.ds(first * wide, count * wide)
        acc[at, :] = acc[at, :] + sum(
            value[a * wide:(a + count) * wide, a * ch:(a + 1) * ch] for a in range(3))

    def ag_copy(ph, block, q, sign):
        at = pl.ds(*ag_rows[q])
        return pltpu.make_async_remote_copy(
            src_ref=hold.at[ph, block, at, :], dst_ref=hold.at[ph, block, at, :],
            send_sem=ag_ssem.at[ph, (1 - sign) // 2, block, q], recv_sem=ag_rsem.at[ph, block, q],
            device_id=(z + sign, s), device_id_type=MESH)

    def pack_field(ph, source, fill=None, first=None):
        if fill is not None:
            fill(cells, edge, 0)
        hold[ph, z, 0:edge, :] = source[cells:cells + edge, :].astype(BF16)
        for q in range(HALVES):
            if first is not None:
                first(q)
            if fill is not None:
                chunked(fill, 0, q * band, band)
            hold[ph, z, edge + q * packed:edge + (q + 1) * packed, :] = dot(
                pack[q], source[q * band:(q + 1) * band, :].astype(BF16)).astype(BF16)
            for sign in (1, -1):
                @pl.when((z + sign >= 0) & (z + sign < n))
                def _():
                    ag_copy(ph, z, q, sign).start()

    def inside(slice_at):
        return (slice_at >= 0) & (slice_at < n)

    def take_and_pass(ph, k, q, sign, passes=True, takes=True):
        block = z - k * sign

        @pl.when((k > 0) & inside(block))
        def _():
            if passes and takes:
                ag_copy(ph, block, q, sign).wait_recv()

            @pl.when(inside(z + sign))
            def _():
                if passes:
                    if not takes:
                        ag_copy(ph, block, q, sign).wait_recv()
                    ag_copy(ph, block, q, sign).start()

            if not passes:
                @pl.when(jnp.logical_not(inside(z + sign)))
                def _():
                    ag_copy(ph, block, q, sign).wait_recv()

    near = jnp.where(z < n - n // 2, 1, 0)

    def consume_way(k, q, way, consume):
        block = z - k * (1 - 2 * way)

        @pl.when((k >= 0) & (k < n) & inside(block) & ((k > 0) | (way == near)))
        def _():
            consume(k, block, q)

    def take_both(ph, k, q, **how):
        @pl.loop(0, 2)
        def _(i):
            way = (near + i) % 2
            take_and_pass(ph, k, q, 1 - 2 * way, **how)

    def gather(ph, consume, each):
        @pl.loop(0, n)
        def _(k):
            for q in range(HALVES):
                take_both(ph, k, q)
                if q:
                    consume_way(k, q - 1, 1 - near, consume)
                else:
                    consume_way(k - 1, HALVES - 1, 1 - near, consume)
                consume_way(k, q, near, consume)
            each(k)

    def gather_passing_first(ph, consume, each):
        @pl.loop(0, n)
        def _(k):
            @pl.when(k == 1)
            def _():
                @pl.loop(1, n)
                def _(ahead):
                    for q in range(HALVES):
                        take_both(ph, ahead, q, takes=False)
            for q in range(HALVES):
                take_both(ph, k, q, passes=False)

                @pl.loop(0, 2)
                def _(i):
                    consume_way(k, q, (near + i) % 2, consume)
            each(k)

    last_pass = jnp.maximum(jnp.where(z < n - 1, z, 0), jnp.where(z > 0, n - 1 - z, 0))

    def forward(ph, field):
        def consume(k, block, q):
            into = taken.at[block]
            if q == 0:
                @pl.when(k > 0)
                def _():
                    weights_to_core(ph, slot_of(block))
            unpack_half(ph, block, q, into)

            @pl.when(k == 0)
            def _():
                add_conv(q, into, lambda a: wv[ph, z, 3 * a * ch:3 * (a + 1) * ch, :])

            @pl.when(k > 0)
            def _():
                slot = slot_of(block)
                if q == 0:
                    weights_arrived(ph, slot)
                add_conv(q, into, lambda a: wf[ph, slot, 3 * a * ch:3 * (a + 1) * ch, :])

        def each(k):
            if ph == 0:
                @pl.when(k == 0)
                def _():
                    weights_round(0)

                @pl.when(k == 1)
                def _():
                    weights_over_z(1)

            @pl.when(k == last_pass)
            def _():
                turn_field(ph, field)
                if ph == 0:
                    load_cotangent()
        (gather if ph else gather_passing_first)(ph, consume, each)

    def turn_field(ph, field):
        main = [field[start:start + ch, :].T for start in range(0, cells, ch)]
        ends = field[cells:cells + edge, :]
        if edge < ch:
            ends = jnp.concatenate([ends, jnp.zeros((ch - edge, ch), F32)], axis=0)
        ends = ends.T
        for i, here in enumerate(main):
            left = jnp.concatenate(
                [ends[:, 0:wide] if i == 0 else main[i - 1][:, ch - wide:], here[:, 0:ch - wide]], axis=1)
            right = jnp.concatenate(
                [here[:, wide:], main[i + 1][:, 0:wide] if i + 1 < len(main) else ends[:, wide:edge]], axis=1)
            for a, v in enumerate((left, here, right)):
                x_t[ph, a * ch:(a + 1) * ch, i * ch:(i + 1) * ch] = v.astype(BF16)

    def c_copy(ph, j):
        return pltpu.make_async_remote_copy(
            src_ref=psend.at[ph, j], dst_ref=crecv.at[ph, j],
            send_sem=c_ssem.at[ph, j], recv_sem=c_rsem.at[ph, j],
            device_id=(z, chip * 2 + 1 - core), device_id_type=MESH)

    def q_copy(ph, j, e, whose, owner):
        return pltpu.make_async_remote_copy(
            src_ref=hsend.at[ph, j, owner], dst_ref=qrecv.at[ph, j, whose],
            send_sem=q_ssem.at[ph, j, e], recv_sem=q_rsem.at[ph, j, whose],
            device_id=(z, ((chip + e) % chips) * 2 + core), device_id_type=MESH)

    def f_copy(ph, j, e, owner):
        return pltpu.make_async_remote_copy(
            src_ref=wout.at[ph, j, core, owner], dst_ref=wout.at[ph, j, core, owner],
            send_sem=f_ssem.at[ph, j, e], recv_sem=f_rsem.at[ph, j, owner],
            device_id=(z, ((chip + e) % chips) * 2 + core), device_id_type=MESH)

    def h_copy(ph, j, whose):
        return pltpu.make_async_remote_copy(
            src_ref=wout.at[ph, j, whose], dst_ref=wout.at[ph, j, whose],
            send_sem=h_ssem.at[ph, j], recv_sem=h_rsem.at[ph, j],
            device_id=(z, chip * 2 + 1 - core), device_id_type=MESH)

    def o_copy(ph, j):
        target = (out_wg1, out_wg2)[ph]
        if aligned:
            target = target.at[:, :, :, pl.ds(pl.multiple_of(j * ch, ch), ch)]
        else:
            target = target.at[j]
        return pltpu.make_async_copy(wout.at[ph, j], target, o_sem.at[ph, j])

    def sum_cores(ph, j):
        for o in range(owners):
            psend[ph, j, o] = part[ph, j, 1 - core, o].astype(BF16)
        c_copy(ph, j).start()

    def sum_chips(ph, j):
        c_copy(ph, j).wait_recv()
        for o in range(owners):
            v = part[ph, j, core, o] + crecv[ph, j, o].astype(F32)
            part[ph, j, core, o] = v
            hsend[ph, j, o] = v.astype(BF16)

        @pl.loop(1, chips)
        def _(e):
            peer = (chip + e) % chips

            @pl.when(peer < owners)
            def _():
                q_copy(ph, j, e, chip, peer).start()

    def spread_chips(ph, j):
        @pl.when(chip < owners)
        def _():
            @pl.loop(1, chips)
            def _(e):
                q_copy(ph, j, e, (chip + e) % chips, chip).wait_recv()
            v = part[ph, j, core, chip]
            for e in range(1, chips):
                v = v + qrecv[ph, j, (chip + e) % chips].astype(F32)
            wout[ph, j, core, chip] = v.astype(BF16)

            @pl.loop(1, chips)
            def _(e):
                f_copy(ph, j, e, chip).start()

    def spread_cores(ph, j):
        @pl.loop(1, chips)
        def _(e):
            peer = (chip + e) % chips

            @pl.when(peer < owners)
            def _():
                f_copy(ph, j, e, peer).wait_recv()
        h_copy(ph, j, core).start()

    def finish(ph, j):
        h_copy(ph, j, 1 - core).wait_recv()
        o_copy(ph, j).start()

    def put_part(ph, j, tap, value):
        start = tap * ch
        done = 0
        while done < ch:
            row = start + done
            side, o, at = row // half_rows, row % half_rows // piece, row % piece
            size = min(ch - done, piece - at)
            part[ph, j, side, o, at:at + size, :] = value[done:done + size, :]
            done += size

    stages = (sum_cores, sum_chips, spread_chips, spread_cores, finish)

    def of_step(k, fn):
        @pl.loop(0, 2)
        def _(way):
            block = z - k * (1 - 2 * way)

            @pl.when((k >= 0) & (k < n) & inside(block) & ((k > 0) | (way == 0)))
            def _():
                fn(block)

    passing = last_pass > 0

    def made_at(step):
        first = jnp.where(passing & (step > 0), jnp.where(step == last_pass, 1, step + 1), step)
        return first, step + 1

    def advance(ph, k):
        for age in range(1, len(stages)):
            step = k - age

            @pl.when((step >= 0) & (step < n))
            def _():
                @pl.loop(*made_at(step))
                def _(made):
                    of_step(made, functools.partial(stages[age], ph))

    def advance_all(ph, age):
        @pl.loop(0, n)
        def _(j):
            stages[age](ph, j)

    def field_grad(ph, block):
        grad = taken[block, 1:rows + 1, :, :].reshape(cells, 3 * ch)
        value = dot(x_t[ph], grad)
        for a in range(3):
            for b in range(3):
                put_part(ph, block, 3 * a + b, value[a * ch:(a + 1) * ch, (2 - b) * ch:(3 - b) * ch])

    def make_grad(ph, block):
        field_grad(ph, block)
        sum_cores(ph, block)

    results = [pltpu.make_async_copy(flat_block, out_block, r_sem.at[0])]

    def backward(ph):
        last = ph == 0

        def consume(k, block, q):
            into = taken.at[block]
            unpack_half(2 + ph, block, q, into)
            if last and q == HALVES - 1:
                @pl.when((k == 0) | (k >= last_pass))
                def _():
                    make_grad(ph, block)
            add_conv(q, into, None, lambda t: wv[ph, block, t * ch:(t + 1) * ch, :])

        def each(k):
            first, end = made_at(k)
            if last:
                @pl.loop(first, end - 1)
                def _(step):
                    of_step(step, functools.partial(make_grad, ph))
                advance(ph, k)
                for age in range(2, len(stages)):
                    @pl.when(k == age - 2)
                    def _():
                        advance_all(1, age)
            else:
                @pl.loop(first, jnp.where(passing | (k < n - 1), end, first))
                def _(step):
                    of_step(step, functools.partial(make_grad, ph))

                @pl.when(k == last_pass)
                def _():
                    to_flat(hid2, flat_block)
                    results[0].start()
        gather(2 + ph, consume, each)

    def fold(v):
        return jnp.sum(v.reshape(v.shape[0] // 8, 8, ch), axis=0)

    def flatten(v):
        return jnp.sum(v, axis=0, keepdims=True)

    zero = jnp.zeros((8, ch), F32)

    def local_moments(ref):
        def sums(start, size, carry):
            at = pl.ds(start, size)
            m = mask[at, :]
            return carry[0] + fold(ref[at, :] * m), carry[1] + fold(m)
        added, number = (flatten(v) for v in chunked(sums, (zero, zero)))
        middle = added / jnp.maximum(number, 1.0)

        def spread(start, size, carry):
            at = pl.ds(start, size)
            c = (ref[at, :] - middle) * mask[at, :]
            return carry + fold(c * c)
        return added, number, flatten(chunked(spread, zero))

    def moments(slot):
        take_stats(slot)
        got = [st_recv[slot, k] for k in range(s_count)]
        added = sum(g[0:1] for g in got)
        number = sum(g[1:2] for g in got)
        mean = added / number
        spread = 0.0
        for g in got:
            off = g[0:1] / jnp.maximum(g[1:2], 1.0) - mean
            spread = spread + (g[2:3] + g[1:2] * off * off)
        return mean, lax.rsqrt(spread / number + EPSILON), number

    def everywhere(fn):
        chunked(fn, 0)
        fn(cells, 2 * wide, 0)

    gain1, shift1, gain2, shift2 = (r[...] for r in (gain1_in, shift1_in, gain2_in, shift2_in))

    weights_over_z(0)

    below = lax.broadcasted_iota(jnp.int32, (band, band), 1) < lax.broadcasted_iota(jnp.int32, (band, band), 0)
    below = below.astype(F32).astype(BF16)

    def make_pack(h):
        lv = mask[h * band:(h + 1) * band, :]
        place = jnp.where(lv > 0.0, dot(below, lv.astype(BF16)), -1.0)
        places[h] = place
        across = place.T[0:1, :]
        spot = lax.broadcasted_iota(jnp.int32, (packed, band), 0).astype(F32)
        pack[h] = jnp.where(spot == across, 1.0, 0.0).astype(BF16)

    def make_unpack(h):
        for start in range(0, packed, ch):
            size = min(ch, packed - start)
            spot = start + lax.broadcasted_iota(jnp.int32, (band, size), 1)
            unpack[h, :, start:start + size] = jnp.where(
                places[h, :, :size] == spot.astype(F32), 1.0, 0.0).astype(BF16)

    for side in range(2):
        edge_copy(1 - side).wait_recv()
        there = jnp.where(s > 0, 1.0, 0.0) if side == 0 else jnp.where(s < s_count - 1, 1.0, 0.0)
        at = slice(cells + side * wide, cells + (side + 1) * wide)
        masked[at, :] = edge_recv[side, 0].astype(F32) * there
        mask[at, :] = edge_recv[side, 1].astype(F32) * there

    def stats_sent(slot):
        for k in range(1, s_count):
            st_copy(slot, k, s).wait_send()

    def row_sent(slot):
        for side in range(2):
            row_copy(slot, side).wait_send()

    def gathered_sent(ph):
        @pl.loop(0, n)
        def _(k):
            for sign in (1, -1):
                block = z - k * sign

                @pl.when(inside(block) & inside(z + sign))
                def _():
                    for q in range(HALVES):
                        ag_copy(ph, block, q, sign).wait_send()

    def grads_sent(ph):
        @pl.loop(0, n)
        def _(j):
            c_copy(ph, j).wait_send()
            h_copy(ph, j, core).wait_send()
            o_copy(ph, j).wait()
            for e in range(1, chips):
                peer = (chip + e) % chips

                @pl.when(peer < owners)
                def _():
                    q_copy(ph, j, e, chip, peer).wait_send()

                @pl.when(chip < owners)
                def _():
                    f_copy(ph, j, e, chip).wait_send()

    pack_field(0, masked, first=make_pack)
    for h in range(HALVES):
        make_unpack(h)
    forward(0, masked)
    send_stats(0, local_moments(acc))
    send_rows(0, acc)
    weights_round(1)
    weights_sent(0)
    for side in range(2):
        edge_copy(side).wait_send()
        cot_copy(side).wait_send()
    mean1, scale1, count = moments(0)

    def activate_one(start, size, carry):
        at = pl.ds(start, size)
        main = start is not cells
        nv = ((acc if main else normed1)[at, :] - mean1) * scale1
        normed1[at, :] = nv
        hid[at, :] = gelu_parts(nv * gain1 + shift1)[0] * mask[at, :]
        if main:
            acc[at, :] = jnp.zeros((size, ch), F32)
        return carry

    def slope_one(start, size, carry):
        at = pl.ds(start, size)
        slope1[at, :] = gelu_parts(normed1[at, :] * gain1 + shift1)[1] * mask[at, :]
        return carry

    take_rows(0, normed1)
    pack_field(1, hid, activate_one)
    everywhere(slope_one)
    forward(1, hid)
    send_stats(1, local_moments(acc))
    send_rows(1, acc)
    gathered_sent(0)
    stats_sent(0)
    row_sent(0)
    mean2, scale2, _ = moments(1)

    def activate_two(source, start, size):
        at = pl.ds(start, size)
        nv = (source[at, :] - mean2) * scale2
        normed2[at, :] = nv
        value, slope = gelu_parts(nv * gain2 + shift2 + masked[at, :])
        t = cotm[at, :] * slope
        through[at, :] = t
        return value, nv, t

    def activate_main(start, size, carry):
        value, nv, t = activate_two(acc, start, size)
        at = pl.ds(start, size)
        hid2[at, :] = value * mask[at, :]
        acc[at, :] = jnp.zeros((size, ch), F32)
        return carry[0] + fold(t * nv), carry[1] + fold(t)

    send_stats(2, [flatten(v) for v in chunked(activate_main, (zero, zero))])
    take_rows(1, normed2)
    take_cotangent()
    activate_two(normed2, cells, edge)
    weights_sent(1)
    gathered_sent(1)
    stats_sent(1)
    row_sent(1)

    def gradient_sums(slot):
        take_stats(slot)
        got = [st_recv[slot, k] for k in range(s_count)]
        return sum(g[0:1] for g in got), sum(g[1:2] for g in got)

    def norm_back(upstream, normed, gain, scale, sums):
        gain_grad, shift_grad = sums
        factor = gain * scale
        level, tilt = shift_grad / count, gain_grad / count

        def fill(start, size, carry):
            at = pl.ds(start, size)
            v = upstream[at, :] - mask[at, :] * (level + normed[at, :] * tilt)
            hid[at, :] = factor * v
            return carry
        return fill

    sums2 = gradient_sums(2)
    pack_field(3, hid, norm_back(through, normed2, gain2, scale2, sums2))
    backward(1)

    def inner_main(start, size, carry):
        at = pl.ds(start, size)
        v = acc[at, :] * slope1[at, :]
        slope1[at, :] = v
        acc[at, :] = jnp.zeros((size, ch), F32)
        return carry[0] + fold(v * normed1[at, :]), carry[1] + fold(v)

    for side, start in ((0, 0), (1, cells - wide)):
        row_send[2, side] = acc[start:start + wide, :]
    send_stats(3, [flatten(v) for v in chunked(inner_main, (zero, zero))])
    for side in range(2):
        row_copy(2, side).start()

    @pl.when(jnp.logical_not(passing))
    def _():
        of_step(n - 1, functools.partial(make_grad, 1))
    for side in range(2):
        row_copy(2, 1 - side).wait_recv()
        at = slice(cells + side * wide, cells + (side + 1) * wide)
        slope1[at, :] = row_recv[2, side] * slope1[at, :]
    stats_sent(2)
    gathered_sent(3)
    sums1 = gradient_sums(3)
    pack_field(2, hid, norm_back(slope1, normed1, gain1, scale1, sums1))
    advance_all(1, 1)
    backward(0)
    advance(0, n)

    def finish_input(start, size, carry):
        at = pl.ds(start, size)
        acc[at, :] = (acc[at, :] + through[at, :]) * mask[at, :]
        return carry

    chunked(finish_input, 0)
    to_flat(acc, flat_input)
    input_copy = pltpu.make_async_copy(flat_input, out_input, r_sem.at[1])
    input_copy.start()
    out_gain1[...], out_shift1[...] = sums1
    out_gain2[...], out_shift2[...] = sums2
    for extra in range(1, len(stages) - 1):
        advance(0, n + extra)

    stats_sent(3)
    row_sent(2)
    gathered_sent(2)
    grads_sent(1)
    grads_sent(0)
    results[0].wait()
    input_copy.wait()


def finish_kernel(count, *refs):
    ins, outs = refs[:count], refs[count:2 * count]
    narrow, wide, in_sem, out_sem, take_sem, give_sem = refs[2 * count:2 * count + 6]
    held = refs[2 * count + 6:]
    rows = narrow.shape[1] // FINISH_PARTS
    parts = [(w, i, pl.ds(i * rows, rows)) for i in range(FINISH_PARTS) for w in range(2)]
    loads = [pltpu.make_async_copy(ins[w].at[at, :], narrow.at[w, at, :], in_sem.at[w, i]) for w, i, at in parts]
    stores = [pltpu.make_async_copy(wide.at[w, at, :], outs[w].at[at, :], out_sem.at[w, i]) for w, i, at in parts]
    takes = [pltpu.make_async_copy(ins[2 + k], v, take_sem.at[k]) for k, v in enumerate(held)]
    gives = [pltpu.make_async_copy(v, outs[2 + k], give_sem.at[k]) for k, v in enumerate(held)]
    for copy in loads + takes:
        copy.start()
    for load, store, (w, i, at) in zip(loads, stores, parts):
        load.wait()
        wide[w, at, :] = narrow[w, at, :].astype(F32)
        store.start()
    for take, give in zip(takes, gives):
        take.wait()
        give.start()
    for copy in stores + gives:
        copy.wait()


def per_device(n, s_count, blocks, weight_one, weight_two, gain_one, shift_one, gain_two, shift_two, cell_live, cotangent):
    rows, wide = cell_live.shape
    ch = blocks.shape[1] // wide
    cells = rows * wide
    total = cells + 2 * wide
    packed = -(-most_live(rows // HALVES, wide) // 16) * 16
    aligned = ch % 128 == 0
    chips = s_count // 2
    tap_rows = 9 * ch
    half_rows = tap_rows // 2
    owners = math.gcd(half_rows // 16, chips)
    piece = half_rows // owners

    if aligned:
        weight_one, weight_two = (w.reshape(tap_rows, n * ch) for w in (weight_one, weight_two))
    else:
        weight_one, weight_two = (
            w.reshape(tap_rows, n, ch).transpose(1, 0, 2) for w in (weight_one, weight_two))
    grad_shape = (2, owners, piece, n * ch) if aligned else (n, 2, owners, piece, ch)
    vmem = pl.BlockSpec(memory_space=pltpu.VMEM)
    hbm = pl.BlockSpec(memory_space=pl.ANY)
    sem = pltpu.SemaphoreType.DMA
    field = pltpu.VMEM((total, ch), F32)
    scratch = [
        pltpu.VMEM((ch * wide, 128), F32),
        pltpu.VMEM((2, n, tap_rows, ch), BF16),
        pltpu.VMEM((2, n - 1, tap_rows, ch), BF16),
        pltpu.VMEM((2, 3 * ch, cells), BF16),
        pltpu.VMEM((HALVES, packed, cells // HALVES), BF16),
        pltpu.VMEM((HALVES, cells // HALVES, packed), BF16),
        pltpu.VMEM((HALVES, cells // HALVES, ch), F32),
        pltpu.VMEM((2, 2, wide, ch), BF16),
        pltpu.VMEM((2, 2, wide, ch), BF16),
        pltpu.VMEM((2, wide, ch), BF16),
        pltpu.VMEM((2, wide, ch), BF16),
        field, field, field, field, field, field, field, field, field,
        pltpu.VMEM((total + 16, ch), F32),
        pltpu.VMEM((cells, ch), F32),
        pltpu.VMEM((4, n, 2 * wide + HALVES * packed, ch), BF16),
        pltpu.VMEM((n, rows + 2, wide, 3 * ch), BF16),
        pltpu.VMEM((2, n, 2, owners, piece, ch), F32),
        pltpu.VMEM((2, n, owners, piece, ch), BF16),
        pltpu.VMEM((2, n, owners, piece, ch), BF16),
        pltpu.VMEM((2, n, owners, piece, ch), BF16),
        pltpu.VMEM((2, n, chips, piece, ch), BF16),
        pltpu.VMEM((2, n, 2, owners, piece, ch), BF16),
        pltpu.VMEM((4, 8, ch), F32),
        pltpu.VMEM((4, s_count, 8, ch), F32),
        pltpu.VMEM((3, 2, wide, ch), F32),
        pltpu.VMEM((3, 2, wide, ch), F32),
        pltpu.VMEM((rows, ch * wide), BF16),
        pltpu.VMEM((rows, ch * wide), F32),
        pltpu.VMEM((rows, ch * wide), BF16),
        sem((2, n)),
        sem((2, n)), sem((2, n)),
        sem((2, n - 1, owners)), sem((2, n - 1, owners)),
        sem((2, n - 1)), sem((2, n - 1)),
        sem((2,)), sem((2,)),
        sem((2,)), sem((2,)),
        sem((4, 2, n, HALVES)), sem((4, n, HALVES)),
        sem((4, s_count)), sem((4, s_count)),
        sem((3, 2)), sem((3, 2)),
        sem((2, n)), sem((2, n)),
        sem((2, n, chips)), sem((2, n, chips)),
        sem((2, n, chips)), sem((2, n, chips)),
        sem((2, n)), sem((2, n)),
        sem((2, n)),
        sem((3,)),
    ]
    block_out, input_grad, wg1, wg2, *sums = pl.pallas_call(
        functools.partial(block_kernel, n, s_count, rows, wide, ch, aligned, packed),
        out_shape=(
            jax.ShapeDtypeStruct((rows, ch * wide), BF16),
            jax.ShapeDtypeStruct((rows, ch * wide), F32),
            jax.ShapeDtypeStruct(grad_shape, BF16),
            jax.ShapeDtypeStruct(grad_shape, BF16),
            *[jax.ShapeDtypeStruct((1, ch), F32)] * 4,
        ),
        in_specs=[vmem, hbm] + [vmem] * 5 + [hbm] * 2,
        out_specs=(hbm, hbm, hbm, hbm, vmem, vmem, vmem, vmem),
        scratch_shapes=scratch,
        compiler_params=pltpu.CompilerParams(
            collective_id=0, has_side_effects=True, vmem_limit_bytes=60 * 1024 * 1024),
    )(blocks, cotangent, cell_live.T,
      *(v.reshape(1, ch) for v in (gain_one, shift_one, gain_two, shift_two)), weight_one, weight_two)

    if not aligned:
        def whole(grad):
            grad = grad.reshape(n, tap_rows, ch).transpose(1, 0, 2)
            return grad.astype(F32).reshape(9, ch, n * ch)
        return (block_out, input_grad, whole(wg1), whole(wg2), *(v.reshape(ch) for v in sums))

    wg1, wg2 = (w.reshape(tap_rows, n * ch) for w in (wg1, wg2))
    wide_grad = jax.ShapeDtypeStruct((tap_rows, n * ch), F32)
    moved = (block_out, input_grad, *sums)
    grad1, grad2, *moved = pl.pallas_call(
        functools.partial(finish_kernel, 2 + len(moved)),
        out_shape=(wide_grad, wide_grad, *(jax.ShapeDtypeStruct(v.shape, v.dtype) for v in moved)),
        in_specs=[pl.BlockSpec(memory_space=pl.ANY)] * (2 + len(moved)),
        out_specs=[pl.BlockSpec(memory_space=pl.ANY)] * (2 + len(moved)),
        scratch_shapes=[
            pltpu.VMEM((2, tap_rows, n * ch), BF16), pltpu.VMEM((2, tap_rows, n * ch), F32),
            sem((2, FINISH_PARTS)), sem((2, FINISH_PARTS)), sem((len(moved),)), sem((len(moved),)),
            *(pltpu.VMEM(v.shape, v.dtype) for v in moved),
        ],
        compiler_params=pltpu.CompilerParams(vmem_limit_bytes=64 * 1024 * 1024),
    )(wg1, wg2, *moved)
    block_out, input_grad, *sums = moved
    grads = (g.reshape(9, ch, n * ch) for g in (grad1, grad2))
    return (block_out, input_grad, *grads, *(v.reshape(ch) for v in sums))


def solution(mesh):
    return jax.shard_map(
        functools.partial(per_device, mesh.shape["chan"], mesh.shape["space"]),
        mesh=mesh,
        in_specs=(
            P("space", "chan"),
            P(None, "chan", None),
            P(None, "chan", None),
            P("chan"),
            P("chan"),
            P("chan"),
            P("chan"),
            P("space", None),
            P("space", "chan"),
        ),
        out_specs=(
            P("space", "chan"),
            P("space", "chan"),
            P(None, "chan", None),
            P(None, "chan", None),
            P("chan"),
            P("chan"),
            P("chan"),
            P("chan"),
        ),
        check_vma=False,
    )
```

```python
import functools
import math

import jax
import jax.numpy as jnp
from jax import lax
from jax.experimental import pallas as pl
from jax.experimental.pallas import tpu as pltpu
from jax.sharding import PartitionSpec as P

EPSILON = 1e-05
MESH = pl.DeviceIdType.MESH
F32 = jnp.float32
BF16 = jnp.bfloat16
ROOT_HALF = 0.7071067811865476
ROOT_TWO_PI = 0.3989422804014327
CHUNK = 64
FINISH_PARTS = 4
UNROLL = 2
HALVES = 2
LARGE, SMALL = 7, 3


def dot(a, b):
    return jnp.dot(a, b, preferred_element_type=F32)


def gelu_parts(v):
    upper = 0.5 * (1.0 + lax.erf(v * ROOT_HALF))
    slope = upper + v * (ROOT_TWO_PI * jnp.exp(-0.5 * v * v))
    return v * upper, slope


def most_live(rows, wide):
    units = (wide + 1) // (SMALL + 1)
    live_rows = rows - rows // (LARGE + 1)
    return min(rows * wide, math.ceil(units * live_rows * LARGE / 2))


def block_kernel(n, s_count, rows, wide, ch, aligned, packed, *refs):
    (x_in, cot_in, live_in, gain1_in, shift1_in, gain2_in, shift2_in, w1_hbm, w2_hbm) = refs[:9]
    (out_block, out_input, out_wg1, out_wg2, out_gain1, out_shift1, out_gain2, out_shift2) = refs[9:17]
    (turned, wv, wf, x_t, pack, unpack, places, edge_send, edge_recv, cot_send, cot_recv, cotm, mask, masked,
     normed1, normed2, through, slope1, hid, hid2, pad, acc, hold, taken,
     part, psend, crecv, hsend, qrecv, dsend, drecv, wout, st_send, st_recv, row_send, row_recv, flat_block, flat_input, cot_flat,
     w_sem, wz_ssem, wz_rsem, wp_ssem, wp_rsem, e_ssem, e_rsem, ce_ssem, ce_rsem, ag_ssem, ag_rsem,
     st_ssem, st_rsem, row_ssem, row_rsem, c_ssem, c_rsem, q_ssem, q_rsem, d_ssem, d_rsem, g_ssem, g_rsem,
     f_ssem, f_rsem, h_ssem, h_rsem, o_sem, r_sem) = refs[17:]

    z = lax.axis_index("chan")
    s = lax.axis_index("space")
    cells = rows * wide
    total = cells + 2 * wide
    band = cells // HALVES
    core, chip, chips = s % 2, s // 2, s_count // 2
    before, after = (s + s_count - 1) % s_count, (s + 1) % s_count
    tap_rows = 9 * ch
    half_rows = tap_rows // 2
    owners = math.gcd(half_rows // 16, chips)
    piece = half_rows // owners

    barrier = pltpu.get_barrier_semaphore()

    @pl.loop(1, s_count)
    def _(k):
        pl.semaphore_signal(barrier, inc=1, device_id=(z, (s + k) % s_count), device_id_type=MESH)

    @pl.loop(1, n)
    def _(k):
        pl.semaphore_signal(barrier, inc=1, device_id=((z + k) % n, s), device_id_type=MESH)

    w_copies = []
    for which, source in enumerate((w1_hbm, w2_hbm)):
        for d in range(n):
            block = source.at[:, d * ch:(d + 1) * ch] if aligned else source.at[d]
            w_copies.append(pltpu.make_async_copy(block, wv.at[which, d], w_sem.at[which, d]))
    for copy in w_copies:
        copy.start()

    cot_load = pltpu.make_async_copy(cot_in, cot_flat, r_sem.at[2])
    cot_load.start()

    def chunked(fn, init, first=0, count=cells):
        def step(i, carry):
            return fn(pl.multiple_of(first + i * CHUNK, CHUNK), CHUNK, carry)
        return lax.fori_loop(0, count // CHUNK, step, init, unroll=UNROLL)

    lanes = 128
    tiles = ch * wide // lanes

    def from_flat(flat, put):
        for i in range(tiles):
            turned[i * lanes:(i + 1) * lanes, 0:rows] = flat[:, i * lanes:(i + 1) * lanes].astype(F32).T
        for w in range(wide):
            put(pl.ds(w, rows, stride=wide), turned[pl.ds(w, ch, stride=wide), 0:rows].T)

    def to_flat(source, flat):
        for w in range(wide):
            turned[pl.ds(w, ch, stride=wide), 0:rows] = source[pl.ds(w, rows, stride=wide), :].T
        for i in range(tiles):
            flat[:, i * lanes:(i + 1) * lanes] = turned[i * lanes:(i + 1) * lanes, 0:rows].T.astype(flat.dtype)

    def edge_copy(side):
        return pltpu.make_async_remote_copy(
            src_ref=edge_send.at[side], dst_ref=edge_recv.at[1 - side],
            send_sem=e_ssem.at[side], recv_sem=e_rsem.at[1 - side],
            device_id=(z, before if side == 0 else after), device_id_type=MESH)


    def cot_copy(side):
        return pltpu.make_async_remote_copy(
            src_ref=cot_send.at[side], dst_ref=cot_recv.at[1 - side],
            send_sem=ce_ssem.at[side], recv_sem=ce_rsem.at[1 - side],
            device_id=(z, before if side == 0 else after), device_id_type=MESH)

    def load_cotangent():
        def put(at, value):
            cotm[at, :] = value
        cot_load.wait()
        from_flat(cot_flat, put)

        def live_only(start, size, carry):
            at = pl.ds(start, size)
            cotm[at, :] = cotm[at, :] * mask[at, :]
            return carry
        chunked(live_only, 0)
        for side, start in ((0, 0), (1, cells - wide)):
            cot_send[side] = cotm[start:start + wide, :].astype(BF16)
            cot_copy(side).start()

    def take_cotangent():
        for side in range(2):
            cot_copy(1 - side).wait_recv()
            at = slice(cells + side * wide, cells + (side + 1) * wide)
            cotm[at, :] = cot_recv[side].astype(F32) * mask[at, :]

    w_parts = math.gcd(tap_rows // 16, s_count)
    w_rows = tap_rows // w_parts
    w_mine = s % w_parts
    w_group = s - w_mine

    def wz_copy(which, k):
        at = pl.ds(w_mine * w_rows, w_rows)
        slot = n - k - 1
        return pltpu.make_async_remote_copy(
            src_ref=wv.at[which, (z + k) % n, at, :], dst_ref=wf.at[which, slot, at, :],
            send_sem=wz_ssem.at[which, slot], recv_sem=wz_rsem.at[which, slot],
            device_id=((z + k) % n, s), device_id_type=MESH)

    def wp_copy(which, slot, k, whose):
        at = pl.ds(whose * w_rows, w_rows)
        return pltpu.make_async_remote_copy(
            src_ref=wf.at[which, slot, at, :], dst_ref=wf.at[which, slot, at, :],
            send_sem=wp_ssem.at[which, slot, k], recv_sem=wp_rsem.at[which, slot, whose],
            device_id=(z, w_group + (w_mine + k) % w_parts), device_id_type=MESH)

    def weights_over_z(which):
        for copy in w_copies[which * n:(which + 1) * n]:
            copy.wait()
        for k in range(1, n):
            wz_copy(which, k).start()

    def slot_of(block):
        return (block - z + n - 1) % n

    def weights_round(which):
        @pl.loop(1, n)
        def _(distance):
            for sign in (1, -1):
                block = z - distance * sign

                @pl.when((block >= 0) & (block < n))
                def _():
                    slot = slot_of(block)
                    wz_copy(which, n - 1 - slot).wait_recv()
                    for k in range(1, w_parts):
                        wp_copy(which, slot, k, w_mine).start()

    def weights_arrived(which, slot):
        @pl.loop(1, w_parts)
        def _(k):
            wp_copy(which, slot, k, (w_mine + k) % w_parts).wait_recv()

    def weights_sent(which):
        for k in range(1, n):
            wz_copy(which, k).wait_send()

        @pl.loop(1, w_parts)
        def _(k):
            for slot in range(n - 1):
                wp_copy(which, slot, k, w_mine).wait_send()

    def row_copy(slot, side):
        return pltpu.make_async_remote_copy(
            src_ref=row_send.at[slot, side], dst_ref=row_recv.at[slot, 1 - side],
            send_sem=row_ssem.at[slot, side], recv_sem=row_rsem.at[slot, 1 - side],
            device_id=(z, before if side == 0 else after), device_id_type=MESH)

    def send_rows(slot, ref):
        for side, start in ((0, 0), (1, cells - wide)):
            row_send[slot, side] = ref[start:start + wide, :]
            row_copy(slot, side).start()

    def take_rows(slot, ref):
        for side in range(2):
            row_copy(slot, 1 - side).wait_recv()
            ref[cells + side * wide:cells + (side + 1) * wide, :] = row_recv[slot, side]

    def st_copy(slot, k, whose):
        return pltpu.make_async_remote_copy(
            src_ref=st_send.at[slot], dst_ref=st_recv.at[slot, whose],
            send_sem=st_ssem.at[slot, k], recv_sem=st_rsem.at[slot, whose],
            device_id=(z, (s + k) % s_count), device_id_type=MESH)

    def send_stats(slot, values):
        for i, v in enumerate(values):
            st_send[slot, i:i + 1, :] = v
        for k in sorted(range(1, s_count), key=lambda k: abs(k - s_count // 2)):
            st_copy(slot, k, s).start()
        st_recv[slot, s] = st_send[slot]

    def take_stats(slot):
        for k in range(1, s_count):
            st_copy(slot, k, (s + k) % s_count).wait_recv()

    strip = 8
    column = lax.broadcasted_iota(jnp.int32, (strip * wide, ch), 0) % wide

    def shift(target, first, count):
        size = count * wide
        where = column[:size]
        here = pad[pl.ds(8 + first * wide, size), :]
        left = jnp.where(where == 0, 0.0, pad[pl.ds(7 + first * wide, size), :])
        right = jnp.where(where == wide - 1, 0.0, pad[pl.ds(9 + first * wide, size), :])
        for b, v in enumerate((left, here, right)):
            target[pl.ds(first, count), :, b * ch:(b + 1) * ch] = v.astype(BF16).reshape(count, wide, ch)

    edge = 2 * wide
    ag_rows = ((0, packed), (packed, edge + packed))
    held_rows = (slice(0, packed), slice(packed + edge, edge + 2 * packed))
    held_edge = (slice(packed, packed + wide), slice(packed + wide, packed + edge))
    band_rows = rows // HALVES

    def unpack_half(ph, block, q, target):
        if q == HALVES - 1:
            pad[8:8 + wide, :] = hold[ph, block, held_edge[0], :].astype(F32)
            pad[8 + wide + cells:8 + 2 * wide + cells, :] = hold[ph, block, held_edge[1], :].astype(F32)
            shift(target, 0, 1)
            shift(target, rows + 1, 1)
        pad[8 + wide + q * band:8 + wide + (q + 1) * band, :] = dot(unpack[q], hold[ph, block, held_rows[q], :])

        for i in range(band_rows // strip):
            shift(target, 1 + q * band_rows + i * strip, strip)

    def add_conv(q, field, taps, turned_taps=None):
        if turned_taps is None:
            rhs = jnp.concatenate([taps(a) for a in range(3)], axis=1)
        else:
            rhs = jnp.concatenate([
                jnp.concatenate([turned_taps(3 * (2 - a) + 2 - b) for b in range(3)], axis=1) for a in range(3)], axis=0)
        contract = (((1,), (0 if turned_taps is None else 1,)), ((), ()))

        def add(first, last):
            count = last - first
            lhs = field[first:last + 2, :, :].reshape((count + 2) * wide, 3 * ch)
            value = lax.dot_general(lhs, rhs, contract, preferred_element_type=F32)
            at = pl.ds(first * wide, count * wide)
            acc[at, :] = acc[at, :] + sum(
                value[a * wide:(a + count) * wide, a * ch:(a + 1) * ch] for a in range(3))

        if q == 0:
            add(1, band_rows - 1)
        else:
            add(band_rows - 1, rows)
            add(0, 1)

    def ag_copy(ph, block, q, sign):
        at = pl.ds(*ag_rows[q])
        return pltpu.make_async_remote_copy(
            src_ref=hold.at[ph, block, at, :], dst_ref=hold.at[ph, block, at, :],
            send_sem=ag_ssem.at[ph, (1 - sign) // 2, block, q], recv_sem=ag_rsem.at[ph, block, q],
            device_id=(z + sign, s), device_id_type=MESH)

    def pack_field(ph, source, fill=None, first=None, edges=None):
        for q in range(HALVES):
            if first is not None:
                first(q)
            if fill is not None:
                chunked(fill, 0, q * band, band)
            hold[ph, z, held_rows[q], :] = dot(pack[q], source[q * band:(q + 1) * band, :].astype(BF16)).astype(BF16)
            if q == HALVES - 1:
                if edges is not None:
                    edges()
                if fill is not None:
                    fill(cells, edge, 0)
                for side in range(2):
                    hold[ph, z, held_edge[side], :] = source[cells + side * wide:cells + (side + 1) * wide, :].astype(BF16)
            for sign in (1, -1):
                @pl.when((z + sign >= 0) & (z + sign < n))
                def _():
                    ag_copy(ph, z, q, sign).start()

    def inside(slice_at):
        return (slice_at >= 0) & (slice_at < n)

    def take_and_pass(ph, k, q, sign, passes=True, takes=True):
        block = z - k * sign

        @pl.when((k > 0) & inside(block))
        def _():
            if passes and takes:
                ag_copy(ph, block, q, sign).wait_recv()

            @pl.when(inside(z + sign))
            def _():
                if passes:
                    if not takes:
                        ag_copy(ph, block, q, sign).wait_recv()
                    ag_copy(ph, block, q, sign).start()

            if not passes:
                @pl.when(jnp.logical_not(inside(z + sign)))
                def _():
                    ag_copy(ph, block, q, sign).wait_recv()

    near = jnp.where(z < n - n // 2, 1, 0)

    def consume_way(k, q, way, consume):
        block = z - k * (1 - 2 * way)

        @pl.when((k >= 0) & (k < n) & inside(block) & ((k > 0) | (way == near)))
        def _():
            consume(k, block, q)

    def take_both(ph, k, q, **how):
        @pl.loop(0, 2)
        def _(i):
            way = (near + i) % 2
            take_and_pass(ph, k, q, 1 - 2 * way, **how)

    def gather(ph, consume, each):
        @pl.loop(0, n)
        def _(k):
            for q in range(HALVES):
                take_both(ph, k, q)
                if q:
                    consume_way(k, q - 1, 1 - near, consume)
                else:
                    consume_way(k - 1, HALVES - 1, 1 - near, consume)
                consume_way(k, q, near, consume)
            each(k)

    def gather_passing_first(ph, consume, each):
        @pl.loop(0, n)
        def _(k):
            @pl.when(k == 1)
            def _():
                @pl.loop(1, n)
                def _(ahead):
                    for q in range(HALVES):
                        take_both(ph, ahead, q, takes=False)
            for q in range(HALVES):
                take_both(ph, k, q, passes=False)

                @pl.loop(0, 2)
                def _(i):
                    consume_way(k, q, (near + i) % 2, consume)
            each(k)

    last_pass = jnp.maximum(jnp.where(z < n - 1, z, 0), jnp.where(z > 0, n - 1 - z, 0))

    def forward(ph, field):
        def consume(k, block, q):
            into = taken.at[block]
            unpack_half(ph, block, q, into)

            @pl.when(k == 0)
            def _():
                add_conv(q, into, lambda a: wv[ph, z, 3 * a * ch:3 * (a + 1) * ch, :])

            @pl.when(k > 0)
            def _():
                slot = slot_of(block)
                if q == 0:
                    weights_arrived(ph, slot)
                add_conv(q, into, lambda a: wf[ph, slot, 3 * a * ch:3 * (a + 1) * ch, :])

        def each(k):
            if ph == 0:
                @pl.when(k == 1)
                def _():
                    weights_over_z(1)

            @pl.when(k == last_pass)
            def _():
                turn_field(ph, field)
                if ph == 0:
                    load_cotangent()
        (gather if ph else gather_passing_first)(ph, consume, each)

    def turn_field(ph, field):
        main = [field[start:start + ch, :].T for start in range(0, cells, ch)]
        ends = field[cells:cells + edge, :]
        if edge < ch:
            ends = jnp.concatenate([ends, jnp.zeros((ch - edge, ch), F32)], axis=0)
        ends = ends.T
        for i, here in enumerate(main):
            left = jnp.concatenate(
                [ends[:, 0:wide] if i == 0 else main[i - 1][:, ch - wide:], here[:, 0:ch - wide]], axis=1)
            right = jnp.concatenate(
                [here[:, wide:], main[i + 1][:, 0:wide] if i + 1 < len(main) else ends[:, wide:edge]], axis=1)
            for a, v in enumerate((left, here, right)):
                x_t[ph, a * ch:(a + 1) * ch, i * ch:(i + 1) * ch] = v.astype(BF16)

    def c_copy(ph, j):
        return pltpu.make_async_remote_copy(
            src_ref=psend.at[ph, j], dst_ref=crecv.at[ph, j],
            send_sem=c_ssem.at[ph, j], recv_sem=c_rsem.at[ph, j],
            device_id=(z, chip * 2 + 1 - core), device_id_type=MESH)

    def q_copy(ph, j, e, whose, owner):
        return pltpu.make_async_remote_copy(
            src_ref=hsend.at[ph, j, owner], dst_ref=qrecv.at[ph, j, whose],
            send_sem=q_ssem.at[ph, j, e], recv_sem=q_rsem.at[ph, j, whose],
            device_id=(z, ((chip + e) % chips) * 2 + core), device_id_type=MESH)

    def f_copy(ph, j, e, owner):
        return pltpu.make_async_remote_copy(
            src_ref=wout.at[ph, j, core, owner], dst_ref=wout.at[ph, j, core, owner],
            send_sem=f_ssem.at[ph, j, e], recv_sem=f_rsem.at[ph, j, owner],
            device_id=(z, ((chip + e) % chips) * 2 + core), device_id_type=MESH)

    def h_copy(ph, j, whose):
        return pltpu.make_async_remote_copy(
            src_ref=wout.at[ph, j, whose], dst_ref=wout.at[ph, j, whose],
            send_sem=h_ssem.at[ph, j], recv_sem=h_rsem.at[ph, j],
            device_id=(z, chip * 2 + 1 - core), device_id_type=MESH)

    def o_copy(ph, j):
        target = (out_wg1, out_wg2)[ph]
        if aligned:
            target = target.at[:, :, :, pl.ds(pl.multiple_of(j * ch, ch), ch)]
        else:
            target = target.at[j]
        return pltpu.make_async_copy(wout.at[ph, j], target, o_sem.at[ph, j])

    def sum_cores(ph, j):
        for o in range(owners):
            psend[ph, j, o] = part[ph, j, 1 - core, o].astype(BF16)
        c_copy(ph, j).start()

    def sum_chips(ph, j):
        c_copy(ph, j).wait_recv()
        for o in range(owners):
            v = part[ph, j, core, o] + crecv[ph, j, o].astype(F32)
            part[ph, j, core, o] = v
            hsend[ph, j, o] = v.astype(BF16)

        @pl.loop(1, chips)
        def _(e):
            peer = (chip + e) % chips

            @pl.when(peer < owners)
            def _():
                q_copy(ph, j, e, chip, peer).start()

    def spread_chips(ph, j):
        @pl.when(chip < owners)
        def _():
            @pl.loop(1, chips)
            def _(e):
                q_copy(ph, j, e, (chip + e) % chips, chip).wait_recv()
            v = part[ph, j, core, chip]
            for e in range(1, chips):
                v = v + qrecv[ph, j, (chip + e) % chips].astype(F32)
            wout[ph, j, core, chip] = v.astype(BF16)

            @pl.loop(1, chips)
            def _(e):
                f_copy(ph, j, e, chip).start()

    def spread_cores(ph, j):
        @pl.loop(1, chips)
        def _(e):
            peer = (chip + e) % chips

            @pl.when(peer < owners)
            def _():
                f_copy(ph, j, e, peer).wait_recv()
        h_copy(ph, j, core).start()

    def finish(ph, j):
        h_copy(ph, j, 1 - core).wait_recv()
        o_copy(ph, j).start()

    def put_part(ph, j, tap, value):
        start = tap * ch
        done = 0
        while done < ch:
            row = start + done
            side, o, at = row // half_rows, row % half_rows // piece, row % piece
            size = min(ch - done, piece - at)
            part[ph, j, side, o, at:at + size, :] = value[done:done + size, :]
            done += size

    stages = (sum_cores, sum_chips, spread_chips, spread_cores, finish)

    straight = owners == chips

    def d_copy(e, whose):
        to = (s + e) % s_count
        return pltpu.make_async_remote_copy(
            src_ref=dsend.at[to % 2, to // 2], dst_ref=drecv.at[whose], send_sem=d_ssem.at[e], recv_sem=d_rsem.at[whose],
            device_id=(z, to), device_id_type=MESH)

    def g_copy(j, e, whose):
        at = wout.at[0, j, whose % 2, whose // 2]
        return pltpu.make_async_remote_copy(
            src_ref=at, dst_ref=at, send_sem=g_ssem.at[e], recv_sem=g_rsem.at[whose],
            device_id=(z, (s + e) % s_count), device_id_type=MESH)

    def straight_out(j):
        for side in range(2):
            for o in range(owners):
                dsend[side, o] = part[0, j, side, o].astype(BF16)
        for e in range(1, s_count):
            d_copy(e, s).start()

    def straight_sum(j):
        for e in range(1, s_count):
            d_copy(e, (s + e) % s_count).wait_recv()
        v = part[0, j, core, chip]
        for e in range(1, s_count):
            v = v + drecv[(s + e) % s_count].astype(F32)
        wout[0, j, core, chip] = v.astype(BF16)
        for e in range(1, s_count):
            g_copy(j, e, s).start()

    def straight_finish(j):
        for e in range(1, s_count):
            g_copy(j, e, (s + e) % s_count).wait_recv()
        o_copy(0, j).start()

    def straight_sent(j):
        for e in range(1, s_count):
            d_copy(e, s).wait_send()
            g_copy(j, e, s).wait_send()
        o_copy(0, j).wait()

    def at_the_end(fn):
        if straight:
            @pl.when(jnp.logical_not(passing))
            def _():
                fn(n - 1 - z)

    def of_step(k, fn):
        @pl.loop(0, 2)
        def _(way):
            block = z - k * (1 - 2 * way)

            @pl.when((k >= 0) & (k < n) & inside(block) & ((k > 0) | (way == 0)))
            def _():
                fn(block)

    passing = last_pass > 0

    def made_at(step):
        first = jnp.where(passing & (step > 0), jnp.where(step == last_pass, 1, step + 1), step)
        return first, step + 1

    def staged(step):
        first, end = made_at(step)
        return first, jnp.where(straight & jnp.logical_not(passing) & (step == n - 1), first, end)

    def advance(ph, k):
        for age in range(1, len(stages)):
            step = k - age

            @pl.when((step >= 0) & (step < n))
            def _():
                @pl.loop(*staged(step))
                def _(made):
                    of_step(made, functools.partial(stages[age], ph))

    def advance_all(ph, age):
        @pl.loop(0, n)
        def _(j):
            stages[age](ph, j)

    def field_grad(ph, block):
        grad = taken[block, 1:rows + 1, :, :].reshape(cells, 3 * ch)
        value = dot(x_t[ph], grad)
        for a in range(3):
            for b in range(3):
                put_part(ph, block, 3 * a + b, value[a * ch:(a + 1) * ch, (2 - b) * ch:(3 - b) * ch])

    def make_grad(ph, block):
        field_grad(ph, block)
        sum_cores(ph, block)

    results = [pltpu.make_async_copy(flat_block, out_block, r_sem.at[0])]

    def backward(ph):
        last = ph == 0

        def consume(k, block, q):
            into = taken.at[block]
            unpack_half(2 + ph, block, q, into)
            if last and q == HALVES - 1:
                @pl.when((k == 0) | (k >= last_pass))
                def _():
                    field_grad(ph, block)
                    if straight:
                        pl.when(passing | (k < n - 1))(lambda: sum_cores(ph, block))
                        pl.when(jnp.logical_not(passing) & (k == n - 1))(lambda: straight_out(block))
                    else:
                        sum_cores(ph, block)
            add_conv(q, into, None, lambda t: wv[ph, block, t * ch:(t + 1) * ch, :])

        def each(k):
            first, end = made_at(k)
            if last:
                @pl.loop(first, end - 1)
                def _(step):
                    of_step(step, functools.partial(make_grad, ph))
                advance(ph, k)
                for age in range(2, len(stages)):
                    @pl.when(k == age - 2)
                    def _():
                        advance_all(1, age)
            else:
                @pl.loop(first, jnp.where(passing | (k < n - 1), end, first))
                def _(step):
                    of_step(step, functools.partial(make_grad, ph))

                @pl.when(k == last_pass)
                def _():
                    to_flat(hid2, flat_block)
                    results[0].start()
        gather(2 + ph, consume, each)

    def fold(v):
        return jnp.sum(v.reshape(v.shape[0] // 8, 8, ch), axis=0)

    def flatten(v):
        return jnp.sum(v, axis=0, keepdims=True)

    zero = jnp.zeros((8, ch), F32)

    def local_moments(ref):
        def sums(start, size, carry):
            at = pl.ds(start, size)
            m = mask[at, :]
            return carry[0] + fold(ref[at, :] * m), carry[1] + fold(m)
        added, number = (flatten(v) for v in chunked(sums, (zero, zero)))
        middle = added / jnp.maximum(number, 1.0)

        def spread(start, size, carry):
            at = pl.ds(start, size)
            c = (ref[at, :] - middle) * mask[at, :]
            return carry + fold(c * c)
        return added, number, flatten(chunked(spread, zero))

    def moments(slot):
        take_stats(slot)
        got = [st_recv[slot, k] for k in range(s_count)]
        added = sum(g[0:1] for g in got)
        number = sum(g[1:2] for g in got)
        mean = added / number
        spread = 0.0
        for g in got:
            off = g[0:1] / jnp.maximum(g[1:2], 1.0) - mean
            spread = spread + (g[2:3] + g[1:2] * off * off)
        return mean, lax.rsqrt(spread / number + EPSILON), number

    def everywhere(fn):
        chunked(fn, 0)
        fn(cells, 2 * wide, 0)

    gain1, shift1, gain2, shift2 = (r[...] for r in (gain1_in, shift1_in, gain2_in, shift2_in))

    pl.semaphore_wait(barrier, s_count - 1 + n - 1)
    weights_over_z(0)

    def put_masked(at, value):
        masked[at, :] = value

    from_flat(x_in, put_masked)

    cell = lax.broadcasted_iota(jnp.int32, (cells, rows), 0)
    pick = (cell // wide == lax.broadcasted_iota(jnp.int32, (cells, rows), 1)).astype(F32).astype(BF16)
    column_of = lax.broadcasted_iota(jnp.int32, (cells, wide), 0) % wide
    picked = lax.dot_general(pick, live_in[...].astype(BF16), (((1,), (1,)), ((), ())), preferred_element_type=F32)
    picked = jnp.where(column_of == lax.broadcasted_iota(jnp.int32, (cells, wide), 1), picked, 0.0)
    mask[0:cells, :] = dot(picked.astype(BF16), jnp.ones((wide, ch), BF16))

    def load_main(start, size, carry):
        at = pl.ds(start, size)
        lv = mask[at, :]
        masked[at, :] = masked[at, :] * lv
        return carry

    chunked(load_main, 0)
    for side, start in ((0, 0), (1, cells - wide)):
        edge_send[side, 0] = masked[start:start + wide, :].astype(BF16)
        edge_send[side, 1] = mask[start:start + wide, :].astype(BF16)

    acc[...] = jnp.zeros_like(acc)
    st_send[...] = jnp.zeros_like(st_send)

    for side in range(2):
        edge_copy(side).start()

    below = lax.broadcasted_iota(jnp.int32, (band, band), 1) < lax.broadcasted_iota(jnp.int32, (band, band), 0)
    below = below.astype(F32).astype(BF16)

    def make_pack(h):
        lv = mask[h * band:(h + 1) * band, :]
        place = jnp.where(lv > 0.0, dot(below, lv.astype(BF16)), -1.0)
        places[h] = place
        across = place.T[0:1, :]
        spot = lax.broadcasted_iota(jnp.int32, (packed, band), 0).astype(F32)
        pack[h] = jnp.where(spot == across, 1.0, 0.0).astype(BF16)

    def make_unpack(h):
        for start in range(0, packed, ch):
            size = min(ch, packed - start)
            spot = start + lax.broadcasted_iota(jnp.int32, (band, size), 1)
            unpack[h, :, start:start + size] = jnp.where(
                places[h, :, :size] == spot.astype(F32), 1.0, 0.0).astype(BF16)

    def take_edges():
        for side in range(2):
            edge_copy(1 - side).wait_recv()
            there = jnp.where(s > 0, 1.0, 0.0) if side == 0 else jnp.where(s < s_count - 1, 1.0, 0.0)
            at = slice(cells + side * wide, cells + (side + 1) * wide)
            masked[at, :] = edge_recv[side, 0].astype(F32) * there
            mask[at, :] = edge_recv[side, 1].astype(F32) * there

    def stats_sent(slot):
        for k in range(1, s_count):
            st_copy(slot, k, s).wait_send()

    def row_sent(slot):
        for side in range(2):
            row_copy(slot, side).wait_send()

    def gathered_sent(ph):
        @pl.loop(0, n)
        def _(k):
            for sign in (1, -1):
                block = z - k * sign

                @pl.when(inside(block) & inside(z + sign))
                def _():
                    for q in range(HALVES):
                        ag_copy(ph, block, q, sign).wait_send()

    def grads_sent(ph):
        if ph == 0:
            at_the_end(straight_sent)
            skipped = jnp.where(passing | (not straight), n, n - 1 - z)
        else:
            skipped = n

        @pl.loop(0, n)
        def _(j):
            pl.when(j != skipped)(lambda: grad_sent(ph, j))

    def grad_sent(ph, j):
        c_copy(ph, j).wait_send()
        h_copy(ph, j, core).wait_send()
        o_copy(ph, j).wait()
        for e in range(1, chips):
            peer = (chip + e) % chips

            @pl.when(peer < owners)
            def _():
                q_copy(ph, j, e, chip, peer).wait_send()

            @pl.when(chip < owners)
            def _():
                f_copy(ph, j, e, chip).wait_send()

    pack_field(0, masked, first=make_pack, edges=take_edges)
    weights_round(0)
    for h in range(HALVES):
        make_unpack(h)
    forward(0, masked)
    send_stats(0, local_moments(acc))
    send_rows(0, acc)
    weights_round(1)
    weights_sent(0)
    for side in range(2):
        edge_copy(side).wait_send()
        cot_copy(side).wait_send()
    mean1, scale1, count = moments(0)

    def activate_one(start, size, carry):
        at = pl.ds(start, size)
        main = start is not cells
        nv = ((acc if main else normed1)[at, :] - mean1) * scale1
        normed1[at, :] = nv
        hid[at, :] = gelu_parts(nv * gain1 + shift1)[0] * mask[at, :]
        if main:
            acc[at, :] = jnp.zeros((size, ch), F32)
        return carry

    def slope_one(start, size, carry):
        at = pl.ds(start, size)
        slope1[at, :] = gelu_parts(normed1[at, :] * gain1 + shift1)[1] * mask[at, :]
        return carry

    pack_field(1, hid, activate_one, edges=lambda: take_rows(0, normed1))
    everywhere(slope_one)
    forward(1, hid)
    send_stats(1, local_moments(acc))
    send_rows(1, acc)
    gathered_sent(0)
    stats_sent(0)
    row_sent(0)
    mean2, scale2, _ = moments(1)

    def activate_two(source, start, size):
        at = pl.ds(start, size)
        nv = (source[at, :] - mean2) * scale2
        normed2[at, :] = nv
        value, slope = gelu_parts(nv * gain2 + shift2 + masked[at, :])
        t = cotm[at, :] * slope
        through[at, :] = t
        return value, nv, t

    def activate_main(start, size, carry):
        value, nv, t = activate_two(acc, start, size)
        at = pl.ds(start, size)
        hid2[at, :] = value * mask[at, :]
        acc[at, :] = jnp.zeros((size, ch), F32)
        return carry[0] + fold(t * nv), carry[1] + fold(t)

    send_stats(2, [flatten(v) for v in chunked(activate_main, (zero, zero))])
    take_rows(1, normed2)
    take_cotangent()
    activate_two(normed2, cells, edge)
    weights_sent(1)
    gathered_sent(1)
    stats_sent(1)
    row_sent(1)

    def gradient_sums(slot):
        take_stats(slot)
        got = [st_recv[slot, k] for k in range(s_count)]
        return sum(g[0:1] for g in got), sum(g[1:2] for g in got)

    def norm_back(upstream, normed, gain, scale, sums):
        gain_grad, shift_grad = sums
        factor = gain * scale
        level, tilt = shift_grad / count, gain_grad / count

        def fill(start, size, carry):
            at = pl.ds(start, size)
            v = upstream[at, :] - mask[at, :] * (level + normed[at, :] * tilt)
            hid[at, :] = factor * v
            return carry
        return fill

    sums2 = gradient_sums(2)
    pack_field(3, hid, norm_back(through, normed2, gain2, scale2, sums2))
    backward(1)

    def inner_main(start, size, carry):
        at = pl.ds(start, size)
        v = acc[at, :] * slope1[at, :]
        slope1[at, :] = v
        acc[at, :] = jnp.zeros((size, ch), F32)
        return carry[0] + fold(v * normed1[at, :]), carry[1] + fold(v)

    for side, start in ((0, 0), (1, cells - wide)):
        row_send[2, side] = acc[start:start + wide, :]
    send_stats(3, [flatten(v) for v in chunked(inner_main, (zero, zero))])
    for side in range(2):
        row_copy(2, side).start()

    @pl.when(jnp.logical_not(passing))
    def _():
        of_step(n - 1, functools.partial(make_grad, 1))
    for side in range(2):
        row_copy(2, 1 - side).wait_recv()
        at = slice(cells + side * wide, cells + (side + 1) * wide)
        slope1[at, :] = row_recv[2, side] * slope1[at, :]
    stats_sent(2)
    gathered_sent(3)
    sums1 = gradient_sums(3)
    pack_field(2, hid, norm_back(slope1, normed1, gain1, scale1, sums1))
    advance_all(1, 1)
    backward(0)
    advance(0, n)

    def finish_input(start, size, carry):
        at = pl.ds(start, size)
        acc[at, :] = (acc[at, :] + through[at, :]) * mask[at, :]
        return carry

    chunked(finish_input, 0)
    to_flat(acc, flat_input)
    input_copy = pltpu.make_async_copy(flat_input, out_input, r_sem.at[1])
    input_copy.start()
    out_gain1[...], out_shift1[...] = sums1
    out_gain2[...], out_shift2[...] = sums2
    at_the_end(straight_sum)
    for extra in range(1, len(stages) - 1):
        advance(0, n + extra)
        if extra == 1:
            at_the_end(straight_finish)

    stats_sent(3)
    row_sent(2)
    gathered_sent(2)
    grads_sent(1)
    grads_sent(0)
    results[0].wait()
    input_copy.wait()


def finish_kernel(count, *refs):
    ins, outs = refs[:count], refs[count:2 * count]
    narrow, wide, in_sem, out_sem, take_sem, give_sem = refs[2 * count:2 * count + 6]
    held = refs[2 * count + 6:]
    rows = narrow.shape[1] // FINISH_PARTS
    parts = [(w, i, pl.ds(i * rows, rows)) for i in range(FINISH_PARTS) for w in range(2)]
    loads = [pltpu.make_async_copy(ins[w].at[at, :], narrow.at[w, at, :], in_sem.at[w, i]) for w, i, at in parts]
    stores = [pltpu.make_async_copy(wide.at[w, at, :], outs[w].at[at, :], out_sem.at[w, i]) for w, i, at in parts]
    takes = [pltpu.make_async_copy(ins[2 + k], v, take_sem.at[k]) for k, v in enumerate(held)]
    gives = [pltpu.make_async_copy(v, outs[2 + k], give_sem.at[k]) for k, v in enumerate(held)]
    for copy in loads + takes:
        copy.start()
    for load, store, (w, i, at) in zip(loads, stores, parts):
        load.wait()
        wide[w, at, :] = narrow[w, at, :].astype(F32)
        store.start()
    for take, give in zip(takes, gives):
        take.wait()
        give.start()
    for copy in stores + gives:
        copy.wait()


def per_device(n, s_count, blocks, weight_one, weight_two, gain_one, shift_one, gain_two, shift_two, cell_live, cotangent):
    rows, wide = cell_live.shape
    ch = blocks.shape[1] // wide
    cells = rows * wide
    total = cells + 2 * wide
    packed = -(-most_live(rows // HALVES, wide) // 16) * 16
    aligned = ch % 128 == 0
    chips = s_count // 2
    tap_rows = 9 * ch
    half_rows = tap_rows // 2
    owners = math.gcd(half_rows // 16, chips)
    piece = half_rows // owners

    if aligned:
        weight_one, weight_two = (w.reshape(tap_rows, n * ch) for w in (weight_one, weight_two))
    else:
        weight_one, weight_two = (
            w.reshape(tap_rows, n, ch).transpose(1, 0, 2) for w in (weight_one, weight_two))
    grad_shape = (2, owners, piece, n * ch) if aligned else (n, 2, owners, piece, ch)
    vmem = pl.BlockSpec(memory_space=pltpu.VMEM)
    hbm = pl.BlockSpec(memory_space=pl.ANY)
    sem = pltpu.SemaphoreType.DMA
    field = pltpu.VMEM((total, ch), F32)
    scratch = [
        pltpu.VMEM((ch * wide, 128), F32),
        pltpu.VMEM((2, n, tap_rows, ch), BF16),
        pltpu.VMEM((2, n - 1, tap_rows, ch), BF16),
        pltpu.VMEM((2, 3 * ch, cells), BF16),
        pltpu.VMEM((HALVES, packed, cells // HALVES), BF16),
        pltpu.VMEM((HALVES, cells // HALVES, packed), BF16),
        pltpu.VMEM((HALVES, cells // HALVES, ch), F32),
        pltpu.VMEM((2, 2, wide, ch), BF16),
        pltpu.VMEM((2, 2, wide, ch), BF16),
        pltpu.VMEM((2, wide, ch), BF16),
        pltpu.VMEM((2, wide, ch), BF16),
        field, field, field, field, field, field, field, field, field,
        pltpu.VMEM((total + 16, ch), F32),
        pltpu.VMEM((cells, ch), F32),
        pltpu.VMEM((4, n, 2 * wide + HALVES * packed, ch), BF16),
        pltpu.VMEM((n, rows + 2, wide, 3 * ch), BF16),
        pltpu.VMEM((2, n, 2, owners, piece, ch), F32),
        pltpu.VMEM((2, n, owners, piece, ch), BF16),
        pltpu.VMEM((2, n, owners, piece, ch), BF16),
        pltpu.VMEM((2, n, owners, piece, ch), BF16),
        pltpu.VMEM((2, n, chips, piece, ch), BF16),
        pltpu.VMEM((2, owners, piece, ch), BF16),
        pltpu.VMEM((s_count, piece, ch), BF16),
        pltpu.VMEM((2, n, 2, owners, piece, ch), BF16),
        pltpu.VMEM((4, 8, ch), F32),
        pltpu.VMEM((4, s_count, 8, ch), F32),
        pltpu.VMEM((3, 2, wide, ch), F32),
        pltpu.VMEM((3, 2, wide, ch), F32),
        pltpu.VMEM((rows, ch * wide), BF16),
        pltpu.VMEM((rows, ch * wide), F32),
        pltpu.VMEM((rows, ch * wide), BF16),
        sem((2, n)),
        sem((2, n)), sem((2, n)),
        sem((2, n - 1, s_count)), sem((2, n - 1, s_count)),
        sem((2,)), sem((2,)),
        sem((2,)), sem((2,)),
        sem((4, 2, n, HALVES)), sem((4, n, HALVES)),
        sem((4, s_count)), sem((4, s_count)),
        sem((3, 2)), sem((3, 2)),
        sem((2, n)), sem((2, n)),
        sem((2, n, chips)), sem((2, n, chips)),
        sem((s_count,)), sem((s_count,)),
        sem((s_count,)), sem((s_count,)),
        sem((2, n, chips)), sem((2, n, chips)),
        sem((2, n)), sem((2, n)),
        sem((2, n)),
        sem((3,)),
    ]
    block_out, input_grad, wg1, wg2, *sums = pl.pallas_call(
        functools.partial(block_kernel, n, s_count, rows, wide, ch, aligned, packed),
        out_shape=(
            jax.ShapeDtypeStruct((rows, ch * wide), BF16),
            jax.ShapeDtypeStruct((rows, ch * wide), F32),
            jax.ShapeDtypeStruct(grad_shape, BF16),
            jax.ShapeDtypeStruct(grad_shape, BF16),
            *[jax.ShapeDtypeStruct((1, ch), F32)] * 4,
        ),
        in_specs=[vmem, hbm] + [vmem] * 5 + [hbm] * 2,
        out_specs=(hbm, hbm, hbm, hbm, vmem, vmem, vmem, vmem),
        scratch_shapes=scratch,
        compiler_params=pltpu.CompilerParams(
            collective_id=0, has_side_effects=True, vmem_limit_bytes=60 * 1024 * 1024),
    )(blocks, cotangent, cell_live.T,
      *(v.reshape(1, ch) for v in (gain_one, shift_one, gain_two, shift_two)), weight_one, weight_two)

    if not aligned:
        def whole(grad):
            grad = grad.reshape(n, tap_rows, ch).transpose(1, 0, 2)
            return grad.astype(F32).reshape(9, ch, n * ch)
        return (block_out, input_grad, whole(wg1), whole(wg2), *(v.reshape(ch) for v in sums))

    wg1, wg2 = (w.reshape(tap_rows, n * ch) for w in (wg1, wg2))
    wide_grad = jax.ShapeDtypeStruct((tap_rows, n * ch), F32)
    moved = (block_out, input_grad, *sums)
    grad1, grad2, *moved = pl.pallas_call(
        functools.partial(finish_kernel, 2 + len(moved)),
        out_shape=(wide_grad, wide_grad, *(jax.ShapeDtypeStruct(v.shape, v.dtype) for v in moved)),
        in_specs=[pl.BlockSpec(memory_space=pl.ANY)] * (2 + len(moved)),
        out_specs=[pl.BlockSpec(memory_space=pl.ANY)] * (2 + len(moved)),
        scratch_shapes=[
            pltpu.VMEM((2, tap_rows, n * ch), BF16), pltpu.VMEM((2, tap_rows, n * ch), F32),
            sem((2, FINISH_PARTS)), sem((2, FINISH_PARTS)), sem((len(moved),)), sem((len(moved),)),
            *(pltpu.VMEM(v.shape, v.dtype) for v in moved),
        ],
        compiler_params=pltpu.CompilerParams(vmem_limit_bytes=64 * 1024 * 1024),
    )(wg1, wg2, *moved)
    block_out, input_grad, *sums = moved
    grads = (g.reshape(9, ch, n * ch) for g in (grad1, grad2))
    return (block_out, input_grad, *grads, *(v.reshape(ch) for v in sums))


def solution(mesh):
    return jax.shard_map(
        functools.partial(per_device, mesh.shape["chan"], mesh.shape["space"]),
        mesh=mesh,
        in_specs=(
            P("space", "chan"),
            P(None, "chan", None),
            P(None, "chan", None),
            P("chan"),
            P("chan"),
            P("chan"),
            P("chan"),
            P("space", None),
            P("space", "chan"),
        ),
        out_specs=(
            P("space", "chan"),
            P("space", "chan"),
            P(None, "chan", None),
            P(None, "chan", None),
            P("chan"),
            P("chan"),
            P("chan"),
            P("chan"),
        ),
        check_vma=False,
    )
```

```python
import functools
import math

import jax
import jax.numpy as jnp
from jax import lax
from jax.experimental import pallas as pl
from jax.experimental.pallas import tpu as pltpu
from jax.sharding import PartitionSpec as P

EPSILON = 1e-05
MESH = pl.DeviceIdType.MESH
F32 = jnp.float32
BF16 = jnp.bfloat16
ROOT_HALF = 0.7071067811865476
ROOT_TWO_PI = 0.3989422804014327
CHUNK = 64
FINISH_PARTS = 4
UNROLL = 2
HALVES = 2
LARGE, SMALL = 7, 3


def dot(a, b):
    return jnp.dot(a, b, preferred_element_type=F32)


def gelu_parts(v):
    upper = 0.5 * (1.0 + lax.erf(v * ROOT_HALF))
    slope = upper + v * (ROOT_TWO_PI * jnp.exp(-0.5 * v * v))
    return v * upper, slope


def most_live(rows, wide):
    units = (wide + 1) // (SMALL + 1)
    live_rows = rows - rows // (LARGE + 1)
    return min(rows * wide, math.ceil(units * live_rows * LARGE / 2))


def block_kernel(n, s_count, rows, wide, ch, aligned, packed, *refs):
    (x_in, cot_in, live_in, gain1_in, shift1_in, gain2_in, shift2_in, w1_hbm, w2_hbm) = refs[:9]
    (out_block, out_input, out_wg1, out_wg2, out_gain1, out_shift1, out_gain2, out_shift2) = refs[9:17]
    (turned, wv, wf, x_t, pack, unpack, places, edge_send, edge_recv, cot_send, cot_recv, cotm, mask, masked,
     normed1, normed2, through, slope1, hid, hid2, pad, acc, hold, taken,
     part, psend, crecv, hsend, qrecv, wout, st_send, st_recv, row_send, row_recv, flat_block, flat_input, cot_flat,
     w_sem, wz_ssem, wz_rsem, wp_ssem, wp_rsem, e_ssem, e_rsem, ce_ssem, ce_rsem, ag_ssem, ag_rsem, far_ssem,
     st_ssem, st_rsem, row_ssem, row_rsem, c_ssem, c_rsem, q_ssem, q_rsem,
     f_ssem, f_rsem, h_ssem, h_rsem, o_sem, r_sem) = refs[17:]

    z = lax.axis_index("chan")
    s = lax.axis_index("space")
    cells = rows * wide
    total = cells + 2 * wide
    band = cells // HALVES
    core, chip, chips = s % 2, s // 2, s_count // 2
    before, after = (s + s_count - 1) % s_count, (s + 1) % s_count
    tap_rows = 9 * ch
    half_rows = tap_rows // 2
    owners = math.gcd(half_rows // 16, chips)
    piece = half_rows // owners

    barrier = pltpu.get_barrier_semaphore()

    @pl.loop(1, s_count)
    def _(k):
        pl.semaphore_signal(barrier, inc=1, device_id=(z, (s + k) % s_count), device_id_type=MESH)

    @pl.loop(1, n)
    def _(k):
        pl.semaphore_signal(barrier, inc=1, device_id=((z + k) % n, s), device_id_type=MESH)

    w_copies = []
    for which, source in enumerate((w1_hbm, w2_hbm)):
        for d in range(n):
            block = source.at[:, d * ch:(d + 1) * ch] if aligned else source.at[d]
            w_copies.append(pltpu.make_async_copy(block, wv.at[which, d], w_sem.at[which, d]))
    for copy in w_copies:
        copy.start()

    cot_load = pltpu.make_async_copy(cot_in, cot_flat, r_sem.at[2])
    cot_load.start()

    def chunked(fn, init, first=0, count=cells):
        def step(i, carry):
            return fn(pl.multiple_of(first + i * CHUNK, CHUNK), CHUNK, carry)
        return lax.fori_loop(0, count // CHUNK, step, init, unroll=UNROLL)

    lanes = 128
    tiles = ch * wide // lanes

    def from_flat(flat, put):
        for i in range(tiles):
            turned[i * lanes:(i + 1) * lanes, 0:rows] = flat[:, i * lanes:(i + 1) * lanes].astype(F32).T
        for w in range(wide):
            put(pl.ds(w, rows, stride=wide), turned[pl.ds(w, ch, stride=wide), 0:rows].T)

    def to_flat(source, flat):
        for w in range(wide):
            turned[pl.ds(w, ch, stride=wide), 0:rows] = source[pl.ds(w, rows, stride=wide), :].T
        for i in range(tiles):
            flat[:, i * lanes:(i + 1) * lanes] = turned[i * lanes:(i + 1) * lanes, 0:rows].T.astype(flat.dtype)

    def edge_copy(side):
        return pltpu.make_async_remote_copy(
            src_ref=edge_send.at[side], dst_ref=edge_recv.at[1 - side],
            send_sem=e_ssem.at[side], recv_sem=e_rsem.at[1 - side],
            device_id=(z, before if side == 0 else after), device_id_type=MESH)


    def cot_copy(side):
        return pltpu.make_async_remote_copy(
            src_ref=cot_send.at[side], dst_ref=cot_recv.at[1 - side],
            send_sem=ce_ssem.at[side], recv_sem=ce_rsem.at[1 - side],
            device_id=(z, before if side == 0 else after), device_id_type=MESH)

    def load_cotangent():
        def put(at, value):
            cotm[at, :] = value
        cot_load.wait()
        from_flat(cot_flat, put)

        def live_only(start, size, carry):
            at = pl.ds(start, size)
            cotm[at, :] = cotm[at, :] * mask[at, :]
            return carry
        chunked(live_only, 0)
        for side, start in ((0, 0), (1, cells - wide)):
            cot_send[side] = cotm[start:start + wide, :].astype(BF16)
            cot_copy(side).start()

    def take_cotangent():
        for side in range(2):
            cot_copy(1 - side).wait_recv()
            at = slice(cells + side * wide, cells + (side + 1) * wide)
            cotm[at, :] = cot_recv[side].astype(F32) * mask[at, :]

    w_parts = math.gcd(tap_rows // 16, s_count)
    w_rows = tap_rows // w_parts
    w_mine = s % w_parts
    w_group = s - w_mine

    def wz_copy(which, k):
        at = pl.ds(w_mine * w_rows, w_rows)
        slot = n - k - 1
        return pltpu.make_async_remote_copy(
            src_ref=wv.at[which, (z + k) % n, at, :], dst_ref=wf.at[which, slot, at, :],
            send_sem=wz_ssem.at[which, slot], recv_sem=wz_rsem.at[which, slot],
            device_id=((z + k) % n, s), device_id_type=MESH)

    def wp_copy(which, slot, k, whose):
        at = pl.ds(whose * w_rows, w_rows)
        return pltpu.make_async_remote_copy(
            src_ref=wf.at[which, slot, at, :], dst_ref=wf.at[which, slot, at, :],
            send_sem=wp_ssem.at[which, slot, k], recv_sem=wp_rsem.at[which, slot, whose],
            device_id=(z, w_group + (w_mine + k) % w_parts), device_id_type=MESH)

    def weights_over_z(which):
        for copy in w_copies[which * n:(which + 1) * n]:
            copy.wait()
        for k in range(1, n):
            wz_copy(which, k).start()

    def slot_of(block):
        return (block - z + n - 1) % n

    def weights_round(which):
        @pl.loop(1, n)
        def _(distance):
            for sign in (1, -1):
                block = z - distance * sign

                @pl.when((block >= 0) & (block < n))
                def _():
                    slot = slot_of(block)
                    wz_copy(which, n - 1 - slot).wait_recv()
                    for k in range(1, w_parts):
                        wp_copy(which, slot, k, w_mine).start()

    def weights_arrived(which, slot):
        @pl.loop(1, w_parts)
        def _(k):
            wp_copy(which, slot, k, (w_mine + k) % w_parts).wait_recv()

    def weights_sent(which):
        for k in range(1, n):
            wz_copy(which, k).wait_send()

        @pl.loop(1, w_parts)
        def _(k):
            for slot in range(n - 1):
                wp_copy(which, slot, k, w_mine).wait_send()

    def row_copy(slot, side):
        return pltpu.make_async_remote_copy(
            src_ref=row_send.at[slot, side], dst_ref=row_recv.at[slot, 1 - side],
            send_sem=row_ssem.at[slot, side], recv_sem=row_rsem.at[slot, 1 - side],
            device_id=(z, before if side == 0 else after), device_id_type=MESH)

    def send_rows(slot, ref):
        for side, start in ((0, 0), (1, cells - wide)):
            row_send[slot, side] = ref[start:start + wide, :]
            row_copy(slot, side).start()

    def take_rows(slot, ref):
        for side in range(2):
            row_copy(slot, 1 - side).wait_recv()
            ref[cells + side * wide:cells + (side + 1) * wide, :] = row_recv[slot, side]

    def st_copy(slot, k, whose):
        return pltpu.make_async_remote_copy(
            src_ref=st_send.at[slot], dst_ref=st_recv.at[slot, whose],
            send_sem=st_ssem.at[slot, k], recv_sem=st_rsem.at[slot, whose],
            device_id=(z, (s + k) % s_count), device_id_type=MESH)

    def send_stats(slot, values):
        for i, v in enumerate(values):
            st_send[slot, i:i + 1, :] = v
        for k in sorted(range(1, s_count), key=lambda k: abs(k - s_count // 2)):
            st_copy(slot, k, s).start()
        st_recv[slot, s] = st_send[slot]

    def take_stats(slot):
        for k in range(1, s_count):
            st_copy(slot, k, (s + k) % s_count).wait_recv()

    strip = 8
    column = lax.broadcasted_iota(jnp.int32, (strip * wide, ch), 0) % wide

    def shift(target, first, count):
        size = count * wide
        where = column[:size]
        here = pad[pl.ds(8 + first * wide, size), :]
        left = jnp.where(where == 0, 0.0, pad[pl.ds(7 + first * wide, size), :])
        right = jnp.where(where == wide - 1, 0.0, pad[pl.ds(9 + first * wide, size), :])
        for b, v in enumerate((left, here, right)):
            target[pl.ds(first, count), :, b * ch:(b + 1) * ch] = v.astype(BF16).reshape(count, wide, ch)

    edge = 2 * wide
    ag_rows = (((0, edge + packed), (edge + packed, packed)), ((0, packed), (packed, edge + packed)))
    held_rows = (slice(0, packed), slice(packed + edge, edge + 2 * packed))
    held_edge = (slice(packed, packed + wide), slice(packed + wide, packed + edge))
    band_rows = rows // HALVES

    def unpack_half(ph, block, q, target):
        if q == (HALVES - 1 if ph == 0 else 0):
            pad[8:8 + wide, :] = hold[ph, block, held_edge[0], :].astype(F32)
            pad[8 + wide + cells:8 + 2 * wide + cells, :] = hold[ph, block, held_edge[1], :].astype(F32)
            shift(target, 0, 1)
            shift(target, rows + 1, 1)
        pad[8 + wide + q * band:8 + wide + (q + 1) * band, :] = dot(unpack[q], hold[ph, block, held_rows[q], :])

        for i in range(band_rows // strip):
            shift(target, 1 + q * band_rows + i * strip, strip)

    def add_conv(ph, q, field, taps, turned_taps=None):
        if turned_taps is None:
            rhs = jnp.concatenate([taps(a) for a in range(3)], axis=1)
        else:
            rhs = jnp.concatenate([
                jnp.concatenate([turned_taps(3 * (2 - a) + 2 - b) for b in range(3)], axis=1) for a in range(3)], axis=0)
        contract = (((1,), (0 if turned_taps is None else 1,)), ((), ()))

        def add(first, last):
            count = last - first
            lhs = field[first:last + 2, :, :].reshape((count + 2) * wide, 3 * ch)
            value = lax.dot_general(lhs, rhs, contract, preferred_element_type=F32)
            at = pl.ds(first * wide, count * wide)
            acc[at, :] = acc[at, :] + sum(
                value[a * wide:(a + count) * wide, a * ch:(a + 1) * ch] for a in range(3))

        if q == 0:
            add(1 if ph == 0 else 0, band_rows - 1)
        else:
            add(band_rows - 1, rows)
            if ph == 0:
                add(0, 1)

    def ag_copy(ph, block, q, sign):
        at = pl.ds(*ag_rows[ph == 0][q])
        return pltpu.make_async_remote_copy(
            src_ref=hold.at[ph, block, at, :], dst_ref=hold.at[ph, block, at, :],
            send_sem=ag_ssem.at[ph, (1 - sign) // 2, block, q], recv_sem=ag_rsem.at[ph, block, q],
            device_id=(z + sign, s), device_id_type=MESH)

    def inside(slice_at):
        return (slice_at >= 0) & (slice_at < n)

    at_end = (z == 0) | (z == n - 1)

    def far_copy(ph, block, q):
        at = pl.ds(*ag_rows[ph == 0][q])
        return pltpu.make_async_remote_copy(
            src_ref=hold.at[ph, block, at, :], dst_ref=hold.at[ph, block, at, :],
            send_sem=far_ssem.at[ph, q], recv_sem=ag_rsem.at[ph, block, q],
            device_id=(n - 1 - z, s), device_id_type=MESH)

    def passes_at(k, sign):
        return inside(z + sign) & ((k < n - 2) | (n <= 2))

    def pack_field(ph, source, fill=None, first=None, edges=None):
        for q in range(HALVES):
            if first is not None:
                first(q)
            if fill is not None:
                chunked(fill, 0, q * band, band)
            hold[ph, z, held_rows[q], :] = dot(pack[q], source[q * band:(q + 1) * band, :].astype(BF16)).astype(BF16)
            if q == (HALVES - 1 if ph == 0 else 0):
                if edges is not None:
                    edges()
                if fill is not None:
                    fill(cells, edge, 0)
                for side in range(2):
                    hold[ph, z, held_edge[side], :] = source[cells + side * wide:cells + (side + 1) * wide, :].astype(BF16)
            for sign in (1, -1):
                @pl.when((z + sign >= 0) & (z + sign < n))
                def _():
                    ag_copy(ph, z, q, sign).start()
            if n > 2:
                @pl.when(at_end)
                def _():
                    far_copy(ph, z, q).start()

    def take_and_pass(ph, k, q, sign, passes=True, takes=True):
        block = z - k * sign

        @pl.when((k > 0) & inside(block))
        def _():
            if passes and takes:
                ag_copy(ph, block, q, sign).wait_recv()

            @pl.when(passes_at(k, sign))
            def _():
                if passes:
                    if not takes:
                        ag_copy(ph, block, q, sign).wait_recv()
                    ag_copy(ph, block, q, sign).start()

            if not passes:
                @pl.when(jnp.logical_not(passes_at(k, sign)))
                def _():
                    ag_copy(ph, block, q, sign).wait_recv()

    near = jnp.where(z < n - n // 2, 1, 0)

    def consume_way(k, q, way, consume):
        block = z - k * (1 - 2 * way)

        @pl.when((k >= 0) & (k < n) & inside(block) & ((k > 0) | (way == near)))
        def _():
            consume(k, block, q)

    def take_both(ph, k, q, **how):
        @pl.loop(0, 2)
        def _(i):
            way = (near + i) % 2
            take_and_pass(ph, k, q, 1 - 2 * way, **how)

    def gather(ph, consume, each):
        @pl.loop(0, n)
        def _(k):
            for q in range(HALVES):
                take_both(ph, k, q)
                if q:
                    consume_way(k, q - 1, 1 - near, consume)
                else:
                    consume_way(k - 1, HALVES - 1, 1 - near, consume)
                consume_way(k, q, near, consume)
            each(k)

    def gather_passing_first(ph, consume, each):
        @pl.loop(0, n)
        def _(k):
            @pl.when(k == 1)
            def _():
                @pl.loop(1, n)
                def _(ahead):
                    for q in range(HALVES):
                        take_both(ph, ahead, q, takes=False)
            for q in range(HALVES):
                take_both(ph, k, q, passes=False)

                @pl.loop(0, 2)
                def _(i):
                    consume_way(k, q, (near + i) % 2, consume)
            each(k)

    last_hop = n - 3 if n > 2 else n
    last_pass = jnp.minimum(jnp.maximum(jnp.where(z < n - 1, z, 0), jnp.where(z > 0, n - 1 - z, 0)), last_hop)

    def forward(ph, field):
        def consume(k, block, q):
            into = taken.at[block]
            unpack_half(ph, block, q, into)

            @pl.when(k == 0)
            def _():
                add_conv(ph, q, into, lambda a: wv[ph, z, 3 * a * ch:3 * (a + 1) * ch, :])

            @pl.when(k > 0)
            def _():
                slot = slot_of(block)
                if q == 0:
                    weights_arrived(ph, slot)
                add_conv(ph, q, into, lambda a: wf[ph, slot, 3 * a * ch:3 * (a + 1) * ch, :])

        def each(k):
            if ph == 0:
                @pl.when(k == 1)
                def _():
                    weights_over_z(1)

            @pl.when(k == last_pass)
            def _():
                turn_field(ph, field)
                if ph == 0:
                    load_cotangent()
        (gather if ph else gather_passing_first)(ph, consume, each)

    def turn_field(ph, field):
        main = [field[start:start + ch, :].T for start in range(0, cells, ch)]
        ends = field[cells:cells + edge, :]
        if edge < ch:
            ends = jnp.concatenate([ends, jnp.zeros((ch - edge, ch), F32)], axis=0)
        ends = ends.T
        for i, here in enumerate(main):
            left = jnp.concatenate(
                [ends[:, 0:wide] if i == 0 else main[i - 1][:, ch - wide:], here[:, 0:ch - wide]], axis=1)
            right = jnp.concatenate(
                [here[:, wide:], main[i + 1][:, 0:wide] if i + 1 < len(main) else ends[:, wide:edge]], axis=1)
            for a, v in enumerate((left, here, right)):
                x_t[ph, a * ch:(a + 1) * ch, i * ch:(i + 1) * ch] = v.astype(BF16)

    def c_copy(ph, j):
        return pltpu.make_async_remote_copy(
            src_ref=psend.at[ph, j], dst_ref=crecv.at[ph, j],
            send_sem=c_ssem.at[ph, j], recv_sem=c_rsem.at[ph, j],
            device_id=(z, chip * 2 + 1 - core), device_id_type=MESH)

    def q_copy(ph, j, e, whose, owner):
        return pltpu.make_async_remote_copy(
            src_ref=hsend.at[ph, j, owner], dst_ref=qrecv.at[ph, j, whose],
            send_sem=q_ssem.at[ph, j, e], recv_sem=q_rsem.at[ph, j, whose],
            device_id=(z, ((chip + e) % chips) * 2 + core), device_id_type=MESH)

    def f_copy(ph, j, e, owner):
        return pltpu.make_async_remote_copy(
            src_ref=wout.at[ph, j, core, owner], dst_ref=wout.at[ph, j, core, owner],
            send_sem=f_ssem.at[ph, j, e], recv_sem=f_rsem.at[ph, j, owner],
            device_id=(z, ((chip + e) % chips) * 2 + core), device_id_type=MESH)

    def h_copy(ph, j, whose):
        return pltpu.make_async_remote_copy(
            src_ref=wout.at[ph, j, whose], dst_ref=wout.at[ph, j, whose],
            send_sem=h_ssem.at[ph, j], recv_sem=h_rsem.at[ph, j],
            device_id=(z, chip * 2 + 1 - core), device_id_type=MESH)

    def o_copy(ph, j):
        target = (out_wg1, out_wg2)[ph]
        if aligned:
            target = target.at[:, :, :, pl.ds(pl.multiple_of(j * ch, ch), ch)]
        else:
            target = target.at[j]
        return pltpu.make_async_copy(wout.at[ph, j], target, o_sem.at[ph, j])

    def sum_cores(ph, j):
        for o in range(owners):
            psend[ph, j, o] = part[ph, j, 1 - core, o].astype(BF16)
        c_copy(ph, j).start()

    def sum_chips(ph, j):
        c_copy(ph, j).wait_recv()
        for o in range(owners):
            v = part[ph, j, core, o] + crecv[ph, j, o].astype(F32)
            part[ph, j, core, o] = v
            hsend[ph, j, o] = v.astype(BF16)

        @pl.loop(1, chips)
        def _(e):
            peer = (chip + e) % chips

            @pl.when(peer < owners)
            def _():
                q_copy(ph, j, e, chip, peer).start()

    def spread_chips(ph, j):
        @pl.when(chip < owners)
        def _():
            @pl.loop(1, chips)
            def _(e):
                q_copy(ph, j, e, (chip + e) % chips, chip).wait_recv()
            v = part[ph, j, core, chip]
            for e in range(1, chips):
                v = v + qrecv[ph, j, (chip + e) % chips].astype(F32)
            wout[ph, j, core, chip] = v.astype(BF16)

            @pl.loop(1, chips)
            def _(e):
                f_copy(ph, j, e, chip).start()

    def spread_cores(ph, j):
        @pl.loop(1, chips)
        def _(e):
            peer = (chip + e) % chips

            @pl.when(peer < owners)
            def _():
                f_copy(ph, j, e, peer).wait_recv()
        h_copy(ph, j, core).start()

    def finish(ph, j):
        h_copy(ph, j, 1 - core).wait_recv()
        o_copy(ph, j).start()

    def put_part(ph, j, tap, value):
        start = tap * ch
        done = 0
        while done < ch:
            row = start + done
            side, o, at = row // half_rows, row % half_rows // piece, row % piece
            size = min(ch - done, piece - at)
            part[ph, j, side, o, at:at + size, :] = value[done:done + size, :]
            done += size

    stages = (sum_cores, sum_chips, spread_chips, spread_cores, finish)

    def of_step(k, fn):
        @pl.loop(0, 2)
        def _(way):
            block = z - k * (1 - 2 * way)

            @pl.when((k >= 0) & (k < n) & inside(block) & ((k > 0) | (way == 0)))
            def _():
                fn(block)

    passing = last_pass > 0

    def made_at(step):
        first = jnp.where(passing & (step > 0) & (step < last_pass), step + 1, jnp.where(passing & (step == last_pass), 1, step))
        return first, step + 1

    def advance(ph, k):
        for age in range(1, len(stages)):
            step = k - age

            @pl.when((step >= 0) & (step < n))
            def _():
                @pl.loop(*made_at(step))
                def _(made):
                    of_step(made, functools.partial(stages[age], ph))

    def advance_all(ph, age):
        @pl.loop(0, n)
        def _(j):
            stages[age](ph, j)

    def field_grad(ph, block):
        grad = taken[block, 1:rows + 1, :, :].reshape(cells, 3 * ch)
        value = dot(x_t[ph], grad)
        for a in range(3):
            for b in range(3):
                put_part(ph, block, 3 * a + b, value[a * ch:(a + 1) * ch, (2 - b) * ch:(3 - b) * ch])

    def make_grad(ph, block):
        field_grad(ph, block)
        sum_cores(ph, block)

    results = [pltpu.make_async_copy(flat_block, out_block, r_sem.at[0])]

    def backward(ph):
        last = ph == 0

        def consume(k, block, q):
            into = taken.at[block]
            unpack_half(2 + ph, block, q, into)

            def grad():
                if q == HALVES - 1:
                    @pl.when(((k == 0) | (k >= last_pass)) & (last | passing | (k < n - 1)))
                    def _():
                        make_grad(ph, block)
            if last:
                grad()
            add_conv(2 + ph, q, into, None, lambda t: wv[ph, block, t * ch:(t + 1) * ch, :])
            if not last:
                grad()

        def each(k):
            first, end = made_at(k)

            @pl.loop(first, end - 1)
            def _(step):
                of_step(step, functools.partial(make_grad, ph))
            if last:
                advance(ph, k)
                for age in range(2, len(stages)):
                    @pl.when(k == age - 2)
                    def _():
                        advance_all(1, age)
            else:
                @pl.when(k == last_pass)
                def _():
                    to_flat(hid2, flat_block)
                    results[0].start()
        gather(2 + ph, consume, each)

    def fold(v):
        return jnp.sum(v.reshape(v.shape[0] // 8, 8, ch), axis=0)

    def flatten(v):
        return jnp.sum(v, axis=0, keepdims=True)

    zero = jnp.zeros((8, ch), F32)

    def local_moments(ref):
        def sums(start, size, carry):
            at = pl.ds(start, size)
            m = mask[at, :]
            return carry[0] + fold(ref[at, :] * m), carry[1] + fold(m)
        added, number = (flatten(v) for v in chunked(sums, (zero, zero)))
        middle = added / jnp.maximum(number, 1.0)

        def spread(start, size, carry):
            at = pl.ds(start, size)
            c = (ref[at, :] - middle) * mask[at, :]
            return carry + fold(c * c)
        return added, number, flatten(chunked(spread, zero))

    def moments(slot):
        take_stats(slot)
        got = [st_recv[slot, k] for k in range(s_count)]
        added = sum(g[0:1] for g in got)
        number = sum(g[1:2] for g in got)
        mean = added / number
        spread = 0.0
        for g in got:
            off = g[0:1] / jnp.maximum(g[1:2], 1.0) - mean
            spread = spread + (g[2:3] + g[1:2] * off * off)
        return mean, lax.rsqrt(spread / number + EPSILON), number

    def everywhere(fn):
        chunked(fn, 0)
        fn(cells, 2 * wide, 0)

    gain1, shift1, gain2, shift2 = (r[...] for r in (gain1_in, shift1_in, gain2_in, shift2_in))

    pl.semaphore_wait(barrier, s_count - 1 + n - 1)
    weights_over_z(0)

    def put_masked(at, value):
        masked[at, :] = value

    from_flat(x_in, put_masked)

    cell = lax.broadcasted_iota(jnp.int32, (cells, rows), 0)
    pick = (cell // wide == lax.broadcasted_iota(jnp.int32, (cells, rows), 1)).astype(F32).astype(BF16)
    column_of = lax.broadcasted_iota(jnp.int32, (cells, wide), 0) % wide
    picked = lax.dot_general(pick, live_in[...].astype(BF16), (((1,), (1,)), ((), ())), preferred_element_type=F32)
    picked = jnp.where(column_of == lax.broadcasted_iota(jnp.int32, (cells, wide), 1), picked, 0.0)
    mask[0:cells, :] = dot(picked.astype(BF16), jnp.ones((wide, ch), BF16))

    def load_main(start, size, carry):
        at = pl.ds(start, size)
        lv = mask[at, :]
        masked[at, :] = masked[at, :] * lv
        return carry

    chunked(load_main, 0)
    for side, start in ((0, 0), (1, cells - wide)):
        edge_send[side, 0] = masked[start:start + wide, :].astype(BF16)
        edge_send[side, 1] = mask[start:start + wide, :].astype(BF16)

    acc[...] = jnp.zeros_like(acc)
    st_send[...] = jnp.zeros_like(st_send)

    for side in range(2):
        edge_copy(side).start()

    below = lax.broadcasted_iota(jnp.int32, (band, band), 1) < lax.broadcasted_iota(jnp.int32, (band, band), 0)
    below = below.astype(F32).astype(BF16)

    def make_pack(h):
        lv = mask[h * band:(h + 1) * band, :]
        place = jnp.where(lv > 0.0, dot(below, lv.astype(BF16)), -1.0)
        places[h] = place
        across = place.T[0:1, :]
        spot = lax.broadcasted_iota(jnp.int32, (packed, band), 0).astype(F32)
        pack[h] = jnp.where(spot == across, 1.0, 0.0).astype(BF16)

    def make_unpack(h):
        for start in range(0, packed, ch):
            size = min(ch, packed - start)
            spot = start + lax.broadcasted_iota(jnp.int32, (band, size), 1)
            unpack[h, :, start:start + size] = jnp.where(
                places[h, :, :size] == spot.astype(F32), 1.0, 0.0).astype(BF16)

    def take_edges():
        for side in range(2):
            edge_copy(1 - side).wait_recv()
            there = jnp.where(s > 0, 1.0, 0.0) if side == 0 else jnp.where(s < s_count - 1, 1.0, 0.0)
            at = slice(cells + side * wide, cells + (side + 1) * wide)
            masked[at, :] = edge_recv[side, 0].astype(F32) * there
            mask[at, :] = edge_recv[side, 1].astype(F32) * there

    def stats_sent(slot):
        for k in range(1, s_count):
            st_copy(slot, k, s).wait_send()

    def row_sent(slot):
        for side in range(2):
            row_copy(slot, side).wait_send()

    def gathered_sent(ph):
        @pl.loop(0, n)
        def _(k):
            for sign in (1, -1):
                block = z - k * sign

                @pl.when(inside(block) & (((k == 0) & inside(z + sign)) | passes_at(k, sign)))
                def _():
                    for q in range(HALVES):
                        ag_copy(ph, block, q, sign).wait_send()
        if n > 2:
            @pl.when(at_end)
            def _():
                for q in range(HALVES):
                    far_copy(ph, z, q).wait_send()

    def grads_sent(ph):
        pl.loop(0, n)(lambda j: grad_sent(ph, j))

    def grad_sent(ph, j):
        c_copy(ph, j).wait_send()
        h_copy(ph, j, core).wait_send()
        o_copy(ph, j).wait()
        for e in range(1, chips):
            peer = (chip + e) % chips

            @pl.when(peer < owners)
            def _():
                q_copy(ph, j, e, chip, peer).wait_send()

            @pl.when(chip < owners)
            def _():
                f_copy(ph, j, e, chip).wait_send()

    pack_field(0, masked, first=make_pack, edges=take_edges)
    weights_round(0)
    for h in range(HALVES):
        make_unpack(h)
    forward(0, masked)
    send_stats(0, local_moments(acc))
    send_rows(0, acc)
    weights_round(1)
    weights_sent(0)
    for side in range(2):
        edge_copy(side).wait_send()
        cot_copy(side).wait_send()
    mean1, scale1, count = moments(0)

    def activate_one(start, size, carry):
        at = pl.ds(start, size)
        main = start is not cells
        nv = ((acc if main else normed1)[at, :] - mean1) * scale1
        normed1[at, :] = nv
        hid[at, :] = gelu_parts(nv * gain1 + shift1)[0] * mask[at, :]
        if main:
            acc[at, :] = jnp.zeros((size, ch), F32)
        return carry

    def slope_one(start, size, carry):
        at = pl.ds(start, size)
        slope1[at, :] = gelu_parts(normed1[at, :] * gain1 + shift1)[1] * mask[at, :]
        return carry

    pack_field(1, hid, activate_one, edges=lambda: take_rows(0, normed1))
    everywhere(slope_one)
    forward(1, hid)
    send_stats(1, local_moments(acc))
    send_rows(1, acc)
    gathered_sent(0)
    stats_sent(0)
    row_sent(0)
    mean2, scale2, _ = moments(1)

    def activate_two(source, start, size):
        at = pl.ds(start, size)
        nv = (source[at, :] - mean2) * scale2
        normed2[at, :] = nv
        value, slope = gelu_parts(nv * gain2 + shift2 + masked[at, :])
        t = cotm[at, :] * slope
        through[at, :] = t
        return value, nv, t

    def activate_main(start, size, carry):
        value, nv, t = activate_two(acc, start, size)
        at = pl.ds(start, size)
        hid2[at, :] = value * mask[at, :]
        acc[at, :] = jnp.zeros((size, ch), F32)
        return carry[0] + fold(t * nv), carry[1] + fold(t)

    send_stats(2, [flatten(v) for v in chunked(activate_main, (zero, zero))])
    take_rows(1, normed2)
    take_cotangent()
    activate_two(normed2, cells, edge)
    weights_sent(1)
    gathered_sent(1)
    stats_sent(1)
    row_sent(1)

    def gradient_sums(slot):
        take_stats(slot)
        got = [st_recv[slot, k] for k in range(s_count)]
        return sum(g[0:1] for g in got), sum(g[1:2] for g in got)

    def norm_back(upstream, normed, gain, scale, sums):
        gain_grad, shift_grad = sums
        factor = gain * scale
        level, tilt = shift_grad / count, gain_grad / count

        def fill(start, size, carry):
            at = pl.ds(start, size)
            v = upstream[at, :] - mask[at, :] * (level + normed[at, :] * tilt)
            hid[at, :] = factor * v
            return carry
        return fill

    sums2 = gradient_sums(2)
    pack_field(3, hid, norm_back(through, normed2, gain2, scale2, sums2))
    backward(1)

    def inner_main(start, size, carry):
        at = pl.ds(start, size)
        v = acc[at, :] * slope1[at, :]
        slope1[at, :] = v
        acc[at, :] = jnp.zeros((size, ch), F32)
        return carry[0] + fold(v * normed1[at, :]), carry[1] + fold(v)

    for side, start in ((0, 0), (1, cells - wide)):
        row_send[2, side] = acc[start:start + wide, :]
    send_stats(3, [flatten(v) for v in chunked(inner_main, (zero, zero))])
    for side in range(2):
        row_copy(2, side).start()

    @pl.when(jnp.logical_not(passing))
    def _():
        of_step(n - 1, functools.partial(make_grad, 1))
    for side in range(2):
        row_copy(2, 1 - side).wait_recv()
        at = slice(cells + side * wide, cells + (side + 1) * wide)
        slope1[at, :] = row_recv[2, side] * slope1[at, :]
    stats_sent(2)
    gathered_sent(3)
    sums1 = gradient_sums(3)
    pack_field(2, hid, norm_back(slope1, normed1, gain1, scale1, sums1))
    advance_all(1, 1)
    backward(0)
    advance(0, n)

    def finish_input(start, size, carry):
        at = pl.ds(start, size)
        acc[at, :] = (acc[at, :] + through[at, :]) * mask[at, :]
        return carry

    chunked(finish_input, 0)
    to_flat(acc, flat_input)
    input_copy = pltpu.make_async_copy(flat_input, out_input, r_sem.at[1])
    input_copy.start()
    out_gain1[...], out_shift1[...] = sums1
    out_gain2[...], out_shift2[...] = sums2
    for extra in range(1, len(stages) - 1):
        advance(0, n + extra)

    stats_sent(3)
    row_sent(2)
    gathered_sent(2)
    grads_sent(1)
    grads_sent(0)
    results[0].wait()
    input_copy.wait()


def finish_kernel(count, *refs):
    ins, outs = refs[:count], refs[count:2 * count]
    narrow, wide, in_sem, out_sem, take_sem, give_sem = refs[2 * count:2 * count + 6]
    held = refs[2 * count + 6:]
    rows = narrow.shape[1] // FINISH_PARTS
    parts = [(w, i, pl.ds(i * rows, rows)) for i in range(FINISH_PARTS) for w in range(2)]
    loads = [pltpu.make_async_copy(ins[w].at[at, :], narrow.at[w, at, :], in_sem.at[w, i]) for w, i, at in parts]
    stores = [pltpu.make_async_copy(wide.at[w, at, :], outs[w].at[at, :], out_sem.at[w, i]) for w, i, at in parts]
    takes = [pltpu.make_async_copy(ins[2 + k], v, take_sem.at[k]) for k, v in enumerate(held)]
    gives = [pltpu.make_async_copy(v, outs[2 + k], give_sem.at[k]) for k, v in enumerate(held)]
    for copy in loads + takes:
        copy.start()
    for load, store, (w, i, at) in zip(loads, stores, parts):
        load.wait()
        wide[w, at, :] = narrow[w, at, :].astype(F32)
        store.start()
    for take, give in zip(takes, gives):
        take.wait()
        give.start()
    for copy in stores + gives:
        copy.wait()


def per_device(n, s_count, blocks, weight_one, weight_two, gain_one, shift_one, gain_two, shift_two, cell_live, cotangent):
    rows, wide = cell_live.shape
    ch = blocks.shape[1] // wide
    cells = rows * wide
    total = cells + 2 * wide
    packed = -(-most_live(rows // HALVES, wide) // 16) * 16
    aligned = ch % 128 == 0
    chips = s_count // 2
    tap_rows = 9 * ch
    half_rows = tap_rows // 2
    owners = math.gcd(half_rows // 16, chips)
    piece = half_rows // owners

    if aligned:
        weight_one, weight_two = (w.reshape(tap_rows, n * ch) for w in (weight_one, weight_two))
    else:
        weight_one, weight_two = (
            w.reshape(tap_rows, n, ch).transpose(1, 0, 2) for w in (weight_one, weight_two))
    grad_shape = (2, owners, piece, n * ch) if aligned else (n, 2, owners, piece, ch)
    vmem = pl.BlockSpec(memory_space=pltpu.VMEM)
    hbm = pl.BlockSpec(memory_space=pl.ANY)
    sem = pltpu.SemaphoreType.DMA
    field = pltpu.VMEM((total, ch), F32)
    scratch = [
        pltpu.VMEM((ch * wide, 128), F32),
        pltpu.VMEM((2, n, tap_rows, ch), BF16),
        pltpu.VMEM((2, n - 1, tap_rows, ch), BF16),
        pltpu.VMEM((2, 3 * ch, cells), BF16),
        pltpu.VMEM((HALVES, packed, cells // HALVES), BF16),
        pltpu.VMEM((HALVES, cells // HALVES, packed), BF16),
        pltpu.VMEM((HALVES, cells // HALVES, ch), F32),
        pltpu.VMEM((2, 2, wide, ch), BF16),
        pltpu.VMEM((2, 2, wide, ch), BF16),
        pltpu.VMEM((2, wide, ch), BF16),
        pltpu.VMEM((2, wide, ch), BF16),
        field, field, field, field, field, field, field, field, field,
        pltpu.VMEM((total + 16, ch), F32),
        pltpu.VMEM((cells, ch), F32),
        pltpu.VMEM((4, n, 2 * wide + HALVES * packed, ch), BF16),
        pltpu.VMEM((n, rows + 2, wide, 3 * ch), BF16),
        pltpu.VMEM((2, n, 2, owners, piece, ch), F32),
        pltpu.VMEM((2, n, owners, piece, ch), BF16),
        pltpu.VMEM((2, n, owners, piece, ch), BF16),
        pltpu.VMEM((2, n, owners, piece, ch), BF16),
        pltpu.VMEM((2, n, chips, piece, ch), BF16),
        pltpu.VMEM((2, n, 2, owners, piece, ch), BF16),
        pltpu.VMEM((4, 8, ch), F32),
        pltpu.VMEM((4, s_count, 8, ch), F32),
        pltpu.VMEM((3, 2, wide, ch), F32),
        pltpu.VMEM((3, 2, wide, ch), F32),
        pltpu.VMEM((rows, ch * wide), BF16),
        pltpu.VMEM((rows, ch * wide), F32),
        pltpu.VMEM((rows, ch * wide), BF16),
        sem((2, n)),
        sem((2, n)), sem((2, n)),
        sem((2, n - 1, s_count)), sem((2, n - 1, s_count)),
        sem((2,)), sem((2,)),
        sem((2,)), sem((2,)),
        sem((4, 2, n, HALVES)), sem((4, n, HALVES)),
        sem((4, HALVES)),
        sem((4, s_count)), sem((4, s_count)),
        sem((3, 2)), sem((3, 2)),
        sem((2, n)), sem((2, n)),
        sem((2, n, chips)), sem((2, n, chips)),
        sem((2, n, chips)), sem((2, n, chips)),
        sem((2, n)), sem((2, n)),
        sem((2, n)),
        sem((3,)),
    ]
    block_out, input_grad, wg1, wg2, *sums = pl.pallas_call(
        functools.partial(block_kernel, n, s_count, rows, wide, ch, aligned, packed),
        out_shape=(
            jax.ShapeDtypeStruct((rows, ch * wide), BF16),
            jax.ShapeDtypeStruct((rows, ch * wide), F32),
            jax.ShapeDtypeStruct(grad_shape, BF16),
            jax.ShapeDtypeStruct(grad_shape, BF16),
            *[jax.ShapeDtypeStruct((1, ch), F32)] * 4,
        ),
        in_specs=[vmem, hbm] + [vmem] * 5 + [hbm] * 2,
        out_specs=(hbm, hbm, hbm, hbm, vmem, vmem, vmem, vmem),
        scratch_shapes=scratch,
        compiler_params=pltpu.CompilerParams(
            collective_id=0, has_side_effects=True, vmem_limit_bytes=60 * 1024 * 1024),
    )(blocks, cotangent, cell_live.T,
      *(v.reshape(1, ch) for v in (gain_one, shift_one, gain_two, shift_two)), weight_one, weight_two)

    if not aligned:
        def whole(grad):
            grad = grad.reshape(n, tap_rows, ch).transpose(1, 0, 2)
            return grad.astype(F32).reshape(9, ch, n * ch)
        return (block_out, input_grad, whole(wg1), whole(wg2), *(v.reshape(ch) for v in sums))

    wg1, wg2 = (w.reshape(tap_rows, n * ch) for w in (wg1, wg2))
    wide_grad = jax.ShapeDtypeStruct((tap_rows, n * ch), F32)
    moved = (block_out, input_grad, *sums)
    grad1, grad2, *moved = pl.pallas_call(
        functools.partial(finish_kernel, 2 + len(moved)),
        out_shape=(wide_grad, wide_grad, *(jax.ShapeDtypeStruct(v.shape, v.dtype) for v in moved)),
        in_specs=[pl.BlockSpec(memory_space=pl.ANY)] * (2 + len(moved)),
        out_specs=[pl.BlockSpec(memory_space=pl.ANY)] * (2 + len(moved)),
        scratch_shapes=[
            pltpu.VMEM((2, tap_rows, n * ch), BF16), pltpu.VMEM((2, tap_rows, n * ch), F32),
            sem((2, FINISH_PARTS)), sem((2, FINISH_PARTS)), sem((len(moved),)), sem((len(moved),)),
            *(pltpu.VMEM(v.shape, v.dtype) for v in moved),
        ],
        compiler_params=pltpu.CompilerParams(vmem_limit_bytes=64 * 1024 * 1024),
    )(wg1, wg2, *moved)
    block_out, input_grad, *sums = moved
    grads = (g.reshape(9, ch, n * ch) for g in (grad1, grad2))
    return (block_out, input_grad, *grads, *(v.reshape(ch) for v in sums))


def solution(mesh):
    return jax.shard_map(
        functools.partial(per_device, mesh.shape["chan"], mesh.shape["space"]),
        mesh=mesh,
        in_specs=(
            P("space", "chan"),
            P(None, "chan", None),
            P(None, "chan", None),
            P("chan"),
            P("chan"),
            P("chan"),
            P("chan"),
            P("space", None),
            P("space", "chan"),
        ),
        out_specs=(
            P("space", "chan"),
            P("space", "chan"),
            P(None, "chan", None),
            P(None, "chan", None),
            P("chan"),
            P("chan"),
            P("chan"),
            P("chan"),
        ),
        check_vma=False,
    )
```

```python
import functools
import math

import jax
import jax.numpy as jnp
from jax import lax
from jax.experimental import pallas as pl
from jax.experimental.pallas import tpu as pltpu
from jax.sharding import PartitionSpec as P

EPSILON = 1e-05
MESH = pl.DeviceIdType.MESH
F32 = jnp.float32
BF16 = jnp.bfloat16
ROOT_HALF = 0.7071067811865476
ROOT_TWO_PI = 0.3989422804014327
CHUNK = 64
FINISH_PARTS = 4
UNROLL = 2
PLAIN_HALVES = 2
SCRATCH_LIMIT = 56 * 1024 * 1024
LARGE, SMALL = 7, 3


def dot(a, b):
    return jnp.dot(a, b, preferred_element_type=F32)


def gelu_parts(v):
    upper = 0.5 * (1.0 + lax.erf(v * ROOT_HALF))
    slope = upper + v * (ROOT_TWO_PI * jnp.exp(-0.5 * v * v))
    return v * upper, slope


def most_live(rows, wide):
    units = (wide + 1) // (SMALL + 1)
    live_rows = rows - rows // (LARGE + 1)
    return min(rows * wide, math.ceil(units * live_rows * LARGE / 2))


def packed_rows(rows, wide):
    return -(-most_live(rows, wide) // 16) * 16


def block_kernel(n, s_count, rows, wide, ch, aligned, packed, *refs):
    (x_in, cot_in, live_in, gain1_in, shift1_in, gain2_in, shift2_in, w1_hbm, w2_hbm) = refs[:9]
    (out_block, out_input, out_wg1, out_wg2, out_gain1, out_shift1, out_gain2, out_shift2) = refs[9:17]
    (turned, wv, wf, wvb, x_t1, x_t2, pack, unpack, places,
     masked, cot, mask, edge_send, edge_recv, cedge_send, cedge_recv, par_send, par_recv,
     mask_c, masked_c, cot_c, normed1, normed2, through, slope1, hid, block_c, pad, acc,
     hold0, hold1, hold3, taken, cot_send, cot_recv, ret_send, ret_recv, thr_n, blk_n,
     part, psend, crecv, hsend, qrecv, zz_send, zz_recv, wout, st_send, st_recv, row_send, row_recv, norm, scales,
     w_sem, wz_ssem, wz_rsem, wp_ssem, wp_rsem, wh_ssem, wh_rsem, e_ssem, e_rsem, ce_ssem, ce_rsem,
     par_ssem, par_rsem, a_ssem, a_rsem, b_ssem, b_rsem, ag_ssem, ag_rsem, cx_ssem, cx_rsem, ret_ssem, ret_rsem,
     st_ssem, st_rsem, row_ssem, row_rsem, c_ssem, c_rsem, q_ssem, q_rsem,
     f_ssem, f_rsem, h_ssem, h_rsem, zz_ssem, zz_rsem, o_sem) = refs[17:]

    parts = n // 2
    z = lax.axis_index("chan")
    s = lax.axis_index("space")
    m, p = z % 2, z // 2
    twin = z + 1 - 2 * m
    cells = rows * wide
    part_rows = rows // parts
    pc = part_rows * wide
    edge = 2 * wide
    pt = pc + edge
    core, chip, chips = s % 2, s // 2, s_count // 2
    before, after = (s + s_count - 1) % s_count, (s + 1) % s_count
    tap_rows = 9 * ch
    half_rows = tap_rows // 2
    owners = math.gcd(half_rows // 16, chips)
    piece = half_rows // owners

    def remote(src, dst, send, recv, at_z, at_s):
        return pltpu.make_async_remote_copy(
            src_ref=src, dst_ref=dst, send_sem=send, recv_sem=recv,
            device_id=(at_z, at_s), device_id_type=MESH)

    def inside(at):
        return (at >= 0) & (at < n)

    barrier = pltpu.get_barrier_semaphore()
    family = parts * s_count

    @pl.loop(1, family)
    def _(k):
        to = (2 * ((p + k // s_count) % parts) + m, (s + k % s_count) % s_count)
        pl.semaphore_signal(barrier, inc=1, device_id=to, device_id_type=MESH)

    @pl.loop(0, parts)
    def _(q):
        pl.semaphore_signal(barrier, inc=1, device_id=(2 * q + 1 - m, s), device_id_type=MESH)

    def place_of(block):
        return block % 2 * parts + block // 2

    w_copies = []
    for which, source in enumerate((w1_hbm, w2_hbm)):
        for d in range(n):
            block = source.at[:, d * ch:(d + 1) * ch] if aligned else source.at[d]
            w_copies.append(pltpu.make_async_copy(block, wv.at[which, place_of(d)], w_sem.at[which, d]))
    for d in range(n):
        block = w2_hbm.at[:, d * ch:(d + 1) * ch] if aligned else w2_hbm.at[d]
        w_copies.append(pltpu.make_async_copy(block, wvb.at[p, place_of(d)], w_sem.at[2, d]))
    for copy in w_copies:
        copy.start()

    def chunked(fn, init, count=pc):
        def step(i, carry):
            return fn(pl.multiple_of(i * CHUNK, CHUNK), CHUNK, carry)
        return lax.fori_loop(0, count // CHUNK, step, init, unroll=UNROLL)

    lanes = 128
    tiles = ch * wide // lanes

    def from_flat(flat, put):
        for i in range(tiles):
            turned[i * lanes:(i + 1) * lanes, 0:rows] = flat[:, i * lanes:(i + 1) * lanes].astype(F32).T
        for w in range(wide):
            put(pl.ds(w, rows, stride=wide), turned[pl.ds(w, ch, stride=wide), 0:rows].T)

    def to_flat(source, flat):
        for w in range(wide):
            turned[pl.ds(w, ch, stride=wide), 0:rows] = source[pl.ds(w, rows, stride=wide), :].T
        for i in range(tiles):
            flat[:, i * lanes:(i + 1) * lanes] = turned[i * lanes:(i + 1) * lanes, 0:rows].T.astype(flat.dtype)


    def edge_copy(side):
        return remote(edge_send.at[side], edge_recv.at[1 - side], e_ssem.at[side], e_rsem.at[1 - side],
                      z, before if side == 0 else after)

    def cedge_copy(side):
        return remote(cedge_send.at[side], cedge_recv.at[1 - side], ce_ssem.at[side], ce_rsem.at[1 - side],
                      z, before if side == 0 else after)

    def others(fn):
        @pl.loop(1, parts)
        def _(k):
            fn((p + k) % parts)

    def par_copy(other, whose):
        return remote(par_send, par_recv.at[whose], par_ssem.at[other], par_rsem.at[whose], 2 * other + m, s)

    group = chip - chip % owners
    my_rows = pl.ds(core * half_rows + (chip % owners) * piece, piece)

    def slot_of(block):
        return (block - z + n - 1) % n

    def wz_copy(which, k):
        to = (z + k) % n
        slot = n - k - 1
        return remote(wv.at[which, pl.ds(to % 2 * parts, parts), my_rows, :], wf.at[which, slot, :, my_rows, :],
                      wz_ssem.at[which * (n - 1) + slot], wz_rsem.at[which * (n - 1) + slot], to, s)

    def wb_copy(other, whose):
        base = 2 * (n - 1)
        return remote(wv.at[1, :, my_rows, :], wvb.at[whose, :, my_rows, :],
                      wz_ssem.at[base + other], wz_rsem.at[base + whose], 2 * other + m, s)

    def forward_weights(which, slot):
        return wf.at[which, slot], which * (n - 1) + slot

    def backward_weights(other):
        return wvb.at[other], 2 * (n - 1) + other

    def wp_copy(view, index, k, whose):
        at = pl.ds(core * half_rows + whose * piece, piece)
        to = group + (chip + k) % owners
        return remote(view.at[:, at, :], view.at[:, at, :], wp_ssem.at[index, k], wp_rsem.at[index, whose], z, to * 2 + core)

    def wh_copy(view, index, whose):
        at = pl.ds(whose * half_rows, half_rows)
        return remote(view.at[:, at, :], view.at[:, at, :], wh_ssem.at[index], wh_rsem.at[index], z, chip * 2 + 1 - core)

    def round_chips(view, index):
        @pl.loop(1, owners)
        def _(k):
            wp_copy(view, index, k, chip % owners).start()

    def round_cores(view, index):
        @pl.loop(1, owners)
        def _(k):
            wp_copy(view, index, k, (chip + k) % owners).wait_recv()
        wh_copy(view, index, core).start()

    def round_done(view, index):
        wh_copy(view, index, 1 - core).wait_recv()

    def weights_over_z(which):
        @pl.loop(1, n)
        def _(k):
            wz_copy(which, k).start()

    def nth_block(i):
        low = jnp.minimum(z, n - 1 - z)
        turn = i % 2 * 2 - 1
        return jnp.where(i <= 2 * low, z + turn * ((i + 1) // 2), z + jnp.where(z < parts, 1, -1) * (i - low))

    def weights_round(which, order):
        @pl.loop(1, n)
        def _(i):
            slot = slot_of(order(i))
            wz_copy(which, n - 1 - slot).wait_recv()
            round_chips(*forward_weights(which, slot))

    def pair_block(i):
        return jnp.where(i < parts, m, 1 - m), (p + i % parts) % parts

    def use_order(i):
        mm, u = pair_block(i)
        return 2 * u + mm

    def row_copy(slot, side):
        if side == 0:
            to_p, to_s = jnp.where(p == 0, parts - 1, p - 1), jnp.where(p == 0, before, s)
        else:
            to_p, to_s = jnp.where(p == parts - 1, 0, p + 1), jnp.where(p == parts - 1, after, s)
        return remote(row_send.at[slot, side], row_recv.at[slot, 1 - side], row_ssem.at[slot, side],
                      row_rsem.at[slot, 1 - side], 2 * to_p + m, to_s)

    def send_rows(slot, ref):
        for side, start in ((0, 0), (1, pc - wide)):
            row_send[slot, side] = ref[:, start:start + wide, :]
            row_copy(slot, side).start()

    def take_rows(slot, ref):
        for side in range(2):
            row_copy(slot, 1 - side).wait_recv()
            ref[:, pc + side * wide:pc + (side + 1) * wide, :] = row_recv[slot, side]

    def st_copy(slot, k, whose):
        to_p, to_s = (p + k // s_count) % parts, (s + k % s_count) % s_count
        return remote(st_send.at[slot], st_recv.at[slot, whose], st_ssem.at[slot, k], st_rsem.at[slot, whose],
                      2 * to_p + m, to_s)

    me = p * s_count + s

    def send_stats(slot, values):
        for i, v in enumerate(values):
            st_send[slot, i:i + 1, :] = v

        @pl.loop(1, family)
        def _(k):
            st_copy(slot, k, me).start()
        st_recv[slot, me] = st_send[slot]

    def take_stats(slot):
        @pl.loop(1, family)
        def _(k):
            st_copy(slot, k, (p + k // s_count) % parts * s_count + (s + k % s_count) % s_count).wait_recv()
        return [st_recv[slot, k] for k in range(family)]

    strip = 8
    column = lax.broadcasted_iota(jnp.int32, (strip * wide, ch), 0) % wide

    def shift(target, first, count):
        size = count * wide
        where = column[:size]
        here = pad[pl.ds(8 + first * wide, size), :]
        left = jnp.where(where == 0, 0.0, pad[pl.ds(7 + first * wide, size), :])
        right = jnp.where(where == wide - 1, 0.0, pad[pl.ds(9 + first * wide, size), :])
        for b, v in enumerate((left, here, right)):
            target[pl.ds(first, count), :, b * ch:(b + 1) * ch] = v.astype(BF16).reshape(count, wide, ch)

    def unpack_chunk(chunk, q):
        pad[8:8 + wide, :] = chunk[0:wide, :].astype(F32)
        pad[8 + wide + pc:8 + edge + pc, :] = chunk[wide:edge, :].astype(F32)
        pad[8 + wide:8 + wide + pc, :] = dot(unpack[q], chunk[edge:edge + packed, :])

    def make_taps(chunk, q, target):
        unpack_chunk(chunk, q)
        shift(target, 0, 1)
        for i in range(part_rows // strip):
            shift(target, 1 + i * strip, strip)
        shift(target, part_rows + 1, 1)

    def from_pad(ref):
        ref[0:pc, :] = pad[8 + wide:8 + wide + pc, :]
        ref[pc:pc + wide, :] = pad[8:8 + wide, :]
        ref[pc + wide:pt, :] = pad[8 + wide + pc:8 + edge + pc, :]

    def rows_of(q):
        return pl.ds(pl.multiple_of(q * pc, pc), pc)

    def rows_around(q):
        above = jnp.where(q == 0, cells, q * pc - wide)
        below = jnp.where(q == parts - 1, cells + wide, (q + 1) * pc)
        return tuple(pl.ds(pl.multiple_of(at, wide), wide) for at in (above, below))

    def make_chunk(q, source, chunk):
        above, below = rows_around(q)
        chunk[0:wide, :] = source[above, :].astype(BF16)
        chunk[wide:edge, :] = source[below, :].astype(BF16)
        chunk[edge:edge + packed, :] = dot(pack[q], source[rows_of(q), :].astype(BF16)).astype(BF16)

    def own_part(source, target):
        above, below = rows_around(p)
        target[0:pc, :] = source[rows_of(p), :]
        target[pc:pc + wide, :] = source[above, :]
        target[pc + wide:pt, :] = source[below, :]

    def add_products(targets, value):
        for i, target in enumerate(targets):
            target[...] = target[...] + sum(
                value[a * wide:a * wide + pc, (3 * i + a) * ch:(3 * i + a + 1) * ch] for a in range(3))

    def add_conv(targets, field, views):
        lhs = field[...].reshape((part_rows + 2) * wide, 3 * ch)
        rhs = jnp.concatenate([view[3 * a * ch:3 * (a + 1) * ch, :] for view in views for a in range(3)], axis=1)
        add_products(targets, dot(lhs, rhs))

    def add_conv_back(targets, field, views):
        lhs = field[...].reshape((part_rows + 2) * wide, 3 * ch)
        rhs = []
        for view in views:
            for a in range(3):
                taps = [3 * (2 - a) + 2 - b for b in range(3)]
                rhs.append(jnp.concatenate([view[tap * ch:(tap + 1) * ch, :] for tap in taps], axis=1))
        value = lax.dot_general(lhs, jnp.concatenate(rhs, axis=0), (((1,), (1,)), ((), ())), preferred_element_type=F32)
        add_products(targets, value)

    def a_copy(j, q, sign):
        return remote(hold0.at[j, q], hold0.at[j, q], a_ssem.at[(1 - sign) // 2, j, q], a_rsem.at[j, q], z + sign, s)

    def wanted(q, sign, at):
        return inside(at) & ((2 * q + 1 >= at) if sign > 0 else (2 * q <= at))

    def pass_on(k):
        for sign in (1, -1):
            block = z - k * sign
            for q in range(parts):
                @pl.when(inside(block) & wanted(q, sign, z + sign))
                def _():
                    a_copy(block, q, sign).wait_recv()
                    a_copy(block, q, sign).start()

    def first_taps(block):
        into = taken.at[block % 2, block // 2]
        make_taps(hold0.at[block, p], p, into)

        @pl.when(block % 2 == m)
        def _():
            from_pad(masked_c.at[block // 2])
        return into

    def b_copy(ph, mm, u):
        return remote(hold1.at[ph, mm, u], hold1.at[ph, mm, u], b_ssem.at[ph, u], b_rsem.at[ph, u], twin, s)

    def pack_own(ph, fill):
        for k in range(parts):
            u = (p + k) % parts
            fill(u)
            chunk = hold1.at[ph, m, u]
            chunk[0:edge, :] = hid[u, pc:pt, :].astype(BF16)
            chunk[edge:edge + packed, :] = dot(pack[p], hid[u, 0:pc, :].astype(BF16)).astype(BF16)
            b_copy(ph, m, u).start()

    def everywhere(fn, u):
        chunked(functools.partial(fn, u), 0)
        fn(u, pc, edge, 0)

    def turn_field(main, ends, put):
        ends = ends()
        if edge < ch:
            ends = jnp.concatenate([ends, jnp.zeros((ch - edge, ch), F32)], axis=0)
        ends = ends.T
        blocks = [main(start).T for start in range(0, pc, ch)]
        for i, here in enumerate(blocks):
            left = jnp.concatenate(
                [ends[:, 0:wide] if i == 0 else blocks[i - 1][:, ch - wide:], here[:, 0:ch - wide]], axis=1)
            right = jnp.concatenate(
                [here[:, wide:], blocks[i + 1][:, 0:wide] if i + 1 < len(blocks) else ends[:, wide:edge]], axis=1)
            for a, v in enumerate((left, here, right)):
                put(a, slice(i * ch, (i + 1) * ch), v.astype(BF16))

    def turn_input():
        @pl.loop(0, parts)
        def _(q):
            around = rows_around(q)

            def put(a, at, value):
                x_t1[q, a * ch:(a + 1) * ch, at] = value
            turn_field(lambda start: masked[pl.ds(pl.multiple_of(q * pc + start, ch), ch), :],
                       lambda: jnp.concatenate([masked[at, :] for at in around], axis=0), put)

    def turn_hidden():
        for u in range(parts):
            def put(a, at, value):
                x_t2[(3 * u + a) * ch:(3 * u + a + 1) * ch, at] = value
            turn_field(lambda start: hid[u, start:start + ch, :], lambda: hid[u, pc:pt, :], put)

    def load_cotangent():
        def put(at, value):
            cot[at, :] = value
        from_flat(cot_in, put)

        def live_only(start, size, carry):
            at = pl.ds(start, size)
            cot[at, :] = cot[at, :] * mask[at, :]
            return carry
        chunked(live_only, 0, cells)
        for side, start in ((0, 0), (1, cells - wide)):
            cedge_send[side] = cot[start:start + wide, :].astype(BF16)
            cedge_copy(side).start()

    def cx_copy(other, whose):
        return remote(cot_send.at[other], cot_recv.at[whose], cx_ssem.at[other], cx_rsem.at[whose], 2 * other + m, s)

    def exchange_cotangent():
        for side in range(2):
            cedge_copy(1 - side).wait_recv()
            at = slice(cells + side * wide, cells + (side + 1) * wide)
            cot[at, :] = cedge_recv[side].astype(F32) * mask[at, :]

        def send(other):
            make_chunk(other, cot, cot_send.at[other])
            cx_copy(other, p).start()
        others(send)
        own_part(cot, cot_c.at[p])

    def take_cotangent():
        def take(other):
            cx_copy(other, other).wait_recv()
            unpack_chunk(cot_recv.at[other], p)
            from_pad(cot_c.at[other])
        others(take)

    def ret_copy(kind, other, whose):
        return remote(ret_send.at[kind, other], ret_recv.at[kind, whose],
                      ret_ssem.at[kind, other], ret_rsem.at[kind, whose], 2 * other + m, s)

    def give_back():
        def send(other):
            for kind, source in enumerate((block_c, through)):
                ret_send[kind, other] = dot(pack[p], source[other, 0:pc, :].astype(BF16)).astype(BF16)
                ret_copy(kind, other, p).start()
        others(send)
        for source, target in ((block_c, blk_n), (through, thr_n)):
            target[rows_of(p), :] = source[p, 0:pc, :]

    def take_back():
        def take(other):
            for kind, target in enumerate((blk_n, thr_n)):
                ret_copy(kind, other, other).wait_recv()
                target[rows_of(other), :] = dot(unpack[other], ret_recv[kind, other])
        others(take)
        to_flat(blk_n, out_block)

    def c_copy(unit):
        return remote(psend.at[unit], crecv.at[unit], c_ssem.at[unit], c_rsem.at[unit], z, chip * 2 + 1 - core)

    def q_copy(unit, e, whose, owner):
        return remote(hsend.at[unit, owner], qrecv.at[unit, whose], q_ssem.at[unit, e], q_rsem.at[unit, whose],
                      z, ((chip + e) % chips) * 2 + core)

    def zz_copy(u, j, whose):
        return remote(zz_send.at[u, j], zz_recv.at[whose, j], zz_ssem.at[u, j], zz_rsem.at[whose, j], 2 * u + m, s)

    def f_copy(which, j, e, owner):
        return remote(wout.at[which, j, core, owner], wout.at[which, j, core, owner],
                      f_ssem.at[which, j, e], f_rsem.at[which, j, owner], z, ((chip + e) % chips) * 2 + core)

    def h_copy(which, j, whose):
        return remote(wout.at[which, j, whose], wout.at[which, j, whose],
                      h_ssem.at[which, j], h_rsem.at[which, j], z, chip * 2 + 1 - core)

    def o_copy(which, j):
        target = (out_wg1, out_wg2)[which]
        if aligned:
            target = target.at[:, :, :, pl.ds(pl.multiple_of(j * ch, ch), ch)]
        else:
            target = target.at[j]
        return pltpu.make_async_copy(wout.at[which, j], target, o_sem.at[which, j])

    def put_part(unit, tap, value):
        start = tap * ch
        done = 0
        while done < ch:
            row = start + done
            side, o, at = row // half_rows, row % half_rows // piece, row % piece
            size = min(ch - done, piece - at)
            part[unit, side, o, at:at + size, :] = value[done:done + size, :]
            done += size

    def put_grad(unit, value):
        for a in range(3):
            for b in range(3):
                put_part(unit, 3 * a + b, value[a * ch:(a + 1) * ch, (2 - b) * ch:(3 - b) * ch])

    def centre(mm, u):
        return taken[mm, u, 1:part_rows + 1, :, :].reshape(pc, 3 * ch)

    def sum_cores(unit):
        for o in range(owners):
            psend[unit, o] = part[unit, 1 - core, o].astype(BF16)
        c_copy(unit).start()

    def sum_chips(unit):
        c_copy(unit).wait_recv()
        for o in range(owners):
            v = part[unit, core, o] + crecv[unit, o].astype(F32)
            part[unit, core, o] = v
            hsend[unit, o] = v.astype(BF16)

        @pl.loop(1, chips)
        def _(e):
            peer = (chip + e) % chips

            @pl.when(peer < owners)
            def _():
                q_copy(unit, e, chip, peer).start()

    def plane_sum(unit):
        @pl.loop(1, chips)
        def _(e):
            q_copy(unit, e, (chip + e) % chips, chip).wait_recv()
        v = part[unit, core, chip]
        for e in range(1, chips):
            v = v + qrecv[unit, (chip + e) % chips].astype(F32)
        return v

    def spread_chips(which, j, v):
        wout[which, j, core, chip] = v.astype(BF16)

        @pl.loop(1, chips)
        def _(e):
            f_copy(which, j, e, chip).start()

    def if_owner(fn):
        pl.when(chip < owners)(fn)

    def spread_first(j):
        @if_owner
        def _():
            spread_chips(0, j, plane_sum(j))

    def unit_of(u, j):
        return n + u * n + j

    def sum_planes(u, j):
        @if_owner
        def _():
            v = plane_sum(unit_of(u, j))

            @pl.when(u == p)
            def _():
                part[unit_of(u, j), core, chip] = v

            @pl.when(u != p)
            def _():
                zz_send[u, j] = v.astype(BF16)
                zz_copy(u, j, p).start()

    def spread_second(j):
        @if_owner
        def _():
            @pl.loop(1, parts)
            def _(k):
                other = (p + k) % parts
                zz_copy(other, j, other).wait_recv()
            v = part[unit_of(p, j), core, chip]
            for k in range(1, parts):
                v = v + zz_recv[(p + k) % parts, j].astype(F32)
            spread_chips(1, j, v)

    def spread_cores(which, j):
        @pl.loop(1, chips)
        def _(e):
            peer = (chip + e) % chips

            @pl.when(peer < owners)
            def _():
                f_copy(which, j, e, peer).wait_recv()
        h_copy(which, j, core).start()

    def finish(which, j):
        h_copy(which, j, 1 - core).wait_recv()
        o_copy(which, j).start()

    def fold(v):
        return jnp.sum(v.reshape(v.shape[0] // 8, 8, ch), axis=0)

    def flatten(v):
        return jnp.sum(v, axis=0, keepdims=True)

    zero = jnp.zeros((8, ch), F32)

    def local_moments():
        def count(start, size, carry):
            return carry + fold(mask_c[pl.ds(start, size), :])
        number = flatten(chunked(count, zero))
        values = [number]
        for u in range(parts):
            def sums(start, size, carry):
                at = pl.ds(start, size)
                return carry + fold(acc[u, at, :] * mask_c[at, :])
            added = flatten(chunked(sums, zero))
            middle = added / jnp.maximum(number, 1.0)

            def spread(start, size, carry):
                at = pl.ds(start, size)
                c = (acc[u, at, :] - middle) * mask_c[at, :]
                return carry + fold(c * c)
            values += [added, flatten(chunked(spread, zero))]
        return values

    def moments(got):
        number = sum(g[0:1] for g in got)
        for u in range(parts):
            mean = sum(g[1 + 2 * u:2 + 2 * u] for g in got) / number
            spread = 0.0
            for g in got:
                off = g[1 + 2 * u:2 + 2 * u] / jnp.maximum(g[0:1], 1.0) - mean
                spread = spread + (g[2 + 2 * u:3 + 2 * u] + g[0:1] * off * off)
            norm[0, u] = mean
            norm[1, u] = lax.rsqrt(spread / number + EPSILON)
        return number

    def gradient_sums(got):
        for i in range(2 * parts):
            norm[2 + i % 2, i // 2] = sum(g[i:i + 1] for g in got)

    sums_of = [acc.at[u] for u in range(parts)]

    weight_waits = [lambda which=which: [c.wait() for c in w_copies[which * n:(which + 1) * n]] for which in range(3)]
    pl.semaphore_wait(barrier, family - 1 + parts)
    weight_waits[0]()
    weights_over_z(0)

    def put_masked(at, value):
        masked[at, :] = value

    from_flat(x_in, put_masked)

    cell = lax.broadcasted_iota(jnp.int32, (cells, rows), 0)
    pick = (cell // wide == lax.broadcasted_iota(jnp.int32, (cells, rows), 1)).astype(F32).astype(BF16)
    column_of = lax.broadcasted_iota(jnp.int32, (cells, wide), 0) % wide
    picked = lax.dot_general(pick, live_in[...].astype(BF16), (((1,), (1,)), ((), ())), preferred_element_type=F32)
    picked = jnp.where(column_of == lax.broadcasted_iota(jnp.int32, (cells, wide), 1), picked, 0.0)
    mask[0:cells, :] = dot(picked.astype(BF16), jnp.ones((wide, ch), BF16))

    def load_main(start, size, carry):
        at = pl.ds(start, size)
        masked[at, :] = masked[at, :] * mask[at, :]
        return carry

    chunked(load_main, 0, cells)
    for side, start in ((0, 0), (1, cells - wide)):
        edge_send[side, 0] = masked[start:start + wide, :].astype(BF16)
        edge_send[side, 1] = mask[start:start + wide, :].astype(BF16)
    acc[...] = jnp.zeros_like(acc)
    st_send[...] = jnp.zeros_like(st_send)
    par_send[...] = jnp.zeros_like(par_send)
    for i, given in enumerate((gain1_in, shift1_in, gain2_in, shift2_in)):
        par_send[i:i + 1, :] = given[...]
    par_recv[p] = par_send[...]

    for side in range(2):
        edge_copy(side).start()
    others(lambda other: par_copy(other, p).start())

    below = lax.broadcasted_iota(jnp.int32, (pc, pc), 1) < lax.broadcasted_iota(jnp.int32, (pc, pc), 0)
    below = below.astype(F32).astype(BF16)

    @pl.loop(0, parts)
    def _(q):
        lv = mask[rows_of(q), :]
        place = jnp.where(lv > 0.0, dot(below, lv.astype(BF16)), -1.0)
        places[q] = place
        across = place.T[0:1, :]
        spot = lax.broadcasted_iota(jnp.int32, (packed, pc), 0).astype(F32)
        pack[q] = jnp.where(spot == across, 1.0, 0.0).astype(BF16)

    for side in range(2):
        edge_copy(1 - side).wait_recv()
        there = jnp.where(s > 0, 1.0, 0.0) if side == 0 else jnp.where(s < s_count - 1, 1.0, 0.0)
        at = slice(cells + side * wide, cells + (side + 1) * wide)
        masked[at, :] = edge_recv[side, 0].astype(F32) * there
        mask[at, :] = edge_recv[side, 1].astype(F32) * there

    @pl.loop(0, parts)
    def _(i):
        q = jnp.where(z < parts, parts - 1 - i, i)
        make_chunk(q, masked, hold0.at[z, q])
        for sign in (1, -1):
            @pl.when(inside(z + sign) & ((2 * q + 1 >= z + sign) if sign > 0 else (2 * q <= z + sign)))
            def _():
                a_copy(z, q, sign).start()
    weights_round(0, nth_block)

    @pl.loop(0, parts)
    def _(q):
        for start in range(0, packed, ch):
            size = min(ch, packed - start)
            spot = start + lax.broadcasted_iota(jnp.int32, (pc, size), 1)
            unpack[q, :, start:start + size] = jnp.where(
                places[q, :, :size] == spot.astype(F32), 1.0, 0.0).astype(BF16)
    own_part(mask, mask_c)

    add_conv(sums_of, first_taps(z), [wv.at[0, m * parts + u] for u in range(parts)])
    load_cotangent()
    for k in range(1, n):
        pass_on(k)
    weight_waits[1]()
    weights_over_z(1)

    @pl.loop(1, n)
    def _(i):
        block = nth_block(i)
        view, index = forward_weights(0, slot_of(block))
        round_cores(view, index)

        @pl.when(i == 1)
        def _():
            turn_input()
        passed = jnp.where(block < z, jnp.where(wanted(p, 1, z + 1), 1, 0), jnp.where(wanted(p, -1, z - 1), 1, 0))

        @pl.when(passed == 0)
        def _():
            a_copy(block, p, 1).wait_recv()
        taps = first_taps(block)
        round_done(view, index)
        add_conv(sums_of, taps, [wf.at[0, slot_of(block), u] for u in range(parts)])

    send_stats(0, local_moments())
    send_rows(0, acc)
    weights_round(1, use_order)
    exchange_cotangent()
    others(lambda other: par_copy(other, other).wait_recv())
    got = take_stats(0)
    count = moments(got)

    def params(u):
        return [par_recv[u, i:i + 1, :] for i in range(4)]

    def activate_one(u, start, size, carry):
        at = pl.ds(start, size)
        main = start is not pc
        gain, shift_by = params(u)[:2]
        nv = ((acc if main else normed1)[u, at, :] - norm[0, u]) * norm[1, u]
        normed1[u, at, :] = nv
        hid[u, at, :] = gelu_parts(nv * gain + shift_by)[0] * mask_c[at, :]
        if main:
            acc[u, at, :] = jnp.zeros((size, ch), F32)
        return carry

    def slope_one(u, start, size, carry):
        at = pl.ds(start, size)
        gain, shift_by = params(u)[:2]
        slope1[u, at, :] = gelu_parts(normed1[u, at, :] * gain + shift_by)[1] * mask_c[at, :]
        return carry

    norm1_scale = [norm[1, u] for u in range(parts)]

    take_rows(0, normed1)
    pack_own(0, functools.partial(everywhere, activate_one))
    others(lambda other: wb_copy(other, p).start())

    @pl.loop(0, 2 * parts)
    def _(i):
        mm, u = pair_block(i)
        into = taken.at[mm, u]

        slot = slot_of(2 * u + mm)
        view, index = forward_weights(1, slot)

        @pl.when(i > 0)
        def _():
            round_cores(view, index)

        @pl.when(i >= parts)
        def _():
            b_copy(0, mm, u).wait_recv()
        make_taps(hold1.at[0, mm, u], p, into)

        @pl.when(i == 0)
        def _():
            add_conv(sums_of, into, [wv.at[1, m * parts + v] for v in range(parts)])
            for v in range(parts):
                everywhere(slope_one, v)

        @pl.when(i > 0)
        def _():
            round_done(view, index)
            add_conv(sums_of, into, [wf.at[1, slot, v] for v in range(parts)])

    send_stats(1, local_moments())
    send_rows(1, acc)

    def wb_round(other):
        wb_copy(other, other).wait_recv()
        round_chips(*backward_weights(other))
    others(wb_round)
    take_cotangent()
    turn_hidden()
    moments(take_stats(1))

    def activate_two(u, start, size, source):
        at = pl.ds(start, size)
        gain, shift_by = params(u)[2:]
        nv = (source[u, at, :] - norm[0, u]) * norm[1, u]
        normed2[u, at, :] = nv
        value, slope = gelu_parts(nv * gain + shift_by + masked_c[u, at, :])
        t = cot_c[u, at, :] * slope
        through[u, at, :] = t
        return value, nv, t

    def activate_main(u, start, size, carry):
        value, nv, t = activate_two(u, start, size, acc)
        at = pl.ds(start, size)
        block_c[u, at, :] = value * mask_c[at, :]
        acc[u, at, :] = jnp.zeros((size, ch), F32)
        return carry[0] + fold(t * nv), carry[1] + fold(t)

    sums = []
    for u in range(parts):
        sums += [flatten(v) for v in chunked(functools.partial(activate_main, u), (zero, zero))]
    send_stats(2, sums)
    take_rows(1, normed2)
    for u in range(parts):
        activate_two(u, pc, edge, normed2)
    others(lambda other: round_cores(*backward_weights(other)))

    def norm_back(upstream, normed, gain_at, scale):
        def fill(u, start, size, carry):
            at = pl.ds(start, size)
            factor = params(u)[gain_at] * scale[u]
            v = upstream[u, at, :] - mask_c[at, :] * (
                norm[3, u] / count + normed[u, at, :] * (norm[2, u] / count))
            hid[u, at, :] = factor * v
            return carry
        return fill

    gradient_sums(take_stats(2))
    for u in range(parts):
        scales[0, u] = norm1_scale[u]
        scales[1, u] = norm[1, u]
    out_gain2[...], out_shift2[...] = norm[2, p], norm[3, p]

    pack_own(1, functools.partial(everywhere, norm_back(through, normed2, 2, scales.at[1])))
    give_back()

    def second_grads(mm, u):
        j = 2 * u + mm
        value = dot(x_t2[...], centre(mm, u))
        for v in range(parts):
            unit = unit_of(v, j)
            put_grad(unit, value[v * 3 * ch:(v + 1) * 3 * ch, :])
            sum_cores(unit)

    @pl.loop(0, 2 * parts)
    def _(i):
        mm, u = pair_block(i)

        @pl.when(i >= parts)
        def _():
            b_copy(1, mm, u).wait_recv()
        into = taken.at[mm, u]
        make_taps(hold1.at[1, mm, u], p, into)

        @pl.when(i == 0)
        def _():
            weight_waits[2]()
            others(lambda other: round_done(*backward_weights(other)))
        add_conv_back(sums_of, into, [wvb.at[v, mm * parts + u] for v in range(parts)])

    for side, start in ((0, 0), (1, pc - wide)):
        row_send[2, side] = acc[:, start:start + wide, :]

    def inner_main(u, start, size, carry):
        at = pl.ds(start, size)
        v = acc[u, at, :] * slope1[u, at, :]
        slope1[u, at, :] = v
        acc[u, at, :] = jnp.zeros((size, ch), F32)
        return carry[0] + fold(v * normed1[u, at, :]), carry[1] + fold(v)

    sums = []
    for u in range(parts):
        sums += [flatten(v) for v in chunked(functools.partial(inner_main, u), (zero, zero))]
    send_stats(3, sums)
    for side in range(2):
        row_copy(2, side).start()
    pl.loop(0, parts)(lambda u: second_grads(m, u))

    def by_parity(mm, fn):
        @pl.loop(0, parts * parts)
        def _(i):
            fn((p + 1 + i // parts) % parts, 2 * (i % parts) + mm)

    for side in range(2):
        row_copy(2, 1 - side).wait_recv()
        at = slice(pc + side * wide, pc + (side + 1) * wide)
        slope1[:, at, :] = row_recv[2, side] * slope1[:, at, :]
    gradient_sums(take_stats(3))
    out_gain1[...], out_shift1[...] = norm[2, p], norm[3, p]

    def ag_copy(block, q, sign):
        return remote(hold3.at[block, q], hold3.at[block, q], ag_ssem.at[(1 - sign) // 2, block, q],
                      ag_rsem.at[block, q], z + sign, s)

    fill = norm_back(slope1, normed1, 0, scales.at[0])
    for u in range(parts):
        everywhere(fill, u)
        chunk = hold3.at[z, u]
        chunk[0:edge, :] = hid[u, pc:pt, :].astype(BF16)
        chunk[edge:edge + packed, :] = dot(pack[p], hid[u, 0:pc, :].astype(BF16)).astype(BF16)
        for sign in (1, -1):
            @pl.when(inside(z + sign))
            def _():
                ag_copy(z, u, sign).start()
    pl.loop(0, parts)(lambda u: second_grads(1 - m, u))
    by_parity(m, lambda v, j: sum_chips(unit_of(v, j)))

    last_pass = jnp.maximum(jnp.where(z < n - 1, z, 0), jnp.where(z > 0, n - 1 - z, 0))

    def made_at(mm):
        return jnp.maximum(jnp.maximum(jnp.abs(mm - z), jnp.abs(2 * (parts - 1) + mm - z)), last_pass)

    def first_grad(mm, u):
        j = 2 * u + mm
        put_grad(j, sum(dot(x_t1[q], centre(2 * q + mm, u)) for q in range(parts)))
        sum_cores(j)

    first_stages = (sum_chips, spread_first, functools.partial(spread_cores, 0), functools.partial(finish, 0))

    def advance(k):
        @pl.loop(0, 2)
        def _(mm):
            made = made_at(mm)
            for age, stage in enumerate(first_stages):
                @pl.when(made + age + 1 == k)
                def _():
                    @pl.loop(0, parts)
                    def _(u):
                        stage(2 * u + mm)

    @pl.loop(0, n)
    def _(k):
        for q in range(parts):
            for sign in (1, -1):
                block = z - k * sign

                @pl.when((k > 0) & inside(block))
                def _():
                    ag_copy(block, q, sign).wait_recv()

                    @pl.when(inside(z + sign))
                    def _():
                        ag_copy(block, q, sign).start()

            @pl.loop(0, 2)
            def _(way):
                block = z - k * (1 - 2 * way)

                @pl.when(inside(block) & ((k > 0) | (way == 0)))
                def _():
                    into = taken.at[block, q]
                    make_taps(hold3.at[block, q], block // 2, into)
                    add_conv_back([acc.at[block // 2]], into, [wv.at[0, block % 2 * parts + q]])

        @pl.loop(0, 2)
        def _(mm):
            @pl.when(made_at(mm) == k)
            def _():
                @pl.loop(0, parts)
                def _(u):
                    first_grad(mm, u)
        advance(k)

        @pl.when(k == 0)
        def _():
            by_parity(1 - m, lambda v, j: sum_chips(unit_of(v, j)))

        @pl.when(k == n - 3)
        def _():
            by_parity(m, sum_planes)
            take_back()

        @pl.when(k == n - 2)
        def _():
            by_parity(1 - m, sum_planes)

        @pl.when(k == n - 1)
        def _():
            @pl.loop(0, n)
            def _(j):
                spread_second(j)

    advance(n)

    def finish_input(start, size, carry):
        at = pl.ds(start, size)
        thr_n[at, :] = (acc[start // pc, pl.ds(pl.multiple_of(start % pc, CHUNK), size), :] + thr_n[at, :]) * mask[at, :]
        return carry

    chunked(finish_input, 0, cells)
    to_flat(thr_n, out_input)

    @pl.loop(0, n)
    def _(j):
        spread_cores(1, j)
    advance(n + 1)

    @pl.loop(0, n)
    def _(j):
        finish(1, j)
    for extra in range(2, len(first_stages)):
        advance(n + extra)

    for side in range(2):
        edge_copy(side).wait_send()
        cedge_copy(side).wait_send()
        for slot in range(3):
            row_copy(slot, side).wait_send()

    def sent_to(other):
        par_copy(other, p).wait_send()
        cx_copy(other, p).wait_send()
        wb_copy(other, p).wait_send()
        for kind in range(2):
            ret_copy(kind, other, p).wait_send()

        @if_owner
        def _():
            @pl.loop(0, n)
            def _(j):
                zz_copy(other, j, p).wait_send()
    others(sent_to)

    @pl.loop(1, family)
    def _(k):
        for slot in range(4):
            st_copy(slot, k, me).wait_send()

    @pl.loop(0, parts)
    def _(u):
        for ph in range(2):
            b_copy(ph, m, u).wait_send()

    def weights_sent(view, index):
        @pl.loop(1, owners)
        def _(k):
            wp_copy(view, index, k, chip % owners).wait_send()
        wh_copy(view, index, core).wait_send()

    @pl.loop(1, n)
    def _(k):
        for which in range(2):
            wz_copy(which, k).wait_send()
            weights_sent(*forward_weights(which, n - k - 1))
    others(lambda other: weights_sent(*backward_weights(other)))

    @pl.loop(0, n)
    def _(k):
        for sign in (1, -1):
            block = z - k * sign

            @pl.when(inside(block) & inside(z + sign))
            def _():
                for q in range(parts):
                    ag_copy(block, q, sign).wait_send()

                    @pl.when(wanted(q, sign, z + sign))
                    def _():
                        a_copy(block, q, sign).wait_send()

    @pl.loop(0, n + parts * n)
    def _(unit):
        c_copy(unit).wait_send()

        @pl.loop(1, chips)
        def _(e):
            peer = (chip + e) % chips

            @pl.when(peer < owners)
            def _():
                q_copy(unit, e, chip, peer).wait_send()

    @pl.loop(0, n)
    def _(j):
        for which in range(2):
            h_copy(which, j, core).wait_send()
            o_copy(which, j).wait()

            @if_owner
            def _():
                @pl.loop(1, chips)
                def _(e):
                    f_copy(which, j, e, chip).wait_send()


def plain_kernel(n, s_count, rows, wide, ch, aligned, packed, *refs):
    (x_in, cot_in, live_in, gain1_in, shift1_in, gain2_in, shift2_in, w1_hbm, w2_hbm) = refs[:9]
    (out_block, out_input, out_wg1, out_wg2, out_gain1, out_shift1, out_gain2, out_shift2) = refs[9:17]
    (turned, wv, wf, x_t, pack, unpack, places, edge_send, edge_recv, cot_send, cot_recv, cotm, mask, masked,
     normed1, normed2, through, slope1, hid, hid2, pad, acc, hold, taken,
     part, psend, crecv, hsend, qrecv, wout, st_send, st_recv, row_send, row_recv,
     w_sem, wz_ssem, wz_rsem, wp_ssem, wp_rsem, e_ssem, e_rsem, ce_ssem, ce_rsem, ag_ssem, ag_rsem,
     st_ssem, st_rsem, row_ssem, row_rsem, c_ssem, c_rsem, q_ssem, q_rsem,
     f_ssem, f_rsem, h_ssem, h_rsem, o_sem) = refs[17:]

    z = lax.axis_index("chan")
    s = lax.axis_index("space")
    cells = rows * wide
    total = cells + 2 * wide
    band = cells // PLAIN_HALVES
    core, chip, chips = s % 2, s // 2, s_count // 2
    before, after = (s + s_count - 1) % s_count, (s + 1) % s_count
    tap_rows = 9 * ch

    barrier = pltpu.get_barrier_semaphore()

    @pl.loop(1, s_count)
    def _(k):
        pl.semaphore_signal(barrier, inc=1, device_id=(z, (s + k) % s_count), device_id_type=MESH)

    @pl.loop(1, n)
    def _(k):
        pl.semaphore_signal(barrier, inc=1, device_id=((z + k) % n, s), device_id_type=MESH)

    w_copies = []
    for which, source in enumerate((w1_hbm, w2_hbm)):
        for d in range(n):
            block = source.at[:, d * ch:(d + 1) * ch] if aligned else source.at[d]
            w_copies.append(pltpu.make_async_copy(block, wv.at[which, d], w_sem.at[which, d]))
    for copy in w_copies:
        copy.start()

    def chunked(fn, init, first=0, count=cells):
        def step(i, carry):
            return fn(pl.multiple_of(first + i * CHUNK, CHUNK), CHUNK, carry)
        return lax.fori_loop(0, count // CHUNK, step, init, unroll=UNROLL)

    lanes = 128
    tiles = ch * wide // lanes

    def from_flat(flat, put):
        for i in range(tiles):
            turned[i * lanes:(i + 1) * lanes, 0:rows] = flat[:, i * lanes:(i + 1) * lanes].astype(F32).T
        for w in range(wide):
            put(pl.ds(w, rows, stride=wide), turned[pl.ds(w, ch, stride=wide), 0:rows].T)

    def to_flat(source, flat):
        for w in range(wide):
            turned[pl.ds(w, ch, stride=wide), 0:rows] = source[pl.ds(w, rows, stride=wide), :].T
        for i in range(tiles):
            flat[:, i * lanes:(i + 1) * lanes] = turned[i * lanes:(i + 1) * lanes, 0:rows].T.astype(flat.dtype)

    def put_masked(at, value):
        masked[at, :] = value

    from_flat(x_in, put_masked)

    cell = lax.broadcasted_iota(jnp.int32, (cells, rows), 0)
    pick = (cell // wide == lax.broadcasted_iota(jnp.int32, (cells, rows), 1)).astype(F32).astype(BF16)
    column_of = lax.broadcasted_iota(jnp.int32, (cells, wide), 0) % wide
    picked = lax.dot_general(pick, live_in[...].astype(BF16), (((1,), (1,)), ((), ())), preferred_element_type=F32)
    picked = jnp.where(column_of == lax.broadcasted_iota(jnp.int32, (cells, wide), 1), picked, 0.0)
    mask[0:cells, :] = dot(picked.astype(BF16), jnp.ones((wide, ch), BF16))

    def load_main(start, size, carry):
        at = pl.ds(start, size)
        lv = mask[at, :]
        masked[at, :] = masked[at, :] * lv
        return carry

    chunked(load_main, 0)
    for side, start in ((0, 0), (1, cells - wide)):
        edge_send[side, 0] = masked[start:start + wide, :].astype(BF16)
        edge_send[side, 1] = mask[start:start + wide, :].astype(BF16)

    acc[...] = jnp.zeros_like(acc)
    st_send[...] = jnp.zeros_like(st_send)

    pl.semaphore_wait(barrier, s_count - 1 + n - 1)

    def edge_copy(side):
        return pltpu.make_async_remote_copy(
            src_ref=edge_send.at[side], dst_ref=edge_recv.at[1 - side],
            send_sem=e_ssem.at[side], recv_sem=e_rsem.at[1 - side],
            device_id=(z, before if side == 0 else after), device_id_type=MESH)

    for side in range(2):
        edge_copy(side).start()

    def cot_copy(side):
        return pltpu.make_async_remote_copy(
            src_ref=cot_send.at[side], dst_ref=cot_recv.at[1 - side],
            send_sem=ce_ssem.at[side], recv_sem=ce_rsem.at[1 - side],
            device_id=(z, before if side == 0 else after), device_id_type=MESH)

    def load_cotangent():
        def put(at, value):
            cotm[at, :] = value
        from_flat(cot_in, put)

        def live_only(start, size, carry):
            at = pl.ds(start, size)
            cotm[at, :] = cotm[at, :] * mask[at, :]
            return carry
        chunked(live_only, 0)
        for side, start in ((0, 0), (1, cells - wide)):
            cot_send[side] = cotm[start:start + wide, :].astype(BF16)
            cot_copy(side).start()

    def take_cotangent():
        for side in range(2):
            cot_copy(1 - side).wait_recv()
            at = slice(cells + side * wide, cells + (side + 1) * wide)
            cotm[at, :] = cot_recv[side].astype(F32) * mask[at, :]

    w_parts = math.gcd(tap_rows // 16, s_count)
    w_rows = tap_rows // w_parts
    w_mine = s % w_parts
    w_group = s - w_mine

    def wz_copy(which, k):
        at = pl.ds(w_mine * w_rows, w_rows)
        slot = n - k - 1
        return pltpu.make_async_remote_copy(
            src_ref=wv.at[which, (z + k) % n, at, :], dst_ref=wf.at[which, slot, at, :],
            send_sem=wz_ssem.at[which, slot], recv_sem=wz_rsem.at[which, slot],
            device_id=((z + k) % n, s), device_id_type=MESH)

    def wp_copy(which, slot, k, whose):
        at = pl.ds(whose * w_rows, w_rows)
        return pltpu.make_async_remote_copy(
            src_ref=wf.at[which, slot, at, :], dst_ref=wf.at[which, slot, at, :],
            send_sem=wp_ssem.at[which, slot, k], recv_sem=wp_rsem.at[which, slot, whose],
            device_id=(z, w_group + (w_mine + k) % w_parts), device_id_type=MESH)

    def weights_over_z(which):
        for copy in w_copies[which * n:(which + 1) * n]:
            copy.wait()

        @pl.loop(1, n)
        def _(k):
            wz_copy(which, k).start()

    def slot_of(block):
        return (block - z + n - 1) % n

    def weights_round(which):
        @pl.loop(1, n)
        def _(distance):
            for sign in (1, -1):
                block = z - distance * sign

                @pl.when((block >= 0) & (block < n))
                def _():
                    slot = slot_of(block)
                    wz_copy(which, n - 1 - slot).wait_recv()

                    @pl.loop(1, w_parts)
                    def _(k):
                        wp_copy(which, slot, k, w_mine).start()

    def weights_arrived(which, slot):
        @pl.loop(1, w_parts)
        def _(k):
            wp_copy(which, slot, k, (w_mine + k) % w_parts).wait_recv()

    def row_copy(slot, side):
        return pltpu.make_async_remote_copy(
            src_ref=row_send.at[slot, side], dst_ref=row_recv.at[slot, 1 - side],
            send_sem=row_ssem.at[slot, side], recv_sem=row_rsem.at[slot, 1 - side],
            device_id=(z, before if side == 0 else after), device_id_type=MESH)

    def send_rows(slot, ref):
        for side, start in ((0, 0), (1, cells - wide)):
            row_send[slot, side] = ref[start:start + wide, :]
            row_copy(slot, side).start()

    def take_rows(slot, ref):
        for side in range(2):
            row_copy(slot, 1 - side).wait_recv()
            ref[cells + side * wide:cells + (side + 1) * wide, :] = row_recv[slot, side]

    def st_copy(slot, k, whose):
        return pltpu.make_async_remote_copy(
            src_ref=st_send.at[slot], dst_ref=st_recv.at[slot, whose],
            send_sem=st_ssem.at[slot, k], recv_sem=st_rsem.at[slot, whose],
            device_id=(z, (s + k) % s_count), device_id_type=MESH)

    def send_stats(slot, values):
        for i, v in enumerate(values):
            st_send[slot, i:i + 1, :] = v
        for k in range(1, s_count):
            st_copy(slot, k, s).start()
        st_recv[slot, s] = st_send[slot]

    def take_stats(slot):
        for k in range(1, s_count):
            st_copy(slot, k, (s + k) % s_count).wait_recv()

    strip = 8
    column = lax.broadcasted_iota(jnp.int32, (strip * wide, ch), 0) % wide

    def shift(target, first, count):
        size = count * wide
        where = column[:size]
        here = pad[pl.ds(8 + first * wide, size), :]
        left = jnp.where(where == 0, 0.0, pad[pl.ds(7 + first * wide, size), :])
        right = jnp.where(where == wide - 1, 0.0, pad[pl.ds(9 + first * wide, size), :])
        for b, v in enumerate((left, here, right)):
            target[pl.ds(first, count), :, b * ch:(b + 1) * ch] = v.astype(BF16).reshape(count, wide, ch)

    edge = 2 * wide
    ag_rows = ((0, edge + packed), (edge + packed, packed))
    band_rows = rows // PLAIN_HALVES

    def unpack_half(ph, block, q, target):
        if q == 0:
            pad[8:8 + wide, :] = hold[ph, block, 0:wide, :].astype(F32)
            pad[8 + wide + cells:8 + 2 * wide + cells, :] = hold[ph, block, wide:edge, :].astype(F32)
            shift(target, 0, 1)
            shift(target, rows + 1, 1)
        pad[8 + wide + q * band:8 + wide + (q + 1) * band, :] = dot(
            unpack[q], hold[ph, block, edge + q * packed:edge + (q + 1) * packed, :])

        for i in range(band_rows // strip):
            shift(target, 1 + q * band_rows + i * strip, strip)

    def add_conv(q, field, taps, turned_taps=None):
        first, last = (0, band_rows - 1) if q == 0 else (band_rows - 1, rows)
        count = last - first
        lhs = field[first:last + 2, :, :].reshape((count + 2) * wide, 3 * ch)
        if turned_taps is None:
            value = dot(lhs, jnp.concatenate([taps(a) for a in range(3)], axis=1))
        else:
            rhs = jnp.concatenate([
                jnp.concatenate([turned_taps(3 * (2 - a) + 2 - b) for b in range(3)], axis=1) for a in range(3)], axis=0)
            value = lax.dot_general(lhs, rhs, (((1,), (1,)), ((), ())), preferred_element_type=F32)
        at = pl.ds(first * wide, count * wide)
        acc[at, :] = acc[at, :] + sum(
            value[a * wide:(a + count) * wide, a * ch:(a + 1) * ch] for a in range(3))

    def ag_copy(ph, block, q, sign):
        at = pl.ds(*ag_rows[q])
        return pltpu.make_async_remote_copy(
            src_ref=hold.at[ph, block, at, :], dst_ref=hold.at[ph, block, at, :],
            send_sem=ag_ssem.at[ph, (1 - sign) // 2, block, q], recv_sem=ag_rsem.at[ph, block, q],
            device_id=(z + sign, s), device_id_type=MESH)

    def pack_field(ph, source, fill=None, first=None):
        if fill is not None:
            fill(cells, edge, 0)
        hold[ph, z, 0:edge, :] = source[cells:cells + edge, :].astype(BF16)
        for q in range(PLAIN_HALVES):
            if first is not None:
                first(q)
            if fill is not None:
                chunked(fill, 0, q * band, band)
            hold[ph, z, edge + q * packed:edge + (q + 1) * packed, :] = dot(
                pack[q], source[q * band:(q + 1) * band, :].astype(BF16)).astype(BF16)
            for sign in (1, -1):
                @pl.when((z + sign >= 0) & (z + sign < n))
                def _():
                    ag_copy(ph, z, q, sign).start()

    def inside(slice_at):
        return (slice_at >= 0) & (slice_at < n)

    def take_and_pass(ph, k, q, sign, passes=True, takes=True):
        block = z - k * sign

        @pl.when((k > 0) & inside(block))
        def _():
            if passes and takes:
                ag_copy(ph, block, q, sign).wait_recv()

            @pl.when(inside(z + sign))
            def _():
                if passes:
                    if not takes:
                        ag_copy(ph, block, q, sign).wait_recv()
                    ag_copy(ph, block, q, sign).start()

            if not passes:
                @pl.when(jnp.logical_not(inside(z + sign)))
                def _():
                    ag_copy(ph, block, q, sign).wait_recv()

    near = jnp.where(z < n - n // 2, 1, 0)

    def consume_way(k, q, way, consume):
        block = z - k * (1 - 2 * way)

        @pl.when((k >= 0) & (k < n) & inside(block) & ((k > 0) | (way == near)))
        def _():
            consume(k, block, q)

    def take_both(ph, k, q, **how):
        @pl.loop(0, 2)
        def _(i):
            way = (near + i) % 2
            take_and_pass(ph, k, q, 1 - 2 * way, **how)

    def gather(ph, consume, each):
        @pl.loop(0, n)
        def _(k):
            for q in range(PLAIN_HALVES):
                take_both(ph, k, q)
                if q:
                    consume_way(k, q - 1, 1 - near, consume)
                else:
                    consume_way(k - 1, PLAIN_HALVES - 1, 1 - near, consume)
                consume_way(k, q, near, consume)
            each(k)

    def gather_passing_first(ph, consume, each):
        @pl.loop(0, n)
        def _(k):
            @pl.when(k == 1)
            def _():
                @pl.loop(1, n)
                def _(ahead):
                    for q in range(PLAIN_HALVES):
                        take_both(ph, ahead, q, takes=False)
            for q in range(PLAIN_HALVES):
                take_both(ph, k, q, passes=False)

                @pl.loop(0, 2)
                def _(i):
                    consume_way(k, q, (near + i) % 2, consume)
            each(k)

    last_pass = jnp.maximum(jnp.where(z < n - 1, z, 0), jnp.where(z > 0, n - 1 - z, 0))

    def forward(ph, field):
        def consume(k, block, q):
            into = taken.at[block]
            unpack_half(ph, block, q, into)

            @pl.when(k == 0)
            def _():
                add_conv(q, into, lambda a: wv[ph, z, 3 * a * ch:3 * (a + 1) * ch, :])

            @pl.when(k > 0)
            def _():
                slot = slot_of(block)
                if q == 0:
                    weights_arrived(ph, slot)
                add_conv(q, into, lambda a: wf[ph, slot, 3 * a * ch:3 * (a + 1) * ch, :])

        def each(k):
            if ph == 0:
                @pl.when(k == 0)
                def _():
                    weights_round(0)

                @pl.when(k == 1)
                def _():
                    weights_over_z(1)

            @pl.when(k == last_pass)
            def _():
                turn_field(ph, field)
                if ph == 0:
                    load_cotangent()
        (gather if ph else gather_passing_first)(ph, consume, each)

    def turn_field(ph, field):
        main = [field[start:start + ch, :].T for start in range(0, cells, ch)]
        ends = field[cells:cells + edge, :]
        if edge < ch:
            ends = jnp.concatenate([ends, jnp.zeros((ch - edge, ch), F32)], axis=0)
        ends = ends.T
        for i, here in enumerate(main):
            left = jnp.concatenate(
                [ends[:, 0:wide] if i == 0 else main[i - 1][:, ch - wide:], here[:, 0:ch - wide]], axis=1)
            right = jnp.concatenate(
                [here[:, wide:], main[i + 1][:, 0:wide] if i + 1 < len(main) else ends[:, wide:edge]], axis=1)
            for a, v in enumerate((left, here, right)):
                x_t[ph, a * ch:(a + 1) * ch, i * ch:(i + 1) * ch] = v.astype(BF16)

    half_rows = tap_rows // 2
    owners = math.gcd(half_rows // 16, chips)
    piece = half_rows // owners

    def c_copy(ph, j):
        return pltpu.make_async_remote_copy(
            src_ref=psend.at[ph, j], dst_ref=crecv.at[ph, j],
            send_sem=c_ssem.at[ph, j], recv_sem=c_rsem.at[ph, j],
            device_id=(z, chip * 2 + 1 - core), device_id_type=MESH)

    def q_copy(ph, j, e, whose, owner):
        return pltpu.make_async_remote_copy(
            src_ref=hsend.at[ph, j, owner], dst_ref=qrecv.at[ph, j, whose],
            send_sem=q_ssem.at[ph, j, e], recv_sem=q_rsem.at[ph, j, whose],
            device_id=(z, ((chip + e) % chips) * 2 + core), device_id_type=MESH)

    def f_copy(ph, j, e, owner):
        return pltpu.make_async_remote_copy(
            src_ref=wout.at[ph, j, core, owner], dst_ref=wout.at[ph, j, core, owner],
            send_sem=f_ssem.at[ph, j, e], recv_sem=f_rsem.at[ph, j, owner],
            device_id=(z, ((chip + e) % chips) * 2 + core), device_id_type=MESH)

    def h_copy(ph, j, whose):
        return pltpu.make_async_remote_copy(
            src_ref=wout.at[ph, j, whose], dst_ref=wout.at[ph, j, whose],
            send_sem=h_ssem.at[ph, j], recv_sem=h_rsem.at[ph, j],
            device_id=(z, chip * 2 + 1 - core), device_id_type=MESH)

    def o_copy(ph, j):
        target = (out_wg1, out_wg2)[ph]
        if aligned:
            target = target.at[:, :, :, pl.ds(pl.multiple_of(j * ch, ch), ch)]
        else:
            target = target.at[j]
        return pltpu.make_async_copy(wout.at[ph, j], target, o_sem.at[ph, j])

    def sum_cores(ph, j):
        for o in range(owners):
            psend[ph, j, o] = part[ph, j, 1 - core, o].astype(BF16)
        c_copy(ph, j).start()

    def sum_chips(ph, j):
        c_copy(ph, j).wait_recv()
        for o in range(owners):
            v = part[ph, j, core, o] + crecv[ph, j, o].astype(F32)
            part[ph, j, core, o] = v
            hsend[ph, j, o] = v.astype(BF16)

        @pl.loop(1, chips)
        def _(e):
            peer = (chip + e) % chips

            @pl.when(peer < owners)
            def _():
                q_copy(ph, j, e, chip, peer).start()

    def spread_chips(ph, j):
        @pl.when(chip < owners)
        def _():
            @pl.loop(1, chips)
            def _(e):
                q_copy(ph, j, e, (chip + e) % chips, chip).wait_recv()
            v = part[ph, j, core, chip]
            for e in range(1, chips):
                v = v + qrecv[ph, j, (chip + e) % chips].astype(F32)
            wout[ph, j, core, chip] = v.astype(BF16)

            @pl.loop(1, chips)
            def _(e):
                f_copy(ph, j, e, chip).start()

    def spread_cores(ph, j):
        @pl.loop(1, chips)
        def _(e):
            peer = (chip + e) % chips

            @pl.when(peer < owners)
            def _():
                f_copy(ph, j, e, peer).wait_recv()
        h_copy(ph, j, core).start()

    def finish(ph, j):
        h_copy(ph, j, 1 - core).wait_recv()
        o_copy(ph, j).start()

    def put_part(ph, j, tap, value):
        start = tap * ch
        done = 0
        while done < ch:
            row = start + done
            side, o, at = row // half_rows, row % half_rows // piece, row % piece
            size = min(ch - done, piece - at)
            part[ph, j, side, o, at:at + size, :] = value[done:done + size, :]
            done += size

    stages = (sum_cores, sum_chips, spread_chips, spread_cores, finish)

    def of_step(k, fn):
        @pl.loop(0, 2)
        def _(way):
            block = z - k * (1 - 2 * way)

            @pl.when((k >= 0) & (k < n) & inside(block) & ((k > 0) | (way == 0)))
            def _():
                fn(block)

    passing = last_pass > 0

    def made_at(step):
        first = jnp.where(passing & (step > 0), jnp.where(step == last_pass, 1, step + 1), step)
        return first, step + 1

    def advance(ph, k):
        for age in range(1, len(stages)):
            step = k - age

            @pl.when((step >= 0) & (step < n))
            def _():
                @pl.loop(*made_at(step))
                def _(made):
                    of_step(made, functools.partial(stages[age], ph))

    def advance_all(ph, age):
        @pl.loop(0, n)
        def _(j):
            stages[age](ph, j)

    def field_grad(ph, block):
        grad = taken[block, 1:rows + 1, :, :].reshape(cells, 3 * ch)
        value = dot(x_t[ph], grad)
        for a in range(3):
            for b in range(3):
                put_part(ph, block, 3 * a + b, value[a * ch:(a + 1) * ch, (2 - b) * ch:(3 - b) * ch])

    def make_grad(ph, block):
        field_grad(ph, block)
        sum_cores(ph, block)

    def backward(ph):
        last = ph == 0

        def consume(k, block, q):
            into = taken.at[block]
            unpack_half(2 + ph, block, q, into)
            if last and q == PLAIN_HALVES - 1:
                @pl.when((k == 0) | (k >= last_pass))
                def _():
                    make_grad(ph, block)
            add_conv(q, into, None, lambda t: wv[ph, block, t * ch:(t + 1) * ch, :])

        def each(k):
            first, end = made_at(k)
            if last:
                @pl.loop(first, end - 1)
                def _(step):
                    of_step(step, functools.partial(make_grad, ph))
                advance(ph, k)
                for age in range(2, len(stages)):
                    @pl.when(k == age - 2)
                    def _():
                        advance_all(1, age)
            else:
                @pl.loop(first, jnp.where(passing | (k < n - 1), end, first))
                def _(step):
                    of_step(step, functools.partial(make_grad, ph))

                @pl.when(k == last_pass)
                def _():
                    to_flat(hid2, out_block)
        gather(2 + ph, consume, each)

    def fold(v):
        return jnp.sum(v.reshape(v.shape[0] // 8, 8, ch), axis=0)

    def flatten(v):
        return jnp.sum(v, axis=0, keepdims=True)

    zero = jnp.zeros((8, ch), F32)

    def local_moments(ref):
        def sums(start, size, carry):
            at = pl.ds(start, size)
            m = mask[at, :]
            return carry[0] + fold(ref[at, :] * m), carry[1] + fold(m)
        added, number = (flatten(v) for v in chunked(sums, (zero, zero)))
        middle = added / jnp.maximum(number, 1.0)

        def spread(start, size, carry):
            at = pl.ds(start, size)
            c = (ref[at, :] - middle) * mask[at, :]
            return carry + fold(c * c)
        return added, number, flatten(chunked(spread, zero))

    def moments(slot):
        take_stats(slot)
        got = [st_recv[slot, k] for k in range(s_count)]
        added = sum(g[0:1] for g in got)
        number = sum(g[1:2] for g in got)
        mean = added / number
        spread = 0.0
        for g in got:
            off = g[0:1] / jnp.maximum(g[1:2], 1.0) - mean
            spread = spread + (g[2:3] + g[1:2] * off * off)
        return mean, lax.rsqrt(spread / number + EPSILON), number

    def everywhere(fn):
        chunked(fn, 0)
        fn(cells, 2 * wide, 0)

    gain1, shift1, gain2, shift2 = (r[...] for r in (gain1_in, shift1_in, gain2_in, shift2_in))

    weights_over_z(0)

    below = lax.broadcasted_iota(jnp.int32, (band, band), 1) < lax.broadcasted_iota(jnp.int32, (band, band), 0)
    below = below.astype(F32).astype(BF16)

    def make_pack(h):
        lv = mask[h * band:(h + 1) * band, :]
        place = jnp.where(lv > 0.0, dot(below, lv.astype(BF16)), -1.0)
        places[h] = place
        across = place.T[0:1, :]
        spot = lax.broadcasted_iota(jnp.int32, (packed, band), 0).astype(F32)
        pack[h] = jnp.where(spot == across, 1.0, 0.0).astype(BF16)

    def make_unpack(h):
        for start in range(0, packed, ch):
            size = min(ch, packed - start)
            spot = start + lax.broadcasted_iota(jnp.int32, (band, size), 1)
            unpack[h, :, start:start + size] = jnp.where(
                places[h, :, :size] == spot.astype(F32), 1.0, 0.0).astype(BF16)

    for side in range(2):
        edge_copy(1 - side).wait_recv()
        there = jnp.where(s > 0, 1.0, 0.0) if side == 0 else jnp.where(s < s_count - 1, 1.0, 0.0)
        at = slice(cells + side * wide, cells + (side + 1) * wide)
        masked[at, :] = edge_recv[side, 0].astype(F32) * there
        mask[at, :] = edge_recv[side, 1].astype(F32) * there

    pack_field(0, masked, first=make_pack)
    for h in range(PLAIN_HALVES):
        make_unpack(h)
    forward(0, masked)
    send_rows(0, acc)
    send_stats(0, local_moments(acc))
    weights_round(1)
    mean1, scale1, count = moments(0)

    def activate_one(start, size, carry):
        at = pl.ds(start, size)
        main = start is not cells
        nv = ((acc if main else normed1)[at, :] - mean1) * scale1
        normed1[at, :] = nv
        hid[at, :] = gelu_parts(nv * gain1 + shift1)[0] * mask[at, :]
        if main:
            acc[at, :] = jnp.zeros((size, ch), F32)
        return carry

    def slope_one(start, size, carry):
        at = pl.ds(start, size)
        slope1[at, :] = gelu_parts(normed1[at, :] * gain1 + shift1)[1] * mask[at, :]
        return carry

    take_rows(0, normed1)
    pack_field(1, hid, activate_one)
    everywhere(slope_one)
    forward(1, hid)
    send_rows(1, acc)
    send_stats(1, local_moments(acc))
    mean2, scale2, _ = moments(1)

    def activate_two(source, start, size):
        at = pl.ds(start, size)
        nv = (source[at, :] - mean2) * scale2
        normed2[at, :] = nv
        value, slope = gelu_parts(nv * gain2 + shift2 + masked[at, :])
        t = cotm[at, :] * slope
        through[at, :] = t
        return value, nv, t

    def activate_main(start, size, carry):
        value, nv, t = activate_two(acc, start, size)
        at = pl.ds(start, size)
        hid2[at, :] = value * mask[at, :]
        acc[at, :] = jnp.zeros((size, ch), F32)
        return carry[0] + fold(t * nv), carry[1] + fold(t)

    send_stats(2, [flatten(v) for v in chunked(activate_main, (zero, zero))])
    take_rows(1, normed2)
    take_cotangent()
    activate_two(normed2, cells, edge)

    def gradient_sums(slot):
        take_stats(slot)
        got = [st_recv[slot, k] for k in range(s_count)]
        return sum(g[0:1] for g in got), sum(g[1:2] for g in got)

    def norm_back(upstream, normed, gain, scale, sums):
        gain_grad, shift_grad = sums
        factor = gain * scale
        level, tilt = shift_grad / count, gain_grad / count

        def fill(start, size, carry):
            at = pl.ds(start, size)
            v = upstream[at, :] - mask[at, :] * (level + normed[at, :] * tilt)
            hid[at, :] = factor * v
            return carry
        return fill

    sums2 = gradient_sums(2)
    pack_field(3, hid, norm_back(through, normed2, gain2, scale2, sums2))
    backward(1)

    send_rows(2, acc)

    def inner_main(start, size, carry):
        at = pl.ds(start, size)
        v = acc[at, :] * slope1[at, :]
        slope1[at, :] = v
        acc[at, :] = jnp.zeros((size, ch), F32)
        return carry[0] + fold(v * normed1[at, :]), carry[1] + fold(v)

    send_stats(3, [flatten(v) for v in chunked(inner_main, (zero, zero))])

    @pl.when(jnp.logical_not(passing))
    def _():
        of_step(n - 1, functools.partial(make_grad, 1))
    for side in range(2):
        row_copy(2, 1 - side).wait_recv()
        at = slice(cells + side * wide, cells + (side + 1) * wide)
        slope1[at, :] = row_recv[2, side] * slope1[at, :]
    sums1 = gradient_sums(3)
    pack_field(2, hid, norm_back(slope1, normed1, gain1, scale1, sums1))
    advance_all(1, 1)
    backward(0)
    advance(0, n)

    def finish_input(start, size, carry):
        at = pl.ds(start, size)
        acc[at, :] = (acc[at, :] + through[at, :]) * mask[at, :]
        return carry

    chunked(finish_input, 0)
    to_flat(acc, out_input)
    out_gain1[...], out_shift1[...] = sums1
    out_gain2[...], out_shift2[...] = sums2
    for extra in range(1, len(stages) - 1):
        advance(0, n + extra)

    for side in range(2):
        edge_copy(side).wait_send()
        cot_copy(side).wait_send()
        for slot in range(3):
            row_copy(slot, side).wait_send()

    @pl.loop(1, s_count)
    def _(k):
        for slot in range(4):
            st_copy(slot, k, s).wait_send()

    @pl.loop(1, n)
    def _(k):
        for which in range(2):
            wz_copy(which, k).wait_send()

    @pl.loop(1, w_parts)
    def _(k):
        for which in range(2):
            for slot in range(n - 1):
                wp_copy(which, slot, k, w_mine).wait_send()

    @pl.loop(0, n)
    def _(k):
        for sign in (1, -1):
            block = z - k * sign

            @pl.when((block >= 0) & (block < n) & (z + sign >= 0) & (z + sign < n))
            def _():
                for ph in range(4):
                    for q in range(PLAIN_HALVES):
                        ag_copy(ph, block, q, sign).wait_send()

    @pl.loop(0, n)
    def _(j):
        for ph in range(2):
            c_copy(ph, j).wait_send()
            h_copy(ph, j, core).wait_send()
            o_copy(ph, j).wait()

            @pl.loop(1, chips)
            def _(e):
                peer = (chip + e) % chips

                @pl.when(peer < owners)
                def _():
                    q_copy(ph, j, e, chip, peer).wait_send()

                @pl.when(chip < owners)
                def _():
                    f_copy(ph, j, e, chip).wait_send()


def finish_kernel(count, *refs):
    ins, outs = refs[:count], refs[count:2 * count]
    narrow, wide, in_sem, out_sem, take_sem, give_sem = refs[2 * count:2 * count + 6]
    held = refs[2 * count + 6:]
    rows = narrow.shape[1] // FINISH_PARTS
    parts = [(w, i, pl.ds(i * rows, rows)) for i in range(FINISH_PARTS) for w in range(2)]
    loads = [pltpu.make_async_copy(ins[w].at[at, :], narrow.at[w, at, :], in_sem.at[w, i]) for w, i, at in parts]
    stores = [pltpu.make_async_copy(wide.at[w, at, :], outs[w].at[at, :], out_sem.at[w, i]) for w, i, at in parts]
    takes = [pltpu.make_async_copy(ins[2 + k], v, take_sem.at[k]) for k, v in enumerate(held)]
    gives = [pltpu.make_async_copy(v, outs[2 + k], give_sem.at[k]) for k, v in enumerate(held)]
    for copy in loads + takes:
        copy.start()
    for load, store, (w, i, at) in zip(loads, stores, parts):
        load.wait()
        wide[w, at, :] = narrow[w, at, :].astype(F32)
        store.start()
    for take, give in zip(takes, gives):
        take.wait()
        give.start()
    for copy in stores + gives:
        copy.wait()


def block_scratch(n, s_count, rows, wide, ch):
    cells = rows * wide
    total = cells + 2 * wide
    parts = n // 2
    part_rows = rows // parts
    pc = part_rows * wide
    pt = pc + 2 * wide
    packed = packed_rows(part_rows, wide)
    chunk = 2 * wide + packed
    chips = s_count // 2
    tap_rows = 9 * ch
    half_rows = tap_rows // 2
    owners = math.gcd(half_rows // 16, chips)
    piece = half_rows // owners
    units = n + parts * n
    family = parts * s_count
    st_rows = -(-(1 + 2 * parts) // 8) * 8

    sem = pltpu.SemaphoreType.DMA
    field = pltpu.VMEM((parts, pt, ch), F32)
    whole_field = pltpu.VMEM((total, ch), F32)
    weight_sets = 2 * (n - 1) + parts
    return [
        pltpu.VMEM((ch * wide, 128), F32),
        pltpu.VMEM((2, n, tap_rows, ch), BF16),
        pltpu.VMEM((2, n - 1, parts, tap_rows, ch), BF16),
        pltpu.VMEM((parts, n, tap_rows, ch), BF16),
        pltpu.VMEM((parts, 3 * ch, pc), BF16),
        pltpu.VMEM((parts * 3 * ch, pc), BF16),
        pltpu.VMEM((parts, packed, pc), BF16),
        pltpu.VMEM((parts, pc, packed), BF16),
        pltpu.VMEM((parts, pc, ch), F32),
        whole_field, whole_field, whole_field,
        pltpu.VMEM((2, 2, wide, ch), BF16),
        pltpu.VMEM((2, 2, wide, ch), BF16),
        pltpu.VMEM((2, wide, ch), BF16),
        pltpu.VMEM((2, wide, ch), BF16),
        pltpu.VMEM((8, ch), F32),
        pltpu.VMEM((parts, 8, ch), F32),
        pltpu.VMEM((pt, ch), F32),
        field, field, field, field, field, field, field, field,
        pltpu.VMEM((pt + 16, ch), F32),
        pltpu.VMEM((parts, pc, ch), F32),
        pltpu.VMEM((n, parts, chunk, ch), BF16),
        pltpu.VMEM((2, 2, parts, chunk, ch), BF16),
        pltpu.VMEM((n, parts, chunk, ch), BF16),
        pltpu.VMEM((n, parts, part_rows + 2, wide, 3 * ch), BF16),
        pltpu.VMEM((parts, chunk, ch), BF16),
        pltpu.VMEM((parts, chunk, ch), BF16),
        pltpu.VMEM((2, parts, packed, ch), BF16),
        pltpu.VMEM((2, parts, packed, ch), BF16),
        pltpu.VMEM((cells, ch), F32),
        pltpu.VMEM((cells, ch), F32),
        pltpu.VMEM((units, 2, owners, piece, ch), F32),
        pltpu.VMEM((units, owners, piece, ch), BF16),
        pltpu.VMEM((units, owners, piece, ch), BF16),
        pltpu.VMEM((units, owners, piece, ch), BF16),
        pltpu.VMEM((units, chips, piece, ch), BF16),
        pltpu.VMEM((parts, n, piece, ch), BF16),
        pltpu.VMEM((parts, n, piece, ch), BF16),
        pltpu.VMEM((2, n, 2, owners, piece, ch), BF16),
        pltpu.VMEM((4, st_rows, ch), F32),
        pltpu.VMEM((4, family, st_rows, ch), F32),
        pltpu.VMEM((3, 2, parts, wide, ch), F32),
        pltpu.VMEM((3, 2, parts, wide, ch), F32),
        pltpu.VMEM((4, parts, 1, ch), F32),
        pltpu.VMEM((2, parts, 1, ch), F32),
        sem((3, n)),
        sem((weight_sets,)), sem((weight_sets,)),
        sem((weight_sets, owners)), sem((weight_sets, owners)),
        sem((weight_sets,)), sem((weight_sets,)),
        sem((2,)), sem((2,)),
        sem((2,)), sem((2,)),
        sem((parts,)), sem((parts,)),
        sem((2, n, parts)), sem((n, parts)),
        sem((2, parts)), sem((2, parts)),
        sem((2, n, parts)), sem((n, parts)),
        sem((parts,)), sem((parts,)),
        sem((2, parts)), sem((2, parts)),
        sem((4, family)), sem((4, family)),
        sem((3, 2)), sem((3, 2)),
        sem((units,)), sem((units,)),
        sem((units, chips)), sem((units, chips)),
        sem((2, n, chips)), sem((2, n, chips)),
        sem((2, n)), sem((2, n)),
        sem((parts, n)), sem((parts, n)),
        sem((2, n)),
    ]


def plain_scratch(n, s_count, rows, wide, ch):
    cells = rows * wide
    total = cells + 2 * wide
    packed = packed_rows(rows // PLAIN_HALVES, wide)
    chips = s_count // 2
    tap_rows = 9 * ch
    half_rows = tap_rows // 2
    owners = math.gcd(half_rows // 16, chips)
    piece = half_rows // owners
    sem = pltpu.SemaphoreType.DMA
    field = pltpu.VMEM((total, ch), F32)
    return [
        pltpu.VMEM((ch * wide, 128), F32),
        pltpu.VMEM((2, n, tap_rows, ch), BF16),
        pltpu.VMEM((2, n - 1, tap_rows, ch), BF16),
        pltpu.VMEM((2, 3 * ch, cells), BF16),
        pltpu.VMEM((PLAIN_HALVES, packed, cells // PLAIN_HALVES), BF16),
        pltpu.VMEM((PLAIN_HALVES, cells // PLAIN_HALVES, packed), BF16),
        pltpu.VMEM((PLAIN_HALVES, cells // PLAIN_HALVES, ch), F32),
        pltpu.VMEM((2, 2, wide, ch), BF16),
        pltpu.VMEM((2, 2, wide, ch), BF16),
        pltpu.VMEM((2, wide, ch), BF16),
        pltpu.VMEM((2, wide, ch), BF16),
        field, field, field, field, field, field, field, field, field,
        pltpu.VMEM((total + 16, ch), F32),
        pltpu.VMEM((cells, ch), F32),
        pltpu.VMEM((4, n, 2 * wide + PLAIN_HALVES * packed, ch), BF16),
        pltpu.VMEM((n, rows + 2, wide, 3 * ch), BF16),
        pltpu.VMEM((2, n, 2, owners, piece, ch), F32),
        pltpu.VMEM((2, n, owners, piece, ch), BF16),
        pltpu.VMEM((2, n, owners, piece, ch), BF16),
        pltpu.VMEM((2, n, owners, piece, ch), BF16),
        pltpu.VMEM((2, n, chips, piece, ch), BF16),
        pltpu.VMEM((2, n, 2, owners, piece, ch), BF16),
        pltpu.VMEM((4, 8, ch), F32),
        pltpu.VMEM((4, s_count, 8, ch), F32),
        pltpu.VMEM((3, 2, wide, ch), F32),
        pltpu.VMEM((3, 2, wide, ch), F32),
        sem((2, n)),
        sem((2, n)), sem((2, n)),
        sem((2, n - 1, s_count)), sem((2, n - 1, s_count)),
        sem((2,)), sem((2,)),
        sem((2,)), sem((2,)),
        sem((4, 2, n, PLAIN_HALVES)), sem((4, n, PLAIN_HALVES)),
        sem((4, s_count)), sem((4, s_count)),
        sem((3, 2)), sem((3, 2)),
        sem((2, n)), sem((2, n)),
        sem((2, n, chips)), sem((2, n, chips)),
        sem((2, n, chips)), sem((2, n, chips)),
        sem((2, n)), sem((2, n)),
        sem((2, n)),
    ]


def scratch_bytes(scratch):
    held = [v for v in scratch if hasattr(v, "dtype") and v.dtype in (F32, BF16)]
    return sum(math.prod(v.shape[:-1]) * -(-v.shape[-1] // 128) * 128 * v.dtype.itemsize for v in held)


def per_device(n, s_count, blocks, weight_one, weight_two, gain_one, shift_one, gain_two, shift_two, cell_live, cotangent):
    rows, wide = cell_live.shape
    ch = blocks.shape[1] // wide
    aligned = ch % 128 == 0
    tap_rows = 9 * ch
    half_rows = tap_rows // 2
    owners = math.gcd(half_rows // 16, s_count // 2)
    piece = half_rows // owners

    sizes = (n, s_count, rows, wide, ch)
    kernel, packed, scratch = block_kernel, packed_rows(rows // (n // 2), wide), block_scratch(*sizes)
    if scratch_bytes(scratch) > SCRATCH_LIMIT:
        kernel, packed, scratch = plain_kernel, packed_rows(rows // PLAIN_HALVES, wide), plain_scratch(*sizes)

    if aligned:
        weight_one, weight_two = (w.reshape(tap_rows, n * ch) for w in (weight_one, weight_two))
    else:
        weight_one, weight_two = (
            w.reshape(tap_rows, n, ch).transpose(1, 0, 2) for w in (weight_one, weight_two))
    grad_shape = (2, owners, piece, n * ch) if aligned else (n, 2, owners, piece, ch)
    vmem = pl.BlockSpec(memory_space=pltpu.VMEM)
    hbm = pl.BlockSpec(memory_space=pl.ANY)
    sem = pltpu.SemaphoreType.DMA
    block_out, input_grad, wg1, wg2, *sums = pl.pallas_call(
        functools.partial(kernel, n, s_count, rows, wide, ch, aligned, packed),
        out_shape=(
            jax.ShapeDtypeStruct((rows, ch * wide), BF16),
            jax.ShapeDtypeStruct((rows, ch * wide), F32),
            jax.ShapeDtypeStruct(grad_shape, BF16),
            jax.ShapeDtypeStruct(grad_shape, BF16),
            *[jax.ShapeDtypeStruct((1, ch), F32)] * 4,
        ),
        in_specs=[vmem] * 7 + [hbm] * 2,
        out_specs=(vmem, vmem, hbm, hbm, vmem, vmem, vmem, vmem),
        scratch_shapes=scratch,
        compiler_params=pltpu.CompilerParams(
            collective_id=0, has_side_effects=True, vmem_limit_bytes=60 * 1024 * 1024),
    )(blocks, cotangent, cell_live.T,
      *(v.reshape(1, ch) for v in (gain_one, shift_one, gain_two, shift_two)), weight_one, weight_two)

    if not aligned:
        def whole(grad):
            grad = grad.reshape(n, tap_rows, ch).transpose(1, 0, 2)
            return grad.astype(F32).reshape(9, ch, n * ch)
        return (block_out, input_grad, whole(wg1), whole(wg2), *(v.reshape(ch) for v in sums))

    wg1, wg2 = (w.reshape(tap_rows, n * ch) for w in (wg1, wg2))
    wide_grad = jax.ShapeDtypeStruct((tap_rows, n * ch), F32)
    moved = (block_out, input_grad, *sums)
    grad1, grad2, *moved = pl.pallas_call(
        functools.partial(finish_kernel, 2 + len(moved)),
        out_shape=(wide_grad, wide_grad, *(jax.ShapeDtypeStruct(v.shape, v.dtype) for v in moved)),
        in_specs=[pl.BlockSpec(memory_space=pl.ANY)] * (2 + len(moved)),
        out_specs=[pl.BlockSpec(memory_space=pl.ANY)] * (2 + len(moved)),
        scratch_shapes=[
            pltpu.VMEM((2, tap_rows, n * ch), BF16), pltpu.VMEM((2, tap_rows, n * ch), F32),
            sem((2, FINISH_PARTS)), sem((2, FINISH_PARTS)), sem((len(moved),)), sem((len(moved),)),
            *(pltpu.VMEM(v.shape, v.dtype) for v in moved),
        ],
        compiler_params=pltpu.CompilerParams(vmem_limit_bytes=64 * 1024 * 1024),
    )(wg1, wg2, *moved)
    block_out, input_grad, *sums = moved
    grads = (g.reshape(9, ch, n * ch) for g in (grad1, grad2))
    return (block_out, input_grad, *grads, *(v.reshape(ch) for v in sums))


def solution(mesh):
    return jax.shard_map(
        functools.partial(per_device, mesh.shape["chan"], mesh.shape["space"]),
        mesh=mesh,
        in_specs=(
            P("space", "chan"),
            P(None, "chan", None),
            P(None, "chan", None),
            P("chan"),
            P("chan"),
            P("chan"),
            P("chan"),
            P("space", None),
            P("space", "chan"),
        ),
        out_specs=(
            P("space", "chan"),
            P("space", "chan"),
            P(None, "chan", None),
            P(None, "chan", None),
            P("chan"),
            P("chan"),
            P("chan"),
            P("chan"),
        ),
        check_vma=False,
    )
```

```python
import functools
import math

import jax
import jax.numpy as jnp
from jax import lax
from jax.experimental import pallas as pl
from jax.experimental.pallas import tpu as pltpu
from jax.sharding import PartitionSpec as P

EPSILON = 1e-05
MESH = pl.DeviceIdType.MESH
F32 = jnp.float32
BF16 = jnp.bfloat16
ROOT_HALF = 0.7071067811865476
ROOT_TWO_PI = 0.3989422804014327
CHUNK = 64
FINISH_PARTS = 4
UNROLL = 1
HALVES = 2
LARGE, SMALL = 7, 3


def dot(a, b):
    return jnp.dot(a, b, preferred_element_type=F32)


def gelu_parts(v):
    upper = 0.5 * (1.0 + lax.erf(v * ROOT_HALF))
    slope = upper + v * (ROOT_TWO_PI * jnp.exp(-0.5 * v * v))
    return v * upper, slope


def most_live(rows, wide):
    units = (wide + 1) // (SMALL + 1)
    live_rows = rows - rows // (LARGE + 1)
    return min(rows * wide, math.ceil(units * live_rows * LARGE / 2))


def block_kernel(n, s_count, rows, wide, ch, aligned, packed, *refs):
    (x_in, cot_in, live_in, gain1_in, shift1_in, gain2_in, shift2_in, w1_hbm, w2_hbm) = refs[:9]
    (out_block, out_input, out_wg1, out_wg2, out_gain1, out_shift1, out_gain2, out_shift2) = refs[9:17]
    (turned, wv, wf, x_t, pack, unpack, places, edge_send, edge_recv, cot_send, cot_recv, cotm, mask, masked,
     normed1, normed2, through, slope1, hid, hid2, pad, acc, hold, taken,
     part, psend, crecv, hsend, qrecv, wout, st_send, st_recv, row_send, row_recv,
     w_sem, wz_ssem, wz_rsem, wp_ssem, wp_rsem, e_ssem, e_rsem, ce_ssem, ce_rsem, ag_ssem, ag_rsem,
     st_ssem, st_rsem, row_ssem, row_rsem, c_ssem, c_rsem, q_ssem, q_rsem,
     f_ssem, f_rsem, h_ssem, h_rsem, o_sem) = refs[17:]

    z = lax.axis_index("chan")
    s = lax.axis_index("space")
    cells = rows * wide
    total = cells + 2 * wide
    band = cells // HALVES
    core, chip, chips = s % 2, s // 2, s_count // 2
    before, after = (s + s_count - 1) % s_count, (s + 1) % s_count
    tap_rows = 9 * ch

    barrier = pltpu.get_barrier_semaphore()

    @pl.loop(1, s_count)
    def _(k):
        pl.semaphore_signal(barrier, inc=1, device_id=(z, (s + k) % s_count), device_id_type=MESH)

    @pl.loop(1, n)
    def _(k):
        pl.semaphore_signal(barrier, inc=1, device_id=((z + k) % n, s), device_id_type=MESH)

    w_copies = []
    for which, source in enumerate((w1_hbm, w2_hbm)):
        for d in range(n):
            block = source.at[:, d * ch:(d + 1) * ch] if aligned else source.at[d]
            w_copies.append(pltpu.make_async_copy(block, wv.at[which, d], w_sem.at[which, d]))
        own = source.at[:, pl.ds(pl.multiple_of(z * ch, ch), ch)] if aligned else source.at[z]
        w_copies.append(pltpu.make_async_copy(own, wf.at[which, n - 1], w_sem.at[which, n]))
    for copy in w_copies:
        copy.start()

    def chunked(fn, init, first=0, count=cells):
        def step(i, carry):
            return fn(pl.multiple_of(first + i * CHUNK, CHUNK), CHUNK, carry)
        return lax.fori_loop(0, count // CHUNK, step, init, unroll=UNROLL)

    lanes = 128
    tiles = ch * wide // lanes

    def from_flat(flat, put):
        @pl.loop(0, tiles)
        def _(i):
            at = pl.ds(pl.multiple_of(i * lanes, lanes), lanes)
            turned[at, 0:rows] = flat[:, at].astype(F32).T

        @pl.loop(0, wide)
        def _(w):
            put(pl.ds(w, rows, stride=wide), turned[pl.ds(w, ch, stride=wide), 0:rows].T)

    def to_flat(source, flat):
        @pl.loop(0, wide)
        def _(w):
            turned[pl.ds(w, ch, stride=wide), 0:rows] = source[pl.ds(w, rows, stride=wide), :].T

        @pl.loop(0, tiles)
        def _(i):
            at = pl.ds(pl.multiple_of(i * lanes, lanes), lanes)
            flat[:, at] = turned[at, 0:rows].T.astype(flat.dtype)

    def put_masked(at, value):
        masked[at, :] = value

    from_flat(x_in, put_masked)

    live = live_in[...].astype(BF16)

    def load_main(start, size, carry):
        at = pl.ds(start, size)
        cell = start + lax.broadcasted_iota(jnp.int32, (size, rows), 0)
        pick = (cell // wide == lax.broadcasted_iota(jnp.int32, (size, rows), 1)).astype(F32).astype(BF16)
        column_of = lax.broadcasted_iota(jnp.int32, (size, wide), 0) % wide
        picked = lax.dot_general(pick, live, (((1,), (1,)), ((), ())), preferred_element_type=F32)
        picked = jnp.where(column_of == lax.broadcasted_iota(jnp.int32, (size, wide), 1), picked, 0.0)
        lv = dot(picked.astype(BF16), jnp.ones((wide, ch), BF16))
        mask[at, :] = lv
        masked[at, :] = masked[at, :] * lv
        return carry

    lax.fori_loop(0, cells // band, lambda i, c: load_main(pl.multiple_of(i * band, band), band, c), 0)
    for side, start in ((0, 0), (1, cells - wide)):
        edge_send[side, 0] = masked[start:start + wide, :].astype(BF16)
        edge_send[side, 1] = mask[start:start + wide, :].astype(BF16)

    lead = 2 * wide
    acc[...] = jnp.zeros_like(acc)
    for block in range(n):
        taken[block, 0:2, :, :] = jnp.zeros((2, wide, 3 * ch), BF16)
    st_send[...] = jnp.zeros_like(st_send)

    pl.semaphore_wait(barrier, s_count - 1 + n - 1)

    def edge_copy(side):
        return pltpu.make_async_remote_copy(
            src_ref=edge_send.at[side], dst_ref=edge_recv.at[1 - side],
            send_sem=e_ssem.at[side], recv_sem=e_rsem.at[1 - side],
            device_id=(z, before if side == 0 else after), device_id_type=MESH)

    for side in range(2):
        edge_copy(side).start()

    def cot_copy(side):
        return pltpu.make_async_remote_copy(
            src_ref=cot_send.at[side], dst_ref=cot_recv.at[1 - side],
            send_sem=ce_ssem.at[side], recv_sem=ce_rsem.at[1 - side],
            device_id=(z, before if side == 0 else after), device_id_type=MESH)

    def load_cotangent():
        def put(at, value):
            cotm[at, :] = value
        from_flat(cot_in, put)

        def live_only(start, size, carry):
            at = pl.ds(start, size)
            cotm[at, :] = cotm[at, :] * mask[at, :]
            return carry
        chunked(live_only, 0)
        for side, start in ((0, 0), (1, cells - wide)):
            cot_send[side] = cotm[start:start + wide, :].astype(BF16)
            cot_copy(side).start()

    def take_cotangent():
        for side in range(2):
            cot_copy(1 - side).wait_recv()
            at = slice(cells + side * wide, cells + (side + 1) * wide)
            cotm[at, :] = cot_recv[side].astype(F32) * mask[at, :]

    w_parts = math.gcd(tap_rows // 16, s_count)
    w_rows = tap_rows // w_parts
    w_mine = s % w_parts
    w_group = s - w_mine

    def wz_copy(which, k):
        at = pl.ds(w_mine * w_rows, w_rows)
        slot = n - k - 1
        return pltpu.make_async_remote_copy(
            src_ref=wv.at[which, (z + k) % n, at, :], dst_ref=wf.at[which, slot, at, :],
            send_sem=wz_ssem.at[which, slot], recv_sem=wz_rsem.at[which, slot],
            device_id=((z + k) % n, s), device_id_type=MESH)

    def wp_copy(which, slot, k, whose):
        at = pl.ds(whose * w_rows, w_rows)
        return pltpu.make_async_remote_copy(
            src_ref=wf.at[which, slot, at, :], dst_ref=wf.at[which, slot, at, :],
            send_sem=wp_ssem.at[which, slot, k], recv_sem=wp_rsem.at[which, slot, whose],
            device_id=(z, w_group + (w_mine + k) % w_parts), device_id_type=MESH)

    def weights_over_z(which):
        for copy in w_copies[which * (n + 1):(which + 1) * (n + 1)]:
            copy.wait()

        @pl.loop(1, n)
        def _(k):
            wz_copy(which, k).start()

    def slot_of(block):
        return (block - z + n - 1) % n

    def weights_round(which):
        @pl.loop(1, n)
        def _(distance):
            for sign in (1, -1):
                block = z - distance * sign

                @pl.when((block >= 0) & (block < n))
                def _():
                    slot = slot_of(block)
                    wz_copy(which, n - 1 - slot).wait_recv()

                    @pl.loop(1, w_parts)
                    def _(k):
                        wp_copy(which, slot, k, w_mine).start()

    def weights_arrived(which, slot):
        @pl.loop(1, w_parts)
        def _(k):
            wp_copy(which, slot, k, (w_mine + k) % w_parts).wait_recv()

    def row_copy(slot, side):
        return pltpu.make_async_remote_copy(
            src_ref=row_send.at[slot, side], dst_ref=row_recv.at[slot, 1 - side],
            send_sem=row_ssem.at[slot, side], recv_sem=row_rsem.at[slot, 1 - side],
            device_id=(z, before if side == 0 else after), device_id_type=MESH)

    def send_rows(slot):
        for side, start in ((0, lead), (1, lead + cells - wide)):
            row_send[slot, side] = acc[start:start + wide, :]
            row_copy(slot, side).start()

    def take_rows(slot, ref):
        for side in range(2):
            row_copy(slot, 1 - side).wait_recv()
            ref[cells + side * wide:cells + (side + 1) * wide, :] = row_recv[slot, side]

    def st_copy(slot, k, whose):
        return pltpu.make_async_remote_copy(
            src_ref=st_send.at[slot], dst_ref=st_recv.at[slot, whose],
            send_sem=st_ssem.at[slot, k], recv_sem=st_rsem.at[slot, whose],
            device_id=(z, (s + k) % s_count), device_id_type=MESH)

    def send_stats(slot, values):
        for i, v in enumerate(values):
            st_send[slot, i:i + 1, :] = v
        @pl.loop(1, s_count)
        def _(k):
            st_copy(slot, k, s).start()
        st_recv[slot, s] = st_send[slot]

    def take_stats(slot):
        @pl.loop(1, s_count)
        def _(k):
            st_copy(slot, k, (s + k) % s_count).wait_recv()

    strip = 8
    column = lax.broadcasted_iota(jnp.int32, (strip * wide, ch), 0) % wide

    def shift(target, first, count):
        size = count * wide
        where = column[:size]
        here = pad[pl.ds(8 + first * wide, size), :]
        left = jnp.where(where == 0, 0.0, pad[pl.ds(7 + first * wide, size), :])
        right = jnp.where(where == wide - 1, 0.0, pad[pl.ds(9 + first * wide, size), :])
        for b, v in enumerate((left, here, right)):
            target[pl.ds(first + 2, count), :, b * ch:(b + 1) * ch] = v.astype(BF16).reshape(count, wide, ch)

    edge = 2 * wide
    held = wide + packed
    band_rows = rows // HALVES
    conv_rows = (rows + 2) // HALVES

    def held_rows(q):
        start = q * held
        return pl.ds(pl.multiple_of(start, wide), wide), pl.ds(pl.multiple_of(start + wide, wide), packed)

    def unpack_half(ph, block, q, target):
        edge_at, cells_at = held_rows(q)
        pad[pl.ds(pl.multiple_of(8 + q * (wide + cells), 8), wide), :] = hold[ph, block, edge_at, :].astype(F32)
        pad[pl.ds(pl.multiple_of(8 + wide + q * band, 8), band), :] = dot(unpack[q], hold[ph, block, cells_at, :])
        shift(target, q * (rows + 1), 1)

        @pl.loop(0, band_rows // strip)
        def _(i):
            shift(target, 1 + q * band_rows + i * strip, strip)

    def add_conv(q, field, taps, turned_taps=None):
        lhs = field[pl.ds(q * conv_rows, conv_rows + 2), :, :].reshape((conv_rows + 2) * wide, 3 * ch)
        if turned_taps is None:
            value = dot(lhs, jnp.concatenate([taps(a) for a in range(3)], axis=1))
        else:
            rhs = jnp.concatenate([
                jnp.concatenate([turned_taps(3 * (2 - a) + 2 - b) for b in range(3)], axis=1) for a in range(3)], axis=0)
            value = lax.dot_general(lhs, rhs, (((1,), (1,)), ((), ())), preferred_element_type=F32)
        size = conv_rows * wide
        at = pl.ds(pl.multiple_of(q * size, wide), size)
        acc[at, :] = acc[at, :] + sum(
            value[a * wide:a * wide + size, a * ch:(a + 1) * ch] for a in range(3))

    def ag_copy(ph, block, q, sign):
        at = pl.ds(pl.multiple_of(q * held, wide), held)
        return pltpu.make_async_remote_copy(
            src_ref=hold.at[ph, block, at, :], dst_ref=hold.at[ph, block, at, :],
            send_sem=ag_ssem.at[ph, (1 - sign) // 2, block, q], recv_sem=ag_rsem.at[ph, block, q],
            device_id=(z + sign, s), device_id_type=MESH)

    def pack_field(ph, source, fill=None, first=None):
        if fill is not None:
            fill(cells, edge, 0)

        @pl.loop(0, HALVES)
        def _(q):
            if first is not None:
                first(q)
            start = pl.multiple_of(q * band, band)
            if fill is not None:
                lax.fori_loop(0, band // CHUNK, lambda i, c: fill(pl.multiple_of(start + i * CHUNK, CHUNK), CHUNK, c), 0)
            edge_at, cells_at = held_rows(q)
            hold[ph, z, edge_at, :] = source[pl.ds(pl.multiple_of(cells + q * wide, wide), wide), :].astype(BF16)
            hold[ph, z, cells_at, :] = dot(pack[q], source[pl.ds(start, band), :].astype(BF16)).astype(BF16)
            for sign in (1, -1):
                @pl.when((z + sign >= 0) & (z + sign < n))
                def _():
                    ag_copy(ph, z, q, sign).start()

    def inside(slice_at):
        return (slice_at >= 0) & (slice_at < n)

    def take_and_pass(ph, k, q, sign, passes=True, takes=True):
        block = z - k * sign

        @pl.when((k > 0) & inside(block))
        def _():
            if passes and takes:
                ag_copy(ph, block, q, sign).wait_recv()

            @pl.when(inside(z + sign))
            def _():
                if passes:
                    if not takes:
                        ag_copy(ph, block, q, sign).wait_recv()
                    ag_copy(ph, block, q, sign).start()

            if not passes:
                @pl.when(jnp.logical_not(inside(z + sign)))
                def _():
                    ag_copy(ph, block, q, sign).wait_recv()

    near = jnp.where(z < n - n // 2, 1, 0)

    def consume_way(k, q, way, consume):
        block = z - k * (1 - 2 * way)

        @pl.when((k >= 0) & (k < n) & inside(block) & ((k > 0) | (way == near)))
        def _():
            consume(k, block, q)

    def take_both(ph, k, q, **how):
        @pl.loop(0, 2)
        def _(i):
            way = (near + i) % 2
            take_and_pass(ph, k, q, 1 - 2 * way, **how)

    def consume_both(k, q, consume):
        @pl.loop(0, 2)
        def _(i):
            consume_way(k, q, (near + i) % 2, consume)

    def gather(ph, consume, each):
        @pl.loop(0, n)
        def _(k):
            @pl.loop(0, HALVES)
            def _(q):
                take_both(ph, k, q)
                consume_both(k, q, consume)
            each(k)

    def gather_passing_first(ph, consume, each):
        @pl.loop(0, n)
        def _(k):
            @pl.when(k == 1)
            def _():
                @pl.loop(1, n)
                def _(ahead):
                    @pl.loop(0, HALVES)
                    def _(q):
                        take_both(ph, ahead, q, takes=False)

            @pl.loop(0, HALVES)
            def _(q):
                take_both(ph, k, q, passes=False)
                consume_both(k, q, consume)
            each(k)

    last_pass = jnp.maximum(jnp.where(z < n - 1, z, 0), jnp.where(z > 0, n - 1 - z, 0))

    def forward(ph, field):
        def consume(k, block, q):
            into = taken.at[block]
            unpack_half(ph, block, q, into)
            slot = slot_of(block)

            @pl.when((k > 0) & (q == 0))
            def _():
                weights_arrived(ph, slot)
            add_conv(q, into, lambda a: wf[ph, slot, 3 * a * ch:3 * (a + 1) * ch, :])

        def each(k):
            if ph == 0:
                @pl.when(k == 0)
                def _():
                    weights_round(0)

                @pl.when(k == 1)
                def _():
                    weights_over_z(1)

            @pl.when(k == last_pass)
            def _():
                turn_field(ph, field)
                if ph == 0:
                    load_cotangent()
        (gather if ph else gather_passing_first)(ph, consume, each)

    def turn_field(ph, field):
        main = [field[start:start + ch, :].T for start in range(0, cells, ch)]
        ends = field[cells:cells + edge, :]
        if edge < ch:
            ends = jnp.concatenate([ends, jnp.zeros((ch - edge, ch), F32)], axis=0)
        ends = ends.T
        for i, here in enumerate(main):
            left = jnp.concatenate(
                [ends[:, 0:wide] if i == 0 else main[i - 1][:, ch - wide:], here[:, 0:ch - wide]], axis=1)
            right = jnp.concatenate(
                [here[:, wide:], main[i + 1][:, 0:wide] if i + 1 < len(main) else ends[:, wide:edge]], axis=1)
            for a, v in enumerate((left, here, right)):
                x_t[ph, a * ch:(a + 1) * ch, i * ch:(i + 1) * ch] = v.astype(BF16)

    half_rows = tap_rows // 2
    owners = math.gcd(half_rows // 16, chips)
    piece = half_rows // owners

    def c_copy(ph, j):
        return pltpu.make_async_remote_copy(
            src_ref=psend.at[ph, j], dst_ref=crecv.at[ph, j],
            send_sem=c_ssem.at[ph, j], recv_sem=c_rsem.at[ph, j],
            device_id=(z, chip * 2 + 1 - core), device_id_type=MESH)

    def q_copy(ph, j, e, whose, owner):
        return pltpu.make_async_remote_copy(
            src_ref=hsend.at[ph, j, owner], dst_ref=qrecv.at[ph, j, whose],
            send_sem=q_ssem.at[ph, j, e], recv_sem=q_rsem.at[ph, j, whose],
            device_id=(z, ((chip + e) % chips) * 2 + core), device_id_type=MESH)

    def f_copy(ph, j, e, owner):
        return pltpu.make_async_remote_copy(
            src_ref=wout.at[ph, j, core, owner], dst_ref=wout.at[ph, j, core, owner],
            send_sem=f_ssem.at[ph, j, e], recv_sem=f_rsem.at[ph, j, owner],
            device_id=(z, ((chip + e) % chips) * 2 + core), device_id_type=MESH)

    def h_copy(ph, j, whose):
        return pltpu.make_async_remote_copy(
            src_ref=wout.at[ph, j, whose], dst_ref=wout.at[ph, j, whose],
            send_sem=h_ssem.at[ph, j], recv_sem=h_rsem.at[ph, j],
            device_id=(z, chip * 2 + 1 - core), device_id_type=MESH)

    def o_copy(ph, j):
        target = (out_wg1, out_wg2)[ph]
        if aligned:
            target = target.at[:, :, :, pl.ds(pl.multiple_of(j * ch, ch), ch)]
        else:
            target = target.at[j]
        return pltpu.make_async_copy(wout.at[ph, j], target, o_sem.at[ph, j])

    def sum_cores(ph, j):
        @pl.loop(0, owners)
        def _(o):
            psend[ph, j, o] = part[ph, j, 1 - core, o].astype(BF16)
        c_copy(ph, j).start()

    def sum_chips(ph, j):
        c_copy(ph, j).wait_recv()
        @pl.loop(0, owners)
        def _(o):
            v = part[ph, j, core, o] + crecv[ph, j, o].astype(F32)
            part[ph, j, core, o] = v
            hsend[ph, j, o] = v.astype(BF16)

        @pl.loop(1, chips)
        def _(e):
            peer = (chip + e) % chips

            @pl.when(peer < owners)
            def _():
                q_copy(ph, j, e, chip, peer).start()

    def spread_chips(ph, j):
        @pl.when(chip < owners)
        def _():
            @pl.loop(1, chips)
            def _(e):
                q_copy(ph, j, e, (chip + e) % chips, chip).wait_recv()
            v = part[ph, j, core, chip]
            for e in range(1, chips):
                v = v + qrecv[ph, j, (chip + e) % chips].astype(F32)
            wout[ph, j, core, chip] = v.astype(BF16)

            @pl.loop(1, chips)
            def _(e):
                f_copy(ph, j, e, chip).start()

    def spread_cores(ph, j):
        @pl.loop(1, chips)
        def _(e):
            peer = (chip + e) % chips

            @pl.when(peer < owners)
            def _():
                f_copy(ph, j, e, peer).wait_recv()
        h_copy(ph, j, core).start()

    def finish(ph, j):
        h_copy(ph, j, 1 - core).wait_recv()
        o_copy(ph, j).start()

    def put_part(ph, j, tap, value):
        start = tap * ch
        done = 0
        while done < ch:
            row = start + done
            side, o, at = row // half_rows, row % half_rows // piece, row % piece
            size = min(ch - done, piece - at)
            part[ph, j, side, o, at:at + size, :] = value[done:done + size, :]
            done += size

    stages = (sum_cores, sum_chips, spread_chips, spread_cores, finish)

    def of_step(k, fn):
        @pl.loop(0, 2)
        def _(way):
            block = z - k * (1 - 2 * way)

            @pl.when((k >= 0) & (k < n) & inside(block) & ((k > 0) | (way == 0)))
            def _():
                fn(block)

    passing = last_pass > 0

    def made_at(step):
        first = jnp.where(passing & (step > 0), jnp.where(step == last_pass, 1, step + 1), step)
        return first, step + 1

    def advance(ph, k):
        for age in range(1, len(stages)):
            step = k - age

            @pl.when((step >= 0) & (step < n))
            def _():
                @pl.loop(*made_at(step))
                def _(made):
                    of_step(made, functools.partial(stages[age], ph))

    def advance_all(ph, age):
        @pl.loop(0, n)
        def _(j):
            stages[age](ph, j)

    def field_grad(ph, block):
        grad = taken[block, 3:rows + 3, :, :].reshape(cells, 3 * ch)
        value = dot(x_t[ph], grad)
        for a in range(3):
            for b in range(3):
                put_part(ph, block, 3 * a + b, value[a * ch:(a + 1) * ch, (2 - b) * ch:(3 - b) * ch])

    def make_grad(ph, block):
        field_grad(ph, block)
        sum_cores(ph, block)

    def backward(ph):
        last = ph == 0

        def consume(k, block, q):
            into = taken.at[block]
            unpack_half(2 + ph, block, q, into)
            if last:
                @pl.when((q == HALVES - 1) & ((k == 0) | (k >= last_pass)))
                def _():
                    make_grad(ph, block)
            add_conv(q, into, None, lambda t: wv[ph, block, t * ch:(t + 1) * ch, :])

        def each(k):
            first, end = made_at(k)
            if last:
                @pl.loop(first, end - 1)
                def _(step):
                    of_step(step, functools.partial(make_grad, ph))
                advance(ph, k)
                for age in range(2, len(stages)):
                    @pl.when(k == age - 2)
                    def _():
                        advance_all(1, age)
            else:
                @pl.loop(first, jnp.where(passing | (k < n - 1), end, first))
                def _(step):
                    of_step(step, functools.partial(make_grad, ph))

                @pl.when(k == last_pass)
                def _():
                    to_flat(hid2, out_block)
        gather(2 + ph, consume, each)

    def fold(v):
        return jnp.sum(v.reshape(v.shape[0] // 8, 8, ch), axis=0)

    def flatten(v):
        return jnp.sum(v, axis=0, keepdims=True)

    zero = jnp.zeros((8, ch), F32)

    def local_moments():
        def sums(start, size, carry):
            at = pl.ds(start, size)
            m = mask[at, :]
            return carry[0] + fold(acc[pl.ds(start + lead, size), :] * m), carry[1] + fold(m)
        added, number = (flatten(v) for v in chunked(sums, (zero, zero)))
        middle = added / jnp.maximum(number, 1.0)

        def spread(start, size, carry):
            at = pl.ds(start, size)
            c = (acc[pl.ds(start + lead, size), :] - middle) * mask[at, :]
            return carry + fold(c * c)
        return added, number, flatten(chunked(spread, zero))

    def moments(slot):
        take_stats(slot)
        got = [st_recv[slot, k] for k in range(s_count)]
        added = sum(g[0:1] for g in got)
        number = sum(g[1:2] for g in got)
        mean = added / number
        spread = 0.0
        for g in got:
            off = g[0:1] / jnp.maximum(g[1:2], 1.0) - mean
            spread = spread + (g[2:3] + g[1:2] * off * off)
        return mean, lax.rsqrt(spread / number + EPSILON), number

    def everywhere(fn):
        chunked(fn, 0)
        fn(cells, 2 * wide, 0)

    gain1, shift1, gain2, shift2 = (r[...] for r in (gain1_in, shift1_in, gain2_in, shift2_in))

    weights_over_z(0)

    below = lax.broadcasted_iota(jnp.int32, (band, band), 1) < lax.broadcasted_iota(jnp.int32, (band, band), 0)
    below = below.astype(F32).astype(BF16)

    def make_pack(h):
        lv = mask[pl.ds(pl.multiple_of(h * band, band), band), :]
        place = jnp.where(lv > 0.0, dot(below, lv.astype(BF16)), -1.0)
        places[h] = place
        across = place.T[0:1, :]
        spot = lax.broadcasted_iota(jnp.int32, (packed, band), 0).astype(F32)
        pack[h] = jnp.where(spot == across, 1.0, 0.0).astype(BF16)

    def make_unpack(h):
        for start in range(0, packed, ch):
            size = min(ch, packed - start)
            spot = start + lax.broadcasted_iota(jnp.int32, (band, size), 1)
            unpack[h, :, start:start + size] = jnp.where(
                places[h, :, :size] == spot.astype(F32), 1.0, 0.0).astype(BF16)

    for side in range(2):
        edge_copy(1 - side).wait_recv()
        there = jnp.where(s > 0, 1.0, 0.0) if side == 0 else jnp.where(s < s_count - 1, 1.0, 0.0)
        at = slice(cells + side * wide, cells + (side + 1) * wide)
        masked[at, :] = edge_recv[side, 0].astype(F32) * there
        mask[at, :] = edge_recv[side, 1].astype(F32) * there

    pack_field(0, masked, first=make_pack)
    pl.loop(0, HALVES)(make_unpack)
    forward(0, masked)
    send_rows(0)
    send_stats(0, local_moments())
    weights_round(1)
    mean1, scale1, count = moments(0)

    def activate_one(start, size, carry):
        at = pl.ds(start, size)
        main = start is not cells
        nv = ((acc[pl.ds(start + lead, size), :] if main else normed1[at, :]) - mean1) * scale1
        normed1[at, :] = nv
        hid[at, :] = gelu_parts(nv * gain1 + shift1)[0] * mask[at, :]
        if main:
            acc[pl.ds(start + lead, size), :] = jnp.zeros((size, ch), F32)
        return carry

    def slope_one(start, size, carry):
        at = pl.ds(start, size)
        slope1[at, :] = gelu_parts(normed1[at, :] * gain1 + shift1)[1] * mask[at, :]
        return carry

    take_rows(0, normed1)
    pack_field(1, hid, activate_one)
    everywhere(slope_one)
    forward(1, hid)
    send_rows(1)
    send_stats(1, local_moments())
    mean2, scale2, _ = moments(1)

    def activate_two(value, start, size):
        at = pl.ds(start, size)
        nv = (value - mean2) * scale2
        normed2[at, :] = nv
        value, slope = gelu_parts(nv * gain2 + shift2 + masked[at, :])
        t = cotm[at, :] * slope
        through[at, :] = t
        return value, nv, t

    def activate_main(start, size, carry):
        at = pl.ds(start, size)
        sums_at = pl.ds(start + lead, size)
        value, nv, t = activate_two(acc[sums_at, :], start, size)
        hid2[at, :] = value * mask[at, :]
        acc[sums_at, :] = jnp.zeros((size, ch), F32)
        return carry[0] + fold(t * nv), carry[1] + fold(t)

    send_stats(2, [flatten(v) for v in chunked(activate_main, (zero, zero))])
    take_rows(1, normed2)
    take_cotangent()
    activate_two(normed2[cells:total, :], cells, edge)

    def gradient_sums(slot):
        take_stats(slot)
        got = [st_recv[slot, k] for k in range(s_count)]
        return sum(g[0:1] for g in got), sum(g[1:2] for g in got)

    def norm_back(upstream, normed, gain, scale, sums):
        gain_grad, shift_grad = sums
        factor = gain * scale
        level, tilt = shift_grad / count, gain_grad / count

        def fill(start, size, carry):
            at = pl.ds(start, size)
            v = upstream[at, :] - mask[at, :] * (level + normed[at, :] * tilt)
            hid[at, :] = factor * v
            return carry
        return fill

    sums2 = gradient_sums(2)
    pack_field(3, hid, norm_back(through, normed2, gain2, scale2, sums2))
    backward(1)

    send_rows(2)

    def inner_main(start, size, carry):
        at = pl.ds(start, size)
        sums_at = pl.ds(start + lead, size)
        v = acc[sums_at, :] * slope1[at, :]
        slope1[at, :] = v
        acc[sums_at, :] = jnp.zeros((size, ch), F32)
        return carry[0] + fold(v * normed1[at, :]), carry[1] + fold(v)

    send_stats(3, [flatten(v) for v in chunked(inner_main, (zero, zero))])

    @pl.when(jnp.logical_not(passing))
    def _():
        of_step(n - 1, functools.partial(make_grad, 1))
    for side in range(2):
        row_copy(2, 1 - side).wait_recv()
        at = slice(cells + side * wide, cells + (side + 1) * wide)
        slope1[at, :] = row_recv[2, side] * slope1[at, :]
    sums1 = gradient_sums(3)
    pack_field(2, hid, norm_back(slope1, normed1, gain1, scale1, sums1))
    advance_all(1, 1)
    backward(0)
    advance(0, n)

    def finish_input(start, size, carry):
        at = pl.ds(start, size)
        through[at, :] = (acc[pl.ds(start + lead, size), :] + through[at, :]) * mask[at, :]
        return carry

    chunked(finish_input, 0)
    to_flat(through, out_input)
    out_gain1[...], out_shift1[...] = sums1
    out_gain2[...], out_shift2[...] = sums2
    for extra in range(1, len(stages) - 1):
        advance(0, n + extra)

    for side in range(2):
        edge_copy(side).wait_send()
        cot_copy(side).wait_send()
        for slot in range(3):
            row_copy(slot, side).wait_send()

    @pl.loop(1, s_count)
    def _(k):
        for slot in range(4):
            st_copy(slot, k, s).wait_send()

    @pl.loop(1, n)
    def _(k):
        for which in range(2):
            wz_copy(which, k).wait_send()

    @pl.loop(1, w_parts)
    def _(k):
        for which in range(2):
            for slot in range(n - 1):
                wp_copy(which, slot, k, w_mine).wait_send()

    @pl.loop(0, n)
    def _(k):
        for sign in (1, -1):
            block = z - k * sign

            @pl.when((block >= 0) & (block < n) & (z + sign >= 0) & (z + sign < n))
            def _():
                for ph in range(4):
                    for q in range(HALVES):
                        ag_copy(ph, block, q, sign).wait_send()

    @pl.loop(0, n)
    def _(j):
        for ph in range(2):
            c_copy(ph, j).wait_send()
            h_copy(ph, j, core).wait_send()
            o_copy(ph, j).wait()

            @pl.loop(1, chips)
            def _(e):
                peer = (chip + e) % chips

                @pl.when(peer < owners)
                def _():
                    q_copy(ph, j, e, chip, peer).wait_send()

                @pl.when(chip < owners)
                def _():
                    f_copy(ph, j, e, chip).wait_send()


def finish_kernel(count, *refs):
    ins, outs = refs[:count], refs[count:2 * count]
    narrow, wide, in_sem, out_sem, take_sem, give_sem = refs[2 * count:2 * count + 6]
    held = refs[2 * count + 6:]
    rows = narrow.shape[1] // FINISH_PARTS
    parts = [(w, i, pl.ds(i * rows, rows)) for i in range(FINISH_PARTS) for w in range(2)]
    loads = [pltpu.make_async_copy(ins[w].at[at, :], narrow.at[w, at, :], in_sem.at[w, i]) for w, i, at in parts]
    stores = [pltpu.make_async_copy(wide.at[w, at, :], outs[w].at[at, :], out_sem.at[w, i]) for w, i, at in parts]
    takes = [pltpu.make_async_copy(ins[2 + k], v, take_sem.at[k]) for k, v in enumerate(held)]
    gives = [pltpu.make_async_copy(v, outs[2 + k], give_sem.at[k]) for k, v in enumerate(held)]
    for copy in loads + takes:
        copy.start()
    for load, store, (w, i, at) in zip(loads, stores, parts):
        load.wait()
        wide[w, at, :] = narrow[w, at, :].astype(F32)
        store.start()
    for take, give in zip(takes, gives):
        take.wait()
        give.start()
    for copy in stores + gives:
        copy.wait()


def per_device(n, s_count, blocks, weight_one, weight_two, gain_one, shift_one, gain_two, shift_two, cell_live, cotangent):
    rows, wide = cell_live.shape
    ch = blocks.shape[1] // wide
    cells = rows * wide
    total = cells + 2 * wide
    packed = -(-most_live(rows // HALVES, wide) // 16) * 16
    aligned = ch % 128 == 0
    chips = s_count // 2
    tap_rows = 9 * ch
    half_rows = tap_rows // 2
    owners = math.gcd(half_rows // 16, chips)
    piece = half_rows // owners

    if aligned:
        weight_one, weight_two = (w.reshape(tap_rows, n * ch) for w in (weight_one, weight_two))
    else:
        weight_one, weight_two = (
            w.reshape(tap_rows, n, ch).transpose(1, 0, 2) for w in (weight_one, weight_two))
    grad_shape = (2, owners, piece, n * ch) if aligned else (n, 2, owners, piece, ch)
    vmem = pl.BlockSpec(memory_space=pltpu.VMEM)
    hbm = pl.BlockSpec(memory_space=pl.ANY)
    sem = pltpu.SemaphoreType.DMA
    field = pltpu.VMEM((total, ch), F32)
    scratch = [
        pltpu.VMEM((ch * wide, 128), F32),
        pltpu.VMEM((2, n, tap_rows, ch), BF16),
        pltpu.VMEM((2, n, tap_rows, ch), BF16),
        pltpu.VMEM((2, 3 * ch, cells), BF16),
        pltpu.VMEM((HALVES, packed, cells // HALVES), BF16),
        pltpu.VMEM((HALVES, cells // HALVES, packed), BF16),
        pltpu.VMEM((HALVES, cells // HALVES, ch), F32),
        pltpu.VMEM((2, 2, wide, ch), BF16),
        pltpu.VMEM((2, 2, wide, ch), BF16),
        pltpu.VMEM((2, wide, ch), BF16),
        pltpu.VMEM((2, wide, ch), BF16),
        field, field, field, field, field, field, field, field, field,
        pltpu.VMEM((total + 16, ch), F32),
        pltpu.VMEM((total, ch), F32),
        pltpu.VMEM((4, n, 2 * wide + HALVES * packed, ch), BF16),
        pltpu.VMEM((n, rows + 4, wide, 3 * ch), BF16),
        pltpu.VMEM((2, n, 2, owners, piece, ch), F32),
        pltpu.VMEM((2, n, owners, piece, ch), BF16),
        pltpu.VMEM((2, n, owners, piece, ch), BF16),
        pltpu.VMEM((2, n, owners, piece, ch), BF16),
        pltpu.VMEM((2, n, chips, piece, ch), BF16),
        pltpu.VMEM((2, n, 2, owners, piece, ch), BF16),
        pltpu.VMEM((4, 8, ch), F32),
        pltpu.VMEM((4, s_count, 8, ch), F32),
        pltpu.VMEM((3, 2, wide, ch), F32),
        pltpu.VMEM((3, 2, wide, ch), F32),
        sem((2, n + 1)),
        sem((2, n)), sem((2, n)),
        sem((2, n - 1, s_count)), sem((2, n - 1, s_count)),
        sem((2,)), sem((2,)),
        sem((2,)), sem((2,)),
        sem((4, 2, n, HALVES)), sem((4, n, HALVES)),
        sem((4, s_count)), sem((4, s_count)),
        sem((3, 2)), sem((3, 2)),
        sem((2, n)), sem((2, n)),
        sem((2, n, chips)), sem((2, n, chips)),
        sem((2, n, chips)), sem((2, n, chips)),
        sem((2, n)), sem((2, n)),
        sem((2, n)),
    ]
    block_out, input_grad, wg1, wg2, *sums = pl.pallas_call(
        functools.partial(block_kernel, n, s_count, rows, wide, ch, aligned, packed),
        out_shape=(
            jax.ShapeDtypeStruct((rows, ch * wide), BF16),
            jax.ShapeDtypeStruct((rows, ch * wide), F32),
            jax.ShapeDtypeStruct(grad_shape, BF16),
            jax.ShapeDtypeStruct(grad_shape, BF16),
            *[jax.ShapeDtypeStruct((1, ch), F32)] * 4,
        ),
        in_specs=[vmem] * 7 + [hbm] * 2,
        out_specs=(vmem, vmem, hbm, hbm, vmem, vmem, vmem, vmem),
        scratch_shapes=scratch,
        compiler_params=pltpu.CompilerParams(
            collective_id=0, has_side_effects=True, vmem_limit_bytes=60 * 1024 * 1024),
    )(blocks, cotangent, cell_live.T,
      *(v.reshape(1, ch) for v in (gain_one, shift_one, gain_two, shift_two)), weight_one, weight_two)

    if not aligned:
        def whole(grad):
            grad = grad.reshape(n, tap_rows, ch).transpose(1, 0, 2)
            return grad.astype(F32).reshape(9, ch, n * ch)
        return (block_out, input_grad, whole(wg1), whole(wg2), *(v.reshape(ch) for v in sums))

    wg1, wg2 = (w.reshape(tap_rows, n * ch) for w in (wg1, wg2))
    wide_grad = jax.ShapeDtypeStruct((tap_rows, n * ch), F32)
    moved = (block_out, input_grad, *sums)
    grad1, grad2, *moved = pl.pallas_call(
        functools.partial(finish_kernel, 2 + len(moved)),
        out_shape=(wide_grad, wide_grad, *(jax.ShapeDtypeStruct(v.shape, v.dtype) for v in moved)),
        in_specs=[pl.BlockSpec(memory_space=pl.ANY)] * (2 + len(moved)),
        out_specs=[pl.BlockSpec(memory_space=pl.ANY)] * (2 + len(moved)),
        scratch_shapes=[
            pltpu.VMEM((2, tap_rows, n * ch), BF16), pltpu.VMEM((2, tap_rows, n * ch), F32),
            sem((2, FINISH_PARTS)), sem((2, FINISH_PARTS)), sem((len(moved),)), sem((len(moved),)),
            *(pltpu.VMEM(v.shape, v.dtype) for v in moved),
        ],
        compiler_params=pltpu.CompilerParams(vmem_limit_bytes=64 * 1024 * 1024),
    )(wg1, wg2, *moved)
    block_out, input_grad, *sums = moved
    grads = (g.reshape(9, ch, n * ch) for g in (grad1, grad2))
    return (block_out, input_grad, *grads, *(v.reshape(ch) for v in sums))


def solution(mesh):
    return jax.shard_map(
        functools.partial(per_device, mesh.shape["chan"], mesh.shape["space"]),
        mesh=mesh,
        in_specs=(
            P("space", "chan"),
            P(None, "chan", None),
            P(None, "chan", None),
            P("chan"),
            P("chan"),
            P("chan"),
            P("chan"),
            P("space", None),
            P("space", "chan"),
        ),
        out_specs=(
            P("space", "chan"),
            P("space", "chan"),
            P(None, "chan", None),
            P(None, "chan", None),
            P("chan"),
            P("chan"),
            P("chan"),
            P("chan"),
        ),
        check_vma=False,
    )
```

```python
import functools
import math

import jax
import jax.numpy as jnp
from jax import lax
from jax.experimental import pallas as pl
from jax.experimental.pallas import tpu as pltpu
from jax.sharding import PartitionSpec as P

EPSILON = 1e-05
MESH = pl.DeviceIdType.MESH
F32 = jnp.float32
BF16 = jnp.bfloat16
ROOT_HALF = 0.7071067811865476
ROOT_TWO_PI = 0.3989422804014327
CHUNK = 64
FINISH_PARTS = 4
UNROLL = 4
HALVES = 2
LARGE, SMALL = 7, 3


def dot(a, b):
    return jnp.dot(a, b, preferred_element_type=F32)


def gelu_parts(v):
    upper = 0.5 * (1.0 + lax.erf(v * ROOT_HALF))
    slope = upper + v * (ROOT_TWO_PI * jnp.exp(-0.5 * v * v))
    return v * upper, slope


def most_live(rows, wide):
    units = (wide + 1) // (SMALL + 1)
    live_rows = rows - rows // (LARGE + 1)
    return min(rows * wide, math.ceil(units * live_rows * LARGE / 2))


def block_kernel(n, s_count, rows, wide, ch, aligned, packed, *refs):
    (x_in, cot_in, live_in, gain1_in, shift1_in, gain2_in, shift2_in, w1_hbm, w2_hbm) = refs[:9]
    (out_block, out_input, out_wg1, out_wg2, out_gain1, out_shift1, out_gain2, out_shift2) = refs[9:17]
    (turned, wv, wf, x_t, pack, unpack, places, edge_send, edge_recv, cotm, mask, masked,
     normed1, normed2, through, slope1, hid, hid2, pad, acc, hold, taken,
     part, psend, crecv, hsend, qrecv, wout, st_send, st_recv, row_send, row_recv,
     w_sem, wz_ssem, wz_rsem, wp_ssem, wp_rsem, e_ssem, e_rsem, ag_ssem, ag_rsem,
     st_ssem, st_rsem, row_ssem, row_rsem, c_ssem, c_rsem, q_ssem, q_rsem,
     f_ssem, f_rsem, h_ssem, h_rsem, o_sem) = refs[17:]

    z = lax.axis_index("chan")
    s = lax.axis_index("space")
    cells = rows * wide
    total = cells + 2 * wide
    band = cells // HALVES
    core, chip, chips = s % 2, s // 2, s_count // 2
    before, after = (s + s_count - 1) % s_count, (s + 1) % s_count
    tap_rows = 9 * ch

    barrier = pltpu.get_barrier_semaphore()

    @pl.loop(1, s_count)
    def _(k):
        pl.semaphore_signal(barrier, inc=1, device_id=(z, (s + k) % s_count), device_id_type=MESH)

    @pl.loop(1, n)
    def _(k):
        pl.semaphore_signal(barrier, inc=1, device_id=((z + k) % n, s), device_id_type=MESH)

    w_copies = []
    for which, source in enumerate((w1_hbm, w2_hbm)):
        for d in range(n):
            block = source.at[:, d * ch:(d + 1) * ch] if aligned else source.at[d]
            w_copies.append(pltpu.make_async_copy(block, wv.at[which, d], w_sem.at[which, d]))
    for copy in w_copies:
        copy.start()

    def chunked(fn, init, first=0, count=cells):
        def step(i, carry):
            return fn(pl.multiple_of(first + i * CHUNK, CHUNK), CHUNK, carry)
        return lax.fori_loop(0, count // CHUNK, step, init, unroll=UNROLL)

    lanes = 128
    tiles = ch * wide // lanes

    def from_flat(flats, puts):
        for i in range(tiles):
            at = slice(i * lanes, (i + 1) * lanes)
            turned[at, :] = jnp.concatenate([flat[:, at].astype(F32) for flat in flats], axis=0).T
        for w in range(wide):
            both = turned[pl.ds(w, ch, stride=wide), :].T
            for i, put in enumerate(puts):
                put(pl.ds(w, rows, stride=wide), both[i * rows:(i + 1) * rows, :])

    def to_flat(source, flat):
        for w in range(wide):
            turned[pl.ds(w, ch, stride=wide), 0:rows] = source[pl.ds(w, rows, stride=wide), :].T
        for i in range(tiles):
            flat[:, i * lanes:(i + 1) * lanes] = turned[i * lanes:(i + 1) * lanes, 0:rows].T.astype(flat.dtype)

    def put_masked(at, value):
        masked[at, :] = value

    def put_cotangent(at, value):
        cotm[at, :] = value

    from_flat((x_in, cot_in), (put_masked, put_cotangent))

    cell = lax.broadcasted_iota(jnp.int32, (cells, rows), 0)
    pick = (cell // wide == lax.broadcasted_iota(jnp.int32, (cells, rows), 1)).astype(F32).astype(BF16)
    column_of = lax.broadcasted_iota(jnp.int32, (cells, wide), 0) % wide
    picked = lax.dot_general(pick, live_in[...].astype(BF16), (((1,), (1,)), ((), ())), preferred_element_type=F32)
    picked = jnp.where(column_of == lax.broadcasted_iota(jnp.int32, (cells, wide), 1), picked, 0.0)
    mask[0:cells, :] = dot(picked.astype(BF16), jnp.ones((wide, ch), BF16))

    def load_main(start, size, carry):
        at = pl.ds(start, size)
        lv = mask[at, :]
        masked[at, :] = masked[at, :] * lv
        cotm[at, :] = cotm[at, :] * lv
        return carry

    chunked(load_main, 0)
    for side, start in ((0, 0), (1, cells - wide)):
        edge_send[side, 0] = masked[start:start + wide, :].astype(BF16)
        edge_send[side, 1] = mask[start:start + wide, :].astype(BF16)
        edge_send[side, 2] = cotm[start:start + wide, :].astype(BF16)

    acc[...] = jnp.zeros_like(acc)
    st_send[...] = jnp.zeros_like(st_send)

    pl.semaphore_wait(barrier, s_count - 1 + n - 1)

    def edge_copy(side):
        return pltpu.make_async_remote_copy(
            src_ref=edge_send.at[side], dst_ref=edge_recv.at[1 - side],
            send_sem=e_ssem.at[side], recv_sem=e_rsem.at[1 - side],
            device_id=(z, before if side == 0 else after), device_id_type=MESH)

    for side in range(2):
        edge_copy(side).start()

    w_parts = math.gcd(tap_rows // 16, s_count)
    w_rows = tap_rows // w_parts
    w_mine = s % w_parts
    w_group = s - w_mine

    def wz_copy(which, k):
        at = pl.ds(w_mine * w_rows, w_rows)
        slot = n - k - 1
        return pltpu.make_async_remote_copy(
            src_ref=wv.at[which, (z + k) % n, at, :], dst_ref=wf.at[which, slot, at, :],
            send_sem=wz_ssem.at[which, slot], recv_sem=wz_rsem.at[which, slot],
            device_id=((z + k) % n, s), device_id_type=MESH)

    def wp_copy(which, slot, k, whose):
        at = pl.ds(whose * w_rows, w_rows)
        return pltpu.make_async_remote_copy(
            src_ref=wf.at[which, slot, at, :], dst_ref=wf.at[which, slot, at, :],
            send_sem=wp_ssem.at[which, slot, k], recv_sem=wp_rsem.at[which, slot, whose],
            device_id=(z, w_group + (w_mine + k) % w_parts), device_id_type=MESH)

    def weights_over_z(which):
        for copy in w_copies[which * n:(which + 1) * n]:
            copy.wait()

        @pl.loop(1, n)
        def _(k):
            wz_copy(which, k).start()

    def slot_of(block):
        return (block - z + n - 1) % n

    def weights_round(which):
        @pl.loop(1, n)
        def _(distance):
            for sign in (1, -1):
                block = z - distance * sign

                @pl.when((block >= 0) & (block < n))
                def _():
                    slot = slot_of(block)
                    wz_copy(which, n - 1 - slot).wait_recv()

                    @pl.loop(1, w_parts)
                    def _(k):
                        wp_copy(which, slot, k, w_mine).start()

    def weights_arrived(which, slot):
        @pl.loop(1, w_parts)
        def _(k):
            wp_copy(which, slot, k, (w_mine + k) % w_parts).wait_recv()

    def row_copy(slot, side):
        return pltpu.make_async_remote_copy(
            src_ref=row_send.at[slot, side], dst_ref=row_recv.at[slot, 1 - side],
            send_sem=row_ssem.at[slot, side], recv_sem=row_rsem.at[slot, 1 - side],
            device_id=(z, before if side == 0 else after), device_id_type=MESH)

    def send_rows(slot, ref):
        for side, start in ((0, 0), (1, cells - wide)):
            row_send[slot, side] = ref[start:start + wide, :]
            row_copy(slot, side).start()

    def take_rows(slot, ref):
        for side in range(2):
            row_copy(slot, 1 - side).wait_recv()
            ref[cells + side * wide:cells + (side + 1) * wide, :] = row_recv[slot, side]

    def st_copy(slot, k, whose):
        return pltpu.make_async_remote_copy(
            src_ref=st_send.at[slot], dst_ref=st_recv.at[slot, whose],
            send_sem=st_ssem.at[slot, k], recv_sem=st_rsem.at[slot, whose],
            device_id=(z, (s + k) % s_count), device_id_type=MESH)

    def send_stats(slot, values):
        for i, v in enumerate(values):
            st_send[slot, i:i + 1, :] = v
        for k in range(1, s_count):
            st_copy(slot, k, s).start()
        st_recv[slot, s] = st_send[slot]

    def take_stats(slot):
        for k in range(1, s_count):
            st_copy(slot, k, (s + k) % s_count).wait_recv()

    strip = 8
    column = lax.broadcasted_iota(jnp.int32, (strip * wide, ch), 0) % wide

    def shift(target, first, count):
        size = count * wide
        where = column[:size]
        here = pad[pl.ds(8 + first * wide, size), :]
        left = jnp.where(where == 0, 0.0, pad[pl.ds(7 + first * wide, size), :])
        right = jnp.where(where == wide - 1, 0.0, pad[pl.ds(9 + first * wide, size), :])
        for b, v in enumerate((left, here, right)):
            target[pl.ds(first, count), :, b * ch:(b + 1) * ch] = v.astype(BF16).reshape(count, wide, ch)

    edge = 2 * wide
    ag_rows = ((0, edge + packed), (edge + packed, packed))
    band_rows = rows // HALVES

    def unpack_half(ph, block, q, target):
        if q == 0:
            pad[8:8 + wide, :] = hold[ph, block, 0:wide, :].astype(F32)
            pad[8 + wide + cells:8 + 2 * wide + cells, :] = hold[ph, block, wide:edge, :].astype(F32)
            shift(target, 0, 1)
            shift(target, rows + 1, 1)
        at = slice(8 + wide + q * band, 8 + wide + (q + 1) * band)
        source = masked if ph == 0 else hid

        @pl.when(block == z)
        def _():
            pad[at, :] = source[q * band:(q + 1) * band, :]

        @pl.when(block != z)
        def _():
            pad[at, :] = dot(unpack[q], hold[ph, block, edge + q * packed:edge + (q + 1) * packed, :])

        for i in range(band_rows // strip):
            shift(target, 1 + q * band_rows + i * strip, strip)

    def add_conv(q, field, taps, turned_taps=None):
        first, last = (0, band_rows - 1) if q == 0 else (band_rows - 1, rows)
        count = last - first
        lhs = field[first:last + 2, :, :].reshape((count + 2) * wide, 3 * ch)
        if turned_taps is None:
            value = dot(lhs, jnp.concatenate([taps(a) for a in range(3)], axis=1))
        else:
            rhs = jnp.concatenate([
                jnp.concatenate([turned_taps(3 * (2 - a) + 2 - b) for b in range(3)], axis=1) for a in range(3)], axis=0)
            value = lax.dot_general(lhs, rhs, (((1,), (1,)), ((), ())), preferred_element_type=F32)
        at = pl.ds(first * wide, count * wide)
        acc[at, :] = acc[at, :] + sum(
            value[a * wide:(a + count) * wide, a * ch:(a + 1) * ch] for a in range(3))

    def ag_copy(ph, block, q, sign):
        at = pl.ds(*ag_rows[q])
        return pltpu.make_async_remote_copy(
            src_ref=hold.at[ph, block, at, :], dst_ref=hold.at[ph, block, at, :],
            send_sem=ag_ssem.at[ph, (1 - sign) // 2, block, q], recv_sem=ag_rsem.at[ph, block, q],
            device_id=(z + sign, s), device_id_type=MESH)

    def pack_field(ph, source, fill=None, first=None):
        if fill is not None:
            fill(cells, edge, 0)
        hold[ph, z, 0:edge, :] = source[cells:cells + edge, :].astype(BF16)
        for q in range(HALVES):
            if first is not None:
                first(q)
            if fill is not None:
                chunked(fill, 0, q * band, band)
            hold[ph, z, edge + q * packed:edge + (q + 1) * packed, :] = dot(
                pack[q], source[q * band:(q + 1) * band, :].astype(BF16)).astype(BF16)
            for sign in (1, -1):
                @pl.when((z + sign >= 0) & (z + sign < n))
                def _():
                    ag_copy(ph, z, q, sign).start()

    def inside(slice_at):
        return (slice_at >= 0) & (slice_at < n)

    def take_and_pass(ph, k, q, sign, passes=True, takes=True):
        block = z - k * sign

        @pl.when((k > 0) & inside(block))
        def _():
            if passes and takes:
                ag_copy(ph, block, q, sign).wait_recv()

            @pl.when(inside(z + sign))
            def _():
                if passes:
                    if not takes:
                        ag_copy(ph, block, q, sign).wait_recv()
                    ag_copy(ph, block, q, sign).start()

            if not passes:
                @pl.when(jnp.logical_not(inside(z + sign)))
                def _():
                    ag_copy(ph, block, q, sign).wait_recv()

    near = jnp.where(z < n - n // 2, 1, 0)

    def consume_way(k, q, way, consume):
        block = z - k * (1 - 2 * way)

        @pl.when((k >= 0) & (k < n) & inside(block) & ((k > 0) | (way == near)))
        def _():
            consume(k, block, q)

    def take_both(ph, k, q, **how):
        @pl.loop(0, 2)
        def _(i):
            way = (near + i) % 2
            take_and_pass(ph, k, q, 1 - 2 * way, **how)

    def gather(ph, consume, each):
        @pl.loop(0, n)
        def _(k):
            for q in range(HALVES):
                take_both(ph, k, q)
                if q:
                    consume_way(k, q - 1, 1 - near, consume)
                else:
                    consume_way(k - 1, HALVES - 1, 1 - near, consume)
                consume_way(k, q, near, consume)
            each(k)

    def gather_passing_first(ph, consume, each):
        @pl.loop(0, n)
        def _(k):
            @pl.when(k == 1)
            def _():
                @pl.loop(1, n)
                def _(ahead):
                    for q in range(HALVES):
                        take_both(ph, ahead, q, takes=False)
            for q in range(HALVES):
                take_both(ph, k, q, passes=False)

                @pl.loop(0, 2)
                def _(i):
                    consume_way(k, q, (near + i) % 2, consume)
            each(k)

    last_pass = jnp.maximum(jnp.where(z < n - 1, z, 0), jnp.where(z > 0, n - 1 - z, 0))

    def forward(ph, field):
        def consume(k, block, q):
            into = taken.at[block]
            unpack_half(ph, block, q, into)

            @pl.when(k == 0)
            def _():
                add_conv(q, into, lambda a: wv[ph, z, 3 * a * ch:3 * (a + 1) * ch, :])

            @pl.when(k > 0)
            def _():
                slot = slot_of(block)
                if q == 0:
                    weights_arrived(ph, slot)
                add_conv(q, into, lambda a: wf[ph, slot, 3 * a * ch:3 * (a + 1) * ch, :])

        def each(k):
            if ph == 0:
                @pl.when(k == 0)
                def _():
                    weights_round(0)

                @pl.when(k == 1)
                def _():
                    weights_over_z(1)

            @pl.when(k == last_pass)
            def _():
                turn_field(ph, field)
        (gather if ph else gather_passing_first)(ph, consume, each)

    def turn_field(ph, field):
        main = [field[start:start + ch, :].T for start in range(0, cells, ch)]
        ends = field[cells:cells + edge, :]
        if edge < ch:
            ends = jnp.concatenate([ends, jnp.zeros((ch - edge, ch), F32)], axis=0)
        ends = ends.T
        for i, here in enumerate(main):
            left = jnp.concatenate(
                [ends[:, 0:wide] if i == 0 else main[i - 1][:, ch - wide:], here[:, 0:ch - wide]], axis=1)
            right = jnp.concatenate(
                [here[:, wide:], main[i + 1][:, 0:wide] if i + 1 < len(main) else ends[:, wide:edge]], axis=1)
            for a, v in enumerate((left, here, right)):
                x_t[ph, a * ch:(a + 1) * ch, i * ch:(i + 1) * ch] = v.astype(BF16)

    half_rows = tap_rows // 2
    owners = math.gcd(half_rows // 16, chips)
    piece = half_rows // owners

    def c_copy(ph, j):
        return pltpu.make_async_remote_copy(
            src_ref=psend.at[ph, j], dst_ref=crecv.at[ph, j],
            send_sem=c_ssem.at[ph, j], recv_sem=c_rsem.at[ph, j],
            device_id=(z, chip * 2 + 1 - core), device_id_type=MESH)

    def q_copy(ph, j, e, whose, owner):
        return pltpu.make_async_remote_copy(
            src_ref=hsend.at[ph, j, owner], dst_ref=qrecv.at[ph, j, whose],
            send_sem=q_ssem.at[ph, j, e], recv_sem=q_rsem.at[ph, j, whose],
            device_id=(z, ((chip + e) % chips) * 2 + core), device_id_type=MESH)

    def f_copy(ph, j, e, owner):
        return pltpu.make_async_remote_copy(
            src_ref=wout.at[ph, j, core, owner], dst_ref=wout.at[ph, j, core, owner],
            send_sem=f_ssem.at[ph, j, e], recv_sem=f_rsem.at[ph, j, owner],
            device_id=(z, ((chip + e) % chips) * 2 + core), device_id_type=MESH)

    def h_copy(ph, j, whose):
        return pltpu.make_async_remote_copy(
            src_ref=wout.at[ph, j, whose], dst_ref=wout.at[ph, j, whose],
            send_sem=h_ssem.at[ph, j], recv_sem=h_rsem.at[ph, j],
            device_id=(z, chip * 2 + 1 - core), device_id_type=MESH)

    def o_copy(ph, j):
        target = (out_wg1, out_wg2)[ph]
        if aligned:
            target = target.at[:, :, :, pl.ds(pl.multiple_of(j * ch, ch), ch)]
        else:
            target = target.at[j]
        return pltpu.make_async_copy(wout.at[ph, j], target, o_sem.at[ph, j])

    def sum_cores(ph, j):
        for o in range(owners):
            psend[ph, j, o] = part[ph, j, 1 - core, o].astype(BF16)
        c_copy(ph, j).start()

    def sum_chips(ph, j):
        c_copy(ph, j).wait_recv()
        for o in range(owners):
            v = part[ph, j, core, o] + crecv[ph, j, o].astype(F32)
            part[ph, j, core, o] = v
            hsend[ph, j, o] = v.astype(BF16)

        @pl.loop(1, chips)
        def _(e):
            peer = (chip + e) % chips

            @pl.when(peer < owners)
            def _():
                q_copy(ph, j, e, chip, peer).start()

    def spread_chips(ph, j):
        @pl.when(chip < owners)
        def _():
            @pl.loop(1, chips)
            def _(e):
                q_copy(ph, j, e, (chip + e) % chips, chip).wait_recv()
            v = part[ph, j, core, chip]
            for e in range(1, chips):
                v = v + qrecv[ph, j, (chip + e) % chips].astype(F32)
            wout[ph, j, core, chip] = v.astype(BF16)

            @pl.loop(1, chips)
            def _(e):
                f_copy(ph, j, e, chip).start()

    def spread_cores(ph, j):
        @pl.loop(1, chips)
        def _(e):
            peer = (chip + e) % chips

            @pl.when(peer < owners)
            def _():
                f_copy(ph, j, e, peer).wait_recv()
        h_copy(ph, j, core).start()

    def finish(ph, j):
        h_copy(ph, j, 1 - core).wait_recv()
        o_copy(ph, j).start()

    def put_part(ph, j, tap, value):
        start = tap * ch
        done = 0
        while done < ch:
            row = start + done
            side, o, at = row // half_rows, row % half_rows // piece, row % piece
            size = min(ch - done, piece - at)
            part[ph, j, side, o, at:at + size, :] = value[done:done + size, :]
            done += size

    stages = (sum_cores, sum_chips, spread_chips, spread_cores, finish)

    def of_step(k, fn):
        @pl.loop(0, 2)
        def _(way):
            block = z - k * (1 - 2 * way)

            @pl.when((k >= 0) & (k < n) & inside(block) & ((k > 0) | (way == 0)))
            def _():
                fn(block)

    passing = last_pass > 0

    def made_at(step):
        first = jnp.where(passing & (step > 0), jnp.where(step == last_pass, 1, step + 1), step)
        return first, step + 1

    def advance(ph, k):
        for age in range(1, len(stages)):
            step = k - age

            @pl.when((step >= 0) & (step < n))
            def _():
                @pl.loop(*made_at(step))
                def _(made):
                    of_step(made, functools.partial(stages[age], ph))

    def advance_all(ph, age):
        @pl.loop(0, n)
        def _(j):
            stages[age](ph, j)

    def field_grad(ph, block):
        grad = taken[block, 1:rows + 1, :, :].reshape(cells, 3 * ch)
        value = dot(x_t[ph], grad)
        for a in range(3):
            for b in range(3):
                put_part(ph, block, 3 * a + b, value[a * ch:(a + 1) * ch, (2 - b) * ch:(3 - b) * ch])

    def make_grad(ph, block):
        field_grad(ph, block)
        sum_cores(ph, block)

    def backward(ph):
        last = ph == 0

        def consume(k, block, q):
            into = taken.at[block]
            unpack_half(2 + ph, block, q, into)
            if last and q == HALVES - 1:
                @pl.when((k == 0) | (k >= last_pass))
                def _():
                    make_grad(ph, block)
            add_conv(q, into, None, lambda t: wv[ph, block, t * ch:(t + 1) * ch, :])

        def each(k):
            first, end = made_at(k)
            if last:
                @pl.loop(first, end - 1)
                def _(step):
                    of_step(step, functools.partial(make_grad, ph))
                advance(ph, k)
                for age in range(2, len(stages)):
                    @pl.when(k == age - 2)
                    def _():
                        advance_all(1, age)
            else:
                @pl.loop(first, jnp.where(passing | (k < n - 1), end, first))
                def _(step):
                    of_step(step, functools.partial(make_grad, ph))

                @pl.when(k == last_pass)
                def _():
                    to_flat(hid2, out_block)
        gather(2 + ph, consume, each)

    def fold(v):
        return jnp.sum(v.reshape(v.shape[0] // 8, 8, ch), axis=0)

    def flatten(v):
        return jnp.sum(v, axis=0, keepdims=True)

    zero = jnp.zeros((8, ch), F32)

    def local_moments(ref):
        def sums(start, size, carry):
            at = pl.ds(start, size)
            m = mask[at, :]
            return carry[0] + fold(ref[at, :] * m), carry[1] + fold(m)
        added, number = (flatten(v) for v in chunked(sums, (zero, zero)))
        middle = added / jnp.maximum(number, 1.0)

        def spread(start, size, carry):
            at = pl.ds(start, size)
            c = (ref[at, :] - middle) * mask[at, :]
            return carry + fold(c * c)
        return added, number, flatten(chunked(spread, zero))

    def moments(slot):
        take_stats(slot)
        got = [st_recv[slot, k] for k in range(s_count)]
        added = sum(g[0:1] for g in got)
        number = sum(g[1:2] for g in got)
        mean = added / number
        spread = 0.0
        for g in got:
            off = g[0:1] / jnp.maximum(g[1:2], 1.0) - mean
            spread = spread + (g[2:3] + g[1:2] * off * off)
        return mean, lax.rsqrt(spread / number + EPSILON), number

    def everywhere(fn):
        chunked(fn, 0)
        fn(cells, 2 * wide, 0)

    gain1, shift1, gain2, shift2 = (r[...] for r in (gain1_in, shift1_in, gain2_in, shift2_in))

    weights_over_z(0)

    below = lax.broadcasted_iota(jnp.int32, (band, band), 1) < lax.broadcasted_iota(jnp.int32, (band, band), 0)
    below = below.astype(F32).astype(BF16)

    def make_pack(h):
        lv = mask[h * band:(h + 1) * band, :]
        place = jnp.where(lv > 0.0, dot(below, lv.astype(BF16)), -1.0)
        places[h] = place
        across = place.T[0:1, :]
        spot = lax.broadcasted_iota(jnp.int32, (packed, band), 0).astype(F32)
        pack[h] = jnp.where(spot == across, 1.0, 0.0).astype(BF16)

    def make_unpack(h):
        for start in range(0, packed, ch):
            size = min(ch, packed - start)
            spot = start + lax.broadcasted_iota(jnp.int32, (band, size), 1)
            unpack[h, :, start:start + size] = jnp.where(
                places[h, :, :size] == spot.astype(F32), 1.0, 0.0).astype(BF16)

    for side in range(2):
        edge_copy(1 - side).wait_recv()
        there = jnp.where(s > 0, 1.0, 0.0) if side == 0 else jnp.where(s < s_count - 1, 1.0, 0.0)
        at = slice(cells + side * wide, cells + (side + 1) * wide)
        masked[at, :] = edge_recv[side, 0].astype(F32) * there
        mask[at, :] = edge_recv[side, 1].astype(F32) * there
        cotm[at, :] = edge_recv[side, 2].astype(F32) * there

    pack_field(0, masked, first=make_pack)
    for h in range(HALVES):
        make_unpack(h)
    forward(0, masked)
    send_rows(0, acc)
    send_stats(0, local_moments(acc))
    mean1, scale1, count = moments(0)

    def activate_one(start, size, carry):
        at = pl.ds(start, size)
        main = start is not cells
        nv = ((acc if main else normed1)[at, :] - mean1) * scale1
        normed1[at, :] = nv
        hid[at, :] = gelu_parts(nv * gain1 + shift1)[0] * mask[at, :]
        if main:
            acc[at, :] = jnp.zeros((size, ch), F32)
        return carry

    def slope_one(start, size, carry):
        at = pl.ds(start, size)
        slope1[at, :] = gelu_parts(normed1[at, :] * gain1 + shift1)[1] * mask[at, :]
        return carry

    take_rows(0, normed1)
    pack_field(1, hid, activate_one)
    weights_round(1)
    everywhere(slope_one)
    forward(1, hid)
    send_rows(1, acc)
    send_stats(1, local_moments(acc))
    mean2, scale2, _ = moments(1)

    def activate_two(source, start, size):
        at = pl.ds(start, size)
        nv = (source[at, :] - mean2) * scale2
        normed2[at, :] = nv
        value, slope = gelu_parts(nv * gain2 + shift2 + masked[at, :])
        t = cotm[at, :] * slope
        through[at, :] = t
        return value, nv, t

    def activate_main(start, size, carry):
        value, nv, t = activate_two(acc, start, size)
        at = pl.ds(start, size)
        hid2[at, :] = value * mask[at, :]
        acc[at, :] = jnp.zeros((size, ch), F32)
        return carry[0] + fold(t * nv), carry[1] + fold(t)

    send_stats(2, [flatten(v) for v in chunked(activate_main, (zero, zero))])
    take_rows(1, normed2)
    activate_two(normed2, cells, edge)

    def gradient_sums(slot):
        take_stats(slot)
        got = [st_recv[slot, k] for k in range(s_count)]
        return sum(g[0:1] for g in got), sum(g[1:2] for g in got)

    def norm_back(upstream, normed, gain, scale, sums):
        gain_grad, shift_grad = sums
        factor = gain * scale
        level, tilt = shift_grad / count, gain_grad / count

        def fill(start, size, carry):
            at = pl.ds(start, size)
            v = upstream[at, :] - mask[at, :] * (level + normed[at, :] * tilt)
            hid[at, :] = factor * v
            return carry
        return fill

    sums2 = gradient_sums(2)
    pack_field(3, hid, norm_back(through, normed2, gain2, scale2, sums2))
    backward(1)

    send_rows(2, acc)

    def inner_main(start, size, carry):
        at = pl.ds(start, size)
        v = acc[at, :] * slope1[at, :]
        slope1[at, :] = v
        acc[at, :] = jnp.zeros((size, ch), F32)
        return carry[0] + fold(v * normed1[at, :]), carry[1] + fold(v)

    send_stats(3, [flatten(v) for v in chunked(inner_main, (zero, zero))])

    @pl.when(jnp.logical_not(passing))
    def _():
        of_step(n - 1, functools.partial(make_grad, 1))
    for side in range(2):
        row_copy(2, 1 - side).wait_recv()
        at = slice(cells + side * wide, cells + (side + 1) * wide)
        slope1[at, :] = row_recv[2, side] * slope1[at, :]
    sums1 = gradient_sums(3)
    pack_field(2, hid, norm_back(slope1, normed1, gain1, scale1, sums1))
    advance_all(1, 1)
    backward(0)
    advance(0, n)

    def finish_input(start, size, carry):
        at = pl.ds(start, size)
        acc[at, :] = (acc[at, :] + through[at, :]) * mask[at, :]
        return carry

    chunked(finish_input, 0)
    to_flat(acc, out_input)
    out_gain1[...], out_shift1[...] = sums1
    out_gain2[...], out_shift2[...] = sums2
    for extra in range(1, len(stages) - 1):
        advance(0, n + extra)

    for side in range(2):
        edge_copy(side).wait_send()
        for slot in range(3):
            row_copy(slot, side).wait_send()

    @pl.loop(1, s_count)
    def _(k):
        for slot in range(4):
            st_copy(slot, k, s).wait_send()

    @pl.loop(1, n)
    def _(k):
        for which in range(2):
            wz_copy(which, k).wait_send()

    @pl.loop(1, w_parts)
    def _(k):
        for which in range(2):
            for slot in range(n - 1):
                wp_copy(which, slot, k, w_mine).wait_send()

    @pl.loop(0, n)
    def _(k):
        for sign in (1, -1):
            block = z - k * sign

            @pl.when((block >= 0) & (block < n) & (z + sign >= 0) & (z + sign < n))
            def _():
                for ph in range(4):
                    for q in range(HALVES):
                        ag_copy(ph, block, q, sign).wait_send()

    @pl.loop(0, n)
    def _(j):
        for ph in range(2):
            c_copy(ph, j).wait_send()
            h_copy(ph, j, core).wait_send()
            o_copy(ph, j).wait()

            @pl.loop(1, chips)
            def _(e):
                peer = (chip + e) % chips

                @pl.when(peer < owners)
                def _():
                    q_copy(ph, j, e, chip, peer).wait_send()

                @pl.when(chip < owners)
                def _():
                    f_copy(ph, j, e, chip).wait_send()


def finish_kernel(count, *refs):
    ins, outs = refs[:count], refs[count:2 * count]
    narrow, wide, in_sem, out_sem, take_sem, give_sem = refs[2 * count:2 * count + 6]
    held = refs[2 * count + 6:]
    rows = narrow.shape[1] // FINISH_PARTS
    parts = [(w, i, pl.ds(i * rows, rows)) for i in range(FINISH_PARTS) for w in range(2)]
    loads = [pltpu.make_async_copy(ins[w].at[at, :], narrow.at[w, at, :], in_sem.at[w, i]) for w, i, at in parts]
    stores = [pltpu.make_async_copy(wide.at[w, at, :], outs[w].at[at, :], out_sem.at[w, i]) for w, i, at in parts]
    takes = [pltpu.make_async_copy(ins[2 + k], v, take_sem.at[k]) for k, v in enumerate(held)]
    gives = [pltpu.make_async_copy(v, outs[2 + k], give_sem.at[k]) for k, v in enumerate(held)]
    for copy in loads + takes:
        copy.start()
    for load, store, (w, i, at) in zip(loads, stores, parts):
        load.wait()
        wide[w, at, :] = narrow[w, at, :].astype(F32)
        store.start()
    for take, give in zip(takes, gives):
        take.wait()
        give.start()
    for copy in stores + gives:
        copy.wait()


def per_device(n, s_count, blocks, weight_one, weight_two, gain_one, shift_one, gain_two, shift_two, cell_live, cotangent):
    rows, wide = cell_live.shape
    ch = blocks.shape[1] // wide
    cells = rows * wide
    total = cells + 2 * wide
    packed = -(-most_live(rows // HALVES, wide) // 16) * 16
    aligned = ch % 128 == 0
    chips = s_count // 2
    tap_rows = 9 * ch
    half_rows = tap_rows // 2
    owners = math.gcd(half_rows // 16, chips)
    piece = half_rows // owners

    if aligned:
        weight_one, weight_two = (w.reshape(tap_rows, n * ch) for w in (weight_one, weight_two))
    else:
        weight_one, weight_two = (
            w.reshape(tap_rows, n, ch).transpose(1, 0, 2) for w in (weight_one, weight_two))
    grad_shape = (2, owners, piece, n * ch) if aligned else (n, 2, owners, piece, ch)
    vmem = pl.BlockSpec(memory_space=pltpu.VMEM)
    hbm = pl.BlockSpec(memory_space=pl.ANY)
    sem = pltpu.SemaphoreType.DMA
    field = pltpu.VMEM((total, ch), F32)
    scratch = [
        pltpu.VMEM((ch * wide, 2 * rows), F32),
        pltpu.VMEM((2, n, tap_rows, ch), BF16),
        pltpu.VMEM((2, n - 1, tap_rows, ch), BF16),
        pltpu.VMEM((2, 3 * ch, cells), BF16),
        pltpu.VMEM((HALVES, packed, cells // HALVES), BF16),
        pltpu.VMEM((HALVES, cells // HALVES, packed), BF16),
        pltpu.VMEM((HALVES, cells // HALVES, ch), F32),
        pltpu.VMEM((2, 3, wide, ch), BF16),
        pltpu.VMEM((2, 3, wide, ch), BF16),
        field, field, field, field, field, field, field, field, field,
        pltpu.VMEM((total + 16, ch), F32),
        pltpu.VMEM((cells, ch), F32),
        pltpu.VMEM((4, n, 2 * wide + HALVES * packed, ch), BF16),
        pltpu.VMEM((n, rows + 2, wide, 3 * ch), BF16),
        pltpu.VMEM((2, n, 2, owners, piece, ch), F32),
        pltpu.VMEM((2, n, owners, piece, ch), BF16),
        pltpu.VMEM((2, n, owners, piece, ch), BF16),
        pltpu.VMEM((2, n, owners, piece, ch), BF16),
        pltpu.VMEM((2, n, chips, piece, ch), BF16),
        pltpu.VMEM((2, n, 2, owners, piece, ch), BF16),
        pltpu.VMEM((4, 8, ch), F32),
        pltpu.VMEM((4, s_count, 8, ch), F32),
        pltpu.VMEM((3, 2, wide, ch), F32),
        pltpu.VMEM((3, 2, wide, ch), F32),
        sem((2, n)),
        sem((2, n)), sem((2, n)),
        sem((2, n - 1, s_count)), sem((2, n - 1, s_count)),
        sem((2,)), sem((2,)),
        sem((4, 2, n, HALVES)), sem((4, n, HALVES)),
        sem((4, s_count)), sem((4, s_count)),
        sem((3, 2)), sem((3, 2)),
        sem((2, n)), sem((2, n)),
        sem((2, n, chips)), sem((2, n, chips)),
        sem((2, n, chips)), sem((2, n, chips)),
        sem((2, n)), sem((2, n)),
        sem((2, n)),
    ]
    block_out, input_grad, wg1, wg2, *sums = pl.pallas_call(
        functools.partial(block_kernel, n, s_count, rows, wide, ch, aligned, packed),
        out_shape=(
            jax.ShapeDtypeStruct((rows, ch * wide), BF16),
            jax.ShapeDtypeStruct((rows, ch * wide), F32),
            jax.ShapeDtypeStruct(grad_shape, BF16),
            jax.ShapeDtypeStruct(grad_shape, BF16),
            *[jax.ShapeDtypeStruct((1, ch), F32)] * 4,
        ),
        in_specs=[vmem] * 7 + [hbm] * 2,
        out_specs=(vmem, vmem, hbm, hbm, vmem, vmem, vmem, vmem),
        scratch_shapes=scratch,
        compiler_params=pltpu.CompilerParams(
            collective_id=0, has_side_effects=True, vmem_limit_bytes=60 * 1024 * 1024),
    )(blocks, cotangent, cell_live.T,
      *(v.reshape(1, ch) for v in (gain_one, shift_one, gain_two, shift_two)), weight_one, weight_two)

    if not aligned:
        def whole(grad):
            grad = grad.reshape(n, tap_rows, ch).transpose(1, 0, 2)
            return grad.astype(F32).reshape(9, ch, n * ch)
        return (block_out, input_grad, whole(wg1), whole(wg2), *(v.reshape(ch) for v in sums))

    wg1, wg2 = (w.reshape(tap_rows, n * ch) for w in (wg1, wg2))
    wide_grad = jax.ShapeDtypeStruct((tap_rows, n * ch), F32)
    moved = (block_out, input_grad, *sums)
    grad1, grad2, *moved = pl.pallas_call(
        functools.partial(finish_kernel, 2 + len(moved)),
        out_shape=(wide_grad, wide_grad, *(jax.ShapeDtypeStruct(v.shape, v.dtype) for v in moved)),
        in_specs=[pl.BlockSpec(memory_space=pl.ANY)] * (2 + len(moved)),
        out_specs=[pl.BlockSpec(memory_space=pl.ANY)] * (2 + len(moved)),
        scratch_shapes=[
            pltpu.VMEM((2, tap_rows, n * ch), BF16), pltpu.VMEM((2, tap_rows, n * ch), F32),
            sem((2, FINISH_PARTS)), sem((2, FINISH_PARTS)), sem((len(moved),)), sem((len(moved),)),
            *(pltpu.VMEM(v.shape, v.dtype) for v in moved),
        ],
        compiler_params=pltpu.CompilerParams(vmem_limit_bytes=64 * 1024 * 1024),
    )(wg1, wg2, *moved)
    block_out, input_grad, *sums = moved
    grads = (g.reshape(9, ch, n * ch) for g in (grad1, grad2))
    return (block_out, input_grad, *grads, *(v.reshape(ch) for v in sums))


def solution(mesh):
    return jax.shard_map(
        functools.partial(per_device, mesh.shape["chan"], mesh.shape["space"]),
        mesh=mesh,
        in_specs=(
            P("space", "chan"),
            P(None, "chan", None),
            P(None, "chan", None),
            P("chan"),
            P("chan"),
            P("chan"),
            P("chan"),
            P("space", None),
            P("space", "chan"),
        ),
        out_specs=(
            P("space", "chan"),
            P("space", "chan"),
            P(None, "chan", None),
            P(None, "chan", None),
            P("chan"),
            P("chan"),
            P("chan"),
            P("chan"),
        ),
        check_vma=False,
    )
```

```python
import functools
import math

import jax
import jax.numpy as jnp
from jax import lax
from jax.experimental import pallas as pl
from jax.experimental.pallas import tpu as pltpu
from jax.sharding import PartitionSpec as P

EPSILON = 1e-05
MESH = pl.DeviceIdType.MESH
F32 = jnp.float32
BF16 = jnp.bfloat16
ROOT_HALF = 0.7071067811865476
ROOT_TWO_PI = 0.3989422804014327
CHUNK = 64
FINISH_PARTS = 4
UNROLL = 2
HALVES = 2
LARGE, SMALL = 7, 3


def dot(a, b):
    return jnp.dot(a, b, preferred_element_type=F32)


def gelu_parts(v):
    upper = 0.5 * (1.0 + lax.erf(v * ROOT_HALF))
    slope = upper + v * (ROOT_TWO_PI * jnp.exp(-0.5 * v * v))
    return v * upper, slope


def most_live(rows, wide):
    units = (wide + 1) // (SMALL + 1)
    live_rows = rows - rows // (LARGE + 1)
    return min(rows * wide, math.ceil(units * live_rows * LARGE / 2))


def block_kernel(n, s_count, rows, wide, ch, aligned, packed, *refs):
    (x_in, cot_in, live_in, gain1_in, shift1_in, gain2_in, shift2_in, w1_hbm, w2_hbm) = refs[:9]
    (out_block, out_input, out_wg1, out_wg2, out_gain1, out_shift1, out_gain2, out_shift2) = refs[9:17]
    (turned, wv, wf, x_t, pack, unpack, places, edge_send, edge_recv, cot_send, cot_recv, cotm, mask, masked,
     normed1, normed2, through, slope1, hid, hid2, pad, acc, hold, taken,
     part, psend, crecv, hsend, qrecv, wout, st_send, st_recv, row_send, row_recv,
     w_sem, wz_ssem, wz_rsem, wp_ssem, wp_rsem, e_ssem, e_rsem, ce_ssem, ce_rsem, ag_ssem, ag_rsem,
     st_ssem, st_rsem, row_ssem, row_rsem, c_ssem, c_rsem, q_ssem, q_rsem,
     f_ssem, f_rsem, h_ssem, h_rsem, o_sem) = refs[17:]

    z = lax.axis_index("chan")
    s = lax.axis_index("space")
    cells = rows * wide
    total = cells + 2 * wide
    band = cells // HALVES
    core, chip, chips = s % 2, s // 2, s_count // 2
    before, after = (s + s_count - 1) % s_count, (s + 1) % s_count
    tap_rows = 9 * ch

    barrier = pltpu.get_barrier_semaphore()

    @pl.loop(1, s_count)
    def _(k):
        pl.semaphore_signal(barrier, inc=1, device_id=(z, (s + k) % s_count), device_id_type=MESH)

    @pl.loop(1, n)
    def _(k):
        pl.semaphore_signal(barrier, inc=1, device_id=((z + k) % n, s), device_id_type=MESH)

    w_copies = []
    for which, source in enumerate((w1_hbm, w2_hbm)):
        for d in range(n):
            block = source.at[:, d * ch:(d + 1) * ch] if aligned else source.at[d]
            w_copies.append(pltpu.make_async_copy(block, wv.at[which, d], w_sem.at[which, d]))
    for copy in w_copies:
        copy.start()

    def chunked(fn, init, first=0, count=cells):
        def step(i, carry):
            return fn(pl.multiple_of(first + i * CHUNK, CHUNK), CHUNK, carry)
        return lax.fori_loop(0, count // CHUNK, step, init, unroll=UNROLL)

    lanes = 128
    tiles = ch * wide // lanes

    def from_flat(flat, put):
        for i in range(tiles):
            turned[i * lanes:(i + 1) * lanes, 0:rows] = flat[:, i * lanes:(i + 1) * lanes].astype(F32).T
        for w in range(wide):
            put(pl.ds(w, rows, stride=wide), turned[pl.ds(w, ch, stride=wide), 0:rows].T)

    def to_flat(source, flat):
        for w in range(wide):
            turned[pl.ds(w, ch, stride=wide), 0:rows] = source[pl.ds(w, rows, stride=wide), :].T
        for i in range(tiles):
            flat[:, i * lanes:(i + 1) * lanes] = turned[i * lanes:(i + 1) * lanes, 0:rows].T.astype(flat.dtype)

    def put_masked(at, value):
        masked[at, :] = value

    from_flat(x_in, put_masked)

    cell = lax.broadcasted_iota(jnp.int32, (cells, rows), 0)
    pick = (cell // wide == lax.broadcasted_iota(jnp.int32, (cells, rows), 1)).astype(F32).astype(BF16)
    column_of = lax.broadcasted_iota(jnp.int32, (cells, wide), 0) % wide
    picked = lax.dot_general(pick, live_in[...].astype(BF16), (((1,), (1,)), ((), ())), preferred_element_type=F32)
    picked = jnp.where(column_of == lax.broadcasted_iota(jnp.int32, (cells, wide), 1), picked, 0.0)
    mask[0:cells, :] = dot(picked.astype(BF16), jnp.ones((wide, ch), BF16))

    def load_main(start, size, carry):
        at = pl.ds(start, size)
        lv = mask[at, :]
        masked[at, :] = masked[at, :] * lv
        return carry

    chunked(load_main, 0)
    for side, start in ((0, 0), (1, cells - wide)):
        edge_send[side, 0] = masked[start:start + wide, :].astype(BF16)
        edge_send[side, 1] = mask[start:start + wide, :].astype(BF16)

    acc[...] = jnp.zeros_like(acc)
    st_send[...] = jnp.zeros_like(st_send)

    pl.semaphore_wait(barrier, s_count - 1 + n - 1)

    def edge_copy(side):
        return pltpu.make_async_remote_copy(
            src_ref=edge_send.at[side], dst_ref=edge_recv.at[1 - side],
            send_sem=e_ssem.at[side], recv_sem=e_rsem.at[1 - side],
            device_id=(z, before if side == 0 else after), device_id_type=MESH)

    for side in range(2):
        edge_copy(side).start()

    def cot_copy(side):
        return pltpu.make_async_remote_copy(
            src_ref=cot_send.at[side], dst_ref=cot_recv.at[1 - side],
            send_sem=ce_ssem.at[side], recv_sem=ce_rsem.at[1 - side],
            device_id=(z, before if side == 0 else after), device_id_type=MESH)

    def load_cotangent():
        def put(at, value):
            cotm[at, :] = value
        from_flat(cot_in, put)

        def live_only(start, size, carry):
            at = pl.ds(start, size)
            cotm[at, :] = cotm[at, :] * mask[at, :]
            return carry
        chunked(live_only, 0)
        for side, start in ((0, 0), (1, cells - wide)):
            cot_send[side] = cotm[start:start + wide, :].astype(BF16)
            cot_copy(side).start()

    def take_cotangent():
        for side in range(2):
            cot_copy(1 - side).wait_recv()
            at = slice(cells + side * wide, cells + (side + 1) * wide)
            cotm[at, :] = cot_recv[side].astype(F32) * mask[at, :]

    w_parts = math.gcd(tap_rows // 16, s_count)
    w_rows = tap_rows // w_parts
    w_mine = s % w_parts
    w_group = s - w_mine

    def wz_copy(which, k):
        at = pl.ds(w_mine * w_rows, w_rows)
        slot = n - k - 1
        return pltpu.make_async_remote_copy(
            src_ref=wv.at[which, (z + k) % n, at, :], dst_ref=wf.at[which, slot, at, :],
            send_sem=wz_ssem.at[which, slot], recv_sem=wz_rsem.at[which, slot],
            device_id=((z + k) % n, s), device_id_type=MESH)

    def wp_copy(which, slot, k, whose):
        at = pl.ds(whose * w_rows, w_rows)
        return pltpu.make_async_remote_copy(
            src_ref=wf.at[which, slot, at, :], dst_ref=wf.at[which, slot, at, :],
            send_sem=wp_ssem.at[which, slot, k], recv_sem=wp_rsem.at[which, slot, whose],
            device_id=(z, w_group + (w_mine + k) % w_parts), device_id_type=MESH)

    def weights_over_z(which):
        for copy in w_copies[which * n:(which + 1) * n]:
            copy.wait()

        @pl.loop(1, n)
        def _(k):
            wz_copy(which, k).start()

    def slot_of(block):
        return (block - z + n - 1) % n

    def weights_round(which):
        @pl.loop(1, n)
        def _(distance):
            for sign in (1, -1):
                block = z - distance * sign

                @pl.when((block >= 0) & (block < n))
                def _():
                    slot = slot_of(block)
                    wz_copy(which, n - 1 - slot).wait_recv()

                    @pl.loop(1, w_parts)
                    def _(k):
                        wp_copy(which, slot, k, w_mine).start()

    def weights_arrived(which, slot):
        @pl.loop(1, w_parts)
        def _(k):
            wp_copy(which, slot, k, (w_mine + k) % w_parts).wait_recv()

    def row_copy(slot, side):
        return pltpu.make_async_remote_copy(
            src_ref=row_send.at[slot, side], dst_ref=row_recv.at[slot, 1 - side],
            send_sem=row_ssem.at[slot, side], recv_sem=row_rsem.at[slot, 1 - side],
            device_id=(z, before if side == 0 else after), device_id_type=MESH)

    def send_rows(slot, ref):
        for side, start in ((0, 0), (1, cells - wide)):
            row_send[slot, side] = ref[start:start + wide, :]
            row_copy(slot, side).start()

    def take_rows(slot, ref):
        for side in range(2):
            row_copy(slot, 1 - side).wait_recv()
            ref[cells + side * wide:cells + (side + 1) * wide, :] = row_recv[slot, side]

    def st_copy(slot, k, whose):
        return pltpu.make_async_remote_copy(
            src_ref=st_send.at[slot], dst_ref=st_recv.at[slot, whose],
            send_sem=st_ssem.at[slot, k], recv_sem=st_rsem.at[slot, whose],
            device_id=(z, (s + k) % s_count), device_id_type=MESH)

    def send_stats(slot, values):
        for i, v in enumerate(values):
            st_send[slot, i:i + 1, :] = v
        for k in range(1, s_count):
            st_copy(slot, k, s).start()
        st_recv[slot, s] = st_send[slot]

    def take_stats(slot):
        for k in range(1, s_count):
            st_copy(slot, k, (s + k) % s_count).wait_recv()

    strip = 8
    column = lax.broadcasted_iota(jnp.int32, (strip * wide, ch), 0) % wide

    def shift(target, first, count):
        size = count * wide
        where = column[:size]
        here = pad[pl.ds(8 + first * wide, size), :]
        left = jnp.where(where == 0, 0.0, pad[pl.ds(7 + first * wide, size), :])
        right = jnp.where(where == wide - 1, 0.0, pad[pl.ds(9 + first * wide, size), :])
        for b, v in enumerate((left, here, right)):
            target[pl.ds(first, count), :, b * ch:(b + 1) * ch] = v.astype(BF16).reshape(count, wide, ch)

    edge = 2 * wide
    ag_rows = ((0, edge + packed), (edge + packed, packed))
    band_rows = rows // HALVES

    def unpack_half(ph, block, q, target):
        if q == 0:
            pad[8:8 + wide, :] = hold[ph, block, 0:wide, :].astype(F32)
            pad[8 + wide + cells:8 + 2 * wide + cells, :] = hold[ph, block, wide:edge, :].astype(F32)
            shift(target, 0, 1)
            shift(target, rows + 1, 1)
        pad[8 + wide + q * band:8 + wide + (q + 1) * band, :] = dot(
            unpack[q], hold[ph, block, edge + q * packed:edge + (q + 1) * packed, :])

        for i in range(band_rows // strip):
            shift(target, 1 + q * band_rows + i * strip, strip)

    def add_conv(q, field, taps, turned_taps=None):
        first, last = (0, band_rows - 1) if q == 0 else (band_rows - 1, rows)
        count = last - first
        lhs = field[first:last + 2, :, :].reshape((count + 2) * wide, 3 * ch)
        if turned_taps is None:
            value = dot(lhs, jnp.concatenate([taps(a) for a in range(3)], axis=1))
        else:
            rhs = jnp.concatenate([
                jnp.concatenate([turned_taps(3 * (2 - a) + 2 - b) for b in range(3)], axis=1) for a in range(3)], axis=0)
            value = lax.dot_general(lhs, rhs, (((1,), (1,)), ((), ())), preferred_element_type=F32)
        at = pl.ds(first * wide, count * wide)
        acc[at, :] = acc[at, :] + sum(
            value[a * wide:(a + count) * wide, a * ch:(a + 1) * ch] for a in range(3))

    def ag_copy(ph, block, q, sign):
        at = pl.ds(*ag_rows[q])
        return pltpu.make_async_remote_copy(
            src_ref=hold.at[ph, block, at, :], dst_ref=hold.at[ph, block, at, :],
            send_sem=ag_ssem.at[ph, (1 - sign) // 2, block, q], recv_sem=ag_rsem.at[ph, block, q],
            device_id=(z + sign, s), device_id_type=MESH)

    def pack_field(ph, source, fill=None, first=None):
        if fill is not None:
            fill(cells, edge, 0)
        hold[ph, z, 0:edge, :] = source[cells:cells + edge, :].astype(BF16)
        for q in range(HALVES):
            if first is not None:
                first(q)
            if fill is not None:
                chunked(fill, 0, q * band, band)
            hold[ph, z, edge + q * packed:edge + (q + 1) * packed, :] = dot(
                pack[q], source[q * band:(q + 1) * band, :].astype(BF16)).astype(BF16)
            for sign in (1, -1):
                @pl.when((z + sign >= 0) & (z + sign < n))
                def _():
                    ag_copy(ph, z, q, sign).start()

    def inside(slice_at):
        return (slice_at >= 0) & (slice_at < n)

    def take_and_pass(ph, k, q, sign, passes=True, takes=True):
        block = z - k * sign

        @pl.when((k > 0) & inside(block))
        def _():
            if passes and takes:
                ag_copy(ph, block, q, sign).wait_recv()

            @pl.when(inside(z + sign))
            def _():
                if passes:
                    if not takes:
                        ag_copy(ph, block, q, sign).wait_recv()
                    ag_copy(ph, block, q, sign).start()

            if not passes:
                @pl.when(jnp.logical_not(inside(z + sign)))
                def _():
                    ag_copy(ph, block, q, sign).wait_recv()

    near = jnp.where(z < n - n // 2, 1, 0)

    def consume_way(k, q, way, consume):
        block = z - k * (1 - 2 * way)

        @pl.when((k >= 0) & (k < n) & inside(block) & ((k > 0) | (way == near)))
        def _():
            consume(k, block, q)

    def take_both(ph, k, q, **how):
        @pl.loop(0, 2)
        def _(i):
            way = (near + i) % 2
            take_and_pass(ph, k, q, 1 - 2 * way, **how)

    def gather(ph, consume, each):
        @pl.loop(0, n)
        def _(k):
            for q in range(HALVES):
                take_both(ph, k, q)
                if q:
                    consume_way(k, q - 1, 1 - near, consume)
                else:
                    consume_way(k - 1, HALVES - 1, 1 - near, consume)
                consume_way(k, q, near, consume)
            each(k)

    def gather_passing_first(ph, consume, each):
        @pl.loop(0, n)
        def _(k):
            @pl.when(k == 1)
            def _():
                @pl.loop(1, n)
                def _(ahead):
                    for q in range(HALVES):
                        take_both(ph, ahead, q, takes=False)
            for q in range(HALVES):
                take_both(ph, k, q, passes=False)

                @pl.loop(0, 2)
                def _(i):
                    consume_way(k, q, (near + i) % 2, consume)
            each(k)

    last_pass = jnp.maximum(jnp.where(z < n - 1, z, 0), jnp.where(z > 0, n - 1 - z, 0))

    def forward(ph, field):
        def consume(k, block, q):
            into = taken.at[block]
            unpack_half(ph, block, q, into)

            @pl.when(k == 0)
            def _():
                add_conv(q, into, lambda a: wv[ph, z, 3 * a * ch:3 * (a + 1) * ch, :])

            @pl.when(k > 0)
            def _():
                slot = slot_of(block)
                if q == 0:
                    weights_arrived(ph, slot)
                add_conv(q, into, lambda a: wf[ph, slot, 3 * a * ch:3 * (a + 1) * ch, :])

        def each(k):
            if ph == 0:
                @pl.when(k == 0)
                def _():
                    weights_round(1)

            @pl.when(k == last_pass)
            def _():
                turn_field(ph, field)
                if ph == 0:
                    load_cotangent()
        (gather if ph else gather_passing_first)(ph, consume, each)

    def turn_field(ph, field):
        main = [field[start:start + ch, :].T for start in range(0, cells, ch)]
        ends = field[cells:cells + edge, :]
        if edge < ch:
            ends = jnp.concatenate([ends, jnp.zeros((ch - edge, ch), F32)], axis=0)
        ends = ends.T
        for i, here in enumerate(main):
            left = jnp.concatenate(
                [ends[:, 0:wide] if i == 0 else main[i - 1][:, ch - wide:], here[:, 0:ch - wide]], axis=1)
            right = jnp.concatenate(
                [here[:, wide:], main[i + 1][:, 0:wide] if i + 1 < len(main) else ends[:, wide:edge]], axis=1)
            for a, v in enumerate((left, here, right)):
                x_t[ph, a * ch:(a + 1) * ch, i * ch:(i + 1) * ch] = v.astype(BF16)

    half_rows = tap_rows // 2
    owners = math.gcd(half_rows // 16, chips)
    piece = half_rows // owners

    def c_copy(ph, j):
        return pltpu.make_async_remote_copy(
            src_ref=psend.at[ph, j], dst_ref=crecv.at[ph, j],
            send_sem=c_ssem.at[ph, j], recv_sem=c_rsem.at[ph, j],
            device_id=(z, chip * 2 + 1 - core), device_id_type=MESH)

    def q_copy(ph, j, e, whose, owner):
        return pltpu.make_async_remote_copy(
            src_ref=hsend.at[ph, j, owner], dst_ref=qrecv.at[ph, j, whose],
            send_sem=q_ssem.at[ph, j, e], recv_sem=q_rsem.at[ph, j, whose],
            device_id=(z, ((chip + e) % chips) * 2 + core), device_id_type=MESH)

    def f_copy(ph, j, e, owner):
        return pltpu.make_async_remote_copy(
            src_ref=wout.at[ph, j, core, owner], dst_ref=wout.at[ph, j, core, owner],
            send_sem=f_ssem.at[ph, j, e], recv_sem=f_rsem.at[ph, j, owner],
            device_id=(z, ((chip + e) % chips) * 2 + core), device_id_type=MESH)

    def h_copy(ph, j, whose):
        return pltpu.make_async_remote_copy(
            src_ref=wout.at[ph, j, whose], dst_ref=wout.at[ph, j, whose],
            send_sem=h_ssem.at[ph, j], recv_sem=h_rsem.at[ph, j],
            device_id=(z, chip * 2 + 1 - core), device_id_type=MESH)

    def o_copy(ph, j):
        target = (out_wg1, out_wg2)[ph]
        if aligned:
            target = target.at[:, :, :, pl.ds(pl.multiple_of(j * ch, ch), ch)]
        else:
            target = target.at[j]
        return pltpu.make_async_copy(wout.at[ph, j], target, o_sem.at[ph, j])

    def sum_cores(ph, j):
        for o in range(owners):
            psend[ph, j, o] = part[ph, j, 1 - core, o].astype(BF16)
        c_copy(ph, j).start()

    def sum_chips(ph, j):
        c_copy(ph, j).wait_recv()
        for o in range(owners):
            v = part[ph, j, core, o] + crecv[ph, j, o].astype(F32)
            part[ph, j, core, o] = v
            hsend[ph, j, o] = v.astype(BF16)

        @pl.loop(1, chips)
        def _(e):
            peer = (chip + e) % chips

            @pl.when(peer < owners)
            def _():
                q_copy(ph, j, e, chip, peer).start()

    def spread_chips(ph, j):
        @pl.when(chip < owners)
        def _():
            @pl.loop(1, chips)
            def _(e):
                q_copy(ph, j, e, (chip + e) % chips, chip).wait_recv()
            v = part[ph, j, core, chip]
            for e in range(1, chips):
                v = v + qrecv[ph, j, (chip + e) % chips].astype(F32)
            wout[ph, j, core, chip] = v.astype(BF16)

            @pl.loop(1, chips)
            def _(e):
                f_copy(ph, j, e, chip).start()

    def spread_cores(ph, j):
        @pl.loop(1, chips)
        def _(e):
            peer = (chip + e) % chips

            @pl.when(peer < owners)
            def _():
                f_copy(ph, j, e, peer).wait_recv()
        h_copy(ph, j, core).start()

    def finish(ph, j):
        h_copy(ph, j, 1 - core).wait_recv()
        o_copy(ph, j).start()

    def put_part(ph, j, tap, value):
        start = tap * ch
        done = 0
        while done < ch:
            row = start + done
            side, o, at = row // half_rows, row % half_rows // piece, row % piece
            size = min(ch - done, piece - at)
            part[ph, j, side, o, at:at + size, :] = value[done:done + size, :]
            done += size

    stages = (sum_cores, sum_chips, spread_chips, spread_cores, finish)

    def of_step(k, fn):
        @pl.loop(0, 2)
        def _(way):
            block = z - k * (1 - 2 * way)

            @pl.when((k >= 0) & (k < n) & inside(block) & ((k > 0) | (way == 0)))
            def _():
                fn(block)

    passing = last_pass > 0

    def made_at(step):
        first = jnp.where(passing & (step > 0), jnp.where(step == last_pass, 1, step + 1), step)
        return first, step + 1

    def advance(ph, k):
        for age in range(1, len(stages)):
            step = k - age

            @pl.when((step >= 0) & (step < n))
            def _():
                @pl.loop(*made_at(step))
                def _(made):
                    of_step(made, functools.partial(stages[age], ph))

    def advance_all(ph, age):
        @pl.loop(0, n)
        def _(j):
            stages[age](ph, j)

    def field_grad(ph, block):
        grad = taken[block, 1:rows + 1, :, :].reshape(cells, 3 * ch)
        value = dot(x_t[ph], grad)
        for a in range(3):
            for b in range(3):
                put_part(ph, block, 3 * a + b, value[a * ch:(a + 1) * ch, (2 - b) * ch:(3 - b) * ch])

    def make_grad(ph, block):
        field_grad(ph, block)
        sum_cores(ph, block)

    def backward(ph):
        last = ph == 0

        def consume(k, block, q):
            into = taken.at[block]
            unpack_half(2 + ph, block, q, into)
            if last and q == HALVES - 1:
                @pl.when((k == 0) | (k >= last_pass))
                def _():
                    make_grad(ph, block)
            add_conv(q, into, None, lambda t: wv[ph, block, t * ch:(t + 1) * ch, :])

        def each(k):
            first, end = made_at(k)
            if last:
                @pl.loop(first, end - 1)
                def _(step):
                    of_step(step, functools.partial(make_grad, ph))
                advance(ph, k)
                for age in range(2, len(stages)):
                    @pl.when(k == age - 2)
                    def _():
                        advance_all(1, age)
            else:
                @pl.loop(first, jnp.where(passing | (k < n - 1), end, first))
                def _(step):
                    of_step(step, functools.partial(make_grad, ph))

                @pl.when(k == last_pass)
                def _():
                    to_flat(hid2, out_block)
        gather(2 + ph, consume, each)

    def fold(v):
        return jnp.sum(v.reshape(v.shape[0] // 8, 8, ch), axis=0)

    def flatten(v):
        return jnp.sum(v, axis=0, keepdims=True)

    zero = jnp.zeros((8, ch), F32)

    def local_moments(ref):
        def sums(start, size, carry):
            at = pl.ds(start, size)
            m = mask[at, :]
            return carry[0] + fold(ref[at, :] * m), carry[1] + fold(m)
        added, number = (flatten(v) for v in chunked(sums, (zero, zero)))
        middle = added / jnp.maximum(number, 1.0)

        def spread(start, size, carry):
            at = pl.ds(start, size)
            c = (ref[at, :] - middle) * mask[at, :]
            return carry + fold(c * c)
        return added, number, flatten(chunked(spread, zero))

    def moments(slot):
        take_stats(slot)
        got = [st_recv[slot, k] for k in range(s_count)]
        added = sum(g[0:1] for g in got)
        number = sum(g[1:2] for g in got)
        mean = added / number
        spread = 0.0
        for g in got:
            off = g[0:1] / jnp.maximum(g[1:2], 1.0) - mean
            spread = spread + (g[2:3] + g[1:2] * off * off)
        return mean, lax.rsqrt(spread / number + EPSILON), number

    def everywhere(fn):
        chunked(fn, 0)
        fn(cells, 2 * wide, 0)

    gain1, shift1, gain2, shift2 = (r[...] for r in (gain1_in, shift1_in, gain2_in, shift2_in))

    weights_over_z(0)
    weights_over_z(1)

    below = lax.broadcasted_iota(jnp.int32, (band, band), 1) < lax.broadcasted_iota(jnp.int32, (band, band), 0)
    below = below.astype(F32).astype(BF16)

    def make_pack(h):
        lv = mask[h * band:(h + 1) * band, :]
        place = jnp.where(lv > 0.0, dot(below, lv.astype(BF16)), -1.0)
        places[h] = place
        across = place.T[0:1, :]
        spot = lax.broadcasted_iota(jnp.int32, (packed, band), 0).astype(F32)
        pack[h] = jnp.where(spot == across, 1.0, 0.0).astype(BF16)

    def make_unpack(h):
        for start in range(0, packed, ch):
            size = min(ch, packed - start)
            spot = start + lax.broadcasted_iota(jnp.int32, (band, size), 1)
            unpack[h, :, start:start + size] = jnp.where(
                places[h, :, :size] == spot.astype(F32), 1.0, 0.0).astype(BF16)

    for side in range(2):
        edge_copy(1 - side).wait_recv()
        there = jnp.where(s > 0, 1.0, 0.0) if side == 0 else jnp.where(s < s_count - 1, 1.0, 0.0)
        at = slice(cells + side * wide, cells + (side + 1) * wide)
        masked[at, :] = edge_recv[side, 0].astype(F32) * there
        mask[at, :] = edge_recv[side, 1].astype(F32) * there

    pack_field(0, masked, first=make_pack)
    weights_round(0)
    for h in range(HALVES):
        make_unpack(h)
    forward(0, masked)
    send_rows(0, acc)
    send_stats(0, local_moments(acc))
    mean1, scale1, count = moments(0)

    def activate_one(start, size, carry):
        at = pl.ds(start, size)
        main = start is not cells
        nv = ((acc if main else normed1)[at, :] - mean1) * scale1
        normed1[at, :] = nv
        hid[at, :] = gelu_parts(nv * gain1 + shift1)[0] * mask[at, :]
        if main:
            acc[at, :] = jnp.zeros((size, ch), F32)
        return carry

    def slope_one(start, size, carry):
        at = pl.ds(start, size)
        slope1[at, :] = gelu_parts(normed1[at, :] * gain1 + shift1)[1] * mask[at, :]
        return carry

    take_rows(0, normed1)
    pack_field(1, hid, activate_one)
    everywhere(slope_one)
    forward(1, hid)
    send_rows(1, acc)
    send_stats(1, local_moments(acc))
    mean2, scale2, _ = moments(1)

    def activate_two(source, start, size):
        at = pl.ds(start, size)
        nv = (source[at, :] - mean2) * scale2
        normed2[at, :] = nv
        value, slope = gelu_parts(nv * gain2 + shift2 + masked[at, :])
        t = cotm[at, :] * slope
        through[at, :] = t
        return value, nv, t

    def activate_main(start, size, carry):
        value, nv, t = activate_two(acc, start, size)
        at = pl.ds(start, size)
        hid2[at, :] = value * mask[at, :]
        acc[at, :] = jnp.zeros((size, ch), F32)
        return carry[0] + fold(t * nv), carry[1] + fold(t)

    send_stats(2, [flatten(v) for v in chunked(activate_main, (zero, zero))])
    take_rows(1, normed2)
    take_cotangent()
    activate_two(normed2, cells, edge)

    def gradient_sums(slot):
        take_stats(slot)
        got = [st_recv[slot, k] for k in range(s_count)]
        return sum(g[0:1] for g in got), sum(g[1:2] for g in got)

    def norm_back(upstream, normed, gain, scale, sums):
        gain_grad, shift_grad = sums
        factor = gain * scale
        level, tilt = shift_grad / count, gain_grad / count

        def fill(start, size, carry):
            at = pl.ds(start, size)
            v = upstream[at, :] - mask[at, :] * (level + normed[at, :] * tilt)
            hid[at, :] = factor * v
            return carry
        return fill

    sums2 = gradient_sums(2)
    pack_field(3, hid, norm_back(through, normed2, gain2, scale2, sums2))
    backward(1)

    send_rows(2, acc)

    def inner_main(start, size, carry):
        at = pl.ds(start, size)
        v = acc[at, :] * slope1[at, :]
        slope1[at, :] = v
        acc[at, :] = jnp.zeros((size, ch), F32)
        return carry[0] + fold(v * normed1[at, :]), carry[1] + fold(v)

    send_stats(3, [flatten(v) for v in chunked(inner_main, (zero, zero))])

    @pl.when(jnp.logical_not(passing))
    def _():
        of_step(n - 1, functools.partial(make_grad, 1))
    for side in range(2):
        row_copy(2, 1 - side).wait_recv()
        at = slice(cells + side * wide, cells + (side + 1) * wide)
        slope1[at, :] = row_recv[2, side] * slope1[at, :]
    sums1 = gradient_sums(3)
    pack_field(2, hid, norm_back(slope1, normed1, gain1, scale1, sums1))
    advance_all(1, 1)
    backward(0)
    advance(0, n)

    def finish_input(start, size, carry):
        at = pl.ds(start, size)
        acc[at, :] = (acc[at, :] + through[at, :]) * mask[at, :]
        return carry

    chunked(finish_input, 0)
    to_flat(acc, out_input)
    out_gain1[...], out_shift1[...] = sums1
    out_gain2[...], out_shift2[...] = sums2
    for extra in range(1, len(stages) - 1):
        advance(0, n + extra)

    for side in range(2):
        edge_copy(side).wait_send()
        cot_copy(side).wait_send()
        for slot in range(3):
            row_copy(slot, side).wait_send()

    @pl.loop(1, s_count)
    def _(k):
        for slot in range(4):
            st_copy(slot, k, s).wait_send()

    @pl.loop(1, n)
    def _(k):
        for which in range(2):
            wz_copy(which, k).wait_send()

    @pl.loop(1, w_parts)
    def _(k):
        for which in range(2):
            for slot in range(n - 1):
                wp_copy(which, slot, k, w_mine).wait_send()

    @pl.loop(0, n)
    def _(k):
        for sign in (1, -1):
            block = z - k * sign

            @pl.when((block >= 0) & (block < n) & (z + sign >= 0) & (z + sign < n))
            def _():
                for ph in range(4):
                    for q in range(HALVES):
                        ag_copy(ph, block, q, sign).wait_send()

    @pl.loop(0, n)
    def _(j):
        for ph in range(2):
            c_copy(ph, j).wait_send()
            h_copy(ph, j, core).wait_send()
            o_copy(ph, j).wait()

            @pl.loop(1, chips)
            def _(e):
                peer = (chip + e) % chips

                @pl.when(peer < owners)
                def _():
                    q_copy(ph, j, e, chip, peer).wait_send()

                @pl.when(chip < owners)
                def _():
                    f_copy(ph, j, e, chip).wait_send()


def finish_kernel(count, *refs):
    ins, outs = refs[:count], refs[count:2 * count]
    narrow, wide, in_sem, out_sem, take_sem, give_sem = refs[2 * count:2 * count + 6]
    held = refs[2 * count + 6:]
    rows = narrow.shape[1] // FINISH_PARTS
    parts = [(w, i, pl.ds(i * rows, rows)) for i in range(FINISH_PARTS) for w in range(2)]
    loads = [pltpu.make_async_copy(ins[w].at[at, :], narrow.at[w, at, :], in_sem.at[w, i]) for w, i, at in parts]
    stores = [pltpu.make_async_copy(wide.at[w, at, :], outs[w].at[at, :], out_sem.at[w, i]) for w, i, at in parts]
    takes = [pltpu.make_async_copy(ins[2 + k], v, take_sem.at[k]) for k, v in enumerate(held)]
    gives = [pltpu.make_async_copy(v, outs[2 + k], give_sem.at[k]) for k, v in enumerate(held)]
    for copy in loads + takes:
        copy.start()
    for load, store, (w, i, at) in zip(loads, stores, parts):
        load.wait()
        wide[w, at, :] = narrow[w, at, :].astype(F32)
        store.start()
    for take, give in zip(takes, gives):
        take.wait()
        give.start()
    for copy in stores + gives:
        copy.wait()


def per_device(n, s_count, blocks, weight_one, weight_two, gain_one, shift_one, gain_two, shift_two, cell_live, cotangent):
    rows, wide = cell_live.shape
    ch = blocks.shape[1] // wide
    cells = rows * wide
    total = cells + 2 * wide
    packed = -(-most_live(rows // HALVES, wide) // 16) * 16
    aligned = ch % 128 == 0
    chips = s_count // 2
    tap_rows = 9 * ch
    half_rows = tap_rows // 2
    owners = math.gcd(half_rows // 16, chips)
    piece = half_rows // owners

    if aligned:
        weight_one, weight_two = (w.reshape(tap_rows, n * ch) for w in (weight_one, weight_two))
    else:
        weight_one, weight_two = (
            w.reshape(tap_rows, n, ch).transpose(1, 0, 2) for w in (weight_one, weight_two))
    grad_shape = (2, owners, piece, n * ch) if aligned else (n, 2, owners, piece, ch)
    vmem = pl.BlockSpec(memory_space=pltpu.VMEM)
    hbm = pl.BlockSpec(memory_space=pl.ANY)
    sem = pltpu.SemaphoreType.DMA
    field = pltpu.VMEM((total, ch), F32)
    scratch = [
        pltpu.VMEM((ch * wide, 128), F32),
        pltpu.VMEM((2, n, tap_rows, ch), BF16),
        pltpu.VMEM((2, n - 1, tap_rows, ch), BF16),
        pltpu.VMEM((2, 3 * ch, cells), BF16),
        pltpu.VMEM((HALVES, packed, cells // HALVES), BF16),
        pltpu.VMEM((HALVES, cells // HALVES, packed), BF16),
        pltpu.VMEM((HALVES, cells // HALVES, ch), F32),
        pltpu.VMEM((2, 2, wide, ch), BF16),
        pltpu.VMEM((2, 2, wide, ch), BF16),
        pltpu.VMEM((2, wide, ch), BF16),
        pltpu.VMEM((2, wide, ch), BF16),
        field, field, field, field, field, field, field, field, field,
        pltpu.VMEM((total + 16, ch), F32),
        pltpu.VMEM((cells, ch), F32),
        pltpu.VMEM((4, n, 2 * wide + HALVES * packed, ch), BF16),
        pltpu.VMEM((n, rows + 2, wide, 3 * ch), BF16),
        pltpu.VMEM((2, n, 2, owners, piece, ch), F32),
        pltpu.VMEM((2, n, owners, piece, ch), BF16),
        pltpu.VMEM((2, n, owners, piece, ch), BF16),
        pltpu.VMEM((2, n, owners, piece, ch), BF16),
        pltpu.VMEM((2, n, chips, piece, ch), BF16),
        pltpu.VMEM((2, n, 2, owners, piece, ch), BF16),
        pltpu.VMEM((4, 8, ch), F32),
        pltpu.VMEM((4, s_count, 8, ch), F32),
        pltpu.VMEM((3, 2, wide, ch), F32),
        pltpu.VMEM((3, 2, wide, ch), F32),
        sem((2, n)),
        sem((2, n)), sem((2, n)),
        sem((2, n - 1, s_count)), sem((2, n - 1, s_count)),
        sem((2,)), sem((2,)),
        sem((2,)), sem((2,)),
        sem((4, 2, n, HALVES)), sem((4, n, HALVES)),
        sem((4, s_count)), sem((4, s_count)),
        sem((3, 2)), sem((3, 2)),
        sem((2, n)), sem((2, n)),
        sem((2, n, chips)), sem((2, n, chips)),
        sem((2, n, chips)), sem((2, n, chips)),
        sem((2, n)), sem((2, n)),
        sem((2, n)),
    ]
    block_out, input_grad, wg1, wg2, *sums = pl.pallas_call(
        functools.partial(block_kernel, n, s_count, rows, wide, ch, aligned, packed),
        out_shape=(
            jax.ShapeDtypeStruct((rows, ch * wide), BF16),
            jax.ShapeDtypeStruct((rows, ch * wide), F32),
            jax.ShapeDtypeStruct(grad_shape, BF16),
            jax.ShapeDtypeStruct(grad_shape, BF16),
            *[jax.ShapeDtypeStruct((1, ch), F32)] * 4,
        ),
        in_specs=[vmem] * 7 + [hbm] * 2,
        out_specs=(vmem, vmem, hbm, hbm, vmem, vmem, vmem, vmem),
        scratch_shapes=scratch,
        compiler_params=pltpu.CompilerParams(
            collective_id=0, has_side_effects=True, vmem_limit_bytes=60 * 1024 * 1024),
    )(blocks, cotangent, cell_live.T,
      *(v.reshape(1, ch) for v in (gain_one, shift_one, gain_two, shift_two)), weight_one, weight_two)

    if not aligned:
        def whole(grad):
            grad = grad.reshape(n, tap_rows, ch).transpose(1, 0, 2)
            return grad.astype(F32).reshape(9, ch, n * ch)
        return (block_out, input_grad, whole(wg1), whole(wg2), *(v.reshape(ch) for v in sums))

    wg1, wg2 = (w.reshape(tap_rows, n * ch) for w in (wg1, wg2))
    wide_grad = jax.ShapeDtypeStruct((tap_rows, n * ch), F32)
    moved = (block_out, input_grad, *sums)
    grad1, grad2, *moved = pl.pallas_call(
        functools.partial(finish_kernel, 2 + len(moved)),
        out_shape=(wide_grad, wide_grad, *(jax.ShapeDtypeStruct(v.shape, v.dtype) for v in moved)),
        in_specs=[pl.BlockSpec(memory_space=pl.ANY)] * (2 + len(moved)),
        out_specs=[pl.BlockSpec(memory_space=pl.ANY)] * (2 + len(moved)),
        scratch_shapes=[
            pltpu.VMEM((2, tap_rows, n * ch), BF16), pltpu.VMEM((2, tap_rows, n * ch), F32),
            sem((2, FINISH_PARTS)), sem((2, FINISH_PARTS)), sem((len(moved),)), sem((len(moved),)),
            *(pltpu.VMEM(v.shape, v.dtype) for v in moved),
        ],
        compiler_params=pltpu.CompilerParams(vmem_limit_bytes=64 * 1024 * 1024),
    )(wg1, wg2, *moved)
    block_out, input_grad, *sums = moved
    grads = (g.reshape(9, ch, n * ch) for g in (grad1, grad2))
    return (block_out, input_grad, *grads, *(v.reshape(ch) for v in sums))


def solution(mesh):
    return jax.shard_map(
        functools.partial(per_device, mesh.shape["chan"], mesh.shape["space"]),
        mesh=mesh,
        in_specs=(
            P("space", "chan"),
            P(None, "chan", None),
            P(None, "chan", None),
            P("chan"),
            P("chan"),
            P("chan"),
            P("chan"),
            P("space", None),
            P("space", "chan"),
        ),
        out_specs=(
            P("space", "chan"),
            P("space", "chan"),
            P(None, "chan", None),
            P(None, "chan", None),
            P("chan"),
            P("chan"),
            P("chan"),
            P("chan"),
        ),
        check_vma=False,
    )
```

```python
import functools
import math

import jax
import jax.numpy as jnp
from jax import lax
from jax.experimental import pallas as pl
from jax.experimental.pallas import tpu as pltpu
from jax.sharding import PartitionSpec as P

EPSILON = 1e-05
MESH = pl.DeviceIdType.MESH
F32 = jnp.float32
BF16 = jnp.bfloat16
ROOT_HALF = 0.7071067811865476
ROOT_TWO_PI = 0.3989422804014327
CHUNK = 64
FINISH_PARTS = 4
UNROLL = 2
HALVES = 2
LARGE, SMALL = 7, 3


def dot(a, b):
    return jnp.dot(a, b, preferred_element_type=F32)


def gelu_parts(v):
    upper = 0.5 * (1.0 + lax.erf(v * ROOT_HALF))
    slope = upper + v * (ROOT_TWO_PI * jnp.exp(-0.5 * v * v))
    return v * upper, slope


def most_live(rows, wide):
    units = (wide + 1) // (SMALL + 1)
    live_rows = rows - rows // (LARGE + 1)
    return min(rows * wide, math.ceil(units * live_rows * LARGE / 2))


def block_kernel(n, s_count, rows, wide, ch, aligned, packed, *refs):
    (x_in, cot_in, live_in, gain1_in, shift1_in, gain2_in, shift2_in, w1_hbm, w2_hbm) = refs[:9]
    (out_block, out_input, out_wg1, out_wg2, out_gain1, out_shift1, out_gain2, out_shift2) = refs[9:17]
    (turned, wv, wf, x_t, pack, unpack, places, packed_taps, total_sum, rs_send, rs_recv, edge_send, edge_recv, cot_send, cot_recv, cotm, mask, masked,
     normed1, normed2, through, slope1, hid, hid2, pad, acc, hold, taken,
     part, psend, crecv, hsend, qrecv, wout, st_send, st_recv, row_send, row_recv,
     w_sem, wz_ssem, wz_rsem, wp_ssem, wp_rsem, rs_ssem, rs_rsem, e_ssem, e_rsem, ce_ssem, ce_rsem, ag_ssem, ag_rsem,
     st_ssem, st_rsem, row_ssem, row_rsem, c_ssem, c_rsem, q_ssem, q_rsem,
     f_ssem, f_rsem, h_ssem, h_rsem, o_sem) = refs[17:]

    z = lax.axis_index("chan")
    s = lax.axis_index("space")
    cells = rows * wide
    total = cells + 2 * wide
    band = cells // HALVES
    core, chip, chips = s % 2, s // 2, s_count // 2
    before, after = (s + s_count - 1) % s_count, (s + 1) % s_count
    tap_rows = 9 * ch

    barrier = pltpu.get_barrier_semaphore()

    @pl.loop(1, s_count)
    def _(k):
        pl.semaphore_signal(barrier, inc=1, device_id=(z, (s + k) % s_count), device_id_type=MESH)

    @pl.loop(1, n)
    def _(k):
        pl.semaphore_signal(barrier, inc=1, device_id=((z + k) % n, s), device_id_type=MESH)

    w_copies = []
    for which, source in enumerate((w1_hbm, w2_hbm)):
        for d in range(n):
            block = source.at[:, d * ch:(d + 1) * ch] if aligned else source.at[d]
            w_copies.append(pltpu.make_async_copy(block, wv.at[which, d], w_sem.at[which, d]))
    for copy in w_copies:
        copy.start()

    def chunked(fn, init, first=0, count=cells):
        def step(i, carry):
            return fn(pl.multiple_of(first + i * CHUNK, CHUNK), CHUNK, carry)
        return lax.fori_loop(0, count // CHUNK, step, init, unroll=UNROLL)

    lanes = 128
    tiles = ch * wide // lanes

    def from_flat(flat, put):
        for i in range(tiles):
            turned[i * lanes:(i + 1) * lanes, 0:rows] = flat[:, i * lanes:(i + 1) * lanes].astype(F32).T
        for w in range(wide):
            put(pl.ds(w, rows, stride=wide), turned[pl.ds(w, ch, stride=wide), 0:rows].T)

    def to_flat(source, flat):
        for w in range(wide):
            turned[pl.ds(w, ch, stride=wide), 0:rows] = source[pl.ds(w, rows, stride=wide), :].T
        for i in range(tiles):
            flat[:, i * lanes:(i + 1) * lanes] = turned[i * lanes:(i + 1) * lanes, 0:rows].T.astype(flat.dtype)

    def put_masked(at, value):
        masked[at, :] = value

    from_flat(x_in, put_masked)

    cell = lax.broadcasted_iota(jnp.int32, (cells, rows), 0)
    pick = (cell // wide == lax.broadcasted_iota(jnp.int32, (cells, rows), 1)).astype(F32).astype(BF16)
    column_of = lax.broadcasted_iota(jnp.int32, (cells, wide), 0) % wide
    picked = lax.dot_general(pick, live_in[...].astype(BF16), (((1,), (1,)), ((), ())), preferred_element_type=F32)
    picked = jnp.where(column_of == lax.broadcasted_iota(jnp.int32, (cells, wide), 1), picked, 0.0)
    mask[0:cells, :] = dot(picked.astype(BF16), jnp.ones((wide, ch), BF16))

    def load_main(start, size, carry):
        at = pl.ds(start, size)
        lv = mask[at, :]
        masked[at, :] = masked[at, :] * lv
        return carry

    chunked(load_main, 0)
    for side, start in ((0, 0), (1, cells - wide)):
        edge_send[side, 0] = masked[start:start + wide, :].astype(BF16)
        edge_send[side, 1] = mask[start:start + wide, :].astype(BF16)

    acc[...] = jnp.zeros_like(acc)
    st_send[...] = jnp.zeros_like(st_send)

    pl.semaphore_wait(barrier, s_count - 1 + n - 1)

    def edge_copy(side):
        return pltpu.make_async_remote_copy(
            src_ref=edge_send.at[side], dst_ref=edge_recv.at[1 - side],
            send_sem=e_ssem.at[side], recv_sem=e_rsem.at[1 - side],
            device_id=(z, before if side == 0 else after), device_id_type=MESH)

    for side in range(2):
        edge_copy(side).start()

    def cot_copy(side):
        return pltpu.make_async_remote_copy(
            src_ref=cot_send.at[side], dst_ref=cot_recv.at[1 - side],
            send_sem=ce_ssem.at[side], recv_sem=ce_rsem.at[1 - side],
            device_id=(z, before if side == 0 else after), device_id_type=MESH)

    def load_cotangent():
        def put(at, value):
            cotm[at, :] = value
        from_flat(cot_in, put)

        def live_only(start, size, carry):
            at = pl.ds(start, size)
            cotm[at, :] = cotm[at, :] * mask[at, :]
            return carry
        chunked(live_only, 0)
        for side, start in ((0, 0), (1, cells - wide)):
            cot_send[side] = cotm[start:start + wide, :].astype(BF16)
            cot_copy(side).start()

    def take_cotangent():
        for side in range(2):
            cot_copy(1 - side).wait_recv()
            at = slice(cells + side * wide, cells + (side + 1) * wide)
            cotm[at, :] = cot_recv[side].astype(F32) * mask[at, :]

    w_parts = math.gcd(tap_rows // 16, s_count)
    w_rows = tap_rows // w_parts
    w_mine = s % w_parts
    w_group = s - w_mine

    def wz_copy(k):
        at = pl.ds(w_mine * w_rows, w_rows)
        slot = n - k - 1
        return pltpu.make_async_remote_copy(
            src_ref=wv.at[1, (z + k) % n, at, :], dst_ref=wf.at[slot, at, :],
            send_sem=wz_ssem.at[slot], recv_sem=wz_rsem.at[slot],
            device_id=((z + k) % n, s), device_id_type=MESH)

    def wp_copy(slot, k, whose):
        at = pl.ds(whose * w_rows, w_rows)
        return pltpu.make_async_remote_copy(
            src_ref=wf.at[slot, at, :], dst_ref=wf.at[slot, at, :],
            send_sem=wp_ssem.at[slot, k], recv_sem=wp_rsem.at[slot, whose],
            device_id=(z, w_group + (w_mine + k) % w_parts), device_id_type=MESH)

    def weights_over_z():
        for copy in w_copies[n:]:
            copy.wait()

        @pl.loop(1, n)
        def _(k):
            wz_copy(k).start()

    def slot_of(block):
        return (block - z + n - 1) % n

    def weights_round():
        @pl.loop(1, n)
        def _(distance):
            for sign in (1, -1):
                block = z - distance * sign

                @pl.when((block >= 0) & (block < n))
                def _():
                    slot = slot_of(block)
                    wz_copy(n - 1 - slot).wait_recv()

                    @pl.loop(1, w_parts)
                    def _(k):
                        wp_copy(slot, k, w_mine).start()

    def weights_arrived(slot):
        @pl.loop(1, w_parts)
        def _(k):
            wp_copy(slot, k, (w_mine + k) % w_parts).wait_recv()

    def row_copy(slot, side):
        return pltpu.make_async_remote_copy(
            src_ref=row_send.at[slot, side], dst_ref=row_recv.at[slot, 1 - side],
            send_sem=row_ssem.at[slot, side], recv_sem=row_rsem.at[slot, 1 - side],
            device_id=(z, before if side == 0 else after), device_id_type=MESH)

    def send_rows(slot, ref):
        for side, start in ((0, 0), (1, cells - wide)):
            row_send[slot, side] = ref[start:start + wide, :]
            row_copy(slot, side).start()

    def take_rows(slot, ref):
        for side in range(2):
            row_copy(slot, 1 - side).wait_recv()
            ref[cells + side * wide:cells + (side + 1) * wide, :] = row_recv[slot, side]

    def st_copy(slot, k, whose):
        return pltpu.make_async_remote_copy(
            src_ref=st_send.at[slot], dst_ref=st_recv.at[slot, whose],
            send_sem=st_ssem.at[slot, k], recv_sem=st_rsem.at[slot, whose],
            device_id=(z, (s + k) % s_count), device_id_type=MESH)

    def send_stats(slot, values):
        for i, v in enumerate(values):
            st_send[slot, i:i + 1, :] = v
        for k in range(1, s_count):
            st_copy(slot, k, s).start()
        st_recv[slot, s] = st_send[slot]

    def take_stats(slot):
        for k in range(1, s_count):
            st_copy(slot, k, (s + k) % s_count).wait_recv()

    strip = 8
    column = lax.broadcasted_iota(jnp.int32, (strip * wide, ch), 0) % wide

    def shift(target, first, count):
        size = count * wide
        where = column[:size]
        here = pad[pl.ds(8 + first * wide, size), :]
        left = jnp.where(where == 0, 0.0, pad[pl.ds(7 + first * wide, size), :])
        right = jnp.where(where == wide - 1, 0.0, pad[pl.ds(9 + first * wide, size), :])
        for b, v in enumerate((left, here, right)):
            target[pl.ds(first, count), :, b * ch:(b + 1) * ch] = v.astype(BF16).reshape(count, wide, ch)

    edge = 2 * wide
    ag_rows = ((0, edge + packed), (edge + packed, packed))
    band_rows = rows // HALVES

    def unpack_half(ph, block, q, target):
        if q == 0:
            pad[8:8 + wide, :] = hold[ph, block, 0:wide, :].astype(F32)
            pad[8 + wide + cells:8 + 2 * wide + cells, :] = hold[ph, block, wide:edge, :].astype(F32)
            shift(target, 0, 1)
            shift(target, rows + 1, 1)
        pad[8 + wide + q * band:8 + wide + (q + 1) * band, :] = dot(
            unpack[q], hold[ph, block, edge + q * packed:edge + (q + 1) * packed, :])

        for i in range(band_rows // strip):
            shift(target, 1 + q * band_rows + i * strip, strip)

    def add_conv(q, field, taps, turned_taps=None):
        first, last = (0, band_rows - 1) if q == 0 else (band_rows - 1, rows)
        count = last - first
        lhs = field[first:last + 2, :, :].reshape((count + 2) * wide, 3 * ch)
        if turned_taps is None:
            value = dot(lhs, jnp.concatenate([taps(a) for a in range(3)], axis=1))
        else:
            rhs = jnp.concatenate([
                jnp.concatenate([turned_taps(3 * (2 - a) + 2 - b) for b in range(3)], axis=1) for a in range(3)], axis=0)
            value = lax.dot_general(lhs, rhs, (((1,), (1,)), ((), ())), preferred_element_type=F32)
        at = pl.ds(first * wide, count * wide)
        acc[at, :] = acc[at, :] + sum(
            value[a * wide:(a + count) * wide, a * ch:(a + 1) * ch] for a in range(3))

    def ag_copy(ph, block, q, sign):
        at = pl.ds(*ag_rows[q])
        return pltpu.make_async_remote_copy(
            src_ref=hold.at[ph, block, at, :], dst_ref=hold.at[ph, block, at, :],
            send_sem=ag_ssem.at[ph, (1 - sign) // 2, block, q], recv_sem=ag_rsem.at[ph, block, q],
            device_id=(z + sign, s), device_id_type=MESH)

    def pack_field(ph, source, fill):
        fill(cells, edge, 0)
        hold[ph, z, 0:edge, :] = source[cells:cells + edge, :].astype(BF16)
        for q in range(HALVES):
            chunked(fill, 0, q * band, band)
            hold[ph, z, edge + q * packed:edge + (q + 1) * packed, :] = dot(
                pack[q], source[q * band:(q + 1) * band, :].astype(BF16)).astype(BF16)
            for sign in (1, -1):
                @pl.when((z + sign >= 0) & (z + sign < n))
                def _():
                    ag_copy(ph, z, q, sign).start()

    def inside(slice_at):
        return (slice_at >= 0) & (slice_at < n)

    def take_and_pass(ph, k, q, sign):
        block = z - k * sign

        @pl.when((k > 0) & inside(block))
        def _():
            ag_copy(ph, block, q, sign).wait_recv()

            @pl.when(inside(z + sign))
            def _():
                ag_copy(ph, block, q, sign).start()

    near = jnp.where(z < n - n // 2, 1, 0)

    def consume_way(k, q, way, consume):
        block = z - k * (1 - 2 * way)

        @pl.when((k >= 0) & (k < n) & inside(block) & ((k > 0) | (way == near)))
        def _():
            consume(k, block, q)

    def take_both(ph, k, q):
        @pl.loop(0, 2)
        def _(i):
            way = (near + i) % 2
            take_and_pass(ph, k, q, 1 - 2 * way)

    def gather(ph, consume, each):
        @pl.loop(0, n)
        def _(k):
            for q in range(HALVES):
                take_both(ph, k, q)
                if q:
                    consume_way(k, q - 1, 1 - near, consume)
                else:
                    consume_way(k - 1, HALVES - 1, 1 - near, consume)
                consume_way(k, q, near, consume)
            each(k)

    last_pass = jnp.maximum(jnp.where(z < n - 1, z, 0), jnp.where(z > 0, n - 1 - z, 0))

    def rs_copy(way, d, q):
        return pltpu.make_async_remote_copy(
            src_ref=rs_send.at[way, d, q], dst_ref=rs_recv.at[way, d, q],
            send_sem=rs_ssem.at[way, d, q], recv_sem=rs_rsem.at[way, d, q],
            device_id=(z + 1 - 2 * way, s), device_id_type=MESH)

    def first_conv():
        into = taken.at[z]
        pad[8:8 + wide, :] = masked[cells:cells + wide, :]
        pad[8 + wide:8 + wide + cells, :] = masked[0:cells, :]
        pad[8 + wide + cells:8 + 2 * wide + cells, :] = masked[cells + wide:total, :]
        shift(into, 0, 1)
        shift(into, rows + 1, 1)

        def pack_taps(q):
            for i in range(band_rows // strip):
                shift(into, 1 + q * band_rows + i * strip, strip)
            if q + 1 < HALVES:
                shift(into, 1 + (q + 1) * band_rows, 1)
            for a in range(3):
                rows_at = into[q * band_rows + a:(q + 1) * band_rows + a, :, :].reshape(band, 3 * ch)
                packed_taps[q, :, 3 * a * ch:3 * (a + 1) * ch] = dot(pack[q], rows_at).astype(BF16)

        def send_sum(turn, q, way):
            i = turn - jnp.where(way == 0, z, n - 1 - z)
            d = jnp.where(way == 0, n - 1 - i, i)
            fed = inside(z - 1 + 2 * way)

            @pl.when((i >= 0) & jnp.where(way == 0, d > z, d < z))
            def _():
                v = dot(packed_taps[q], wv[0, d])

                @pl.when(fed)
                def _():
                    rs_copy(way, d, q).wait_recv()
                    rs_send[way, d, q] = (v + rs_recv[way, d, q].astype(F32)).astype(BF16)

                @pl.when(jnp.logical_not(fed))
                def _():
                    rs_send[way, d, q] = v.astype(BF16)
                rs_copy(way, d, q).start()

        for turn in range(n - 1):
            for q in range(HALVES):
                if turn == 0:
                    pack_taps(q)
                    if q == 0:
                        for copy in w_copies[:n]:
                            copy.wait()

                @pl.loop(0, 2)
                def _(i):
                    send_sum(turn, q, (near + i) % 2)
            if turn == 0:
                weights_round()
        turn_field(0, masked)
        for q in range(HALVES):
            total_sum[q] = dot(packed_taps[q], wv[0, z])
        for q in range(HALVES):
            for way in range(2):
                @pl.when(inside(z - 1 + 2 * way))
                def _():
                    rs_copy(way, z, q).wait_recv()
                    total_sum[q] = total_sum[q] + rs_recv[way, z, q].astype(F32)
            v = total_sum[q]
            high = v.astype(BF16)
            low = (v - high.astype(F32)).astype(BF16)
            acc[q * band:(q + 1) * band, :] = dot(unpack[q], high) + dot(unpack[q], low)

    def sums_sent():
        @pl.loop(0, n)
        def _(d):
            for way in range(2):
                @pl.when(jnp.where(way == 0, d > z, d < z))
                def _():
                    for q in range(HALVES):
                        rs_copy(way, d, q).wait_send()

    def second_conv():
        def consume(k, block, q):
            into = taken.at[block]
            unpack_half(1, block, q, into)

            @pl.when(k == 0)
            def _():
                add_conv(q, into, lambda a: wv[1, z, 3 * a * ch:3 * (a + 1) * ch, :])

            @pl.when(k > 0)
            def _():
                slot = slot_of(block)
                if q == 0:
                    weights_arrived(slot)
                add_conv(q, into, lambda a: wf[slot, 3 * a * ch:3 * (a + 1) * ch, :])

        def each(k):
            @pl.when(k == last_pass)
            def _():
                turn_field(1, hid)
                load_cotangent()
        gather(1, consume, each)

    def turn_field(ph, field):
        main = [field[start:start + ch, :].T for start in range(0, cells, ch)]
        ends = field[cells:cells + edge, :]
        if edge < ch:
            ends = jnp.concatenate([ends, jnp.zeros((ch - edge, ch), F32)], axis=0)
        ends = ends.T
        for i, here in enumerate(main):
            left = jnp.concatenate(
                [ends[:, 0:wide] if i == 0 else main[i - 1][:, ch - wide:], here[:, 0:ch - wide]], axis=1)
            right = jnp.concatenate(
                [here[:, wide:], main[i + 1][:, 0:wide] if i + 1 < len(main) else ends[:, wide:edge]], axis=1)
            for a, v in enumerate((left, here, right)):
                x_t[ph, a * ch:(a + 1) * ch, i * ch:(i + 1) * ch] = v.astype(BF16)

    half_rows = tap_rows // 2
    owners = math.gcd(half_rows // 16, chips)
    piece = half_rows // owners

    def c_copy(ph, j):
        return pltpu.make_async_remote_copy(
            src_ref=psend.at[ph, j], dst_ref=crecv.at[ph, j],
            send_sem=c_ssem.at[ph, j], recv_sem=c_rsem.at[ph, j],
            device_id=(z, chip * 2 + 1 - core), device_id_type=MESH)

    def q_copy(ph, j, e, whose, owner):
        return pltpu.make_async_remote_copy(
            src_ref=hsend.at[ph, j, owner], dst_ref=qrecv.at[ph, j, whose],
            send_sem=q_ssem.at[ph, j, e], recv_sem=q_rsem.at[ph, j, whose],
            device_id=(z, ((chip + e) % chips) * 2 + core), device_id_type=MESH)

    def f_copy(ph, j, e, owner):
        return pltpu.make_async_remote_copy(
            src_ref=wout.at[ph, j, core, owner], dst_ref=wout.at[ph, j, core, owner],
            send_sem=f_ssem.at[ph, j, e], recv_sem=f_rsem.at[ph, j, owner],
            device_id=(z, ((chip + e) % chips) * 2 + core), device_id_type=MESH)

    def h_copy(ph, j, whose):
        return pltpu.make_async_remote_copy(
            src_ref=wout.at[ph, j, whose], dst_ref=wout.at[ph, j, whose],
            send_sem=h_ssem.at[ph, j], recv_sem=h_rsem.at[ph, j],
            device_id=(z, chip * 2 + 1 - core), device_id_type=MESH)

    def o_copy(ph, j):
        target = (out_wg1, out_wg2)[ph]
        if aligned:
            target = target.at[:, :, :, pl.ds(pl.multiple_of(j * ch, ch), ch)]
        else:
            target = target.at[j]
        return pltpu.make_async_copy(wout.at[ph, j], target, o_sem.at[ph, j])

    def sum_cores(ph, j):
        for o in range(owners):
            psend[ph, j, o] = part[ph, j, 1 - core, o].astype(BF16)
        c_copy(ph, j).start()

    def sum_chips(ph, j):
        c_copy(ph, j).wait_recv()
        for o in range(owners):
            v = part[ph, j, core, o] + crecv[ph, j, o].astype(F32)
            part[ph, j, core, o] = v
            hsend[ph, j, o] = v.astype(BF16)

        @pl.loop(1, chips)
        def _(e):
            peer = (chip + e) % chips

            @pl.when(peer < owners)
            def _():
                q_copy(ph, j, e, chip, peer).start()

    def spread_chips(ph, j):
        @pl.when(chip < owners)
        def _():
            @pl.loop(1, chips)
            def _(e):
                q_copy(ph, j, e, (chip + e) % chips, chip).wait_recv()
            v = part[ph, j, core, chip]
            for e in range(1, chips):
                v = v + qrecv[ph, j, (chip + e) % chips].astype(F32)
            wout[ph, j, core, chip] = v.astype(BF16)

            @pl.loop(1, chips)
            def _(e):
                f_copy(ph, j, e, chip).start()

    def spread_cores(ph, j):
        @pl.loop(1, chips)
        def _(e):
            peer = (chip + e) % chips

            @pl.when(peer < owners)
            def _():
                f_copy(ph, j, e, peer).wait_recv()
        h_copy(ph, j, core).start()

    def finish(ph, j):
        h_copy(ph, j, 1 - core).wait_recv()
        o_copy(ph, j).start()

    def put_part(ph, j, tap, value):
        start = tap * ch
        done = 0
        while done < ch:
            row = start + done
            side, o, at = row // half_rows, row % half_rows // piece, row % piece
            size = min(ch - done, piece - at)
            part[ph, j, side, o, at:at + size, :] = value[done:done + size, :]
            done += size

    stages = (sum_cores, sum_chips, spread_chips, spread_cores, finish)

    def of_step(k, fn):
        @pl.loop(0, 2)
        def _(way):
            block = z - k * (1 - 2 * way)

            @pl.when((k >= 0) & (k < n) & inside(block) & ((k > 0) | (way == 0)))
            def _():
                fn(block)

    passing = last_pass > 0

    def made_at(step):
        first = jnp.where(passing & (step > 0), jnp.where(step == last_pass, 1, step + 1), step)
        return first, step + 1

    def advance(ph, k):
        for age in range(1, len(stages)):
            step = k - age

            @pl.when((step >= 0) & (step < n))
            def _():
                @pl.loop(*made_at(step))
                def _(made):
                    of_step(made, functools.partial(stages[age], ph))

    def advance_all(ph, age):
        @pl.loop(0, n)
        def _(j):
            stages[age](ph, j)

    def field_grad(ph, block):
        grad = taken[block, 1:rows + 1, :, :].reshape(cells, 3 * ch)
        value = dot(x_t[ph], grad)
        for a in range(3):
            for b in range(3):
                put_part(ph, block, 3 * a + b, value[a * ch:(a + 1) * ch, (2 - b) * ch:(3 - b) * ch])

    def make_grad(ph, block):
        field_grad(ph, block)
        sum_cores(ph, block)

    def backward(ph):
        last = ph == 0

        def consume(k, block, q):
            into = taken.at[block]
            unpack_half(2 + ph, block, q, into)
            if last and q == HALVES - 1:
                @pl.when((k == 0) | (k >= last_pass))
                def _():
                    make_grad(ph, block)
            add_conv(q, into, None, lambda t: wv[ph, block, t * ch:(t + 1) * ch, :])

        def each(k):
            first, end = made_at(k)
            if last:
                @pl.loop(first, end - 1)
                def _(step):
                    of_step(step, functools.partial(make_grad, ph))
                advance(ph, k)
                for age in range(2, len(stages)):
                    @pl.when(k == age - 2)
                    def _():
                        advance_all(1, age)
            else:
                @pl.loop(first, jnp.where(passing | (k < n - 1), end, first))
                def _(step):
                    of_step(step, functools.partial(make_grad, ph))

                @pl.when(k == last_pass)
                def _():
                    to_flat(hid2, out_block)
        gather(2 + ph, consume, each)

    def fold(v):
        return jnp.sum(v.reshape(v.shape[0] // 8, 8, ch), axis=0)

    def flatten(v):
        return jnp.sum(v, axis=0, keepdims=True)

    zero = jnp.zeros((8, ch), F32)

    def local_moments(ref):
        def sums(start, size, carry):
            at = pl.ds(start, size)
            m = mask[at, :]
            return carry[0] + fold(ref[at, :] * m), carry[1] + fold(m)
        added, number = (flatten(v) for v in chunked(sums, (zero, zero)))
        middle = added / jnp.maximum(number, 1.0)

        def spread(start, size, carry):
            at = pl.ds(start, size)
            c = (ref[at, :] - middle) * mask[at, :]
            return carry + fold(c * c)
        return added, number, flatten(chunked(spread, zero))

    def moments(slot):
        take_stats(slot)
        got = [st_recv[slot, k] for k in range(s_count)]
        added = sum(g[0:1] for g in got)
        number = sum(g[1:2] for g in got)
        mean = added / number
        spread = 0.0
        for g in got:
            off = g[0:1] / jnp.maximum(g[1:2], 1.0) - mean
            spread = spread + (g[2:3] + g[1:2] * off * off)
        return mean, lax.rsqrt(spread / number + EPSILON), number

    def everywhere(fn):
        chunked(fn, 0)
        fn(cells, 2 * wide, 0)

    gain1, shift1, gain2, shift2 = (r[...] for r in (gain1_in, shift1_in, gain2_in, shift2_in))

    weights_over_z()

    below = lax.broadcasted_iota(jnp.int32, (band, band), 1) < lax.broadcasted_iota(jnp.int32, (band, band), 0)
    below = below.astype(F32).astype(BF16)

    def make_pack(h):
        lv = mask[h * band:(h + 1) * band, :]
        place = jnp.where(lv > 0.0, dot(below, lv.astype(BF16)), -1.0)
        places[h] = place
        across = place.T[0:1, :]
        spot = lax.broadcasted_iota(jnp.int32, (packed, band), 0).astype(F32)
        pack[h] = jnp.where(spot == across, 1.0, 0.0).astype(BF16)

    def make_unpack(h):
        for start in range(0, packed, ch):
            size = min(ch, packed - start)
            spot = start + lax.broadcasted_iota(jnp.int32, (band, size), 1)
            unpack[h, :, start:start + size] = jnp.where(
                places[h, :, :size] == spot.astype(F32), 1.0, 0.0).astype(BF16)

    for h in range(HALVES):
        make_pack(h)
        make_unpack(h)

    for side in range(2):
        edge_copy(1 - side).wait_recv()
        there = jnp.where(s > 0, 1.0, 0.0) if side == 0 else jnp.where(s < s_count - 1, 1.0, 0.0)
        at = slice(cells + side * wide, cells + (side + 1) * wide)
        masked[at, :] = edge_recv[side, 0].astype(F32) * there
        mask[at, :] = edge_recv[side, 1].astype(F32) * there

    first_conv()
    send_stats(0, local_moments(acc))
    send_rows(0, acc)
    mean1, scale1, count = moments(0)

    def activate_one(start, size, carry):
        at = pl.ds(start, size)
        main = start is not cells
        nv = ((acc if main else normed1)[at, :] - mean1) * scale1
        normed1[at, :] = nv
        hid[at, :] = gelu_parts(nv * gain1 + shift1)[0] * mask[at, :]
        if main:
            acc[at, :] = jnp.zeros((size, ch), F32)
        return carry

    def slope_one(start, size, carry):
        at = pl.ds(start, size)
        slope1[at, :] = gelu_parts(normed1[at, :] * gain1 + shift1)[1] * mask[at, :]
        return carry

    take_rows(0, normed1)
    pack_field(1, hid, activate_one)
    everywhere(slope_one)
    second_conv()
    send_rows(1, acc)
    send_stats(1, local_moments(acc))
    mean2, scale2, _ = moments(1)

    def activate_two(source, start, size):
        at = pl.ds(start, size)
        nv = (source[at, :] - mean2) * scale2
        normed2[at, :] = nv
        value, slope = gelu_parts(nv * gain2 + shift2 + masked[at, :])
        t = cotm[at, :] * slope
        through[at, :] = t
        return value, nv, t

    def activate_main(start, size, carry):
        value, nv, t = activate_two(acc, start, size)
        at = pl.ds(start, size)
        hid2[at, :] = value * mask[at, :]
        acc[at, :] = jnp.zeros((size, ch), F32)
        return carry[0] + fold(t * nv), carry[1] + fold(t)

    send_stats(2, [flatten(v) for v in chunked(activate_main, (zero, zero))])
    take_rows(1, normed2)
    take_cotangent()
    activate_two(normed2, cells, edge)

    def gradient_sums(slot):
        take_stats(slot)
        got = [st_recv[slot, k] for k in range(s_count)]
        return sum(g[0:1] for g in got), sum(g[1:2] for g in got)

    def norm_back(upstream, normed, gain, scale, sums):
        gain_grad, shift_grad = sums
        factor = gain * scale
        level, tilt = shift_grad / count, gain_grad / count

        def fill(start, size, carry):
            at = pl.ds(start, size)
            v = upstream[at, :] - mask[at, :] * (level + normed[at, :] * tilt)
            hid[at, :] = factor * v
            return carry
        return fill

    sums2 = gradient_sums(2)
    pack_field(3, hid, norm_back(through, normed2, gain2, scale2, sums2))
    backward(1)

    send_rows(2, acc)

    def inner_main(start, size, carry):
        at = pl.ds(start, size)
        v = acc[at, :] * slope1[at, :]
        slope1[at, :] = v
        acc[at, :] = jnp.zeros((size, ch), F32)
        return carry[0] + fold(v * normed1[at, :]), carry[1] + fold(v)

    send_stats(3, [flatten(v) for v in chunked(inner_main, (zero, zero))])

    @pl.when(jnp.logical_not(passing))
    def _():
        of_step(n - 1, functools.partial(make_grad, 1))
    for side in range(2):
        row_copy(2, 1 - side).wait_recv()
        at = slice(cells + side * wide, cells + (side + 1) * wide)
        slope1[at, :] = row_recv[2, side] * slope1[at, :]
    sums1 = gradient_sums(3)
    pack_field(2, hid, norm_back(slope1, normed1, gain1, scale1, sums1))
    advance_all(1, 1)
    backward(0)
    advance(0, n)

    def finish_input(start, size, carry):
        at = pl.ds(start, size)
        acc[at, :] = (acc[at, :] + through[at, :]) * mask[at, :]
        return carry

    chunked(finish_input, 0)
    to_flat(acc, out_input)
    out_gain1[...], out_shift1[...] = sums1
    out_gain2[...], out_shift2[...] = sums2
    for extra in range(1, len(stages) - 1):
        advance(0, n + extra)

    for side in range(2):
        edge_copy(side).wait_send()
        cot_copy(side).wait_send()
        for slot in range(3):
            row_copy(slot, side).wait_send()

    @pl.loop(1, s_count)
    def _(k):
        for slot in range(4):
            st_copy(slot, k, s).wait_send()

    @pl.loop(1, n)
    def _(k):
        wz_copy(k).wait_send()

    @pl.loop(1, w_parts)
    def _(k):
        for slot in range(n - 1):
            wp_copy(slot, k, w_mine).wait_send()
    sums_sent()

    @pl.loop(0, n)
    def _(k):
        for sign in (1, -1):
            block = z - k * sign

            @pl.when((block >= 0) & (block < n) & (z + sign >= 0) & (z + sign < n))
            def _():
                for ph in range(1, 4):
                    for q in range(HALVES):
                        ag_copy(ph, block, q, sign).wait_send()

    @pl.loop(0, n)
    def _(j):
        for ph in range(2):
            c_copy(ph, j).wait_send()
            h_copy(ph, j, core).wait_send()
            o_copy(ph, j).wait()

            @pl.loop(1, chips)
            def _(e):
                peer = (chip + e) % chips

                @pl.when(peer < owners)
                def _():
                    q_copy(ph, j, e, chip, peer).wait_send()

                @pl.when(chip < owners)
                def _():
                    f_copy(ph, j, e, chip).wait_send()


def finish_kernel(count, *refs):
    ins, outs = refs[:count], refs[count:2 * count]
    narrow, wide, in_sem, out_sem, take_sem, give_sem = refs[2 * count:2 * count + 6]
    held = refs[2 * count + 6:]
    rows = narrow.shape[1] // FINISH_PARTS
    parts = [(w, i, pl.ds(i * rows, rows)) for i in range(FINISH_PARTS) for w in range(2)]
    loads = [pltpu.make_async_copy(ins[w].at[at, :], narrow.at[w, at, :], in_sem.at[w, i]) for w, i, at in parts]
    stores = [pltpu.make_async_copy(wide.at[w, at, :], outs[w].at[at, :], out_sem.at[w, i]) for w, i, at in parts]
    takes = [pltpu.make_async_copy(ins[2 + k], v, take_sem.at[k]) for k, v in enumerate(held)]
    gives = [pltpu.make_async_copy(v, outs[2 + k], give_sem.at[k]) for k, v in enumerate(held)]
    for copy in loads + takes:
        copy.start()
    for load, store, (w, i, at) in zip(loads, stores, parts):
        load.wait()
        wide[w, at, :] = narrow[w, at, :].astype(F32)
        store.start()
    for take, give in zip(takes, gives):
        take.wait()
        give.start()
    for copy in stores + gives:
        copy.wait()


def per_device(n, s_count, blocks, weight_one, weight_two, gain_one, shift_one, gain_two, shift_two, cell_live, cotangent):
    rows, wide = cell_live.shape
    ch = blocks.shape[1] // wide
    cells = rows * wide
    total = cells + 2 * wide
    packed = -(-most_live(rows // HALVES, wide) // 16) * 16
    aligned = ch % 128 == 0
    chips = s_count // 2
    tap_rows = 9 * ch
    half_rows = tap_rows // 2
    owners = math.gcd(half_rows // 16, chips)
    piece = half_rows // owners

    if aligned:
        weight_one, weight_two = (w.reshape(tap_rows, n * ch) for w in (weight_one, weight_two))
    else:
        weight_one, weight_two = (
            w.reshape(tap_rows, n, ch).transpose(1, 0, 2) for w in (weight_one, weight_two))
    grad_shape = (2, owners, piece, n * ch) if aligned else (n, 2, owners, piece, ch)
    vmem = pl.BlockSpec(memory_space=pltpu.VMEM)
    hbm = pl.BlockSpec(memory_space=pl.ANY)
    sem = pltpu.SemaphoreType.DMA
    field = pltpu.VMEM((total, ch), F32)
    scratch = [
        pltpu.VMEM((ch * wide, 128), F32),
        pltpu.VMEM((2, n, tap_rows, ch), BF16),
        pltpu.VMEM((n - 1, tap_rows, ch), BF16),
        pltpu.VMEM((2, 3 * ch, cells), BF16),
        pltpu.VMEM((HALVES, packed, cells // HALVES), BF16),
        pltpu.VMEM((HALVES, cells // HALVES, packed), BF16),
        pltpu.VMEM((HALVES, cells // HALVES, ch), F32),
        pltpu.VMEM((HALVES, packed, tap_rows), BF16),
        pltpu.VMEM((HALVES, packed, ch), F32),
        pltpu.VMEM((2, n, HALVES, packed, ch), BF16),
        pltpu.VMEM((2, n, HALVES, packed, ch), BF16),
        pltpu.VMEM((2, 2, wide, ch), BF16),
        pltpu.VMEM((2, 2, wide, ch), BF16),
        pltpu.VMEM((2, wide, ch), BF16),
        pltpu.VMEM((2, wide, ch), BF16),
        field, field, field, field, field, field, field, field, field,
        pltpu.VMEM((total + 16, ch), F32),
        pltpu.VMEM((cells, ch), F32),
        pltpu.VMEM((4, n, 2 * wide + HALVES * packed, ch), BF16),
        pltpu.VMEM((n, rows + 2, wide, 3 * ch), BF16),
        pltpu.VMEM((2, n, 2, owners, piece, ch), F32),
        pltpu.VMEM((2, n, owners, piece, ch), BF16),
        pltpu.VMEM((2, n, owners, piece, ch), BF16),
        pltpu.VMEM((2, n, owners, piece, ch), BF16),
        pltpu.VMEM((2, n, chips, piece, ch), BF16),
        pltpu.VMEM((2, n, 2, owners, piece, ch), BF16),
        pltpu.VMEM((4, 8, ch), F32),
        pltpu.VMEM((4, s_count, 8, ch), F32),
        pltpu.VMEM((3, 2, wide, ch), F32),
        pltpu.VMEM((3, 2, wide, ch), F32),
        sem((2, n)),
        sem((n,)), sem((n,)),
        sem((n - 1, s_count)), sem((n - 1, s_count)),
        sem((2, n, HALVES)), sem((2, n, HALVES)),
        sem((2,)), sem((2,)),
        sem((2,)), sem((2,)),
        sem((4, 2, n, HALVES)), sem((4, n, HALVES)),
        sem((4, s_count)), sem((4, s_count)),
        sem((3, 2)), sem((3, 2)),
        sem((2, n)), sem((2, n)),
        sem((2, n, chips)), sem((2, n, chips)),
        sem((2, n, chips)), sem((2, n, chips)),
        sem((2, n)), sem((2, n)),
        sem((2, n)),
    ]
    block_out, input_grad, wg1, wg2, *sums = pl.pallas_call(
        functools.partial(block_kernel, n, s_count, rows, wide, ch, aligned, packed),
        out_shape=(
            jax.ShapeDtypeStruct((rows, ch * wide), BF16),
            jax.ShapeDtypeStruct((rows, ch * wide), F32),
            jax.ShapeDtypeStruct(grad_shape, BF16),
            jax.ShapeDtypeStruct(grad_shape, BF16),
            *[jax.ShapeDtypeStruct((1, ch), F32)] * 4,
        ),
        in_specs=[vmem] * 7 + [hbm] * 2,
        out_specs=(vmem, vmem, hbm, hbm, vmem, vmem, vmem, vmem),
        scratch_shapes=scratch,
        compiler_params=pltpu.CompilerParams(
            collective_id=0, has_side_effects=True, vmem_limit_bytes=60 * 1024 * 1024),
    )(blocks, cotangent, cell_live.T,
      *(v.reshape(1, ch) for v in (gain_one, shift_one, gain_two, shift_two)), weight_one, weight_two)

    if not aligned:
        def whole(grad):
            grad = grad.reshape(n, tap_rows, ch).transpose(1, 0, 2)
            return grad.astype(F32).reshape(9, ch, n * ch)
        return (block_out, input_grad, whole(wg1), whole(wg2), *(v.reshape(ch) for v in sums))

    wg1, wg2 = (w.reshape(tap_rows, n * ch) for w in (wg1, wg2))
    wide_grad = jax.ShapeDtypeStruct((tap_rows, n * ch), F32)
    moved = (block_out, input_grad, *sums)
    grad1, grad2, *moved = pl.pallas_call(
        functools.partial(finish_kernel, 2 + len(moved)),
        out_shape=(wide_grad, wide_grad, *(jax.ShapeDtypeStruct(v.shape, v.dtype) for v in moved)),
        in_specs=[pl.BlockSpec(memory_space=pl.ANY)] * (2 + len(moved)),
        out_specs=[pl.BlockSpec(memory_space=pl.ANY)] * (2 + len(moved)),
        scratch_shapes=[
            pltpu.VMEM((2, tap_rows, n * ch), BF16), pltpu.VMEM((2, tap_rows, n * ch), F32),
            sem((2, FINISH_PARTS)), sem((2, FINISH_PARTS)), sem((len(moved),)), sem((len(moved),)),
            *(pltpu.VMEM(v.shape, v.dtype) for v in moved),
        ],
        compiler_params=pltpu.CompilerParams(vmem_limit_bytes=64 * 1024 * 1024),
    )(wg1, wg2, *moved)
    block_out, input_grad, *sums = moved
    grads = (g.reshape(9, ch, n * ch) for g in (grad1, grad2))
    return (block_out, input_grad, *grads, *(v.reshape(ch) for v in sums))


def solution(mesh):
    return jax.shard_map(
        functools.partial(per_device, mesh.shape["chan"], mesh.shape["space"]),
        mesh=mesh,
        in_specs=(
            P("space", "chan"),
            P(None, "chan", None),
            P(None, "chan", None),
            P("chan"),
            P("chan"),
            P("chan"),
            P("chan"),
            P("space", None),
            P("space", "chan"),
        ),
        out_specs=(
            P("space", "chan"),
            P("space", "chan"),
            P(None, "chan", None),
            P(None, "chan", None),
            P("chan"),
            P("chan"),
            P("chan"),
            P("chan"),
        ),
        check_vma=False,
    )
```

```python
import functools
import math

import jax
import jax.numpy as jnp
from jax import lax
from jax.experimental import pallas as pl
from jax.experimental.pallas import tpu as pltpu
from jax.sharding import PartitionSpec as P

EPSILON = 1e-05
MESH = pl.DeviceIdType.MESH
F32 = jnp.float32
BF16 = jnp.bfloat16
ROOT_HALF = 0.7071067811865476
ROOT_TWO_PI = 0.3989422804014327
CHUNK = 64
FINISH_PARTS = 4
UNROLL = 2
HALVES = 2
LARGE, SMALL = 7, 3


def dot(a, b):
    return jnp.dot(a, b, preferred_element_type=F32)


def gelu_parts(v):
    upper = 0.5 * (1.0 + lax.erf(v * ROOT_HALF))
    slope = upper + v * (ROOT_TWO_PI * jnp.exp(-0.5 * v * v))
    return v * upper, slope


def most_live(rows, wide):
    units = (wide + 1) // (SMALL + 1)
    live_rows = rows - rows // (LARGE + 1)
    return min(rows * wide, math.ceil(units * live_rows * LARGE / 2))


def block_kernel(n, s_count, rows, wide, ch, aligned, packed, *refs):
    (x_in, cot_in, live_in, gain1_in, shift1_in, gain2_in, shift2_in, w1_hbm, w2_hbm) = refs[:9]
    (out_block, out_input, out_wg1, out_wg2, out_gain1, out_shift1, out_gain2, out_shift2) = refs[9:17]
    (turned, wv, wf, x_t, pack, unpack, places, edge_send, edge_recv, cot_send, cot_recv, cotm, mask, masked,
     normed1, normed2, through, slope1, hid, hid2, pad, acc, hold, taken,
     part, psend, crecv, hsend, qrecv, wout, st_send, st_recv, row_send, row_recv,
     w_sem, wz_ssem, wz_rsem, wp_ssem, wp_rsem, e_ssem, e_rsem, ce_ssem, ce_rsem, ag_ssem, ag_rsem,
     st_ssem, st_rsem, row_ssem, row_rsem, c_ssem, c_rsem, q_ssem, q_rsem,
     f_ssem, f_rsem, h_ssem, h_rsem, o_sem) = refs[17:]

    z = lax.axis_index("chan")
    s = lax.axis_index("space")
    cells = rows * wide
    total = cells + 2 * wide
    band = cells // HALVES
    core, chip, chips = s % 2, s // 2, s_count // 2
    before, after = (s + s_count - 1) % s_count, (s + 1) % s_count
    tap_rows = 9 * ch

    barrier = pltpu.get_barrier_semaphore()

    @pl.loop(1, s_count)
    def _(k):
        pl.semaphore_signal(barrier, inc=1, device_id=(z, (s + k) % s_count), device_id_type=MESH)

    @pl.loop(1, n)
    def _(k):
        pl.semaphore_signal(barrier, inc=1, device_id=((z + k) % n, s), device_id_type=MESH)

    w_copies = []
    for which, source in enumerate((w1_hbm, w2_hbm)):
        for d in range(n):
            block = source.at[:, d * ch:(d + 1) * ch] if aligned else source.at[d]
            w_copies.append(pltpu.make_async_copy(block, wv.at[which, d], w_sem.at[which, d]))
    for copy in w_copies:
        copy.start()

    def chunked(fn, init, first=0, count=cells):
        def step(i, carry):
            return fn(pl.multiple_of(first + i * CHUNK, CHUNK), CHUNK, carry)
        return lax.fori_loop(0, count // CHUNK, step, init, unroll=UNROLL)

    lanes = 128
    tiles = ch * wide // lanes

    def from_flat(flat, put):
        for i in range(tiles):
            turned[i * lanes:(i + 1) * lanes, 0:rows] = flat[:, i * lanes:(i + 1) * lanes].astype(F32).T
        for w in range(wide):
            put(pl.ds(w, rows, stride=wide), turned[pl.ds(w, ch, stride=wide), 0:rows].T)

    def to_flat(source, flat):
        for w in range(wide):
            turned[pl.ds(w, ch, stride=wide), 0:rows] = source[pl.ds(w, rows, stride=wide), :].T
        for i in range(tiles):
            flat[:, i * lanes:(i + 1) * lanes] = turned[i * lanes:(i + 1) * lanes, 0:rows].T.astype(flat.dtype)

    def put_masked(at, value):
        masked[at, :] = value

    from_flat(x_in, put_masked)

    cell = lax.broadcasted_iota(jnp.int32, (cells, rows), 0)
    pick = (cell // wide == lax.broadcasted_iota(jnp.int32, (cells, rows), 1)).astype(F32).astype(BF16)
    column_of = lax.broadcasted_iota(jnp.int32, (cells, wide), 0) % wide
    picked = lax.dot_general(pick, live_in[...].astype(BF16), (((1,), (1,)), ((), ())), preferred_element_type=F32)
    picked = jnp.where(column_of == lax.broadcasted_iota(jnp.int32, (cells, wide), 1), picked, 0.0)
    mask[0:cells, :] = dot(picked.astype(BF16), jnp.ones((wide, ch), BF16))

    def load_main(start, size, carry):
        at = pl.ds(start, size)
        lv = mask[at, :]
        masked[at, :] = masked[at, :] * lv
        return carry

    chunked(load_main, 0)
    for side, start in ((0, 0), (1, cells - wide)):
        edge_send[side, 0] = masked[start:start + wide, :].astype(BF16)
        edge_send[side, 1] = mask[start:start + wide, :].astype(BF16)

    acc[...] = jnp.zeros_like(acc)
    st_send[...] = jnp.zeros_like(st_send)

    pl.semaphore_wait(barrier, s_count - 1 + n - 1)

    def edge_copy(side):
        return pltpu.make_async_remote_copy(
            src_ref=edge_send.at[side], dst_ref=edge_recv.at[1 - side],
            send_sem=e_ssem.at[side], recv_sem=e_rsem.at[1 - side],
            device_id=(z, before if side == 0 else after), device_id_type=MESH)

    for side in range(2):
        edge_copy(side).start()

    def cot_copy(side):
        return pltpu.make_async_remote_copy(
            src_ref=cot_send.at[side], dst_ref=cot_recv.at[1 - side],
            send_sem=ce_ssem.at[side], recv_sem=ce_rsem.at[1 - side],
            device_id=(z, before if side == 0 else after), device_id_type=MESH)

    def load_cotangent():
        def put(at, value):
            cotm[at, :] = value
        from_flat(cot_in, put)

        def live_only(start, size, carry):
            at = pl.ds(start, size)
            cotm[at, :] = cotm[at, :] * mask[at, :]
            return carry
        chunked(live_only, 0)
        for side, start in ((0, 0), (1, cells - wide)):
            cot_send[side] = cotm[start:start + wide, :].astype(BF16)
            cot_copy(side).start()

    def take_cotangent():
        for side in range(2):
            cot_copy(1 - side).wait_recv()
            at = slice(cells + side * wide, cells + (side + 1) * wide)
            cotm[at, :] = cot_recv[side].astype(F32) * mask[at, :]

    w_parts = math.gcd(tap_rows // 16, s_count)
    w_rows = tap_rows // w_parts
    w_mine = s % w_parts
    w_group = s - w_mine

    def wz_copy(which, k):
        at = pl.ds(w_mine * w_rows, w_rows)
        slot = n - k - 1
        return pltpu.make_async_remote_copy(
            src_ref=wv.at[which, (z + k) % n, at, :], dst_ref=wf.at[which, slot, at, :],
            send_sem=wz_ssem.at[which, slot], recv_sem=wz_rsem.at[which, slot],
            device_id=((z + k) % n, s), device_id_type=MESH)

    def wp_copy(which, slot, k, whose):
        at = pl.ds(whose * w_rows, w_rows)
        return pltpu.make_async_remote_copy(
            src_ref=wf.at[which, slot, at, :], dst_ref=wf.at[which, slot, at, :],
            send_sem=wp_ssem.at[which, slot, k], recv_sem=wp_rsem.at[which, slot, whose],
            device_id=(z, w_group + (w_mine + k) % w_parts), device_id_type=MESH)

    def weights_over_z(which):
        for copy in w_copies[which * n:(which + 1) * n]:
            copy.wait()

        @pl.loop(1, n)
        def _(k):
            wz_copy(which, k).start()

    def slot_of(block):
        return (block - z + n - 1) % n

    def weights_round(which):
        @pl.loop(1, n)
        def _(distance):
            for sign in (1, -1):
                block = z - distance * sign

                @pl.when((block >= 0) & (block < n))
                def _():
                    slot = slot_of(block)
                    wz_copy(which, n - 1 - slot).wait_recv()

                    @pl.loop(1, w_parts)
                    def _(k):
                        wp_copy(which, slot, k, w_mine).start()

    def weights_arrived(which, slot):
        @pl.loop(1, w_parts)
        def _(k):
            wp_copy(which, slot, k, (w_mine + k) % w_parts).wait_recv()

    def row_copy(slot, side):
        return pltpu.make_async_remote_copy(
            src_ref=row_send.at[slot, side], dst_ref=row_recv.at[slot, 1 - side],
            send_sem=row_ssem.at[slot, side], recv_sem=row_rsem.at[slot, 1 - side],
            device_id=(z, before if side == 0 else after), device_id_type=MESH)

    def send_rows(slot, ref):
        for side, start in ((0, 0), (1, cells - wide)):
            row_send[slot, side] = ref[start:start + wide, :]
            row_copy(slot, side).start()

    def take_rows(slot, ref):
        for side in range(2):
            row_copy(slot, 1 - side).wait_recv()
            ref[cells + side * wide:cells + (side + 1) * wide, :] = row_recv[slot, side]

    def st_copy(slot, k, whose):
        return pltpu.make_async_remote_copy(
            src_ref=st_send.at[slot], dst_ref=st_recv.at[slot, whose],
            send_sem=st_ssem.at[slot, k], recv_sem=st_rsem.at[slot, whose],
            device_id=(z, (s + k) % s_count), device_id_type=MESH)

    def send_stats(slot, values):
        for i, v in enumerate(values):
            st_send[slot, i:i + 1, :] = v
        for k in range(1, s_count):
            st_copy(slot, k, s).start()
        st_recv[slot, s] = st_send[slot]

    def take_stats(slot):
        for k in range(1, s_count):
            st_copy(slot, k, (s + k) % s_count).wait_recv()

    strip = 8
    column = lax.broadcasted_iota(jnp.int32, (strip * wide, ch), 0) % wide

    def shift(target, first, count):
        size = count * wide
        where = column[:size]
        here = pad[pl.ds(8 + first * wide, size), :]
        left = jnp.where(where == 0, 0.0, pad[pl.ds(7 + first * wide, size), :])
        right = jnp.where(where == wide - 1, 0.0, pad[pl.ds(9 + first * wide, size), :])
        for b, v in enumerate((left, here, right)):
            target[pl.ds(first, count), :, b * ch:(b + 1) * ch] = v.astype(BF16).reshape(count, wide, ch)

    edge = 2 * wide
    ag_rows = ((0, edge + packed), (edge + packed, packed))
    band_rows = rows // HALVES

    def unpack_half(ph, block, q, target):
        if q == 0:
            pad[8:8 + wide, :] = hold[ph, block, 0:wide, :].astype(F32)
            pad[8 + wide + cells:8 + 2 * wide + cells, :] = hold[ph, block, wide:edge, :].astype(F32)
            shift(target, 0, 1)
            shift(target, rows + 1, 1)
        pad[8 + wide + q * band:8 + wide + (q + 1) * band, :] = dot(
            unpack[q], hold[ph, block, edge + q * packed:edge + (q + 1) * packed, :])

        for i in range(band_rows // strip):
            shift(target, 1 + q * band_rows + i * strip, strip)

    def add_conv(q, field, taps, turned_taps=None):
        first, last = (0, band_rows - 1) if q == 0 else (band_rows - 1, rows)
        count = last - first
        lhs = field[first:last + 2, :, :].reshape((count + 2) * wide, 3 * ch)
        if turned_taps is None:
            value = dot(lhs, jnp.concatenate([taps(a) for a in range(3)], axis=1))
        else:
            rhs = jnp.concatenate([
                jnp.concatenate([turned_taps(3 * (2 - a) + 2 - b) for b in range(3)], axis=1) for a in range(3)], axis=0)
            value = lax.dot_general(lhs, rhs, (((1,), (1,)), ((), ())), preferred_element_type=F32)
        at = pl.ds(first * wide, count * wide)
        acc[at, :] = acc[at, :] + sum(
            value[a * wide:(a + count) * wide, a * ch:(a + 1) * ch] for a in range(3))

    def ag_copy(ph, block, q, sign):
        at = pl.ds(*ag_rows[q])
        return pltpu.make_async_remote_copy(
            src_ref=hold.at[ph, block, at, :], dst_ref=hold.at[ph, block, at, :],
            send_sem=ag_ssem.at[ph, (1 - sign) // 2, block, q], recv_sem=ag_rsem.at[ph, block, q],
            device_id=(z + sign, s), device_id_type=MESH)

    def pack_field(ph, source, fill=None, first=None):
        if fill is not None:
            fill(cells, edge, 0)
        hold[ph, z, 0:edge, :] = source[cells:cells + edge, :].astype(BF16)
        for q in range(HALVES):
            if first is not None:
                first(q)
            if fill is not None:
                chunked(fill, 0, q * band, band)
            hold[ph, z, edge + q * packed:edge + (q + 1) * packed, :] = dot(
                pack[q], source[q * band:(q + 1) * band, :].astype(BF16)).astype(BF16)
            for sign in (1, -1):
                @pl.when((z + sign >= 0) & (z + sign < n))
                def _():
                    ag_copy(ph, z, q, sign).start()

    def inside(slice_at):
        return (slice_at >= 0) & (slice_at < n)

    def take_and_pass(ph, k, q, sign, passes=True, takes=True):
        block = z - k * sign

        @pl.when((k > 0) & inside(block))
        def _():
            if passes and takes:
                ag_copy(ph, block, q, sign).wait_recv()

            @pl.when(inside(z + sign))
            def _():
                if passes:
                    if not takes:
                        ag_copy(ph, block, q, sign).wait_recv()
                    ag_copy(ph, block, q, sign).start()

            if not passes:
                @pl.when(jnp.logical_not(inside(z + sign)))
                def _():
                    ag_copy(ph, block, q, sign).wait_recv()

    near = jnp.where(z < n - n // 2, 1, 0)

    def consume_way(k, q, way, consume):
        block = z - k * (1 - 2 * way)

        @pl.when((k >= 0) & (k < n) & inside(block) & ((k > 0) | (way == near)))
        def _():
            consume(k, block, q)

    def take_both(ph, k, q, **how):
        @pl.loop(0, 2)
        def _(i):
            way = (near + i) % 2
            take_and_pass(ph, k, q, 1 - 2 * way, **how)

    def gather(ph, consume, each):
        @pl.loop(0, n)
        def _(k):
            for q in range(HALVES):
                take_both(ph, k, q)
                if q:
                    consume_way(k, q - 1, 1 - near, consume)
                else:
                    consume_way(k - 1, HALVES - 1, 1 - near, consume)
                consume_way(k, q, near, consume)
            each(k)

    def gather_passing_first(ph, consume, each):
        @pl.loop(0, n)
        def _(k):
            @pl.when(k == 1)
            def _():
                @pl.loop(1, n)
                def _(ahead):
                    for q in range(HALVES):
                        take_both(ph, ahead, q, takes=False)
            for q in range(HALVES):
                take_both(ph, k, q, passes=False)

                @pl.loop(0, 2)
                def _(i):
                    consume_way(k, q, (near + i) % 2, consume)
            each(k)

    last_pass = jnp.maximum(jnp.where(z < n - 1, z, 0), jnp.where(z > 0, n - 1 - z, 0))

    def forward(ph, field):
        def consume(k, block, q):
            into = taken.at[block]
            unpack_half(ph, block, q, into)

            @pl.when(k == 0)
            def _():
                add_conv(q, into, lambda a: wv[ph, z, 3 * a * ch:3 * (a + 1) * ch, :])

            @pl.when(k > 0)
            def _():
                slot = slot_of(block)
                if q == 0:
                    weights_arrived(ph, slot)
                add_conv(q, into, lambda a: wf[ph, slot, 3 * a * ch:3 * (a + 1) * ch, :])

        def each(k):
            if ph == 0:
                @pl.when(k == 0)
                def _():
                    weights_round(0)

                @pl.when(k == 1)
                def _():
                    weights_over_z(1)
        (gather if ph else gather_passing_first)(ph, consume, each)

    def turn_field(ph, field):
        main = [field[start:start + ch, :].T for start in range(0, cells, ch)]
        ends = field[cells:cells + edge, :]
        if edge < ch:
            ends = jnp.concatenate([ends, jnp.zeros((ch - edge, ch), F32)], axis=0)
        ends = ends.T
        for i, here in enumerate(main):
            left = jnp.concatenate(
                [ends[:, 0:wide] if i == 0 else main[i - 1][:, ch - wide:], here[:, 0:ch - wide]], axis=1)
            right = jnp.concatenate(
                [here[:, wide:], main[i + 1][:, 0:wide] if i + 1 < len(main) else ends[:, wide:edge]], axis=1)
            for a, v in enumerate((left, here, right)):
                x_t[ph, a * ch:(a + 1) * ch, i * ch:(i + 1) * ch] = v.astype(BF16)

    half_rows = tap_rows // 2
    owners = math.gcd(half_rows // 16, chips)
    piece = half_rows // owners

    def c_copy(ph, j):
        return pltpu.make_async_remote_copy(
            src_ref=psend.at[ph, j], dst_ref=crecv.at[ph, j],
            send_sem=c_ssem.at[ph, j], recv_sem=c_rsem.at[ph, j],
            device_id=(z, chip * 2 + 1 - core), device_id_type=MESH)

    def q_copy(ph, j, e, whose, owner):
        return pltpu.make_async_remote_copy(
            src_ref=hsend.at[ph, j, owner], dst_ref=qrecv.at[ph, j, whose],
            send_sem=q_ssem.at[ph, j, e], recv_sem=q_rsem.at[ph, j, whose],
            device_id=(z, ((chip + e) % chips) * 2 + core), device_id_type=MESH)

    def f_copy(ph, j, e, owner):
        return pltpu.make_async_remote_copy(
            src_ref=wout.at[ph, j, core, owner], dst_ref=wout.at[ph, j, core, owner],
            send_sem=f_ssem.at[ph, j, e], recv_sem=f_rsem.at[ph, j, owner],
            device_id=(z, ((chip + e) % chips) * 2 + core), device_id_type=MESH)

    def h_copy(ph, j, whose):
        return pltpu.make_async_remote_copy(
            src_ref=wout.at[ph, j, whose], dst_ref=wout.at[ph, j, whose],
            send_sem=h_ssem.at[ph, j], recv_sem=h_rsem.at[ph, j],
            device_id=(z, chip * 2 + 1 - core), device_id_type=MESH)

    def o_copy(ph, j):
        target = (out_wg1, out_wg2)[ph]
        if aligned:
            target = target.at[:, :, :, pl.ds(pl.multiple_of(j * ch, ch), ch)]
        else:
            target = target.at[j]
        return pltpu.make_async_copy(wout.at[ph, j], target, o_sem.at[ph, j])

    def sum_cores(ph, j):
        for o in range(owners):
            psend[ph, j, o] = part[ph, j, 1 - core, o].astype(BF16)
        c_copy(ph, j).start()

    def sum_chips(ph, j):
        c_copy(ph, j).wait_recv()
        for o in range(owners):
            v = part[ph, j, core, o] + crecv[ph, j, o].astype(F32)
            part[ph, j, core, o] = v
            hsend[ph, j, o] = v.astype(BF16)

        @pl.loop(1, chips)
        def _(e):
            peer = (chip + e) % chips

            @pl.when(peer < owners)
            def _():
                q_copy(ph, j, e, chip, peer).start()

    def spread_chips(ph, j):
        @pl.when(chip < owners)
        def _():
            @pl.loop(1, chips)
            def _(e):
                q_copy(ph, j, e, (chip + e) % chips, chip).wait_recv()
            v = part[ph, j, core, chip]
            for e in range(1, chips):
                v = v + qrecv[ph, j, (chip + e) % chips].astype(F32)
            wout[ph, j, core, chip] = v.astype(BF16)

            @pl.loop(1, chips)
            def _(e):
                f_copy(ph, j, e, chip).start()

    def spread_cores(ph, j):
        @pl.loop(1, chips)
        def _(e):
            peer = (chip + e) % chips

            @pl.when(peer < owners)
            def _():
                f_copy(ph, j, e, peer).wait_recv()
        h_copy(ph, j, core).start()

    def finish(ph, j):
        h_copy(ph, j, 1 - core).wait_recv()
        o_copy(ph, j).start()

    def put_part(ph, j, tap, value):
        start = tap * ch
        done = 0
        while done < ch:
            row = start + done
            side, o, at = row // half_rows, row % half_rows // piece, row % piece
            size = min(ch - done, piece - at)
            part[ph, j, side, o, at:at + size, :] = value[done:done + size, :]
            done += size

    stages = (sum_cores, sum_chips, spread_chips, spread_cores, finish)

    def of_step(k, fn):
        @pl.loop(0, 2)
        def _(way):
            block = z - k * (1 - 2 * way)

            @pl.when((k >= 0) & (k < n) & inside(block) & ((k > 0) | (way == 0)))
            def _():
                fn(block)

    passing = last_pass > 0

    def made_at(step):
        first = jnp.where(passing & (step > 0), jnp.where(step == last_pass, 1, step + 1), step)
        return first, step + 1

    def advance(ph, k):
        for age in range(1, len(stages)):
            step = k - age

            @pl.when((step >= 0) & (step < n))
            def _():
                @pl.loop(*made_at(step))
                def _(made):
                    of_step(made, functools.partial(stages[age], ph))

    def advance_all(ph, age):
        @pl.loop(0, n)
        def _(j):
            stages[age](ph, j)

    def field_grad(ph, block):
        grad = taken[block, 1:rows + 1, :, :].reshape(cells, 3 * ch)
        value = dot(x_t[ph], grad)
        for a in range(3):
            for b in range(3):
                put_part(ph, block, 3 * a + b, value[a * ch:(a + 1) * ch, (2 - b) * ch:(3 - b) * ch])

    def make_grad(ph, block):
        field_grad(ph, block)
        sum_cores(ph, block)

    def backward(ph):
        last = ph == 0

        def consume(k, block, q):
            into = taken.at[block]
            unpack_half(2 + ph, block, q, into)
            if last and q == HALVES - 1:
                @pl.when((k == 0) | (k >= last_pass))
                def _():
                    make_grad(ph, block)
            add_conv(q, into, None, lambda t: wv[ph, block, t * ch:(t + 1) * ch, :])

        def each(k):
            first, end = made_at(k)
            if last:
                @pl.loop(first, end - 1)
                def _(step):
                    of_step(step, functools.partial(make_grad, ph))
                advance(ph, k)
                for age in range(2, len(stages)):
                    @pl.when(k == age - 2)
                    def _():
                        advance_all(1, age)
            else:
                @pl.loop(first, jnp.where(passing | (k < n - 2), end, first))
                def _(step):
                    of_step(step, functools.partial(make_grad, ph))
        gather(2 + ph, consume, each)

    def fold(v):
        return jnp.sum(v.reshape(v.shape[0] // 8, 8, ch), axis=0)

    def flatten(v):
        return jnp.sum(v, axis=0, keepdims=True)

    zero = jnp.zeros((8, ch), F32)

    def local_moments(ref):
        def sums(start, size, carry):
            at = pl.ds(start, size)
            m = mask[at, :]
            return carry[0] + fold(ref[at, :] * m), carry[1] + fold(m)
        added, number = (flatten(v) for v in chunked(sums, (zero, zero)))
        middle = added / jnp.maximum(number, 1.0)

        def spread(start, size, carry):
            at = pl.ds(start, size)
            c = (ref[at, :] - middle) * mask[at, :]
            return carry + fold(c * c)
        return added, number, flatten(chunked(spread, zero))

    def moments(slot):
        take_stats(slot)
        got = [st_recv[slot, k] for k in range(s_count)]
        added = sum(g[0:1] for g in got)
        number = sum(g[1:2] for g in got)
        mean = added / number
        spread = 0.0
        for g in got:
            off = g[0:1] / jnp.maximum(g[1:2], 1.0) - mean
            spread = spread + (g[2:3] + g[1:2] * off * off)
        return mean, lax.rsqrt(spread / number + EPSILON), number

    def everywhere(fn):
        chunked(fn, 0)
        fn(cells, 2 * wide, 0)

    gain1, shift1, gain2, shift2 = (r[...] for r in (gain1_in, shift1_in, gain2_in, shift2_in))

    weights_over_z(0)

    below = lax.broadcasted_iota(jnp.int32, (band, band), 1) < lax.broadcasted_iota(jnp.int32, (band, band), 0)
    below = below.astype(F32).astype(BF16)

    def make_pack(h):
        lv = mask[h * band:(h + 1) * band, :]
        place = jnp.where(lv > 0.0, dot(below, lv.astype(BF16)), -1.0)
        places[h] = place
        across = place.T[0:1, :]
        spot = lax.broadcasted_iota(jnp.int32, (packed, band), 0).astype(F32)
        pack[h] = jnp.where(spot == across, 1.0, 0.0).astype(BF16)

    def make_unpack(h):
        for start in range(0, packed, ch):
            size = min(ch, packed - start)
            spot = start + lax.broadcasted_iota(jnp.int32, (band, size), 1)
            unpack[h, :, start:start + size] = jnp.where(
                places[h, :, :size] == spot.astype(F32), 1.0, 0.0).astype(BF16)

    for side in range(2):
        edge_copy(1 - side).wait_recv()
        there = jnp.where(s > 0, 1.0, 0.0) if side == 0 else jnp.where(s < s_count - 1, 1.0, 0.0)
        at = slice(cells + side * wide, cells + (side + 1) * wide)
        masked[at, :] = edge_recv[side, 0].astype(F32) * there
        mask[at, :] = edge_recv[side, 1].astype(F32) * there

    pack_field(0, masked, first=make_pack)
    for h in range(HALVES):
        make_unpack(h)
    forward(0, masked)
    send_rows(0, acc)
    send_stats(0, local_moments(acc))
    weights_round(1)
    load_cotangent()
    mean1, scale1, count = moments(0)

    def activate_one(start, size, carry):
        at = pl.ds(start, size)
        main = start is not cells
        nv = ((acc if main else normed1)[at, :] - mean1) * scale1
        normed1[at, :] = nv
        hid[at, :] = gelu_parts(nv * gain1 + shift1)[0] * mask[at, :]
        if main:
            acc[at, :] = jnp.zeros((size, ch), F32)
        return carry

    def slope_one(start, size, carry):
        at = pl.ds(start, size)
        slope1[at, :] = gelu_parts(normed1[at, :] * gain1 + shift1)[1] * mask[at, :]
        return carry

    take_rows(0, normed1)
    pack_field(1, hid, activate_one)
    everywhere(slope_one)
    forward(1, hid)
    send_rows(1, acc)
    send_stats(1, local_moments(acc))
    turn_field(0, masked)
    turn_field(1, hid)
    mean2, scale2, _ = moments(1)

    def activate_two(source, start, size):
        at = pl.ds(start, size)
        nv = (source[at, :] - mean2) * scale2
        normed2[at, :] = nv
        value, slope = gelu_parts(nv * gain2 + shift2 + masked[at, :])
        t = cotm[at, :] * slope
        through[at, :] = t
        return value, nv, t

    def activate_main(start, size, carry):
        value, nv, t = activate_two(acc, start, size)
        at = pl.ds(start, size)
        hid2[at, :] = value * mask[at, :]
        acc[at, :] = jnp.zeros((size, ch), F32)
        return carry[0] + fold(t * nv), carry[1] + fold(t)

    send_stats(2, [flatten(v) for v in chunked(activate_main, (zero, zero))])
    take_rows(1, normed2)
    take_cotangent()
    activate_two(normed2, cells, edge)
    to_flat(hid2, out_block)

    def gradient_sums(slot):
        take_stats(slot)
        got = [st_recv[slot, k] for k in range(s_count)]
        return sum(g[0:1] for g in got), sum(g[1:2] for g in got)

    def norm_back(upstream, normed, gain, scale, sums):
        gain_grad, shift_grad = sums
        factor = gain * scale
        level, tilt = shift_grad / count, gain_grad / count

        def fill(start, size, carry):
            at = pl.ds(start, size)
            v = upstream[at, :] - mask[at, :] * (level + normed[at, :] * tilt)
            hid[at, :] = factor * v
            return carry
        return fill

    sums2 = gradient_sums(2)
    pack_field(3, hid, norm_back(through, normed2, gain2, scale2, sums2))
    backward(1)

    send_rows(2, acc)

    def inner_main(start, size, carry):
        at = pl.ds(start, size)
        v = acc[at, :] * slope1[at, :]
        slope1[at, :] = v
        acc[at, :] = jnp.zeros((size, ch), F32)
        return carry[0] + fold(v * normed1[at, :]), carry[1] + fold(v)

    send_stats(3, [flatten(v) for v in chunked(inner_main, (zero, zero))])

    @pl.when(jnp.logical_not(passing))
    def _():
        for step in range(n - 2, n):
            of_step(step, functools.partial(make_grad, 1))
    for side in range(2):
        row_copy(2, 1 - side).wait_recv()
        at = slice(cells + side * wide, cells + (side + 1) * wide)
        slope1[at, :] = row_recv[2, side] * slope1[at, :]
    sums1 = gradient_sums(3)
    pack_field(2, hid, norm_back(slope1, normed1, gain1, scale1, sums1))
    advance_all(1, 1)
    backward(0)
    advance(0, n)

    def finish_input(start, size, carry):
        at = pl.ds(start, size)
        acc[at, :] = (acc[at, :] + through[at, :]) * mask[at, :]
        return carry

    chunked(finish_input, 0)
    to_flat(acc, out_input)
    out_gain1[...], out_shift1[...] = sums1
    out_gain2[...], out_shift2[...] = sums2
    for extra in range(1, len(stages) - 1):
        advance(0, n + extra)

    for side in range(2):
        edge_copy(side).wait_send()
        cot_copy(side).wait_send()
        for slot in range(3):
            row_copy(slot, side).wait_send()

    @pl.loop(1, s_count)
    def _(k):
        for slot in range(4):
            st_copy(slot, k, s).wait_send()

    @pl.loop(1, n)
    def _(k):
        for which in range(2):
            wz_copy(which, k).wait_send()

    @pl.loop(1, w_parts)
    def _(k):
        for which in range(2):
            for slot in range(n - 1):
                wp_copy(which, slot, k, w_mine).wait_send()

    @pl.loop(0, n)
    def _(k):
        for sign in (1, -1):
            block = z - k * sign

            @pl.when((block >= 0) & (block < n) & (z + sign >= 0) & (z + sign < n))
            def _():
                for ph in range(4):
                    for q in range(HALVES):
                        ag_copy(ph, block, q, sign).wait_send()

    @pl.loop(0, n)
    def _(j):
        for ph in range(2):
            c_copy(ph, j).wait_send()
            h_copy(ph, j, core).wait_send()
            o_copy(ph, j).wait()

            @pl.loop(1, chips)
            def _(e):
                peer = (chip + e) % chips

                @pl.when(peer < owners)
                def _():
                    q_copy(ph, j, e, chip, peer).wait_send()

                @pl.when(chip < owners)
                def _():
                    f_copy(ph, j, e, chip).wait_send()


def finish_kernel(count, *refs):
    ins, outs = refs[:count], refs[count:2 * count]
    narrow, wide, in_sem, out_sem, take_sem, give_sem = refs[2 * count:2 * count + 6]
    held = refs[2 * count + 6:]
    rows = narrow.shape[1] // FINISH_PARTS
    parts = [(w, i, pl.ds(i * rows, rows)) for i in range(FINISH_PARTS) for w in range(2)]
    loads = [pltpu.make_async_copy(ins[w].at[at, :], narrow.at[w, at, :], in_sem.at[w, i]) for w, i, at in parts]
    stores = [pltpu.make_async_copy(wide.at[w, at, :], outs[w].at[at, :], out_sem.at[w, i]) for w, i, at in parts]
    takes = [pltpu.make_async_copy(ins[2 + k], v, take_sem.at[k]) for k, v in enumerate(held)]
    gives = [pltpu.make_async_copy(v, outs[2 + k], give_sem.at[k]) for k, v in enumerate(held)]
    for copy in loads + takes:
        copy.start()
    for load, store, (w, i, at) in zip(loads, stores, parts):
        load.wait()
        wide[w, at, :] = narrow[w, at, :].astype(F32)
        store.start()
    for take, give in zip(takes, gives):
        take.wait()
        give.start()
    for copy in stores + gives:
        copy.wait()


def per_device(n, s_count, blocks, weight_one, weight_two, gain_one, shift_one, gain_two, shift_two, cell_live, cotangent):
    rows, wide = cell_live.shape
    ch = blocks.shape[1] // wide
    cells = rows * wide
    total = cells + 2 * wide
    packed = -(-most_live(rows // HALVES, wide) // 16) * 16
    aligned = ch % 128 == 0
    chips = s_count // 2
    tap_rows = 9 * ch
    half_rows = tap_rows // 2
    owners = math.gcd(half_rows // 16, chips)
    piece = half_rows // owners

    if aligned:
        weight_one, weight_two = (w.reshape(tap_rows, n * ch) for w in (weight_one, weight_two))
    else:
        weight_one, weight_two = (
            w.reshape(tap_rows, n, ch).transpose(1, 0, 2) for w in (weight_one, weight_two))
    grad_shape = (2, owners, piece, n * ch) if aligned else (n, 2, owners, piece, ch)
    vmem = pl.BlockSpec(memory_space=pltpu.VMEM)
    hbm = pl.BlockSpec(memory_space=pl.ANY)
    sem = pltpu.SemaphoreType.DMA
    field = pltpu.VMEM((total, ch), F32)
    scratch = [
        pltpu.VMEM((ch * wide, 128), F32),
        pltpu.VMEM((2, n, tap_rows, ch), BF16),
        pltpu.VMEM((2, n - 1, tap_rows, ch), BF16),
        pltpu.VMEM((2, 3 * ch, cells), BF16),
        pltpu.VMEM((HALVES, packed, cells // HALVES), BF16),
        pltpu.VMEM((HALVES, cells // HALVES, packed), BF16),
        pltpu.VMEM((HALVES, cells // HALVES, ch), F32),
        pltpu.VMEM((2, 2, wide, ch), BF16),
        pltpu.VMEM((2, 2, wide, ch), BF16),
        pltpu.VMEM((2, wide, ch), BF16),
        pltpu.VMEM((2, wide, ch), BF16),
        field, field, field, field, field, field, field, field, field,
        pltpu.VMEM((total + 16, ch), F32),
        pltpu.VMEM((cells, ch), F32),
        pltpu.VMEM((4, n, 2 * wide + HALVES * packed, ch), BF16),
        pltpu.VMEM((n, rows + 2, wide, 3 * ch), BF16),
        pltpu.VMEM((2, n, 2, owners, piece, ch), F32),
        pltpu.VMEM((2, n, owners, piece, ch), BF16),
        pltpu.VMEM((2, n, owners, piece, ch), BF16),
        pltpu.VMEM((2, n, owners, piece, ch), BF16),
        pltpu.VMEM((2, n, chips, piece, ch), BF16),
        pltpu.VMEM((2, n, 2, owners, piece, ch), BF16),
        pltpu.VMEM((4, 8, ch), F32),
        pltpu.VMEM((4, s_count, 8, ch), F32),
        pltpu.VMEM((3, 2, wide, ch), F32),
        pltpu.VMEM((3, 2, wide, ch), F32),
        sem((2, n)),
        sem((2, n)), sem((2, n)),
        sem((2, n - 1, s_count)), sem((2, n - 1, s_count)),
        sem((2,)), sem((2,)),
        sem((2,)), sem((2,)),
        sem((4, 2, n, HALVES)), sem((4, n, HALVES)),
        sem((4, s_count)), sem((4, s_count)),
        sem((3, 2)), sem((3, 2)),
        sem((2, n)), sem((2, n)),
        sem((2, n, chips)), sem((2, n, chips)),
        sem((2, n, chips)), sem((2, n, chips)),
        sem((2, n)), sem((2, n)),
        sem((2, n)),
    ]
    block_out, input_grad, wg1, wg2, *sums = pl.pallas_call(
        functools.partial(block_kernel, n, s_count, rows, wide, ch, aligned, packed),
        out_shape=(
            jax.ShapeDtypeStruct((rows, ch * wide), BF16),
            jax.ShapeDtypeStruct((rows, ch * wide), F32),
            jax.ShapeDtypeStruct(grad_shape, BF16),
            jax.ShapeDtypeStruct(grad_shape, BF16),
            *[jax.ShapeDtypeStruct((1, ch), F32)] * 4,
        ),
        in_specs=[vmem] * 7 + [hbm] * 2,
        out_specs=(vmem, vmem, hbm, hbm, vmem, vmem, vmem, vmem),
        scratch_shapes=scratch,
        compiler_params=pltpu.CompilerParams(
            collective_id=0, has_side_effects=True, vmem_limit_bytes=60 * 1024 * 1024),
    )(blocks, cotangent, cell_live.T,
      *(v.reshape(1, ch) for v in (gain_one, shift_one, gain_two, shift_two)), weight_one, weight_two)

    if not aligned:
        def whole(grad):
            grad = grad.reshape(n, tap_rows, ch).transpose(1, 0, 2)
            return grad.astype(F32).reshape(9, ch, n * ch)
        return (block_out, input_grad, whole(wg1), whole(wg2), *(v.reshape(ch) for v in sums))

    wg1, wg2 = (w.reshape(tap_rows, n * ch) for w in (wg1, wg2))
    wide_grad = jax.ShapeDtypeStruct((tap_rows, n * ch), F32)
    moved = (block_out, input_grad, *sums)
    grad1, grad2, *moved = pl.pallas_call(
        functools.partial(finish_kernel, 2 + len(moved)),
        out_shape=(wide_grad, wide_grad, *(jax.ShapeDtypeStruct(v.shape, v.dtype) for v in moved)),
        in_specs=[pl.BlockSpec(memory_space=pl.ANY)] * (2 + len(moved)),
        out_specs=[pl.BlockSpec(memory_space=pl.ANY)] * (2 + len(moved)),
        scratch_shapes=[
            pltpu.VMEM((2, tap_rows, n * ch), BF16), pltpu.VMEM((2, tap_rows, n * ch), F32),
            sem((2, FINISH_PARTS)), sem((2, FINISH_PARTS)), sem((len(moved),)), sem((len(moved),)),
            *(pltpu.VMEM(v.shape, v.dtype) for v in moved),
        ],
        compiler_params=pltpu.CompilerParams(vmem_limit_bytes=64 * 1024 * 1024),
    )(wg1, wg2, *moved)
    block_out, input_grad, *sums = moved
    grads = (g.reshape(9, ch, n * ch) for g in (grad1, grad2))
    return (block_out, input_grad, *grads, *(v.reshape(ch) for v in sums))


def solution(mesh):
    return jax.shard_map(
        functools.partial(per_device, mesh.shape["chan"], mesh.shape["space"]),
        mesh=mesh,
        in_specs=(
            P("space", "chan"),
            P(None, "chan", None),
            P(None, "chan", None),
            P("chan"),
            P("chan"),
            P("chan"),
            P("chan"),
            P("space", None),
            P("space", "chan"),
        ),
        out_specs=(
            P("space", "chan"),
            P("space", "chan"),
            P(None, "chan", None),
            P(None, "chan", None),
            P("chan"),
            P("chan"),
            P("chan"),
            P("chan"),
        ),
        check_vma=False,
    )
```

```python
import functools
import math

import jax
import jax.numpy as jnp
from jax import lax
from jax.experimental import pallas as pl
from jax.experimental.pallas import tpu as pltpu
from jax.sharding import PartitionSpec as P

EPSILON = 1e-05
MESH = pl.DeviceIdType.MESH
F32 = jnp.float32
BF16 = jnp.bfloat16
ROOT_HALF = 0.7071067811865476
ROOT_TWO_PI = 0.3989422804014327
CHUNK = 64
FINISH_PARTS = 4
UNROLL = 2
HALVES = 2
LARGE, SMALL = 7, 3


def dot(a, b):
    return jnp.dot(a, b, preferred_element_type=F32)


def gelu_parts(v):
    upper = 0.5 * (1.0 + lax.erf(v * ROOT_HALF))
    slope = upper + v * (ROOT_TWO_PI * jnp.exp(-0.5 * v * v))
    return v * upper, slope


def most_live(rows, wide):
    units = (wide + 1) // (SMALL + 1)
    live_rows = rows - rows // (LARGE + 1)
    return min(rows * wide, math.ceil(units * live_rows * LARGE / 2))


def block_kernel(n, s_count, rows, wide, ch, aligned, packed, *refs):
    (x_in, cot_in, live_in, gain1_in, shift1_in, gain2_in, shift2_in, w1_hbm, w2_hbm) = refs[:9]
    (out_block, out_input, out_wg1, out_wg2, out_gain1, out_shift1, out_gain2, out_shift2) = refs[9:17]
    (turned, wv, wf, x_t, pack, unpack, places, edge_send, edge_recv, cot_send, cot_recv, cotm, mask, masked,
     normed1, normed2, through, slope1, hid, hid2, pad, acc, hold, taken,
     part, psend, crecv, hsend, qrecv, wout, st_send, st_recv, row_send, row_recv,
     w_sem, wz_ssem, wz_rsem, wp_ssem, wp_rsem, e_ssem, e_rsem, ce_ssem, ce_rsem, ag_ssem, ag_rsem,
     st_ssem, st_rsem, row_ssem, row_rsem, c_ssem, c_rsem, q_ssem, q_rsem,
     f_ssem, f_rsem, h_ssem, h_rsem, o_sem) = refs[17:]

    z = lax.axis_index("chan")
    s = lax.axis_index("space")
    cells = rows * wide
    total = cells + 2 * wide
    band = cells // HALVES
    core, chip, chips = s % 2, s // 2, s_count // 2
    before, after = (s + s_count - 1) % s_count, (s + 1) % s_count
    tap_rows = 9 * ch

    barrier = pltpu.get_barrier_semaphore()

    @pl.loop(1, s_count)
    def _(k):
        pl.semaphore_signal(barrier, inc=1, device_id=(z, (s + k) % s_count), device_id_type=MESH)

    @pl.loop(1, n)
    def _(k):
        pl.semaphore_signal(barrier, inc=1, device_id=((z + k) % n, s), device_id_type=MESH)

    w_copies = []
    for which, source in enumerate((w1_hbm, w2_hbm)):
        for d in range(n):
            block = source.at[:, d * ch:(d + 1) * ch] if aligned else source.at[d]
            w_copies.append(pltpu.make_async_copy(block, wv.at[which, d], w_sem.at[which, d]))
    for copy in w_copies:
        copy.start()

    def chunked(fn, init, first=0, count=cells, unroll=UNROLL):
        def step(i, carry):
            return fn(pl.multiple_of(first + i * CHUNK, CHUNK), CHUNK, carry)
        return lax.fori_loop(0, count // CHUNK, step, init, unroll=unroll)

    lanes = 128
    tiles = ch * wide // lanes

    def from_flat(flat, put):
        for i in range(tiles):
            turned[i * lanes:(i + 1) * lanes, 0:rows] = flat[:, i * lanes:(i + 1) * lanes].astype(F32).T
        for w in range(wide):
            put(pl.ds(w, rows, stride=wide), turned[pl.ds(w, ch, stride=wide), 0:rows].T)

    def to_flat(source, flat):
        for w in range(wide):
            turned[pl.ds(w, ch, stride=wide), 0:rows] = source[pl.ds(w, rows, stride=wide), :].T
        for i in range(tiles):
            flat[:, i * lanes:(i + 1) * lanes] = turned[i * lanes:(i + 1) * lanes, 0:rows].T.astype(flat.dtype)

    def put_masked(at, value):
        masked[at, :] = value

    from_flat(x_in, put_masked)

    cell = lax.broadcasted_iota(jnp.int32, (cells, rows), 0)
    pick = (cell // wide == lax.broadcasted_iota(jnp.int32, (cells, rows), 1)).astype(F32).astype(BF16)
    column_of = lax.broadcasted_iota(jnp.int32, (cells, wide), 0) % wide
    picked = lax.dot_general(pick, live_in[...].astype(BF16), (((1,), (1,)), ((), ())), preferred_element_type=F32)
    picked = jnp.where(column_of == lax.broadcasted_iota(jnp.int32, (cells, wide), 1), picked, 0.0)
    mask[0:cells, :] = dot(picked.astype(BF16), jnp.ones((wide, ch), BF16))

    def load_main(start, size, carry):
        at = pl.ds(start, size)
        lv = mask[at, :]
        masked[at, :] = masked[at, :] * lv
        return carry

    chunked(load_main, 0)
    for side, start in ((0, 0), (1, cells - wide)):
        edge_send[side, 0] = masked[start:start + wide, :].astype(BF16)
        edge_send[side, 1] = mask[start:start + wide, :].astype(BF16)

    acc[...] = jnp.zeros_like(acc)
    st_send[...] = jnp.zeros_like(st_send)

    pl.semaphore_wait(barrier, s_count - 1 + n - 1)

    def edge_copy(side):
        return pltpu.make_async_remote_copy(
            src_ref=edge_send.at[side], dst_ref=edge_recv.at[1 - side],
            send_sem=e_ssem.at[side], recv_sem=e_rsem.at[1 - side],
            device_id=(z, before if side == 0 else after), device_id_type=MESH)

    for side in range(2):
        edge_copy(side).start()

    def cot_copy(side):
        return pltpu.make_async_remote_copy(
            src_ref=cot_send.at[side], dst_ref=cot_recv.at[1 - side],
            send_sem=ce_ssem.at[side], recv_sem=ce_rsem.at[1 - side],
            device_id=(z, before if side == 0 else after), device_id_type=MESH)

    def load_cotangent():
        def put(at, value):
            cotm[at, :] = value
        from_flat(cot_in, put)

        def live_only(start, size, carry):
            at = pl.ds(start, size)
            cotm[at, :] = cotm[at, :] * mask[at, :]
            return carry
        chunked(live_only, 0)
        for side, start in ((0, 0), (1, cells - wide)):
            cot_send[side] = cotm[start:start + wide, :].astype(BF16)
            cot_copy(side).start()

    def take_cotangent():
        for side in range(2):
            cot_copy(1 - side).wait_recv()
            at = slice(cells + side * wide, cells + (side + 1) * wide)
            cotm[at, :] = cot_recv[side].astype(F32) * mask[at, :]

    w_parts = math.gcd(tap_rows // 16, s_count)
    w_rows = tap_rows // w_parts
    w_mine = s % w_parts
    w_group = s - w_mine

    def wz_copy(which, k):
        at = pl.ds(w_mine * w_rows, w_rows)
        slot = n - k - 1
        return pltpu.make_async_remote_copy(
            src_ref=wv.at[which, (z + k) % n, at, :], dst_ref=wf.at[which, slot, at, :],
            send_sem=wz_ssem.at[which, slot], recv_sem=wz_rsem.at[which, slot],
            device_id=((z + k) % n, s), device_id_type=MESH)

    def wp_copy(which, slot, k, whose):
        at = pl.ds(whose * w_rows, w_rows)
        return pltpu.make_async_remote_copy(
            src_ref=wf.at[which, slot, at, :], dst_ref=wf.at[which, slot, at, :],
            send_sem=wp_ssem.at[which, slot, k], recv_sem=wp_rsem.at[which, slot, whose],
            device_id=(z, w_group + (w_mine + k) % w_parts), device_id_type=MESH)

    def weights_over_z(which):
        for copy in w_copies[which * n:(which + 1) * n]:
            copy.wait()

        @pl.loop(1, n)
        def _(k):
            wz_copy(which, k).start()

    def slot_of(block):
        return (block - z + n - 1) % n

    def weights_round(which):
        @pl.loop(1, n)
        def _(distance):
            for sign in (1, -1):
                block = z - distance * sign

                @pl.when((block >= 0) & (block < n))
                def _():
                    slot = slot_of(block)
                    wz_copy(which, n - 1 - slot).wait_recv()

                    @pl.loop(1, w_parts)
                    def _(k):
                        wp_copy(which, slot, k, w_mine).start()

    def weights_arrived(which, slot):
        @pl.loop(1, w_parts)
        def _(k):
            wp_copy(which, slot, k, (w_mine + k) % w_parts).wait_recv()

    def row_copy(slot, side):
        return pltpu.make_async_remote_copy(
            src_ref=row_send.at[slot, side], dst_ref=row_recv.at[slot, 1 - side],
            send_sem=row_ssem.at[slot, side], recv_sem=row_rsem.at[slot, 1 - side],
            device_id=(z, before if side == 0 else after), device_id_type=MESH)

    def send_rows(slot, ref):
        for side, start in ((0, 0), (1, cells - wide)):
            row_send[slot, side] = ref[start:start + wide, :]
            row_copy(slot, side).start()

    def take_rows(slot, ref):
        for side in range(2):
            row_copy(slot, 1 - side).wait_recv()
            ref[cells + side * wide:cells + (side + 1) * wide, :] = row_recv[slot, side]

    def st_copy(slot, k, whose):
        return pltpu.make_async_remote_copy(
            src_ref=st_send.at[slot], dst_ref=st_recv.at[slot, whose],
            send_sem=st_ssem.at[slot, k], recv_sem=st_rsem.at[slot, whose],
            device_id=(z, (s + k) % s_count), device_id_type=MESH)

    def send_stats(slot, values):
        for i, v in enumerate(values):
            st_send[slot, i:i + 1, :] = v
        for k in range(1, s_count):
            st_copy(slot, k, s).start()
        st_recv[slot, s] = st_send[slot]

    def take_stats(slot):
        for k in range(1, s_count):
            st_copy(slot, k, (s + k) % s_count).wait_recv()

    strip = 8
    column = lax.broadcasted_iota(jnp.int32, (strip * wide, ch), 0) % wide

    def shift(target, first, count):
        size = count * wide
        where = column[:size]
        here = pad[pl.ds(8 + first * wide, size), :]
        left = jnp.where(where == 0, 0.0, pad[pl.ds(7 + first * wide, size), :])
        right = jnp.where(where == wide - 1, 0.0, pad[pl.ds(9 + first * wide, size), :])
        for b, v in enumerate((left, here, right)):
            target[pl.ds(first, count), :, b * ch:(b + 1) * ch] = v.astype(BF16).reshape(count, wide, ch)

    edge = 2 * wide
    ag_rows = ((0, edge + packed), (edge + packed, packed))
    band_rows = rows // HALVES

    def unpack_some(ph, block, q, target):
        if q != 1:
            pad[8:8 + wide, :] = hold[ph, block, 0:wide, :].astype(F32)
            pad[8 + wide + cells:8 + 2 * wide + cells, :] = hold[ph, block, wide:edge, :].astype(F32)
            shift(target, 0, 1)
            shift(target, rows + 1, 1)
        for h in range(HALVES) if q is None else (q,):
            pad[8 + wide + h * band:8 + wide + (h + 1) * band, :] = dot(
                unpack[h], hold[ph, block, edge + h * packed:edge + (h + 1) * packed, :])
            for i in range(band_rows // strip):
                shift(target, 1 + h * band_rows + i * strip, strip)

    def add_conv(q, field, taps, turned_taps=None):
        first = band_rows - 1 if q == 1 else 0
        last = band_rows - 1 if q == 0 else rows
        count = last - first
        lhs = field[first:last + 2, :, :].reshape((count + 2) * wide, 3 * ch)
        if turned_taps is None:
            value = dot(lhs, jnp.concatenate([taps(a) for a in range(3)], axis=1))
        else:
            rhs = jnp.concatenate([
                jnp.concatenate([turned_taps(3 * (2 - a) + 2 - b) for b in range(3)], axis=1) for a in range(3)], axis=0)
            value = lax.dot_general(lhs, rhs, (((1,), (1,)), ((), ())), preferred_element_type=F32)
        at = pl.ds(first * wide, count * wide)
        acc[at, :] = acc[at, :] + sum(
            value[a * wide:(a + count) * wide, a * ch:(a + 1) * ch] for a in range(3))

    def ag_copy(ph, block, q, sign):
        at = pl.ds(*ag_rows[q])
        return pltpu.make_async_remote_copy(
            src_ref=hold.at[ph, block, at, :], dst_ref=hold.at[ph, block, at, :],
            send_sem=ag_ssem.at[ph, (1 - sign) // 2, block, q], recv_sem=ag_rsem.at[ph, block, q],
            device_id=(z + sign, s), device_id_type=MESH)

    def pack_field(ph, source, fill=None, first=None):
        if fill is not None:
            fill(cells, edge, 0)
        hold[ph, z, 0:edge, :] = source[cells:cells + edge, :].astype(BF16)
        for q in range(HALVES):
            if first is not None:
                first(q)
            if fill is not None:
                chunked(fill, 0, q * band, band)
            hold[ph, z, edge + q * packed:edge + (q + 1) * packed, :] = dot(
                pack[q], source[q * band:(q + 1) * band, :].astype(BF16)).astype(BF16)
            for sign in (1, -1):
                @pl.when((z + sign >= 0) & (z + sign < n))
                def _():
                    ag_copy(ph, z, q, sign).start()

    def inside(slice_at):
        return (slice_at >= 0) & (slice_at < n)

    def take_and_pass(ph, k, q, sign, passes=True, takes=True):
        block = z - k * sign

        @pl.when((k > 0) & inside(block))
        def _():
            if passes and takes:
                ag_copy(ph, block, q, sign).wait_recv()

            @pl.when(inside(z + sign))
            def _():
                if passes:
                    if not takes:
                        ag_copy(ph, block, q, sign).wait_recv()
                    ag_copy(ph, block, q, sign).start()

            if not passes:
                @pl.when(jnp.logical_not(inside(z + sign)))
                def _():
                    ag_copy(ph, block, q, sign).wait_recv()

    near = jnp.where(z < n - n // 2, 1, 0)

    last_step = jnp.maximum(z, n - 1 - z)

    def consume_way(k, q, way, consume):
        block = z - k * (1 - 2 * way)
        valid = (k >= 0) & (k < n) & inside(block) & ((k > 0) | (way == near))

        @pl.when(valid & (k == last_step))
        def _():
            consume(k, block, q)

        if q == HALVES - 1:
            @pl.when(valid & (k < last_step))
            def _():
                consume(k, block, None)

    def take_both(ph, k, q, **how):
        @pl.loop(0, 2)
        def _(i):
            way = (near + i) % 2
            take_and_pass(ph, k, q, 1 - 2 * way, **how)

    def gather(ph, consume, each):
        @pl.loop(0, n)
        def _(k):
            for q in range(HALVES):
                take_both(ph, k, q)
                if q:
                    consume_way(k, q - 1, 1 - near, consume)
                else:
                    consume_way(k - 1, HALVES - 1, 1 - near, consume)
                consume_way(k, q, near, consume)
            each(k)

    def gather_passing_first(ph, consume, each):
        @pl.loop(0, n)
        def _(k):
            @pl.when(k == 1)
            def _():
                @pl.loop(1, n)
                def _(ahead):
                    for q in range(HALVES):
                        take_both(ph, ahead, q, takes=False)
            for q in range(HALVES):
                take_both(ph, k, q, passes=False)

                @pl.loop(0, 2)
                def _(i):
                    consume_way(k, q, (near + i) % 2, consume)
            each(k)

    last_pass = jnp.maximum(jnp.where(z < n - 1, z, 0), jnp.where(z > 0, n - 1 - z, 0))

    def forward(ph, field):
        def consume(k, block, q):
            into = taken.at[block]
            unpack_some(ph, block, q, into)

            @pl.when(k == 0)
            def _():
                add_conv(q, into, lambda a: wv[ph, z, 3 * a * ch:3 * (a + 1) * ch, :])

            @pl.when(k > 0)
            def _():
                slot = slot_of(block)
                if q != 1:
                    weights_arrived(ph, slot)
                add_conv(q, into, lambda a: wf[ph, slot, 3 * a * ch:3 * (a + 1) * ch, :])

        def each(k):
            if ph == 0:
                @pl.when(k == 0)
                def _():
                    weights_round(0)

                @pl.when(k == 1)
                def _():
                    weights_over_z(1)
        (gather if ph else gather_passing_first)(ph, consume, each)

    def turn_field(ph, field):
        main = [field[start:start + ch, :].T for start in range(0, cells, ch)]
        ends = field[cells:cells + edge, :]
        if edge < ch:
            ends = jnp.concatenate([ends, jnp.zeros((ch - edge, ch), F32)], axis=0)
        ends = ends.T
        for i, here in enumerate(main):
            left = jnp.concatenate(
                [ends[:, 0:wide] if i == 0 else main[i - 1][:, ch - wide:], here[:, 0:ch - wide]], axis=1)
            right = jnp.concatenate(
                [here[:, wide:], main[i + 1][:, 0:wide] if i + 1 < len(main) else ends[:, wide:edge]], axis=1)
            for a, v in enumerate((left, here, right)):
                x_t[ph, a * ch:(a + 1) * ch, i * ch:(i + 1) * ch] = v.astype(BF16)

    half_rows = tap_rows // 2
    owners = math.gcd(half_rows // 16, chips)
    piece = half_rows // owners

    def c_copy(ph, j):
        return pltpu.make_async_remote_copy(
            src_ref=psend.at[ph, j], dst_ref=crecv.at[ph, j],
            send_sem=c_ssem.at[ph, j], recv_sem=c_rsem.at[ph, j],
            device_id=(z, chip * 2 + 1 - core), device_id_type=MESH)

    def q_copy(ph, j, e, whose, owner):
        return pltpu.make_async_remote_copy(
            src_ref=hsend.at[ph, j, owner], dst_ref=qrecv.at[ph, j, whose],
            send_sem=q_ssem.at[ph, j, e], recv_sem=q_rsem.at[ph, j, whose],
            device_id=(z, ((chip + e) % chips) * 2 + core), device_id_type=MESH)

    def f_copy(ph, j, e, owner):
        return pltpu.make_async_remote_copy(
            src_ref=wout.at[ph, j, core, owner], dst_ref=wout.at[ph, j, core, owner],
            send_sem=f_ssem.at[ph, j, e], recv_sem=f_rsem.at[ph, j, owner],
            device_id=(z, ((chip + e) % chips) * 2 + core), device_id_type=MESH)

    def h_copy(ph, j, whose):
        return pltpu.make_async_remote_copy(
            src_ref=wout.at[ph, j, whose], dst_ref=wout.at[ph, j, whose],
            send_sem=h_ssem.at[ph, j], recv_sem=h_rsem.at[ph, j],
            device_id=(z, chip * 2 + 1 - core), device_id_type=MESH)

    def o_copy(ph, j):
        target = (out_wg1, out_wg2)[ph]
        if aligned:
            target = target.at[:, :, :, pl.ds(pl.multiple_of(j * ch, ch), ch)]
        else:
            target = target.at[j]
        return pltpu.make_async_copy(wout.at[ph, j], target, o_sem.at[ph, j])

    def sum_cores(ph, j):
        for o in range(owners):
            psend[ph, j, o] = part[ph, j, 1 - core, o].astype(BF16)
        c_copy(ph, j).start()

    def sum_chips(ph, j):
        c_copy(ph, j).wait_recv()
        for o in range(owners):
            v = part[ph, j, core, o] + crecv[ph, j, o].astype(F32)
            part[ph, j, core, o] = v
            hsend[ph, j, o] = v.astype(BF16)

        @pl.loop(1, chips)
        def _(e):
            peer = (chip + e) % chips

            @pl.when(peer < owners)
            def _():
                q_copy(ph, j, e, chip, peer).start()

    def spread_chips(ph, j):
        @pl.when(chip < owners)
        def _():
            @pl.loop(1, chips)
            def _(e):
                q_copy(ph, j, e, (chip + e) % chips, chip).wait_recv()
            v = part[ph, j, core, chip]
            for e in range(1, chips):
                v = v + qrecv[ph, j, (chip + e) % chips].astype(F32)
            wout[ph, j, core, chip] = v.astype(BF16)

            @pl.loop(1, chips)
            def _(e):
                f_copy(ph, j, e, chip).start()

    def spread_cores(ph, j):
        @pl.loop(1, chips)
        def _(e):
            peer = (chip + e) % chips

            @pl.when(peer < owners)
            def _():
                f_copy(ph, j, e, peer).wait_recv()
        h_copy(ph, j, core).start()

    def finish(ph, j):
        h_copy(ph, j, 1 - core).wait_recv()
        o_copy(ph, j).start()

    def put_part(ph, j, tap, value):
        start = tap * ch
        done = 0
        while done < ch:
            row = start + done
            side, o, at = row // half_rows, row % half_rows // piece, row % piece
            size = min(ch - done, piece - at)
            part[ph, j, side, o, at:at + size, :] = value[done:done + size, :]
            done += size

    stages = (sum_cores, sum_chips, spread_chips, spread_cores, finish)

    def of_step(k, fn):
        @pl.loop(0, 2)
        def _(way):
            block = z - k * (1 - 2 * way)

            @pl.when((k >= 0) & (k < n) & inside(block) & ((k > 0) | (way == 0)))
            def _():
                fn(block)

    passing = last_pass > 0

    def made_at(step):
        first = jnp.where(passing & (step > 0), jnp.where(step == last_pass, 1, step + 1), step)
        return first, step + 1

    def advance(ph, k):
        for age in range(1, len(stages)):
            step = k - age

            @pl.when((step >= 0) & (step < n))
            def _():
                @pl.loop(*made_at(step))
                def _(made):
                    of_step(made, functools.partial(stages[age], ph))

    def advance_all(ph, age):
        @pl.loop(0, n)
        def _(j):
            stages[age](ph, j)

    def field_grad(ph, block):
        grad = taken[block, 1:rows + 1, :, :].reshape(cells, 3 * ch)
        value = dot(x_t[ph], grad)
        for a in range(3):
            for b in range(3):
                put_part(ph, block, 3 * a + b, value[a * ch:(a + 1) * ch, (2 - b) * ch:(3 - b) * ch])

    def make_grad(ph, block):
        field_grad(ph, block)
        sum_cores(ph, block)

    def backward(ph):
        last = ph == 0

        def consume(k, block, q):
            into = taken.at[block]
            unpack_some(2 + ph, block, q, into)
            if last and q != 0:
                @pl.when((k == 0) | (k >= last_pass))
                def _():
                    make_grad(ph, block)
            add_conv(q, into, None, lambda t: wv[ph, block, t * ch:(t + 1) * ch, :])

        def each(k):
            first, end = made_at(k)
            if last:
                @pl.loop(first, end - 1)
                def _(step):
                    of_step(step, functools.partial(make_grad, ph))
                advance(ph, k)
                for age in range(2, len(stages)):
                    @pl.when(k == age - 2)
                    def _():
                        advance_all(1, age)
            else:
                @pl.loop(first, jnp.where(passing | (k < n - 2), end, first))
                def _(step):
                    of_step(step, functools.partial(make_grad, ph))
        gather(2 + ph, consume, each)

    def fold(v):
        return jnp.sum(v.reshape(v.shape[0] // 8, 8, ch), axis=0)

    def flatten(v):
        return jnp.sum(v, axis=0, keepdims=True)

    zero = jnp.zeros((8, ch), F32)

    def local_moments(ref):
        def sums(start, size, carry):
            at = pl.ds(start, size)
            m = mask[at, :]
            return carry[0] + fold(ref[at, :] * m), carry[1] + fold(m)
        added, number = (flatten(v) for v in chunked(sums, (zero, zero), unroll=8))
        middle = added / jnp.maximum(number, 1.0)

        def spread(start, size, carry):
            at = pl.ds(start, size)
            c = (ref[at, :] - middle) * mask[at, :]
            return carry + fold(c * c)
        return added, number, flatten(chunked(spread, zero, unroll=8))

    def moments(slot):
        take_stats(slot)
        got = [st_recv[slot, k] for k in range(s_count)]
        added = sum(g[0:1] for g in got)
        number = sum(g[1:2] for g in got)
        mean = added / number
        spread = 0.0
        for g in got:
            off = g[0:1] / jnp.maximum(g[1:2], 1.0) - mean
            spread = spread + (g[2:3] + g[1:2] * off * off)
        return mean, lax.rsqrt(spread / number + EPSILON), number

    def everywhere(fn):
        chunked(fn, 0)
        fn(cells, 2 * wide, 0)

    gain1, shift1, gain2, shift2 = (r[...] for r in (gain1_in, shift1_in, gain2_in, shift2_in))

    weights_over_z(0)

    below = lax.broadcasted_iota(jnp.int32, (band, band), 1) < lax.broadcasted_iota(jnp.int32, (band, band), 0)
    below = below.astype(F32).astype(BF16)

    def make_pack(h):
        lv = mask[h * band:(h + 1) * band, :]
        place = jnp.where(lv > 0.0, dot(below, lv.astype(BF16)), -1.0)
        places[h] = place
        across = place.T[0:1, :]
        spot = lax.broadcasted_iota(jnp.int32, (packed, band), 0).astype(F32)
        pack[h] = jnp.where(spot == across, 1.0, 0.0).astype(BF16)

    def make_unpack(h):
        for start in range(0, packed, ch):
            size = min(ch, packed - start)
            spot = start + lax.broadcasted_iota(jnp.int32, (band, size), 1)
            unpack[h, :, start:start + size] = jnp.where(
                places[h, :, :size] == spot.astype(F32), 1.0, 0.0).astype(BF16)

    for side in range(2):
        edge_copy(1 - side).wait_recv()
        there = jnp.where(s > 0, 1.0, 0.0) if side == 0 else jnp.where(s < s_count - 1, 1.0, 0.0)
        at = slice(cells + side * wide, cells + (side + 1) * wide)
        masked[at, :] = edge_recv[side, 0].astype(F32) * there
        mask[at, :] = edge_recv[side, 1].astype(F32) * there

    pack_field(0, masked, first=make_pack)
    for h in range(HALVES):
        make_unpack(h)
    forward(0, masked)
    send_rows(0, acc)
    send_stats(0, local_moments(acc))
    weights_round(1)
    load_cotangent()
    mean1, scale1, count = moments(0)

    def activate_one(start, size, carry):
        at = pl.ds(start, size)
        main = start is not cells
        nv = ((acc if main else normed1)[at, :] - mean1) * scale1
        normed1[at, :] = nv
        hid[at, :] = gelu_parts(nv * gain1 + shift1)[0] * mask[at, :]
        if main:
            acc[at, :] = jnp.zeros((size, ch), F32)
        return carry

    def slope_one(start, size, carry):
        at = pl.ds(start, size)
        slope1[at, :] = gelu_parts(normed1[at, :] * gain1 + shift1)[1] * mask[at, :]
        return carry

    take_rows(0, normed1)
    pack_field(1, hid, activate_one)
    everywhere(slope_one)
    forward(1, hid)
    send_rows(1, acc)
    send_stats(1, local_moments(acc))
    turn_field(0, masked)
    turn_field(1, hid)
    mean2, scale2, _ = moments(1)

    def activate_two(source, start, size):
        at = pl.ds(start, size)
        nv = (source[at, :] - mean2) * scale2
        normed2[at, :] = nv
        value, slope = gelu_parts(nv * gain2 + shift2 + masked[at, :])
        t = cotm[at, :] * slope
        through[at, :] = t
        return value, nv, t

    def activate_main(start, size, carry):
        value, nv, t = activate_two(acc, start, size)
        at = pl.ds(start, size)
        hid2[at, :] = value * mask[at, :]
        acc[at, :] = jnp.zeros((size, ch), F32)
        return carry[0] + fold(t * nv), carry[1] + fold(t)

    send_stats(2, [flatten(v) for v in chunked(activate_main, (zero, zero))])
    take_rows(1, normed2)
    take_cotangent()
    activate_two(normed2, cells, edge)
    to_flat(hid2, out_block)

    def gradient_sums(slot):
        take_stats(slot)
        got = [st_recv[slot, k] for k in range(s_count)]
        return sum(g[0:1] for g in got), sum(g[1:2] for g in got)

    def norm_back(upstream, normed, gain, scale, sums):
        gain_grad, shift_grad = sums
        factor = gain * scale
        level, tilt = shift_grad / count, gain_grad / count

        def fill(start, size, carry):
            at = pl.ds(start, size)
            v = upstream[at, :] - mask[at, :] * (level + normed[at, :] * tilt)
            hid[at, :] = factor * v
            return carry
        return fill

    sums2 = gradient_sums(2)
    pack_field(3, hid, norm_back(through, normed2, gain2, scale2, sums2))
    backward(1)

    send_rows(2, acc)

    def inner_main(start, size, carry):
        at = pl.ds(start, size)
        v = acc[at, :] * slope1[at, :]
        slope1[at, :] = v
        acc[at, :] = jnp.zeros((size, ch), F32)
        return carry[0] + fold(v * normed1[at, :]), carry[1] + fold(v)

    send_stats(3, [flatten(v) for v in chunked(inner_main, (zero, zero), unroll=4)])

    @pl.when(jnp.logical_not(passing))
    def _():
        for step in range(n - 2, n):
            of_step(step, functools.partial(make_grad, 1))
    for side in range(2):
        row_copy(2, 1 - side).wait_recv()
        at = slice(cells + side * wide, cells + (side + 1) * wide)
        slope1[at, :] = row_recv[2, side] * slope1[at, :]
    sums1 = gradient_sums(3)
    pack_field(2, hid, norm_back(slope1, normed1, gain1, scale1, sums1))
    advance_all(1, 1)
    backward(0)
    advance(0, n)

    def finish_input(start, size, carry):
        at = pl.ds(start, size)
        acc[at, :] = (acc[at, :] + through[at, :]) * mask[at, :]
        return carry

    chunked(finish_input, 0, unroll=8)
    to_flat(acc, out_input)
    out_gain1[...], out_shift1[...] = sums1
    out_gain2[...], out_shift2[...] = sums2
    for extra in range(1, len(stages) - 1):
        advance(0, n + extra)

    for side in range(2):
        edge_copy(side).wait_send()
        cot_copy(side).wait_send()
        for slot in range(3):
            row_copy(slot, side).wait_send()

    @pl.loop(1, s_count)
    def _(k):
        for slot in range(4):
            st_copy(slot, k, s).wait_send()

    @pl.loop(1, n)
    def _(k):
        for which in range(2):
            wz_copy(which, k).wait_send()

    @pl.loop(1, w_parts)
    def _(k):
        for which in range(2):
            for slot in range(n - 1):
                wp_copy(which, slot, k, w_mine).wait_send()

    @pl.loop(0, n)
    def _(k):
        for sign in (1, -1):
            block = z - k * sign

            @pl.when((block >= 0) & (block < n) & (z + sign >= 0) & (z + sign < n))
            def _():
                for ph in range(4):
                    for q in range(HALVES):
                        ag_copy(ph, block, q, sign).wait_send()

    @pl.loop(0, n)
    def _(j):
        for ph in range(2):
            c_copy(ph, j).wait_send()
            h_copy(ph, j, core).wait_send()
            o_copy(ph, j).wait()

            @pl.loop(1, chips)
            def _(e):
                peer = (chip + e) % chips

                @pl.when(peer < owners)
                def _():
                    q_copy(ph, j, e, chip, peer).wait_send()

                @pl.when(chip < owners)
                def _():
                    f_copy(ph, j, e, chip).wait_send()


def finish_kernel(count, *refs):
    ins, outs = refs[:count], refs[count:2 * count]
    narrow, wide, in_sem, out_sem, take_sem, give_sem = refs[2 * count:2 * count + 6]
    held = refs[2 * count + 6:]
    rows = narrow.shape[1] // FINISH_PARTS
    parts = [(w, i, pl.ds(i * rows, rows)) for i in range(FINISH_PARTS) for w in range(2)]
    loads = [pltpu.make_async_copy(ins[w].at[at, :], narrow.at[w, at, :], in_sem.at[w, i]) for w, i, at in parts]
    stores = [pltpu.make_async_copy(wide.at[w, at, :], outs[w].at[at, :], out_sem.at[w, i]) for w, i, at in parts]
    takes = [pltpu.make_async_copy(ins[2 + k], v, take_sem.at[k]) for k, v in enumerate(held)]
    gives = [pltpu.make_async_copy(v, outs[2 + k], give_sem.at[k]) for k, v in enumerate(held)]
    for copy in loads + takes:
        copy.start()
    for load, store, (w, i, at) in zip(loads, stores, parts):
        load.wait()
        wide[w, at, :] = narrow[w, at, :].astype(F32)
        store.start()
    for take, give in zip(takes, gives):
        take.wait()
        give.start()
    for copy in stores + gives:
        copy.wait()


def per_device(n, s_count, blocks, weight_one, weight_two, gain_one, shift_one, gain_two, shift_two, cell_live, cotangent):
    rows, wide = cell_live.shape
    ch = blocks.shape[1] // wide
    cells = rows * wide
    total = cells + 2 * wide
    packed = -(-most_live(rows // HALVES, wide) // 16) * 16
    aligned = ch % 128 == 0
    chips = s_count // 2
    tap_rows = 9 * ch
    half_rows = tap_rows // 2
    owners = math.gcd(half_rows // 16, chips)
    piece = half_rows // owners

    if aligned:
        weight_one, weight_two = (w.reshape(tap_rows, n * ch) for w in (weight_one, weight_two))
    else:
        weight_one, weight_two = (
            w.reshape(tap_rows, n, ch).transpose(1, 0, 2) for w in (weight_one, weight_two))
    grad_shape = (2, owners, piece, n * ch) if aligned else (n, 2, owners, piece, ch)
    vmem = pl.BlockSpec(memory_space=pltpu.VMEM)
    hbm = pl.BlockSpec(memory_space=pl.ANY)
    sem = pltpu.SemaphoreType.DMA
    field = pltpu.VMEM((total, ch), F32)
    scratch = [
        pltpu.VMEM((ch * wide, 128), F32),
        pltpu.VMEM((2, n, tap_rows, ch), BF16),
        pltpu.VMEM((2, n - 1, tap_rows, ch), BF16),
        pltpu.VMEM((2, 3 * ch, cells), BF16),
        pltpu.VMEM((HALVES, packed, cells // HALVES), BF16),
        pltpu.VMEM((HALVES, cells // HALVES, packed), BF16),
        pltpu.VMEM((HALVES, cells // HALVES, ch), F32),
        pltpu.VMEM((2, 2, wide, ch), BF16),
        pltpu.VMEM((2, 2, wide, ch), BF16),
        pltpu.VMEM((2, wide, ch), BF16),
        pltpu.VMEM((2, wide, ch), BF16),
        field, field, field, field, field, field, field, field, field,
        pltpu.VMEM((total + 16, ch), F32),
        pltpu.VMEM((cells, ch), F32),
        pltpu.VMEM((4, n, 2 * wide + HALVES * packed, ch), BF16),
        pltpu.VMEM((n, rows + 2, wide, 3 * ch), BF16),
        pltpu.VMEM((2, n, 2, owners, piece, ch), F32),
        pltpu.VMEM((2, n, owners, piece, ch), BF16),
        pltpu.VMEM((2, n, owners, piece, ch), BF16),
        pltpu.VMEM((2, n, owners, piece, ch), BF16),
        pltpu.VMEM((2, n, chips, piece, ch), BF16),
        pltpu.VMEM((2, n, 2, owners, piece, ch), BF16),
        pltpu.VMEM((4, 8, ch), F32),
        pltpu.VMEM((4, s_count, 8, ch), F32),
        pltpu.VMEM((3, 2, wide, ch), F32),
        pltpu.VMEM((3, 2, wide, ch), F32),
        sem((2, n)),
        sem((2, n)), sem((2, n)),
        sem((2, n - 1, s_count)), sem((2, n - 1, s_count)),
        sem((2,)), sem((2,)),
        sem((2,)), sem((2,)),
        sem((4, 2, n, HALVES)), sem((4, n, HALVES)),
        sem((4, s_count)), sem((4, s_count)),
        sem((3, 2)), sem((3, 2)),
        sem((2, n)), sem((2, n)),
        sem((2, n, chips)), sem((2, n, chips)),
        sem((2, n, chips)), sem((2, n, chips)),
        sem((2, n)), sem((2, n)),
        sem((2, n)),
    ]
    block_out, input_grad, wg1, wg2, *sums = pl.pallas_call(
        functools.partial(block_kernel, n, s_count, rows, wide, ch, aligned, packed),
        out_shape=(
            jax.ShapeDtypeStruct((rows, ch * wide), BF16),
            jax.ShapeDtypeStruct((rows, ch * wide), F32),
            jax.ShapeDtypeStruct(grad_shape, BF16),
            jax.ShapeDtypeStruct(grad_shape, BF16),
            *[jax.ShapeDtypeStruct((1, ch), F32)] * 4,
        ),
        in_specs=[vmem] * 7 + [hbm] * 2,
        out_specs=(vmem, vmem, hbm, hbm, vmem, vmem, vmem, vmem),
        scratch_shapes=scratch,
        compiler_params=pltpu.CompilerParams(
            collective_id=0, has_side_effects=True, vmem_limit_bytes=60 * 1024 * 1024),
    )(blocks, cotangent, cell_live.T,
      *(v.reshape(1, ch) for v in (gain_one, shift_one, gain_two, shift_two)), weight_one, weight_two)

    if not aligned:
        def whole(grad):
            grad = grad.reshape(n, tap_rows, ch).transpose(1, 0, 2)
            return grad.astype(F32).reshape(9, ch, n * ch)
        return (block_out, input_grad, whole(wg1), whole(wg2), *(v.reshape(ch) for v in sums))

    wg1, wg2 = (w.reshape(tap_rows, n * ch) for w in (wg1, wg2))
    wide_grad = jax.ShapeDtypeStruct((tap_rows, n * ch), F32)
    moved = (block_out, input_grad, *sums)
    grad1, grad2, *moved = pl.pallas_call(
        functools.partial(finish_kernel, 2 + len(moved)),
        out_shape=(wide_grad, wide_grad, *(jax.ShapeDtypeStruct(v.shape, v.dtype) for v in moved)),
        in_specs=[pl.BlockSpec(memory_space=pl.ANY)] * (2 + len(moved)),
        out_specs=[pl.BlockSpec(memory_space=pl.ANY)] * (2 + len(moved)),
        scratch_shapes=[
            pltpu.VMEM((2, tap_rows, n * ch), BF16), pltpu.VMEM((2, tap_rows, n * ch), F32),
            sem((2, FINISH_PARTS)), sem((2, FINISH_PARTS)), sem((len(moved),)), sem((len(moved),)),
            *(pltpu.VMEM(v.shape, v.dtype) for v in moved),
        ],
        compiler_params=pltpu.CompilerParams(vmem_limit_bytes=64 * 1024 * 1024),
    )(wg1, wg2, *moved)
    block_out, input_grad, *sums = moved
    grads = (g.reshape(9, ch, n * ch) for g in (grad1, grad2))
    return (block_out, input_grad, *grads, *(v.reshape(ch) for v in sums))


def solution(mesh):
    return jax.shard_map(
        functools.partial(per_device, mesh.shape["chan"], mesh.shape["space"]),
        mesh=mesh,
        in_specs=(
            P("space", "chan"),
            P(None, "chan", None),
            P(None, "chan", None),
            P("chan"),
            P("chan"),
            P("chan"),
            P("chan"),
            P("space", None),
            P("space", "chan"),
        ),
        out_specs=(
            P("space", "chan"),
            P("space", "chan"),
            P(None, "chan", None),
            P(None, "chan", None),
            P("chan"),
            P("chan"),
            P("chan"),
            P("chan"),
        ),
        check_vma=False,
    )
```

```python
import functools
import math

import jax
import jax.numpy as jnp
from jax import lax
from jax.experimental import pallas as pl
from jax.experimental.pallas import tpu as pltpu
from jax.sharding import PartitionSpec as P

EPSILON = 1e-05
MESH = pl.DeviceIdType.MESH
F32 = jnp.float32
BF16 = jnp.bfloat16
ROOT_HALF = 0.7071067811865476
ROOT_TWO_PI = 0.3989422804014327
CHUNK = 64
FINISH_PARTS = 4
UNROLL = 2
HALVES = 2
LARGE, SMALL = 7, 3


def dot(a, b):
    return jnp.dot(a, b, preferred_element_type=F32)


def gelu_parts(v):
    upper = 0.5 * (1.0 + lax.erf(v * ROOT_HALF))
    slope = upper + v * (ROOT_TWO_PI * jnp.exp(-0.5 * v * v))
    return v * upper, slope


def most_live(rows, wide):
    units = (wide + 1) // (SMALL + 1)
    live_rows = rows - rows // (LARGE + 1)
    return min(rows * wide, math.ceil(units * live_rows * LARGE / 2))


def block_kernel(n, s_count, rows, wide, ch, aligned, packed, *refs):
    (x_in, cot_in, live_in, gain1_in, shift1_in, gain2_in, shift2_in, w1_hbm, w2_hbm) = refs[:9]
    (out_block, out_input, out_wg1, out_wg2, out_gain1, out_shift1, out_gain2, out_shift2) = refs[9:17]
    (turned, wv, wf, x_t, pack, unpack, places, edge_send, edge_recv, cot_send, cot_recv, cotm, mask, masked,
     normed1, normed2, through, slope1, hid, hid2, pad, pad_edge, acc, hold, taken,
     part, psend, crecv, hsend, qrecv, wout, st_send, st_recv, row_send, row_recv,
     w_sem, wz_ssem, wz_rsem, wp_ssem, wp_rsem, e_ssem, e_rsem, ce_ssem, ce_rsem, ag_ssem, ag_rsem,
     st_ssem, st_rsem, row_ssem, row_rsem, c_ssem, c_rsem, q_ssem, q_rsem,
     f_ssem, f_rsem, h_ssem, h_rsem, o_sem) = refs[17:]

    z = lax.axis_index("chan")
    s = lax.axis_index("space")
    cells = rows * wide
    total = cells + 2 * wide
    band = cells // HALVES
    core, chip, chips = s % 2, s // 2, s_count // 2
    before, after = (s + s_count - 1) % s_count, (s + 1) % s_count
    tap_rows = 9 * ch

    barrier = pltpu.get_barrier_semaphore()

    @pl.loop(1, s_count)
    def _(k):
        pl.semaphore_signal(barrier, inc=1, device_id=(z, (s + k) % s_count), device_id_type=MESH)

    @pl.loop(1, n)
    def _(k):
        pl.semaphore_signal(barrier, inc=1, device_id=((z + k) % n, s), device_id_type=MESH)

    w_copies = []
    for which, source in enumerate((w1_hbm, w2_hbm)):
        for d in range(n):
            block = source.at[:, d * ch:(d + 1) * ch] if aligned else source.at[d]
            w_copies.append(pltpu.make_async_copy(block, wv.at[which, d], w_sem.at[which, d]))
        own = source.at[:, pl.ds(pl.multiple_of(z * ch, ch), ch)] if aligned else source.at[z]
        w_copies.append(pltpu.make_async_copy(own, wf.at[which, n - 1], w_sem.at[which, n]))
    for copy in w_copies:
        copy.start()

    def chunked(fn, init, first=0, count=cells):
        def step(i, carry):
            return fn(pl.multiple_of(first + i * CHUNK, CHUNK), CHUNK, carry)
        return lax.fori_loop(0, count // CHUNK, step, init, unroll=UNROLL)

    lanes = 128
    tiles = ch * wide // lanes

    def from_flat(flat, put):
        for i in range(tiles):
            turned[i * lanes:(i + 1) * lanes, 0:rows] = flat[:, i * lanes:(i + 1) * lanes].astype(F32).T
        for w in range(wide):
            put(pl.ds(w, rows, stride=wide), turned[pl.ds(w, ch, stride=wide), 0:rows].T)

    def to_flat(source, flat):
        for w in range(wide):
            turned[pl.ds(w, ch, stride=wide), 0:rows] = source[pl.ds(w, rows, stride=wide), :].T
        for i in range(tiles):
            flat[:, i * lanes:(i + 1) * lanes] = turned[i * lanes:(i + 1) * lanes, 0:rows].T.astype(flat.dtype)

    def put_masked(at, value):
        masked[at, :] = value

    from_flat(x_in, put_masked)

    cell = lax.broadcasted_iota(jnp.int32, (cells, rows), 0)
    pick = (cell // wide == lax.broadcasted_iota(jnp.int32, (cells, rows), 1)).astype(F32).astype(BF16)
    column_of = lax.broadcasted_iota(jnp.int32, (cells, wide), 0) % wide
    picked = lax.dot_general(pick, live_in[...].astype(BF16), (((1,), (1,)), ((), ())), preferred_element_type=F32)
    picked = jnp.where(column_of == lax.broadcasted_iota(jnp.int32, (cells, wide), 1), picked, 0.0)
    mask[0:cells, :] = dot(picked.astype(BF16), jnp.ones((wide, ch), BF16))

    def load_main(start, size, carry):
        at = pl.ds(start, size)
        lv = mask[at, :]
        masked[at, :] = masked[at, :] * lv
        return carry

    chunked(load_main, 0)
    for side, start in ((0, 0), (1, cells - wide)):
        edge_send[side, 0] = masked[start:start + wide, :].astype(BF16)
        edge_send[side, 1] = mask[start:start + wide, :].astype(BF16)

    lead = 2 * wide
    acc[...] = jnp.zeros_like(acc)
    for block in range(n):
        taken[block, 0:2, :, :] = jnp.zeros((2, wide, 3 * ch), BF16)
    st_send[...] = jnp.zeros_like(st_send)

    pl.semaphore_wait(barrier, s_count - 1 + n - 1)

    def edge_copy(side):
        return pltpu.make_async_remote_copy(
            src_ref=edge_send.at[side], dst_ref=edge_recv.at[1 - side],
            send_sem=e_ssem.at[side], recv_sem=e_rsem.at[1 - side],
            device_id=(z, before if side == 0 else after), device_id_type=MESH)

    for side in range(2):
        edge_copy(side).start()

    def cot_copy(side):
        return pltpu.make_async_remote_copy(
            src_ref=cot_send.at[side], dst_ref=cot_recv.at[1 - side],
            send_sem=ce_ssem.at[side], recv_sem=ce_rsem.at[1 - side],
            device_id=(z, before if side == 0 else after), device_id_type=MESH)

    def load_cotangent():
        def put(at, value):
            cotm[at, :] = value
        from_flat(cot_in, put)

        def live_only(start, size, carry):
            at = pl.ds(start, size)
            cotm[at, :] = cotm[at, :] * mask[at, :]
            return carry
        chunked(live_only, 0)
        for side, start in ((0, 0), (1, cells - wide)):
            cot_send[side] = cotm[start:start + wide, :].astype(BF16)
            cot_copy(side).start()

    def take_cotangent():
        for side in range(2):
            cot_copy(1 - side).wait_recv()
            at = slice(cells + side * wide, cells + (side + 1) * wide)
            cotm[at, :] = cot_recv[side].astype(F32) * mask[at, :]

    w_parts = math.gcd(tap_rows // 16, s_count)
    w_rows = tap_rows // w_parts
    w_mine = s % w_parts
    w_group = s - w_mine

    def wz_copy(which, k):
        at = pl.ds(w_mine * w_rows, w_rows)
        slot = n - k - 1
        return pltpu.make_async_remote_copy(
            src_ref=wv.at[which, (z + k) % n, at, :], dst_ref=wf.at[which, slot, at, :],
            send_sem=wz_ssem.at[which, slot], recv_sem=wz_rsem.at[which, slot],
            device_id=((z + k) % n, s), device_id_type=MESH)

    def wp_copy(which, slot, k, whose):
        at = pl.ds(whose * w_rows, w_rows)
        return pltpu.make_async_remote_copy(
            src_ref=wf.at[which, slot, at, :], dst_ref=wf.at[which, slot, at, :],
            send_sem=wp_ssem.at[which, slot, k], recv_sem=wp_rsem.at[which, slot, whose],
            device_id=(z, w_group + (w_mine + k) % w_parts), device_id_type=MESH)

    def weights_over_z(which):
        for copy in w_copies[which * (n + 1):(which + 1) * (n + 1)]:
            copy.wait()

        @pl.loop(1, n)
        def _(k):
            wz_copy(which, k).start()

    def slot_of(block):
        return (block - z + n - 1) % n

    def weights_round(which):
        @pl.loop(1, n)
        def _(distance):
            for sign in (1, -1):
                block = z - distance * sign

                @pl.when((block >= 0) & (block < n))
                def _():
                    slot = slot_of(block)
                    wz_copy(which, n - 1 - slot).wait_recv()

                    @pl.loop(1, w_parts)
                    def _(k):
                        wp_copy(which, slot, k, w_mine).start()

    def weights_arrived(which, slot):
        @pl.loop(1, w_parts)
        def _(k):
            wp_copy(which, slot, k, (w_mine + k) % w_parts).wait_recv()

    def row_copy(slot, side):
        return pltpu.make_async_remote_copy(
            src_ref=row_send.at[slot, side], dst_ref=row_recv.at[slot, 1 - side],
            send_sem=row_ssem.at[slot, side], recv_sem=row_rsem.at[slot, 1 - side],
            device_id=(z, before if side == 0 else after), device_id_type=MESH)

    def send_rows(slot):
        for side, start in ((0, lead), (1, lead + cells - wide)):
            row_send[slot, side] = acc[start:start + wide, :]
            row_copy(slot, side).start()

    def take_rows(slot, ref):
        for side in range(2):
            row_copy(slot, 1 - side).wait_recv()
            ref[cells + side * wide:cells + (side + 1) * wide, :] = row_recv[slot, side]

    def st_copy(slot, k, whose):
        return pltpu.make_async_remote_copy(
            src_ref=st_send.at[slot], dst_ref=st_recv.at[slot, whose],
            send_sem=st_ssem.at[slot, k], recv_sem=st_rsem.at[slot, whose],
            device_id=(z, (s + k) % s_count), device_id_type=MESH)

    def send_stats(slot, values):
        for i, v in enumerate(values):
            st_send[slot, i:i + 1, :] = v
        for k in range(1, s_count):
            st_copy(slot, k, s).start()
        st_recv[slot, s] = st_send[slot]

    def take_stats(slot):
        for k in range(1, s_count):
            st_copy(slot, k, (s + k) % s_count).wait_recv()

    strip = 8
    column = lax.broadcasted_iota(jnp.int32, (strip * wide, ch), 0) % wide

    def shift(source, start, count, target, first):
        size = count * wide
        where = column[:size]
        here = source[8 + start:8 + start + size, :]
        left = jnp.where(where == 0, 0.0, source[7 + start:7 + start + size, :])
        right = jnp.where(where == wide - 1, 0.0, source[9 + start:9 + start + size, :])
        for b, v in enumerate((left, here, right)):
            target[pl.ds(first + 3, count), :, b * ch:(b + 1) * ch] = v.astype(BF16).reshape(count, wide, ch)

    edge = 2 * wide
    held = wide + packed
    band_rows = rows // HALVES
    conv_rows = (rows + 2) // HALVES

    def held_rows(q):
        start = q * held
        return pl.ds(pl.multiple_of(start, wide), wide), pl.ds(pl.multiple_of(start + wide, wide), packed)

    def unpack_half(ph, block, q, target):
        edge_at, cells_at = held_rows(q)
        pad[8:8 + band, :] = dot(unpack[q], hold[ph, block, cells_at, :])
        pad_edge[8:8 + wide, :] = hold[ph, block, edge_at, :].astype(F32)
        shift(pad_edge, 0, 1, target, q * (rows + 1) - 1)
        for i in range(band_rows // strip):
            shift(pad, i * strip * wide, strip, target, q * band_rows + i * strip)

    def add_conv(q, field, taps, turned_taps=None):
        lhs = field[pl.ds(q * conv_rows, conv_rows + 2), :, :].reshape((conv_rows + 2) * wide, 3 * ch)
        if turned_taps is None:
            value = dot(lhs, jnp.concatenate([taps(a) for a in range(3)], axis=1))
        else:
            rhs = jnp.concatenate([
                jnp.concatenate([turned_taps(3 * (2 - a) + 2 - b) for b in range(3)], axis=1) for a in range(3)], axis=0)
            value = lax.dot_general(lhs, rhs, (((1,), (1,)), ((), ())), preferred_element_type=F32)
        size = conv_rows * wide
        at = pl.ds(pl.multiple_of(q * size, wide), size)
        acc[at, :] = acc[at, :] + sum(
            value[a * wide:a * wide + size, a * ch:(a + 1) * ch] for a in range(3))

    def ag_copy(ph, block, q, sign):
        at = pl.ds(pl.multiple_of(q * held, wide), held)
        return pltpu.make_async_remote_copy(
            src_ref=hold.at[ph, block, at, :], dst_ref=hold.at[ph, block, at, :],
            send_sem=ag_ssem.at[ph, (1 - sign) // 2, block, q], recv_sem=ag_rsem.at[ph, block, q],
            device_id=(z + sign, s), device_id_type=MESH)

    def pack_field(ph, source, fill=None, first=None):
        if fill is not None:
            fill(cells, edge, 0)
        for q in range(HALVES):
            if first is not None:
                first(q)
            if fill is not None:
                chunked(fill, 0, q * band, band)
            edge_at, cells_at = held_rows(q)
            hold[ph, z, edge_at, :] = source[cells + q * wide:cells + (q + 1) * wide, :].astype(BF16)
            hold[ph, z, cells_at, :] = dot(pack[q], source[q * band:(q + 1) * band, :].astype(BF16)).astype(BF16)
            for sign in (1, -1):
                @pl.when((z + sign >= 0) & (z + sign < n))
                def _():
                    ag_copy(ph, z, q, sign).start()

    def inside(slice_at):
        return (slice_at >= 0) & (slice_at < n)

    def take_and_pass(ph, k, q, sign, passes=True, takes=True):
        block = z - k * sign

        @pl.when((k > 0) & inside(block))
        def _():
            if passes and takes:
                ag_copy(ph, block, q, sign).wait_recv()

            @pl.when(inside(z + sign))
            def _():
                if passes:
                    if not takes:
                        ag_copy(ph, block, q, sign).wait_recv()
                    ag_copy(ph, block, q, sign).start()

            if not passes:
                @pl.when(jnp.logical_not(inside(z + sign)))
                def _():
                    ag_copy(ph, block, q, sign).wait_recv()

    near = jnp.where(z < n - n // 2, 1, 0)

    def consume_way(k, q, way, consume):
        block = z - k * (1 - 2 * way)

        @pl.when((k >= 0) & (k < n) & inside(block) & ((k > 0) | (way == near)))
        def _():
            consume(k, block, q)

    def take_both(ph, k, q, **how):
        @pl.loop(0, 2)
        def _(i):
            way = (near + i) % 2
            take_and_pass(ph, k, q, 1 - 2 * way, **how)

    def consume_both(k, q, consume):
        @pl.loop(0, 2)
        def _(i):
            consume_way(k, q, (near + i) % 2, consume)

    def gather(ph, consume, each):
        @pl.loop(0, n)
        def _(k):
            @pl.loop(0, HALVES)
            def _(q):
                take_both(ph, k, q)
                consume_both(k, q, consume)
            each(k)

    def gather_passing_first(ph, consume, each):
        @pl.loop(0, n)
        def _(k):
            @pl.when(k == 1)
            def _():
                @pl.loop(1, n)
                def _(ahead):
                    @pl.loop(0, HALVES)
                    def _(q):
                        take_both(ph, ahead, q, takes=False)

            @pl.loop(0, HALVES)
            def _(q):
                take_both(ph, k, q, passes=False)
                consume_both(k, q, consume)
            each(k)

    last_pass = jnp.maximum(jnp.where(z < n - 1, z, 0), jnp.where(z > 0, n - 1 - z, 0))

    def forward(ph, field):
        def consume(k, block, q):
            into = taken.at[block]
            unpack_half(ph, block, q, into)
            slot = slot_of(block)

            @pl.when((k > 0) & (q == 0))
            def _():
                weights_arrived(ph, slot)
            add_conv(q, into, lambda a: wf[ph, slot, 3 * a * ch:3 * (a + 1) * ch, :])

        def each(k):
            if ph == 0:
                @pl.when(k == 0)
                def _():
                    weights_round(0)

                @pl.when(k == 1)
                def _():
                    weights_over_z(1)
        (gather if ph else gather_passing_first)(ph, consume, each)

    def turn_field(ph, field):
        main = [field[start:start + ch, :].T for start in range(0, cells, ch)]
        ends = field[cells:cells + edge, :]
        if edge < ch:
            ends = jnp.concatenate([ends, jnp.zeros((ch - edge, ch), F32)], axis=0)
        ends = ends.T
        for i, here in enumerate(main):
            left = jnp.concatenate(
                [ends[:, 0:wide] if i == 0 else main[i - 1][:, ch - wide:], here[:, 0:ch - wide]], axis=1)
            right = jnp.concatenate(
                [here[:, wide:], main[i + 1][:, 0:wide] if i + 1 < len(main) else ends[:, wide:edge]], axis=1)
            for a, v in enumerate((left, here, right)):
                x_t[ph, a * ch:(a + 1) * ch, i * ch:(i + 1) * ch] = v.astype(BF16)

    half_rows = tap_rows // 2
    owners = math.gcd(half_rows // 16, chips)
    piece = half_rows // owners

    def c_copy(ph, j):
        return pltpu.make_async_remote_copy(
            src_ref=psend.at[ph, j], dst_ref=crecv.at[ph, j],
            send_sem=c_ssem.at[ph, j], recv_sem=c_rsem.at[ph, j],
            device_id=(z, chip * 2 + 1 - core), device_id_type=MESH)

    def q_copy(ph, j, e, whose, owner):
        return pltpu.make_async_remote_copy(
            src_ref=hsend.at[ph, j, owner], dst_ref=qrecv.at[ph, j, whose],
            send_sem=q_ssem.at[ph, j, e], recv_sem=q_rsem.at[ph, j, whose],
            device_id=(z, ((chip + e) % chips) * 2 + core), device_id_type=MESH)

    def f_copy(ph, j, e, owner):
        return pltpu.make_async_remote_copy(
            src_ref=wout.at[ph, j, core, owner], dst_ref=wout.at[ph, j, core, owner],
            send_sem=f_ssem.at[ph, j, e], recv_sem=f_rsem.at[ph, j, owner],
            device_id=(z, ((chip + e) % chips) * 2 + core), device_id_type=MESH)

    def h_copy(ph, j, whose):
        return pltpu.make_async_remote_copy(
            src_ref=wout.at[ph, j, whose], dst_ref=wout.at[ph, j, whose],
            send_sem=h_ssem.at[ph, j], recv_sem=h_rsem.at[ph, j],
            device_id=(z, chip * 2 + 1 - core), device_id_type=MESH)

    def o_copy(ph, j):
        target = (out_wg1, out_wg2)[ph]
        if aligned:
            target = target.at[:, :, :, pl.ds(pl.multiple_of(j * ch, ch), ch)]
        else:
            target = target.at[j]
        return pltpu.make_async_copy(wout.at[ph, j], target, o_sem.at[ph, j])

    def sum_cores(ph, j):
        for o in range(owners):
            psend[ph, j, o] = part[ph, j, 1 - core, o].astype(BF16)
        c_copy(ph, j).start()

    def sum_chips(ph, j):
        c_copy(ph, j).wait_recv()
        for o in range(owners):
            v = part[ph, j, core, o] + crecv[ph, j, o].astype(F32)
            part[ph, j, core, o] = v
            hsend[ph, j, o] = v.astype(BF16)

        @pl.loop(1, chips)
        def _(e):
            peer = (chip + e) % chips

            @pl.when(peer < owners)
            def _():
                q_copy(ph, j, e, chip, peer).start()

    def spread_chips(ph, j):
        @pl.when(chip < owners)
        def _():
            @pl.loop(1, chips)
            def _(e):
                q_copy(ph, j, e, (chip + e) % chips, chip).wait_recv()
            v = part[ph, j, core, chip]
            for e in range(1, chips):
                v = v + qrecv[ph, j, (chip + e) % chips].astype(F32)
            wout[ph, j, core, chip] = v.astype(BF16)

            @pl.loop(1, chips)
            def _(e):
                f_copy(ph, j, e, chip).start()

    def spread_cores(ph, j):
        @pl.loop(1, chips)
        def _(e):
            peer = (chip + e) % chips

            @pl.when(peer < owners)
            def _():
                f_copy(ph, j, e, peer).wait_recv()
        h_copy(ph, j, core).start()

    def finish(ph, j):
        h_copy(ph, j, 1 - core).wait_recv()
        o_copy(ph, j).start()

    def put_part(ph, j, tap, value):
        start = tap * ch
        done = 0
        while done < ch:
            row = start + done
            side, o, at = row // half_rows, row % half_rows // piece, row % piece
            size = min(ch - done, piece - at)
            part[ph, j, side, o, at:at + size, :] = value[done:done + size, :]
            done += size

    stages = (sum_cores, sum_chips, spread_chips, spread_cores, finish)

    def of_step(k, fn):
        @pl.loop(0, 2)
        def _(way):
            block = z - k * (1 - 2 * way)

            @pl.when((k >= 0) & (k < n) & inside(block) & ((k > 0) | (way == 0)))
            def _():
                fn(block)

    passing = last_pass > 0

    def made_at(step):
        first = jnp.where(passing & (step > 0), jnp.where(step == last_pass, 1, step + 1), step)
        return first, step + 1

    def advance(ph, k):
        for age in range(1, len(stages)):
            step = k - age

            @pl.when((step >= 0) & (step < n))
            def _():
                @pl.loop(*made_at(step))
                def _(made):
                    of_step(made, functools.partial(stages[age], ph))

    def advance_all(ph, age):
        @pl.loop(0, n)
        def _(j):
            stages[age](ph, j)

    def field_grad(ph, block):
        grad = taken[block, 3:rows + 3, :, :].reshape(cells, 3 * ch)
        value = dot(x_t[ph], grad)
        for a in range(3):
            for b in range(3):
                put_part(ph, block, 3 * a + b, value[a * ch:(a + 1) * ch, (2 - b) * ch:(3 - b) * ch])

    def make_grad(ph, block):
        field_grad(ph, block)
        sum_cores(ph, block)

    def backward(ph):
        last = ph == 0

        def consume(k, block, q):
            into = taken.at[block]
            unpack_half(2 + ph, block, q, into)
            if last:
                @pl.when((q == HALVES - 1) & ((k == 0) | (k >= last_pass)))
                def _():
                    make_grad(ph, block)
            add_conv(q, into, None, lambda t: wv[ph, block, t * ch:(t + 1) * ch, :])

        def each(k):
            first, end = made_at(k)
            if last:
                @pl.loop(first, end - 1)
                def _(step):
                    of_step(step, functools.partial(make_grad, ph))
                advance(ph, k)
                for age in range(2, len(stages)):
                    @pl.when(k == age - 2)
                    def _():
                        advance_all(1, age)
            else:
                @pl.loop(first, jnp.where(passing | (k < n - 2), end, first))
                def _(step):
                    of_step(step, functools.partial(make_grad, ph))
        gather(2 + ph, consume, each)

    def fold(v):
        return jnp.sum(v.reshape(v.shape[0] // 8, 8, ch), axis=0)

    def flatten(v):
        return jnp.sum(v, axis=0, keepdims=True)

    zero = jnp.zeros((8, ch), F32)

    def local_moments():
        def sums(start, size, carry):
            at = pl.ds(start, size)
            m = mask[at, :]
            return carry[0] + fold(acc[pl.ds(start + lead, size), :] * m), carry[1] + fold(m)
        added, number = (flatten(v) for v in chunked(sums, (zero, zero)))
        middle = added / jnp.maximum(number, 1.0)

        def spread(start, size, carry):
            at = pl.ds(start, size)
            c = (acc[pl.ds(start + lead, size), :] - middle) * mask[at, :]
            return carry + fold(c * c)
        return added, number, flatten(chunked(spread, zero))

    def moments(slot):
        take_stats(slot)
        got = [st_recv[slot, k] for k in range(s_count)]
        added = sum(g[0:1] for g in got)
        number = sum(g[1:2] for g in got)
        mean = added / number
        spread = 0.0
        for g in got:
            off = g[0:1] / jnp.maximum(g[1:2], 1.0) - mean
            spread = spread + (g[2:3] + g[1:2] * off * off)
        return mean, lax.rsqrt(spread / number + EPSILON), number

    def everywhere(fn):
        chunked(fn, 0)
        fn(cells, 2 * wide, 0)

    gain1, shift1, gain2, shift2 = (r[...] for r in (gain1_in, shift1_in, gain2_in, shift2_in))

    weights_over_z(0)

    below = lax.broadcasted_iota(jnp.int32, (band, band), 1) < lax.broadcasted_iota(jnp.int32, (band, band), 0)
    below = below.astype(F32).astype(BF16)

    def make_pack(h):
        lv = mask[h * band:(h + 1) * band, :]
        place = jnp.where(lv > 0.0, dot(below, lv.astype(BF16)), -1.0)
        places[h] = place
        across = place.T[0:1, :]
        spot = lax.broadcasted_iota(jnp.int32, (packed, band), 0).astype(F32)
        pack[h] = jnp.where(spot == across, 1.0, 0.0).astype(BF16)

    def make_unpack(h):
        for start in range(0, packed, ch):
            size = min(ch, packed - start)
            spot = start + lax.broadcasted_iota(jnp.int32, (band, size), 1)
            unpack[h, :, start:start + size] = jnp.where(
                places[h, :, :size] == spot.astype(F32), 1.0, 0.0).astype(BF16)

    for side in range(2):
        edge_copy(1 - side).wait_recv()
        there = jnp.where(s > 0, 1.0, 0.0) if side == 0 else jnp.where(s < s_count - 1, 1.0, 0.0)
        at = slice(cells + side * wide, cells + (side + 1) * wide)
        masked[at, :] = edge_recv[side, 0].astype(F32) * there
        mask[at, :] = edge_recv[side, 1].astype(F32) * there

    pack_field(0, masked, first=make_pack)
    for h in range(HALVES):
        make_unpack(h)
    forward(0, masked)
    send_rows(0)
    send_stats(0, local_moments())
    weights_round(1)
    load_cotangent()
    mean1, scale1, count = moments(0)

    def activate_one(start, size, carry):
        at = pl.ds(start, size)
        main = start is not cells
        nv = ((acc[pl.ds(start + lead, size), :] if main else normed1[at, :]) - mean1) * scale1
        normed1[at, :] = nv
        hid[at, :] = gelu_parts(nv * gain1 + shift1)[0] * mask[at, :]
        if main:
            acc[pl.ds(start + lead, size), :] = jnp.zeros((size, ch), F32)
        return carry

    def slope_one(start, size, carry):
        at = pl.ds(start, size)
        slope1[at, :] = gelu_parts(normed1[at, :] * gain1 + shift1)[1] * mask[at, :]
        return carry

    take_rows(0, normed1)
    pack_field(1, hid, activate_one)
    everywhere(slope_one)
    forward(1, hid)
    send_rows(1)
    send_stats(1, local_moments())
    turn_field(0, masked)
    turn_field(1, hid)
    mean2, scale2, _ = moments(1)

    def activate_two(value, start, size):
        at = pl.ds(start, size)
        nv = (value - mean2) * scale2
        normed2[at, :] = nv
        value, slope = gelu_parts(nv * gain2 + shift2 + masked[at, :])
        t = cotm[at, :] * slope
        through[at, :] = t
        return value, nv, t

    def activate_main(start, size, carry):
        at = pl.ds(start, size)
        sums_at = pl.ds(start + lead, size)
        value, nv, t = activate_two(acc[sums_at, :], start, size)
        hid2[at, :] = value * mask[at, :]
        acc[sums_at, :] = jnp.zeros((size, ch), F32)
        return carry[0] + fold(t * nv), carry[1] + fold(t)

    send_stats(2, [flatten(v) for v in chunked(activate_main, (zero, zero))])
    take_rows(1, normed2)
    take_cotangent()
    activate_two(normed2[cells:total, :], cells, edge)
    to_flat(hid2, out_block)

    def gradient_sums(slot):
        take_stats(slot)
        got = [st_recv[slot, k] for k in range(s_count)]
        return sum(g[0:1] for g in got), sum(g[1:2] for g in got)

    def norm_back(upstream, normed, gain, scale, sums):
        gain_grad, shift_grad = sums
        factor = gain * scale
        level, tilt = shift_grad / count, gain_grad / count

        def fill(start, size, carry):
            at = pl.ds(start, size)
            v = upstream[at, :] - mask[at, :] * (level + normed[at, :] * tilt)
            hid[at, :] = factor * v
            return carry
        return fill

    sums2 = gradient_sums(2)
    pack_field(3, hid, norm_back(through, normed2, gain2, scale2, sums2))
    backward(1)

    send_rows(2)

    def inner_main(start, size, carry):
        at = pl.ds(start, size)
        sums_at = pl.ds(start + lead, size)
        v = acc[sums_at, :] * slope1[at, :]
        slope1[at, :] = v
        acc[sums_at, :] = jnp.zeros((size, ch), F32)
        return carry[0] + fold(v * normed1[at, :]), carry[1] + fold(v)

    send_stats(3, [flatten(v) for v in chunked(inner_main, (zero, zero))])

    @pl.when(jnp.logical_not(passing))
    def _():
        for step in range(n - 2, n):
            of_step(step, functools.partial(make_grad, 1))
    for side in range(2):
        row_copy(2, 1 - side).wait_recv()
        at = slice(cells + side * wide, cells + (side + 1) * wide)
        slope1[at, :] = row_recv[2, side] * slope1[at, :]
    sums1 = gradient_sums(3)
    pack_field(2, hid, norm_back(slope1, normed1, gain1, scale1, sums1))
    advance_all(1, 1)
    backward(0)
    advance(0, n)

    def finish_input(start, size, carry):
        at = pl.ds(start, size)
        through[at, :] = (acc[pl.ds(start + lead, size), :] + through[at, :]) * mask[at, :]
        return carry

    chunked(finish_input, 0)
    to_flat(through, out_input)
    out_gain1[...], out_shift1[...] = sums1
    out_gain2[...], out_shift2[...] = sums2
    for extra in range(1, len(stages) - 1):
        advance(0, n + extra)

    for side in range(2):
        edge_copy(side).wait_send()
        cot_copy(side).wait_send()
        for slot in range(3):
            row_copy(slot, side).wait_send()

    @pl.loop(1, s_count)
    def _(k):
        for slot in range(4):
            st_copy(slot, k, s).wait_send()

    @pl.loop(1, n)
    def _(k):
        for which in range(2):
            wz_copy(which, k).wait_send()

    @pl.loop(1, w_parts)
    def _(k):
        for which in range(2):
            for slot in range(n - 1):
                wp_copy(which, slot, k, w_mine).wait_send()

    @pl.loop(0, n)
    def _(k):
        for sign in (1, -1):
            block = z - k * sign

            @pl.when((block >= 0) & (block < n) & (z + sign >= 0) & (z + sign < n))
            def _():
                for ph in range(4):
                    for q in range(HALVES):
                        ag_copy(ph, block, q, sign).wait_send()

    @pl.loop(0, n)
    def _(j):
        for ph in range(2):
            c_copy(ph, j).wait_send()
            h_copy(ph, j, core).wait_send()
            o_copy(ph, j).wait()

            @pl.loop(1, chips)
            def _(e):
                peer = (chip + e) % chips

                @pl.when(peer < owners)
                def _():
                    q_copy(ph, j, e, chip, peer).wait_send()

                @pl.when(chip < owners)
                def _():
                    f_copy(ph, j, e, chip).wait_send()


def finish_kernel(count, *refs):
    ins, outs = refs[:count], refs[count:2 * count]
    narrow, wide, in_sem, out_sem, take_sem, give_sem = refs[2 * count:2 * count + 6]
    held = refs[2 * count + 6:]
    rows = narrow.shape[1] // FINISH_PARTS
    parts = [(w, i, pl.ds(i * rows, rows)) for i in range(FINISH_PARTS) for w in range(2)]
    loads = [pltpu.make_async_copy(ins[w].at[at, :], narrow.at[w, at, :], in_sem.at[w, i]) for w, i, at in parts]
    stores = [pltpu.make_async_copy(wide.at[w, at, :], outs[w].at[at, :], out_sem.at[w, i]) for w, i, at in parts]
    takes = [pltpu.make_async_copy(ins[2 + k], v, take_sem.at[k]) for k, v in enumerate(held)]
    gives = [pltpu.make_async_copy(v, outs[2 + k], give_sem.at[k]) for k, v in enumerate(held)]
    for copy in loads + takes:
        copy.start()
    for load, store, (w, i, at) in zip(loads, stores, parts):
        load.wait()
        wide[w, at, :] = narrow[w, at, :].astype(F32)
        store.start()
    for take, give in zip(takes, gives):
        take.wait()
        give.start()
    for copy in stores + gives:
        copy.wait()


def per_device(n, s_count, blocks, weight_one, weight_two, gain_one, shift_one, gain_two, shift_two, cell_live, cotangent):
    rows, wide = cell_live.shape
    ch = blocks.shape[1] // wide
    cells = rows * wide
    total = cells + 2 * wide
    packed = -(-most_live(rows // HALVES, wide) // 16) * 16
    aligned = ch % 128 == 0
    chips = s_count // 2
    tap_rows = 9 * ch
    half_rows = tap_rows // 2
    owners = math.gcd(half_rows // 16, chips)
    piece = half_rows // owners

    if aligned:
        weight_one, weight_two = (w.reshape(tap_rows, n * ch) for w in (weight_one, weight_two))
    else:
        weight_one, weight_two = (
            w.reshape(tap_rows, n, ch).transpose(1, 0, 2) for w in (weight_one, weight_two))
    grad_shape = (2, owners, piece, n * ch) if aligned else (n, 2, owners, piece, ch)
    vmem = pl.BlockSpec(memory_space=pltpu.VMEM)
    hbm = pl.BlockSpec(memory_space=pl.ANY)
    sem = pltpu.SemaphoreType.DMA
    field = pltpu.VMEM((total, ch), F32)
    scratch = [
        pltpu.VMEM((ch * wide, 128), F32),
        pltpu.VMEM((2, n, tap_rows, ch), BF16),
        pltpu.VMEM((2, n, tap_rows, ch), BF16),
        pltpu.VMEM((2, 3 * ch, cells), BF16),
        pltpu.VMEM((HALVES, packed, cells // HALVES), BF16),
        pltpu.VMEM((HALVES, cells // HALVES, packed), BF16),
        pltpu.VMEM((HALVES, cells // HALVES, ch), F32),
        pltpu.VMEM((2, 2, wide, ch), BF16),
        pltpu.VMEM((2, 2, wide, ch), BF16),
        pltpu.VMEM((2, wide, ch), BF16),
        pltpu.VMEM((2, wide, ch), BF16),
        field, field, field, field, field, field, field, field, field,
        pltpu.VMEM((cells // HALVES + 16, ch), F32),
        pltpu.VMEM((wide + 16, ch), F32),
        pltpu.VMEM((total, ch), F32),
        pltpu.VMEM((4, n, 2 * wide + HALVES * packed, ch), BF16),
        pltpu.VMEM((n, rows + 4, wide, 3 * ch), BF16),
        pltpu.VMEM((2, n, 2, owners, piece, ch), F32),
        pltpu.VMEM((2, n, owners, piece, ch), BF16),
        pltpu.VMEM((2, n, owners, piece, ch), BF16),
        pltpu.VMEM((2, n, owners, piece, ch), BF16),
        pltpu.VMEM((2, n, chips, piece, ch), BF16),
        pltpu.VMEM((2, n, 2, owners, piece, ch), BF16),
        pltpu.VMEM((4, 8, ch), F32),
        pltpu.VMEM((4, s_count, 8, ch), F32),
        pltpu.VMEM((3, 2, wide, ch), F32),
        pltpu.VMEM((3, 2, wide, ch), F32),
        sem((2, n + 1)),
        sem((2, n)), sem((2, n)),
        sem((2, n - 1, s_count)), sem((2, n - 1, s_count)),
        sem((2,)), sem((2,)),
        sem((2,)), sem((2,)),
        sem((4, 2, n, HALVES)), sem((4, n, HALVES)),
        sem((4, s_count)), sem((4, s_count)),
        sem((3, 2)), sem((3, 2)),
        sem((2, n)), sem((2, n)),
        sem((2, n, chips)), sem((2, n, chips)),
        sem((2, n, chips)), sem((2, n, chips)),
        sem((2, n)), sem((2, n)),
        sem((2, n)),
    ]
    block_out, input_grad, wg1, wg2, *sums = pl.pallas_call(
        functools.partial(block_kernel, n, s_count, rows, wide, ch, aligned, packed),
        out_shape=(
            jax.ShapeDtypeStruct((rows, ch * wide), BF16),
            jax.ShapeDtypeStruct((rows, ch * wide), F32),
            jax.ShapeDtypeStruct(grad_shape, BF16),
            jax.ShapeDtypeStruct(grad_shape, BF16),
            *[jax.ShapeDtypeStruct((1, ch), F32)] * 4,
        ),
        in_specs=[vmem] * 7 + [hbm] * 2,
        out_specs=(vmem, vmem, hbm, hbm, vmem, vmem, vmem, vmem),
        scratch_shapes=scratch,
        compiler_params=pltpu.CompilerParams(
            collective_id=0, has_side_effects=True, vmem_limit_bytes=60 * 1024 * 1024),
    )(blocks, cotangent, cell_live.T,
      *(v.reshape(1, ch) for v in (gain_one, shift_one, gain_two, shift_two)), weight_one, weight_two)

    if not aligned:
        def whole(grad):
            grad = grad.reshape(n, tap_rows, ch).transpose(1, 0, 2)
            return grad.astype(F32).reshape(9, ch, n * ch)
        return (block_out, input_grad, whole(wg1), whole(wg2), *(v.reshape(ch) for v in sums))

    wg1, wg2 = (w.reshape(tap_rows, n * ch) for w in (wg1, wg2))
    wide_grad = jax.ShapeDtypeStruct((tap_rows, n * ch), F32)
    moved = (block_out, input_grad, *sums)
    grad1, grad2, *moved = pl.pallas_call(
        functools.partial(finish_kernel, 2 + len(moved)),
        out_shape=(wide_grad, wide_grad, *(jax.ShapeDtypeStruct(v.shape, v.dtype) for v in moved)),
        in_specs=[pl.BlockSpec(memory_space=pl.ANY)] * (2 + len(moved)),
        out_specs=[pl.BlockSpec(memory_space=pl.ANY)] * (2 + len(moved)),
        scratch_shapes=[
            pltpu.VMEM((2, tap_rows, n * ch), BF16), pltpu.VMEM((2, tap_rows, n * ch), F32),
            sem((2, FINISH_PARTS)), sem((2, FINISH_PARTS)), sem((len(moved),)), sem((len(moved),)),
            *(pltpu.VMEM(v.shape, v.dtype) for v in moved),
        ],
        compiler_params=pltpu.CompilerParams(vmem_limit_bytes=64 * 1024 * 1024),
    )(wg1, wg2, *moved)
    block_out, input_grad, *sums = moved
    grads = (g.reshape(9, ch, n * ch) for g in (grad1, grad2))
    return (block_out, input_grad, *grads, *(v.reshape(ch) for v in sums))


def solution(mesh):
    return jax.shard_map(
        functools.partial(per_device, mesh.shape["chan"], mesh.shape["space"]),
        mesh=mesh,
        in_specs=(
            P("space", "chan"),
            P(None, "chan", None),
            P(None, "chan", None),
            P("chan"),
            P("chan"),
            P("chan"),
            P("chan"),
            P("space", None),
            P("space", "chan"),
        ),
        out_specs=(
            P("space", "chan"),
            P("space", "chan"),
            P(None, "chan", None),
            P(None, "chan", None),
            P("chan"),
            P("chan"),
            P("chan"),
            P("chan"),
        ),
        check_vma=False,
    )
```

```python
import functools
import math

import jax
import jax.numpy as jnp
from jax import lax
from jax.experimental import pallas as pl
from jax.experimental.pallas import tpu as pltpu
from jax.sharding import PartitionSpec as P

EPSILON = 1e-05
MESH = pl.DeviceIdType.MESH
F32 = jnp.float32
BF16 = jnp.bfloat16
ROOT_HALF = 0.7071067811865476
ROOT_TWO_PI = 0.3989422804014327
CHUNK = 64
FINISH_PARTS = 4
UNROLL = 2
HALVES = 2
LARGE, SMALL = 7, 3


def dot(a, b):
    return jnp.dot(a, b, preferred_element_type=F32)


def gelu_parts(v):
    upper = 0.5 * (1.0 + lax.erf(v * ROOT_HALF))
    slope = upper + v * (ROOT_TWO_PI * jnp.exp(-0.5 * v * v))
    return v * upper, slope


def most_live(rows, wide):
    units = (wide + 1) // (SMALL + 1)
    live_rows = rows - rows // (LARGE + 1)
    return min(rows * wide, math.ceil(units * live_rows * LARGE / 2))


def block_kernel(n, s_count, rows, wide, ch, aligned, packed, *refs):
    (x_in, cot_in, live_in, gain1_in, shift1_in, gain2_in, shift2_in, w1_hbm, w2_hbm) = refs[:9]
    (out_block, out_input, out_wg1, out_wg2, out_gain1, out_shift1, out_gain2, out_shift2) = refs[9:17]
    (turned, wv, wf, x_t, pack, unpack, places, edge_send, edge_recv, cot_send, cot_recv, cotm, mask, masked,
     normed1, normed2, through, slope1, hid, hid2, pad, acc, hold, taken,
     part, psend, crecv, hsend, qrecv, wout, st_send, st_recv, row_send, row_recv,
     w_sem, wz_ssem, wz_rsem, wp_ssem, wp_rsem, e_ssem, e_rsem, ce_ssem, ce_rsem, ag_ssem, ag_rsem,
     st_ssem, st_rsem, row_ssem, row_rsem, c_ssem, c_rsem, q_ssem, q_rsem,
     f_ssem, f_rsem, h_ssem, h_rsem, o_sem) = refs[17:]

    z = lax.axis_index("chan")
    s = lax.axis_index("space")
    cells = rows * wide
    total = cells + 2 * wide
    band = cells // HALVES
    core, chip, chips = s % 2, s // 2, s_count // 2
    before, after = (s + s_count - 1) % s_count, (s + 1) % s_count
    tap_rows = 9 * ch

    barrier = pltpu.get_barrier_semaphore()

    @pl.loop(1, s_count)
    def _(k):
        pl.semaphore_signal(barrier, inc=1, device_id=(z, (s + k) % s_count), device_id_type=MESH)

    @pl.loop(1, n)
    def _(k):
        pl.semaphore_signal(barrier, inc=1, device_id=((z + k) % n, s), device_id_type=MESH)

    w_copies = []
    for which, source in enumerate((w1_hbm, w2_hbm)):
        for d in range(n):
            block = source.at[:, d * ch:(d + 1) * ch] if aligned else source.at[d]
            w_copies.append(pltpu.make_async_copy(block, wv.at[which, d], w_sem.at[which, d]))
    for copy in w_copies:
        copy.start()

    def chunked(fn, init, first=0, count=cells):
        def step(i, carry):
            return fn(pl.multiple_of(first + i * CHUNK, CHUNK), CHUNK, carry)
        return lax.fori_loop(0, count // CHUNK, step, init, unroll=UNROLL)

    lanes = 128
    tiles = ch * wide // lanes

    def from_flat(flat, put):
        for i in range(tiles):
            turned[i * lanes:(i + 1) * lanes, 0:rows] = flat[:, i * lanes:(i + 1) * lanes].astype(F32).T
        for w in range(wide):
            put(pl.ds(w, rows, stride=wide), turned[pl.ds(w, ch, stride=wide), 0:rows].T)

    def to_flat(source, flat):
        for w in range(wide):
            turned[pl.ds(w, ch, stride=wide), 0:rows] = source[pl.ds(w, rows, stride=wide), :].T
        for i in range(tiles):
            flat[:, i * lanes:(i + 1) * lanes] = turned[i * lanes:(i + 1) * lanes, 0:rows].T.astype(flat.dtype)

    def put_masked(at, value):
        masked[at, :] = value

    from_flat(x_in, put_masked)

    cell = lax.broadcasted_iota(jnp.int32, (cells, rows), 0)
    pick = (cell // wide == lax.broadcasted_iota(jnp.int32, (cells, rows), 1)).astype(F32).astype(BF16)
    column_of = lax.broadcasted_iota(jnp.int32, (cells, wide), 0) % wide
    picked = lax.dot_general(pick, live_in[...].astype(BF16), (((1,), (1,)), ((), ())), preferred_element_type=F32)
    picked = jnp.where(column_of == lax.broadcasted_iota(jnp.int32, (cells, wide), 1), picked, 0.0)
    mask[0:cells, :] = dot(picked.astype(BF16), jnp.ones((wide, ch), BF16))

    def load_main(start, size, carry):
        at = pl.ds(start, size)
        lv = mask[at, :]
        masked[at, :] = masked[at, :] * lv
        return carry

    chunked(load_main, 0)
    for side, start in ((0, 0), (1, cells - wide)):
        edge_send[side, 0] = masked[start:start + wide, :].astype(BF16)
        edge_send[side, 1] = mask[start:start + wide, :].astype(BF16)

    acc[...] = jnp.zeros_like(acc)
    st_send[...] = jnp.zeros_like(st_send)

    pl.semaphore_wait(barrier, s_count - 1 + n - 1)

    def edge_copy(side):
        return pltpu.make_async_remote_copy(
            src_ref=edge_send.at[side], dst_ref=edge_recv.at[1 - side],
            send_sem=e_ssem.at[side], recv_sem=e_rsem.at[1 - side],
            device_id=(z, before if side == 0 else after), device_id_type=MESH)

    for side in range(2):
        edge_copy(side).start()

    def cot_copy(side):
        return pltpu.make_async_remote_copy(
            src_ref=cot_send.at[side], dst_ref=cot_recv.at[1 - side],
            send_sem=ce_ssem.at[side], recv_sem=ce_rsem.at[1 - side],
            device_id=(z, before if side == 0 else after), device_id_type=MESH)

    def load_cotangent():
        def put(at, value):
            cotm[at, :] = value
        from_flat(cot_in, put)

        def live_only(start, size, carry):
            at = pl.ds(start, size)
            cotm[at, :] = cotm[at, :] * mask[at, :]
            return carry
        chunked(live_only, 0)
        for side, start in ((0, 0), (1, cells - wide)):
            cot_send[side] = cotm[start:start + wide, :].astype(BF16)
            cot_copy(side).start()

    def take_cotangent():
        for side in range(2):
            cot_copy(1 - side).wait_recv()
            at = slice(cells + side * wide, cells + (side + 1) * wide)
            cotm[at, :] = cot_recv[side].astype(F32) * mask[at, :]

    w_parts = math.gcd(tap_rows // 16, s_count)
    w_rows = tap_rows // w_parts
    w_mine = s % w_parts
    w_group = s - w_mine

    def wz_copy(which, k):
        at = pl.ds(w_mine * w_rows, w_rows)
        slot = n - k - 1
        return pltpu.make_async_remote_copy(
            src_ref=wv.at[which, (z + k) % n, at, :], dst_ref=wf.at[which, slot, at, :],
            send_sem=wz_ssem.at[which, slot], recv_sem=wz_rsem.at[which, slot],
            device_id=((z + k) % n, s), device_id_type=MESH)

    def wp_copy(which, slot, k, whose):
        at = pl.ds(whose * w_rows, w_rows)
        return pltpu.make_async_remote_copy(
            src_ref=wf.at[which, slot, at, :], dst_ref=wf.at[which, slot, at, :],
            send_sem=wp_ssem.at[which, slot, k], recv_sem=wp_rsem.at[which, slot, whose],
            device_id=(z, w_group + (w_mine + k) % w_parts), device_id_type=MESH)

    def weights_over_z(which):
        for copy in w_copies[which * n:(which + 1) * n]:
            copy.wait()

        @pl.loop(1, n)
        def _(k):
            wz_copy(which, k).start()

    def slot_of(block):
        return (block - z + n - 1) % n

    def weights_round(which):
        @pl.loop(1, n)
        def _(distance):
            for sign in (1, -1):
                block = z - distance * sign

                @pl.when((block >= 0) & (block < n))
                def _():
                    slot = slot_of(block)
                    wz_copy(which, n - 1 - slot).wait_recv()

                    @pl.loop(1, w_parts)
                    def _(k):
                        wp_copy(which, slot, k, w_mine).start()

    def weights_arrived(which, slot):
        @pl.loop(1, w_parts)
        def _(k):
            wp_copy(which, slot, k, (w_mine + k) % w_parts).wait_recv()

    def row_copy(slot, side):
        return pltpu.make_async_remote_copy(
            src_ref=row_send.at[slot, side], dst_ref=row_recv.at[slot, 1 - side],
            send_sem=row_ssem.at[slot, side], recv_sem=row_rsem.at[slot, 1 - side],
            device_id=(z, before if side == 0 else after), device_id_type=MESH)

    def send_rows(slot, ref):
        for side, start in ((0, 0), (1, cells - wide)):
            row_send[slot, side] = ref[start:start + wide, :]
            row_copy(slot, side).start()

    def take_rows(slot, ref):
        for side in range(2):
            row_copy(slot, 1 - side).wait_recv()
            ref[cells + side * wide:cells + (side + 1) * wide, :] = row_recv[slot, side]

    def st_copy(slot, k, whose):
        return pltpu.make_async_remote_copy(
            src_ref=st_send.at[slot], dst_ref=st_recv.at[slot, whose],
            send_sem=st_ssem.at[slot, k], recv_sem=st_rsem.at[slot, whose],
            device_id=(z, (s + k) % s_count), device_id_type=MESH)

    def send_stats(slot, values):
        for i, v in enumerate(values):
            st_send[slot, i:i + 1, :] = v
        for k in range(1, s_count):
            st_copy(slot, k, s).start()
        st_recv[slot, s] = st_send[slot]

    def take_stats(slot):
        for k in range(1, s_count):
            st_copy(slot, k, (s + k) % s_count).wait_recv()

    strip = 8
    column = lax.broadcasted_iota(jnp.int32, (strip * wide, ch), 0) % wide

    def shift(target, first, count):
        size = count * wide
        where = column[:size]
        here = pad[pl.ds(8 + first * wide, size), :]
        left = jnp.where(where == 0, 0.0, pad[pl.ds(7 + first * wide, size), :])
        right = jnp.where(where == wide - 1, 0.0, pad[pl.ds(9 + first * wide, size), :])
        for b, v in enumerate((left, here, right)):
            target[pl.ds(first, count), :, b * ch:(b + 1) * ch] = v.astype(BF16).reshape(count, wide, ch)

    edge = 2 * wide
    ag_rows = ((0, edge + packed), (edge + packed, packed))
    band_rows = rows // HALVES

    def unpack_half(ph, block, q, target):
        if q == 0:
            pad[8:8 + wide, :] = hold[ph, block, 0:wide, :].astype(F32)
            pad[8 + wide + cells:8 + 2 * wide + cells, :] = hold[ph, block, wide:edge, :].astype(F32)
            shift(target, 0, 1)
            shift(target, rows + 1, 1)
        pad[8 + wide + q * band:8 + wide + (q + 1) * band, :] = dot(
            unpack[q], hold[ph, block, edge + q * packed:edge + (q + 1) * packed, :])

        for i in range(band_rows // strip):
            shift(target, 1 + q * band_rows + i * strip, strip)

    def add_conv(q, field, taps, turned_taps=None):
        first, last = (0, band_rows - 1) if q == 0 else (band_rows - 1, rows)
        count = last - first
        lhs = field[first:last + 2, :, :].reshape((count + 2) * wide, 3 * ch)
        if turned_taps is None:
            value = dot(lhs, jnp.concatenate([taps(a) for a in range(3)], axis=1))
        else:
            rhs = jnp.concatenate([
                jnp.concatenate([turned_taps(3 * (2 - a) + 2 - b) for b in range(3)], axis=1) for a in range(3)], axis=0)
            value = lax.dot_general(lhs, rhs, (((1,), (1,)), ((), ())), preferred_element_type=F32)
        at = pl.ds(first * wide, count * wide)
        acc[at, :] = acc[at, :] + sum(
            value[a * wide:(a + count) * wide, a * ch:(a + 1) * ch] for a in range(3))

    def ag_copy(ph, block, q, sign):
        at = pl.ds(*ag_rows[q])
        return pltpu.make_async_remote_copy(
            src_ref=hold.at[ph, block, at, :], dst_ref=hold.at[ph, block, at, :],
            send_sem=ag_ssem.at[ph, (1 - sign) // 2, block, q], recv_sem=ag_rsem.at[ph, block, q],
            device_id=(z + sign, s), device_id_type=MESH)

    def pack_field(ph, source, fill=None, first=None):
        if fill is not None:
            fill(cells, edge, 0)
        hold[ph, z, 0:edge, :] = source[cells:cells + edge, :].astype(BF16)
        for q in range(HALVES):
            if first is not None:
                first(q)
            if fill is not None:
                chunked(fill, 0, q * band, band)
            hold[ph, z, edge + q * packed:edge + (q + 1) * packed, :] = dot(
                pack[q], source[q * band:(q + 1) * band, :].astype(BF16)).astype(BF16)
            for sign in (1, -1):
                @pl.when((z + sign >= 0) & (z + sign < n))
                def _():
                    ag_copy(ph, z, q, sign).start()

    def inside(slice_at):
        return (slice_at >= 0) & (slice_at < n)

    def take_and_pass(ph, k, q, sign, passes=True, takes=True):
        block = z - k * sign

        @pl.when((k > 0) & inside(block))
        def _():
            if passes and takes:
                ag_copy(ph, block, q, sign).wait_recv()

            @pl.when(inside(z + sign))
            def _():
                if passes:
                    if not takes:
                        ag_copy(ph, block, q, sign).wait_recv()
                    ag_copy(ph, block, q, sign).start()

            if not passes:
                @pl.when(jnp.logical_not(inside(z + sign)))
                def _():
                    ag_copy(ph, block, q, sign).wait_recv()

    near = jnp.where(z < n - n // 2, 1, 0)

    def consume_way(k, q, way, consume):
        block = z - k * (1 - 2 * way)

        @pl.when((k >= 0) & (k < n) & inside(block) & ((k > 0) | (way == near)))
        def _():
            consume(k, block, q)

    def take_both(ph, k, q, **how):
        @pl.loop(0, 2)
        def _(i):
            way = (near + i) % 2
            take_and_pass(ph, k, q, 1 - 2 * way, **how)

    def gather(ph, consume, each):
        @pl.loop(0, n)
        def _(k):
            for q in range(HALVES):
                take_both(ph, k, q)
                if q:
                    consume_way(k, q - 1, 1 - near, consume)
                else:
                    consume_way(k - 1, HALVES - 1, 1 - near, consume)
                consume_way(k, q, near, consume)
            each(k)

    def gather_passing_first(ph, consume, each):
        @pl.loop(0, n)
        def _(k):
            @pl.when(k == 1)
            def _():
                @pl.loop(1, n)
                def _(ahead):
                    for q in range(HALVES):
                        take_both(ph, ahead, q, takes=False)
            for q in range(HALVES):
                take_both(ph, k, q, passes=False)

                @pl.loop(0, 2)
                def _(i):
                    consume_way(k, q, (near + i) % 2, consume)
            each(k)

    last_pass = jnp.maximum(jnp.where(z < n - 1, z, 0), jnp.where(z > 0, n - 1 - z, 0))

    def forward(ph, field):
        def consume(k, block, q):
            into = taken.at[block]
            unpack_half(ph, block, q, into)

            @pl.when(k == 0)
            def _():
                add_conv(q, into, lambda a: wv[ph, z, 3 * a * ch:3 * (a + 1) * ch, :])

            @pl.when(k > 0)
            def _():
                slot = slot_of(block)
                if q == 0:
                    weights_arrived(ph, slot)
                add_conv(q, into, lambda a: wf[ph, slot, 3 * a * ch:3 * (a + 1) * ch, :])

        def each(k):
            if ph == 0:
                @pl.when(k == 0)
                def _():
                    weights_round(0)

                @pl.when(k == 1)
                def _():
                    weights_over_z(1)
            if ph == 1:
                @pl.when(k == last_pass)
                def _():
                    everywhere(slope_one)
        (gather if ph else gather_passing_first)(ph, consume, each)

    def turn_field(ph, field):
        main = [field[start:start + ch, :].T for start in range(0, cells, ch)]
        ends = field[cells:cells + edge, :]
        if edge < ch:
            ends = jnp.concatenate([ends, jnp.zeros((ch - edge, ch), F32)], axis=0)
        ends = ends.T
        for i, here in enumerate(main):
            left = jnp.concatenate(
                [ends[:, 0:wide] if i == 0 else main[i - 1][:, ch - wide:], here[:, 0:ch - wide]], axis=1)
            right = jnp.concatenate(
                [here[:, wide:], main[i + 1][:, 0:wide] if i + 1 < len(main) else ends[:, wide:edge]], axis=1)
            for a, v in enumerate((left, here, right)):
                x_t[ph, a * ch:(a + 1) * ch, i * ch:(i + 1) * ch] = v.astype(BF16)

    half_rows = tap_rows // 2
    owners = math.gcd(half_rows // 16, chips)
    piece = half_rows // owners

    def c_copy(ph, j):
        return pltpu.make_async_remote_copy(
            src_ref=psend.at[ph, j], dst_ref=crecv.at[ph, j],
            send_sem=c_ssem.at[ph, j], recv_sem=c_rsem.at[ph, j],
            device_id=(z, chip * 2 + 1 - core), device_id_type=MESH)

    def q_copy(ph, j, e, whose, owner):
        return pltpu.make_async_remote_copy(
            src_ref=hsend.at[ph, j, owner], dst_ref=qrecv.at[ph, j, whose],
            send_sem=q_ssem.at[ph, j, e], recv_sem=q_rsem.at[ph, j, whose],
            device_id=(z, ((chip + e) % chips) * 2 + core), device_id_type=MESH)

    def f_copy(ph, j, e, owner):
        return pltpu.make_async_remote_copy(
            src_ref=wout.at[ph, j, core, owner], dst_ref=wout.at[ph, j, core, owner],
            send_sem=f_ssem.at[ph, j, e], recv_sem=f_rsem.at[ph, j, owner],
            device_id=(z, ((chip + e) % chips) * 2 + core), device_id_type=MESH)

    def h_copy(ph, j, whose):
        return pltpu.make_async_remote_copy(
            src_ref=wout.at[ph, j, whose], dst_ref=wout.at[ph, j, whose],
            send_sem=h_ssem.at[ph, j], recv_sem=h_rsem.at[ph, j],
            device_id=(z, chip * 2 + 1 - core), device_id_type=MESH)

    def o_copy(ph, j):
        target = (out_wg1, out_wg2)[ph]
        if aligned:
            target = target.at[:, :, :, pl.ds(pl.multiple_of(j * ch, ch), ch)]
        else:
            target = target.at[j]
        return pltpu.make_async_copy(wout.at[ph, j], target, o_sem.at[ph, j])

    def sum_cores(ph, j):
        for o in range(owners):
            psend[ph, j, o] = part[ph, j, 1 - core, o].astype(BF16)
        c_copy(ph, j).start()

    def sum_chips(ph, j):
        c_copy(ph, j).wait_recv()
        for o in range(owners):
            v = part[ph, j, core, o] + crecv[ph, j, o].astype(F32)
            part[ph, j, core, o] = v
            hsend[ph, j, o] = v.astype(BF16)

        @pl.loop(1, chips)
        def _(e):
            peer = (chip + e) % chips

            @pl.when(peer < owners)
            def _():
                q_copy(ph, j, e, chip, peer).start()

    def spread_chips(ph, j):
        @pl.when(chip < owners)
        def _():
            @pl.loop(1, chips)
            def _(e):
                q_copy(ph, j, e, (chip + e) % chips, chip).wait_recv()
            v = part[ph, j, core, chip]
            for e in range(1, chips):
                v = v + qrecv[ph, j, (chip + e) % chips].astype(F32)
            wout[ph, j, core, chip] = v.astype(BF16)

            @pl.loop(1, chips)
            def _(e):
                f_copy(ph, j, e, chip).start()

    def spread_cores(ph, j):
        @pl.loop(1, chips)
        def _(e):
            peer = (chip + e) % chips

            @pl.when(peer < owners)
            def _():
                f_copy(ph, j, e, peer).wait_recv()
        h_copy(ph, j, core).start()

    def finish(ph, j):
        h_copy(ph, j, 1 - core).wait_recv()
        o_copy(ph, j).start()

    def put_part(ph, j, tap, value):
        start = tap * ch
        done = 0
        while done < ch:
            row = start + done
            side, o, at = row // half_rows, row % half_rows // piece, row % piece
            size = min(ch - done, piece - at)
            part[ph, j, side, o, at:at + size, :] = value[done:done + size, :]
            done += size

    stages = (sum_cores, sum_chips, spread_chips, spread_cores, finish)

    def of_step(k, fn):
        @pl.loop(0, 2)
        def _(way):
            block = z - k * (1 - 2 * way)

            @pl.when((k >= 0) & (k < n) & inside(block) & ((k > 0) | (way == 0)))
            def _():
                fn(block)

    passing = last_pass > 0

    def made_at(step):
        first = jnp.where(passing, jnp.where(step == last_pass, 0, step + 1), step)
        return first, step + 1

    def advance(ph, k):
        for age in range(1, len(stages)):
            step = k - age

            @pl.when((step >= 0) & (step < n))
            def _():
                @pl.loop(*made_at(step))
                def _(made):
                    of_step(made, functools.partial(stages[age], ph))

    def advance_all(ph, age):
        @pl.loop(0, n)
        def _(j):
            stages[age](ph, j)

    def field_grad(ph, block):
        grad = taken[block, 1:rows + 1, :, :].reshape(cells, 3 * ch)
        value = dot(x_t[ph], grad)
        for a in range(3):
            for b in range(3):
                put_part(ph, block, 3 * a + b, value[a * ch:(a + 1) * ch, (2 - b) * ch:(3 - b) * ch])

    def advance_second(k):
        for age in range(1, len(stages)):
            @pl.when(k == last_pass + age - 1)
            def _():
                advance_all(1, age)

    def make_grad(ph, block):
        field_grad(ph, block)
        sum_cores(ph, block)

    def backward(ph):
        last = ph == 0

        def consume(k, block, q):
            into = taken.at[block]
            unpack_half(2 + ph, block, q, into)
            if last and q == HALVES - 1:
                @pl.when(k >= last_pass)
                def _():
                    make_grad(ph, block)
            add_conv(q, into, None, lambda t: wv[ph, block, t * ch:(t + 1) * ch, :])

        def each(k):
            first, end = made_at(k)
            if last:
                @pl.loop(first, end - 1)
                def _(step):
                    of_step(step, functools.partial(make_grad, ph))
                advance(ph, k)
                advance_second(k)
            else:
                @pl.loop(first, jnp.where(passing | (k < n - 2), end, first))
                def _(step):
                    of_step(step, functools.partial(make_grad, ph))
        gather(2 + ph, consume, each)

    def fold(v):
        return jnp.sum(v.reshape(v.shape[0] // 8, 8, ch), axis=0)

    def flatten(v):
        return jnp.sum(v, axis=0, keepdims=True)

    zero = jnp.zeros((8, ch), F32)

    def local_moments(ref):
        def sums(start, size, carry):
            at = pl.ds(start, size)
            m = mask[at, :]
            return carry[0] + fold(ref[at, :] * m), carry[1] + fold(m)
        added, number = (flatten(v) for v in chunked(sums, (zero, zero)))
        middle = added / jnp.maximum(number, 1.0)

        def spread(start, size, carry):
            at = pl.ds(start, size)
            c = (ref[at, :] - middle) * mask[at, :]
            return carry + fold(c * c)
        return added, number, flatten(chunked(spread, zero))

    def moments(slot):
        take_stats(slot)
        got = [st_recv[slot, k] for k in range(s_count)]
        added = sum(g[0:1] for g in got)
        number = sum(g[1:2] for g in got)
        mean = added / number
        spread = 0.0
        for g in got:
            off = g[0:1] / jnp.maximum(g[1:2], 1.0) - mean
            spread = spread + (g[2:3] + g[1:2] * off * off)
        return mean, lax.rsqrt(spread / number + EPSILON), number

    def everywhere(fn):
        chunked(fn, 0)
        fn(cells, 2 * wide, 0)

    gain1, shift1, gain2, shift2 = (r[...] for r in (gain1_in, shift1_in, gain2_in, shift2_in))

    weights_over_z(0)

    below = lax.broadcasted_iota(jnp.int32, (band, band), 1) < lax.broadcasted_iota(jnp.int32, (band, band), 0)
    below = below.astype(F32).astype(BF16)

    def make_pack(h):
        lv = mask[h * band:(h + 1) * band, :]
        place = jnp.where(lv > 0.0, dot(below, lv.astype(BF16)), -1.0)
        places[h] = place
        across = place.T[0:1, :]
        spot = lax.broadcasted_iota(jnp.int32, (packed, band), 0).astype(F32)
        pack[h] = jnp.where(spot == across, 1.0, 0.0).astype(BF16)

    def make_unpack(h):
        for start in range(0, packed, ch):
            size = min(ch, packed - start)
            spot = start + lax.broadcasted_iota(jnp.int32, (band, size), 1)
            unpack[h, :, start:start + size] = jnp.where(
                places[h, :, :size] == spot.astype(F32), 1.0, 0.0).astype(BF16)

    for side in range(2):
        edge_copy(1 - side).wait_recv()
        there = jnp.where(s > 0, 1.0, 0.0) if side == 0 else jnp.where(s < s_count - 1, 1.0, 0.0)
        at = slice(cells + side * wide, cells + (side + 1) * wide)
        masked[at, :] = edge_recv[side, 0].astype(F32) * there
        mask[at, :] = edge_recv[side, 1].astype(F32) * there

    pack_field(0, masked, first=make_pack)
    for h in range(HALVES):
        make_unpack(h)
    forward(0, masked)
    send_rows(0, acc)
    send_stats(0, local_moments(acc))
    weights_round(1)
    load_cotangent()
    mean1, scale1, count = moments(0)

    def activate_one(start, size, carry):
        at = pl.ds(start, size)
        main = start is not cells
        nv = ((acc if main else normed1)[at, :] - mean1) * scale1
        normed1[at, :] = nv
        hid[at, :] = gelu_parts(nv * gain1 + shift1)[0] * mask[at, :]
        if main:
            acc[at, :] = jnp.zeros((size, ch), F32)
        return carry

    def slope_one(start, size, carry):
        at = pl.ds(start, size)
        slope1[at, :] = gelu_parts(normed1[at, :] * gain1 + shift1)[1] * mask[at, :]
        return carry

    take_rows(0, normed1)
    pack_field(1, hid, activate_one)
    forward(1, hid)
    send_rows(1, acc)
    send_stats(1, local_moments(acc))
    turn_field(0, masked)
    turn_field(1, hid)
    mean2, scale2, _ = moments(1)

    def activate_two(source, start, size):
        at = pl.ds(start, size)
        nv = (source[at, :] - mean2) * scale2
        normed2[at, :] = nv
        value, slope = gelu_parts(nv * gain2 + shift2 + masked[at, :])
        t = cotm[at, :] * slope
        through[at, :] = t
        return value, nv, t

    def activate_main(start, size, carry):
        value, nv, t = activate_two(acc, start, size)
        at = pl.ds(start, size)
        hid2[at, :] = value * mask[at, :]
        acc[at, :] = jnp.zeros((size, ch), F32)
        return carry[0] + fold(t * nv), carry[1] + fold(t)

    send_stats(2, [flatten(v) for v in chunked(activate_main, (zero, zero))])
    take_rows(1, normed2)
    take_cotangent()
    activate_two(normed2, cells, edge)
    to_flat(hid2, out_block)

    def gradient_sums(slot):
        take_stats(slot)
        got = [st_recv[slot, k] for k in range(s_count)]
        return sum(g[0:1] for g in got), sum(g[1:2] for g in got)

    def norm_back(upstream, normed, gain, scale, sums):
        gain_grad, shift_grad = sums
        factor = gain * scale
        level, tilt = shift_grad / count, gain_grad / count

        def fill(start, size, carry):
            at = pl.ds(start, size)
            v = upstream[at, :] - mask[at, :] * (level + normed[at, :] * tilt)
            hid[at, :] = factor * v
            return carry
        return fill

    sums2 = gradient_sums(2)
    pack_field(3, hid, norm_back(through, normed2, gain2, scale2, sums2))
    backward(1)

    send_rows(2, acc)

    def inner_main(start, size, carry):
        at = pl.ds(start, size)
        v = acc[at, :] * slope1[at, :]
        slope1[at, :] = v
        acc[at, :] = jnp.zeros((size, ch), F32)
        return carry[0] + fold(v * normed1[at, :]), carry[1] + fold(v)

    send_stats(3, [flatten(v) for v in chunked(inner_main, (zero, zero))])

    @pl.when(jnp.logical_not(passing))
    def _():
        for step in range(n - 2, n):
            of_step(step, functools.partial(make_grad, 1))
    for side in range(2):
        row_copy(2, 1 - side).wait_recv()
        at = slice(cells + side * wide, cells + (side + 1) * wide)
        slope1[at, :] = row_recv[2, side] * slope1[at, :]
    sums1 = gradient_sums(3)
    pack_field(2, hid, norm_back(slope1, normed1, gain1, scale1, sums1))
    backward(0)
    advance_second(n)
    advance(0, n)

    def finish_input(start, size, carry):
        at = pl.ds(start, size)
        acc[at, :] = (acc[at, :] + through[at, :]) * mask[at, :]
        return carry

    chunked(finish_input, 0)
    to_flat(acc, out_input)
    out_gain1[...], out_shift1[...] = sums1
    out_gain2[...], out_shift2[...] = sums2
    for extra in range(1, len(stages) - 1):
        advance_second(n + extra)
        advance(0, n + extra)

    for side in range(2):
        edge_copy(side).wait_send()
        cot_copy(side).wait_send()
        for slot in range(3):
            row_copy(slot, side).wait_send()

    @pl.loop(1, s_count)
    def _(k):
        for slot in range(4):
            st_copy(slot, k, s).wait_send()

    @pl.loop(1, n)
    def _(k):
        for which in range(2):
            wz_copy(which, k).wait_send()

    @pl.loop(1, w_parts)
    def _(k):
        for which in range(2):
            for slot in range(n - 1):
                wp_copy(which, slot, k, w_mine).wait_send()

    @pl.loop(0, n)
    def _(k):
        for sign in (1, -1):
            block = z - k * sign

            @pl.when((block >= 0) & (block < n) & (z + sign >= 0) & (z + sign < n))
            def _():
                for ph in range(4):
                    for q in range(HALVES):
                        ag_copy(ph, block, q, sign).wait_send()

    @pl.loop(0, n)
    def _(j):
        for ph in range(2):
            c_copy(ph, j).wait_send()
            h_copy(ph, j, core).wait_send()
            o_copy(ph, j).wait()

            @pl.loop(1, chips)
            def _(e):
                peer = (chip + e) % chips

                @pl.when(peer < owners)
                def _():
                    q_copy(ph, j, e, chip, peer).wait_send()

                @pl.when(chip < owners)
                def _():
                    f_copy(ph, j, e, chip).wait_send()


def finish_kernel(count, *refs):
    ins, outs = refs[:count], refs[count:2 * count]
    narrow, wide, in_sem, out_sem, take_sem, give_sem = refs[2 * count:2 * count + 6]
    held = refs[2 * count + 6:]
    rows = narrow.shape[1] // FINISH_PARTS
    parts = [(w, i, pl.ds(i * rows, rows)) for i in range(FINISH_PARTS) for w in range(2)]
    loads = [pltpu.make_async_copy(ins[w].at[at, :], narrow.at[w, at, :], in_sem.at[w, i]) for w, i, at in parts]
    stores = [pltpu.make_async_copy(wide.at[w, at, :], outs[w].at[at, :], out_sem.at[w, i]) for w, i, at in parts]
    takes = [pltpu.make_async_copy(ins[2 + k], v, take_sem.at[k]) for k, v in enumerate(held)]
    gives = [pltpu.make_async_copy(v, outs[2 + k], give_sem.at[k]) for k, v in enumerate(held)]
    for copy in loads + takes:
        copy.start()
    for load, store, (w, i, at) in zip(loads, stores, parts):
        load.wait()
        wide[w, at, :] = narrow[w, at, :].astype(F32)
        store.start()
    for take, give in zip(takes, gives):
        take.wait()
        give.start()
    for copy in stores + gives:
        copy.wait()


def per_device(n, s_count, blocks, weight_one, weight_two, gain_one, shift_one, gain_two, shift_two, cell_live, cotangent):
    rows, wide = cell_live.shape
    ch = blocks.shape[1] // wide
    cells = rows * wide
    total = cells + 2 * wide
    packed = -(-most_live(rows // HALVES, wide) // 16) * 16
    aligned = ch % 128 == 0
    chips = s_count // 2
    tap_rows = 9 * ch
    half_rows = tap_rows // 2
    owners = math.gcd(half_rows // 16, chips)
    piece = half_rows // owners

    if aligned:
        weight_one, weight_two = (w.reshape(tap_rows, n * ch) for w in (weight_one, weight_two))
    else:
        weight_one, weight_two = (
            w.reshape(tap_rows, n, ch).transpose(1, 0, 2) for w in (weight_one, weight_two))
    grad_shape = (2, owners, piece, n * ch) if aligned else (n, 2, owners, piece, ch)
    vmem = pl.BlockSpec(memory_space=pltpu.VMEM)
    hbm = pl.BlockSpec(memory_space=pl.ANY)
    sem = pltpu.SemaphoreType.DMA
    field = pltpu.VMEM((total, ch), F32)
    scratch = [
        pltpu.VMEM((ch * wide, 128), F32),
        pltpu.VMEM((2, n, tap_rows, ch), BF16),
        pltpu.VMEM((2, n - 1, tap_rows, ch), BF16),
        pltpu.VMEM((2, 3 * ch, cells), BF16),
        pltpu.VMEM((HALVES, packed, cells // HALVES), BF16),
        pltpu.VMEM((HALVES, cells // HALVES, packed), BF16),
        pltpu.VMEM((HALVES, cells // HALVES, ch), F32),
        pltpu.VMEM((2, 2, wide, ch), BF16),
        pltpu.VMEM((2, 2, wide, ch), BF16),
        pltpu.VMEM((2, wide, ch), BF16),
        pltpu.VMEM((2, wide, ch), BF16),
        field, field, field, field, field, field, field, field, field,
        pltpu.VMEM((total + 16, ch), F32),
        pltpu.VMEM((cells, ch), F32),
        pltpu.VMEM((4, n, 2 * wide + HALVES * packed, ch), BF16),
        pltpu.VMEM((n, rows + 2, wide, 3 * ch), BF16),
        pltpu.VMEM((2, n, 2, owners, piece, ch), F32),
        pltpu.VMEM((2, n, owners, piece, ch), BF16),
        pltpu.VMEM((2, n, owners, piece, ch), BF16),
        pltpu.VMEM((2, n, owners, piece, ch), BF16),
        pltpu.VMEM((2, n, chips, piece, ch), BF16),
        pltpu.VMEM((2, n, 2, owners, piece, ch), BF16),
        pltpu.VMEM((4, 8, ch), F32),
        pltpu.VMEM((4, s_count, 8, ch), F32),
        pltpu.VMEM((3, 2, wide, ch), F32),
        pltpu.VMEM((3, 2, wide, ch), F32),
        sem((2, n)),
        sem((2, n)), sem((2, n)),
        sem((2, n - 1, s_count)), sem((2, n - 1, s_count)),
        sem((2,)), sem((2,)),
        sem((2,)), sem((2,)),
        sem((4, 2, n, HALVES)), sem((4, n, HALVES)),
        sem((4, s_count)), sem((4, s_count)),
        sem((3, 2)), sem((3, 2)),
        sem((2, n)), sem((2, n)),
        sem((2, n, chips)), sem((2, n, chips)),
        sem((2, n, chips)), sem((2, n, chips)),
        sem((2, n)), sem((2, n)),
        sem((2, n)),
    ]
    block_out, input_grad, wg1, wg2, *sums = pl.pallas_call(
        functools.partial(block_kernel, n, s_count, rows, wide, ch, aligned, packed),
        out_shape=(
            jax.ShapeDtypeStruct((rows, ch * wide), BF16),
            jax.ShapeDtypeStruct((rows, ch * wide), F32),
            jax.ShapeDtypeStruct(grad_shape, BF16),
            jax.ShapeDtypeStruct(grad_shape, BF16),
            *[jax.ShapeDtypeStruct((1, ch), F32)] * 4,
        ),
        in_specs=[vmem] * 7 + [hbm] * 2,
        out_specs=(vmem, vmem, hbm, hbm, vmem, vmem, vmem, vmem),
        scratch_shapes=scratch,
        compiler_params=pltpu.CompilerParams(
            collective_id=0, has_side_effects=True, vmem_limit_bytes=60 * 1024 * 1024),
    )(blocks, cotangent, cell_live.T,
      *(v.reshape(1, ch) for v in (gain_one, shift_one, gain_two, shift_two)), weight_one, weight_two)

    if not aligned:
        def whole(grad):
            grad = grad.reshape(n, tap_rows, ch).transpose(1, 0, 2)
            return grad.astype(F32).reshape(9, ch, n * ch)
        return (block_out, input_grad, whole(wg1), whole(wg2), *(v.reshape(ch) for v in sums))

    wg1, wg2 = (w.reshape(tap_rows, n * ch) for w in (wg1, wg2))
    wide_grad = jax.ShapeDtypeStruct((tap_rows, n * ch), F32)
    moved = (block_out, input_grad, *sums)
    grad1, grad2, *moved = pl.pallas_call(
        functools.partial(finish_kernel, 2 + len(moved)),
        out_shape=(wide_grad, wide_grad, *(jax.ShapeDtypeStruct(v.shape, v.dtype) for v in moved)),
        in_specs=[pl.BlockSpec(memory_space=pl.ANY)] * (2 + len(moved)),
        out_specs=[pl.BlockSpec(memory_space=pl.ANY)] * (2 + len(moved)),
        scratch_shapes=[
            pltpu.VMEM((2, tap_rows, n * ch), BF16), pltpu.VMEM((2, tap_rows, n * ch), F32),
            sem((2, FINISH_PARTS)), sem((2, FINISH_PARTS)), sem((len(moved),)), sem((len(moved),)),
            *(pltpu.VMEM(v.shape, v.dtype) for v in moved),
        ],
        compiler_params=pltpu.CompilerParams(vmem_limit_bytes=64 * 1024 * 1024),
    )(wg1, wg2, *moved)
    block_out, input_grad, *sums = moved
    grads = (g.reshape(9, ch, n * ch) for g in (grad1, grad2))
    return (block_out, input_grad, *grads, *(v.reshape(ch) for v in sums))


def solution(mesh):
    return jax.shard_map(
        functools.partial(per_device, mesh.shape["chan"], mesh.shape["space"]),
        mesh=mesh,
        in_specs=(
            P("space", "chan"),
            P(None, "chan", None),
            P(None, "chan", None),
            P("chan"),
            P("chan"),
            P("chan"),
            P("chan"),
            P("space", None),
            P("space", "chan"),
        ),
        out_specs=(
            P("space", "chan"),
            P("space", "chan"),
            P(None, "chan", None),
            P(None, "chan", None),
            P("chan"),
            P("chan"),
            P("chan"),
            P("chan"),
        ),
        check_vma=False,
    )
```

```python
import functools
import math

import jax
import jax.numpy as jnp
from jax import lax
from jax.experimental import pallas as pl
from jax.experimental.pallas import tpu as pltpu
from jax.sharding import PartitionSpec as P

EPSILON = 1e-05
MESH = pl.DeviceIdType.MESH
F32 = jnp.float32
BF16 = jnp.bfloat16
ROOT_HALF = 0.7071067811865476
ROOT_TWO_PI = 0.3989422804014327
CHUNK = 64
FINISH_PARTS = 4
UNROLL = 2
HALVES = 2
LARGE, SMALL = 7, 3


def dot(a, b):
    return jnp.dot(a, b, preferred_element_type=F32)


def gelu_parts(v):
    upper = 0.5 * (1.0 + lax.erf(v * ROOT_HALF))
    slope = upper + v * (ROOT_TWO_PI * jnp.exp(-0.5 * v * v))
    return v * upper, slope


def most_live(rows, wide):
    units = (wide + 1) // (SMALL + 1)
    live_rows = rows - rows // (LARGE + 1)
    return min(rows * wide, math.ceil(units * live_rows * LARGE / 2))


def block_kernel(n, s_count, rows, wide, ch, aligned, packed, *refs):
    (x_in, cot_in, live_in, gain1_in, shift1_in, gain2_in, shift2_in, w1_hbm, w2_hbm) = refs[:9]
    (out_block, out_input, out_wg1, out_wg2, out_gain1, out_shift1, out_gain2, out_shift2) = refs[9:17]
    (turned, wv, wf, x_t, pack, unpack, places, edge_send, edge_recv, cot_send, cot_recv, cotm, mask, masked,
     normed1, normed2, through, slope1, hid, hid2, pad, acc, hold, taken,
     part, psend, crecv, hsend, qrecv, wout, st_send, st_recv, row_send, row_recv,
     w_sem, wz_ssem, wz_rsem, wp_ssem, wp_rsem, e_ssem, e_rsem, ce_ssem, ce_rsem, ag_ssem, ag_rsem,
     st_ssem, st_rsem, row_ssem, row_rsem, c_ssem, c_rsem, q_ssem, q_rsem,
     f_ssem, f_rsem, h_ssem, h_rsem, o_sem) = refs[17:]

    z = lax.axis_index("chan")
    s = lax.axis_index("space")
    cells = rows * wide
    total = cells + 2 * wide
    band = cells // HALVES
    core, chip, chips = s % 2, s // 2, s_count // 2
    before, after = (s + s_count - 1) % s_count, (s + 1) % s_count
    tap_rows = 9 * ch

    barrier = pltpu.get_barrier_semaphore()

    @pl.loop(1, s_count)
    def _(k):
        pl.semaphore_signal(barrier, inc=1, device_id=(z, (s + k) % s_count), device_id_type=MESH)

    @pl.loop(1, n)
    def _(k):
        pl.semaphore_signal(barrier, inc=1, device_id=((z + k) % n, s), device_id_type=MESH)

    w_copies = []
    for which, source in enumerate((w1_hbm, w2_hbm)):
        for d in range(n):
            block = source.at[:, d * ch:(d + 1) * ch] if aligned else source.at[d]
            w_copies.append(pltpu.make_async_copy(block, wv.at[which, d], w_sem.at[which, d]))
    for copy in w_copies:
        copy.start()

    def chunked(fn, init, first=0, count=cells):
        def step(i, carry):
            return fn(pl.multiple_of(first + i * CHUNK, CHUNK), CHUNK, carry)
        return lax.fori_loop(0, count // CHUNK, step, init, unroll=UNROLL)

    lanes = 128
    tiles = ch * wide // lanes

    def from_flat(flat, put):
        for i in range(tiles):
            turned[i * lanes:(i + 1) * lanes, 0:rows] = flat[:, i * lanes:(i + 1) * lanes].astype(F32).T
        for w in range(wide):
            put(pl.ds(w, rows, stride=wide), turned[pl.ds(w, ch, stride=wide), 0:rows].T)

    def to_flat(source, flat):
        for w in range(wide):
            turned[pl.ds(w, ch, stride=wide), 0:rows] = source[pl.ds(w, rows, stride=wide), :].T
        for i in range(tiles):
            flat[:, i * lanes:(i + 1) * lanes] = turned[i * lanes:(i + 1) * lanes, 0:rows].T.astype(flat.dtype)

    def put_masked(at, value):
        masked[at, :] = value

    from_flat(x_in, put_masked)

    cell = lax.broadcasted_iota(jnp.int32, (cells, rows), 0)
    pick = (cell // wide == lax.broadcasted_iota(jnp.int32, (cells, rows), 1)).astype(F32).astype(BF16)
    column_of = lax.broadcasted_iota(jnp.int32, (cells, wide), 0) % wide
    picked = lax.dot_general(pick, live_in[...].astype(BF16), (((1,), (1,)), ((), ())), preferred_element_type=F32)
    picked = jnp.where(column_of == lax.broadcasted_iota(jnp.int32, (cells, wide), 1), picked, 0.0)
    mask[0:cells, :] = dot(picked.astype(BF16), jnp.ones((wide, ch), BF16))

    def load_main(start, size, carry):
        at = pl.ds(start, size)
        lv = mask[at, :]
        masked[at, :] = masked[at, :] * lv
        return carry

    chunked(load_main, 0)
    for side, start in ((0, 0), (1, cells - wide)):
        edge_send[side, 0] = masked[start:start + wide, :].astype(BF16)
        edge_send[side, 1] = mask[start:start + wide, :].astype(BF16)

    acc[...] = jnp.zeros_like(acc)
    for block in range(n):
        for row in (rows // HALVES + 1, rows + 2):
            taken[block, row:row + 1, :, :] = jnp.zeros((1, wide, 3 * ch), BF16)
    st_send[...] = jnp.zeros_like(st_send)

    pl.semaphore_wait(barrier, s_count - 1 + n - 1)

    def edge_copy(side):
        return pltpu.make_async_remote_copy(
            src_ref=edge_send.at[side], dst_ref=edge_recv.at[1 - side],
            send_sem=e_ssem.at[side], recv_sem=e_rsem.at[1 - side],
            device_id=(z, before if side == 0 else after), device_id_type=MESH)

    for side in range(2):
        edge_copy(side).start()

    def cot_copy(side):
        return pltpu.make_async_remote_copy(
            src_ref=cot_send.at[side], dst_ref=cot_recv.at[1 - side],
            send_sem=ce_ssem.at[side], recv_sem=ce_rsem.at[1 - side],
            device_id=(z, before if side == 0 else after), device_id_type=MESH)

    def load_cotangent():
        def put(at, value):
            cotm[at, :] = value
        from_flat(cot_in, put)

        def live_only(start, size, carry):
            at = pl.ds(start, size)
            cotm[at, :] = cotm[at, :] * mask[at, :]
            return carry
        chunked(live_only, 0)
        for side, start in ((0, 0), (1, cells - wide)):
            cot_send[side] = cotm[start:start + wide, :].astype(BF16)
            cot_copy(side).start()

    def take_cotangent():
        for side in range(2):
            cot_copy(1 - side).wait_recv()
            at = slice(cells + side * wide, cells + (side + 1) * wide)
            cotm[at, :] = cot_recv[side].astype(F32) * mask[at, :]

    w_parts = math.gcd(tap_rows // 16, s_count)
    w_rows = tap_rows // w_parts
    w_mine = s % w_parts
    w_group = s - w_mine

    def wz_copy(which, k):
        at = pl.ds(w_mine * w_rows, w_rows)
        slot = n - k - 1
        return pltpu.make_async_remote_copy(
            src_ref=wv.at[which, (z + k) % n, at, :], dst_ref=wf.at[which, slot, at, :],
            send_sem=wz_ssem.at[which, slot], recv_sem=wz_rsem.at[which, slot],
            device_id=((z + k) % n, s), device_id_type=MESH)

    def wp_copy(which, slot, k, whose):
        at = pl.ds(whose * w_rows, w_rows)
        return pltpu.make_async_remote_copy(
            src_ref=wf.at[which, slot, at, :], dst_ref=wf.at[which, slot, at, :],
            send_sem=wp_ssem.at[which, slot, k], recv_sem=wp_rsem.at[which, slot, whose],
            device_id=(z, w_group + (w_mine + k) % w_parts), device_id_type=MESH)

    def weights_over_z(which):
        for copy in w_copies[which * n:(which + 1) * n]:
            copy.wait()

        @pl.loop(1, n)
        def _(k):
            wz_copy(which, k).start()

    def slot_of(block):
        return (block - z + n - 1) % n

    def weights_round(which):
        @pl.loop(1, n)
        def _(distance):
            for sign in (1, -1):
                block = z - distance * sign

                @pl.when((block >= 0) & (block < n))
                def _():
                    slot = slot_of(block)
                    wz_copy(which, n - 1 - slot).wait_recv()

                    @pl.loop(1, w_parts)
                    def _(k):
                        wp_copy(which, slot, k, w_mine).start()

    def weights_arrived(which, slot):
        @pl.loop(1, w_parts)
        def _(k):
            wp_copy(which, slot, k, (w_mine + k) % w_parts).wait_recv()

    def row_copy(slot, side):
        return pltpu.make_async_remote_copy(
            src_ref=row_send.at[slot, side], dst_ref=row_recv.at[slot, 1 - side],
            send_sem=row_ssem.at[slot, side], recv_sem=row_rsem.at[slot, 1 - side],
            device_id=(z, before if side == 0 else after), device_id_type=MESH)

    def send_rows(slot, ref):
        for side, start in ((0, 0), (1, cells - wide)):
            row_send[slot, side] = ref[start:start + wide, :]
            row_copy(slot, side).start()

    def take_rows(slot, ref):
        for side in range(2):
            row_copy(slot, 1 - side).wait_recv()
            ref[cells + side * wide:cells + (side + 1) * wide, :] = row_recv[slot, side]

    def st_copy(slot, k, whose):
        return pltpu.make_async_remote_copy(
            src_ref=st_send.at[slot], dst_ref=st_recv.at[slot, whose],
            send_sem=st_ssem.at[slot, k], recv_sem=st_rsem.at[slot, whose],
            device_id=(z, (s + k) % s_count), device_id_type=MESH)

    def send_stats(slot, values):
        for i, v in enumerate(values):
            st_send[slot, i:i + 1, :] = v
        for k in range(1, s_count):
            st_copy(slot, k, s).start()
        st_recv[slot, s] = st_send[slot]

    def take_stats(slot):
        for k in range(1, s_count):
            st_copy(slot, k, (s + k) % s_count).wait_recv()

    strip = 8
    column = lax.broadcasted_iota(jnp.int32, (strip * wide, ch), 0) % wide

    def shift(target, first, count):
        size = count * wide
        where = column[:size]
        here = pad[pl.ds(8 + first * wide, size), :]
        left = jnp.where(where == 0, 0.0, pad[pl.ds(7 + first * wide, size), :])
        right = jnp.where(where == wide - 1, 0.0, pad[pl.ds(9 + first * wide, size), :])
        for b, v in enumerate((left, here, right)):
            target[pl.ds(first, count), :, b * ch:(b + 1) * ch] = v.astype(BF16).reshape(count, wide, ch)

    edge = 2 * wide
    ag_rows = ((0, edge + packed), (edge + packed, packed))
    band_rows = rows // HALVES

    def unpack_half(ph, block, q, target):
        if q == 0:
            pad[8:8 + wide, :] = hold[ph, block, 0:wide, :].astype(F32)
            pad[8 + wide + cells:8 + 2 * wide + cells, :] = hold[ph, block, wide:edge, :].astype(F32)
            shift(target, 0, 1)
            shift(target, rows + 1, 1)
        for j in range(2):
            start = edge + q * packed + j * (packed - unpack.shape[3])
            at = 8 + wide + q * band + j * (band // 2)
            pad[at:at + band // 2, :] = dot(unpack[q, j], hold[ph, block, start:start + unpack.shape[3], :])

        for i in range(band_rows // strip):
            shift(target, 1 + q * band_rows + i * strip, strip)

    def add_conv(q, field, taps, turned_taps=None):
        first, last = (0, band_rows - 1) if q == 0 else (band_rows - 1, rows)
        count = last - first
        size = (count + 2) * wide
        lhs = jnp.concatenate([
            field[first + i:last + 2 + i, :, :].reshape(size, 3 * ch) for i in range(2)], axis=1)
        if turned_taps is None:
            none = jnp.zeros((3 * ch, ch), BF16)
            rhs = jnp.concatenate([
                jnp.concatenate([taps(0), taps(2)], axis=1), jnp.concatenate([taps(1), none], axis=1)], axis=0)
            value = dot(lhs, rhs)
        else:
            def row_taps(a):
                return [turned_taps(3 * (2 - a) + 2 - b) for b in range(3)]
            none = jnp.zeros((ch, 3 * ch), BF16)
            rhs = jnp.concatenate([
                jnp.concatenate(row_taps(0) + row_taps(1), axis=1), jnp.concatenate(row_taps(2) + [none], axis=1)], axis=0)
            value = lax.dot_general(lhs, rhs, (((1,), (1,)), ((), ())), preferred_element_type=F32)
        at = pl.ds(first * wide, count * wide)
        acc[at, :] = acc[at, :] + value[0:count * wide, 0:ch] + value[2 * wide:size, ch:2 * ch]

    def ag_copy(ph, block, q, sign):
        at = pl.ds(*ag_rows[q])
        return pltpu.make_async_remote_copy(
            src_ref=hold.at[ph, block, at, :], dst_ref=hold.at[ph, block, at, :],
            send_sem=ag_ssem.at[ph, (1 - sign) // 2, block, q], recv_sem=ag_rsem.at[ph, block, q],
            device_id=(z + sign, s), device_id_type=MESH)

    def pack_field(ph, source, fill=None, first=None):
        if fill is not None:
            fill(cells, edge, 0)
        hold[ph, z, 0:edge, :] = source[cells:cells + edge, :].astype(BF16)
        for q in range(HALVES):
            if first is not None:
                first(q)
            if fill is not None:
                chunked(fill, 0, q * band, band)
            hold[ph, z, edge + q * packed:edge + (q + 1) * packed, :] = dot(
                pack[q], source[q * band:(q + 1) * band, :].astype(BF16)).astype(BF16)
            for sign in (1, -1):
                @pl.when((z + sign >= 0) & (z + sign < n))
                def _():
                    ag_copy(ph, z, q, sign).start()

    def inside(slice_at):
        return (slice_at >= 0) & (slice_at < n)

    def take_and_pass(ph, k, q, sign, passes=True, takes=True):
        block = z - k * sign

        @pl.when((k > 0) & inside(block))
        def _():
            if passes and takes:
                ag_copy(ph, block, q, sign).wait_recv()

            @pl.when(inside(z + sign))
            def _():
                if passes:
                    if not takes:
                        ag_copy(ph, block, q, sign).wait_recv()
                    ag_copy(ph, block, q, sign).start()

            if not passes:
                @pl.when(jnp.logical_not(inside(z + sign)))
                def _():
                    ag_copy(ph, block, q, sign).wait_recv()

    near = jnp.where(z < n - n // 2, 1, 0)

    def consume_way(k, q, way, consume):
        block = z - k * (1 - 2 * way)

        @pl.when((k >= 0) & (k < n) & inside(block) & ((k > 0) | (way == near)))
        def _():
            consume(k, block, q)

    def take_both(ph, k, q, **how):
        @pl.loop(0, 2)
        def _(i):
            way = (near + i) % 2
            take_and_pass(ph, k, q, 1 - 2 * way, **how)

    def gather(ph, consume, each):
        @pl.loop(0, n)
        def _(k):
            for q in range(HALVES):
                take_both(ph, k, q)
                if q:
                    consume_way(k, q - 1, 1 - near, consume)
                else:
                    consume_way(k - 1, HALVES - 1, 1 - near, consume)
                consume_way(k, q, near, consume)
            each(k)

    def gather_passing_first(ph, consume, each):
        @pl.loop(0, n)
        def _(k):
            @pl.when(k == 1)
            def _():
                @pl.loop(1, n)
                def _(ahead):
                    for q in range(HALVES):
                        take_both(ph, ahead, q, takes=False)
            for q in range(HALVES):
                take_both(ph, k, q, passes=False)

                @pl.loop(0, 2)
                def _(i):
                    consume_way(k, q, (near + i) % 2, consume)
            each(k)

    last_pass = jnp.maximum(jnp.where(z < n - 1, z, 0), jnp.where(z > 0, n - 1 - z, 0))

    def forward(ph, field):
        def consume(k, block, q):
            into = taken.at[block]
            unpack_half(ph, block, q, into)

            @pl.when(k == 0)
            def _():
                add_conv(q, into, lambda a: wv[ph, z, 3 * a * ch:3 * (a + 1) * ch, :])

            @pl.when(k > 0)
            def _():
                slot = slot_of(block)
                if q == 0:
                    weights_arrived(ph, slot)
                add_conv(q, into, lambda a: wf[ph, slot, 3 * a * ch:3 * (a + 1) * ch, :])

        def each(k):
            if ph == 0:
                @pl.when(k == 0)
                def _():
                    weights_round(0)

                @pl.when(k == 1)
                def _():
                    weights_over_z(1)
        (gather if ph else gather_passing_first)(ph, consume, each)

    def turn_field(ph, field):
        main = [field[start:start + ch, :].T for start in range(0, cells, ch)]
        ends = field[cells:cells + edge, :]
        if edge < ch:
            ends = jnp.concatenate([ends, jnp.zeros((ch - edge, ch), F32)], axis=0)
        ends = ends.T
        for i, here in enumerate(main):
            left = jnp.concatenate(
                [ends[:, 0:wide] if i == 0 else main[i - 1][:, ch - wide:], here[:, 0:ch - wide]], axis=1)
            right = jnp.concatenate(
                [here[:, wide:], main[i + 1][:, 0:wide] if i + 1 < len(main) else ends[:, wide:edge]], axis=1)
            for a, v in enumerate((left, here, right)):
                x_t[ph, a * ch:(a + 1) * ch, i * ch:(i + 1) * ch] = v.astype(BF16)

    half_rows = tap_rows // 2
    owners = math.gcd(half_rows // 16, chips)
    piece = half_rows // owners

    def c_copy(ph, j):
        return pltpu.make_async_remote_copy(
            src_ref=psend.at[ph, j], dst_ref=crecv.at[ph, j],
            send_sem=c_ssem.at[ph, j], recv_sem=c_rsem.at[ph, j],
            device_id=(z, chip * 2 + 1 - core), device_id_type=MESH)

    def q_copy(ph, j, e, whose, owner):
        return pltpu.make_async_remote_copy(
            src_ref=hsend.at[ph, j, owner], dst_ref=qrecv.at[ph, j, whose],
            send_sem=q_ssem.at[ph, j, e], recv_sem=q_rsem.at[ph, j, whose],
            device_id=(z, ((chip + e) % chips) * 2 + core), device_id_type=MESH)

    def f_copy(ph, j, e, owner):
        return pltpu.make_async_remote_copy(
            src_ref=wout.at[ph, j, core, owner], dst_ref=wout.at[ph, j, core, owner],
            send_sem=f_ssem.at[ph, j, e], recv_sem=f_rsem.at[ph, j, owner],
            device_id=(z, ((chip + e) % chips) * 2 + core), device_id_type=MESH)

    def h_copy(ph, j, whose):
        return pltpu.make_async_remote_copy(
            src_ref=wout.at[ph, j, whose], dst_ref=wout.at[ph, j, whose],
            send_sem=h_ssem.at[ph, j], recv_sem=h_rsem.at[ph, j],
            device_id=(z, chip * 2 + 1 - core), device_id_type=MESH)

    def o_copy(ph, j):
        target = (out_wg1, out_wg2)[ph]
        if aligned:
            target = target.at[:, :, :, pl.ds(pl.multiple_of(j * ch, ch), ch)]
        else:
            target = target.at[j]
        return pltpu.make_async_copy(wout.at[ph, j], target, o_sem.at[ph, j])

    def sum_cores(ph, j):
        for o in range(owners):
            psend[ph, j, o] = part[ph, j, 1 - core, o].astype(BF16)
        c_copy(ph, j).start()

    def sum_chips(ph, j):
        c_copy(ph, j).wait_recv()
        for o in range(owners):
            v = part[ph, j, core, o] + crecv[ph, j, o].astype(F32)
            part[ph, j, core, o] = v
            hsend[ph, j, o] = v.astype(BF16)

        @pl.loop(1, chips)
        def _(e):
            peer = (chip + e) % chips

            @pl.when(peer < owners)
            def _():
                q_copy(ph, j, e, chip, peer).start()

    def spread_chips(ph, j):
        @pl.when(chip < owners)
        def _():
            @pl.loop(1, chips)
            def _(e):
                q_copy(ph, j, e, (chip + e) % chips, chip).wait_recv()
            v = part[ph, j, core, chip]
            for e in range(1, chips):
                v = v + qrecv[ph, j, (chip + e) % chips].astype(F32)
            wout[ph, j, core, chip] = v.astype(BF16)

            @pl.loop(1, chips)
            def _(e):
                f_copy(ph, j, e, chip).start()

    def spread_cores(ph, j):
        @pl.loop(1, chips)
        def _(e):
            peer = (chip + e) % chips

            @pl.when(peer < owners)
            def _():
                f_copy(ph, j, e, peer).wait_recv()
        h_copy(ph, j, core).start()

    def finish(ph, j):
        h_copy(ph, j, 1 - core).wait_recv()
        o_copy(ph, j).start()

    def put_part(ph, j, tap, value):
        start = tap * ch
        done = 0
        while done < ch:
            row = start + done
            side, o, at = row // half_rows, row % half_rows // piece, row % piece
            size = min(ch - done, piece - at)
            part[ph, j, side, o, at:at + size, :] = value[done:done + size, :]
            done += size

    stages = (sum_cores, sum_chips, spread_chips, spread_cores, finish)

    def of_step(k, fn):
        @pl.loop(0, 2)
        def _(way):
            block = z - k * (1 - 2 * way)

            @pl.when((k >= 0) & (k < n) & inside(block) & ((k > 0) | (way == 0)))
            def _():
                fn(block)

    passing = last_pass > 0

    def made_at(step):
        first = jnp.where(passing & (step > 0), jnp.where(step == last_pass, 1, step + 1), step)
        return first, step + 1

    def advance(ph, k):
        for age in range(1, len(stages)):
            step = k - age

            @pl.when((step >= 0) & (step < n))
            def _():
                @pl.loop(*made_at(step))
                def _(made):
                    of_step(made, functools.partial(stages[age], ph))

    def advance_all(ph, age):
        @pl.loop(0, n)
        def _(j):
            stages[age](ph, j)

    def field_grad(ph, block):
        grad = taken[block, 1:rows + 1, :, :].reshape(cells, 3 * ch)
        value = dot(x_t[ph], grad)
        for a in range(3):
            for b in range(3):
                put_part(ph, block, 3 * a + b, value[a * ch:(a + 1) * ch, (2 - b) * ch:(3 - b) * ch])

    def make_grad(ph, block):
        field_grad(ph, block)
        sum_cores(ph, block)

    def backward(ph):
        last = ph == 0

        def consume(k, block, q):
            into = taken.at[block]
            unpack_half(2 + ph, block, q, into)
            if last and q == HALVES - 1:
                @pl.when((k == 0) | (k >= last_pass))
                def _():
                    make_grad(ph, block)
            add_conv(q, into, None, lambda t: wv[ph, block, t * ch:(t + 1) * ch, :])

        def each(k):
            first, end = made_at(k)
            if last:
                @pl.loop(first, end - 1)
                def _(step):
                    of_step(step, functools.partial(make_grad, ph))
                advance(ph, k)
                for age in range(2, len(stages)):
                    @pl.when(k == age - 2)
                    def _():
                        advance_all(1, age)
            else:
                @pl.loop(first, jnp.where(passing | (k < n - 2), end, first))
                def _(step):
                    of_step(step, functools.partial(make_grad, ph))
        gather(2 + ph, consume, each)

    def fold(v):
        return jnp.sum(v.reshape(v.shape[0] // 8, 8, ch), axis=0)

    def flatten(v):
        return jnp.sum(v, axis=0, keepdims=True)

    zero = jnp.zeros((8, ch), F32)

    def local_moments(ref):
        def sums(start, size, carry):
            at = pl.ds(start, size)
            m = mask[at, :]
            return carry[0] + fold(ref[at, :] * m), carry[1] + fold(m)
        added, number = (flatten(v) for v in chunked(sums, (zero, zero)))
        middle = added / jnp.maximum(number, 1.0)

        def spread(start, size, carry):
            at = pl.ds(start, size)
            c = (ref[at, :] - middle) * mask[at, :]
            return carry + fold(c * c)
        return added, number, flatten(chunked(spread, zero))

    def moments(slot):
        take_stats(slot)
        got = [st_recv[slot, k] for k in range(s_count)]
        added = sum(g[0:1] for g in got)
        number = sum(g[1:2] for g in got)
        mean = added / number
        spread = 0.0
        for g in got:
            off = g[0:1] / jnp.maximum(g[1:2], 1.0) - mean
            spread = spread + (g[2:3] + g[1:2] * off * off)
        return mean, lax.rsqrt(spread / number + EPSILON), number

    def everywhere(fn):
        chunked(fn, 0)
        fn(cells, 2 * wide, 0)

    gain1, shift1, gain2, shift2 = (r[...] for r in (gain1_in, shift1_in, gain2_in, shift2_in))

    weights_over_z(0)

    quarter = band // 2
    kept = packed // 2
    window = unpack.shape[3]
    below = lax.broadcasted_iota(jnp.int32, (quarter, quarter), 1) < lax.broadcasted_iota(jnp.int32, (quarter, quarter), 0)
    below = below.astype(F32).astype(BF16)

    def make_pack(h):
        for j in range(2):
            lv = mask[h * band + j * quarter:h * band + (j + 1) * quarter, :]
            place = jnp.where(lv > 0.0, dot(below, lv.astype(BF16)) + j * kept, -1.0)
            places[h, j] = place
            across = place.T[0:1, :]
            spot = lax.broadcasted_iota(jnp.int32, (packed, quarter), 0).astype(F32)
            pack[h, :, j * quarter:(j + 1) * quarter] = jnp.where(spot == across, 1.0, 0.0).astype(BF16)

    def make_unpack(h):
        for j in range(2):
            for start in range(0, window, ch):
                size = min(ch, window - start)
                spot = start + j * (packed - window) + lax.broadcasted_iota(jnp.int32, (quarter, size), 1)
                unpack[h, j, :, start:start + size] = jnp.where(
                    places[h, j, :, :size] == spot.astype(F32), 1.0, 0.0).astype(BF16)

    for side in range(2):
        edge_copy(1 - side).wait_recv()
        there = jnp.where(s > 0, 1.0, 0.0) if side == 0 else jnp.where(s < s_count - 1, 1.0, 0.0)
        at = slice(cells + side * wide, cells + (side + 1) * wide)
        masked[at, :] = edge_recv[side, 0].astype(F32) * there
        mask[at, :] = edge_recv[side, 1].astype(F32) * there

    pack_field(0, masked, first=make_pack)
    for h in range(HALVES):
        make_unpack(h)
    forward(0, masked)
    send_rows(0, acc)
    send_stats(0, local_moments(acc))
    weights_round(1)
    load_cotangent()
    mean1, scale1, count = moments(0)

    def activate_one(start, size, carry):
        at = pl.ds(start, size)
        main = start is not cells
        nv = ((acc if main else normed1)[at, :] - mean1) * scale1
        normed1[at, :] = nv
        hid[at, :] = gelu_parts(nv * gain1 + shift1)[0] * mask[at, :]
        if main:
            acc[at, :] = jnp.zeros((size, ch), F32)
        return carry

    def slope_one(start, size, carry):
        at = pl.ds(start, size)
        slope1[at, :] = gelu_parts(normed1[at, :] * gain1 + shift1)[1] * mask[at, :]
        return carry

    take_rows(0, normed1)
    pack_field(1, hid, activate_one)
    everywhere(slope_one)
    forward(1, hid)
    send_rows(1, acc)
    send_stats(1, local_moments(acc))
    turn_field(0, masked)
    turn_field(1, hid)
    mean2, scale2, _ = moments(1)

    def activate_two(source, start, size):
        at = pl.ds(start, size)
        nv = (source[at, :] - mean2) * scale2
        normed2[at, :] = nv
        value, slope = gelu_parts(nv * gain2 + shift2 + masked[at, :])
        t = cotm[at, :] * slope
        through[at, :] = t
        return value, nv, t

    def activate_main(start, size, carry):
        value, nv, t = activate_two(acc, start, size)
        at = pl.ds(start, size)
        hid2[at, :] = value * mask[at, :]
        acc[at, :] = jnp.zeros((size, ch), F32)
        return carry[0] + fold(t * nv), carry[1] + fold(t)

    send_stats(2, [flatten(v) for v in chunked(activate_main, (zero, zero))])
    take_rows(1, normed2)
    take_cotangent()
    activate_two(normed2, cells, edge)
    to_flat(hid2, out_block)

    def gradient_sums(slot):
        take_stats(slot)
        got = [st_recv[slot, k] for k in range(s_count)]
        return sum(g[0:1] for g in got), sum(g[1:2] for g in got)

    def norm_back(upstream, normed, gain, scale, sums):
        gain_grad, shift_grad = sums
        factor = gain * scale
        level, tilt = shift_grad / count, gain_grad / count

        def fill(start, size, carry):
            at = pl.ds(start, size)
            v = upstream[at, :] - mask[at, :] * (level + normed[at, :] * tilt)
            hid[at, :] = factor * v
            return carry
        return fill

    sums2 = gradient_sums(2)
    pack_field(3, hid, norm_back(through, normed2, gain2, scale2, sums2))
    backward(1)

    send_rows(2, acc)

    def inner_main(start, size, carry):
        at = pl.ds(start, size)
        v = acc[at, :] * slope1[at, :]
        slope1[at, :] = v
        acc[at, :] = jnp.zeros((size, ch), F32)
        return carry[0] + fold(v * normed1[at, :]), carry[1] + fold(v)

    send_stats(3, [flatten(v) for v in chunked(inner_main, (zero, zero))])

    @pl.when(jnp.logical_not(passing))
    def _():
        for step in range(n - 2, n):
            of_step(step, functools.partial(make_grad, 1))
    for side in range(2):
        row_copy(2, 1 - side).wait_recv()
        at = slice(cells + side * wide, cells + (side + 1) * wide)
        slope1[at, :] = row_recv[2, side] * slope1[at, :]
    sums1 = gradient_sums(3)
    pack_field(2, hid, norm_back(slope1, normed1, gain1, scale1, sums1))
    advance_all(1, 1)
    backward(0)
    advance(0, n)

    def finish_input(start, size, carry):
        at = pl.ds(start, size)
        acc[at, :] = (acc[at, :] + through[at, :]) * mask[at, :]
        return carry

    chunked(finish_input, 0)
    to_flat(acc, out_input)
    out_gain1[...], out_shift1[...] = sums1
    out_gain2[...], out_shift2[...] = sums2
    for extra in range(1, len(stages) - 1):
        advance(0, n + extra)

    for side in range(2):
        edge_copy(side).wait_send()
        cot_copy(side).wait_send()
        for slot in range(3):
            row_copy(slot, side).wait_send()

    @pl.loop(1, s_count)
    def _(k):
        for slot in range(4):
            st_copy(slot, k, s).wait_send()

    @pl.loop(1, n)
    def _(k):
        for which in range(2):
            wz_copy(which, k).wait_send()

    @pl.loop(1, w_parts)
    def _(k):
        for which in range(2):
            for slot in range(n - 1):
                wp_copy(which, slot, k, w_mine).wait_send()

    @pl.loop(0, n)
    def _(k):
        for sign in (1, -1):
            block = z - k * sign

            @pl.when((block >= 0) & (block < n) & (z + sign >= 0) & (z + sign < n))
            def _():
                for ph in range(4):
                    for q in range(HALVES):
                        ag_copy(ph, block, q, sign).wait_send()

    @pl.loop(0, n)
    def _(j):
        for ph in range(2):
            c_copy(ph, j).wait_send()
            h_copy(ph, j, core).wait_send()
            o_copy(ph, j).wait()

            @pl.loop(1, chips)
            def _(e):
                peer = (chip + e) % chips

                @pl.when(peer < owners)
                def _():
                    q_copy(ph, j, e, chip, peer).wait_send()

                @pl.when(chip < owners)
                def _():
                    f_copy(ph, j, e, chip).wait_send()


def finish_kernel(count, *refs):
    ins, outs = refs[:count], refs[count:2 * count]
    narrow, wide, in_sem, out_sem, take_sem, give_sem = refs[2 * count:2 * count + 6]
    held = refs[2 * count + 6:]
    rows = narrow.shape[1] // FINISH_PARTS
    parts = [(w, i, pl.ds(i * rows, rows)) for i in range(FINISH_PARTS) for w in range(2)]
    loads = [pltpu.make_async_copy(ins[w].at[at, :], narrow.at[w, at, :], in_sem.at[w, i]) for w, i, at in parts]
    stores = [pltpu.make_async_copy(wide.at[w, at, :], outs[w].at[at, :], out_sem.at[w, i]) for w, i, at in parts]
    takes = [pltpu.make_async_copy(ins[2 + k], v, take_sem.at[k]) for k, v in enumerate(held)]
    gives = [pltpu.make_async_copy(v, outs[2 + k], give_sem.at[k]) for k, v in enumerate(held)]
    for copy in loads + takes:
        copy.start()
    for load, store, (w, i, at) in zip(loads, stores, parts):
        load.wait()
        wide[w, at, :] = narrow[w, at, :].astype(F32)
        store.start()
    for take, give in zip(takes, gives):
        take.wait()
        give.start()
    for copy in stores + gives:
        copy.wait()


def per_device(n, s_count, blocks, weight_one, weight_two, gain_one, shift_one, gain_two, shift_two, cell_live, cotangent):
    rows, wide = cell_live.shape
    ch = blocks.shape[1] // wide
    cells = rows * wide
    total = cells + 2 * wide
    packed = 2 * -(-most_live(rows // HALVES // 2, wide) // 8) * 8
    aligned = ch % 128 == 0
    chips = s_count // 2
    tap_rows = 9 * ch
    half_rows = tap_rows // 2
    owners = math.gcd(half_rows // 16, chips)
    piece = half_rows // owners

    if aligned:
        weight_one, weight_two = (w.reshape(tap_rows, n * ch) for w in (weight_one, weight_two))
    else:
        weight_one, weight_two = (
            w.reshape(tap_rows, n, ch).transpose(1, 0, 2) for w in (weight_one, weight_two))
    grad_shape = (2, owners, piece, n * ch) if aligned else (n, 2, owners, piece, ch)
    vmem = pl.BlockSpec(memory_space=pltpu.VMEM)
    hbm = pl.BlockSpec(memory_space=pl.ANY)
    sem = pltpu.SemaphoreType.DMA
    field = pltpu.VMEM((total, ch), F32)
    scratch = [
        pltpu.VMEM((ch * wide, 128), F32),
        pltpu.VMEM((2, n, tap_rows, ch), BF16),
        pltpu.VMEM((2, n - 1, tap_rows, ch), BF16),
        pltpu.VMEM((2, 3 * ch, cells), BF16),
        pltpu.VMEM((HALVES, packed, cells // HALVES), BF16),
        pltpu.VMEM((HALVES, 2, cells // HALVES // 2, -(-packed // 2 // 16) * 16), BF16),
        pltpu.VMEM((HALVES, 2, cells // HALVES // 2, ch), F32),
        pltpu.VMEM((2, 2, wide, ch), BF16),
        pltpu.VMEM((2, 2, wide, ch), BF16),
        pltpu.VMEM((2, wide, ch), BF16),
        pltpu.VMEM((2, wide, ch), BF16),
        field, field, field, field, field, field, field, field, field,
        pltpu.VMEM((total + 16, ch), F32),
        pltpu.VMEM((cells, ch), F32),
        pltpu.VMEM((4, n, 2 * wide + HALVES * packed, ch), BF16),
        pltpu.VMEM((n, rows + 3, wide, 3 * ch), BF16),
        pltpu.VMEM((2, n, 2, owners, piece, ch), F32),
        pltpu.VMEM((2, n, owners, piece, ch), BF16),
        pltpu.VMEM((2, n, owners, piece, ch), BF16),
        pltpu.VMEM((2, n, owners, piece, ch), BF16),
        pltpu.VMEM((2, n, chips, piece, ch), BF16),
        pltpu.VMEM((2, n, 2, owners, piece, ch), BF16),
        pltpu.VMEM((4, 8, ch), F32),
        pltpu.VMEM((4, s_count, 8, ch), F32),
        pltpu.VMEM((3, 2, wide, ch), F32),
        pltpu.VMEM((3, 2, wide, ch), F32),
        sem((2, n)),
        sem((2, n)), sem((2, n)),
        sem((2, n - 1, s_count)), sem((2, n - 1, s_count)),
        sem((2,)), sem((2,)),
        sem((2,)), sem((2,)),
        sem((4, 2, n, HALVES)), sem((4, n, HALVES)),
        sem((4, s_count)), sem((4, s_count)),
        sem((3, 2)), sem((3, 2)),
        sem((2, n)), sem((2, n)),
        sem((2, n, chips)), sem((2, n, chips)),
        sem((2, n, chips)), sem((2, n, chips)),
        sem((2, n)), sem((2, n)),
        sem((2, n)),
    ]
    block_out, input_grad, wg1, wg2, *sums = pl.pallas_call(
        functools.partial(block_kernel, n, s_count, rows, wide, ch, aligned, packed),
        out_shape=(
            jax.ShapeDtypeStruct((rows, ch * wide), BF16),
            jax.ShapeDtypeStruct((rows, ch * wide), F32),
            jax.ShapeDtypeStruct(grad_shape, BF16),
            jax.ShapeDtypeStruct(grad_shape, BF16),
            *[jax.ShapeDtypeStruct((1, ch), F32)] * 4,
        ),
        in_specs=[vmem] * 7 + [hbm] * 2,
        out_specs=(vmem, vmem, hbm, hbm, vmem, vmem, vmem, vmem),
        scratch_shapes=scratch,
        compiler_params=pltpu.CompilerParams(
            collective_id=0, has_side_effects=True, vmem_limit_bytes=60 * 1024 * 1024),
    )(blocks, cotangent, cell_live.T,
      *(v.reshape(1, ch) for v in (gain_one, shift_one, gain_two, shift_two)), weight_one, weight_two)

    if not aligned:
        def whole(grad):
            grad = grad.reshape(n, tap_rows, ch).transpose(1, 0, 2)
            return grad.astype(F32).reshape(9, ch, n * ch)
        return (block_out, input_grad, whole(wg1), whole(wg2), *(v.reshape(ch) for v in sums))

    wg1, wg2 = (w.reshape(tap_rows, n * ch) for w in (wg1, wg2))
    wide_grad = jax.ShapeDtypeStruct((tap_rows, n * ch), F32)
    moved = (block_out, input_grad, *sums)
    grad1, grad2, *moved = pl.pallas_call(
        functools.partial(finish_kernel, 2 + len(moved)),
        out_shape=(wide_grad, wide_grad, *(jax.ShapeDtypeStruct(v.shape, v.dtype) for v in moved)),
        in_specs=[pl.BlockSpec(memory_space=pl.ANY)] * (2 + len(moved)),
        out_specs=[pl.BlockSpec(memory_space=pl.ANY)] * (2 + len(moved)),
        scratch_shapes=[
            pltpu.VMEM((2, tap_rows, n * ch), BF16), pltpu.VMEM((2, tap_rows, n * ch), F32),
            sem((2, FINISH_PARTS)), sem((2, FINISH_PARTS)), sem((len(moved),)), sem((len(moved),)),
            *(pltpu.VMEM(v.shape, v.dtype) for v in moved),
        ],
        compiler_params=pltpu.CompilerParams(vmem_limit_bytes=64 * 1024 * 1024),
    )(wg1, wg2, *moved)
    block_out, input_grad, *sums = moved
    grads = (g.reshape(9, ch, n * ch) for g in (grad1, grad2))
    return (block_out, input_grad, *grads, *(v.reshape(ch) for v in sums))


def solution(mesh):
    return jax.shard_map(
        functools.partial(per_device, mesh.shape["chan"], mesh.shape["space"]),
        mesh=mesh,
        in_specs=(
            P("space", "chan"),
            P(None, "chan", None),
            P(None, "chan", None),
            P("chan"),
            P("chan"),
            P("chan"),
            P("chan"),
            P("space", None),
            P("space", "chan"),
        ),
        out_specs=(
            P("space", "chan"),
            P("space", "chan"),
            P(None, "chan", None),
            P(None, "chan", None),
            P("chan"),
            P("chan"),
            P("chan"),
            P("chan"),
        ),
        check_vma=False,
    )
```

```python
import functools
import math

import jax
import jax.numpy as jnp
from jax import lax
from jax.experimental import pallas as pl
from jax.experimental.pallas import tpu as pltpu
from jax.sharding import PartitionSpec as P

EPSILON = 1e-05
MESH = pl.DeviceIdType.MESH
F32 = jnp.float32
BF16 = jnp.bfloat16
ROOT_HALF = 0.7071067811865476
ROOT_TWO_PI = 0.3989422804014327
CHUNK = 64
FINISH_PARTS = 4
UNROLL = 2
HALVES = 2
LARGE, SMALL = 7, 3


def dot(a, b):
    return jnp.dot(a, b, preferred_element_type=F32)


def gelu_parts(v):
    upper = 0.5 * (1.0 + lax.erf(v * ROOT_HALF))
    slope = upper + v * (ROOT_TWO_PI * jnp.exp(-0.5 * v * v))
    return v * upper, slope


def most_live(rows, wide):
    units = (wide + 1) // (SMALL + 1)
    live_rows = rows - rows // (LARGE + 1)
    return min(rows * wide, math.ceil(units * live_rows * LARGE / 2))


def block_kernel(n, s_count, rows, wide, ch, aligned, packed, *refs):
    (x_in, cot_in, live_in, gain1_in, shift1_in, gain2_in, shift2_in, w1_hbm, w2_hbm) = refs[:9]
    (out_block, out_input, out_wg1, out_wg2, out_gain1, out_shift1, out_gain2, out_shift2) = refs[9:17]
    (turned, wv, wf, x_t, pack, unpack, places, edge_send, edge_recv, cot_send, cot_recv, cotm, mask, masked,
     normed1, normed2, through, slope1, hid, hid2, pad, acc, hold, taken,
     part, psend, crecv, hsend, qrecv, wout, st_send, st_recv, row_send, row_recv,
     w_sem, wz_ssem, wz_rsem, wp_ssem, wp_rsem, e_ssem, e_rsem, ce_ssem, ce_rsem, ag_ssem, ag_rsem,
     st_ssem, st_rsem, row_ssem, row_rsem, c_ssem, c_rsem, q_ssem, q_rsem,
     f_ssem, f_rsem, h_ssem, h_rsem, o_sem) = refs[17:]

    z = lax.axis_index("chan")
    s = lax.axis_index("space")
    cells = rows * wide
    total = cells + 2 * wide
    band = cells // HALVES
    core, chip, chips = s % 2, s // 2, s_count // 2
    before, after = (s + s_count - 1) % s_count, (s + 1) % s_count
    tap_rows = 9 * ch

    barrier = pltpu.get_barrier_semaphore()

    @pl.loop(1, s_count)
    def _(k):
        pl.semaphore_signal(barrier, inc=1, device_id=(z, (s + k) % s_count), device_id_type=MESH)

    @pl.loop(1, n)
    def _(k):
        pl.semaphore_signal(barrier, inc=1, device_id=((z + k) % n, s), device_id_type=MESH)

    w_copies = []
    for which, source in enumerate((w1_hbm, w2_hbm)):
        for d in range(n):
            block = source.at[:, d * ch:(d + 1) * ch] if aligned else source.at[d]
            w_copies.append(pltpu.make_async_copy(block, wv.at[which, d], w_sem.at[which, d]))
    for copy in w_copies:
        copy.start()

    def chunked(fn, init, first=0, count=cells):
        def step(i, carry):
            return fn(pl.multiple_of(first + i * CHUNK, CHUNK), CHUNK, carry)
        return lax.fori_loop(0, count // CHUNK, step, init, unroll=UNROLL)

    lanes = 128
    tiles = ch * wide // lanes

    def from_flat(flat, put):
        for i in range(tiles):
            turned[i * lanes:(i + 1) * lanes, 0:rows] = flat[:, i * lanes:(i + 1) * lanes].astype(F32).T
        for w in range(wide):
            put(pl.ds(w, rows, stride=wide), turned[pl.ds(w, ch, stride=wide), 0:rows].T)

    def to_flat(source, flat):
        for w in range(wide):
            turned[pl.ds(w, ch, stride=wide), 0:rows] = source[pl.ds(w, rows, stride=wide), :].T
        for i in range(tiles):
            flat[:, i * lanes:(i + 1) * lanes] = turned[i * lanes:(i + 1) * lanes, 0:rows].T.astype(flat.dtype)

    def put_masked(at, value):
        masked[at, :] = value

    from_flat(x_in, put_masked)

    cell = lax.broadcasted_iota(jnp.int32, (cells, rows), 0)
    pick = (cell // wide == lax.broadcasted_iota(jnp.int32, (cells, rows), 1)).astype(F32).astype(BF16)
    column_of = lax.broadcasted_iota(jnp.int32, (cells, wide), 0) % wide
    picked = lax.dot_general(pick, live_in[...].astype(BF16), (((1,), (1,)), ((), ())), preferred_element_type=F32)
    picked = jnp.where(column_of == lax.broadcasted_iota(jnp.int32, (cells, wide), 1), picked, 0.0)
    mask[0:cells, :] = dot(picked.astype(BF16), jnp.ones((wide, ch), BF16))

    def load_main(start, size, carry):
        at = pl.ds(start, size)
        lv = mask[at, :]
        masked[at, :] = masked[at, :] * lv
        return carry

    chunked(load_main, 0)
    for side, start in ((0, 0), (1, cells - wide)):
        edge_send[side, 0] = masked[start:start + wide, :].astype(BF16)
        edge_send[side, 1] = mask[start:start + wide, :].astype(BF16)

    acc[...] = jnp.zeros_like(acc)
    for block in range(n):
        for row in (rows // HALVES + 1, rows + 2):
            taken[block, row:row + 1, :, :] = jnp.zeros((1, wide, 3 * ch), BF16)
    st_send[...] = jnp.zeros_like(st_send)

    pl.semaphore_wait(barrier, s_count - 1 + n - 1)

    def edge_copy(side):
        return pltpu.make_async_remote_copy(
            src_ref=edge_send.at[side], dst_ref=edge_recv.at[1 - side],
            send_sem=e_ssem.at[side], recv_sem=e_rsem.at[1 - side],
            device_id=(z, before if side == 0 else after), device_id_type=MESH)

    for side in range(2):
        edge_copy(side).start()

    def cot_copy(side):
        return pltpu.make_async_remote_copy(
            src_ref=cot_send.at[side], dst_ref=cot_recv.at[1 - side],
            send_sem=ce_ssem.at[side], recv_sem=ce_rsem.at[1 - side],
            device_id=(z, before if side == 0 else after), device_id_type=MESH)

    def load_cotangent():
        def put(at, value):
            cotm[at, :] = value
        from_flat(cot_in, put)

        def live_only(start, size, carry):
            at = pl.ds(start, size)
            cotm[at, :] = cotm[at, :] * mask[at, :]
            return carry
        chunked(live_only, 0)
        for side, start in ((0, 0), (1, cells - wide)):
            cot_send[side] = cotm[start:start + wide, :].astype(BF16)
            cot_copy(side).start()

    def take_cotangent():
        for side in range(2):
            cot_copy(1 - side).wait_recv()
            at = slice(cells + side * wide, cells + (side + 1) * wide)
            cotm[at, :] = cot_recv[side].astype(F32) * mask[at, :]

    w_parts = math.gcd(tap_rows // 16, s_count)
    w_rows = tap_rows // w_parts
    w_mine = s % w_parts
    w_group = s - w_mine

    def wz_copy(which, k):
        at = pl.ds(w_mine * w_rows, w_rows)
        slot = n - k - 1
        return pltpu.make_async_remote_copy(
            src_ref=wv.at[which, (z + k) % n, at, :], dst_ref=wf.at[which, slot, at, :],
            send_sem=wz_ssem.at[which, slot], recv_sem=wz_rsem.at[which, slot],
            device_id=((z + k) % n, s), device_id_type=MESH)

    def wp_copy(which, slot, k, whose):
        at = pl.ds(whose * w_rows, w_rows)
        return pltpu.make_async_remote_copy(
            src_ref=wf.at[which, slot, at, :], dst_ref=wf.at[which, slot, at, :],
            send_sem=wp_ssem.at[which, slot, k], recv_sem=wp_rsem.at[which, slot, whose],
            device_id=(z, w_group + (w_mine + k) % w_parts), device_id_type=MESH)

    def weights_over_z(which):
        for copy in w_copies[which * n:(which + 1) * n]:
            copy.wait()

        @pl.loop(1, n)
        def _(k):
            wz_copy(which, k).start()

    def slot_of(block):
        return (block - z + n - 1) % n

    def weights_round(which):
        @pl.loop(1, n)
        def _(distance):
            for sign in (1, -1):
                block = z - distance * sign

                @pl.when((block >= 0) & (block < n))
                def _():
                    slot = slot_of(block)
                    wz_copy(which, n - 1 - slot).wait_recv()

                    @pl.loop(1, w_parts)
                    def _(k):
                        wp_copy(which, slot, k, w_mine).start()

    def weights_arrived(which, slot):
        @pl.loop(1, w_parts)
        def _(k):
            wp_copy(which, slot, k, (w_mine + k) % w_parts).wait_recv()

    def row_copy(slot, side):
        return pltpu.make_async_remote_copy(
            src_ref=row_send.at[slot, side], dst_ref=row_recv.at[slot, 1 - side],
            send_sem=row_ssem.at[slot, side], recv_sem=row_rsem.at[slot, 1 - side],
            device_id=(z, before if side == 0 else after), device_id_type=MESH)

    def send_rows(slot, ref):
        for side, start in ((0, 0), (1, cells - wide)):
            row_send[slot, side] = ref[start:start + wide, :]
            row_copy(slot, side).start()

    def take_rows(slot, ref):
        for side in range(2):
            row_copy(slot, 1 - side).wait_recv()
            ref[cells + side * wide:cells + (side + 1) * wide, :] = row_recv[slot, side]

    def st_copy(slot, k, whose):
        return pltpu.make_async_remote_copy(
            src_ref=st_send.at[slot], dst_ref=st_recv.at[slot, whose],
            send_sem=st_ssem.at[slot, k], recv_sem=st_rsem.at[slot, whose],
            device_id=(z, (s + k) % s_count), device_id_type=MESH)

    def send_stats(slot, values):
        for i, v in enumerate(values):
            st_send[slot, i:i + 1, :] = v
        for k in range(1, s_count):
            st_copy(slot, k, s).start()
        st_recv[slot, s] = st_send[slot]

    def take_stats(slot):
        for k in range(1, s_count):
            st_copy(slot, k, (s + k) % s_count).wait_recv()

    strip = 8
    column = lax.broadcasted_iota(jnp.int32, (strip * wide, ch), 0) % wide

    def shift(target, first, count):
        size = count * wide
        where = column[:size]
        here = pad[pl.ds(8 + first * wide, size), :]
        left = jnp.where(where == 0, 0.0, pad[pl.ds(7 + first * wide, size), :])
        right = jnp.where(where == wide - 1, 0.0, pad[pl.ds(9 + first * wide, size), :])
        for b, v in enumerate((left, here, right)):
            target[pl.ds(first, count), :, b * ch:(b + 1) * ch] = v.astype(BF16).reshape(count, wide, ch)

    edge = 2 * wide
    ag_rows = ((0, edge + packed), (edge + packed, packed))
    band_rows = rows // HALVES

    def unpack_half(ph, block, q, target):
        if q == 0:
            pad[8:8 + wide, :] = hold[ph, block, 0:wide, :].astype(F32)
            pad[8 + wide + cells:8 + 2 * wide + cells, :] = hold[ph, block, wide:edge, :].astype(F32)
            shift(target, 0, 1)
            shift(target, rows + 1, 1)
        for j in range(2):
            start = edge + q * packed + j * (packed - unpack.shape[3])
            at = 8 + wide + q * band + j * (band // 2)
            pad[at:at + band // 2, :] = dot(unpack[q, j], hold[ph, block, start:start + unpack.shape[3], :])

        for i in range(band_rows // strip):
            shift(target, 1 + q * band_rows + i * strip, strip)

    def add_conv(q, field, taps, turned_taps=None):
        first, last = (0, band_rows - 1) if q == 0 else (band_rows - 1, rows)
        count = last - first
        size = (count + 2) * wide
        lhs = jnp.concatenate([
            field[first + i:last + 2 + i, :, :].reshape(size, 3 * ch) for i in range(2)], axis=1)
        if turned_taps is None:
            none = jnp.zeros((3 * ch, ch), BF16)
            rhs = jnp.concatenate([
                jnp.concatenate([taps(0), taps(2)], axis=1), jnp.concatenate([taps(1), none], axis=1)], axis=0)
            value = dot(lhs, rhs)
        else:
            def row_taps(a):
                return [turned_taps(3 * (2 - a) + 2 - b) for b in range(3)]
            none = jnp.zeros((ch, 3 * ch), BF16)
            rhs = jnp.concatenate([
                jnp.concatenate(row_taps(0) + row_taps(1), axis=1), jnp.concatenate(row_taps(2) + [none], axis=1)], axis=0)
            value = lax.dot_general(lhs, rhs, (((1,), (1,)), ((), ())), preferred_element_type=F32)
        at = pl.ds(first * wide, count * wide)
        acc[at, :] = acc[at, :] + value[0:count * wide, 0:ch] + value[2 * wide:size, ch:2 * ch]

    def ag_copy(ph, block, q, sign):
        at = pl.ds(*ag_rows[q])
        return pltpu.make_async_remote_copy(
            src_ref=hold.at[ph, block, at, :], dst_ref=hold.at[ph, block, at, :],
            send_sem=ag_ssem.at[ph, (1 - sign) // 2, block, q], recv_sem=ag_rsem.at[ph, block, q],
            device_id=(z + sign, s), device_id_type=MESH)

    def pack_field(ph, source, fill=None, first=None):
        if fill is not None:
            fill(cells, edge, 0)
        hold[ph, z, 0:edge, :] = source[cells:cells + edge, :].astype(BF16)
        for q in range(HALVES):
            if first is not None:
                first(q)
            if fill is not None:
                chunked(fill, 0, q * band, band)
            hold[ph, z, edge + q * packed:edge + (q + 1) * packed, :] = dot(
                pack[q], source[q * band:(q + 1) * band, :].astype(BF16)).astype(BF16)
            for sign in (1, -1):
                @pl.when((z + sign >= 0) & (z + sign < n))
                def _():
                    ag_copy(ph, z, q, sign).start()

    def inside(slice_at):
        return (slice_at >= 0) & (slice_at < n)

    def take_and_pass(ph, k, q, sign, passes=True, takes=True):
        block = z - k * sign

        @pl.when((k > 0) & inside(block))
        def _():
            if passes and takes:
                ag_copy(ph, block, q, sign).wait_recv()

            @pl.when(inside(z + sign))
            def _():
                if passes:
                    if not takes:
                        ag_copy(ph, block, q, sign).wait_recv()
                    ag_copy(ph, block, q, sign).start()

            if not passes:
                @pl.when(jnp.logical_not(inside(z + sign)))
                def _():
                    ag_copy(ph, block, q, sign).wait_recv()

    near = jnp.where(z < n - n // 2, 1, 0)

    def consume_way(k, q, way, consume):
        block = z - k * (1 - 2 * way)

        @pl.when((k >= 0) & (k < n) & inside(block) & ((k > 0) | (way == near)))
        def _():
            consume(k, block, q)

    def take_both(ph, k, q, **how):
        @pl.loop(0, 2)
        def _(i):
            way = (near + i) % 2
            take_and_pass(ph, k, q, 1 - 2 * way, **how)

    def gather(ph, consume, each):
        @pl.loop(0, n)
        def _(k):
            for q in range(HALVES):
                take_both(ph, k, q)
                if q:
                    consume_way(k, q - 1, 1 - near, consume)
                else:
                    consume_way(k - 1, HALVES - 1, 1 - near, consume)
                consume_way(k, q, near, consume)
            each(k)

    def gather_passing_first(ph, consume, each):
        @pl.loop(0, n)
        def _(k):
            @pl.when(k == 1)
            def _():
                @pl.loop(1, n)
                def _(ahead):
                    for q in range(HALVES):
                        take_both(ph, ahead, q, takes=False)
            for q in range(HALVES):
                take_both(ph, k, q, passes=False)

                @pl.loop(0, 2)
                def _(i):
                    consume_way(k, q, (near + i) % 2, consume)
            each(k)

    last_pass = jnp.maximum(jnp.where(z < n - 1, z, 0), jnp.where(z > 0, n - 1 - z, 0))

    def forward(ph, field):
        def consume(k, block, q):
            into = taken.at[block]
            unpack_half(ph, block, q, into)

            @pl.when(k == 0)
            def _():
                add_conv(q, into, lambda a: wv[ph, z, 3 * a * ch:3 * (a + 1) * ch, :])

            @pl.when(k > 0)
            def _():
                slot = slot_of(block)
                if q == 0:
                    weights_arrived(ph, slot)
                add_conv(q, into, lambda a: wf[ph, slot, 3 * a * ch:3 * (a + 1) * ch, :])

        def each(k):
            pass
        (gather if ph else gather_passing_first)(ph, consume, each)

    def turn_field(ph, field):
        main = [field[start:start + ch, :].T for start in range(0, cells, ch)]
        ends = field[cells:cells + edge, :]
        if edge < ch:
            ends = jnp.concatenate([ends, jnp.zeros((ch - edge, ch), F32)], axis=0)
        ends = ends.T
        for i, here in enumerate(main):
            left = jnp.concatenate(
                [ends[:, 0:wide] if i == 0 else main[i - 1][:, ch - wide:], here[:, 0:ch - wide]], axis=1)
            right = jnp.concatenate(
                [here[:, wide:], main[i + 1][:, 0:wide] if i + 1 < len(main) else ends[:, wide:edge]], axis=1)
            for a, v in enumerate((left, here, right)):
                x_t[ph, a * ch:(a + 1) * ch, i * ch:(i + 1) * ch] = v.astype(BF16)

    half_rows = tap_rows // 2
    owners = math.gcd(half_rows // 16, chips)
    piece = half_rows // owners

    def c_copy(ph, j):
        return pltpu.make_async_remote_copy(
            src_ref=psend.at[ph, j], dst_ref=crecv.at[ph, j],
            send_sem=c_ssem.at[ph, j], recv_sem=c_rsem.at[ph, j],
            device_id=(z, chip * 2 + 1 - core), device_id_type=MESH)

    def q_copy(ph, j, e, whose, owner):
        return pltpu.make_async_remote_copy(
            src_ref=hsend.at[ph, j, owner], dst_ref=qrecv.at[ph, j, whose],
            send_sem=q_ssem.at[ph, j, e], recv_sem=q_rsem.at[ph, j, whose],
            device_id=(z, ((chip + e) % chips) * 2 + core), device_id_type=MESH)

    def f_copy(ph, j, e, owner):
        return pltpu.make_async_remote_copy(
            src_ref=wout.at[ph, j, core, owner], dst_ref=wout.at[ph, j, core, owner],
            send_sem=f_ssem.at[ph, j, e], recv_sem=f_rsem.at[ph, j, owner],
            device_id=(z, ((chip + e) % chips) * 2 + core), device_id_type=MESH)

    def h_copy(ph, j, whose):
        return pltpu.make_async_remote_copy(
            src_ref=wout.at[ph, j, whose], dst_ref=wout.at[ph, j, whose],
            send_sem=h_ssem.at[ph, j], recv_sem=h_rsem.at[ph, j],
            device_id=(z, chip * 2 + 1 - core), device_id_type=MESH)

    def o_copy(ph, j):
        target = (out_wg1, out_wg2)[ph]
        if aligned:
            target = target.at[:, :, :, pl.ds(pl.multiple_of(j * ch, ch), ch)]
        else:
            target = target.at[j]
        return pltpu.make_async_copy(wout.at[ph, j], target, o_sem.at[ph, j])

    def sum_cores(ph, j):
        for o in range(owners):
            psend[ph, j, o] = part[ph, j, 1 - core, o].astype(BF16)
        c_copy(ph, j).start()

    def sum_chips(ph, j):
        c_copy(ph, j).wait_recv()
        for o in range(owners):
            v = part[ph, j, core, o] + crecv[ph, j, o].astype(F32)
            part[ph, j, core, o] = v
            hsend[ph, j, o] = v.astype(BF16)

        @pl.loop(1, chips)
        def _(e):
            peer = (chip + e) % chips

            @pl.when(peer < owners)
            def _():
                q_copy(ph, j, e, chip, peer).start()

    def spread_chips(ph, j):
        @pl.when(chip < owners)
        def _():
            @pl.loop(1, chips)
            def _(e):
                q_copy(ph, j, e, (chip + e) % chips, chip).wait_recv()
            v = part[ph, j, core, chip]
            for e in range(1, chips):
                v = v + qrecv[ph, j, (chip + e) % chips].astype(F32)
            wout[ph, j, core, chip] = v.astype(BF16)

            @pl.loop(1, chips)
            def _(e):
                f_copy(ph, j, e, chip).start()

    def spread_cores(ph, j):
        @pl.loop(1, chips)
        def _(e):
            peer = (chip + e) % chips

            @pl.when(peer < owners)
            def _():
                f_copy(ph, j, e, peer).wait_recv()
        h_copy(ph, j, core).start()

    def finish(ph, j):
        h_copy(ph, j, 1 - core).wait_recv()
        o_copy(ph, j).start()

    def put_part(ph, j, tap, value):
        start = tap * ch
        done = 0
        while done < ch:
            row = start + done
            side, o, at = row // half_rows, row % half_rows // piece, row % piece
            size = min(ch - done, piece - at)
            part[ph, j, side, o, at:at + size, :] = value[done:done + size, :]
            done += size

    stages = (sum_cores, sum_chips, spread_chips, spread_cores, finish)

    def of_step(k, fn):
        @pl.loop(0, 2)
        def _(way):
            block = z - k * (1 - 2 * way)

            @pl.when((k >= 0) & (k < n) & inside(block) & ((k > 0) | (way == 0)))
            def _():
                fn(block)

    passing = last_pass > 0

    def made_at(step):
        first = jnp.where(passing & (step > 0), jnp.where(step == last_pass, 1, step + 1), step)
        return first, step + 1

    def advance(ph, k):
        for age in range(1, len(stages)):
            step = k - age

            @pl.when((step >= 0) & (step < n))
            def _():
                @pl.loop(*made_at(step))
                def _(made):
                    of_step(made, functools.partial(stages[age], ph))

    def advance_all(ph, age):
        @pl.loop(0, n)
        def _(j):
            stages[age](ph, j)

    def field_grad(ph, block):
        grad = taken[block, 1:rows + 1, :, :].reshape(cells, 3 * ch)
        value = dot(x_t[ph], grad)
        for a in range(3):
            for b in range(3):
                put_part(ph, block, 3 * a + b, value[a * ch:(a + 1) * ch, (2 - b) * ch:(3 - b) * ch])

    def make_grad(ph, block):
        field_grad(ph, block)
        sum_cores(ph, block)

    def backward(ph):
        last = ph == 0

        def consume(k, block, q):
            into = taken.at[block]
            unpack_half(2 + ph, block, q, into)
            if last and q == HALVES - 1:
                @pl.when((k == 0) | (k >= last_pass))
                def _():
                    make_grad(ph, block)
            add_conv(q, into, None, lambda t: wv[ph, block, t * ch:(t + 1) * ch, :])

        def each(k):
            first, end = made_at(k)
            if last:
                @pl.loop(first, end - 1)
                def _(step):
                    of_step(step, functools.partial(make_grad, ph))
                advance(ph, k)
                for age in range(2, len(stages)):
                    @pl.when(k == age - 2)
                    def _():
                        advance_all(1, age)
            else:
                @pl.loop(first, jnp.where(passing | (k < n - 2), end, first))
                def _(step):
                    of_step(step, functools.partial(make_grad, ph))
        gather(2 + ph, consume, each)

    def fold(v):
        return jnp.sum(v.reshape(v.shape[0] // 8, 8, ch), axis=0)

    def flatten(v):
        return jnp.sum(v, axis=0, keepdims=True)

    zero = jnp.zeros((8, ch), F32)

    def local_moments(ref):
        def sums(start, size, carry):
            at = pl.ds(start, size)
            m = mask[at, :]
            return carry[0] + fold(ref[at, :] * m), carry[1] + fold(m)
        added, number = (flatten(v) for v in chunked(sums, (zero, zero)))
        middle = added / jnp.maximum(number, 1.0)

        def spread(start, size, carry):
            at = pl.ds(start, size)
            c = (ref[at, :] - middle) * mask[at, :]
            return carry + fold(c * c)
        return added, number, flatten(chunked(spread, zero))

    def moments(slot):
        take_stats(slot)
        got = [st_recv[slot, k] for k in range(s_count)]
        added = sum(g[0:1] for g in got)
        number = sum(g[1:2] for g in got)
        mean = added / number
        spread = 0.0
        for g in got:
            off = g[0:1] / jnp.maximum(g[1:2], 1.0) - mean
            spread = spread + (g[2:3] + g[1:2] * off * off)
        return mean, lax.rsqrt(spread / number + EPSILON), number

    def everywhere(fn):
        chunked(fn, 0)
        fn(cells, 2 * wide, 0)

    gain1, shift1, gain2, shift2 = (r[...] for r in (gain1_in, shift1_in, gain2_in, shift2_in))

    weights_over_z(0)
    weights_over_z(1)

    quarter = band // 2
    kept = packed // 2
    window = unpack.shape[3]
    below = lax.broadcasted_iota(jnp.int32, (quarter, quarter), 1) < lax.broadcasted_iota(jnp.int32, (quarter, quarter), 0)
    below = below.astype(F32).astype(BF16)

    def make_pack(h):
        for j in range(2):
            lv = mask[h * band + j * quarter:h * band + (j + 1) * quarter, :]
            place = jnp.where(lv > 0.0, dot(below, lv.astype(BF16)) + j * kept, -1.0)
            places[h, j] = place
            across = place.T[0:1, :]
            spot = lax.broadcasted_iota(jnp.int32, (packed, quarter), 0).astype(F32)
            pack[h, :, j * quarter:(j + 1) * quarter] = jnp.where(spot == across, 1.0, 0.0).astype(BF16)

    def make_unpack(h):
        for j in range(2):
            for start in range(0, window, ch):
                size = min(ch, window - start)
                spot = start + j * (packed - window) + lax.broadcasted_iota(jnp.int32, (quarter, size), 1)
                unpack[h, j, :, start:start + size] = jnp.where(
                    places[h, j, :, :size] == spot.astype(F32), 1.0, 0.0).astype(BF16)

    for side in range(2):
        edge_copy(1 - side).wait_recv()
        there = jnp.where(s > 0, 1.0, 0.0) if side == 0 else jnp.where(s < s_count - 1, 1.0, 0.0)
        at = slice(cells + side * wide, cells + (side + 1) * wide)
        masked[at, :] = edge_recv[side, 0].astype(F32) * there
        mask[at, :] = edge_recv[side, 1].astype(F32) * there

    pack_field(0, masked, first=make_pack)
    weights_round(0)
    for h in range(HALVES):
        make_unpack(h)
    forward(0, masked)
    send_rows(0, acc)
    send_stats(0, local_moments(acc))
    weights_round(1)
    load_cotangent()
    mean1, scale1, count = moments(0)

    def activate_one(start, size, carry):
        at = pl.ds(start, size)
        main = start is not cells
        nv = ((acc if main else normed1)[at, :] - mean1) * scale1
        normed1[at, :] = nv
        hid[at, :] = gelu_parts(nv * gain1 + shift1)[0] * mask[at, :]
        if main:
            acc[at, :] = jnp.zeros((size, ch), F32)
        return carry

    def slope_one(start, size, carry):
        at = pl.ds(start, size)
        slope1[at, :] = gelu_parts(normed1[at, :] * gain1 + shift1)[1] * mask[at, :]
        return carry

    take_rows(0, normed1)
    pack_field(1, hid, activate_one)
    everywhere(slope_one)
    forward(1, hid)
    send_rows(1, acc)
    send_stats(1, local_moments(acc))
    turn_field(0, masked)
    turn_field(1, hid)
    mean2, scale2, _ = moments(1)

    def activate_two(source, start, size):
        at = pl.ds(start, size)
        nv = (source[at, :] - mean2) * scale2
        normed2[at, :] = nv
        value, slope = gelu_parts(nv * gain2 + shift2 + masked[at, :])
        t = cotm[at, :] * slope
        through[at, :] = t
        return value, nv, t

    def activate_main(start, size, carry):
        value, nv, t = activate_two(acc, start, size)
        at = pl.ds(start, size)
        hid2[at, :] = value * mask[at, :]
        acc[at, :] = jnp.zeros((size, ch), F32)
        return carry[0] + fold(t * nv), carry[1] + fold(t)

    send_stats(2, [flatten(v) for v in chunked(activate_main, (zero, zero))])
    take_rows(1, normed2)
    take_cotangent()
    activate_two(normed2, cells, edge)
    to_flat(hid2, out_block)

    def gradient_sums(slot):
        take_stats(slot)
        got = [st_recv[slot, k] for k in range(s_count)]
        return sum(g[0:1] for g in got), sum(g[1:2] for g in got)

    def norm_back(upstream, normed, gain, scale, sums):
        gain_grad, shift_grad = sums
        factor = gain * scale
        level, tilt = shift_grad / count, gain_grad / count

        def fill(start, size, carry):
            at = pl.ds(start, size)
            v = upstream[at, :] - mask[at, :] * (level + normed[at, :] * tilt)
            hid[at, :] = factor * v
            return carry
        return fill

    sums2 = gradient_sums(2)
    pack_field(3, hid, norm_back(through, normed2, gain2, scale2, sums2))
    backward(1)

    send_rows(2, acc)

    def inner_main(start, size, carry):
        at = pl.ds(start, size)
        v = acc[at, :] * slope1[at, :]
        slope1[at, :] = v
        acc[at, :] = jnp.zeros((size, ch), F32)
        return carry[0] + fold(v * normed1[at, :]), carry[1] + fold(v)

    send_stats(3, [flatten(v) for v in chunked(inner_main, (zero, zero))])

    @pl.when(jnp.logical_not(passing))
    def _():
        for step in range(n - 2, n):
            of_step(step, functools.partial(make_grad, 1))
    for side in range(2):
        row_copy(2, 1 - side).wait_recv()
        at = slice(cells + side * wide, cells + (side + 1) * wide)
        slope1[at, :] = row_recv[2, side] * slope1[at, :]
    sums1 = gradient_sums(3)
    pack_field(2, hid, norm_back(slope1, normed1, gain1, scale1, sums1))
    advance_all(1, 1)
    backward(0)
    advance(0, n)

    def finish_input(start, size, carry):
        at = pl.ds(start, size)
        acc[at, :] = (acc[at, :] + through[at, :]) * mask[at, :]
        return carry

    chunked(finish_input, 0)
    to_flat(acc, out_input)
    out_gain1[...], out_shift1[...] = sums1
    out_gain2[...], out_shift2[...] = sums2
    for extra in range(1, len(stages) - 1):
        advance(0, n + extra)

    for side in range(2):
        edge_copy(side).wait_send()
        cot_copy(side).wait_send()
        for slot in range(3):
            row_copy(slot, side).wait_send()

    @pl.loop(1, s_count)
    def _(k):
        for slot in range(4):
            st_copy(slot, k, s).wait_send()

    @pl.loop(1, n)
    def _(k):
        for which in range(2):
            wz_copy(which, k).wait_send()

    @pl.loop(1, w_parts)
    def _(k):
        for which in range(2):
            for slot in range(n - 1):
                wp_copy(which, slot, k, w_mine).wait_send()

    @pl.loop(0, n)
    def _(k):
        for sign in (1, -1):
            block = z - k * sign

            @pl.when((block >= 0) & (block < n) & (z + sign >= 0) & (z + sign < n))
            def _():
                for ph in range(4):
                    for q in range(HALVES):
                        ag_copy(ph, block, q, sign).wait_send()

    @pl.loop(0, n)
    def _(j):
        for ph in range(2):
            c_copy(ph, j).wait_send()
            h_copy(ph, j, core).wait_send()
            o_copy(ph, j).wait()

            @pl.loop(1, chips)
            def _(e):
                peer = (chip + e) % chips

                @pl.when(peer < owners)
                def _():
                    q_copy(ph, j, e, chip, peer).wait_send()

                @pl.when(chip < owners)
                def _():
                    f_copy(ph, j, e, chip).wait_send()


def finish_kernel(count, *refs):
    ins, outs = refs[:count], refs[count:2 * count]
    narrow, wide, in_sem, out_sem, take_sem, give_sem = refs[2 * count:2 * count + 6]
    held = refs[2 * count + 6:]
    rows = narrow.shape[1] // FINISH_PARTS
    parts = [(w, i, pl.ds(i * rows, rows)) for i in range(FINISH_PARTS) for w in range(2)]
    loads = [pltpu.make_async_copy(ins[w].at[at, :], narrow.at[w, at, :], in_sem.at[w, i]) for w, i, at in parts]
    stores = [pltpu.make_async_copy(wide.at[w, at, :], outs[w].at[at, :], out_sem.at[w, i]) for w, i, at in parts]
    takes = [pltpu.make_async_copy(ins[2 + k], v, take_sem.at[k]) for k, v in enumerate(held)]
    gives = [pltpu.make_async_copy(v, outs[2 + k], give_sem.at[k]) for k, v in enumerate(held)]
    for copy in loads + takes:
        copy.start()
    for load, store, (w, i, at) in zip(loads, stores, parts):
        load.wait()
        wide[w, at, :] = narrow[w, at, :].astype(F32)
        store.start()
    for take, give in zip(takes, gives):
        take.wait()
        give.start()
    for copy in stores + gives:
        copy.wait()


def per_device(n, s_count, blocks, weight_one, weight_two, gain_one, shift_one, gain_two, shift_two, cell_live, cotangent):
    rows, wide = cell_live.shape
    ch = blocks.shape[1] // wide
    cells = rows * wide
    total = cells + 2 * wide
    packed = 2 * -(-most_live(rows // HALVES // 2, wide) // 8) * 8
    aligned = ch % 128 == 0
    chips = s_count // 2
    tap_rows = 9 * ch
    half_rows = tap_rows // 2
    owners = math.gcd(half_rows // 16, chips)
    piece = half_rows // owners

    if aligned:
        weight_one, weight_two = (w.reshape(tap_rows, n * ch) for w in (weight_one, weight_two))
    else:
        weight_one, weight_two = (
            w.reshape(tap_rows, n, ch).transpose(1, 0, 2) for w in (weight_one, weight_two))
    grad_shape = (2, owners, piece, n * ch) if aligned else (n, 2, owners, piece, ch)
    vmem = pl.BlockSpec(memory_space=pltpu.VMEM)
    hbm = pl.BlockSpec(memory_space=pl.ANY)
    sem = pltpu.SemaphoreType.DMA
    field = pltpu.VMEM((total, ch), F32)
    scratch = [
        pltpu.VMEM((ch * wide, 128), F32),
        pltpu.VMEM((2, n, tap_rows, ch), BF16),
        pltpu.VMEM((2, n - 1, tap_rows, ch), BF16),
        pltpu.VMEM((2, 3 * ch, cells), BF16),
        pltpu.VMEM((HALVES, packed, cells // HALVES), BF16),
        pltpu.VMEM((HALVES, 2, cells // HALVES // 2, -(-packed // 2 // 16) * 16), BF16),
        pltpu.VMEM((HALVES, 2, cells // HALVES // 2, ch), F32),
        pltpu.VMEM((2, 2, wide, ch), BF16),
        pltpu.VMEM((2, 2, wide, ch), BF16),
        pltpu.VMEM((2, wide, ch), BF16),
        pltpu.VMEM((2, wide, ch), BF16),
        field, field, field, field, field, field, field, field, field,
        pltpu.VMEM((total + 16, ch), F32),
        pltpu.VMEM((cells, ch), F32),
        pltpu.VMEM((4, n, 2 * wide + HALVES * packed, ch), BF16),
        pltpu.VMEM((n, rows + 3, wide, 3 * ch), BF16),
        pltpu.VMEM((2, n, 2, owners, piece, ch), F32),
        pltpu.VMEM((2, n, owners, piece, ch), BF16),
        pltpu.VMEM((2, n, owners, piece, ch), BF16),
        pltpu.VMEM((2, n, owners, piece, ch), BF16),
        pltpu.VMEM((2, n, chips, piece, ch), BF16),
        pltpu.VMEM((2, n, 2, owners, piece, ch), BF16),
        pltpu.VMEM((4, 8, ch), F32),
        pltpu.VMEM((4, s_count, 8, ch), F32),
        pltpu.VMEM((3, 2, wide, ch), F32),
        pltpu.VMEM((3, 2, wide, ch), F32),
        sem((2, n)),
        sem((2, n)), sem((2, n)),
        sem((2, n - 1, s_count)), sem((2, n - 1, s_count)),
        sem((2,)), sem((2,)),
        sem((2,)), sem((2,)),
        sem((4, 2, n, HALVES)), sem((4, n, HALVES)),
        sem((4, s_count)), sem((4, s_count)),
        sem((3, 2)), sem((3, 2)),
        sem((2, n)), sem((2, n)),
        sem((2, n, chips)), sem((2, n, chips)),
        sem((2, n, chips)), sem((2, n, chips)),
        sem((2, n)), sem((2, n)),
        sem((2, n)),
    ]
    block_out, input_grad, wg1, wg2, *sums = pl.pallas_call(
        functools.partial(block_kernel, n, s_count, rows, wide, ch, aligned, packed),
        out_shape=(
            jax.ShapeDtypeStruct((rows, ch * wide), BF16),
            jax.ShapeDtypeStruct((rows, ch * wide), F32),
            jax.ShapeDtypeStruct(grad_shape, BF16),
            jax.ShapeDtypeStruct(grad_shape, BF16),
            *[jax.ShapeDtypeStruct((1, ch), F32)] * 4,
        ),
        in_specs=[vmem] * 7 + [hbm] * 2,
        out_specs=(vmem, vmem, hbm, hbm, vmem, vmem, vmem, vmem),
        scratch_shapes=scratch,
        compiler_params=pltpu.CompilerParams(
            collective_id=0, has_side_effects=True, vmem_limit_bytes=60 * 1024 * 1024),
    )(blocks, cotangent, cell_live.T,
      *(v.reshape(1, ch) for v in (gain_one, shift_one, gain_two, shift_two)), weight_one, weight_two)

    if not aligned:
        def whole(grad):
            grad = grad.reshape(n, tap_rows, ch).transpose(1, 0, 2)
            return grad.astype(F32).reshape(9, ch, n * ch)
        return (block_out, input_grad, whole(wg1), whole(wg2), *(v.reshape(ch) for v in sums))

    wg1, wg2 = (w.reshape(tap_rows, n * ch) for w in (wg1, wg2))
    wide_grad = jax.ShapeDtypeStruct((tap_rows, n * ch), F32)
    moved = (block_out, input_grad, *sums)
    grad1, grad2, *moved = pl.pallas_call(
        functools.partial(finish_kernel, 2 + len(moved)),
        out_shape=(wide_grad, wide_grad, *(jax.ShapeDtypeStruct(v.shape, v.dtype) for v in moved)),
        in_specs=[pl.BlockSpec(memory_space=pl.ANY)] * (2 + len(moved)),
        out_specs=[pl.BlockSpec(memory_space=pl.ANY)] * (2 + len(moved)),
        scratch_shapes=[
            pltpu.VMEM((2, tap_rows, n * ch), BF16), pltpu.VMEM((2, tap_rows, n * ch), F32),
            sem((2, FINISH_PARTS)), sem((2, FINISH_PARTS)), sem((len(moved),)), sem((len(moved),)),
            *(pltpu.VMEM(v.shape, v.dtype) for v in moved),
        ],
        compiler_params=pltpu.CompilerParams(vmem_limit_bytes=64 * 1024 * 1024),
    )(wg1, wg2, *moved)
    block_out, input_grad, *sums = moved
    grads = (g.reshape(9, ch, n * ch) for g in (grad1, grad2))
    return (block_out, input_grad, *grads, *(v.reshape(ch) for v in sums))


def solution(mesh):
    return jax.shard_map(
        functools.partial(per_device, mesh.shape["chan"], mesh.shape["space"]),
        mesh=mesh,
        in_specs=(
            P("space", "chan"),
            P(None, "chan", None),
            P(None, "chan", None),
            P("chan"),
            P("chan"),
            P("chan"),
            P("chan"),
            P("space", None),
            P("space", "chan"),
        ),
        out_specs=(
            P("space", "chan"),
            P("space", "chan"),
            P(None, "chan", None),
            P(None, "chan", None),
            P("chan"),
            P("chan"),
            P("chan"),
            P("chan"),
        ),
        check_vma=False,
    )
```

```python
import functools
import math

import jax
import jax.numpy as jnp
from jax import lax
from jax.experimental import pallas as pl
from jax.experimental.pallas import tpu as pltpu
from jax.sharding import PartitionSpec as P

EPSILON = 1e-05
MESH = pl.DeviceIdType.MESH
F32 = jnp.float32
BF16 = jnp.bfloat16
ROOT_HALF = 0.7071067811865476
ROOT_TWO_PI = 0.3989422804014327
CHUNK = 64
FINISH_PARTS = 4
UNROLL = 2
HALVES = 2
LARGE, SMALL = 7, 3


def dot(a, b):
    return jnp.dot(a, b, preferred_element_type=F32)


def gelu_parts(v):
    upper = 0.5 * (1.0 + lax.erf(v * ROOT_HALF))
    slope = upper + v * (ROOT_TWO_PI * jnp.exp(-0.5 * v * v))
    return v * upper, slope


def most_live(rows, wide):
    units = (wide + 1) // (SMALL + 1)
    live_rows = rows - rows // (LARGE + 1)
    return min(rows * wide, math.ceil(units * live_rows * LARGE / 2))


def block_kernel(n, s_count, rows, wide, ch, aligned, packed, *refs):
    (x_in, cot_in, live_in, gain1_in, shift1_in, gain2_in, shift2_in, w1_hbm, w2_hbm) = refs[:9]
    (out_block, out_input, out_wg1, out_wg2, out_gain1, out_shift1, out_gain2, out_shift2) = refs[9:17]
    (turned, wv, wf, x_t, pack, unpack, places, edge_send, edge_recv, cot_send, cot_recv, cotm, mask, masked,
     normed1, normed2, through, slope1, hid, hid2, pad, acc, hold, taken,
     part, psend, crecv, hsend, qrecv, wout, st_send, st_recv, row_send, row_recv,
     w_sem, wz_ssem, wz_rsem, wp_ssem, wp_rsem, e_ssem, e_rsem, ce_ssem, ce_rsem, ag_ssem, ag_rsem,
     st_ssem, st_rsem, row_ssem, row_rsem, c_ssem, c_rsem, q_ssem, q_rsem,
     f_ssem, f_rsem, h_ssem, h_rsem, o_sem) = refs[17:]

    z = lax.axis_index("chan")
    s = lax.axis_index("space")
    cells = rows * wide
    total = cells + 2 * wide
    band = cells // HALVES
    core, chip, chips = s % 2, s // 2, s_count // 2
    before, after = (s + s_count - 1) % s_count, (s + 1) % s_count
    tap_rows = 9 * ch

    barrier = pltpu.get_barrier_semaphore()

    @pl.loop(1, s_count)
    def _(k):
        pl.semaphore_signal(barrier, inc=1, device_id=(z, (s + k) % s_count), device_id_type=MESH)

    @pl.loop(1, n)
    def _(k):
        pl.semaphore_signal(barrier, inc=1, device_id=((z + k) % n, s), device_id_type=MESH)

    w_copies = []
    for which, source in enumerate((w1_hbm, w2_hbm)):
        for d in range(n):
            block = source.at[:, d * ch:(d + 1) * ch] if aligned else source.at[d]
            w_copies.append(pltpu.make_async_copy(block, wv.at[which, d], w_sem.at[which, d]))
    for copy in w_copies:
        copy.start()

    def chunked(fn, init, first=0, count=cells):
        def step(i, carry):
            return fn(pl.multiple_of(first + i * CHUNK, CHUNK), CHUNK, carry)
        return lax.fori_loop(0, count // CHUNK, step, init, unroll=UNROLL)

    lanes = 128
    tiles = ch * wide // lanes

    def from_flat(flat, put):
        for i in range(tiles):
            turned[i * lanes:(i + 1) * lanes, 0:rows] = flat[:, i * lanes:(i + 1) * lanes].astype(F32).T
        for w in range(wide):
            put(pl.ds(w, rows, stride=wide), turned[pl.ds(w, ch, stride=wide), 0:rows].T)

    def to_flat(source, flat):
        for w in range(wide):
            turned[pl.ds(w, ch, stride=wide), 0:rows] = source[pl.ds(w, rows, stride=wide), :].T
        for i in range(tiles):
            flat[:, i * lanes:(i + 1) * lanes] = turned[i * lanes:(i + 1) * lanes, 0:rows].T.astype(flat.dtype)

    def put_masked(at, value):
        masked[at, :] = value

    from_flat(x_in, put_masked)

    cell = lax.broadcasted_iota(jnp.int32, (cells, rows), 0)
    pick = (cell // wide == lax.broadcasted_iota(jnp.int32, (cells, rows), 1)).astype(F32).astype(BF16)
    column_of = lax.broadcasted_iota(jnp.int32, (cells, wide), 0) % wide
    picked = lax.dot_general(pick, live_in[...].astype(BF16), (((1,), (1,)), ((), ())), preferred_element_type=F32)
    picked = jnp.where(column_of == lax.broadcasted_iota(jnp.int32, (cells, wide), 1), picked, 0.0)
    mask[0:cells, :] = dot(picked.astype(BF16), jnp.ones((wide, ch), BF16))

    def load_main(start, size, carry):
        at = pl.ds(start, size)
        lv = mask[at, :]
        masked[at, :] = masked[at, :] * lv
        return carry

    chunked(load_main, 0)
    for side, start in ((0, 0), (1, cells - wide)):
        edge_send[side, 0] = masked[start:start + wide, :].astype(BF16)
        edge_send[side, 1] = mask[start:start + wide, :].astype(BF16)

    acc[...] = jnp.zeros_like(acc)
    for block in range(n):
        for row in (rows // HALVES + 1, rows + 2):
            taken[block, row:row + 1, :, :] = jnp.zeros((1, wide, 3 * ch), BF16)
    st_send[...] = jnp.zeros_like(st_send)

    pl.semaphore_wait(barrier, s_count - 1 + n - 1)

    def edge_copy(side):
        return pltpu.make_async_remote_copy(
            src_ref=edge_send.at[side], dst_ref=edge_recv.at[1 - side],
            send_sem=e_ssem.at[side], recv_sem=e_rsem.at[1 - side],
            device_id=(z, before if side == 0 else after), device_id_type=MESH)

    for side in range(2):
        edge_copy(side).start()

    def cot_copy(side):
        return pltpu.make_async_remote_copy(
            src_ref=cot_send.at[side], dst_ref=cot_recv.at[1 - side],
            send_sem=ce_ssem.at[side], recv_sem=ce_rsem.at[1 - side],
            device_id=(z, before if side == 0 else after), device_id_type=MESH)

    def load_cotangent():
        def put(at, value):
            cotm[at, :] = value
        from_flat(cot_in, put)

        def live_only(start, size, carry):
            at = pl.ds(start, size)
            cotm[at, :] = cotm[at, :] * mask[at, :]
            return carry
        chunked(live_only, 0)
        for side, start in ((0, 0), (1, cells - wide)):
            cot_send[side] = cotm[start:start + wide, :].astype(BF16)
            cot_copy(side).start()

    def take_cotangent():
        for side in range(2):
            cot_copy(1 - side).wait_recv()
            at = slice(cells + side * wide, cells + (side + 1) * wide)
            cotm[at, :] = cot_recv[side].astype(F32) * mask[at, :]

    w_parts = math.gcd(tap_rows // 16, s_count)
    w_rows = tap_rows // w_parts
    w_mine = s % w_parts
    w_group = s - w_mine

    def wz_copy(which, k):
        at = pl.ds(w_mine * w_rows, w_rows)
        slot = n - k - 1
        return pltpu.make_async_remote_copy(
            src_ref=wv.at[which, (z + k) % n, at, :], dst_ref=wf.at[which, slot, at, :],
            send_sem=wz_ssem.at[which, slot], recv_sem=wz_rsem.at[which, slot],
            device_id=((z + k) % n, s), device_id_type=MESH)

    def wp_copy(which, slot, k, whose):
        at = pl.ds(whose * w_rows, w_rows)
        return pltpu.make_async_remote_copy(
            src_ref=wf.at[which, slot, at, :], dst_ref=wf.at[which, slot, at, :],
            send_sem=wp_ssem.at[which, slot, k], recv_sem=wp_rsem.at[which, slot, whose],
            device_id=(z, w_group + (w_mine + k) % w_parts), device_id_type=MESH)

    def weights_over_z(which):
        for copy in w_copies[which * n:(which + 1) * n]:
            copy.wait()

        @pl.loop(1, n)
        def _(k):
            wz_copy(which, k).start()

    def slot_of(block):
        return (block - z + n - 1) % n

    def weights_round(which):
        @pl.loop(1, n)
        def _(distance):
            for sign in (1, -1):
                block = z - distance * sign

                @pl.when((block >= 0) & (block < n))
                def _():
                    slot = slot_of(block)
                    wz_copy(which, n - 1 - slot).wait_recv()

                    @pl.loop(1, w_parts)
                    def _(k):
                        wp_copy(which, slot, k, w_mine).start()

    def weights_arrived(which, slot):
        @pl.loop(1, w_parts)
        def _(k):
            wp_copy(which, slot, k, (w_mine + k) % w_parts).wait_recv()

    def row_copy(slot, side):
        return pltpu.make_async_remote_copy(
            src_ref=row_send.at[slot, side], dst_ref=row_recv.at[slot, 1 - side],
            send_sem=row_ssem.at[slot, side], recv_sem=row_rsem.at[slot, 1 - side],
            device_id=(z, before if side == 0 else after), device_id_type=MESH)

    def send_rows(slot, ref):
        for side, start in ((0, 0), (1, cells - wide)):
            row_send[slot, side] = ref[start:start + wide, :]
            row_copy(slot, side).start()

    def take_rows(slot, ref):
        for side in range(2):
            row_copy(slot, 1 - side).wait_recv()
            ref[cells + side * wide:cells + (side + 1) * wide, :] = row_recv[slot, side]

    def st_copy(slot, k, whose):
        return pltpu.make_async_remote_copy(
            src_ref=st_send.at[slot], dst_ref=st_recv.at[slot, whose],
            send_sem=st_ssem.at[slot, k], recv_sem=st_rsem.at[slot, whose],
            device_id=(z, (s + k) % s_count), device_id_type=MESH)

    def send_stats(slot, values):
        for i, v in enumerate(values):
            st_send[slot, i:i + 1, :] = v
        for k in range(1, s_count):
            st_copy(slot, k, s).start()
        st_recv[slot, s] = st_send[slot]

    def take_stats(slot):
        for k in range(1, s_count):
            st_copy(slot, k, (s + k) % s_count).wait_recv()

    strip = 8
    column = lax.broadcasted_iota(jnp.int32, (strip * wide, ch), 0) % wide

    def shift(target, first, count):
        size = count * wide
        where = column[:size]
        here = pad[pl.ds(8 + first * wide, size), :]
        left = jnp.where(where == 0, 0.0, pad[pl.ds(7 + first * wide, size), :])
        right = jnp.where(where == wide - 1, 0.0, pad[pl.ds(9 + first * wide, size), :])
        for b, v in enumerate((left, here, right)):
            target[pl.ds(first, count), :, b * ch:(b + 1) * ch] = v.astype(BF16).reshape(count, wide, ch)

    edge = 2 * wide
    ag_rows = ((0, edge + packed), (edge + packed, packed))
    band_rows = rows // HALVES

    def unpack_half(ph, block, q, target):
        if q == 0:
            pad[8:8 + wide, :] = hold[ph, block, 0:wide, :].astype(F32)
            pad[8 + wide + cells:8 + 2 * wide + cells, :] = hold[ph, block, wide:edge, :].astype(F32)
            shift(target, 0, 1)
            shift(target, rows + 1, 1)
        for j in range(2):
            start = edge + q * packed + j * (packed - unpack.shape[3])
            at = 8 + wide + q * band + j * (band // 2)
            pad[at:at + band // 2, :] = dot(unpack[q, j], hold[ph, block, start:start + unpack.shape[3], :])

        for i in range(band_rows // strip):
            shift(target, 1 + q * band_rows + i * strip, strip)

    def add_conv(q, field, taps, turned_taps=None):
        first, last = (0, band_rows - 1) if q == 0 else (band_rows - 1, rows)
        count = last - first
        size = (count + 2) * wide
        lhs = jnp.concatenate([
            field[first + i:last + 2 + i, :, :].reshape(size, 3 * ch) for i in range(2)], axis=1)
        if turned_taps is None:
            none = jnp.zeros((3 * ch, ch), BF16)
            rhs = jnp.concatenate([
                jnp.concatenate([taps(0), taps(2)], axis=1), jnp.concatenate([taps(1), none], axis=1)], axis=0)
            value = dot(lhs, rhs)
        else:
            def row_taps(a):
                return [turned_taps(3 * (2 - a) + 2 - b) for b in range(3)]
            none = jnp.zeros((ch, 3 * ch), BF16)
            rhs = jnp.concatenate([
                jnp.concatenate(row_taps(0) + row_taps(1), axis=1), jnp.concatenate(row_taps(2) + [none], axis=1)], axis=0)
            value = lax.dot_general(lhs, rhs, (((1,), (1,)), ((), ())), preferred_element_type=F32)
        at = pl.ds(first * wide, count * wide)
        acc[at, :] = acc[at, :] + value[0:count * wide, 0:ch] + value[2 * wide:size, ch:2 * ch]

    def ag_copy(ph, block, q, sign):
        at = pl.ds(*ag_rows[q])
        return pltpu.make_async_remote_copy(
            src_ref=hold.at[ph, block, at, :], dst_ref=hold.at[ph, block, at, :],
            send_sem=ag_ssem.at[ph, (1 - sign) // 2, block, q], recv_sem=ag_rsem.at[ph, block, q],
            device_id=(z + sign, s), device_id_type=MESH)

    def pack_field(ph, source, fill=None, first=None):
        if fill is not None:
            fill(cells, edge, 0)
        hold[ph, z, 0:edge, :] = source[cells:cells + edge, :].astype(BF16)
        for q in range(HALVES):
            if first is not None:
                first(q)
            if fill is not None:
                chunked(fill, 0, q * band, band)
            hold[ph, z, edge + q * packed:edge + (q + 1) * packed, :] = dot(
                pack[q], source[q * band:(q + 1) * band, :].astype(BF16)).astype(BF16)
            for sign in (1, -1):
                @pl.when((z + sign >= 0) & (z + sign < n))
                def _():
                    ag_copy(ph, z, q, sign).start()

    def inside(slice_at):
        return (slice_at >= 0) & (slice_at < n)

    def take_and_pass(ph, k, q, sign, passes=True, takes=True):
        block = z - k * sign

        @pl.when((k > 0) & inside(block))
        def _():
            if passes and takes:
                ag_copy(ph, block, q, sign).wait_recv()

            @pl.when(inside(z + sign))
            def _():
                if passes:
                    if not takes:
                        ag_copy(ph, block, q, sign).wait_recv()
                    ag_copy(ph, block, q, sign).start()

            if not passes:
                @pl.when(jnp.logical_not(inside(z + sign)))
                def _():
                    ag_copy(ph, block, q, sign).wait_recv()

    near = jnp.where(z < n - n // 2, 1, 0)

    def consume_way(k, q, way, consume):
        block = z - k * (1 - 2 * way)

        @pl.when((k >= 0) & (k < n) & inside(block) & ((k > 0) | (way == near)))
        def _():
            consume(k, block, q)

    def take_both(ph, k, q, **how):
        @pl.loop(0, 2)
        def _(i):
            way = (near + i) % 2
            take_and_pass(ph, k, q, 1 - 2 * way, **how)

    def gather(ph, consume, each):
        @pl.loop(0, n)
        def _(k):
            for q in range(HALVES):
                take_both(ph, k, q)
                if q:
                    consume_way(k, q - 1, 1 - near, consume)
                else:
                    consume_way(k - 1, HALVES - 1, 1 - near, consume)
                consume_way(k, q, near, consume)
            each(k)

    def gather_passing_first(ph, consume, each):
        @pl.loop(0, n)
        def _(k):
            @pl.when(k == 1)
            def _():
                @pl.loop(1, n)
                def _(ahead):
                    for q in range(HALVES):
                        take_both(ph, ahead, q, takes=False)
            for q in range(HALVES):
                take_both(ph, k, q, passes=False)

                @pl.loop(0, 2)
                def _(i):
                    consume_way(k, q, (near + i) % 2, consume)
            each(k)

    last_pass = jnp.maximum(jnp.where(z < n - 1, z, 0), jnp.where(z > 0, n - 1 - z, 0))

    def forward(ph, field):
        def consume(k, block, q):
            into = taken.at[block]
            unpack_half(ph, block, q, into)

            @pl.when(k == 0)
            def _():
                add_conv(q, into, lambda a: wv[ph, z, 3 * a * ch:3 * (a + 1) * ch, :])

            @pl.when(k > 0)
            def _():
                slot = slot_of(block)
                if q == 0:
                    weights_arrived(ph, slot)
                add_conv(q, into, lambda a: wf[ph, slot, 3 * a * ch:3 * (a + 1) * ch, :])

        def each(k):
            if ph == 0:
                @pl.when(k == 0)
                def _():
                    weights_round(0)

                @pl.when(k == 1)
                def _():
                    weights_over_z(1)
        (gather if ph else gather_passing_first)(ph, consume, each)

    def turn_field(ph, field):
        main = [field[start:start + ch, :].T for start in range(0, cells, ch)]
        ends = field[cells:cells + edge, :]
        if edge < ch:
            ends = jnp.concatenate([ends, jnp.zeros((ch - edge, ch), F32)], axis=0)
        ends = ends.T
        for i, here in enumerate(main):
            left = jnp.concatenate(
                [ends[:, 0:wide] if i == 0 else main[i - 1][:, ch - wide:], here[:, 0:ch - wide]], axis=1)
            right = jnp.concatenate(
                [here[:, wide:], main[i + 1][:, 0:wide] if i + 1 < len(main) else ends[:, wide:edge]], axis=1)
            for a, v in enumerate((left, here, right)):
                x_t[ph, a * ch:(a + 1) * ch, i * ch:(i + 1) * ch] = v.astype(BF16)

    half_rows = tap_rows // 2
    owners = math.gcd(half_rows // 16, chips)
    piece = half_rows // owners

    def c_copy(ph, j):
        return pltpu.make_async_remote_copy(
            src_ref=psend.at[ph, j], dst_ref=crecv.at[ph, j],
            send_sem=c_ssem.at[ph, j], recv_sem=c_rsem.at[ph, j],
            device_id=(z, chip * 2 + 1 - core), device_id_type=MESH)

    def q_copy(ph, j, e, whose, owner):
        return pltpu.make_async_remote_copy(
            src_ref=hsend.at[ph, j, owner], dst_ref=qrecv.at[ph, j, whose],
            send_sem=q_ssem.at[ph, j, e], recv_sem=q_rsem.at[ph, j, whose],
            device_id=(z, ((chip + e) % chips) * 2 + core), device_id_type=MESH)

    def f_copy(ph, j, e, owner):
        return pltpu.make_async_remote_copy(
            src_ref=wout.at[ph, j, core, owner], dst_ref=wout.at[ph, j, core, owner],
            send_sem=f_ssem.at[ph, j, e], recv_sem=f_rsem.at[ph, j, owner],
            device_id=(z, ((chip + e) % chips) * 2 + core), device_id_type=MESH)

    def h_copy(ph, j, whose):
        return pltpu.make_async_remote_copy(
            src_ref=wout.at[ph, j, whose], dst_ref=wout.at[ph, j, whose],
            send_sem=h_ssem.at[ph, j], recv_sem=h_rsem.at[ph, j],
            device_id=(z, chip * 2 + 1 - core), device_id_type=MESH)

    def o_copy(ph, j):
        target = (out_wg1, out_wg2)[ph]
        if aligned:
            target = target.at[:, :, :, pl.ds(pl.multiple_of(j * ch, ch), ch)]
        else:
            target = target.at[j]
        return pltpu.make_async_copy(wout.at[ph, j], target, o_sem.at[ph, j])

    def sum_cores(ph, j):
        for o in range(owners):
            psend[ph, j, o] = part[ph, j, 1 - core, o].astype(BF16)
        c_copy(ph, j).start()

    def sum_chips(ph, j):
        c_copy(ph, j).wait_recv()
        for o in range(owners):
            v = part[ph, j, core, o] + crecv[ph, j, o].astype(F32)
            part[ph, j, core, o] = v
            hsend[ph, j, o] = v.astype(BF16)

        @pl.loop(1, chips)
        def _(e):
            peer = (chip + e) % chips

            @pl.when(peer < owners)
            def _():
                q_copy(ph, j, e, chip, peer).start()

    def spread_chips(ph, j):
        @pl.when(chip < owners)
        def _():
            @pl.loop(1, chips)
            def _(e):
                q_copy(ph, j, e, (chip + e) % chips, chip).wait_recv()
            v = part[ph, j, core, chip]
            for e in range(1, chips):
                v = v + qrecv[ph, j, (chip + e) % chips].astype(F32)
            wout[ph, j, core, chip] = v.astype(BF16)

            @pl.loop(1, chips)
            def _(e):
                f_copy(ph, j, e, chip).start()

    def spread_cores(ph, j):
        @pl.loop(1, chips)
        def _(e):
            peer = (chip + e) % chips

            @pl.when(peer < owners)
            def _():
                f_copy(ph, j, e, peer).wait_recv()
        h_copy(ph, j, core).start()

    def finish(ph, j):
        h_copy(ph, j, 1 - core).wait_recv()
        o_copy(ph, j).start()

    def put_part(ph, j, tap, value):
        start = tap * ch
        done = 0
        while done < ch:
            row = start + done
            side, o, at = row // half_rows, row % half_rows // piece, row % piece
            size = min(ch - done, piece - at)
            part[ph, j, side, o, at:at + size, :] = value[done:done + size, :]
            done += size

    stages = (sum_cores, sum_chips, spread_chips, spread_cores, finish)

    def of_step(k, fn):
        @pl.loop(0, 2)
        def _(way):
            block = z - k * (1 - 2 * way)

            @pl.when((k >= 0) & (k < n) & inside(block) & ((k > 0) | (way == 0)))
            def _():
                fn(block)

    passing = last_pass > 0

    def made_at(step):
        first = jnp.where(passing & (step > 0), jnp.where(step == last_pass, 1, step + 1), step)
        return first, step + 1

    def advance(ph, k):
        for age in range(1, len(stages)):
            step = k - age

            @pl.when((step >= 0) & (step < n))
            def _():
                @pl.loop(*made_at(step))
                def _(made):
                    of_step(made, functools.partial(stages[age], ph))

    def field_grad(ph, block):
        grad = taken[block, 1:rows + 1, :, :].reshape(cells, 3 * ch)
        value = dot(x_t[ph], grad)
        for a in range(3):
            for b in range(3):
                put_part(ph, block, 3 * a + b, value[a * ch:(a + 1) * ch, (2 - b) * ch:(3 - b) * ch])

    def make_grad(ph, block):
        field_grad(ph, block)
        sum_cores(ph, block)

    def backward(ph):
        last = ph == 0

        def consume(k, block, q):
            into = taken.at[block]
            unpack_half(2 + ph, block, q, into)
            if last and q == HALVES - 1:
                @pl.when((k == 0) | (k >= last_pass))
                def _():
                    make_grad(ph, block)
            add_conv(q, into, None, lambda t: wv[ph, block, t * ch:(t + 1) * ch, :])

        def each(k):
            first, end = made_at(k)
            if last:
                @pl.loop(first, end - 1)
                def _(step):
                    of_step(step, functools.partial(make_grad, ph))
                advance(ph, k)
                for extra in range(1, len(stages) - 1):
                    @pl.when(k == extra - 1)
                    def _():
                        advance(1, n + extra)
            else:
                @pl.loop(first, jnp.where(passing | (k < n - 1), end, first))
                def _(step):
                    of_step(step, functools.partial(make_grad, ph))
                advance(ph, k)
        gather(2 + ph, consume, each)

    def fold(v):
        return jnp.sum(v.reshape(v.shape[0] // 8, 8, ch), axis=0)

    def flatten(v):
        return jnp.sum(v, axis=0, keepdims=True)

    zero = jnp.zeros((8, ch), F32)

    def local_moments(ref):
        def sums(start, size, carry):
            at = pl.ds(start, size)
            m = mask[at, :]
            return carry[0] + fold(ref[at, :] * m), carry[1] + fold(m)
        added, number = (flatten(v) for v in chunked(sums, (zero, zero)))
        middle = added / jnp.maximum(number, 1.0)

        def spread(start, size, carry):
            at = pl.ds(start, size)
            c = (ref[at, :] - middle) * mask[at, :]
            return carry + fold(c * c)
        return added, number, flatten(chunked(spread, zero))

    def moments(slot):
        take_stats(slot)
        got = [st_recv[slot, k] for k in range(s_count)]
        added = sum(g[0:1] for g in got)
        number = sum(g[1:2] for g in got)
        mean = added / number
        spread = 0.0
        for g in got:
            off = g[0:1] / jnp.maximum(g[1:2], 1.0) - mean
            spread = spread + (g[2:3] + g[1:2] * off * off)
        return mean, lax.rsqrt(spread / number + EPSILON), number

    def everywhere(fn):
        chunked(fn, 0)
        fn(cells, 2 * wide, 0)

    gain1, shift1, gain2, shift2 = (r[...] for r in (gain1_in, shift1_in, gain2_in, shift2_in))

    weights_over_z(0)

    quarter = band // 2
    kept = packed // 2
    window = unpack.shape[3]
    below = lax.broadcasted_iota(jnp.int32, (quarter, quarter), 1) < lax.broadcasted_iota(jnp.int32, (quarter, quarter), 0)
    below = below.astype(F32).astype(BF16)

    def make_pack(h):
        for j in range(2):
            lv = mask[h * band + j * quarter:h * band + (j + 1) * quarter, :]
            place = jnp.where(lv > 0.0, dot(below, lv.astype(BF16)) + j * kept, -1.0)
            places[h, j] = place
            across = place.T[0:1, :]
            spot = lax.broadcasted_iota(jnp.int32, (packed, quarter), 0).astype(F32)
            pack[h, :, j * quarter:(j + 1) * quarter] = jnp.where(spot == across, 1.0, 0.0).astype(BF16)

    def make_unpack(h):
        for j in range(2):
            for start in range(0, window, ch):
                size = min(ch, window - start)
                spot = start + j * (packed - window) + lax.broadcasted_iota(jnp.int32, (quarter, size), 1)
                unpack[h, j, :, start:start + size] = jnp.where(
                    places[h, j, :, :size] == spot.astype(F32), 1.0, 0.0).astype(BF16)

    for side in range(2):
        edge_copy(1 - side).wait_recv()
        there = jnp.where(s > 0, 1.0, 0.0) if side == 0 else jnp.where(s < s_count - 1, 1.0, 0.0)
        at = slice(cells + side * wide, cells + (side + 1) * wide)
        masked[at, :] = edge_recv[side, 0].astype(F32) * there
        mask[at, :] = edge_recv[side, 1].astype(F32) * there

    pack_field(0, masked, first=make_pack)
    for h in range(HALVES):
        make_unpack(h)
    forward(0, masked)
    send_rows(0, acc)
    send_stats(0, local_moments(acc))
    weights_round(1)
    load_cotangent()
    mean1, scale1, count = moments(0)

    def activate_one(start, size, carry):
        at = pl.ds(start, size)
        main = start is not cells
        nv = ((acc if main else normed1)[at, :] - mean1) * scale1
        normed1[at, :] = nv
        hid[at, :] = gelu_parts(nv * gain1 + shift1)[0] * mask[at, :]
        if main:
            acc[at, :] = jnp.zeros((size, ch), F32)
        return carry

    def slope_one(start, size, carry):
        at = pl.ds(start, size)
        slope1[at, :] = gelu_parts(normed1[at, :] * gain1 + shift1)[1] * mask[at, :]
        return carry

    take_rows(0, normed1)
    pack_field(1, hid, activate_one)
    everywhere(slope_one)
    forward(1, hid)
    send_rows(1, acc)
    send_stats(1, local_moments(acc))
    turn_field(0, masked)
    turn_field(1, hid)
    mean2, scale2, _ = moments(1)

    def activate_two(source, start, size):
        at = pl.ds(start, size)
        nv = (source[at, :] - mean2) * scale2
        normed2[at, :] = nv
        value, slope = gelu_parts(nv * gain2 + shift2 + masked[at, :])
        t = cotm[at, :] * slope
        through[at, :] = t
        return value, nv, t

    def activate_main(start, size, carry):
        value, nv, t = activate_two(acc, start, size)
        at = pl.ds(start, size)
        hid2[at, :] = value * mask[at, :]
        acc[at, :] = jnp.zeros((size, ch), F32)
        return carry[0] + fold(t * nv), carry[1] + fold(t)

    send_stats(2, [flatten(v) for v in chunked(activate_main, (zero, zero))])
    take_rows(1, normed2)
    take_cotangent()
    activate_two(normed2, cells, edge)
    to_flat(hid2, out_block)

    def gradient_sums(slot):
        take_stats(slot)
        got = [st_recv[slot, k] for k in range(s_count)]
        return sum(g[0:1] for g in got), sum(g[1:2] for g in got)

    def norm_back(upstream, normed, gain, scale, sums):
        gain_grad, shift_grad = sums
        factor = gain * scale
        level, tilt = shift_grad / count, gain_grad / count

        def fill(start, size, carry):
            at = pl.ds(start, size)
            v = upstream[at, :] - mask[at, :] * (level + normed[at, :] * tilt)
            hid[at, :] = factor * v
            return carry
        return fill

    sums2 = gradient_sums(2)
    pack_field(3, hid, norm_back(through, normed2, gain2, scale2, sums2))
    backward(1)

    send_rows(2, acc)

    def inner_main(start, size, carry):
        at = pl.ds(start, size)
        v = acc[at, :] * slope1[at, :]
        slope1[at, :] = v
        acc[at, :] = jnp.zeros((size, ch), F32)
        return carry[0] + fold(v * normed1[at, :]), carry[1] + fold(v)

    send_stats(3, [flatten(v) for v in chunked(inner_main, (zero, zero))])

    @pl.when(jnp.logical_not(passing))
    def _():
        of_step(n - 1, functools.partial(make_grad, 1))
    for side in range(2):
        row_copy(2, 1 - side).wait_recv()
        at = slice(cells + side * wide, cells + (side + 1) * wide)
        slope1[at, :] = row_recv[2, side] * slope1[at, :]
    sums1 = gradient_sums(3)
    pack_field(2, hid, norm_back(slope1, normed1, gain1, scale1, sums1))
    advance(1, n)
    backward(0)
    advance(0, n)

    def finish_input(start, size, carry):
        at = pl.ds(start, size)
        acc[at, :] = (acc[at, :] + through[at, :]) * mask[at, :]
        return carry

    chunked(finish_input, 0)
    to_flat(acc, out_input)
    out_gain1[...], out_shift1[...] = sums1
    out_gain2[...], out_shift2[...] = sums2
    for extra in range(1, len(stages) - 1):
        advance(0, n + extra)

    for side in range(2):
        edge_copy(side).wait_send()
        cot_copy(side).wait_send()
        for slot in range(3):
            row_copy(slot, side).wait_send()

    @pl.loop(1, s_count)
    def _(k):
        for slot in range(4):
            st_copy(slot, k, s).wait_send()

    @pl.loop(1, n)
    def _(k):
        for which in range(2):
            wz_copy(which, k).wait_send()

    @pl.loop(1, w_parts)
    def _(k):
        for which in range(2):
            for slot in range(n - 1):
                wp_copy(which, slot, k, w_mine).wait_send()

    @pl.loop(0, n)
    def _(k):
        for sign in (1, -1):
            block = z - k * sign

            @pl.when((block >= 0) & (block < n) & (z + sign >= 0) & (z + sign < n))
            def _():
                for ph in range(4):
                    for q in range(HALVES):
                        ag_copy(ph, block, q, sign).wait_send()

    @pl.loop(0, n)
    def _(j):
        for ph in range(2):
            c_copy(ph, j).wait_send()
            h_copy(ph, j, core).wait_send()
            o_copy(ph, j).wait()

            @pl.loop(1, chips)
            def _(e):
                peer = (chip + e) % chips

                @pl.when(peer < owners)
                def _():
                    q_copy(ph, j, e, chip, peer).wait_send()

                @pl.when(chip < owners)
                def _():
                    f_copy(ph, j, e, chip).wait_send()


def finish_kernel(count, *refs):
    ins, outs = refs[:count], refs[count:2 * count]
    narrow, wide, in_sem, out_sem, take_sem, give_sem = refs[2 * count:2 * count + 6]
    held = refs[2 * count + 6:]
    rows = narrow.shape[1] // FINISH_PARTS
    parts = [(w, i, pl.ds(i * rows, rows)) for i in range(FINISH_PARTS) for w in range(2)]
    loads = [pltpu.make_async_copy(ins[w].at[at, :], narrow.at[w, at, :], in_sem.at[w, i]) for w, i, at in parts]
    stores = [pltpu.make_async_copy(wide.at[w, at, :], outs[w].at[at, :], out_sem.at[w, i]) for w, i, at in parts]
    takes = [pltpu.make_async_copy(ins[2 + k], v, take_sem.at[k]) for k, v in enumerate(held)]
    gives = [pltpu.make_async_copy(v, outs[2 + k], give_sem.at[k]) for k, v in enumerate(held)]
    for copy in loads + takes:
        copy.start()
    for load, store, (w, i, at) in zip(loads, stores, parts):
        load.wait()
        wide[w, at, :] = narrow[w, at, :].astype(F32)
        store.start()
    for take, give in zip(takes, gives):
        take.wait()
        give.start()
    for copy in stores + gives:
        copy.wait()


def per_device(n, s_count, blocks, weight_one, weight_two, gain_one, shift_one, gain_two, shift_two, cell_live, cotangent):
    rows, wide = cell_live.shape
    ch = blocks.shape[1] // wide
    cells = rows * wide
    total = cells + 2 * wide
    packed = 2 * -(-most_live(rows // HALVES // 2, wide) // 8) * 8
    aligned = ch % 128 == 0
    chips = s_count // 2
    tap_rows = 9 * ch
    half_rows = tap_rows // 2
    owners = math.gcd(half_rows // 16, chips)
    piece = half_rows // owners

    if aligned:
        weight_one, weight_two = (w.reshape(tap_rows, n * ch) for w in (weight_one, weight_two))
    else:
        weight_one, weight_two = (
            w.reshape(tap_rows, n, ch).transpose(1, 0, 2) for w in (weight_one, weight_two))
    grad_shape = (2, owners, piece, n * ch) if aligned else (n, 2, owners, piece, ch)
    vmem = pl.BlockSpec(memory_space=pltpu.VMEM)
    hbm = pl.BlockSpec(memory_space=pl.ANY)
    sem = pltpu.SemaphoreType.DMA
    field = pltpu.VMEM((total, ch), F32)
    scratch = [
        pltpu.VMEM((ch * wide, 128), F32),
        pltpu.VMEM((2, n, tap_rows, ch), BF16),
        pltpu.VMEM((2, n - 1, tap_rows, ch), BF16),
        pltpu.VMEM((2, 3 * ch, cells), BF16),
        pltpu.VMEM((HALVES, packed, cells // HALVES), BF16),
        pltpu.VMEM((HALVES, 2, cells // HALVES // 2, -(-packed // 2 // 16) * 16), BF16),
        pltpu.VMEM((HALVES, 2, cells // HALVES // 2, ch), F32),
        pltpu.VMEM((2, 2, wide, ch), BF16),
        pltpu.VMEM((2, 2, wide, ch), BF16),
        pltpu.VMEM((2, wide, ch), BF16),
        pltpu.VMEM((2, wide, ch), BF16),
        field, field, field, field, field, field, field, field, field,
        pltpu.VMEM((total + 16, ch), F32),
        pltpu.VMEM((cells, ch), F32),
        pltpu.VMEM((4, n, 2 * wide + HALVES * packed, ch), BF16),
        pltpu.VMEM((n, rows + 3, wide, 3 * ch), BF16),
        pltpu.VMEM((2, n, 2, owners, piece, ch), F32),
        pltpu.VMEM((2, n, owners, piece, ch), BF16),
        pltpu.VMEM((2, n, owners, piece, ch), BF16),
        pltpu.VMEM((2, n, owners, piece, ch), BF16),
        pltpu.VMEM((2, n, chips, piece, ch), BF16),
        pltpu.VMEM((2, n, 2, owners, piece, ch), BF16),
        pltpu.VMEM((4, 8, ch), F32),
        pltpu.VMEM((4, s_count, 8, ch), F32),
        pltpu.VMEM((3, 2, wide, ch), F32),
        pltpu.VMEM((3, 2, wide, ch), F32),
        sem((2, n)),
        sem((2, n)), sem((2, n)),
        sem((2, n - 1, s_count)), sem((2, n - 1, s_count)),
        sem((2,)), sem((2,)),
        sem((2,)), sem((2,)),
        sem((4, 2, n, HALVES)), sem((4, n, HALVES)),
        sem((4, s_count)), sem((4, s_count)),
        sem((3, 2)), sem((3, 2)),
        sem((2, n)), sem((2, n)),
        sem((2, n, chips)), sem((2, n, chips)),
        sem((2, n, chips)), sem((2, n, chips)),
        sem((2, n)), sem((2, n)),
        sem((2, n)),
    ]
    block_out, input_grad, wg1, wg2, *sums = pl.pallas_call(
        functools.partial(block_kernel, n, s_count, rows, wide, ch, aligned, packed),
        out_shape=(
            jax.ShapeDtypeStruct((rows, ch * wide), BF16),
            jax.ShapeDtypeStruct((rows, ch * wide), F32),
            jax.ShapeDtypeStruct(grad_shape, BF16),
            jax.ShapeDtypeStruct(grad_shape, BF16),
            *[jax.ShapeDtypeStruct((1, ch), F32)] * 4,
        ),
        in_specs=[vmem] * 7 + [hbm] * 2,
        out_specs=(vmem, vmem, hbm, hbm, vmem, vmem, vmem, vmem),
        scratch_shapes=scratch,
        compiler_params=pltpu.CompilerParams(
            collective_id=0, has_side_effects=True, vmem_limit_bytes=60 * 1024 * 1024),
    )(blocks, cotangent, cell_live.T,
      *(v.reshape(1, ch) for v in (gain_one, shift_one, gain_two, shift_two)), weight_one, weight_two)

    if not aligned:
        def whole(grad):
            grad = grad.reshape(n, tap_rows, ch).transpose(1, 0, 2)
            return grad.astype(F32).reshape(9, ch, n * ch)
        return (block_out, input_grad, whole(wg1), whole(wg2), *(v.reshape(ch) for v in sums))

    wg1, wg2 = (w.reshape(tap_rows, n * ch) for w in (wg1, wg2))
    wide_grad = jax.ShapeDtypeStruct((tap_rows, n * ch), F32)
    moved = (block_out, input_grad, *sums)
    grad1, grad2, *moved = pl.pallas_call(
        functools.partial(finish_kernel, 2 + len(moved)),
        out_shape=(wide_grad, wide_grad, *(jax.ShapeDtypeStruct(v.shape, v.dtype) for v in moved)),
        in_specs=[pl.BlockSpec(memory_space=pl.ANY)] * (2 + len(moved)),
        out_specs=[pl.BlockSpec(memory_space=pl.ANY)] * (2 + len(moved)),
        scratch_shapes=[
            pltpu.VMEM((2, tap_rows, n * ch), BF16), pltpu.VMEM((2, tap_rows, n * ch), F32),
            sem((2, FINISH_PARTS)), sem((2, FINISH_PARTS)), sem((len(moved),)), sem((len(moved),)),
            *(pltpu.VMEM(v.shape, v.dtype) for v in moved),
        ],
        compiler_params=pltpu.CompilerParams(vmem_limit_bytes=64 * 1024 * 1024),
    )(wg1, wg2, *moved)
    block_out, input_grad, *sums = moved
    grads = (g.reshape(9, ch, n * ch) for g in (grad1, grad2))
    return (block_out, input_grad, *grads, *(v.reshape(ch) for v in sums))


def solution(mesh):
    return jax.shard_map(
        functools.partial(per_device, mesh.shape["chan"], mesh.shape["space"]),
        mesh=mesh,
        in_specs=(
            P("space", "chan"),
            P(None, "chan", None),
            P(None, "chan", None),
            P("chan"),
            P("chan"),
            P("chan"),
            P("chan"),
            P("space", None),
            P("space", "chan"),
        ),
        out_specs=(
            P("space", "chan"),
            P("space", "chan"),
            P(None, "chan", None),
            P(None, "chan", None),
            P("chan"),
            P("chan"),
            P("chan"),
            P("chan"),
        ),
        check_vma=False,
    )
```

```python
import functools
import math

import jax
import jax.numpy as jnp
from jax import lax
from jax.experimental import pallas as pl
from jax.experimental.pallas import tpu as pltpu
from jax.sharding import PartitionSpec as P

EPSILON = 1e-05
MESH = pl.DeviceIdType.MESH
F32 = jnp.float32
BF16 = jnp.bfloat16
ROOT_HALF = 0.7071067811865476
ROOT_TWO_PI = 0.3989422804014327
CHUNK = 64
FINISH_PARTS = 8
UNROLL = 2
HALVES = 2
LARGE, SMALL = 7, 3


def dot(a, b):
    return jnp.dot(a, b, preferred_element_type=F32)


def gelu_parts(v):
    upper = 0.5 * (1.0 + lax.erf(v * ROOT_HALF))
    slope = upper + v * (ROOT_TWO_PI * jnp.exp(-0.5 * v * v))
    return v * upper, slope


def most_live(rows, wide):
    units = (wide + 1) // (SMALL + 1)
    live_rows = rows - rows // (LARGE + 1)
    return min(rows * wide, math.ceil(units * live_rows * LARGE / 2))


def block_kernel(n, s_count, rows, wide, ch, aligned, packed, *refs):
    (x_in, cot_in, live_in, gain1_in, shift1_in, gain2_in, shift2_in, w1_hbm, w2_hbm) = refs[:9]
    (out_block, out_input, out_wg1, out_wg2, out_gain1, out_shift1, out_gain2, out_shift2) = refs[9:17]
    (turned, wv, wf, x_t, pack, unpack, places, edge_send, edge_recv, cot_send, cot_recv, cotm, mask, masked,
     normed1, normed2, through, slope1, hid, hid2, pad, acc, hold, taken,
     part, psend, crecv, hsend, qrecv, wout, st_send, st_recv, row_send, row_recv, flat_block, flat_input,
     w_sem, wz_ssem, wz_rsem, wp_ssem, wp_rsem, e_ssem, e_rsem, ce_ssem, ce_rsem, ag_ssem, ag_rsem,
     st_ssem, st_rsem, row_ssem, row_rsem, c_ssem, c_rsem, q_ssem, q_rsem,
     f_ssem, f_rsem, h_ssem, h_rsem, o_sem, r_sem) = refs[17:]

    z = lax.axis_index("chan")
    s = lax.axis_index("space")
    cells = rows * wide
    total = cells + 2 * wide
    band = cells // HALVES
    core, chip, chips = s % 2, s // 2, s_count // 2
    before, after = (s + s_count - 1) % s_count, (s + 1) % s_count
    tap_rows = 9 * ch

    barrier = pltpu.get_barrier_semaphore()

    @pl.loop(1, s_count)
    def _(k):
        pl.semaphore_signal(barrier, inc=1, device_id=(z, (s + k) % s_count), device_id_type=MESH)

    @pl.loop(1, n)
    def _(k):
        pl.semaphore_signal(barrier, inc=1, device_id=((z + k) % n, s), device_id_type=MESH)

    w_copies = []
    for which, source in enumerate((w1_hbm, w2_hbm)):
        for d in range(n):
            block = source.at[:, d * ch:(d + 1) * ch] if aligned else source.at[d]
            w_copies.append(pltpu.make_async_copy(block, wv.at[which, d], w_sem.at[which, d]))
    for copy in w_copies:
        copy.start()

    def chunked(fn, init, first=0, count=cells):
        def step(i, carry):
            return fn(pl.multiple_of(first + i * CHUNK, CHUNK), CHUNK, carry)
        return lax.fori_loop(0, count // CHUNK, step, init, unroll=UNROLL)

    lanes = 128
    tiles = ch * wide // lanes

    def from_flat(flat, put):
        for i in range(tiles):
            turned[i * lanes:(i + 1) * lanes, 0:rows] = flat[:, i * lanes:(i + 1) * lanes].astype(F32).T
        for w in range(wide):
            put(pl.ds(w, rows, stride=wide), turned[pl.ds(w, ch, stride=wide), 0:rows].T)

    def to_flat(source, flat):
        for w in range(wide):
            turned[pl.ds(w, ch, stride=wide), 0:rows] = source[pl.ds(w, rows, stride=wide), :].T
        for i in range(tiles):
            flat[:, i * lanes:(i + 1) * lanes] = turned[i * lanes:(i + 1) * lanes, 0:rows].T.astype(flat.dtype)

    def put_masked(at, value):
        masked[at, :] = value

    from_flat(x_in, put_masked)

    cell = lax.broadcasted_iota(jnp.int32, (cells, rows), 0)
    pick = (cell // wide == lax.broadcasted_iota(jnp.int32, (cells, rows), 1)).astype(F32).astype(BF16)
    column_of = lax.broadcasted_iota(jnp.int32, (cells, wide), 0) % wide
    picked = lax.dot_general(pick, live_in[...].astype(BF16), (((1,), (1,)), ((), ())), preferred_element_type=F32)
    picked = jnp.where(column_of == lax.broadcasted_iota(jnp.int32, (cells, wide), 1), picked, 0.0)
    mask[0:cells, :] = dot(picked.astype(BF16), jnp.ones((wide, ch), BF16))

    def load_main(start, size, carry):
        at = pl.ds(start, size)
        lv = mask[at, :]
        masked[at, :] = masked[at, :] * lv
        return carry

    chunked(load_main, 0)
    for side, start in ((0, 0), (1, cells - wide)):
        edge_send[side, 0] = masked[start:start + wide, :].astype(BF16)
        edge_send[side, 1] = mask[start:start + wide, :].astype(BF16)

    acc[...] = jnp.zeros_like(acc)
    for block in range(n):
        for row in (rows // HALVES + 1, rows + 2):
            taken[block, row:row + 1, :, :] = jnp.zeros((1, wide, 3 * ch), BF16)
    st_send[...] = jnp.zeros_like(st_send)

    pl.semaphore_wait(barrier, s_count - 1 + n - 1)

    def edge_copy(side):
        return pltpu.make_async_remote_copy(
            src_ref=edge_send.at[side], dst_ref=edge_recv.at[1 - side],
            send_sem=e_ssem.at[side], recv_sem=e_rsem.at[1 - side],
            device_id=(z, before if side == 0 else after), device_id_type=MESH)

    for side in range(2):
        edge_copy(side).start()

    def cot_copy(side):
        return pltpu.make_async_remote_copy(
            src_ref=cot_send.at[side], dst_ref=cot_recv.at[1 - side],
            send_sem=ce_ssem.at[side], recv_sem=ce_rsem.at[1 - side],
            device_id=(z, before if side == 0 else after), device_id_type=MESH)

    def load_cotangent():
        def put(at, value):
            cotm[at, :] = value
        from_flat(cot_in, put)

        def live_only(start, size, carry):
            at = pl.ds(start, size)
            cotm[at, :] = cotm[at, :] * mask[at, :]
            return carry
        chunked(live_only, 0)
        for side, start in ((0, 0), (1, cells - wide)):
            cot_send[side] = cotm[start:start + wide, :].astype(BF16)
            cot_copy(side).start()

    def take_cotangent():
        for side in range(2):
            cot_copy(1 - side).wait_recv()
            at = slice(cells + side * wide, cells + (side + 1) * wide)
            cotm[at, :] = cot_recv[side].astype(F32) * mask[at, :]

    w_parts = math.gcd(tap_rows // 16, s_count)
    w_rows = tap_rows // w_parts
    w_mine = s % w_parts
    w_group = s - w_mine

    def wz_copy(which, k):
        at = pl.ds(w_mine * w_rows, w_rows)
        slot = n - k - 1
        return pltpu.make_async_remote_copy(
            src_ref=wv.at[which, (z + k) % n, at, :], dst_ref=wf.at[which, slot, at, :],
            send_sem=wz_ssem.at[which, slot], recv_sem=wz_rsem.at[which, slot],
            device_id=((z + k) % n, s), device_id_type=MESH)

    def wp_copy(which, slot, k, whose):
        at = pl.ds(whose * w_rows, w_rows)
        return pltpu.make_async_remote_copy(
            src_ref=wf.at[which, slot, at, :], dst_ref=wf.at[which, slot, at, :],
            send_sem=wp_ssem.at[which, slot, k], recv_sem=wp_rsem.at[which, slot, whose],
            device_id=(z, w_group + (w_mine + k) % w_parts), device_id_type=MESH)

    def weights_over_z(which):
        for copy in w_copies[which * n:(which + 1) * n]:
            copy.wait()

        @pl.loop(1, n)
        def _(k):
            wz_copy(which, k).start()

    def slot_of(block):
        return (block - z + n - 1) % n

    def weights_round(which):
        @pl.loop(1, n)
        def _(distance):
            for sign in (1, -1):
                block = z - distance * sign

                @pl.when((block >= 0) & (block < n))
                def _():
                    slot = slot_of(block)
                    wz_copy(which, n - 1 - slot).wait_recv()

                    @pl.loop(1, w_parts)
                    def _(k):
                        wp_copy(which, slot, k, w_mine).start()

    def weights_arrived(which, slot):
        @pl.loop(1, w_parts)
        def _(k):
            wp_copy(which, slot, k, (w_mine + k) % w_parts).wait_recv()

    def row_copy(slot, side):
        return pltpu.make_async_remote_copy(
            src_ref=row_send.at[slot, side], dst_ref=row_recv.at[slot, 1 - side],
            send_sem=row_ssem.at[slot, side], recv_sem=row_rsem.at[slot, 1 - side],
            device_id=(z, before if side == 0 else after), device_id_type=MESH)

    def send_rows(slot, ref):
        for side, start in ((0, 0), (1, cells - wide)):
            row_send[slot, side] = ref[start:start + wide, :]
            row_copy(slot, side).start()

    def take_rows(slot, ref):
        for side in range(2):
            row_copy(slot, 1 - side).wait_recv()
            ref[cells + side * wide:cells + (side + 1) * wide, :] = row_recv[slot, side]

    def st_copy(slot, k, whose):
        return pltpu.make_async_remote_copy(
            src_ref=st_send.at[slot], dst_ref=st_recv.at[slot, whose],
            send_sem=st_ssem.at[slot, k], recv_sem=st_rsem.at[slot, whose],
            device_id=(z, (s + k) % s_count), device_id_type=MESH)

    def send_stats(slot, values):
        for i, v in enumerate(values):
            st_send[slot, i:i + 1, :] = v
        for k in range(1, s_count):
            st_copy(slot, k, s).start()
        st_recv[slot, s] = st_send[slot]

    def take_stats(slot):
        for k in range(1, s_count):
            st_copy(slot, k, (s + k) % s_count).wait_recv()

    strip = 8
    column = lax.broadcasted_iota(jnp.int32, (strip * wide, ch), 0) % wide

    def shift(target, first, count):
        size = count * wide
        where = column[:size]
        here = pad[pl.ds(8 + first * wide, size), :]
        left = jnp.where(where == 0, 0.0, pad[pl.ds(7 + first * wide, size), :])
        right = jnp.where(where == wide - 1, 0.0, pad[pl.ds(9 + first * wide, size), :])
        for b, v in enumerate((left, here, right)):
            target[pl.ds(first, count), :, b * ch:(b + 1) * ch] = v.astype(BF16).reshape(count, wide, ch)

    edge = 2 * wide
    ag_rows = ((0, edge + packed), (edge + packed, packed))
    band_rows = rows // HALVES

    def unpack_half(ph, block, q, target):
        if q == 0:
            pad[8:8 + wide, :] = hold[ph, block, 0:wide, :].astype(F32)
            pad[8 + wide + cells:8 + 2 * wide + cells, :] = hold[ph, block, wide:edge, :].astype(F32)
            shift(target, 0, 1)
            shift(target, rows + 1, 1)
        for j in range(2):
            start = edge + q * packed + j * (packed - unpack.shape[3])
            at = 8 + wide + q * band + j * (band // 2)
            pad[at:at + band // 2, :] = dot(unpack[q, j], hold[ph, block, start:start + unpack.shape[3], :])

        for i in range(band_rows // strip):
            shift(target, 1 + q * band_rows + i * strip, strip)

    def add_conv(q, field, taps, turned_taps=None):
        first, last = (0, band_rows - 1) if q == 0 else (band_rows - 1, rows)
        count = last - first
        size = (count + 2) * wide
        lhs = jnp.concatenate([
            field[first + i:last + 2 + i, :, :].reshape(size, 3 * ch) for i in range(2)], axis=1)
        if turned_taps is None:
            none = jnp.zeros((3 * ch, ch), BF16)
            rhs = jnp.concatenate([
                jnp.concatenate([taps(0), taps(2)], axis=1), jnp.concatenate([taps(1), none], axis=1)], axis=0)
            value = dot(lhs, rhs)
        else:
            def row_taps(a):
                return [turned_taps(3 * (2 - a) + 2 - b) for b in range(3)]
            none = jnp.zeros((ch, 3 * ch), BF16)
            rhs = jnp.concatenate([
                jnp.concatenate(row_taps(0) + row_taps(1), axis=1), jnp.concatenate(row_taps(2) + [none], axis=1)], axis=0)
            value = lax.dot_general(lhs, rhs, (((1,), (1,)), ((), ())), preferred_element_type=F32)
        at = pl.ds(first * wide, count * wide)
        acc[at, :] = acc[at, :] + value[0:count * wide, 0:ch] + value[2 * wide:size, ch:2 * ch]

    def ag_copy(ph, block, q, sign):
        at = pl.ds(*ag_rows[q])
        return pltpu.make_async_remote_copy(
            src_ref=hold.at[ph, block, at, :], dst_ref=hold.at[ph, block, at, :],
            send_sem=ag_ssem.at[ph, (1 - sign) // 2, block, q], recv_sem=ag_rsem.at[ph, block, q],
            device_id=(z + sign, s), device_id_type=MESH)

    def pack_field(ph, source, fill=None, first=None):
        if fill is not None:
            fill(cells, edge, 0)
        hold[ph, z, 0:edge, :] = source[cells:cells + edge, :].astype(BF16)
        for q in range(HALVES):
            if first is not None:
                first(q)
            if fill is not None:
                chunked(fill, 0, q * band, band)
            hold[ph, z, edge + q * packed:edge + (q + 1) * packed, :] = dot(
                pack[q], source[q * band:(q + 1) * band, :].astype(BF16)).astype(BF16)
            for sign in (1, -1):
                @pl.when((z + sign >= 0) & (z + sign < n))
                def _():
                    ag_copy(ph, z, q, sign).start()

    def inside(slice_at):
        return (slice_at >= 0) & (slice_at < n)

    def take_and_pass(ph, k, q, sign, passes=True, takes=True):
        block = z - k * sign

        @pl.when((k > 0) & inside(block))
        def _():
            if passes and takes:
                ag_copy(ph, block, q, sign).wait_recv()

            @pl.when(inside(z + sign))
            def _():
                if passes:
                    if not takes:
                        ag_copy(ph, block, q, sign).wait_recv()
                    ag_copy(ph, block, q, sign).start()

            if not passes:
                @pl.when(jnp.logical_not(inside(z + sign)))
                def _():
                    ag_copy(ph, block, q, sign).wait_recv()

    near = jnp.where(z < n - n // 2, 1, 0)

    def consume_way(k, q, way, consume):
        block = z - k * (1 - 2 * way)

        @pl.when((k >= 0) & (k < n) & inside(block) & ((k > 0) | (way == near)))
        def _():
            consume(k, block, q)

    def take_both(ph, k, q, **how):
        @pl.loop(0, 2)
        def _(i):
            way = (near + i) % 2
            take_and_pass(ph, k, q, 1 - 2 * way, **how)

    def gather(ph, consume, each):
        @pl.loop(0, n)
        def _(k):
            for q in range(HALVES):
                take_both(ph, k, q)
                if q:
                    consume_way(k, q - 1, 1 - near, consume)
                else:
                    consume_way(k - 1, HALVES - 1, 1 - near, consume)
                consume_way(k, q, near, consume)
            each(k)

    def gather_passing_first(ph, consume, each):
        @pl.loop(0, n)
        def _(k):
            @pl.when(k == 1)
            def _():
                @pl.loop(1, n)
                def _(ahead):
                    for q in range(HALVES):
                        take_both(ph, ahead, q, takes=False)
            for q in range(HALVES):
                take_both(ph, k, q, passes=False)

                @pl.loop(0, 2)
                def _(i):
                    consume_way(k, q, (near + i) % 2, consume)
            each(k)

    last_pass = jnp.maximum(jnp.where(z < n - 1, z, 0), jnp.where(z > 0, n - 1 - z, 0))

    def forward(ph, field):
        def consume(k, block, q):
            into = taken.at[block]
            unpack_half(ph, block, q, into)

            @pl.when(k == 0)
            def _():
                add_conv(q, into, lambda a: wv[ph, z, 3 * a * ch:3 * (a + 1) * ch, :])

            @pl.when(k > 0)
            def _():
                slot = slot_of(block)
                if q == 0:
                    weights_arrived(ph, slot)
                add_conv(q, into, lambda a: wf[ph, slot, 3 * a * ch:3 * (a + 1) * ch, :])

        def each(k):
            if ph == 0:
                @pl.when(k == 0)
                def _():
                    weights_round(0)

                @pl.when(k == 1)
                def _():
                    weights_over_z(1)

                @pl.when(k == last_pass)
                def _():
                    load_cotangent()
        (gather if ph else gather_passing_first)(ph, consume, each)

    def turn_field(ph, field):
        main = [field[start:start + ch, :].T for start in range(0, cells, ch)]
        ends = field[cells:cells + edge, :]
        if edge < ch:
            ends = jnp.concatenate([ends, jnp.zeros((ch - edge, ch), F32)], axis=0)
        ends = ends.T
        for i, here in enumerate(main):
            left = jnp.concatenate(
                [ends[:, 0:wide] if i == 0 else main[i - 1][:, ch - wide:], here[:, 0:ch - wide]], axis=1)
            right = jnp.concatenate(
                [here[:, wide:], main[i + 1][:, 0:wide] if i + 1 < len(main) else ends[:, wide:edge]], axis=1)
            for a, v in enumerate((left, here, right)):
                x_t[ph, a * ch:(a + 1) * ch, i * ch:(i + 1) * ch] = v.astype(BF16)

    half_rows = tap_rows // 2
    owners = math.gcd(half_rows // 16, chips)
    piece = half_rows // owners

    def c_copy(ph, j):
        return pltpu.make_async_remote_copy(
            src_ref=psend.at[ph, j], dst_ref=crecv.at[ph, j],
            send_sem=c_ssem.at[ph, j], recv_sem=c_rsem.at[ph, j],
            device_id=(z, chip * 2 + 1 - core), device_id_type=MESH)

    def q_copy(ph, j, e, whose, owner):
        return pltpu.make_async_remote_copy(
            src_ref=hsend.at[ph, j, owner], dst_ref=qrecv.at[ph, j, whose],
            send_sem=q_ssem.at[ph, j, e], recv_sem=q_rsem.at[ph, j, whose],
            device_id=(z, ((chip + e) % chips) * 2 + core), device_id_type=MESH)

    def f_copy(ph, j, e, owner):
        return pltpu.make_async_remote_copy(
            src_ref=wout.at[ph, j, core, owner], dst_ref=wout.at[ph, j, core, owner],
            send_sem=f_ssem.at[ph, j, e], recv_sem=f_rsem.at[ph, j, owner],
            device_id=(z, ((chip + e) % chips) * 2 + core), device_id_type=MESH)

    def h_copy(ph, j, whose):
        return pltpu.make_async_remote_copy(
            src_ref=wout.at[ph, j, whose], dst_ref=wout.at[ph, j, whose],
            send_sem=h_ssem.at[ph, j], recv_sem=h_rsem.at[ph, j],
            device_id=(z, chip * 2 + 1 - core), device_id_type=MESH)

    def o_copy(ph, j):
        target = (out_wg1, out_wg2)[ph]
        if aligned:
            target = target.at[:, :, :, pl.ds(pl.multiple_of(j * ch, ch), ch)]
        else:
            target = target.at[j]
        return pltpu.make_async_copy(wout.at[ph, j], target, o_sem.at[ph, j])

    def sum_cores(ph, j):
        for o in range(owners):
            psend[ph, j, o] = part[ph, j, 1 - core, o].astype(BF16)
        c_copy(ph, j).start()

    def sum_chips(ph, j):
        c_copy(ph, j).wait_recv()
        for o in range(owners):
            v = part[ph, j, core, o] + crecv[ph, j, o].astype(F32)
            part[ph, j, core, o] = v
            hsend[ph, j, o] = v.astype(BF16)

        @pl.loop(1, chips)
        def _(e):
            peer = (chip + e) % chips

            @pl.when(peer < owners)
            def _():
                q_copy(ph, j, e, chip, peer).start()

    def spread_chips(ph, j):
        @pl.when(chip < owners)
        def _():
            @pl.loop(1, chips)
            def _(e):
                q_copy(ph, j, e, (chip + e) % chips, chip).wait_recv()
            v = part[ph, j, core, chip]
            for e in range(1, chips):
                v = v + qrecv[ph, j, (chip + e) % chips].astype(F32)
            wout[ph, j, core, chip] = v.astype(BF16)

            @pl.loop(1, chips)
            def _(e):
                f_copy(ph, j, e, chip).start()

    def spread_cores(ph, j):
        @pl.loop(1, chips)
        def _(e):
            peer = (chip + e) % chips

            @pl.when(peer < owners)
            def _():
                f_copy(ph, j, e, peer).wait_recv()
        h_copy(ph, j, core).start()

    def finish(ph, j):
        h_copy(ph, j, 1 - core).wait_recv()
        o_copy(ph, j).start()

    def put_part(ph, j, tap, value):
        start = tap * ch
        done = 0
        while done < ch:
            row = start + done
            side, o, at = row // half_rows, row % half_rows // piece, row % piece
            size = min(ch - done, piece - at)
            part[ph, j, side, o, at:at + size, :] = value[done:done + size, :]
            done += size

    stages = (sum_cores, sum_chips, spread_chips, spread_cores, finish)

    def of_step(k, fn):
        @pl.loop(0, 2)
        def _(way):
            block = z - k * (1 - 2 * way)

            @pl.when((k >= 0) & (k < n) & inside(block) & ((k > 0) | (way == 0)))
            def _():
                fn(block)

    passing = last_pass > 0

    def made_at(step):
        first = jnp.where(passing & (step > 0), jnp.where(step == last_pass, 1, step + 1), step)
        return first, step + 1

    def advance(ph, k):
        for age in range(1, len(stages)):
            step = k - age

            @pl.when((step >= 0) & (step < n))
            def _():
                @pl.loop(*made_at(step))
                def _(made):
                    of_step(made, functools.partial(stages[age], ph))

    def advance_all(ph, age):
        @pl.loop(0, n)
        def _(j):
            stages[age](ph, j)

    def field_grad(ph, block):
        grad = taken[block, 1:rows + 1, :, :].reshape(cells, 3 * ch)
        value = dot(x_t[ph], grad)
        for a in range(3):
            for b in range(3):
                put_part(ph, block, 3 * a + b, value[a * ch:(a + 1) * ch, (2 - b) * ch:(3 - b) * ch])

    def make_grad(ph, block):
        field_grad(ph, block)
        sum_cores(ph, block)

    def backward(ph):
        last = ph == 0

        def consume(k, block, q):
            into = taken.at[block]
            unpack_half(2 + ph, block, q, into)
            if last and q == HALVES - 1:
                @pl.when((k == 0) | (k >= last_pass))
                def _():
                    make_grad(ph, block)
            add_conv(q, into, None, lambda t: wv[ph, block, t * ch:(t + 1) * ch, :])

        def each(k):
            first, end = made_at(k)
            if last:
                @pl.loop(first, end - 1)
                def _(step):
                    of_step(step, functools.partial(make_grad, ph))
                advance(ph, k)
                for age in range(2, len(stages)):
                    @pl.when(k == age - 2)
                    def _():
                        advance_all(1, age)
            else:
                @pl.loop(first, jnp.where(passing | (k < n - 1), end, first))
                def _(step):
                    of_step(step, functools.partial(make_grad, ph))
        gather(2 + ph, consume, each)

    def fold(v):
        return jnp.sum(v.reshape(v.shape[0] // 8, 8, ch), axis=0)

    def flatten(v):
        return jnp.sum(v, axis=0, keepdims=True)

    zero = jnp.zeros((8, ch), F32)

    def local_moments(ref):
        def sums(start, size, carry):
            at = pl.ds(start, size)
            m = mask[at, :]
            return carry[0] + fold(ref[at, :] * m), carry[1] + fold(m)
        added, number = (flatten(v) for v in chunked(sums, (zero, zero)))
        middle = added / jnp.maximum(number, 1.0)

        def spread(start, size, carry):
            at = pl.ds(start, size)
            c = (ref[at, :] - middle) * mask[at, :]
            return carry + fold(c * c)
        return added, number, flatten(chunked(spread, zero))

    def moments(slot):
        take_stats(slot)
        got = [st_recv[slot, k] for k in range(s_count)]
        added = sum(g[0:1] for g in got)
        number = sum(g[1:2] for g in got)
        mean = added / number
        spread = 0.0
        for g in got:
            off = g[0:1] / jnp.maximum(g[1:2], 1.0) - mean
            spread = spread + (g[2:3] + g[1:2] * off * off)
        return mean, lax.rsqrt(spread / number + EPSILON), number

    def everywhere(fn):
        chunked(fn, 0)
        fn(cells, 2 * wide, 0)

    gain1, shift1, gain2, shift2 = (r[...] for r in (gain1_in, shift1_in, gain2_in, shift2_in))

    weights_over_z(0)

    quarter = band // 2
    kept = packed // 2
    window = unpack.shape[3]
    below = lax.broadcasted_iota(jnp.int32, (quarter, quarter), 1) < lax.broadcasted_iota(jnp.int32, (quarter, quarter), 0)
    below = below.astype(F32).astype(BF16)

    def make_pack(h):
        for j in range(2):
            lv = mask[h * band + j * quarter:h * band + (j + 1) * quarter, :]
            place = jnp.where(lv > 0.0, dot(below, lv.astype(BF16)) + j * kept, -1.0)
            places[h, j] = place
            across = place.T[0:1, :]
            spot = lax.broadcasted_iota(jnp.int32, (packed, quarter), 0).astype(F32)
            pack[h, :, j * quarter:(j + 1) * quarter] = jnp.where(spot == across, 1.0, 0.0).astype(BF16)

    def make_unpack(h):
        for j in range(2):
            for start in range(0, window, ch):
                size = min(ch, window - start)
                spot = start + j * (packed - window) + lax.broadcasted_iota(jnp.int32, (quarter, size), 1)
                unpack[h, j, :, start:start + size] = jnp.where(
                    places[h, j, :, :size] == spot.astype(F32), 1.0, 0.0).astype(BF16)

    for side in range(2):
        edge_copy(1 - side).wait_recv()
        there = jnp.where(s > 0, 1.0, 0.0) if side == 0 else jnp.where(s < s_count - 1, 1.0, 0.0)
        at = slice(cells + side * wide, cells + (side + 1) * wide)
        masked[at, :] = edge_recv[side, 0].astype(F32) * there
        mask[at, :] = edge_recv[side, 1].astype(F32) * there

    def stats_sent(slot):
        for k in range(1, s_count):
            st_copy(slot, k, s).wait_send()

    def row_sent(slot):
        for side in range(2):
            row_copy(slot, side).wait_send()

    def gathered_sent(ph):
        @pl.loop(0, n)
        def _(k):
            for sign in (1, -1):
                block = z - k * sign

                @pl.when(inside(block) & inside(z + sign))
                def _():
                    for q in range(HALVES):
                        ag_copy(ph, block, q, sign).wait_send()

    def weights_sent(which):
        for k in range(1, n):
            wz_copy(which, k).wait_send()

        @pl.loop(1, w_parts)
        def _(k):
            for slot in range(n - 1):
                wp_copy(which, slot, k, w_mine).wait_send()

    def grads_sent(ph):
        @pl.loop(0, n)
        def _(j):
            c_copy(ph, j).wait_send()
            h_copy(ph, j, core).wait_send()
            o_copy(ph, j).wait()
            for e in range(1, chips):
                peer = (chip + e) % chips

                @pl.when(peer < owners)
                def _():
                    q_copy(ph, j, e, chip, peer).wait_send()

                @pl.when(chip < owners)
                def _():
                    f_copy(ph, j, e, chip).wait_send()

    block_copy = pltpu.make_async_copy(flat_block, out_block, r_sem.at[0])

    pack_field(0, masked, first=make_pack)
    for h in range(HALVES):
        make_unpack(h)
    forward(0, masked)
    send_rows(0, acc)
    send_stats(0, local_moments(acc))
    weights_round(1)
    mean1, scale1, count = moments(0)

    def activate_one(start, size, carry):
        at = pl.ds(start, size)
        main = start is not cells
        nv = ((acc if main else normed1)[at, :] - mean1) * scale1
        normed1[at, :] = nv
        hid[at, :] = gelu_parts(nv * gain1 + shift1)[0] * mask[at, :]
        if main:
            acc[at, :] = jnp.zeros((size, ch), F32)
        return carry

    def slope_one(start, size, carry):
        at = pl.ds(start, size)
        slope1[at, :] = gelu_parts(normed1[at, :] * gain1 + shift1)[1] * mask[at, :]
        return carry

    take_rows(0, normed1)
    pack_field(1, hid, activate_one)
    everywhere(slope_one)
    forward(1, hid)
    send_rows(1, acc)
    send_stats(1, local_moments(acc))
    turn_field(0, masked)
    turn_field(1, hid)
    weights_sent(0)
    gathered_sent(0)
    stats_sent(0)
    row_sent(0)
    for side in range(2):
        edge_copy(side).wait_send()
        cot_copy(side).wait_send()
    mean2, scale2, _ = moments(1)

    def activate_two(source, start, size):
        at = pl.ds(start, size)
        nv = (source[at, :] - mean2) * scale2
        normed2[at, :] = nv
        value, slope = gelu_parts(nv * gain2 + shift2 + masked[at, :])
        t = cotm[at, :] * slope
        through[at, :] = t
        return value, nv, t

    def activate_main(start, size, carry):
        value, nv, t = activate_two(acc, start, size)
        at = pl.ds(start, size)
        hid2[at, :] = value * mask[at, :]
        acc[at, :] = jnp.zeros((size, ch), F32)
        return carry[0] + fold(t * nv), carry[1] + fold(t)

    send_stats(2, [flatten(v) for v in chunked(activate_main, (zero, zero))])
    take_rows(1, normed2)
    take_cotangent()
    activate_two(normed2, cells, edge)
    to_flat(hid2, flat_block)
    block_copy.start()
    weights_sent(1)
    gathered_sent(1)

    def gradient_sums(slot):
        take_stats(slot)
        got = [st_recv[slot, k] for k in range(s_count)]
        return sum(g[0:1] for g in got), sum(g[1:2] for g in got)

    def norm_back(upstream, normed, gain, scale, sums):
        gain_grad, shift_grad = sums
        factor = gain * scale
        level, tilt = shift_grad / count, gain_grad / count

        def fill(start, size, carry):
            at = pl.ds(start, size)
            v = upstream[at, :] - mask[at, :] * (level + normed[at, :] * tilt)
            hid[at, :] = factor * v
            return carry
        return fill

    sums2 = gradient_sums(2)
    pack_field(3, hid, norm_back(through, normed2, gain2, scale2, sums2))
    backward(1)

    send_rows(2, acc)

    def inner_main(start, size, carry):
        at = pl.ds(start, size)
        v = acc[at, :] * slope1[at, :]
        slope1[at, :] = v
        acc[at, :] = jnp.zeros((size, ch), F32)
        return carry[0] + fold(v * normed1[at, :]), carry[1] + fold(v)

    send_stats(3, [flatten(v) for v in chunked(inner_main, (zero, zero))])

    @pl.when(jnp.logical_not(passing))
    def _():
        of_step(n - 1, functools.partial(make_grad, 1))
    for side in range(2):
        row_copy(2, 1 - side).wait_recv()
        at = slice(cells + side * wide, cells + (side + 1) * wide)
        slope1[at, :] = row_recv[2, side] * slope1[at, :]
    stats_sent(1)
    row_sent(1)
    stats_sent(2)
    gathered_sent(3)
    sums1 = gradient_sums(3)
    pack_field(2, hid, norm_back(slope1, normed1, gain1, scale1, sums1))
    advance_all(1, 1)
    backward(0)
    advance(0, n)

    def finish_input(start, size, carry):
        at = pl.ds(start, size)
        acc[at, :] = (acc[at, :] + through[at, :]) * mask[at, :]
        return carry

    chunked(finish_input, 0)
    to_flat(acc, flat_input)
    input_copy = pltpu.make_async_copy(flat_input, out_input, r_sem.at[1])
    input_copy.start()
    out_gain1[...], out_shift1[...] = sums1
    out_gain2[...], out_shift2[...] = sums2
    for extra in range(1, len(stages) - 1):
        advance(0, n + extra)

    stats_sent(3)
    row_sent(2)
    gathered_sent(2)
    grads_sent(1)
    grads_sent(0)
    block_copy.wait()
    input_copy.wait()


def finish_kernel(count, *refs):
    ins, outs = refs[:count], refs[count:2 * count]
    narrow, wide, in_sem, out_sem, take_sem, give_sem = refs[2 * count:2 * count + 6]
    held = refs[2 * count + 6:]
    rows = narrow.shape[1] // FINISH_PARTS
    parts = [(w, i, pl.ds(i * rows, rows)) for i in range(FINISH_PARTS) for w in range(2)]
    loads = [pltpu.make_async_copy(ins[w].at[at, :], narrow.at[w, at, :], in_sem.at[w, i]) for w, i, at in parts]
    stores = [pltpu.make_async_copy(wide.at[w, at, :], outs[w].at[at, :], out_sem.at[w, i]) for w, i, at in parts]
    takes = [pltpu.make_async_copy(ins[2 + k], v, take_sem.at[k]) for k, v in enumerate(held)]
    gives = [pltpu.make_async_copy(v, outs[2 + k], give_sem.at[k]) for k, v in enumerate(held)]
    for copy in loads + takes:
        copy.start()
    for load, store, (w, i, at) in zip(loads, stores, parts):
        load.wait()
        wide[w, at, :] = narrow[w, at, :].astype(F32)
        store.start()
    for take, give in zip(takes, gives):
        take.wait()
        give.start()
    for copy in stores + gives:
        copy.wait()


def per_device(n, s_count, blocks, weight_one, weight_two, gain_one, shift_one, gain_two, shift_two, cell_live, cotangent):
    rows, wide = cell_live.shape
    ch = blocks.shape[1] // wide
    cells = rows * wide
    total = cells + 2 * wide
    packed = 2 * -(-most_live(rows // HALVES // 2, wide) // 8) * 8
    aligned = ch % 128 == 0
    chips = s_count // 2
    tap_rows = 9 * ch
    half_rows = tap_rows // 2
    owners = math.gcd(half_rows // 16, chips)
    piece = half_rows // owners

    if aligned:
        weight_one, weight_two = (w.reshape(tap_rows, n * ch) for w in (weight_one, weight_two))
    else:
        weight_one, weight_two = (
            w.reshape(tap_rows, n, ch).transpose(1, 0, 2) for w in (weight_one, weight_two))
    grad_shape = (2, owners, piece, n * ch) if aligned else (n, 2, owners, piece, ch)
    vmem = pl.BlockSpec(memory_space=pltpu.VMEM)
    hbm = pl.BlockSpec(memory_space=pl.ANY)
    sem = pltpu.SemaphoreType.DMA
    field = pltpu.VMEM((total, ch), F32)
    scratch = [
        pltpu.VMEM((ch * wide, 128), F32),
        pltpu.VMEM((2, n, tap_rows, ch), BF16),
        pltpu.VMEM((2, n - 1, tap_rows, ch), BF16),
        pltpu.VMEM((2, 3 * ch, cells), BF16),
        pltpu.VMEM((HALVES, packed, cells // HALVES), BF16),
        pltpu.VMEM((HALVES, 2, cells // HALVES // 2, -(-packed // 2 // 16) * 16), BF16),
        pltpu.VMEM((HALVES, 2, cells // HALVES // 2, ch), F32),
        pltpu.VMEM((2, 2, wide, ch), BF16),
        pltpu.VMEM((2, 2, wide, ch), BF16),
        pltpu.VMEM((2, wide, ch), BF16),
        pltpu.VMEM((2, wide, ch), BF16),
        field, field, field, field, field, field, field, field, field,
        pltpu.VMEM((total + 16, ch), F32),
        pltpu.VMEM((cells, ch), F32),
        pltpu.VMEM((4, n, 2 * wide + HALVES * packed, ch), BF16),
        pltpu.VMEM((n, rows + 3, wide, 3 * ch), BF16),
        pltpu.VMEM((2, n, 2, owners, piece, ch), F32),
        pltpu.VMEM((2, n, owners, piece, ch), BF16),
        pltpu.VMEM((2, n, owners, piece, ch), BF16),
        pltpu.VMEM((2, n, owners, piece, ch), BF16),
        pltpu.VMEM((2, n, chips, piece, ch), BF16),
        pltpu.VMEM((2, n, 2, owners, piece, ch), BF16),
        pltpu.VMEM((4, 8, ch), F32),
        pltpu.VMEM((4, s_count, 8, ch), F32),
        pltpu.VMEM((3, 2, wide, ch), F32),
        pltpu.VMEM((3, 2, wide, ch), F32),
        pltpu.VMEM((rows, ch * wide), BF16),
        pltpu.VMEM((rows, ch * wide), F32),
        sem((2, n)),
        sem((2, n)), sem((2, n)),
        sem((2, n - 1, s_count)), sem((2, n - 1, s_count)),
        sem((2,)), sem((2,)),
        sem((2,)), sem((2,)),
        sem((4, 2, n, HALVES)), sem((4, n, HALVES)),
        sem((4, s_count)), sem((4, s_count)),
        sem((3, 2)), sem((3, 2)),
        sem((2, n)), sem((2, n)),
        sem((2, n, chips)), sem((2, n, chips)),
        sem((2, n, chips)), sem((2, n, chips)),
        sem((2, n)), sem((2, n)),
        sem((2, n)),
        sem((2,)),
    ]
    block_out, input_grad, wg1, wg2, *sums = pl.pallas_call(
        functools.partial(block_kernel, n, s_count, rows, wide, ch, aligned, packed),
        out_shape=(
            jax.ShapeDtypeStruct((rows, ch * wide), BF16),
            jax.ShapeDtypeStruct((rows, ch * wide), F32),
            jax.ShapeDtypeStruct(grad_shape, BF16),
            jax.ShapeDtypeStruct(grad_shape, BF16),
            *[jax.ShapeDtypeStruct((1, ch), F32)] * 4,
        ),
        in_specs=[vmem] * 7 + [hbm] * 2,
        out_specs=(hbm, hbm, hbm, hbm, vmem, vmem, vmem, vmem),
        scratch_shapes=scratch,
        compiler_params=pltpu.CompilerParams(
            collective_id=0, has_side_effects=True, vmem_limit_bytes=60 * 1024 * 1024),
    )(blocks, cotangent, cell_live.T,
      *(v.reshape(1, ch) for v in (gain_one, shift_one, gain_two, shift_two)), weight_one, weight_two)

    if not aligned:
        def whole(grad):
            grad = grad.reshape(n, tap_rows, ch).transpose(1, 0, 2)
            return grad.astype(F32).reshape(9, ch, n * ch)
        return (block_out, input_grad, whole(wg1), whole(wg2), *(v.reshape(ch) for v in sums))

    wg1, wg2 = (w.reshape(tap_rows, n * ch) for w in (wg1, wg2))
    wide_grad = jax.ShapeDtypeStruct((tap_rows, n * ch), F32)
    moved = (block_out, input_grad, *sums)
    grad1, grad2, *moved = pl.pallas_call(
        functools.partial(finish_kernel, 2 + len(moved)),
        out_shape=(wide_grad, wide_grad, *(jax.ShapeDtypeStruct(v.shape, v.dtype) for v in moved)),
        in_specs=[pl.BlockSpec(memory_space=pl.ANY)] * (2 + len(moved)),
        out_specs=[pl.BlockSpec(memory_space=pl.ANY)] * (2 + len(moved)),
        scratch_shapes=[
            pltpu.VMEM((2, tap_rows, n * ch), BF16), pltpu.VMEM((2, tap_rows, n * ch), F32),
            sem((2, FINISH_PARTS)), sem((2, FINISH_PARTS)), sem((len(moved),)), sem((len(moved),)),
            *(pltpu.VMEM(v.shape, v.dtype) for v in moved),
        ],
        compiler_params=pltpu.CompilerParams(vmem_limit_bytes=64 * 1024 * 1024),
    )(wg1, wg2, *moved)
    block_out, input_grad, *sums = moved
    grads = (g.reshape(9, ch, n * ch) for g in (grad1, grad2))
    return (block_out, input_grad, *grads, *(v.reshape(ch) for v in sums))


def solution(mesh):
    return jax.shard_map(
        functools.partial(per_device, mesh.shape["chan"], mesh.shape["space"]),
        mesh=mesh,
        in_specs=(
            P("space", "chan"),
            P(None, "chan", None),
            P(None, "chan", None),
            P("chan"),
            P("chan"),
            P("chan"),
            P("chan"),
            P("space", None),
            P("space", "chan"),
        ),
        out_specs=(
            P("space", "chan"),
            P("space", "chan"),
            P(None, "chan", None),
            P(None, "chan", None),
            P("chan"),
            P("chan"),
            P("chan"),
            P("chan"),
        ),
        check_vma=False,
    )
```

```python
import functools
import math

import jax
import jax.numpy as jnp
from jax import lax
from jax.experimental import pallas as pl
from jax.experimental.pallas import tpu as pltpu
from jax.sharding import PartitionSpec as P

EPSILON = 1e-05
MESH = pl.DeviceIdType.MESH
F32 = jnp.float32
BF16 = jnp.bfloat16
ROOT_HALF = 0.7071067811865476
ROOT_TWO_PI = 0.3989422804014327
CHUNK = 64
FINISH_PARTS = 4
UNROLL = 2
HALVES = 2
LARGE, SMALL = 7, 3


def dot(a, b):
    return jnp.dot(a, b, preferred_element_type=F32)


def gelu_parts(v):
    upper = 0.5 * (1.0 + lax.erf(v * ROOT_HALF))
    slope = upper + v * (ROOT_TWO_PI * jnp.exp(-0.5 * v * v))
    return v * upper, slope


def most_live(rows, wide):
    units = (wide + 1) // (SMALL + 1)
    live_rows = rows - rows // (LARGE + 1)
    return min(rows * wide, math.ceil(units * live_rows * LARGE / 2))


def block_kernel(n, s_count, rows, wide, ch, aligned, packed, *refs):
    (x_in, cot_in, live_in, gain1_in, shift1_in, gain2_in, shift2_in, w1_hbm, w2_hbm) = refs[:9]
    (out_block, out_input, out_wg1, out_wg2, out_gain1, out_shift1, out_gain2, out_shift2) = refs[9:17]
    (turned, wv, wf, x_t, pack, unpack, places, edge_send, edge_recv, cot_send, cot_recv, cotm, mask, masked,
     normed1, normed2, through, slope1, hid, hid2, pad, acc, hold, taken,
     part, psend, crecv, hsend, qrecv, wout, st_send, st_recv, row_send, row_recv, early, flat_block, flat_input,
     w_sem, wz_ssem, wz_rsem, wp_ssem, wp_rsem, e_ssem, e_rsem, ce_ssem, ce_rsem, ag_ssem, ag_rsem,
     st_ssem, st_rsem, row_ssem, row_rsem, c_ssem, c_rsem, q_ssem, q_rsem,
     f_ssem, f_rsem, h_ssem, h_rsem, o_sem, r_sem) = refs[17:]

    z = lax.axis_index("chan")
    s = lax.axis_index("space")
    cells = rows * wide
    total = cells + 2 * wide
    band = cells // HALVES
    core, chip, chips = s % 2, s // 2, s_count // 2
    before, after = (s + s_count - 1) % s_count, (s + 1) % s_count
    tap_rows = 9 * ch

    barrier = pltpu.get_barrier_semaphore()

    @pl.loop(1, s_count)
    def _(k):
        pl.semaphore_signal(barrier, inc=1, device_id=(z, (s + k) % s_count), device_id_type=MESH)

    @pl.loop(1, n)
    def _(k):
        pl.semaphore_signal(barrier, inc=1, device_id=((z + k) % n, s), device_id_type=MESH)

    w_copies = []
    for which, source in enumerate((w1_hbm, w2_hbm)):
        for d in range(n):
            block = source.at[:, d * ch:(d + 1) * ch] if aligned else source.at[d]
            w_copies.append(pltpu.make_async_copy(block, wv.at[which, d], w_sem.at[which, d]))
    for copy in w_copies:
        copy.start()

    def chunked(fn, init, first=0, count=cells):
        def step(i, carry):
            return fn(pl.multiple_of(first + i * CHUNK, CHUNK), CHUNK, carry)
        return lax.fori_loop(0, count // CHUNK, step, init, unroll=UNROLL)

    lanes = 128
    tiles = ch * wide // lanes

    def from_flat(flat, put):
        for i in range(tiles):
            turned[i * lanes:(i + 1) * lanes, 0:rows] = flat[:, i * lanes:(i + 1) * lanes].astype(F32).T
        for w in range(wide):
            put(pl.ds(w, rows, stride=wide), turned[pl.ds(w, ch, stride=wide), 0:rows].T)

    def to_flat(source, flat):
        for w in range(wide):
            turned[pl.ds(w, ch, stride=wide), 0:rows] = source[pl.ds(w, rows, stride=wide), :].T
        for i in range(tiles):
            flat[:, i * lanes:(i + 1) * lanes] = turned[i * lanes:(i + 1) * lanes, 0:rows].T.astype(flat.dtype)

    def put_masked(at, value):
        masked[at, :] = value

    from_flat(x_in, put_masked)

    cell = lax.broadcasted_iota(jnp.int32, (cells, rows), 0)
    pick = (cell // wide == lax.broadcasted_iota(jnp.int32, (cells, rows), 1)).astype(F32).astype(BF16)
    column_of = lax.broadcasted_iota(jnp.int32, (cells, wide), 0) % wide
    picked = lax.dot_general(pick, live_in[...].astype(BF16), (((1,), (1,)), ((), ())), preferred_element_type=F32)
    picked = jnp.where(column_of == lax.broadcasted_iota(jnp.int32, (cells, wide), 1), picked, 0.0)
    mask[0:cells, :] = dot(picked.astype(BF16), jnp.ones((wide, ch), BF16))

    def load_main(start, size, carry):
        at = pl.ds(start, size)
        lv = mask[at, :]
        masked[at, :] = masked[at, :] * lv
        return carry

    chunked(load_main, 0)
    for side, start in ((0, 0), (1, cells - wide)):
        edge_send[side, 0] = masked[start:start + wide, :].astype(BF16)
        edge_send[side, 1] = mask[start:start + wide, :].astype(BF16)

    acc[...] = jnp.zeros_like(acc)
    for block in range(n):
        for row in (rows // HALVES + 1, rows + 2):
            taken[block, row:row + 1, :, :] = jnp.zeros((1, wide, 3 * ch), BF16)
    st_send[...] = jnp.zeros_like(st_send)

    pl.semaphore_wait(barrier, s_count - 1 + n - 1)

    def edge_copy(side):
        return pltpu.make_async_remote_copy(
            src_ref=edge_send.at[side], dst_ref=edge_recv.at[1 - side],
            send_sem=e_ssem.at[side], recv_sem=e_rsem.at[1 - side],
            device_id=(z, before if side == 0 else after), device_id_type=MESH)

    for side in range(2):
        edge_copy(side).start()

    def cot_copy(side):
        return pltpu.make_async_remote_copy(
            src_ref=cot_send.at[side], dst_ref=cot_recv.at[1 - side],
            send_sem=ce_ssem.at[side], recv_sem=ce_rsem.at[1 - side],
            device_id=(z, before if side == 0 else after), device_id_type=MESH)

    def load_cotangent():
        def put(at, value):
            cotm[at, :] = value
        from_flat(cot_in, put)

        def live_only(start, size, carry):
            at = pl.ds(start, size)
            cotm[at, :] = cotm[at, :] * mask[at, :]
            return carry
        chunked(live_only, 0)
        for side, start in ((0, 0), (1, cells - wide)):
            cot_send[side] = cotm[start:start + wide, :].astype(BF16)
            cot_copy(side).start()

    def take_cotangent():
        for side in range(2):
            cot_copy(1 - side).wait_recv()
            at = slice(cells + side * wide, cells + (side + 1) * wide)
            cotm[at, :] = cot_recv[side].astype(F32) * mask[at, :]

    w_parts = math.gcd(tap_rows // 16, s_count)
    w_rows = tap_rows // w_parts
    w_mine = s % w_parts
    w_group = s - w_mine

    def wz_copy(which, k):
        at = pl.ds(w_mine * w_rows, w_rows)
        slot = n - k - 1
        return pltpu.make_async_remote_copy(
            src_ref=wv.at[which, (z + k) % n, at, :], dst_ref=wf.at[which, slot, at, :],
            send_sem=wz_ssem.at[which, slot], recv_sem=wz_rsem.at[which, slot],
            device_id=((z + k) % n, s), device_id_type=MESH)

    def wp_copy(which, slot, k, whose):
        at = pl.ds(whose * w_rows, w_rows)
        return pltpu.make_async_remote_copy(
            src_ref=wf.at[which, slot, at, :], dst_ref=wf.at[which, slot, at, :],
            send_sem=wp_ssem.at[which, slot, k], recv_sem=wp_rsem.at[which, slot, whose],
            device_id=(z, w_group + (w_mine + k) % w_parts), device_id_type=MESH)

    def weights_over_z(which):
        for copy in w_copies[which * n:(which + 1) * n]:
            copy.wait()

        @pl.loop(1, n)
        def _(k):
            wz_copy(which, k).start()

    def slot_of(block):
        return (block - z + n - 1) % n

    def weights_round(which):
        @pl.loop(1, n)
        def _(distance):
            for sign in (1, -1):
                block = z - distance * sign

                @pl.when((block >= 0) & (block < n))
                def _():
                    slot = slot_of(block)
                    wz_copy(which, n - 1 - slot).wait_recv()

                    @pl.loop(1, w_parts)
                    def _(k):
                        wp_copy(which, slot, k, w_mine).start()

    def weights_arrived(which, slot):
        @pl.loop(1, w_parts)
        def _(k):
            wp_copy(which, slot, k, (w_mine + k) % w_parts).wait_recv()

    def row_copy(slot, side):
        return pltpu.make_async_remote_copy(
            src_ref=row_send.at[slot, side], dst_ref=row_recv.at[slot, 1 - side],
            send_sem=row_ssem.at[slot, side], recv_sem=row_rsem.at[slot, 1 - side],
            device_id=(z, before if side == 0 else after), device_id_type=MESH)

    def send_row(slot, side):
        start = side * (cells - wide)
        row_send[slot, side] = acc[start:start + wide, :]
        row_copy(slot, side).start()

    settled = (rows // HALVES - 1) * wide

    def take_rows(slot, ref):
        for side in range(2):
            row_copy(slot, 1 - side).wait_recv()
            ref[cells + side * wide:cells + (side + 1) * wide, :] = row_recv[slot, side]

    def st_copy(slot, k, whose):
        return pltpu.make_async_remote_copy(
            src_ref=st_send.at[slot], dst_ref=st_recv.at[slot, whose],
            send_sem=st_ssem.at[slot, k], recv_sem=st_rsem.at[slot, whose],
            device_id=(z, (s + k) % s_count), device_id_type=MESH)

    def send_stats(slot, values):
        for i, v in enumerate(values):
            st_send[slot, i:i + 1, :] = v
        for k in range(1, s_count):
            st_copy(slot, k, s).start()
        st_recv[slot, s] = st_send[slot]

    def take_stats(slot):
        for k in range(1, s_count):
            st_copy(slot, k, (s + k) % s_count).wait_recv()

    strip = 8
    column = lax.broadcasted_iota(jnp.int32, (strip * wide, ch), 0) % wide

    def shift(target, first, count):
        size = count * wide
        where = column[:size]
        here = pad[pl.ds(8 + first * wide, size), :]
        left = jnp.where(where == 0, 0.0, pad[pl.ds(7 + first * wide, size), :])
        right = jnp.where(where == wide - 1, 0.0, pad[pl.ds(9 + first * wide, size), :])
        for b, v in enumerate((left, here, right)):
            target[pl.ds(first, count), :, b * ch:(b + 1) * ch] = v.astype(BF16).reshape(count, wide, ch)

    edge = 2 * wide
    ag_rows = ((0, edge + packed), (edge + packed, packed))
    band_rows = rows // HALVES

    def unpack_half(ph, block, q, target):
        if q == 0:
            pad[8:8 + wide, :] = hold[ph, block, 0:wide, :].astype(F32)
            pad[8 + wide + cells:8 + 2 * wide + cells, :] = hold[ph, block, wide:edge, :].astype(F32)
            shift(target, 0, 1)
            shift(target, rows + 1, 1)
        for j in range(2):
            start = edge + q * packed + j * (packed - unpack.shape[3])
            at = 8 + wide + q * band + j * (band // 2)
            pad[at:at + band // 2, :] = dot(unpack[q, j], hold[ph, block, start:start + unpack.shape[3], :])

        for i in range(band_rows // strip):
            shift(target, 1 + q * band_rows + i * strip, strip)

    def add_conv(q, field, taps, turned_taps=None):
        first, last = (0, band_rows - 1) if q == 0 else (band_rows - 1, rows)
        count = last - first
        size = (count + 2) * wide
        lhs = jnp.concatenate([
            field[first + i:last + 2 + i, :, :].reshape(size, 3 * ch) for i in range(2)], axis=1)
        if turned_taps is None:
            none = jnp.zeros((3 * ch, ch), BF16)
            rhs = jnp.concatenate([
                jnp.concatenate([taps(0), taps(2)], axis=1), jnp.concatenate([taps(1), none], axis=1)], axis=0)
            value = dot(lhs, rhs)
        else:
            def row_taps(a):
                return [turned_taps(3 * (2 - a) + 2 - b) for b in range(3)]
            none = jnp.zeros((ch, 3 * ch), BF16)
            rhs = jnp.concatenate([
                jnp.concatenate(row_taps(0) + row_taps(1), axis=1), jnp.concatenate(row_taps(2) + [none], axis=1)], axis=0)
            value = lax.dot_general(lhs, rhs, (((1,), (1,)), ((), ())), preferred_element_type=F32)
        at = pl.ds(first * wide, count * wide)
        acc[at, :] = acc[at, :] + value[0:count * wide, 0:ch] + value[2 * wide:size, ch:2 * ch]

    def ag_copy(ph, block, q, sign):
        at = pl.ds(*ag_rows[q])
        return pltpu.make_async_remote_copy(
            src_ref=hold.at[ph, block, at, :], dst_ref=hold.at[ph, block, at, :],
            send_sem=ag_ssem.at[ph, (1 - sign) // 2, block, q], recv_sem=ag_rsem.at[ph, block, q],
            device_id=(z + sign, s), device_id_type=MESH)

    def pack_field(ph, source, fill=None, first=None):
        if fill is not None:
            fill(cells, edge, 0)
        hold[ph, z, 0:edge, :] = source[cells:cells + edge, :].astype(BF16)
        for q in range(HALVES):
            if first is not None:
                first(q)
            if fill is not None:
                chunked(fill, 0, q * band, band)
            hold[ph, z, edge + q * packed:edge + (q + 1) * packed, :] = dot(
                pack[q], source[q * band:(q + 1) * band, :].astype(BF16)).astype(BF16)
            for sign in (1, -1):
                @pl.when((z + sign >= 0) & (z + sign < n))
                def _():
                    ag_copy(ph, z, q, sign).start()

    def inside(slice_at):
        return (slice_at >= 0) & (slice_at < n)

    def take_and_pass(ph, k, q, sign, passes=True, takes=True):
        block = z - k * sign

        @pl.when((k > 0) & inside(block))
        def _():
            if passes and takes:
                ag_copy(ph, block, q, sign).wait_recv()

            @pl.when(inside(z + sign))
            def _():
                if passes:
                    if not takes:
                        ag_copy(ph, block, q, sign).wait_recv()
                    ag_copy(ph, block, q, sign).start()

            if not passes:
                @pl.when(jnp.logical_not(inside(z + sign)))
                def _():
                    ag_copy(ph, block, q, sign).wait_recv()

    near = jnp.where(z < n - n // 2, 1, 0)

    def consume_way(k, q, way, consume):
        block = z - k * (1 - 2 * way)

        @pl.when((k >= 0) & (k < n) & inside(block) & ((k > 0) | (way == near)))
        def _():
            consume(k, block, q)

    def take_both(ph, k, q, **how):
        @pl.loop(0, 2)
        def _(i):
            way = (near + i) % 2
            take_and_pass(ph, k, q, 1 - 2 * way, **how)

    def gather(ph, consume, each):
        @pl.loop(0, n)
        def _(k):
            for q in range(HALVES):
                take_both(ph, k, q)
                if q:
                    consume_way(k, q - 1, 1 - near, consume)
                else:
                    consume_way(k - 1, HALVES - 1, 1 - near, consume)
                consume_way(k, q, near, consume)
            each(k)

    def gather_passing_first(ph, consume, each):
        @pl.loop(0, n)
        def _(k):
            @pl.when(k == 1)
            def _():
                @pl.loop(1, n)
                def _(ahead):
                    for q in range(HALVES):
                        take_both(ph, ahead, q, takes=False)
            for q in range(HALVES):
                take_both(ph, k, q, passes=False)

                @pl.loop(0, 2)
                def _(i):
                    consume_way(k, q, (near + i) % 2, consume)
            each(k)

    last_step = jnp.maximum(z, n - 1 - z)

    last_pass = jnp.maximum(jnp.where(z < n - 1, z, 0), jnp.where(z > 0, n - 1 - z, 0))

    def forward(ph, field):
        def consume(k, block, q):
            into = taken.at[block]
            unpack_half(ph, block, q, into)

            @pl.when(k == 0)
            def _():
                add_conv(q, into, lambda a: wv[ph, z, 3 * a * ch:3 * (a + 1) * ch, :])

            @pl.when(k > 0)
            def _():
                slot = slot_of(block)
                if q == 0:
                    weights_arrived(ph, slot)
                add_conv(q, into, lambda a: wf[ph, slot, 3 * a * ch:3 * (a + 1) * ch, :])

            if q == 0:
                pl.when(k == last_step)(lambda: early_moments(ph))

        def each(k):
            if ph == 0:
                @pl.when(k == 0)
                def _():
                    weights_round(0)

                @pl.when(k == 1)
                def _():
                    weights_over_z(1)

                @pl.when(k == last_pass)
                def _():
                    load_cotangent()
        (gather if ph else gather_passing_first)(ph, consume, each)

    def turn_field(ph, field):
        main = [field[start:start + ch, :].T for start in range(0, cells, ch)]
        ends = field[cells:cells + edge, :]
        if edge < ch:
            ends = jnp.concatenate([ends, jnp.zeros((ch - edge, ch), F32)], axis=0)
        ends = ends.T
        for i, here in enumerate(main):
            left = jnp.concatenate(
                [ends[:, 0:wide] if i == 0 else main[i - 1][:, ch - wide:], here[:, 0:ch - wide]], axis=1)
            right = jnp.concatenate(
                [here[:, wide:], main[i + 1][:, 0:wide] if i + 1 < len(main) else ends[:, wide:edge]], axis=1)
            for a, v in enumerate((left, here, right)):
                x_t[ph, a * ch:(a + 1) * ch, i * ch:(i + 1) * ch] = v.astype(BF16)

    half_rows = tap_rows // 2
    owners = math.gcd(half_rows // 16, chips)
    piece = half_rows // owners

    def c_copy(ph, j):
        return pltpu.make_async_remote_copy(
            src_ref=psend.at[ph, j], dst_ref=crecv.at[ph, j],
            send_sem=c_ssem.at[ph, j], recv_sem=c_rsem.at[ph, j],
            device_id=(z, chip * 2 + 1 - core), device_id_type=MESH)

    def q_copy(ph, j, e, whose, owner):
        return pltpu.make_async_remote_copy(
            src_ref=hsend.at[ph, j, owner], dst_ref=qrecv.at[ph, j, whose],
            send_sem=q_ssem.at[ph, j, e], recv_sem=q_rsem.at[ph, j, whose],
            device_id=(z, ((chip + e) % chips) * 2 + core), device_id_type=MESH)

    def f_copy(ph, j, e, owner):
        return pltpu.make_async_remote_copy(
            src_ref=wout.at[ph, j, core, owner], dst_ref=wout.at[ph, j, core, owner],
            send_sem=f_ssem.at[ph, j, e], recv_sem=f_rsem.at[ph, j, owner],
            device_id=(z, ((chip + e) % chips) * 2 + core), device_id_type=MESH)

    def h_copy(ph, j, whose):
        return pltpu.make_async_remote_copy(
            src_ref=wout.at[ph, j, whose], dst_ref=wout.at[ph, j, whose],
            send_sem=h_ssem.at[ph, j], recv_sem=h_rsem.at[ph, j],
            device_id=(z, chip * 2 + 1 - core), device_id_type=MESH)

    def o_copy(ph, j):
        target = (out_wg1, out_wg2)[ph]
        if aligned:
            target = target.at[:, :, :, pl.ds(pl.multiple_of(j * ch, ch), ch)]
        else:
            target = target.at[j]
        return pltpu.make_async_copy(wout.at[ph, j], target, o_sem.at[ph, j])

    def sum_cores(ph, j):
        for o in range(owners):
            psend[ph, j, o] = part[ph, j, 1 - core, o].astype(BF16)
        c_copy(ph, j).start()

    def sum_chips(ph, j):
        c_copy(ph, j).wait_recv()
        for o in range(owners):
            v = part[ph, j, core, o] + crecv[ph, j, o].astype(F32)
            part[ph, j, core, o] = v
            hsend[ph, j, o] = v.astype(BF16)

        @pl.loop(1, chips)
        def _(e):
            peer = (chip + e) % chips

            @pl.when(peer < owners)
            def _():
                q_copy(ph, j, e, chip, peer).start()

    def spread_chips(ph, j):
        @pl.when(chip < owners)
        def _():
            @pl.loop(1, chips)
            def _(e):
                q_copy(ph, j, e, (chip + e) % chips, chip).wait_recv()
            v = part[ph, j, core, chip]
            for e in range(1, chips):
                v = v + qrecv[ph, j, (chip + e) % chips].astype(F32)
            wout[ph, j, core, chip] = v.astype(BF16)

            @pl.loop(1, chips)
            def _(e):
                f_copy(ph, j, e, chip).start()

    def spread_cores(ph, j):
        @pl.loop(1, chips)
        def _(e):
            peer = (chip + e) % chips

            @pl.when(peer < owners)
            def _():
                f_copy(ph, j, e, peer).wait_recv()
        h_copy(ph, j, core).start()

    def finish(ph, j):
        h_copy(ph, j, 1 - core).wait_recv()
        o_copy(ph, j).start()

    def put_part(ph, j, tap, value):
        start = tap * ch
        done = 0
        while done < ch:
            row = start + done
            side, o, at = row // half_rows, row % half_rows // piece, row % piece
            size = min(ch - done, piece - at)
            part[ph, j, side, o, at:at + size, :] = value[done:done + size, :]
            done += size

    stages = (sum_cores, sum_chips, spread_chips, spread_cores, finish)

    def of_step(k, fn):
        @pl.loop(0, 2)
        def _(way):
            block = z - k * (1 - 2 * way)

            @pl.when((k >= 0) & (k < n) & inside(block) & ((k > 0) | (way == 0)))
            def _():
                fn(block)

    passing = last_pass > 0

    def made_at(step):
        first = jnp.where(passing & (step > 0), jnp.where(step == last_pass, 1, step + 1), step)
        return first, step + 1

    def advance(ph, k):
        for age in range(1, len(stages)):
            step = k - age

            @pl.when((step >= 0) & (step < n))
            def _():
                @pl.loop(*made_at(step))
                def _(made):
                    of_step(made, functools.partial(stages[age], ph))

    def advance_all(ph, age):
        @pl.loop(0, n)
        def _(j):
            stages[age](ph, j)

    def field_grad(ph, block):
        grad = taken[block, 1:rows + 1, :, :].reshape(cells, 3 * ch)
        value = dot(x_t[ph], grad)
        for a in range(3):
            for b in range(3):
                put_part(ph, block, 3 * a + b, value[a * ch:(a + 1) * ch, (2 - b) * ch:(3 - b) * ch])

    def make_grad(ph, block):
        field_grad(ph, block)
        sum_cores(ph, block)

    def inner_sums(first, last, side):
        start = side * (cells - wide)
        row_send[2, side] = acc[start:start + wide, :]
        at = slice(first, last)
        v = acc[at, :] * slope1[at, :]
        slope1[at, :] = v
        acc[at, :] = jnp.zeros((last - first, ch), F32)
        return fold(v * normed1[at, :]), fold(v)

    def early_inner():
        for i, v in enumerate(inner_sums(0, settled, 0)):
            early[8 * i:8 * i + 8, :] = v
        row_copy(2, 0).start()

    def backward(ph):
        last = ph == 0

        def consume(k, block, q):
            into = taken.at[block]
            unpack_half(2 + ph, block, q, into)
            if last and q == HALVES - 1:
                @pl.when((k == 0) | (k >= last_pass))
                def _():
                    make_grad(ph, block)
            add_conv(q, into, None, lambda t: wv[ph, block, t * ch:(t + 1) * ch, :])
            if q == 0 and not last:
                pl.when(k == last_step)(early_inner)

        def each(k):
            first, end = made_at(k)
            if last:
                @pl.loop(first, end - 1)
                def _(step):
                    of_step(step, functools.partial(make_grad, ph))
                advance(ph, k)
                for age in range(2, len(stages)):
                    @pl.when(k == age - 2)
                    def _():
                        advance_all(1, age)
            else:
                @pl.loop(first, jnp.where(passing | (k < n - 1), end, first))
                def _(step):
                    of_step(step, functools.partial(make_grad, ph))
        gather(2 + ph, consume, each)

    def fold(v):
        return jnp.sum(v.reshape(v.shape[0] // 8, 8, ch), axis=0)

    def flatten(v):
        return jnp.sum(v, axis=0, keepdims=True)

    zero = jnp.zeros((8, ch), F32)

    def part_moments(first, last):
        m = mask[first:last, :]
        v = acc[first:last, :]
        number, added = flatten(fold(m)), flatten(fold(v * m))
        c = (v - added / jnp.maximum(number, 1.0)) * m
        return added, number, flatten(fold(c * c))

    def early_moments(slot):
        for i, v in enumerate(part_moments(0, settled)):
            early[i:i + 1, :] = v
        send_row(slot, 0)

    def combine(added, number, spread):
        total_added, total_number = sum(added), sum(number)
        mean = total_added / jnp.maximum(total_number, 1.0)
        about = 0.0
        for a, k, q in zip(added, number, spread):
            off = a / jnp.maximum(k, 1.0) - mean
            about = about + (q + k * off * off)
        return total_added, total_number, about

    def local_moments():
        late = part_moments(settled, cells)
        return combine(*([early[i:i + 1, :], v] for i, v in enumerate(late)))

    def moments(slot):
        take_stats(slot)
        added, number, about = (st_recv[slot, :, i, :] for i in range(3))
        count = flatten(number)
        mean = flatten(added) / count
        off = added / jnp.maximum(number, 1.0) - mean
        return mean, lax.rsqrt(flatten(about + number * off * off) / count + EPSILON), count

    def everywhere(fn):
        chunked(fn, 0)
        fn(cells, 2 * wide, 0)

    gain1, shift1, gain2, shift2 = (r[...] for r in (gain1_in, shift1_in, gain2_in, shift2_in))

    weights_over_z(0)

    quarter = band // 2
    kept = packed // 2
    window = unpack.shape[3]
    below = lax.broadcasted_iota(jnp.int32, (quarter, quarter), 1) < lax.broadcasted_iota(jnp.int32, (quarter, quarter), 0)
    below = below.astype(F32).astype(BF16)

    def make_pack(h):
        for j in range(2):
            lv = mask[h * band + j * quarter:h * band + (j + 1) * quarter, :]
            place = jnp.where(lv > 0.0, dot(below, lv.astype(BF16)) + j * kept, -1.0)
            places[h, j] = place
            across = place.T[0:1, :]
            spot = lax.broadcasted_iota(jnp.int32, (packed, quarter), 0).astype(F32)
            pack[h, :, j * quarter:(j + 1) * quarter] = jnp.where(spot == across, 1.0, 0.0).astype(BF16)

    def make_unpack(h):
        for j in range(2):
            for start in range(0, window, ch):
                size = min(ch, window - start)
                spot = start + j * (packed - window) + lax.broadcasted_iota(jnp.int32, (quarter, size), 1)
                unpack[h, j, :, start:start + size] = jnp.where(
                    places[h, j, :, :size] == spot.astype(F32), 1.0, 0.0).astype(BF16)

    for side in range(2):
        edge_copy(1 - side).wait_recv()
        there = jnp.where(s > 0, 1.0, 0.0) if side == 0 else jnp.where(s < s_count - 1, 1.0, 0.0)
        at = slice(cells + side * wide, cells + (side + 1) * wide)
        masked[at, :] = edge_recv[side, 0].astype(F32) * there
        mask[at, :] = edge_recv[side, 1].astype(F32) * there

    def stats_sent(slot):
        for k in range(1, s_count):
            st_copy(slot, k, s).wait_send()

    def row_sent(slot):
        for side in range(2):
            row_copy(slot, side).wait_send()

    def gathered_sent(ph):
        @pl.loop(0, n)
        def _(k):
            for sign in (1, -1):
                block = z - k * sign

                @pl.when(inside(block) & inside(z + sign))
                def _():
                    for q in range(HALVES):
                        ag_copy(ph, block, q, sign).wait_send()

    def weights_sent(which):
        for k in range(1, n):
            wz_copy(which, k).wait_send()

        @pl.loop(1, w_parts)
        def _(k):
            for slot in range(n - 1):
                wp_copy(which, slot, k, w_mine).wait_send()

    def grads_sent(ph):
        @pl.loop(0, n)
        def _(j):
            c_copy(ph, j).wait_send()
            h_copy(ph, j, core).wait_send()
            o_copy(ph, j).wait()
            for e in range(1, chips):
                peer = (chip + e) % chips

                @pl.when(peer < owners)
                def _():
                    q_copy(ph, j, e, chip, peer).wait_send()

                @pl.when(chip < owners)
                def _():
                    f_copy(ph, j, e, chip).wait_send()

    block_copy = pltpu.make_async_copy(flat_block, out_block, r_sem.at[0])

    pack_field(0, masked, first=make_pack)
    for h in range(HALVES):
        make_unpack(h)
    forward(0, masked)
    send_stats(0, local_moments())
    send_row(0, 1)
    weights_round(1)
    mean1, scale1, count = moments(0)

    def activate_one(start, size, carry):
        at = pl.ds(start, size)
        main = start is not cells
        nv = ((acc if main else normed1)[at, :] - mean1) * scale1
        normed1[at, :] = nv
        hid[at, :] = gelu_parts(nv * gain1 + shift1)[0] * mask[at, :]
        if main:
            acc[at, :] = jnp.zeros((size, ch), F32)
        return carry

    def slope_one(start, size, carry):
        at = pl.ds(start, size)
        slope1[at, :] = gelu_parts(normed1[at, :] * gain1 + shift1)[1] * mask[at, :]
        return carry

    take_rows(0, normed1)
    pack_field(1, hid, activate_one)
    everywhere(slope_one)
    forward(1, hid)
    send_stats(1, local_moments())
    send_row(1, 1)
    turn_field(0, masked)
    turn_field(1, hid)
    weights_sent(0)
    gathered_sent(0)
    stats_sent(0)
    row_sent(0)
    for side in range(2):
        edge_copy(side).wait_send()
        cot_copy(side).wait_send()
    mean2, scale2, _ = moments(1)

    def activate_two(source, start, size):
        at = pl.ds(start, size)
        nv = (source[at, :] - mean2) * scale2
        normed2[at, :] = nv
        value, slope = gelu_parts(nv * gain2 + shift2 + masked[at, :])
        t = cotm[at, :] * slope
        through[at, :] = t
        return value, nv, t

    def activate_main(start, size, carry):
        value, nv, t = activate_two(acc, start, size)
        at = pl.ds(start, size)
        hid2[at, :] = value * mask[at, :]
        acc[at, :] = jnp.zeros((size, ch), F32)
        return carry[0] + fold(t * nv), carry[1] + fold(t)

    send_stats(2, [flatten(v) for v in chunked(activate_main, (zero, zero))])
    take_rows(1, normed2)
    take_cotangent()
    activate_two(normed2, cells, edge)
    to_flat(hid2, flat_block)
    block_copy.start()
    weights_sent(1)
    gathered_sent(1)

    def gradient_sums(slot):
        take_stats(slot)
        return flatten(st_recv[slot, :, 0, :]), flatten(st_recv[slot, :, 1, :])

    def norm_back(upstream, normed, gain, scale, sums):
        gain_grad, shift_grad = sums
        factor = gain * scale
        level, tilt = shift_grad / count, gain_grad / count

        def fill(start, size, carry):
            at = pl.ds(start, size)
            v = upstream[at, :] - mask[at, :] * (level + normed[at, :] * tilt)
            hid[at, :] = factor * v
            return carry
        return fill

    sums2 = gradient_sums(2)
    pack_field(3, hid, norm_back(through, normed2, gain2, scale2, sums2))
    backward(1)

    parts = inner_sums(settled, cells, 1)
    send_stats(3, [flatten(early[8 * i:8 * i + 8, :] + v) for i, v in enumerate(parts)])
    row_copy(2, 1).start()

    @pl.when(jnp.logical_not(passing))
    def _():
        of_step(n - 1, functools.partial(make_grad, 1))
    for side in range(2):
        row_copy(2, 1 - side).wait_recv()
        at = slice(cells + side * wide, cells + (side + 1) * wide)
        slope1[at, :] = row_recv[2, side] * slope1[at, :]
    stats_sent(1)
    row_sent(1)
    stats_sent(2)
    gathered_sent(3)
    sums1 = gradient_sums(3)
    pack_field(2, hid, norm_back(slope1, normed1, gain1, scale1, sums1))
    advance_all(1, 1)
    backward(0)
    advance(0, n)

    def finish_input(start, size, carry):
        at = pl.ds(start, size)
        acc[at, :] = (acc[at, :] + through[at, :]) * mask[at, :]
        return carry

    chunked(finish_input, 0)
    to_flat(acc, flat_input)
    input_copy = pltpu.make_async_copy(flat_input, out_input, r_sem.at[1])
    input_copy.start()
    out_gain1[...], out_shift1[...] = sums1
    out_gain2[...], out_shift2[...] = sums2
    for extra in range(1, len(stages) - 1):
        advance(0, n + extra)

    stats_sent(3)
    row_sent(2)
    gathered_sent(2)
    grads_sent(1)
    grads_sent(0)
    block_copy.wait()
    input_copy.wait()


def finish_kernel(count, *refs):
    ins, outs = refs[:count], refs[count:2 * count]
    narrow, wide, in_sem, out_sem, take_sem, give_sem = refs[2 * count:2 * count + 6]
    held = refs[2 * count + 6:]
    rows = narrow.shape[1] // FINISH_PARTS
    parts = [(w, i, pl.ds(i * rows, rows)) for i in range(FINISH_PARTS) for w in range(2)]
    loads = [pltpu.make_async_copy(ins[w].at[at, :], narrow.at[w, at, :], in_sem.at[w, i]) for w, i, at in parts]
    stores = [pltpu.make_async_copy(wide.at[w, at, :], outs[w].at[at, :], out_sem.at[w, i]) for w, i, at in parts]
    takes = [pltpu.make_async_copy(ins[2 + k], v, take_sem.at[k]) for k, v in enumerate(held)]
    gives = [pltpu.make_async_copy(v, outs[2 + k], give_sem.at[k]) for k, v in enumerate(held)]
    for copy in loads + takes:
        copy.start()
    for load, store, (w, i, at) in zip(loads, stores, parts):
        load.wait()
        wide[w, at, :] = narrow[w, at, :].astype(F32)
        store.start()
    for take, give in zip(takes, gives):
        take.wait()
        give.start()
    for copy in stores + gives:
        copy.wait()


def per_device(n, s_count, blocks, weight_one, weight_two, gain_one, shift_one, gain_two, shift_two, cell_live, cotangent):
    rows, wide = cell_live.shape
    ch = blocks.shape[1] // wide
    cells = rows * wide
    total = cells + 2 * wide
    packed = 2 * -(-most_live(rows // HALVES // 2, wide) // 8) * 8
    aligned = ch % 128 == 0
    chips = s_count // 2
    tap_rows = 9 * ch
    half_rows = tap_rows // 2
    owners = math.gcd(half_rows // 16, chips)
    piece = half_rows // owners

    if aligned:
        weight_one, weight_two = (w.reshape(tap_rows, n * ch) for w in (weight_one, weight_two))
    else:
        weight_one, weight_two = (
            w.reshape(tap_rows, n, ch).transpose(1, 0, 2) for w in (weight_one, weight_two))
    grad_shape = (2, owners, piece, n * ch) if aligned else (n, 2, owners, piece, ch)
    vmem = pl.BlockSpec(memory_space=pltpu.VMEM)
    hbm = pl.BlockSpec(memory_space=pl.ANY)
    sem = pltpu.SemaphoreType.DMA
    field = pltpu.VMEM((total, ch), F32)
    scratch = [
        pltpu.VMEM((ch * wide, 128), F32),
        pltpu.VMEM((2, n, tap_rows, ch), BF16),
        pltpu.VMEM((2, n - 1, tap_rows, ch), BF16),
        pltpu.VMEM((2, 3 * ch, cells), BF16),
        pltpu.VMEM((HALVES, packed, cells // HALVES), BF16),
        pltpu.VMEM((HALVES, 2, cells // HALVES // 2, -(-packed // 2 // 16) * 16), BF16),
        pltpu.VMEM((HALVES, 2, cells // HALVES // 2, ch), F32),
        pltpu.VMEM((2, 2, wide, ch), BF16),
        pltpu.VMEM((2, 2, wide, ch), BF16),
        pltpu.VMEM((2, wide, ch), BF16),
        pltpu.VMEM((2, wide, ch), BF16),
        field, field, field, field, field, field, field, field, field,
        pltpu.VMEM((total + 16, ch), F32),
        pltpu.VMEM((cells, ch), F32),
        pltpu.VMEM((4, n, 2 * wide + HALVES * packed, ch), BF16),
        pltpu.VMEM((n, rows + 3, wide, 3 * ch), BF16),
        pltpu.VMEM((2, n, 2, owners, piece, ch), F32),
        pltpu.VMEM((2, n, owners, piece, ch), BF16),
        pltpu.VMEM((2, n, owners, piece, ch), BF16),
        pltpu.VMEM((2, n, owners, piece, ch), BF16),
        pltpu.VMEM((2, n, chips, piece, ch), BF16),
        pltpu.VMEM((2, n, 2, owners, piece, ch), BF16),
        pltpu.VMEM((4, 8, ch), F32),
        pltpu.VMEM((4, s_count, 8, ch), F32),
        pltpu.VMEM((3, 2, wide, ch), F32),
        pltpu.VMEM((3, 2, wide, ch), F32),
        pltpu.VMEM((16, ch), F32),
        pltpu.VMEM((rows, ch * wide), BF16),
        pltpu.VMEM((rows, ch * wide), F32),
        sem((2, n)),
        sem((2, n)), sem((2, n)),
        sem((2, n - 1, s_count)), sem((2, n - 1, s_count)),
        sem((2,)), sem((2,)),
        sem((2,)), sem((2,)),
        sem((4, 2, n, HALVES)), sem((4, n, HALVES)),
        sem((4, s_count)), sem((4, s_count)),
        sem((3, 2)), sem((3, 2)),
        sem((2, n)), sem((2, n)),
        sem((2, n, chips)), sem((2, n, chips)),
        sem((2, n, chips)), sem((2, n, chips)),
        sem((2, n)), sem((2, n)),
        sem((2, n)),
        sem((2,)),
    ]
    block_out, input_grad, wg1, wg2, *sums = pl.pallas_call(
        functools.partial(block_kernel, n, s_count, rows, wide, ch, aligned, packed),
        out_shape=(
            jax.ShapeDtypeStruct((rows, ch * wide), BF16),
            jax.ShapeDtypeStruct((rows, ch * wide), F32),
            jax.ShapeDtypeStruct(grad_shape, BF16),
            jax.ShapeDtypeStruct(grad_shape, BF16),
            *[jax.ShapeDtypeStruct((1, ch), F32)] * 4,
        ),
        in_specs=[vmem] * 7 + [hbm] * 2,
        out_specs=(hbm, hbm, hbm, hbm, vmem, vmem, vmem, vmem),
        scratch_shapes=scratch,
        compiler_params=pltpu.CompilerParams(
            collective_id=0, has_side_effects=True, vmem_limit_bytes=60 * 1024 * 1024),
    )(blocks, cotangent, cell_live.T,
      *(v.reshape(1, ch) for v in (gain_one, shift_one, gain_two, shift_two)), weight_one, weight_two)

    if not aligned:
        def whole(grad):
            grad = grad.reshape(n, tap_rows, ch).transpose(1, 0, 2)
            return grad.astype(F32).reshape(9, ch, n * ch)
        return (block_out, input_grad, whole(wg1), whole(wg2), *(v.reshape(ch) for v in sums))

    wg1, wg2 = (w.reshape(tap_rows, n * ch) for w in (wg1, wg2))
    wide_grad = jax.ShapeDtypeStruct((tap_rows, n * ch), F32)
    moved = (block_out, input_grad, *sums)
    grad1, grad2, *moved = pl.pallas_call(
        functools.partial(finish_kernel, 2 + len(moved)),
        out_shape=(wide_grad, wide_grad, *(jax.ShapeDtypeStruct(v.shape, v.dtype) for v in moved)),
        in_specs=[pl.BlockSpec(memory_space=pl.ANY)] * (2 + len(moved)),
        out_specs=[pl.BlockSpec(memory_space=pl.ANY)] * (2 + len(moved)),
        scratch_shapes=[
            pltpu.VMEM((2, tap_rows, n * ch), BF16), pltpu.VMEM((2, tap_rows, n * ch), F32),
            sem((2, FINISH_PARTS)), sem((2, FINISH_PARTS)), sem((len(moved),)), sem((len(moved),)),
            *(pltpu.VMEM(v.shape, v.dtype) for v in moved),
        ],
        compiler_params=pltpu.CompilerParams(vmem_limit_bytes=64 * 1024 * 1024),
    )(wg1, wg2, *moved)
    block_out, input_grad, *sums = moved
    grads = (g.reshape(9, ch, n * ch) for g in (grad1, grad2))
    return (block_out, input_grad, *grads, *(v.reshape(ch) for v in sums))


def solution(mesh):
    return jax.shard_map(
        functools.partial(per_device, mesh.shape["chan"], mesh.shape["space"]),
        mesh=mesh,
        in_specs=(
            P("space", "chan"),
            P(None, "chan", None),
            P(None, "chan", None),
            P("chan"),
            P("chan"),
            P("chan"),
            P("chan"),
            P("space", None),
            P("space", "chan"),
        ),
        out_specs=(
            P("space", "chan"),
            P("space", "chan"),
            P(None, "chan", None),
            P(None, "chan", None),
            P("chan"),
            P("chan"),
            P("chan"),
            P("chan"),
        ),
        check_vma=False,
    )
```

```python
import functools
import math

import jax
import jax.numpy as jnp
from jax import lax
from jax.experimental import pallas as pl
from jax.experimental.pallas import tpu as pltpu
from jax.sharding import PartitionSpec as P

EPSILON = 1e-05
MESH = pl.DeviceIdType.MESH
F32 = jnp.float32
BF16 = jnp.bfloat16
ROOT_HALF = 0.7071067811865476
ROOT_TWO_PI = 0.3989422804014327
CHUNK = 64
FINISH_PARTS = 4
UNROLL = 2
HALVES = 2
LARGE, SMALL = 7, 3


def dot(a, b):
    return jnp.dot(a, b, preferred_element_type=F32)


def gelu_parts(v):
    upper = 0.5 * (1.0 + lax.erf(v * ROOT_HALF))
    slope = upper + v * (ROOT_TWO_PI * jnp.exp(-0.5 * v * v))
    return v * upper, slope


def most_live(rows, wide):
    units = (wide + 1) // (SMALL + 1)
    live_rows = rows - rows // (LARGE + 1)
    return min(rows * wide, math.ceil(units * live_rows * LARGE / 2))


def block_kernel(n, s_count, rows, wide, ch, aligned, packed, *refs):
    (x_in, cot_in, live_in, gain1_in, shift1_in, gain2_in, shift2_in, w1_hbm, w2_hbm) = refs[:9]
    (out_block, out_input, out_wg1, out_wg2, out_gain1, out_shift1, out_gain2, out_shift2) = refs[9:17]
    (turned, wv, wf, x_t, pack, unpack, places, edge_send, edge_recv, cot_send, cot_recv, cotm, mask, masked,
     normed1, normed2, through, slope1, hid, hid2, pad, acc, hold, taken,
     part, psend, crecv, hsend, qrecv, wout, st_send, st_recv, row_send, row_recv, early, flat_block, flat_input,
     w_sem, wz_ssem, wz_rsem, wp_ssem, wp_rsem, e_ssem, e_rsem, ce_ssem, ce_rsem, ag_ssem, ag_rsem,
     st_ssem, st_rsem, row_ssem, row_rsem, c_ssem, c_rsem, q_ssem, q_rsem,
     f_ssem, f_rsem, h_ssem, h_rsem, o_sem, r_sem) = refs[17:]

    z = lax.axis_index("chan")
    s = lax.axis_index("space")
    cells = rows * wide
    total = cells + 2 * wide
    band = cells // HALVES
    core, chip, chips = s % 2, s // 2, s_count // 2
    before, after = (s + s_count - 1) % s_count, (s + 1) % s_count
    tap_rows = 9 * ch

    barrier = pltpu.get_barrier_semaphore()

    @pl.loop(1, s_count)
    def _(k):
        pl.semaphore_signal(barrier, inc=1, device_id=(z, (s + k) % s_count), device_id_type=MESH)

    @pl.loop(1, n)
    def _(k):
        pl.semaphore_signal(barrier, inc=1, device_id=((z + k) % n, s), device_id_type=MESH)

    w_copies = []
    for which, source in enumerate((w1_hbm, w2_hbm)):
        for d in range(n):
            block = source.at[:, d * ch:(d + 1) * ch] if aligned else source.at[d]
            w_copies.append(pltpu.make_async_copy(block, wv.at[which, d], w_sem.at[which, d]))
    for copy in w_copies:
        copy.start()

    def chunked(fn, init, first=0, count=cells):
        def step(i, carry):
            return fn(pl.multiple_of(first + i * CHUNK, CHUNK), CHUNK, carry)
        return lax.fori_loop(0, count // CHUNK, step, init, unroll=UNROLL)

    lanes = 128
    tiles = ch * wide // lanes

    def from_flat(flat, put):
        for i in range(tiles):
            turned[i * lanes:(i + 1) * lanes, 0:rows] = flat[:, i * lanes:(i + 1) * lanes].astype(F32).T
        for w in range(wide):
            put(pl.ds(w, rows, stride=wide), turned[pl.ds(w, ch, stride=wide), 0:rows].T)

    def to_flat(source, flat):
        for w in range(wide):
            turned[pl.ds(w, ch, stride=wide), 0:rows] = source[pl.ds(w, rows, stride=wide), :].T
        for i in range(tiles):
            flat[:, i * lanes:(i + 1) * lanes] = turned[i * lanes:(i + 1) * lanes, 0:rows].T.astype(flat.dtype)

    def put_masked(at, value):
        masked[at, :] = value

    from_flat(x_in, put_masked)

    cell = lax.broadcasted_iota(jnp.int32, (cells, rows), 0)
    pick = (cell // wide == lax.broadcasted_iota(jnp.int32, (cells, rows), 1)).astype(F32).astype(BF16)
    column_of = lax.broadcasted_iota(jnp.int32, (cells, wide), 0) % wide
    picked = lax.dot_general(pick, live_in[...].astype(BF16), (((1,), (1,)), ((), ())), preferred_element_type=F32)
    picked = jnp.where(column_of == lax.broadcasted_iota(jnp.int32, (cells, wide), 1), picked, 0.0)
    mask[0:cells, :] = dot(picked.astype(BF16), jnp.ones((wide, ch), BF16))

    def load_main(start, size, carry):
        at = pl.ds(start, size)
        lv = mask[at, :]
        masked[at, :] = masked[at, :] * lv
        return carry

    chunked(load_main, 0)
    for side, start in ((0, 0), (1, cells - wide)):
        edge_send[side, 0] = masked[start:start + wide, :].astype(BF16)
        edge_send[side, 1] = mask[start:start + wide, :].astype(BF16)

    acc[...] = jnp.zeros_like(acc)
    for block in range(n):
        for row in (rows // HALVES + 1, rows + 2):
            taken[block, row:row + 1, :, :] = jnp.zeros((1, wide, 3 * ch), BF16)
    st_send[...] = jnp.zeros_like(st_send)

    pl.semaphore_wait(barrier, s_count - 1 + n - 1)

    def edge_copy(side):
        return pltpu.make_async_remote_copy(
            src_ref=edge_send.at[side], dst_ref=edge_recv.at[1 - side],
            send_sem=e_ssem.at[side], recv_sem=e_rsem.at[1 - side],
            device_id=(z, before if side == 0 else after), device_id_type=MESH)

    for side in range(2):
        edge_copy(side).start()

    def cot_copy(side):
        return pltpu.make_async_remote_copy(
            src_ref=cot_send.at[side], dst_ref=cot_recv.at[1 - side],
            send_sem=ce_ssem.at[side], recv_sem=ce_rsem.at[1 - side],
            device_id=(z, before if side == 0 else after), device_id_type=MESH)

    def load_cotangent():
        def put(at, value):
            cotm[at, :] = value
        from_flat(cot_in, put)

        def live_only(start, size, carry):
            at = pl.ds(start, size)
            cotm[at, :] = cotm[at, :] * mask[at, :]
            return carry
        chunked(live_only, 0)
        for side, start in ((0, 0), (1, cells - wide)):
            cot_send[side] = cotm[start:start + wide, :].astype(BF16)
            cot_copy(side).start()

    def take_cotangent():
        for side in range(2):
            cot_copy(1 - side).wait_recv()
            at = slice(cells + side * wide, cells + (side + 1) * wide)
            cotm[at, :] = cot_recv[side].astype(F32) * mask[at, :]

    w_parts = math.gcd(tap_rows // 16, s_count)
    w_rows = tap_rows // w_parts
    w_mine = s % w_parts
    w_group = s - w_mine

    def wz_copy(which, k):
        at = pl.ds(w_mine * w_rows, w_rows)
        slot = n - k - 1
        return pltpu.make_async_remote_copy(
            src_ref=wv.at[which, (z + k) % n, at, :], dst_ref=wf.at[which, slot, at, :],
            send_sem=wz_ssem.at[which, slot], recv_sem=wz_rsem.at[which, slot],
            device_id=((z + k) % n, s), device_id_type=MESH)

    def wp_copy(which, slot, k, whose):
        at = pl.ds(whose * w_rows, w_rows)
        return pltpu.make_async_remote_copy(
            src_ref=wf.at[which, slot, at, :], dst_ref=wf.at[which, slot, at, :],
            send_sem=wp_ssem.at[which, slot, k], recv_sem=wp_rsem.at[which, slot, whose],
            device_id=(z, w_group + (w_mine + k) % w_parts), device_id_type=MESH)

    def weights_over_z(which):
        for copy in w_copies[which * n:(which + 1) * n]:
            copy.wait()

        @pl.loop(1, n)
        def _(k):
            wz_copy(which, k).start()

    def slot_of(block):
        return (block - z + n - 1) % n

    def weights_round(which):
        @pl.loop(1, n)
        def _(distance):
            for sign in (1, -1):
                block = z - distance * sign

                @pl.when((block >= 0) & (block < n))
                def _():
                    slot = slot_of(block)
                    wz_copy(which, n - 1 - slot).wait_recv()

                    @pl.loop(1, w_parts)
                    def _(k):
                        wp_copy(which, slot, k, w_mine).start()

    def weights_arrived(which, slot):
        @pl.loop(1, w_parts)
        def _(k):
            wp_copy(which, slot, k, (w_mine + k) % w_parts).wait_recv()

    def row_copy(slot, side):
        return pltpu.make_async_remote_copy(
            src_ref=row_send.at[slot, side], dst_ref=row_recv.at[slot, 1 - side],
            send_sem=row_ssem.at[slot, side], recv_sem=row_rsem.at[slot, 1 - side],
            device_id=(z, before if side == 0 else after), device_id_type=MESH)

    def send_row(slot, side):
        start = side * (cells - wide)
        row_send[slot, side] = acc[start:start + wide, :]
        row_copy(slot, side).start()

    settled = (rows // HALVES - 1) * wide

    def take_rows(slot, ref):
        for side in range(2):
            row_copy(slot, 1 - side).wait_recv()
            ref[cells + side * wide:cells + (side + 1) * wide, :] = row_recv[slot, side]

    def st_copy(slot, k, whose):
        return pltpu.make_async_remote_copy(
            src_ref=st_send.at[slot], dst_ref=st_recv.at[slot, whose],
            send_sem=st_ssem.at[slot, k], recv_sem=st_rsem.at[slot, whose],
            device_id=(z, (s + k) % s_count), device_id_type=MESH)

    def send_stats(slot, values):
        for i, v in enumerate(values):
            st_send[slot, i:i + 1, :] = v
        for k in range(1, s_count):
            st_copy(slot, k, s).start()
        st_recv[slot, s] = st_send[slot]

    def take_stats(slot):
        for k in range(1, s_count):
            st_copy(slot, k, (s + k) % s_count).wait_recv()

    strip = 8
    column = lax.broadcasted_iota(jnp.int32, (strip * wide, ch), 0) % wide

    def shift(target, first, count):
        size = count * wide
        where = column[:size]
        here = pad[pl.ds(8 + first * wide, size), :]
        left = jnp.where(where == 0, 0.0, pad[pl.ds(7 + first * wide, size), :])
        right = jnp.where(where == wide - 1, 0.0, pad[pl.ds(9 + first * wide, size), :])
        for b, v in enumerate((left, here, right)):
            target[pl.ds(first, count), :, b * ch:(b + 1) * ch] = v.astype(BF16).reshape(count, wide, ch)

    edge = 2 * wide
    ag_rows = ((0, edge + packed), (edge + packed, packed))
    band_rows = rows // HALVES

    def unpack_half(ph, block, q, target):
        if q == 0:
            pad[8:8 + wide, :] = hold[ph, block, 0:wide, :].astype(F32)
            pad[8 + wide + cells:8 + 2 * wide + cells, :] = hold[ph, block, wide:edge, :].astype(F32)
            shift(target, 0, 1)
            shift(target, rows + 1, 1)
        for j in range(2):
            start = edge + q * packed + j * (packed - unpack.shape[3])
            at = 8 + wide + q * band + j * (band // 2)
            pad[at:at + band // 2, :] = dot(unpack[q, j], hold[ph, block, start:start + unpack.shape[3], :])

        for i in range(band_rows // strip):
            shift(target, 1 + q * band_rows + i * strip, strip)

    def add_conv(q, field, taps, turned_taps=None):
        first, last = (0, band_rows - 1) if q == 0 else (band_rows - 1, rows)
        count = last - first
        size = (count + 2) * wide
        lhs = jnp.concatenate([
            field[first + i:last + 2 + i, :, :].reshape(size, 3 * ch) for i in range(2)], axis=1)
        if turned_taps is None:
            none = jnp.zeros((3 * ch, ch), BF16)
            rhs = jnp.concatenate([
                jnp.concatenate([taps(0), taps(2)], axis=1), jnp.concatenate([taps(1), none], axis=1)], axis=0)
            value = dot(lhs, rhs)
        else:
            def row_taps(a):
                return [turned_taps(3 * (2 - a) + 2 - b) for b in range(3)]
            none = jnp.zeros((ch, 3 * ch), BF16)
            rhs = jnp.concatenate([
                jnp.concatenate(row_taps(0) + row_taps(1), axis=1), jnp.concatenate(row_taps(2) + [none], axis=1)], axis=0)
            value = lax.dot_general(lhs, rhs, (((1,), (1,)), ((), ())), preferred_element_type=F32)
        at = pl.ds(first * wide, count * wide)
        acc[at, :] = acc[at, :] + value[0:count * wide, 0:ch] + value[2 * wide:size, ch:2 * ch]

    def ag_copy(ph, block, q, sign):
        at = pl.ds(*ag_rows[q])
        return pltpu.make_async_remote_copy(
            src_ref=hold.at[ph, block, at, :], dst_ref=hold.at[ph, block, at, :],
            send_sem=ag_ssem.at[ph, (1 - sign) // 2, block, q], recv_sem=ag_rsem.at[ph, block, q],
            device_id=(z + sign, s), device_id_type=MESH)

    def pack_field(ph, source, fill=None, first=None):
        if fill is not None:
            fill(cells, edge, 0)
        hold[ph, z, 0:edge, :] = source[cells:cells + edge, :].astype(BF16)
        for q in range(HALVES):
            if first is not None:
                first(q)
            if fill is not None:
                chunked(fill, 0, q * band, band)
            hold[ph, z, edge + q * packed:edge + (q + 1) * packed, :] = dot(
                pack[q], source[q * band:(q + 1) * band, :].astype(BF16)).astype(BF16)
            for sign in (1, -1):
                @pl.when((z + sign >= 0) & (z + sign < n))
                def _():
                    ag_copy(ph, z, q, sign).start()

    def inside(slice_at):
        return (slice_at >= 0) & (slice_at < n)

    def take_and_pass(ph, k, q, sign, passes=True, takes=True):
        block = z - k * sign

        @pl.when((k > 0) & inside(block))
        def _():
            if passes and takes:
                ag_copy(ph, block, q, sign).wait_recv()

            @pl.when(inside(z + sign))
            def _():
                if passes:
                    if not takes:
                        ag_copy(ph, block, q, sign).wait_recv()
                    ag_copy(ph, block, q, sign).start()

            if not passes:
                @pl.when(jnp.logical_not(inside(z + sign)))
                def _():
                    ag_copy(ph, block, q, sign).wait_recv()

    near = jnp.where(z < n - n // 2, 1, 0)

    def consume_way(k, q, way, consume):
        block = z - k * (1 - 2 * way)

        @pl.when((k >= 0) & (k < n) & inside(block) & ((k > 0) | (way == near)))
        def _():
            consume(k, block, q)

    def take_both(ph, k, q, **how):
        @pl.loop(0, 2)
        def _(i):
            way = (near + i) % 2
            take_and_pass(ph, k, q, 1 - 2 * way, **how)

    def gather(ph, consume, each):
        @pl.loop(0, n)
        def _(k):
            for q in range(HALVES):
                take_both(ph, k, q)
                if q:
                    consume_way(k, q - 1, 1 - near, consume)
                else:
                    consume_way(k - 1, HALVES - 1, 1 - near, consume)
                consume_way(k, q, near, consume)
            each(k)

    def gather_passing_first(ph, consume, each):
        @pl.loop(0, n)
        def _(k):
            @pl.when(k == 1)
            def _():
                @pl.loop(1, n)
                def _(ahead):
                    for q in range(HALVES):
                        take_both(ph, ahead, q, takes=False)
            for q in range(HALVES):
                take_both(ph, k, q, passes=False)

                @pl.loop(0, 2)
                def _(i):
                    consume_way(k, q, (near + i) % 2, consume)
            each(k)

    last_step = jnp.maximum(z, n - 1 - z)

    last_pass = jnp.maximum(jnp.where(z < n - 1, z, 0), jnp.where(z > 0, n - 1 - z, 0))

    def forward(ph, field):
        def consume(k, block, q):
            into = taken.at[block]
            unpack_half(ph, block, q, into)

            @pl.when(k == 0)
            def _():
                add_conv(q, into, lambda a: wv[ph, z, 3 * a * ch:3 * (a + 1) * ch, :])

            @pl.when(k > 0)
            def _():
                slot = slot_of(block)
                if q == 0:
                    weights_arrived(ph, slot)
                add_conv(q, into, lambda a: wf[ph, slot, 3 * a * ch:3 * (a + 1) * ch, :])

            if q == 0:
                pl.when(k == last_step)(lambda: early_moments(ph))

        def each(k):
            if ph == 0:
                @pl.when(k == 0)
                def _():
                    weights_round(0)

                @pl.when(k == last_pass)
                def _():
                    load_cotangent()
        (gather if ph else gather_passing_first)(ph, consume, each)

    def turn_field(ph, field):
        main = [field[start:start + ch, :].T for start in range(0, cells, ch)]
        ends = field[cells:cells + edge, :]
        if edge < ch:
            ends = jnp.concatenate([ends, jnp.zeros((ch - edge, ch), F32)], axis=0)
        ends = ends.T
        for i, here in enumerate(main):
            left = jnp.concatenate(
                [ends[:, 0:wide] if i == 0 else main[i - 1][:, ch - wide:], here[:, 0:ch - wide]], axis=1)
            right = jnp.concatenate(
                [here[:, wide:], main[i + 1][:, 0:wide] if i + 1 < len(main) else ends[:, wide:edge]], axis=1)
            for a, v in enumerate((left, here, right)):
                x_t[ph, a * ch:(a + 1) * ch, i * ch:(i + 1) * ch] = v.astype(BF16)

    half_rows = tap_rows // 2
    owners = math.gcd(half_rows // 16, chips)
    piece = half_rows // owners

    def c_copy(ph, j):
        return pltpu.make_async_remote_copy(
            src_ref=psend.at[ph, j], dst_ref=crecv.at[ph, j],
            send_sem=c_ssem.at[ph, j], recv_sem=c_rsem.at[ph, j],
            device_id=(z, chip * 2 + 1 - core), device_id_type=MESH)

    def q_copy(ph, j, e, whose, owner):
        return pltpu.make_async_remote_copy(
            src_ref=hsend.at[ph, j, owner], dst_ref=qrecv.at[ph, j, whose],
            send_sem=q_ssem.at[ph, j, e], recv_sem=q_rsem.at[ph, j, whose],
            device_id=(z, ((chip + e) % chips) * 2 + core), device_id_type=MESH)

    def f_copy(ph, j, e, owner):
        return pltpu.make_async_remote_copy(
            src_ref=wout.at[ph, j, core, owner], dst_ref=wout.at[ph, j, core, owner],
            send_sem=f_ssem.at[ph, j, e], recv_sem=f_rsem.at[ph, j, owner],
            device_id=(z, ((chip + e) % chips) * 2 + core), device_id_type=MESH)

    def h_copy(ph, j, whose):
        return pltpu.make_async_remote_copy(
            src_ref=wout.at[ph, j, whose], dst_ref=wout.at[ph, j, whose],
            send_sem=h_ssem.at[ph, j], recv_sem=h_rsem.at[ph, j],
            device_id=(z, chip * 2 + 1 - core), device_id_type=MESH)

    def o_copy(ph, j):
        target = (out_wg1, out_wg2)[ph]
        if aligned:
            target = target.at[:, :, :, pl.ds(pl.multiple_of(j * ch, ch), ch)]
        else:
            target = target.at[j]
        return pltpu.make_async_copy(wout.at[ph, j], target, o_sem.at[ph, j])

    def sum_cores(ph, j):
        for o in range(owners):
            psend[ph, j, o] = part[ph, j, 1 - core, o].astype(BF16)
        c_copy(ph, j).start()

    def sum_chips(ph, j):
        c_copy(ph, j).wait_recv()
        for o in range(owners):
            v = part[ph, j, core, o] + crecv[ph, j, o].astype(F32)
            part[ph, j, core, o] = v
            hsend[ph, j, o] = v.astype(BF16)

        @pl.loop(1, chips)
        def _(e):
            peer = (chip + e) % chips

            @pl.when(peer < owners)
            def _():
                q_copy(ph, j, e, chip, peer).start()

    def spread_chips(ph, j):
        @pl.when(chip < owners)
        def _():
            @pl.loop(1, chips)
            def _(e):
                q_copy(ph, j, e, (chip + e) % chips, chip).wait_recv()
            v = part[ph, j, core, chip]
            for e in range(1, chips):
                v = v + qrecv[ph, j, (chip + e) % chips].astype(F32)
            wout[ph, j, core, chip] = v.astype(BF16)

            @pl.loop(1, chips)
            def _(e):
                f_copy(ph, j, e, chip).start()

    def spread_cores(ph, j):
        @pl.loop(1, chips)
        def _(e):
            peer = (chip + e) % chips

            @pl.when(peer < owners)
            def _():
                f_copy(ph, j, e, peer).wait_recv()
        h_copy(ph, j, core).start()

    def finish(ph, j):
        h_copy(ph, j, 1 - core).wait_recv()
        o_copy(ph, j).start()

    def put_part(ph, j, tap, value):
        start = tap * ch
        done = 0
        while done < ch:
            row = start + done
            side, o, at = row // half_rows, row % half_rows // piece, row % piece
            size = min(ch - done, piece - at)
            part[ph, j, side, o, at:at + size, :] = value[done:done + size, :]
            done += size

    stages = (sum_cores, sum_chips, spread_chips, spread_cores, finish)

    def of_step(k, fn):
        @pl.loop(0, 2)
        def _(way):
            block = z - k * (1 - 2 * way)

            @pl.when((k >= 0) & (k < n) & inside(block) & ((k > 0) | (way == 0)))
            def _():
                fn(block)

    passing = last_pass > 0

    def made_at(step):
        first = jnp.where(passing & (step > 0), jnp.where(step == last_pass, 1, step + 1), step)
        return first, step + 1

    def advance(ph, k):
        for age in range(1, len(stages)):
            step = k - age

            @pl.when((step >= 0) & (step < n))
            def _():
                @pl.loop(*made_at(step))
                def _(made):
                    of_step(made, functools.partial(stages[age], ph))

    def advance_all(ph, age):
        @pl.loop(0, n)
        def _(j):
            stages[age](ph, j)

    def field_grad(ph, block):
        grad = taken[block, 1:rows + 1, :, :].reshape(cells, 3 * ch)
        value = dot(x_t[ph], grad)
        for a in range(3):
            for b in range(3):
                put_part(ph, block, 3 * a + b, value[a * ch:(a + 1) * ch, (2 - b) * ch:(3 - b) * ch])

    def make_grad(ph, block):
        field_grad(ph, block)
        sum_cores(ph, block)

    def inner_sums(first, last, side):
        start = side * (cells - wide)
        row_send[2, side] = acc[start:start + wide, :]
        at = slice(first, last)
        v = acc[at, :] * slope1[at, :]
        slope1[at, :] = v
        acc[at, :] = jnp.zeros((last - first, ch), F32)
        return fold(v * normed1[at, :]), fold(v)

    def early_inner():
        for i, v in enumerate(inner_sums(0, settled, 0)):
            early[8 * i:8 * i + 8, :] = v
        row_copy(2, 0).start()

    def backward(ph):
        last = ph == 0

        def consume(k, block, q):
            into = taken.at[block]
            unpack_half(2 + ph, block, q, into)
            if last and q == HALVES - 1:
                @pl.when((k == 0) | (k >= last_pass))
                def _():
                    make_grad(ph, block)
            add_conv(q, into, None, lambda t: wv[ph, block, t * ch:(t + 1) * ch, :])
            if q == 0 and not last:
                pl.when(k == last_step)(early_inner)

        def each(k):
            first, end = made_at(k)
            if last:
                @pl.loop(first, end - 1)
                def _(step):
                    of_step(step, functools.partial(make_grad, ph))
                advance(ph, k)
                for age in range(2, len(stages)):
                    @pl.when(k == age - 2)
                    def _():
                        advance_all(1, age)
            else:
                @pl.loop(first, jnp.where(passing | (k < n - 1), end, first))
                def _(step):
                    of_step(step, functools.partial(make_grad, ph))
        gather(2 + ph, consume, each)

    def fold(v):
        return jnp.sum(v.reshape(v.shape[0] // 8, 8, ch), axis=0)

    def flatten(v):
        return jnp.sum(v, axis=0, keepdims=True)

    zero = jnp.zeros((8, ch), F32)

    def part_moments(first, last):
        m = mask[first:last, :]
        v = acc[first:last, :]
        number, added = flatten(fold(m)), flatten(fold(v * m))
        c = (v - added / jnp.maximum(number, 1.0)) * m
        return added, number, flatten(fold(c * c))

    def early_moments(slot):
        for i, v in enumerate(part_moments(0, settled)):
            early[i:i + 1, :] = v
        send_row(slot, 0)

    def combine(added, number, spread):
        total_added, total_number = sum(added), sum(number)
        mean = total_added / jnp.maximum(total_number, 1.0)
        about = 0.0
        for a, k, q in zip(added, number, spread):
            off = a / jnp.maximum(k, 1.0) - mean
            about = about + (q + k * off * off)
        return total_added, total_number, about

    def local_moments():
        late = part_moments(settled, cells)
        return combine(*([early[i:i + 1, :], v] for i, v in enumerate(late)))

    def moments(slot):
        take_stats(slot)
        added, number, about = (st_recv[slot, :, i, :] for i in range(3))
        count = flatten(number)
        mean = flatten(added) / count
        off = added / jnp.maximum(number, 1.0) - mean
        return mean, lax.rsqrt(flatten(about + number * off * off) / count + EPSILON), count

    def everywhere(fn):
        chunked(fn, 0)
        fn(cells, 2 * wide, 0)

    gain1, shift1, gain2, shift2 = (r[...] for r in (gain1_in, shift1_in, gain2_in, shift2_in))

    weights_over_z(0)

    quarter = band // 2
    kept = packed // 2
    window = unpack.shape[3]
    below = lax.broadcasted_iota(jnp.int32, (quarter, quarter), 1) < lax.broadcasted_iota(jnp.int32, (quarter, quarter), 0)
    below = below.astype(F32).astype(BF16)

    def make_pack(h):
        for j in range(2):
            lv = mask[h * band + j * quarter:h * band + (j + 1) * quarter, :]
            place = jnp.where(lv > 0.0, dot(below, lv.astype(BF16)) + j * kept, -1.0)
            places[h, j] = place
            across = place.T[0:1, :]
            spot = lax.broadcasted_iota(jnp.int32, (packed, quarter), 0).astype(F32)
            pack[h, :, j * quarter:(j + 1) * quarter] = jnp.where(spot == across, 1.0, 0.0).astype(BF16)

    def make_unpack(h):
        for j in range(2):
            for start in range(0, window, ch):
                size = min(ch, window - start)
                spot = start + j * (packed - window) + lax.broadcasted_iota(jnp.int32, (quarter, size), 1)
                unpack[h, j, :, start:start + size] = jnp.where(
                    places[h, j, :, :size] == spot.astype(F32), 1.0, 0.0).astype(BF16)

    for side in range(2):
        edge_copy(1 - side).wait_recv()
        there = jnp.where(s > 0, 1.0, 0.0) if side == 0 else jnp.where(s < s_count - 1, 1.0, 0.0)
        at = slice(cells + side * wide, cells + (side + 1) * wide)
        masked[at, :] = edge_recv[side, 0].astype(F32) * there
        mask[at, :] = edge_recv[side, 1].astype(F32) * there

    def stats_sent(slot):
        for k in range(1, s_count):
            st_copy(slot, k, s).wait_send()

    def row_sent(slot):
        for side in range(2):
            row_copy(slot, side).wait_send()

    def gathered_sent(ph):
        @pl.loop(0, n)
        def _(k):
            for sign in (1, -1):
                block = z - k * sign

                @pl.when(inside(block) & inside(z + sign))
                def _():
                    for q in range(HALVES):
                        ag_copy(ph, block, q, sign).wait_send()

    def weights_sent(which):
        for k in range(1, n):
            wz_copy(which, k).wait_send()

        @pl.loop(1, w_parts)
        def _(k):
            for slot in range(n - 1):
                wp_copy(which, slot, k, w_mine).wait_send()

    def grads_sent(ph):
        @pl.loop(0, n)
        def _(j):
            c_copy(ph, j).wait_send()
            h_copy(ph, j, core).wait_send()
            o_copy(ph, j).wait()
            for e in range(1, chips):
                peer = (chip + e) % chips

                @pl.when(peer < owners)
                def _():
                    q_copy(ph, j, e, chip, peer).wait_send()

                @pl.when(chip < owners)
                def _():
                    f_copy(ph, j, e, chip).wait_send()

    block_copy = pltpu.make_async_copy(flat_block, out_block, r_sem.at[0])

    pack_field(0, masked, first=make_pack)
    for h in range(HALVES):
        make_unpack(h)
    forward(0, masked)
    send_stats(0, local_moments())
    send_row(0, 1)
    weights_over_z(1)
    mean1, scale1, count = moments(0)

    def activate_one(start, size, carry):
        at = pl.ds(start, size)
        main = start is not cells
        nv = ((acc if main else normed1)[at, :] - mean1) * scale1
        normed1[at, :] = nv
        hid[at, :] = gelu_parts(nv * gain1 + shift1)[0] * mask[at, :]
        if main:
            acc[at, :] = jnp.zeros((size, ch), F32)
        return carry

    def slope_one(start, size, carry):
        at = pl.ds(start, size)
        slope1[at, :] = gelu_parts(normed1[at, :] * gain1 + shift1)[1] * mask[at, :]
        return carry

    take_rows(0, normed1)
    pack_field(1, hid, activate_one)
    weights_round(1)
    everywhere(slope_one)
    forward(1, hid)
    send_stats(1, local_moments())
    send_row(1, 1)
    turn_field(0, masked)
    turn_field(1, hid)
    weights_sent(0)
    gathered_sent(0)
    stats_sent(0)
    row_sent(0)
    for side in range(2):
        edge_copy(side).wait_send()
        cot_copy(side).wait_send()
    mean2, scale2, _ = moments(1)

    def activate_two(source, start, size):
        at = pl.ds(start, size)
        nv = (source[at, :] - mean2) * scale2
        normed2[at, :] = nv
        value, slope = gelu_parts(nv * gain2 + shift2 + masked[at, :])
        t = cotm[at, :] * slope
        through[at, :] = t
        return value, nv, t

    def activate_main(start, size, carry):
        value, nv, t = activate_two(acc, start, size)
        at = pl.ds(start, size)
        hid2[at, :] = value * mask[at, :]
        acc[at, :] = jnp.zeros((size, ch), F32)
        return carry[0] + fold(t * nv), carry[1] + fold(t)

    send_stats(2, [flatten(v) for v in chunked(activate_main, (zero, zero))])
    take_rows(1, normed2)
    take_cotangent()
    activate_two(normed2, cells, edge)
    to_flat(hid2, flat_block)
    block_copy.start()
    weights_sent(1)
    gathered_sent(1)

    def gradient_sums(slot):
        take_stats(slot)
        return flatten(st_recv[slot, :, 0, :]), flatten(st_recv[slot, :, 1, :])

    def norm_back(upstream, normed, gain, scale, sums):
        gain_grad, shift_grad = sums
        factor = gain * scale
        level, tilt = shift_grad / count, gain_grad / count

        def fill(start, size, carry):
            at = pl.ds(start, size)
            v = upstream[at, :] - mask[at, :] * (level + normed[at, :] * tilt)
            hid[at, :] = factor * v
            return carry
        return fill

    sums2 = gradient_sums(2)
    pack_field(3, hid, norm_back(through, normed2, gain2, scale2, sums2))
    backward(1)

    parts = inner_sums(settled, cells, 1)
    send_stats(3, [flatten(early[8 * i:8 * i + 8, :] + v) for i, v in enumerate(parts)])
    row_copy(2, 1).start()

    @pl.when(jnp.logical_not(passing))
    def _():
        of_step(n - 1, functools.partial(make_grad, 1))
    for side in range(2):
        row_copy(2, 1 - side).wait_recv()
        at = slice(cells + side * wide, cells + (side + 1) * wide)
        slope1[at, :] = row_recv[2, side] * slope1[at, :]
    stats_sent(1)
    row_sent(1)
    stats_sent(2)
    gathered_sent(3)
    sums1 = gradient_sums(3)
    pack_field(2, hid, norm_back(slope1, normed1, gain1, scale1, sums1))
    advance_all(1, 1)
    backward(0)
    advance(0, n)

    def finish_input(start, size, carry):
        at = pl.ds(start, size)
        acc[at, :] = (acc[at, :] + through[at, :]) * mask[at, :]
        return carry

    chunked(finish_input, 0)
    to_flat(acc, flat_input)
    input_copy = pltpu.make_async_copy(flat_input, out_input, r_sem.at[1])
    input_copy.start()
    out_gain1[...], out_shift1[...] = sums1
    out_gain2[...], out_shift2[...] = sums2
    for extra in range(1, len(stages) - 1):
        advance(0, n + extra)

    stats_sent(3)
    row_sent(2)
    gathered_sent(2)
    grads_sent(1)
    grads_sent(0)
    block_copy.wait()
    input_copy.wait()


def finish_kernel(count, *refs):
    ins, outs = refs[:count], refs[count:2 * count]
    narrow, wide, in_sem, out_sem, take_sem, give_sem = refs[2 * count:2 * count + 6]
    held = refs[2 * count + 6:]
    rows = narrow.shape[1] // FINISH_PARTS
    parts = [(w, i, pl.ds(i * rows, rows)) for i in range(FINISH_PARTS) for w in range(2)]
    loads = [pltpu.make_async_copy(ins[w].at[at, :], narrow.at[w, at, :], in_sem.at[w, i]) for w, i, at in parts]
    stores = [pltpu.make_async_copy(wide.at[w, at, :], outs[w].at[at, :], out_sem.at[w, i]) for w, i, at in parts]
    takes = [pltpu.make_async_copy(ins[2 + k], v, take_sem.at[k]) for k, v in enumerate(held)]
    gives = [pltpu.make_async_copy(v, outs[2 + k], give_sem.at[k]) for k, v in enumerate(held)]
    for copy in loads + takes:
        copy.start()
    for load, store, (w, i, at) in zip(loads, stores, parts):
        load.wait()
        wide[w, at, :] = narrow[w, at, :].astype(F32)
        store.start()
    for take, give in zip(takes, gives):
        take.wait()
        give.start()
    for copy in stores + gives:
        copy.wait()


def per_device(n, s_count, blocks, weight_one, weight_two, gain_one, shift_one, gain_two, shift_two, cell_live, cotangent):
    rows, wide = cell_live.shape
    ch = blocks.shape[1] // wide
    cells = rows * wide
    total = cells + 2 * wide
    packed = 2 * -(-most_live(rows // HALVES // 2, wide) // 8) * 8
    aligned = ch % 128 == 0
    chips = s_count // 2
    tap_rows = 9 * ch
    half_rows = tap_rows // 2
    owners = math.gcd(half_rows // 16, chips)
    piece = half_rows // owners

    if aligned:
        weight_one, weight_two = (w.reshape(tap_rows, n * ch) for w in (weight_one, weight_two))
    else:
        weight_one, weight_two = (
            w.reshape(tap_rows, n, ch).transpose(1, 0, 2) for w in (weight_one, weight_two))
    grad_shape = (2, owners, piece, n * ch) if aligned else (n, 2, owners, piece, ch)
    vmem = pl.BlockSpec(memory_space=pltpu.VMEM)
    hbm = pl.BlockSpec(memory_space=pl.ANY)
    sem = pltpu.SemaphoreType.DMA
    field = pltpu.VMEM((total, ch), F32)
    scratch = [
        pltpu.VMEM((ch * wide, 128), F32),
        pltpu.VMEM((2, n, tap_rows, ch), BF16),
        pltpu.VMEM((2, n - 1, tap_rows, ch), BF16),
        pltpu.VMEM((2, 3 * ch, cells), BF16),
        pltpu.VMEM((HALVES, packed, cells // HALVES), BF16),
        pltpu.VMEM((HALVES, 2, cells // HALVES // 2, -(-packed // 2 // 16) * 16), BF16),
        pltpu.VMEM((HALVES, 2, cells // HALVES // 2, ch), F32),
        pltpu.VMEM((2, 2, wide, ch), BF16),
        pltpu.VMEM((2, 2, wide, ch), BF16),
        pltpu.VMEM((2, wide, ch), BF16),
        pltpu.VMEM((2, wide, ch), BF16),
        field, field, field, field, field, field, field, field, field,
        pltpu.VMEM((total + 16, ch), F32),
        pltpu.VMEM((cells, ch), F32),
        pltpu.VMEM((4, n, 2 * wide + HALVES * packed, ch), BF16),
        pltpu.VMEM((n, rows + 3, wide, 3 * ch), BF16),
        pltpu.VMEM((2, n, 2, owners, piece, ch), F32),
        pltpu.VMEM((2, n, owners, piece, ch), BF16),
        pltpu.VMEM((2, n, owners, piece, ch), BF16),
        pltpu.VMEM((2, n, owners, piece, ch), BF16),
        pltpu.VMEM((2, n, chips, piece, ch), BF16),
        pltpu.VMEM((2, n, 2, owners, piece, ch), BF16),
        pltpu.VMEM((4, 8, ch), F32),
        pltpu.VMEM((4, s_count, 8, ch), F32),
        pltpu.VMEM((3, 2, wide, ch), F32),
        pltpu.VMEM((3, 2, wide, ch), F32),
        pltpu.VMEM((16, ch), F32),
        pltpu.VMEM((rows, ch * wide), BF16),
        pltpu.VMEM((rows, ch * wide), F32),
        sem((2, n)),
        sem((2, n)), sem((2, n)),
        sem((2, n - 1, s_count)), sem((2, n - 1, s_count)),
        sem((2,)), sem((2,)),
        sem((2,)), sem((2,)),
        sem((4, 2, n, HALVES)), sem((4, n, HALVES)),
        sem((4, s_count)), sem((4, s_count)),
        sem((3, 2)), sem((3, 2)),
        sem((2, n)), sem((2, n)),
        sem((2, n, chips)), sem((2, n, chips)),
        sem((2, n, chips)), sem((2, n, chips)),
        sem((2, n)), sem((2, n)),
        sem((2, n)),
        sem((2,)),
    ]
    block_out, input_grad, wg1, wg2, *sums = pl.pallas_call(
        functools.partial(block_kernel, n, s_count, rows, wide, ch, aligned, packed),
        out_shape=(
            jax.ShapeDtypeStruct((rows, ch * wide), BF16),
            jax.ShapeDtypeStruct((rows, ch * wide), F32),
            jax.ShapeDtypeStruct(grad_shape, BF16),
            jax.ShapeDtypeStruct(grad_shape, BF16),
            *[jax.ShapeDtypeStruct((1, ch), F32)] * 4,
        ),
        in_specs=[vmem] * 7 + [hbm] * 2,
        out_specs=(hbm, hbm, hbm, hbm, vmem, vmem, vmem, vmem),
        scratch_shapes=scratch,
        compiler_params=pltpu.CompilerParams(
            collective_id=0, has_side_effects=True, vmem_limit_bytes=60 * 1024 * 1024),
    )(blocks, cotangent, cell_live.T,
      *(v.reshape(1, ch) for v in (gain_one, shift_one, gain_two, shift_two)), weight_one, weight_two)

    if not aligned:
        def whole(grad):
            grad = grad.reshape(n, tap_rows, ch).transpose(1, 0, 2)
            return grad.astype(F32).reshape(9, ch, n * ch)
        return (block_out, input_grad, whole(wg1), whole(wg2), *(v.reshape(ch) for v in sums))

    wg1, wg2 = (w.reshape(tap_rows, n * ch) for w in (wg1, wg2))
    wide_grad = jax.ShapeDtypeStruct((tap_rows, n * ch), F32)
    moved = (block_out, input_grad, *sums)
    grad1, grad2, *moved = pl.pallas_call(
        functools.partial(finish_kernel, 2 + len(moved)),
        out_shape=(wide_grad, wide_grad, *(jax.ShapeDtypeStruct(v.shape, v.dtype) for v in moved)),
        in_specs=[pl.BlockSpec(memory_space=pl.ANY)] * (2 + len(moved)),
        out_specs=[pl.BlockSpec(memory_space=pl.ANY)] * (2 + len(moved)),
        scratch_shapes=[
            pltpu.VMEM((2, tap_rows, n * ch), BF16), pltpu.VMEM((2, tap_rows, n * ch), F32),
            sem((2, FINISH_PARTS)), sem((2, FINISH_PARTS)), sem((len(moved),)), sem((len(moved),)),
            *(pltpu.VMEM(v.shape, v.dtype) for v in moved),
        ],
        compiler_params=pltpu.CompilerParams(vmem_limit_bytes=64 * 1024 * 1024),
    )(wg1, wg2, *moved)
    block_out, input_grad, *sums = moved
    grads = (g.reshape(9, ch, n * ch) for g in (grad1, grad2))
    return (block_out, input_grad, *grads, *(v.reshape(ch) for v in sums))


def solution(mesh):
    return jax.shard_map(
        functools.partial(per_device, mesh.shape["chan"], mesh.shape["space"]),
        mesh=mesh,
        in_specs=(
            P("space", "chan"),
            P(None, "chan", None),
            P(None, "chan", None),
            P("chan"),
            P("chan"),
            P("chan"),
            P("chan"),
            P("space", None),
            P("space", "chan"),
        ),
        out_specs=(
            P("space", "chan"),
            P("space", "chan"),
            P(None, "chan", None),
            P(None, "chan", None),
            P("chan"),
            P("chan"),
            P("chan"),
            P("chan"),
        ),
        check_vma=False,
    )
```

```python
import functools
import math

import jax
import jax.numpy as jnp
from jax import lax
from jax.experimental import pallas as pl
from jax.experimental.pallas import tpu as pltpu
from jax.sharding import PartitionSpec as P

EPSILON = 1e-05
MESH = pl.DeviceIdType.MESH
F32 = jnp.float32
BF16 = jnp.bfloat16
ROOT_HALF = 0.7071067811865476
ROOT_TWO_PI = 0.3989422804014327
CHUNK = 64
FINISH_PARTS = 4
UNROLL = 2
HALVES = 2
LARGE, SMALL = 7, 3


def dot(a, b):
    return jnp.dot(a, b, preferred_element_type=F32)


def gelu_parts(v):
    upper = 0.5 * (1.0 + lax.erf(v * ROOT_HALF))
    slope = upper + v * (ROOT_TWO_PI * jnp.exp(-0.5 * v * v))
    return v * upper, slope


def most_live(rows, wide):
    units = (wide + 1) // (SMALL + 1)
    live_rows = rows - rows // (LARGE + 1)
    return min(rows * wide, math.ceil(units * live_rows * LARGE / 2))


def block_kernel(n, s_count, rows, wide, ch, aligned, packed, *refs):
    (x_in, cot_in, live_in, gain1_in, shift1_in, gain2_in, shift2_in, w1_hbm, w2_hbm) = refs[:9]
    (out_block, out_input, out_wg1, out_wg2, out_gain1, out_shift1, out_gain2, out_shift2) = refs[9:17]
    (turned, wv, wf, x_t, pack, unpack, places, edge_send, edge_recv, cot_send, cot_recv, cotm, mask, masked,
     normed1, normed2, through, slope1, hid, hid2, pad, acc, hold, taken,
     part, psend, crecv, hsend, qrecv, wout, st_send, st_recv, row_send, row_recv, early, flat_block, flat_input,
     w_sem, wz_ssem, wz_rsem, wp_ssem, wp_rsem, wh_ssem, wh_rsem, e_ssem, e_rsem, ce_ssem, ce_rsem, ag_ssem, ag_rsem,
     st_ssem, st_rsem, row_ssem, row_rsem, c_ssem, c_rsem, q_ssem, q_rsem,
     f_ssem, f_rsem, h_ssem, h_rsem, o_sem, r_sem) = refs[17:]

    z = lax.axis_index("chan")
    s = lax.axis_index("space")
    cells = rows * wide
    total = cells + 2 * wide
    band = cells // HALVES
    core, chip, chips = s % 2, s // 2, s_count // 2
    before, after = (s + s_count - 1) % s_count, (s + 1) % s_count
    tap_rows = 9 * ch
    half_rows = tap_rows // 2
    owners = math.gcd(half_rows // 16, chips)
    piece = half_rows // owners

    barrier = pltpu.get_barrier_semaphore()

    @pl.loop(1, s_count)
    def _(k):
        pl.semaphore_signal(barrier, inc=1, device_id=(z, (s + k) % s_count), device_id_type=MESH)

    @pl.loop(1, n)
    def _(k):
        pl.semaphore_signal(barrier, inc=1, device_id=((z + k) % n, s), device_id_type=MESH)

    w_copies = []
    for which, source in enumerate((w1_hbm, w2_hbm)):
        for d in range(n):
            block = source.at[:, d * ch:(d + 1) * ch] if aligned else source.at[d]
            w_copies.append(pltpu.make_async_copy(block, wv.at[which, d], w_sem.at[which, d]))
    for copy in w_copies:
        copy.start()

    def chunked(fn, init, first=0, count=cells):
        def step(i, carry):
            return fn(pl.multiple_of(first + i * CHUNK, CHUNK), CHUNK, carry)
        return lax.fori_loop(0, count // CHUNK, step, init, unroll=UNROLL)

    lanes = 128
    tiles = ch * wide // lanes

    def from_flat(flat, put):
        for i in range(tiles):
            turned[i * lanes:(i + 1) * lanes, 0:rows] = flat[:, i * lanes:(i + 1) * lanes].astype(F32).T
        for w in range(wide):
            put(pl.ds(w, rows, stride=wide), turned[pl.ds(w, ch, stride=wide), 0:rows].T)

    def to_flat(source, flat):
        for w in range(wide):
            turned[pl.ds(w, ch, stride=wide), 0:rows] = source[pl.ds(w, rows, stride=wide), :].T
        for i in range(tiles):
            flat[:, i * lanes:(i + 1) * lanes] = turned[i * lanes:(i + 1) * lanes, 0:rows].T.astype(flat.dtype)

    def put_masked(at, value):
        masked[at, :] = value

    from_flat(x_in, put_masked)

    cell = lax.broadcasted_iota(jnp.int32, (cells, rows), 0)
    pick = (cell // wide == lax.broadcasted_iota(jnp.int32, (cells, rows), 1)).astype(F32).astype(BF16)
    column_of = lax.broadcasted_iota(jnp.int32, (cells, wide), 0) % wide
    picked = lax.dot_general(pick, live_in[...].astype(BF16), (((1,), (1,)), ((), ())), preferred_element_type=F32)
    picked = jnp.where(column_of == lax.broadcasted_iota(jnp.int32, (cells, wide), 1), picked, 0.0)
    mask[0:cells, :] = dot(picked.astype(BF16), jnp.ones((wide, ch), BF16))

    def load_main(start, size, carry):
        at = pl.ds(start, size)
        lv = mask[at, :]
        masked[at, :] = masked[at, :] * lv
        return carry

    chunked(load_main, 0)
    for side, start in ((0, 0), (1, cells - wide)):
        edge_send[side, 0] = masked[start:start + wide, :].astype(BF16)
        edge_send[side, 1] = mask[start:start + wide, :].astype(BF16)

    acc[...] = jnp.zeros_like(acc)
    for block in range(n):
        for row in (rows // HALVES + 1, rows + 2):
            taken[block, row:row + 1, :, :] = jnp.zeros((1, wide, 3 * ch), BF16)
    st_send[...] = jnp.zeros_like(st_send)

    pl.semaphore_wait(barrier, s_count - 1 + n - 1)

    def edge_copy(side):
        return pltpu.make_async_remote_copy(
            src_ref=edge_send.at[side], dst_ref=edge_recv.at[1 - side],
            send_sem=e_ssem.at[side], recv_sem=e_rsem.at[1 - side],
            device_id=(z, before if side == 0 else after), device_id_type=MESH)

    for side in range(2):
        edge_copy(side).start()

    def cot_copy(side):
        return pltpu.make_async_remote_copy(
            src_ref=cot_send.at[side], dst_ref=cot_recv.at[1 - side],
            send_sem=ce_ssem.at[side], recv_sem=ce_rsem.at[1 - side],
            device_id=(z, before if side == 0 else after), device_id_type=MESH)

    def load_cotangent():
        def put(at, value):
            cotm[at, :] = value
        from_flat(cot_in, put)

        def live_only(start, size, carry):
            at = pl.ds(start, size)
            cotm[at, :] = cotm[at, :] * mask[at, :]
            return carry
        chunked(live_only, 0)
        for side, start in ((0, 0), (1, cells - wide)):
            cot_send[side] = cotm[start:start + wide, :].astype(BF16)
            cot_copy(side).start()

    def take_cotangent():
        for side in range(2):
            cot_copy(1 - side).wait_recv()
            at = slice(cells + side * wide, cells + (side + 1) * wide)
            cotm[at, :] = cot_recv[side].astype(F32) * mask[at, :]

    w_parts = math.gcd(tap_rows // 16, s_count)
    w_rows = tap_rows // w_parts
    w_mine = s % w_parts
    w_group = s - w_mine

    c_group = chip - chip % owners
    c_mine = core * half_rows + (chip % owners) * piece

    def wz_copy(which, k):
        at = pl.ds(c_mine, piece) if which else pl.ds(w_mine * w_rows, w_rows)
        slot = n - k - 1
        return pltpu.make_async_remote_copy(
            src_ref=wv.at[which, (z + k) % n, at, :], dst_ref=wf.at[which, slot, at, :],
            send_sem=wz_ssem.at[which, slot], recv_sem=wz_rsem.at[which, slot],
            device_id=((z + k) % n, s), device_id_type=MESH)

    def wp_copy(which, slot, k, whose):
        if which:
            at = pl.ds(core * half_rows + whose * piece, piece)
            to = (c_group + (chip + k) % owners) * 2 + core
        else:
            at = pl.ds(whose * w_rows, w_rows)
            to = w_group + (w_mine + k) % w_parts
        return pltpu.make_async_remote_copy(
            src_ref=wf.at[which, slot, at, :], dst_ref=wf.at[which, slot, at, :],
            send_sem=wp_ssem.at[which, slot, k], recv_sem=wp_rsem.at[which, slot, whose],
            device_id=(z, to), device_id_type=MESH)

    def wh_copy(slot, whose):
        at = pl.ds(whose * half_rows, half_rows)
        return pltpu.make_async_remote_copy(
            src_ref=wf.at[1, slot, at, :], dst_ref=wf.at[1, slot, at, :],
            send_sem=wh_ssem.at[slot], recv_sem=wh_rsem.at[slot],
            device_id=(z, chip * 2 + 1 - core), device_id_type=MESH)

    def weights_to_core():
        for slot in range(n - 1):
            for k in range(1, owners):
                wp_copy(1, slot, k, (chip + k) % owners).wait_recv()
            wh_copy(slot, core).start()

    def weights_over_z(which):
        for copy in w_copies[which * n:(which + 1) * n]:
            copy.wait()

        @pl.loop(1, n)
        def _(k):
            wz_copy(which, k).start()

    def slot_of(block):
        return (block - z + n - 1) % n

    def weights_round(which):
        @pl.loop(1, n)
        def _(distance):
            for sign in (1, -1):
                block = z - distance * sign

                @pl.when((block >= 0) & (block < n))
                def _():
                    slot = slot_of(block)
                    wz_copy(which, n - 1 - slot).wait_recv()

                    @pl.loop(1, owners if which else w_parts)
                    def _(k):
                        wp_copy(which, slot, k, chip % owners if which else w_mine).start()

    def weights_arrived(which, slot):
        if which:
            wh_copy(slot, 1 - core).wait_recv()
        else:
            @pl.loop(1, w_parts)
            def _(k):
                wp_copy(which, slot, k, (w_mine + k) % w_parts).wait_recv()

    def row_copy(slot, side):
        return pltpu.make_async_remote_copy(
            src_ref=row_send.at[slot, side], dst_ref=row_recv.at[slot, 1 - side],
            send_sem=row_ssem.at[slot, side], recv_sem=row_rsem.at[slot, 1 - side],
            device_id=(z, before if side == 0 else after), device_id_type=MESH)

    def send_row(slot, side):
        start = side * (cells - wide)
        row_send[slot, side] = acc[start:start + wide, :]
        row_copy(slot, side).start()

    settled = (rows // HALVES - 1) * wide

    def take_rows(slot, ref):
        for side in range(2):
            row_copy(slot, 1 - side).wait_recv()
            ref[cells + side * wide:cells + (side + 1) * wide, :] = row_recv[slot, side]

    def st_copy(slot, k, whose):
        return pltpu.make_async_remote_copy(
            src_ref=st_send.at[slot], dst_ref=st_recv.at[slot, whose],
            send_sem=st_ssem.at[slot, k], recv_sem=st_rsem.at[slot, whose],
            device_id=(z, (s + k) % s_count), device_id_type=MESH)

    def send_stats(slot, values):
        for i, v in enumerate(values):
            st_send[slot, i:i + 1, :] = v
        for k in range(1, s_count):
            st_copy(slot, k, s).start()
        st_recv[slot, s] = st_send[slot]

    def take_stats(slot):
        for k in range(1, s_count):
            st_copy(slot, k, (s + k) % s_count).wait_recv()

    strip = 8
    column = lax.broadcasted_iota(jnp.int32, (strip * wide, ch), 0) % wide

    def shift(target, first, count):
        size = count * wide
        where = column[:size]
        here = pad[pl.ds(8 + first * wide, size), :]
        left = jnp.where(where == 0, 0.0, pad[pl.ds(7 + first * wide, size), :])
        right = jnp.where(where == wide - 1, 0.0, pad[pl.ds(9 + first * wide, size), :])
        for b, v in enumerate((left, here, right)):
            target[pl.ds(first, count), :, b * ch:(b + 1) * ch] = v.astype(BF16).reshape(count, wide, ch)

    edge = 2 * wide
    ag_rows = ((0, edge + packed), (edge + packed, packed))
    band_rows = rows // HALVES

    def unpack_half(ph, block, q, target):
        if q == 0:
            pad[8:8 + wide, :] = hold[ph, block, 0:wide, :].astype(F32)
            pad[8 + wide + cells:8 + 2 * wide + cells, :] = hold[ph, block, wide:edge, :].astype(F32)
            shift(target, 0, 1)
            shift(target, rows + 1, 1)
        for j in range(2):
            start = edge + q * packed + j * (packed - unpack.shape[3])
            at = 8 + wide + q * band + j * (band // 2)
            pad[at:at + band // 2, :] = dot(unpack[q, j], hold[ph, block, start:start + unpack.shape[3], :])

        for i in range(band_rows // strip):
            shift(target, 1 + q * band_rows + i * strip, strip)

    def add_conv(q, field, taps, turned_taps=None):
        first, last = (0, band_rows - 1) if q == 0 else (band_rows - 1, rows)
        count = last - first
        size = (count + 2) * wide
        lhs = jnp.concatenate([
            field[first + i:last + 2 + i, :, :].reshape(size, 3 * ch) for i in range(2)], axis=1)
        if turned_taps is None:
            none = jnp.zeros((3 * ch, ch), BF16)
            rhs = jnp.concatenate([
                jnp.concatenate([taps(0), taps(2)], axis=1), jnp.concatenate([taps(1), none], axis=1)], axis=0)
            value = dot(lhs, rhs)
        else:
            def row_taps(a):
                return [turned_taps(3 * (2 - a) + 2 - b) for b in range(3)]
            none = jnp.zeros((ch, 3 * ch), BF16)
            rhs = jnp.concatenate([
                jnp.concatenate(row_taps(0) + row_taps(1), axis=1), jnp.concatenate(row_taps(2) + [none], axis=1)], axis=0)
            value = lax.dot_general(lhs, rhs, (((1,), (1,)), ((), ())), preferred_element_type=F32)
        at = pl.ds(first * wide, count * wide)
        acc[at, :] = acc[at, :] + value[0:count * wide, 0:ch] + value[2 * wide:size, ch:2 * ch]

    def ag_copy(ph, block, q, sign):
        at = pl.ds(*ag_rows[q])
        return pltpu.make_async_remote_copy(
            src_ref=hold.at[ph, block, at, :], dst_ref=hold.at[ph, block, at, :],
            send_sem=ag_ssem.at[ph, (1 - sign) // 2, block, q], recv_sem=ag_rsem.at[ph, block, q],
            device_id=(z + sign, s), device_id_type=MESH)

    def pack_field(ph, source, fill=None, first=None):
        if fill is not None:
            fill(cells, edge, 0)
        hold[ph, z, 0:edge, :] = source[cells:cells + edge, :].astype(BF16)
        for q in range(HALVES):
            if first is not None:
                first(q)
            if fill is not None:
                chunked(fill, 0, q * band, band)
            hold[ph, z, edge + q * packed:edge + (q + 1) * packed, :] = dot(
                pack[q], source[q * band:(q + 1) * band, :].astype(BF16)).astype(BF16)
            for sign in (1, -1):
                @pl.when((z + sign >= 0) & (z + sign < n))
                def _():
                    ag_copy(ph, z, q, sign).start()

    def inside(slice_at):
        return (slice_at >= 0) & (slice_at < n)

    def take_and_pass(ph, k, q, sign, passes=True, takes=True):
        block = z - k * sign

        @pl.when((k > 0) & inside(block))
        def _():
            if passes and takes:
                ag_copy(ph, block, q, sign).wait_recv()

            @pl.when(inside(z + sign))
            def _():
                if passes:
                    if not takes:
                        ag_copy(ph, block, q, sign).wait_recv()
                    ag_copy(ph, block, q, sign).start()

            if not passes:
                @pl.when(jnp.logical_not(inside(z + sign)))
                def _():
                    ag_copy(ph, block, q, sign).wait_recv()

    near = jnp.where(z < n - n // 2, 1, 0)

    def consume_way(k, q, way, consume):
        block = z - k * (1 - 2 * way)

        @pl.when((k >= 0) & (k < n) & inside(block) & ((k > 0) | (way == near)))
        def _():
            consume(k, block, q)

    def take_both(ph, k, q, **how):
        @pl.loop(0, 2)
        def _(i):
            way = (near + i) % 2
            take_and_pass(ph, k, q, 1 - 2 * way, **how)

    def gather(ph, consume, each):
        @pl.loop(0, n)
        def _(k):
            for q in range(HALVES):
                take_both(ph, k, q)
                if q:
                    consume_way(k, q - 1, 1 - near, consume)
                else:
                    consume_way(k - 1, HALVES - 1, 1 - near, consume)
                consume_way(k, q, near, consume)
            each(k)

    def gather_passing_first(ph, consume, each):
        @pl.loop(0, n)
        def _(k):
            @pl.when(k == 1)
            def _():
                @pl.loop(1, n)
                def _(ahead):
                    for q in range(HALVES):
                        take_both(ph, ahead, q, takes=False)
            for q in range(HALVES):
                take_both(ph, k, q, passes=False)

                @pl.loop(0, 2)
                def _(i):
                    consume_way(k, q, (near + i) % 2, consume)
            each(k)

    last_step = jnp.maximum(z, n - 1 - z)

    last_pass = jnp.maximum(jnp.where(z < n - 1, z, 0), jnp.where(z > 0, n - 1 - z, 0))

    def forward(ph, field):
        def consume(k, block, q):
            into = taken.at[block]
            unpack_half(ph, block, q, into)

            @pl.when(k == 0)
            def _():
                add_conv(q, into, lambda a: wv[ph, z, 3 * a * ch:3 * (a + 1) * ch, :])

            @pl.when(k > 0)
            def _():
                slot = slot_of(block)
                if q == 0:
                    weights_arrived(ph, slot)
                add_conv(q, into, lambda a: wf[ph, slot, 3 * a * ch:3 * (a + 1) * ch, :])

            if q == 0:
                pl.when(k == last_step)(lambda: early_moments(ph))

        def each(k):
            if ph == 1:
                pl.when(k == 0)(weights_to_core)
            else:
                @pl.when(k == 0)
                def _():
                    weights_round(0)

                @pl.when(k == 1)
                def _():
                    weights_over_z(1)

                @pl.when(k == last_pass)
                def _():
                    load_cotangent()
        (gather if ph else gather_passing_first)(ph, consume, each)

    def turn_field(ph, field):
        main = [field[start:start + ch, :].T for start in range(0, cells, ch)]
        ends = field[cells:cells + edge, :]
        if edge < ch:
            ends = jnp.concatenate([ends, jnp.zeros((ch - edge, ch), F32)], axis=0)
        ends = ends.T
        for i, here in enumerate(main):
            left = jnp.concatenate(
                [ends[:, 0:wide] if i == 0 else main[i - 1][:, ch - wide:], here[:, 0:ch - wide]], axis=1)
            right = jnp.concatenate(
                [here[:, wide:], main[i + 1][:, 0:wide] if i + 1 < len(main) else ends[:, wide:edge]], axis=1)
            for a, v in enumerate((left, here, right)):
                x_t[ph, a * ch:(a + 1) * ch, i * ch:(i + 1) * ch] = v.astype(BF16)


    def c_copy(ph, j):
        return pltpu.make_async_remote_copy(
            src_ref=psend.at[ph, j], dst_ref=crecv.at[ph, j],
            send_sem=c_ssem.at[ph, j], recv_sem=c_rsem.at[ph, j],
            device_id=(z, chip * 2 + 1 - core), device_id_type=MESH)

    def q_copy(ph, j, e, whose, owner):
        return pltpu.make_async_remote_copy(
            src_ref=hsend.at[ph, j, owner], dst_ref=qrecv.at[ph, j, whose],
            send_sem=q_ssem.at[ph, j, e], recv_sem=q_rsem.at[ph, j, whose],
            device_id=(z, ((chip + e) % chips) * 2 + core), device_id_type=MESH)

    def f_copy(ph, j, e, owner):
        return pltpu.make_async_remote_copy(
            src_ref=wout.at[ph, j, core, owner], dst_ref=wout.at[ph, j, core, owner],
            send_sem=f_ssem.at[ph, j, e], recv_sem=f_rsem.at[ph, j, owner],
            device_id=(z, ((chip + e) % chips) * 2 + core), device_id_type=MESH)

    def h_copy(ph, j, whose):
        return pltpu.make_async_remote_copy(
            src_ref=wout.at[ph, j, whose], dst_ref=wout.at[ph, j, whose],
            send_sem=h_ssem.at[ph, j], recv_sem=h_rsem.at[ph, j],
            device_id=(z, chip * 2 + 1 - core), device_id_type=MESH)

    def o_copy(ph, j):
        target = (out_wg1, out_wg2)[ph]
        if aligned:
            target = target.at[:, :, :, pl.ds(pl.multiple_of(j * ch, ch), ch)]
        else:
            target = target.at[j]
        return pltpu.make_async_copy(wout.at[ph, j], target, o_sem.at[ph, j])

    def sum_cores(ph, j):
        for o in range(owners):
            psend[ph, j, o] = part[ph, j, 1 - core, o].astype(BF16)
        c_copy(ph, j).start()

    def sum_chips(ph, j):
        c_copy(ph, j).wait_recv()
        for o in range(owners):
            v = part[ph, j, core, o] + crecv[ph, j, o].astype(F32)
            part[ph, j, core, o] = v
            hsend[ph, j, o] = v.astype(BF16)

        @pl.loop(1, chips)
        def _(e):
            peer = (chip + e) % chips

            @pl.when(peer < owners)
            def _():
                q_copy(ph, j, e, chip, peer).start()

    def spread_chips(ph, j):
        @pl.when(chip < owners)
        def _():
            @pl.loop(1, chips)
            def _(e):
                q_copy(ph, j, e, (chip + e) % chips, chip).wait_recv()
            v = part[ph, j, core, chip]
            for e in range(1, chips):
                v = v + qrecv[ph, j, (chip + e) % chips].astype(F32)
            wout[ph, j, core, chip] = v.astype(BF16)

            @pl.loop(1, chips)
            def _(e):
                f_copy(ph, j, e, chip).start()

    def spread_cores(ph, j):
        @pl.loop(1, chips)
        def _(e):
            peer = (chip + e) % chips

            @pl.when(peer < owners)
            def _():
                f_copy(ph, j, e, peer).wait_recv()
        h_copy(ph, j, core).start()

    def finish(ph, j):
        h_copy(ph, j, 1 - core).wait_recv()
        o_copy(ph, j).start()

    def put_part(ph, j, tap, value):
        start = tap * ch
        done = 0
        while done < ch:
            row = start + done
            side, o, at = row // half_rows, row % half_rows // piece, row % piece
            size = min(ch - done, piece - at)
            part[ph, j, side, o, at:at + size, :] = value[done:done + size, :]
            done += size

    stages = (sum_cores, sum_chips, spread_chips, spread_cores, finish)

    def of_step(k, fn):
        @pl.loop(0, 2)
        def _(way):
            block = z - k * (1 - 2 * way)

            @pl.when((k >= 0) & (k < n) & inside(block) & ((k > 0) | (way == 0)))
            def _():
                fn(block)

    passing = last_pass > 0

    def made_at(step):
        first = jnp.where(passing & (step > 0), jnp.where(step == last_pass, 1, step + 1), step)
        return first, step + 1

    def advance(ph, k):
        for age in range(1, len(stages)):
            step = k - age

            @pl.when((step >= 0) & (step < n))
            def _():
                @pl.loop(*made_at(step))
                def _(made):
                    of_step(made, functools.partial(stages[age], ph))

    def advance_all(ph, age):
        @pl.loop(0, n)
        def _(j):
            stages[age](ph, j)

    def field_grad(ph, block):
        grad = taken[block, 1:rows + 1, :, :].reshape(cells, 3 * ch)
        value = dot(x_t[ph], grad)
        for a in range(3):
            for b in range(3):
                put_part(ph, block, 3 * a + b, value[a * ch:(a + 1) * ch, (2 - b) * ch:(3 - b) * ch])

    def make_grad(ph, block):
        field_grad(ph, block)
        sum_cores(ph, block)

    def inner_sums(first, last, side):
        start = side * (cells - wide)
        row_send[2, side] = acc[start:start + wide, :]
        at = slice(first, last)
        v = acc[at, :] * slope1[at, :]
        slope1[at, :] = v
        acc[at, :] = jnp.zeros((last - first, ch), F32)
        return fold(v * normed1[at, :]), fold(v)

    def early_inner():
        for i, v in enumerate(inner_sums(0, settled, 0)):
            early[8 * i:8 * i + 8, :] = v
        row_copy(2, 0).start()

    def backward(ph):
        last = ph == 0

        def consume(k, block, q):
            into = taken.at[block]
            unpack_half(2 + ph, block, q, into)
            if last and q == HALVES - 1:
                @pl.when((k == 0) | (k >= last_pass))
                def _():
                    make_grad(ph, block)
            add_conv(q, into, None, lambda t: wv[ph, block, t * ch:(t + 1) * ch, :])
            if q == 0 and not last:
                pl.when(k == last_step)(early_inner)

        def each(k):
            first, end = made_at(k)
            if last:
                @pl.loop(first, end - 1)
                def _(step):
                    of_step(step, functools.partial(make_grad, ph))
                advance(ph, k)
                for age in range(2, len(stages)):
                    @pl.when(k == age - 2)
                    def _():
                        advance_all(1, age)
            else:
                @pl.loop(first, jnp.where(passing | (k < n - 1), end, first))
                def _(step):
                    of_step(step, functools.partial(make_grad, ph))
        gather(2 + ph, consume, each)

    def fold(v):
        return jnp.sum(v.reshape(v.shape[0] // 8, 8, ch), axis=0)

    def flatten(v):
        return jnp.sum(v, axis=0, keepdims=True)

    zero = jnp.zeros((8, ch), F32)

    def part_moments(first, last):
        m = mask[first:last, :]
        v = acc[first:last, :]
        number, added = flatten(fold(m)), flatten(fold(v * m))
        c = (v - added / jnp.maximum(number, 1.0)) * m
        return added, number, flatten(fold(c * c))

    def early_moments(slot):
        for i, v in enumerate(part_moments(0, settled)):
            early[i:i + 1, :] = v
        send_row(slot, 0)

    def combine(added, number, spread):
        total_added, total_number = sum(added), sum(number)
        mean = total_added / jnp.maximum(total_number, 1.0)
        about = 0.0
        for a, k, q in zip(added, number, spread):
            off = a / jnp.maximum(k, 1.0) - mean
            about = about + (q + k * off * off)
        return total_added, total_number, about

    def local_moments():
        late = part_moments(settled, cells)
        return combine(*([early[i:i + 1, :], v] for i, v in enumerate(late)))

    def moments(slot):
        take_stats(slot)
        added, number, about = (st_recv[slot, :, i, :] for i in range(3))
        count = flatten(number)
        mean = flatten(added) / count
        off = added / jnp.maximum(number, 1.0) - mean
        return mean, lax.rsqrt(flatten(about + number * off * off) / count + EPSILON), count

    def everywhere(fn):
        chunked(fn, 0)
        fn(cells, 2 * wide, 0)

    gain1, shift1, gain2, shift2 = (r[...] for r in (gain1_in, shift1_in, gain2_in, shift2_in))

    weights_over_z(0)

    quarter = band // 2
    kept = packed // 2
    window = unpack.shape[3]
    below = lax.broadcasted_iota(jnp.int32, (quarter, quarter), 1) < lax.broadcasted_iota(jnp.int32, (quarter, quarter), 0)
    below = below.astype(F32).astype(BF16)

    def make_pack(h):
        for j in range(2):
            lv = mask[h * band + j * quarter:h * band + (j + 1) * quarter, :]
            place = jnp.where(lv > 0.0, dot(below, lv.astype(BF16)) + j * kept, -1.0)
            places[h, j] = place
            across = place.T[0:1, :]
            spot = lax.broadcasted_iota(jnp.int32, (packed, quarter), 0).astype(F32)
            pack[h, :, j * quarter:(j + 1) * quarter] = jnp.where(spot == across, 1.0, 0.0).astype(BF16)

    def make_unpack(h):
        for j in range(2):
            for start in range(0, window, ch):
                size = min(ch, window - start)
                spot = start + j * (packed - window) + lax.broadcasted_iota(jnp.int32, (quarter, size), 1)
                unpack[h, j, :, start:start + size] = jnp.where(
                    places[h, j, :, :size] == spot.astype(F32), 1.0, 0.0).astype(BF16)

    for side in range(2):
        edge_copy(1 - side).wait_recv()
        there = jnp.where(s > 0, 1.0, 0.0) if side == 0 else jnp.where(s < s_count - 1, 1.0, 0.0)
        at = slice(cells + side * wide, cells + (side + 1) * wide)
        masked[at, :] = edge_recv[side, 0].astype(F32) * there
        mask[at, :] = edge_recv[side, 1].astype(F32) * there

    def stats_sent(slot):
        for k in range(1, s_count):
            st_copy(slot, k, s).wait_send()

    def row_sent(slot):
        for side in range(2):
            row_copy(slot, side).wait_send()

    def gathered_sent(ph):
        @pl.loop(0, n)
        def _(k):
            for sign in (1, -1):
                block = z - k * sign

                @pl.when(inside(block) & inside(z + sign))
                def _():
                    for q in range(HALVES):
                        ag_copy(ph, block, q, sign).wait_send()

    def weights_sent(which):
        for k in range(1, n):
            wz_copy(which, k).wait_send()

        @pl.loop(1, owners if which else w_parts)
        def _(k):
            for slot in range(n - 1):
                wp_copy(which, slot, k, chip % owners if which else w_mine).wait_send()
        if which:
            for slot in range(n - 1):
                wh_copy(slot, core).wait_send()

    def grads_sent(ph):
        @pl.loop(0, n)
        def _(j):
            c_copy(ph, j).wait_send()
            h_copy(ph, j, core).wait_send()
            o_copy(ph, j).wait()
            for e in range(1, chips):
                peer = (chip + e) % chips

                @pl.when(peer < owners)
                def _():
                    q_copy(ph, j, e, chip, peer).wait_send()

                @pl.when(chip < owners)
                def _():
                    f_copy(ph, j, e, chip).wait_send()

    block_copy = pltpu.make_async_copy(flat_block, out_block, r_sem.at[0])

    pack_field(0, masked, first=make_pack)
    for h in range(HALVES):
        make_unpack(h)
    forward(0, masked)
    send_stats(0, local_moments())
    send_row(0, 1)
    weights_round(1)
    mean1, scale1, count = moments(0)

    def activate_one(start, size, carry):
        at = pl.ds(start, size)
        main = start is not cells
        nv = ((acc if main else normed1)[at, :] - mean1) * scale1
        normed1[at, :] = nv
        hid[at, :] = gelu_parts(nv * gain1 + shift1)[0] * mask[at, :]
        if main:
            acc[at, :] = jnp.zeros((size, ch), F32)
        return carry

    def slope_one(start, size, carry):
        at = pl.ds(start, size)
        slope1[at, :] = gelu_parts(normed1[at, :] * gain1 + shift1)[1] * mask[at, :]
        return carry

    take_rows(0, normed1)
    pack_field(1, hid, activate_one)
    everywhere(slope_one)
    forward(1, hid)
    send_stats(1, local_moments())
    send_row(1, 1)
    turn_field(0, masked)
    turn_field(1, hid)
    weights_sent(0)
    gathered_sent(0)
    stats_sent(0)
    row_sent(0)
    for side in range(2):
        edge_copy(side).wait_send()
        cot_copy(side).wait_send()
    mean2, scale2, _ = moments(1)

    def activate_two(source, start, size):
        at = pl.ds(start, size)
        nv = (source[at, :] - mean2) * scale2
        normed2[at, :] = nv
        value, slope = gelu_parts(nv * gain2 + shift2 + masked[at, :])
        t = cotm[at, :] * slope
        through[at, :] = t
        return value, nv, t

    def activate_main(start, size, carry):
        value, nv, t = activate_two(acc, start, size)
        at = pl.ds(start, size)
        hid2[at, :] = value * mask[at, :]
        acc[at, :] = jnp.zeros((size, ch), F32)
        return carry[0] + fold(t * nv), carry[1] + fold(t)

    send_stats(2, [flatten(v) for v in chunked(activate_main, (zero, zero))])
    take_rows(1, normed2)
    take_cotangent()
    activate_two(normed2, cells, edge)
    to_flat(hid2, flat_block)
    block_copy.start()
    weights_sent(1)
    gathered_sent(1)

    def gradient_sums(slot):
        take_stats(slot)
        return flatten(st_recv[slot, :, 0, :]), flatten(st_recv[slot, :, 1, :])

    def norm_back(upstream, normed, gain, scale, sums):
        gain_grad, shift_grad = sums
        factor = gain * scale
        level, tilt = shift_grad / count, gain_grad / count

        def fill(start, size, carry):
            at = pl.ds(start, size)
            v = upstream[at, :] - mask[at, :] * (level + normed[at, :] * tilt)
            hid[at, :] = factor * v
            return carry
        return fill

    sums2 = gradient_sums(2)
    pack_field(3, hid, norm_back(through, normed2, gain2, scale2, sums2))
    backward(1)

    parts = inner_sums(settled, cells, 1)
    send_stats(3, [flatten(early[8 * i:8 * i + 8, :] + v) for i, v in enumerate(parts)])
    row_copy(2, 1).start()

    @pl.when(jnp.logical_not(passing))
    def _():
        of_step(n - 1, functools.partial(make_grad, 1))
    for side in range(2):
        row_copy(2, 1 - side).wait_recv()
        at = slice(cells + side * wide, cells + (side + 1) * wide)
        slope1[at, :] = row_recv[2, side] * slope1[at, :]
    stats_sent(1)
    row_sent(1)
    stats_sent(2)
    gathered_sent(3)
    sums1 = gradient_sums(3)
    pack_field(2, hid, norm_back(slope1, normed1, gain1, scale1, sums1))
    advance_all(1, 1)
    backward(0)
    advance(0, n)

    def finish_input(start, size, carry):
        at = pl.ds(start, size)
        acc[at, :] = (acc[at, :] + through[at, :]) * mask[at, :]
        return carry

    chunked(finish_input, 0)
    to_flat(acc, flat_input)
    input_copy = pltpu.make_async_copy(flat_input, out_input, r_sem.at[1])
    input_copy.start()
    out_gain1[...], out_shift1[...] = sums1
    out_gain2[...], out_shift2[...] = sums2
    for extra in range(1, len(stages) - 1):
        advance(0, n + extra)

    stats_sent(3)
    row_sent(2)
    gathered_sent(2)
    grads_sent(1)
    grads_sent(0)
    block_copy.wait()
    input_copy.wait()


def finish_kernel(count, *refs):
    ins, outs = refs[:count], refs[count:2 * count]
    narrow, wide, in_sem, out_sem, take_sem, give_sem = refs[2 * count:2 * count + 6]
    held = refs[2 * count + 6:]
    rows = narrow.shape[1] // FINISH_PARTS
    parts = [(w, i, pl.ds(i * rows, rows)) for i in range(FINISH_PARTS) for w in range(2)]
    loads = [pltpu.make_async_copy(ins[w].at[at, :], narrow.at[w, at, :], in_sem.at[w, i]) for w, i, at in parts]
    stores = [pltpu.make_async_copy(wide.at[w, at, :], outs[w].at[at, :], out_sem.at[w, i]) for w, i, at in parts]
    takes = [pltpu.make_async_copy(ins[2 + k], v, take_sem.at[k]) for k, v in enumerate(held)]
    gives = [pltpu.make_async_copy(v, outs[2 + k], give_sem.at[k]) for k, v in enumerate(held)]
    for copy in loads + takes:
        copy.start()
    for load, store, (w, i, at) in zip(loads, stores, parts):
        load.wait()
        wide[w, at, :] = narrow[w, at, :].astype(F32)
        store.start()
    for take, give in zip(takes, gives):
        take.wait()
        give.start()
    for copy in stores + gives:
        copy.wait()


def per_device(n, s_count, blocks, weight_one, weight_two, gain_one, shift_one, gain_two, shift_two, cell_live, cotangent):
    rows, wide = cell_live.shape
    ch = blocks.shape[1] // wide
    cells = rows * wide
    total = cells + 2 * wide
    packed = 2 * -(-most_live(rows // HALVES // 2, wide) // 8) * 8
    aligned = ch % 128 == 0
    chips = s_count // 2
    tap_rows = 9 * ch
    half_rows = tap_rows // 2
    owners = math.gcd(half_rows // 16, chips)
    piece = half_rows // owners

    if aligned:
        weight_one, weight_two = (w.reshape(tap_rows, n * ch) for w in (weight_one, weight_two))
    else:
        weight_one, weight_two = (
            w.reshape(tap_rows, n, ch).transpose(1, 0, 2) for w in (weight_one, weight_two))
    grad_shape = (2, owners, piece, n * ch) if aligned else (n, 2, owners, piece, ch)
    vmem = pl.BlockSpec(memory_space=pltpu.VMEM)
    hbm = pl.BlockSpec(memory_space=pl.ANY)
    sem = pltpu.SemaphoreType.DMA
    field = pltpu.VMEM((total, ch), F32)
    scratch = [
        pltpu.VMEM((ch * wide, 128), F32),
        pltpu.VMEM((2, n, tap_rows, ch), BF16),
        pltpu.VMEM((2, n - 1, tap_rows, ch), BF16),
        pltpu.VMEM((2, 3 * ch, cells), BF16),
        pltpu.VMEM((HALVES, packed, cells // HALVES), BF16),
        pltpu.VMEM((HALVES, 2, cells // HALVES // 2, -(-packed // 2 // 16) * 16), BF16),
        pltpu.VMEM((HALVES, 2, cells // HALVES // 2, ch), F32),
        pltpu.VMEM((2, 2, wide, ch), BF16),
        pltpu.VMEM((2, 2, wide, ch), BF16),
        pltpu.VMEM((2, wide, ch), BF16),
        pltpu.VMEM((2, wide, ch), BF16),
        field, field, field, field, field, field, field, field, field,
        pltpu.VMEM((total + 16, ch), F32),
        pltpu.VMEM((cells, ch), F32),
        pltpu.VMEM((4, n, 2 * wide + HALVES * packed, ch), BF16),
        pltpu.VMEM((n, rows + 3, wide, 3 * ch), BF16),
        pltpu.VMEM((2, n, 2, owners, piece, ch), F32),
        pltpu.VMEM((2, n, owners, piece, ch), BF16),
        pltpu.VMEM((2, n, owners, piece, ch), BF16),
        pltpu.VMEM((2, n, owners, piece, ch), BF16),
        pltpu.VMEM((2, n, chips, piece, ch), BF16),
        pltpu.VMEM((2, n, 2, owners, piece, ch), BF16),
        pltpu.VMEM((4, 8, ch), F32),
        pltpu.VMEM((4, s_count, 8, ch), F32),
        pltpu.VMEM((3, 2, wide, ch), F32),
        pltpu.VMEM((3, 2, wide, ch), F32),
        pltpu.VMEM((16, ch), F32),
        pltpu.VMEM((rows, ch * wide), BF16),
        pltpu.VMEM((rows, ch * wide), F32),
        sem((2, n)),
        sem((2, n)), sem((2, n)),
        sem((2, n - 1, s_count)), sem((2, n - 1, s_count)),
        sem((n - 1,)), sem((n - 1,)),
        sem((2,)), sem((2,)),
        sem((2,)), sem((2,)),
        sem((4, 2, n, HALVES)), sem((4, n, HALVES)),
        sem((4, s_count)), sem((4, s_count)),
        sem((3, 2)), sem((3, 2)),
        sem((2, n)), sem((2, n)),
        sem((2, n, chips)), sem((2, n, chips)),
        sem((2, n, chips)), sem((2, n, chips)),
        sem((2, n)), sem((2, n)),
        sem((2, n)),
        sem((2,)),
    ]
    block_out, input_grad, wg1, wg2, *sums = pl.pallas_call(
        functools.partial(block_kernel, n, s_count, rows, wide, ch, aligned, packed),
        out_shape=(
            jax.ShapeDtypeStruct((rows, ch * wide), BF16),
            jax.ShapeDtypeStruct((rows, ch * wide), F32),
            jax.ShapeDtypeStruct(grad_shape, BF16),
            jax.ShapeDtypeStruct(grad_shape, BF16),
            *[jax.ShapeDtypeStruct((1, ch), F32)] * 4,
        ),
        in_specs=[vmem] * 7 + [hbm] * 2,
        out_specs=(hbm, hbm, hbm, hbm, vmem, vmem, vmem, vmem),
        scratch_shapes=scratch,
        compiler_params=pltpu.CompilerParams(
            collective_id=0, has_side_effects=True, vmem_limit_bytes=60 * 1024 * 1024),
    )(blocks, cotangent, cell_live.T,
      *(v.reshape(1, ch) for v in (gain_one, shift_one, gain_two, shift_two)), weight_one, weight_two)

    if not aligned:
        def whole(grad):
            grad = grad.reshape(n, tap_rows, ch).transpose(1, 0, 2)
            return grad.astype(F32).reshape(9, ch, n * ch)
        return (block_out, input_grad, whole(wg1), whole(wg2), *(v.reshape(ch) for v in sums))

    wg1, wg2 = (w.reshape(tap_rows, n * ch) for w in (wg1, wg2))
    wide_grad = jax.ShapeDtypeStruct((tap_rows, n * ch), F32)
    moved = (block_out, input_grad, *sums)
    grad1, grad2, *moved = pl.pallas_call(
        functools.partial(finish_kernel, 2 + len(moved)),
        out_shape=(wide_grad, wide_grad, *(jax.ShapeDtypeStruct(v.shape, v.dtype) for v in moved)),
        in_specs=[pl.BlockSpec(memory_space=pl.ANY)] * (2 + len(moved)),
        out_specs=[pl.BlockSpec(memory_space=pl.ANY)] * (2 + len(moved)),
        scratch_shapes=[
            pltpu.VMEM((2, tap_rows, n * ch), BF16), pltpu.VMEM((2, tap_rows, n * ch), F32),
            sem((2, FINISH_PARTS)), sem((2, FINISH_PARTS)), sem((len(moved),)), sem((len(moved),)),
            *(pltpu.VMEM(v.shape, v.dtype) for v in moved),
        ],
        compiler_params=pltpu.CompilerParams(vmem_limit_bytes=64 * 1024 * 1024),
    )(wg1, wg2, *moved)
    block_out, input_grad, *sums = moved
    grads = (g.reshape(9, ch, n * ch) for g in (grad1, grad2))
    return (block_out, input_grad, *grads, *(v.reshape(ch) for v in sums))


def solution(mesh):
    return jax.shard_map(
        functools.partial(per_device, mesh.shape["chan"], mesh.shape["space"]),
        mesh=mesh,
        in_specs=(
            P("space", "chan"),
            P(None, "chan", None),
            P(None, "chan", None),
            P("chan"),
            P("chan"),
            P("chan"),
            P("chan"),
            P("space", None),
            P("space", "chan"),
        ),
        out_specs=(
            P("space", "chan"),
            P("space", "chan"),
            P(None, "chan", None),
            P(None, "chan", None),
            P("chan"),
            P("chan"),
            P("chan"),
            P("chan"),
        ),
        check_vma=False,
    )
```

```python
import functools
import math

import jax
import jax.numpy as jnp
from jax import lax
from jax.experimental import pallas as pl
from jax.experimental.pallas import tpu as pltpu
from jax.sharding import PartitionSpec as P

EPSILON = 1e-05
MESH = pl.DeviceIdType.MESH
F32 = jnp.float32
BF16 = jnp.bfloat16
ROOT_HALF = 0.7071067811865476
ROOT_TWO_PI = 0.3989422804014327
CHUNK = 64
FINISH_PARTS = 4
UNROLL = 2
HALVES = 2
LARGE, SMALL = 7, 3


def dot(a, b):
    return jnp.dot(a, b, preferred_element_type=F32)


def gelu_parts(v):
    upper = 0.5 * (1.0 + lax.erf(v * ROOT_HALF))
    slope = upper + v * (ROOT_TWO_PI * jnp.exp(-0.5 * v * v))
    return v * upper, slope


def most_live(rows, wide):
    units = (wide + 1) // (SMALL + 1)
    live_rows = rows - rows // (LARGE + 1)
    return min(rows * wide, math.ceil(units * live_rows * LARGE / 2))


def block_kernel(n, s_count, rows, wide, ch, aligned, packed, *refs):
    (x_in, cot_in, live_in, gain1_in, shift1_in, gain2_in, shift2_in, w1_hbm, w2_hbm) = refs[:9]
    (out_block, out_input, out_wg1, out_wg2, out_gain1, out_shift1, out_gain2, out_shift2) = refs[9:17]
    (turned, wv, wf, x_t, pack, unpack, places, edge_send, edge_recv, cot_send, cot_recv, cotm, mask, masked,
     normed1, normed2, through, slope1, hid, hid2, pad, acc, hold, taken,
     part, psend, crecv, hsend, qrecv, wout, st_send, st_recv, row_send, row_recv, early, flat_block, flat_input,
     w_sem, wz_ssem, wz_rsem, wp_ssem, wp_rsem, e_ssem, e_rsem, ce_ssem, ce_rsem, ag_ssem, ag_rsem,
     st_ssem, st_rsem, row_ssem, row_rsem, c_ssem, c_rsem, q_ssem, q_rsem,
     f_ssem, f_rsem, h_ssem, h_rsem, o_sem, r_sem) = refs[17:]

    z = lax.axis_index("chan")
    s = lax.axis_index("space")
    cells = rows * wide
    total = cells + 2 * wide
    band = cells // HALVES
    core, chip, chips = s % 2, s // 2, s_count // 2
    before, after = (s + s_count - 1) % s_count, (s + 1) % s_count
    tap_rows = 9 * ch

    barrier = pltpu.get_barrier_semaphore()

    @pl.loop(1, s_count)
    def _(k):
        pl.semaphore_signal(barrier, inc=1, device_id=(z, (s + k) % s_count), device_id_type=MESH)

    @pl.loop(1, n)
    def _(k):
        pl.semaphore_signal(barrier, inc=1, device_id=((z + k) % n, s), device_id_type=MESH)

    w_copies = []
    for which, source in enumerate((w1_hbm, w2_hbm)):
        for d in range(n):
            block = source.at[:, d * ch:(d + 1) * ch] if aligned else source.at[d]
            w_copies.append(pltpu.make_async_copy(block, wv.at[which, d], w_sem.at[which, d]))
    for copy in w_copies:
        copy.start()

    def chunked(fn, init, first=0, count=cells):
        def step(i, carry):
            return fn(pl.multiple_of(first + i * CHUNK, CHUNK), CHUNK, carry)
        return lax.fori_loop(0, count // CHUNK, step, init, unroll=UNROLL)

    lanes = 128
    tiles = ch * wide // lanes

    def from_flat(flat, put):
        for i in range(tiles):
            turned[i * lanes:(i + 1) * lanes, 0:rows] = flat[:, i * lanes:(i + 1) * lanes].astype(F32).T
        for w in range(wide):
            put(pl.ds(w, rows, stride=wide), turned[pl.ds(w, ch, stride=wide), 0:rows].T)

    def to_flat(source, flat):
        for w in range(wide):
            turned[pl.ds(w, ch, stride=wide), 0:rows] = source[pl.ds(w, rows, stride=wide), :].T
        for i in range(tiles):
            flat[:, i * lanes:(i + 1) * lanes] = turned[i * lanes:(i + 1) * lanes, 0:rows].T.astype(flat.dtype)

    def put_masked(at, value):
        masked[at, :] = value

    from_flat(x_in, put_masked)

    cell = lax.broadcasted_iota(jnp.int32, (cells, rows), 0)
    pick = (cell // wide == lax.broadcasted_iota(jnp.int32, (cells, rows), 1)).astype(F32).astype(BF16)
    column_of = lax.broadcasted_iota(jnp.int32, (cells, wide), 0) % wide
    picked = lax.dot_general(pick, live_in[...].astype(BF16), (((1,), (1,)), ((), ())), preferred_element_type=F32)
    picked = jnp.where(column_of == lax.broadcasted_iota(jnp.int32, (cells, wide), 1), picked, 0.0)
    mask[0:cells, :] = dot(picked.astype(BF16), jnp.ones((wide, ch), BF16))

    def load_main(start, size, carry):
        at = pl.ds(start, size)
        lv = mask[at, :]
        masked[at, :] = masked[at, :] * lv
        return carry

    chunked(load_main, 0)
    for side, start in ((0, 0), (1, cells - wide)):
        edge_send[side, 0] = masked[start:start + wide, :].astype(BF16)
        edge_send[side, 1] = mask[start:start + wide, :].astype(BF16)

    acc[...] = jnp.zeros_like(acc)
    for block in range(n):
        for row in (rows // HALVES + 1, rows + 2):
            taken[block, row:row + 1, :, :] = jnp.zeros((1, wide, 3 * ch), BF16)
    st_send[...] = jnp.zeros_like(st_send)

    pl.semaphore_wait(barrier, s_count - 1 + n - 1)

    def edge_copy(side):
        return pltpu.make_async_remote_copy(
            src_ref=edge_send.at[side], dst_ref=edge_recv.at[1 - side],
            send_sem=e_ssem.at[side], recv_sem=e_rsem.at[1 - side],
            device_id=(z, before if side == 0 else after), device_id_type=MESH)

    for side in range(2):
        edge_copy(side).start()

    def cot_copy(side):
        return pltpu.make_async_remote_copy(
            src_ref=cot_send.at[side], dst_ref=cot_recv.at[1 - side],
            send_sem=ce_ssem.at[side], recv_sem=ce_rsem.at[1 - side],
            device_id=(z, before if side == 0 else after), device_id_type=MESH)

    def load_cotangent():
        def put(at, value):
            cotm[at, :] = value
        from_flat(cot_in, put)

        def live_only(start, size, carry):
            at = pl.ds(start, size)
            cotm[at, :] = cotm[at, :] * mask[at, :]
            return carry
        chunked(live_only, 0)
        for side, start in ((0, 0), (1, cells - wide)):
            cot_send[side] = cotm[start:start + wide, :].astype(BF16)
            cot_copy(side).start()

    def take_cotangent():
        for side in range(2):
            cot_copy(1 - side).wait_recv()
            at = slice(cells + side * wide, cells + (side + 1) * wide)
            cotm[at, :] = cot_recv[side].astype(F32) * mask[at, :]

    w_parts = math.gcd(tap_rows // 16, s_count)
    w_rows = tap_rows // w_parts
    w_mine = s % w_parts
    w_group = s - w_mine

    def wz_copy(which, k):
        at = pl.ds(w_mine * w_rows, w_rows)
        slot = n - k - 1
        return pltpu.make_async_remote_copy(
            src_ref=wv.at[which, (z + k) % n, at, :], dst_ref=wf.at[which, slot, at, :],
            send_sem=wz_ssem.at[which, slot], recv_sem=wz_rsem.at[which, slot],
            device_id=((z + k) % n, s), device_id_type=MESH)

    def wp_copy(which, slot, k, whose):
        at = pl.ds(whose * w_rows, w_rows)
        return pltpu.make_async_remote_copy(
            src_ref=wf.at[which, slot, at, :], dst_ref=wf.at[which, slot, at, :],
            send_sem=wp_ssem.at[which, slot, k], recv_sem=wp_rsem.at[which, slot, whose],
            device_id=(z, w_group + (w_mine + k) % w_parts), device_id_type=MESH)

    def weights_over_z(which):
        for copy in w_copies[which * n:(which + 1) * n]:
            copy.wait()

        @pl.loop(1, n)
        def _(k):
            wz_copy(which, k).start()

    def slot_of(block):
        return (block - z + n - 1) % n

    def weights_round(which):
        @pl.loop(1, n)
        def _(distance):
            for sign in (1, -1):
                block = z - distance * sign

                @pl.when((block >= 0) & (block < n))
                def _():
                    slot = slot_of(block)
                    wz_copy(which, n - 1 - slot).wait_recv()

                    @pl.loop(1, w_parts)
                    def _(k):
                        wp_copy(which, slot, k, w_mine).start()

    def weights_arrived(which, slot):
        @pl.loop(1, w_parts)
        def _(k):
            wp_copy(which, slot, k, (w_mine + k) % w_parts).wait_recv()

    def row_copy(slot, side):
        return pltpu.make_async_remote_copy(
            src_ref=row_send.at[slot, side], dst_ref=row_recv.at[slot, 1 - side],
            send_sem=row_ssem.at[slot, side], recv_sem=row_rsem.at[slot, 1 - side],
            device_id=(z, before if side == 0 else after), device_id_type=MESH)

    def send_row(slot, side):
        start = side * (cells - wide)
        row_send[slot, side] = acc[start:start + wide, :]
        row_copy(slot, side).start()

    settled = (rows // HALVES - 1) * wide

    def take_rows(slot, ref):
        for side in range(2):
            row_copy(slot, 1 - side).wait_recv()
            ref[cells + side * wide:cells + (side + 1) * wide, :] = row_recv[slot, side]

    def st_copy(slot, k, whose):
        return pltpu.make_async_remote_copy(
            src_ref=st_send.at[slot], dst_ref=st_recv.at[slot, whose],
            send_sem=st_ssem.at[slot, k], recv_sem=st_rsem.at[slot, whose],
            device_id=(z, (s + k) % s_count), device_id_type=MESH)

    def send_stats(slot, values):
        for i, v in enumerate(values):
            st_send[slot, i:i + 1, :] = v
        for k in range(1, s_count):
            st_copy(slot, k, s).start()
        st_recv[slot, s] = st_send[slot]

    def take_stats(slot):
        for k in range(1, s_count):
            st_copy(slot, k, (s + k) % s_count).wait_recv()

    strip = 8
    column = lax.broadcasted_iota(jnp.int32, (strip * wide, ch), 0) % wide

    def shift(target, first, count):
        size = count * wide
        where = column[:size]
        here = pad[pl.ds(8 + first * wide, size), :]
        left = jnp.where(where == 0, 0.0, pad[pl.ds(7 + first * wide, size), :])
        right = jnp.where(where == wide - 1, 0.0, pad[pl.ds(9 + first * wide, size), :])
        for b, v in enumerate((left, here, right)):
            target[pl.ds(first, count), :, b * ch:(b + 1) * ch] = v.astype(BF16).reshape(count, wide, ch)

    edge = 2 * wide
    ag_rows = ((0, edge + packed), (edge + packed, packed))
    band_rows = rows // HALVES

    def unpack_half(ph, block, q, target):
        if q == 0:
            pad[8:8 + wide, :] = hold[ph, block, 0:wide, :].astype(F32)
            pad[8 + wide + cells:8 + 2 * wide + cells, :] = hold[ph, block, wide:edge, :].astype(F32)
            shift(target, 0, 1)
            shift(target, rows + 1, 1)
        for j in range(2):
            start = edge + q * packed + j * (packed - unpack.shape[3])
            at = 8 + wide + q * band + j * (band // 2)
            pad[at:at + band // 2, :] = dot(unpack[q, j], hold[ph, block, start:start + unpack.shape[3], :])

        for i in range(band_rows // strip):
            shift(target, 1 + q * band_rows + i * strip, strip)

    def add_conv(q, field, taps, turned_taps=None):
        first, last = (0, band_rows - 1) if q == 0 else (band_rows - 1, rows)
        count = last - first
        size = (count + 2) * wide
        lhs = jnp.concatenate([
            field[first + i:last + 2 + i, :, :].reshape(size, 3 * ch) for i in range(2)], axis=1)
        if turned_taps is None:
            none = jnp.zeros((3 * ch, ch), BF16)
            rhs = jnp.concatenate([
                jnp.concatenate([taps(0), taps(2)], axis=1), jnp.concatenate([taps(1), none], axis=1)], axis=0)
            value = dot(lhs, rhs)
        else:
            def row_taps(a):
                return [turned_taps(3 * (2 - a) + 2 - b) for b in range(3)]
            none = jnp.zeros((ch, 3 * ch), BF16)
            rhs = jnp.concatenate([
                jnp.concatenate(row_taps(0) + row_taps(1), axis=1), jnp.concatenate(row_taps(2) + [none], axis=1)], axis=0)
            value = lax.dot_general(lhs, rhs, (((1,), (1,)), ((), ())), preferred_element_type=F32)
        at = pl.ds(first * wide, count * wide)
        acc[at, :] = acc[at, :] + value[0:count * wide, 0:ch] + value[2 * wide:size, ch:2 * ch]

    def ag_copy(ph, block, q, sign):
        at = pl.ds(*ag_rows[q])
        return pltpu.make_async_remote_copy(
            src_ref=hold.at[ph, block, at, :], dst_ref=hold.at[ph, block, at, :],
            send_sem=ag_ssem.at[ph, (1 - sign) // 2, block, q], recv_sem=ag_rsem.at[ph, block, q],
            device_id=(z + sign, s), device_id_type=MESH)

    def pack_field(ph, source, fill=None, first=None):
        if fill is not None:
            fill(cells, edge, 0)
        hold[ph, z, 0:edge, :] = source[cells:cells + edge, :].astype(BF16)
        for q in range(HALVES):
            if first is not None:
                first(q)
            if fill is not None:
                chunked(fill, 0, q * band, band)
            hold[ph, z, edge + q * packed:edge + (q + 1) * packed, :] = dot(
                pack[q], source[q * band:(q + 1) * band, :].astype(BF16)).astype(BF16)
            for sign in (1, -1):
                @pl.when((z + sign >= 0) & (z + sign < n))
                def _():
                    ag_copy(ph, z, q, sign).start()

    def inside(slice_at):
        return (slice_at >= 0) & (slice_at < n)

    def take_and_pass(ph, k, q, sign, passes=True, takes=True):
        block = z - k * sign

        @pl.when((k > 0) & inside(block))
        def _():
            if passes and takes:
                ag_copy(ph, block, q, sign).wait_recv()

            @pl.when(inside(z + sign))
            def _():
                if passes:
                    if not takes:
                        ag_copy(ph, block, q, sign).wait_recv()
                    ag_copy(ph, block, q, sign).start()

            if not passes:
                @pl.when(jnp.logical_not(inside(z + sign)))
                def _():
                    ag_copy(ph, block, q, sign).wait_recv()

    near = jnp.where(z < n - n // 2, 1, 0)

    def consume_way(k, q, way, consume):
        block = z - k * (1 - 2 * way)

        @pl.when((k >= 0) & (k < n) & inside(block) & ((k > 0) | (way == near)))
        def _():
            consume(k, block, q)

    def take_both(ph, k, q, **how):
        @pl.loop(0, 2)
        def _(i):
            way = (near + i) % 2
            take_and_pass(ph, k, q, 1 - 2 * way, **how)

    def gather(ph, consume, each):
        @pl.loop(0, n)
        def _(k):
            for q in range(HALVES):
                take_both(ph, k, q)
                if q:
                    consume_way(k, q - 1, 1 - near, consume)
                else:
                    consume_way(k - 1, HALVES - 1, 1 - near, consume)
                consume_way(k, q, near, consume)
            each(k)

    def gather_passing_first(ph, consume, each):
        @pl.loop(0, n)
        def _(k):
            @pl.when(k == 1)
            def _():
                @pl.loop(1, n)
                def _(ahead):
                    for q in range(HALVES):
                        take_both(ph, ahead, q, takes=False)
            for q in range(HALVES):
                take_both(ph, k, q, passes=False)

                @pl.loop(0, 2)
                def _(i):
                    consume_way(k, q, (near + i) % 2, consume)
            each(k)

    last_step = jnp.maximum(z, n - 1 - z)

    last_pass = jnp.maximum(jnp.where(z < n - 1, z, 0), jnp.where(z > 0, n - 1 - z, 0))

    def forward(ph, field):
        def consume(k, block, q):
            into = taken.at[block]
            unpack_half(ph, block, q, into)

            @pl.when(k == 0)
            def _():
                add_conv(q, into, lambda a: wv[ph, z, 3 * a * ch:3 * (a + 1) * ch, :])

            @pl.when(k > 0)
            def _():
                slot = slot_of(block)
                if q == 0:
                    weights_arrived(ph, slot)
                add_conv(q, into, lambda a: wf[ph, slot, 3 * a * ch:3 * (a + 1) * ch, :])

            if q == 0:
                pl.when(k == last_step)(lambda: early_moments(ph))

        def each(k):
            if ph == 0:
                @pl.when(k == 0)
                def _():
                    weights_round(0)

                @pl.when(k == 1)
                def _():
                    weights_over_z(1)

                @pl.when(k == last_pass)
                def _():
                    load_cotangent()
            if ph == 1:
                pl.when(k == last_pass)(lambda: everywhere(slope_one))
        (gather if ph else gather_passing_first)(ph, consume, each)

    def turn_field(ph, field):
        main = [field[start:start + ch, :].T for start in range(0, cells, ch)]
        ends = field[cells:cells + edge, :]
        if edge < ch:
            ends = jnp.concatenate([ends, jnp.zeros((ch - edge, ch), F32)], axis=0)
        ends = ends.T
        for i, here in enumerate(main):
            left = jnp.concatenate(
                [ends[:, 0:wide] if i == 0 else main[i - 1][:, ch - wide:], here[:, 0:ch - wide]], axis=1)
            right = jnp.concatenate(
                [here[:, wide:], main[i + 1][:, 0:wide] if i + 1 < len(main) else ends[:, wide:edge]], axis=1)
            for a, v in enumerate((left, here, right)):
                x_t[ph, a * ch:(a + 1) * ch, i * ch:(i + 1) * ch] = v.astype(BF16)

    half_rows = tap_rows // 2
    owners = math.gcd(half_rows // 16, chips)
    piece = half_rows // owners

    def c_copy(ph, j):
        return pltpu.make_async_remote_copy(
            src_ref=psend.at[ph, j], dst_ref=crecv.at[ph, j],
            send_sem=c_ssem.at[ph, j], recv_sem=c_rsem.at[ph, j],
            device_id=(z, chip * 2 + 1 - core), device_id_type=MESH)

    def q_copy(ph, j, e, whose, owner):
        return pltpu.make_async_remote_copy(
            src_ref=hsend.at[ph, j, owner], dst_ref=qrecv.at[ph, j, whose],
            send_sem=q_ssem.at[ph, j, e], recv_sem=q_rsem.at[ph, j, whose],
            device_id=(z, ((chip + e) % chips) * 2 + core), device_id_type=MESH)

    def f_copy(ph, j, e, owner):
        return pltpu.make_async_remote_copy(
            src_ref=wout.at[ph, j, core, owner], dst_ref=wout.at[ph, j, core, owner],
            send_sem=f_ssem.at[ph, j, e], recv_sem=f_rsem.at[ph, j, owner],
            device_id=(z, ((chip + e) % chips) * 2 + core), device_id_type=MESH)

    def h_copy(ph, j, whose):
        return pltpu.make_async_remote_copy(
            src_ref=wout.at[ph, j, whose], dst_ref=wout.at[ph, j, whose],
            send_sem=h_ssem.at[ph, j], recv_sem=h_rsem.at[ph, j],
            device_id=(z, chip * 2 + 1 - core), device_id_type=MESH)

    def o_copy(ph, j):
        target = (out_wg1, out_wg2)[ph]
        if aligned:
            target = target.at[:, :, :, pl.ds(pl.multiple_of(j * ch, ch), ch)]
        else:
            target = target.at[j]
        return pltpu.make_async_copy(wout.at[ph, j], target, o_sem.at[ph, j])

    def sum_cores(ph, j):
        for o in range(owners):
            psend[ph, j, o] = part[ph, j, 1 - core, o].astype(BF16)
        c_copy(ph, j).start()

    def sum_chips(ph, j):
        c_copy(ph, j).wait_recv()
        for o in range(owners):
            v = part[ph, j, core, o] + crecv[ph, j, o].astype(F32)
            part[ph, j, core, o] = v
            hsend[ph, j, o] = v.astype(BF16)

        @pl.loop(1, chips)
        def _(e):
            peer = (chip + e) % chips

            @pl.when(peer < owners)
            def _():
                q_copy(ph, j, e, chip, peer).start()

    def spread_chips(ph, j):
        @pl.when(chip < owners)
        def _():
            @pl.loop(1, chips)
            def _(e):
                q_copy(ph, j, e, (chip + e) % chips, chip).wait_recv()
            v = part[ph, j, core, chip]
            for e in range(1, chips):
                v = v + qrecv[ph, j, (chip + e) % chips].astype(F32)
            wout[ph, j, core, chip] = v.astype(BF16)

            @pl.loop(1, chips)
            def _(e):
                f_copy(ph, j, e, chip).start()

    def spread_cores(ph, j):
        @pl.loop(1, chips)
        def _(e):
            peer = (chip + e) % chips

            @pl.when(peer < owners)
            def _():
                f_copy(ph, j, e, peer).wait_recv()
        h_copy(ph, j, core).start()

    def finish(ph, j):
        h_copy(ph, j, 1 - core).wait_recv()
        o_copy(ph, j).start()

    def put_part(ph, j, tap, value):
        start = tap * ch
        done = 0
        while done < ch:
            row = start + done
            side, o, at = row // half_rows, row % half_rows // piece, row % piece
            size = min(ch - done, piece - at)
            part[ph, j, side, o, at:at + size, :] = value[done:done + size, :]
            done += size

    stages = (sum_cores, sum_chips, spread_chips, spread_cores, finish)

    def of_step(k, fn):
        @pl.loop(0, 2)
        def _(way):
            block = z - k * (1 - 2 * way)

            @pl.when((k >= 0) & (k < n) & inside(block) & ((k > 0) | (way == 0)))
            def _():
                fn(block)

    passing = last_pass > 0

    def made_at(step):
        first = jnp.where(passing & (step > 0), jnp.where(step == last_pass, 1, step + 1), step)
        return first, step + 1

    def advance(ph, k):
        for age in range(1, len(stages)):
            step = k - age

            @pl.when((step >= 0) & (step < n))
            def _():
                @pl.loop(*made_at(step))
                def _(made):
                    of_step(made, functools.partial(stages[age], ph))

    def advance_all(ph, age):
        @pl.loop(0, n)
        def _(j):
            stages[age](ph, j)

    def field_grad(ph, block):
        grad = taken[block, 1:rows + 1, :, :].reshape(cells, 3 * ch)
        value = dot(x_t[ph], grad)
        for a in range(3):
            for b in range(3):
                put_part(ph, block, 3 * a + b, value[a * ch:(a + 1) * ch, (2 - b) * ch:(3 - b) * ch])

    def make_grad(ph, block):
        field_grad(ph, block)
        sum_cores(ph, block)

    def inner_sums(first, last, side):
        start = side * (cells - wide)
        row_send[2, side] = acc[start:start + wide, :]
        at = slice(first, last)
        v = acc[at, :] * slope1[at, :]
        slope1[at, :] = v
        acc[at, :] = jnp.zeros((last - first, ch), F32)
        return fold(v * normed1[at, :]), fold(v)

    def early_inner():
        for i, v in enumerate(inner_sums(0, settled, 0)):
            early[8 * i:8 * i + 8, :] = v
        row_copy(2, 0).start()

    def backward(ph):
        last = ph == 0

        def consume(k, block, q):
            into = taken.at[block]
            unpack_half(2 + ph, block, q, into)
            if last and q == HALVES - 1:
                @pl.when((k == 0) | (k >= last_pass))
                def _():
                    make_grad(ph, block)
            add_conv(q, into, None, lambda t: wv[ph, block, t * ch:(t + 1) * ch, :])
            if q == 0 and not last:
                pl.when(k == last_step)(early_inner)

        def each(k):
            first, end = made_at(k)
            if last:
                @pl.loop(first, end - 1)
                def _(step):
                    of_step(step, functools.partial(make_grad, ph))
                advance(ph, k)
                for age in range(2, len(stages)):
                    @pl.when(k == age - 2)
                    def _():
                        advance_all(1, age)
            else:
                @pl.loop(first, jnp.where(passing | (k < n - 1), end, first))
                def _(step):
                    of_step(step, functools.partial(make_grad, ph))
        gather(2 + ph, consume, each)

    def fold(v):
        return jnp.sum(v.reshape(v.shape[0] // 8, 8, ch), axis=0)

    def flatten(v):
        return jnp.sum(v, axis=0, keepdims=True)

    zero = jnp.zeros((8, ch), F32)

    def part_moments(first, last):
        m = mask[first:last, :]
        v = acc[first:last, :]
        number, added = flatten(fold(m)), flatten(fold(v * m))
        c = (v - added / jnp.maximum(number, 1.0)) * m
        return added, number, flatten(fold(c * c))

    def early_moments(slot):
        for i, v in enumerate(part_moments(0, settled)):
            early[i:i + 1, :] = v
        send_row(slot, 0)

    def combine(added, number, spread):
        total_added, total_number = sum(added), sum(number)
        mean = total_added / jnp.maximum(total_number, 1.0)
        about = 0.0
        for a, k, q in zip(added, number, spread):
            off = a / jnp.maximum(k, 1.0) - mean
            about = about + (q + k * off * off)
        return total_added, total_number, about

    def local_moments():
        late = part_moments(settled, cells)
        return combine(*([early[i:i + 1, :], v] for i, v in enumerate(late)))

    def moments(slot):
        take_stats(slot)
        added, number, about = (st_recv[slot, :, i, :] for i in range(3))
        count = flatten(number)
        mean = flatten(added) / count
        off = added / jnp.maximum(number, 1.0) - mean
        return mean, lax.rsqrt(flatten(about + number * off * off) / count + EPSILON), count

    def everywhere(fn):
        chunked(fn, 0)
        fn(cells, 2 * wide, 0)

    gain1, shift1, gain2, shift2 = (r[...] for r in (gain1_in, shift1_in, gain2_in, shift2_in))

    weights_over_z(0)

    quarter = band // 2
    kept = packed // 2
    window = unpack.shape[3]
    below = lax.broadcasted_iota(jnp.int32, (quarter, quarter), 1) < lax.broadcasted_iota(jnp.int32, (quarter, quarter), 0)
    below = below.astype(F32).astype(BF16)

    def make_pack(h):
        for j in range(2):
            lv = mask[h * band + j * quarter:h * band + (j + 1) * quarter, :]
            place = jnp.where(lv > 0.0, dot(below, lv.astype(BF16)) + j * kept, -1.0)
            places[h, j] = place
            across = place.T[0:1, :]
            spot = lax.broadcasted_iota(jnp.int32, (packed, quarter), 0).astype(F32)
            pack[h, :, j * quarter:(j + 1) * quarter] = jnp.where(spot == across, 1.0, 0.0).astype(BF16)

    def make_unpack(h):
        for j in range(2):
            for start in range(0, window, ch):
                size = min(ch, window - start)
                spot = start + j * (packed - window) + lax.broadcasted_iota(jnp.int32, (quarter, size), 1)
                unpack[h, j, :, start:start + size] = jnp.where(
                    places[h, j, :, :size] == spot.astype(F32), 1.0, 0.0).astype(BF16)

    for side in range(2):
        edge_copy(1 - side).wait_recv()
        there = jnp.where(s > 0, 1.0, 0.0) if side == 0 else jnp.where(s < s_count - 1, 1.0, 0.0)
        at = slice(cells + side * wide, cells + (side + 1) * wide)
        masked[at, :] = edge_recv[side, 0].astype(F32) * there
        mask[at, :] = edge_recv[side, 1].astype(F32) * there

    def stats_sent(slot):
        for k in range(1, s_count):
            st_copy(slot, k, s).wait_send()

    def row_sent(slot):
        for side in range(2):
            row_copy(slot, side).wait_send()

    def gathered_sent(ph):
        @pl.loop(0, n)
        def _(k):
            for sign in (1, -1):
                block = z - k * sign

                @pl.when(inside(block) & inside(z + sign))
                def _():
                    for q in range(HALVES):
                        ag_copy(ph, block, q, sign).wait_send()

    def weights_sent(which):
        for k in range(1, n):
            wz_copy(which, k).wait_send()

        @pl.loop(1, w_parts)
        def _(k):
            for slot in range(n - 1):
                wp_copy(which, slot, k, w_mine).wait_send()

    def grads_sent(ph):
        @pl.loop(0, n)
        def _(j):
            c_copy(ph, j).wait_send()
            h_copy(ph, j, core).wait_send()
            o_copy(ph, j).wait()
            for e in range(1, chips):
                peer = (chip + e) % chips

                @pl.when(peer < owners)
                def _():
                    q_copy(ph, j, e, chip, peer).wait_send()

                @pl.when(chip < owners)
                def _():
                    f_copy(ph, j, e, chip).wait_send()

    block_copy = pltpu.make_async_copy(flat_block, out_block, r_sem.at[0])

    pack_field(0, masked, first=make_pack)
    for h in range(HALVES):
        make_unpack(h)
    forward(0, masked)
    send_stats(0, local_moments())
    send_row(0, 1)
    weights_round(1)
    mean1, scale1, count = moments(0)

    def activate_one(start, size, carry):
        at = pl.ds(start, size)
        main = start is not cells
        nv = ((acc if main else normed1)[at, :] - mean1) * scale1
        normed1[at, :] = nv
        hid[at, :] = gelu_parts(nv * gain1 + shift1)[0] * mask[at, :]
        if main:
            acc[at, :] = jnp.zeros((size, ch), F32)
        return carry

    def slope_one(start, size, carry):
        at = pl.ds(start, size)
        slope1[at, :] = gelu_parts(normed1[at, :] * gain1 + shift1)[1] * mask[at, :]
        return carry

    take_rows(0, normed1)
    pack_field(1, hid, activate_one)
    forward(1, hid)
    send_stats(1, local_moments())
    send_row(1, 1)
    turn_field(0, masked)
    turn_field(1, hid)
    weights_sent(0)
    gathered_sent(0)
    stats_sent(0)
    row_sent(0)
    for side in range(2):
        edge_copy(side).wait_send()
        cot_copy(side).wait_send()
    mean2, scale2, _ = moments(1)

    def activate_two(source, start, size):
        at = pl.ds(start, size)
        nv = (source[at, :] - mean2) * scale2
        normed2[at, :] = nv
        value, slope = gelu_parts(nv * gain2 + shift2 + masked[at, :])
        t = cotm[at, :] * slope
        through[at, :] = t
        return value, nv, t

    def activate_main(start, size, carry):
        value, nv, t = activate_two(acc, start, size)
        at = pl.ds(start, size)
        hid2[at, :] = value * mask[at, :]
        acc[at, :] = jnp.zeros((size, ch), F32)
        return carry[0] + fold(t * nv), carry[1] + fold(t)

    send_stats(2, [flatten(v) for v in chunked(activate_main, (zero, zero))])
    take_rows(1, normed2)
    take_cotangent()
    activate_two(normed2, cells, edge)
    to_flat(hid2, flat_block)
    block_copy.start()
    weights_sent(1)
    gathered_sent(1)

    def gradient_sums(slot):
        take_stats(slot)
        return flatten(st_recv[slot, :, 0, :]), flatten(st_recv[slot, :, 1, :])

    def norm_back(upstream, normed, gain, scale, sums):
        gain_grad, shift_grad = sums
        factor = gain * scale
        level, tilt = shift_grad / count, gain_grad / count

        def fill(start, size, carry):
            at = pl.ds(start, size)
            v = upstream[at, :] - mask[at, :] * (level + normed[at, :] * tilt)
            hid[at, :] = factor * v
            return carry
        return fill

    sums2 = gradient_sums(2)
    pack_field(3, hid, norm_back(through, normed2, gain2, scale2, sums2))
    backward(1)

    parts = inner_sums(settled, cells, 1)
    send_stats(3, [flatten(early[8 * i:8 * i + 8, :] + v) for i, v in enumerate(parts)])
    row_copy(2, 1).start()

    @pl.when(jnp.logical_not(passing))
    def _():
        of_step(n - 1, functools.partial(make_grad, 1))
    for side in range(2):
        row_copy(2, 1 - side).wait_recv()
        at = slice(cells + side * wide, cells + (side + 1) * wide)
        slope1[at, :] = row_recv[2, side] * slope1[at, :]
    stats_sent(1)
    row_sent(1)
    stats_sent(2)
    gathered_sent(3)
    sums1 = gradient_sums(3)
    pack_field(2, hid, norm_back(slope1, normed1, gain1, scale1, sums1))
    advance_all(1, 1)
    backward(0)
    advance(0, n)

    def finish_input(start, size, carry):
        at = pl.ds(start, size)
        acc[at, :] = (acc[at, :] + through[at, :]) * mask[at, :]
        return carry

    chunked(finish_input, 0)
    to_flat(acc, flat_input)
    input_copy = pltpu.make_async_copy(flat_input, out_input, r_sem.at[1])
    input_copy.start()
    out_gain1[...], out_shift1[...] = sums1
    out_gain2[...], out_shift2[...] = sums2
    for extra in range(1, len(stages) - 1):
        advance(0, n + extra)

    stats_sent(3)
    row_sent(2)
    gathered_sent(2)
    grads_sent(1)
    grads_sent(0)
    block_copy.wait()
    input_copy.wait()


def finish_kernel(count, *refs):
    ins, outs = refs[:count], refs[count:2 * count]
    narrow, wide, in_sem, out_sem, take_sem, give_sem = refs[2 * count:2 * count + 6]
    held = refs[2 * count + 6:]
    rows = narrow.shape[1] // FINISH_PARTS
    parts = [(w, i, pl.ds(i * rows, rows)) for i in range(FINISH_PARTS) for w in range(2)]
    loads = [pltpu.make_async_copy(ins[w].at[at, :], narrow.at[w, at, :], in_sem.at[w, i]) for w, i, at in parts]
    stores = [pltpu.make_async_copy(wide.at[w, at, :], outs[w].at[at, :], out_sem.at[w, i]) for w, i, at in parts]
    takes = [pltpu.make_async_copy(ins[2 + k], v, take_sem.at[k]) for k, v in enumerate(held)]
    gives = [pltpu.make_async_copy(v, outs[2 + k], give_sem.at[k]) for k, v in enumerate(held)]
    for copy in loads + takes:
        copy.start()
    for load, store, (w, i, at) in zip(loads, stores, parts):
        load.wait()
        wide[w, at, :] = narrow[w, at, :].astype(F32)
        store.start()
    for take, give in zip(takes, gives):
        take.wait()
        give.start()
    for copy in stores + gives:
        copy.wait()


def per_device(n, s_count, blocks, weight_one, weight_two, gain_one, shift_one, gain_two, shift_two, cell_live, cotangent):
    rows, wide = cell_live.shape
    ch = blocks.shape[1] // wide
    cells = rows * wide
    total = cells + 2 * wide
    packed = 2 * -(-most_live(rows // HALVES // 2, wide) // 8) * 8
    aligned = ch % 128 == 0
    chips = s_count // 2
    tap_rows = 9 * ch
    half_rows = tap_rows // 2
    owners = math.gcd(half_rows // 16, chips)
    piece = half_rows // owners

    if aligned:
        weight_one, weight_two = (w.reshape(tap_rows, n * ch) for w in (weight_one, weight_two))
    else:
        weight_one, weight_two = (
            w.reshape(tap_rows, n, ch).transpose(1, 0, 2) for w in (weight_one, weight_two))
    grad_shape = (2, owners, piece, n * ch) if aligned else (n, 2, owners, piece, ch)
    vmem = pl.BlockSpec(memory_space=pltpu.VMEM)
    hbm = pl.BlockSpec(memory_space=pl.ANY)
    sem = pltpu.SemaphoreType.DMA
    field = pltpu.VMEM((total, ch), F32)
    scratch = [
        pltpu.VMEM((ch * wide, 128), F32),
        pltpu.VMEM((2, n, tap_rows, ch), BF16),
        pltpu.VMEM((2, n - 1, tap_rows, ch), BF16),
        pltpu.VMEM((2, 3 * ch, cells), BF16),
        pltpu.VMEM((HALVES, packed, cells // HALVES), BF16),
        pltpu.VMEM((HALVES, 2, cells // HALVES // 2, -(-packed // 2 // 16) * 16), BF16),
        pltpu.VMEM((HALVES, 2, cells // HALVES // 2, ch), F32),
        pltpu.VMEM((2, 2, wide, ch), BF16),
        pltpu.VMEM((2, 2, wide, ch), BF16),
        pltpu.VMEM((2, wide, ch), BF16),
        pltpu.VMEM((2, wide, ch), BF16),
        field, field, field, field, field, field, field, field, field,
        pltpu.VMEM((total + 16, ch), F32),
        pltpu.VMEM((cells, ch), F32),
        pltpu.VMEM((4, n, 2 * wide + HALVES * packed, ch), BF16),
        pltpu.VMEM((n, rows + 3, wide, 3 * ch), BF16),
        pltpu.VMEM((2, n, 2, owners, piece, ch), F32),
        pltpu.VMEM((2, n, owners, piece, ch), BF16),
        pltpu.VMEM((2, n, owners, piece, ch), BF16),
        pltpu.VMEM((2, n, owners, piece, ch), BF16),
        pltpu.VMEM((2, n, chips, piece, ch), BF16),
        pltpu.VMEM((2, n, 2, owners, piece, ch), BF16),
        pltpu.VMEM((4, 8, ch), F32),
        pltpu.VMEM((4, s_count, 8, ch), F32),
        pltpu.VMEM((3, 2, wide, ch), F32),
        pltpu.VMEM((3, 2, wide, ch), F32),
        pltpu.VMEM((16, ch), F32),
        pltpu.VMEM((rows, ch * wide), BF16),
        pltpu.VMEM((rows, ch * wide), F32),
        sem((2, n)),
        sem((2, n)), sem((2, n)),
        sem((2, n - 1, s_count)), sem((2, n - 1, s_count)),
        sem((2,)), sem((2,)),
        sem((2,)), sem((2,)),
        sem((4, 2, n, HALVES)), sem((4, n, HALVES)),
        sem((4, s_count)), sem((4, s_count)),
        sem((3, 2)), sem((3, 2)),
        sem((2, n)), sem((2, n)),
        sem((2, n, chips)), sem((2, n, chips)),
        sem((2, n, chips)), sem((2, n, chips)),
        sem((2, n)), sem((2, n)),
        sem((2, n)),
        sem((2,)),
    ]
    block_out, input_grad, wg1, wg2, *sums = pl.pallas_call(
        functools.partial(block_kernel, n, s_count, rows, wide, ch, aligned, packed),
        out_shape=(
            jax.ShapeDtypeStruct((rows, ch * wide), BF16),
            jax.ShapeDtypeStruct((rows, ch * wide), F32),
            jax.ShapeDtypeStruct(grad_shape, BF16),
            jax.ShapeDtypeStruct(grad_shape, BF16),
            *[jax.ShapeDtypeStruct((1, ch), F32)] * 4,
        ),
        in_specs=[vmem] * 7 + [hbm] * 2,
        out_specs=(hbm, hbm, hbm, hbm, vmem, vmem, vmem, vmem),
        scratch_shapes=scratch,
        compiler_params=pltpu.CompilerParams(
            collective_id=0, has_side_effects=True, vmem_limit_bytes=60 * 1024 * 1024),
    )(blocks, cotangent, cell_live.T,
      *(v.reshape(1, ch) for v in (gain_one, shift_one, gain_two, shift_two)), weight_one, weight_two)

    if not aligned:
        def whole(grad):
            grad = grad.reshape(n, tap_rows, ch).transpose(1, 0, 2)
            return grad.astype(F32).reshape(9, ch, n * ch)
        return (block_out, input_grad, whole(wg1), whole(wg2), *(v.reshape(ch) for v in sums))

    wg1, wg2 = (w.reshape(tap_rows, n * ch) for w in (wg1, wg2))
    wide_grad = jax.ShapeDtypeStruct((tap_rows, n * ch), F32)
    moved = (block_out, input_grad, *sums)
    grad1, grad2, *moved = pl.pallas_call(
        functools.partial(finish_kernel, 2 + len(moved)),
        out_shape=(wide_grad, wide_grad, *(jax.ShapeDtypeStruct(v.shape, v.dtype) for v in moved)),
        in_specs=[pl.BlockSpec(memory_space=pl.ANY)] * (2 + len(moved)),
        out_specs=[pl.BlockSpec(memory_space=pl.ANY)] * (2 + len(moved)),
        scratch_shapes=[
            pltpu.VMEM((2, tap_rows, n * ch), BF16), pltpu.VMEM((2, tap_rows, n * ch), F32),
            sem((2, FINISH_PARTS)), sem((2, FINISH_PARTS)), sem((len(moved),)), sem((len(moved),)),
            *(pltpu.VMEM(v.shape, v.dtype) for v in moved),
        ],
        compiler_params=pltpu.CompilerParams(vmem_limit_bytes=64 * 1024 * 1024),
    )(wg1, wg2, *moved)
    block_out, input_grad, *sums = moved
    grads = (g.reshape(9, ch, n * ch) for g in (grad1, grad2))
    return (block_out, input_grad, *grads, *(v.reshape(ch) for v in sums))


def solution(mesh):
    return jax.shard_map(
        functools.partial(per_device, mesh.shape["chan"], mesh.shape["space"]),
        mesh=mesh,
        in_specs=(
            P("space", "chan"),
            P(None, "chan", None),
            P(None, "chan", None),
            P("chan"),
            P("chan"),
            P("chan"),
            P("chan"),
            P("space", None),
            P("space", "chan"),
        ),
        out_specs=(
            P("space", "chan"),
            P("space", "chan"),
            P(None, "chan", None),
            P(None, "chan", None),
            P("chan"),
            P("chan"),
            P("chan"),
            P("chan"),
        ),
        check_vma=False,
    )
```

```python
import functools
import math

import jax
import jax.numpy as jnp
from jax import lax
from jax.experimental import pallas as pl
from jax.experimental.pallas import tpu as pltpu
from jax.sharding import PartitionSpec as P

EPSILON = 1e-05
MESH = pl.DeviceIdType.MESH
F32 = jnp.float32
BF16 = jnp.bfloat16
ROOT_HALF = 0.7071067811865476
ROOT_TWO_PI = 0.3989422804014327
CHUNK = 64
FINISH_PARTS = 4
UNROLL = 2
HALVES = 2
LARGE, SMALL = 7, 3


def dot(a, b):
    return jnp.dot(a, b, preferred_element_type=F32)


def gelu_parts(v):
    upper = 0.5 * (1.0 + lax.erf(v * ROOT_HALF))
    slope = upper + v * (ROOT_TWO_PI * jnp.exp(-0.5 * v * v))
    return v * upper, slope


def most_live(rows, wide):
    units = (wide + 1) // (SMALL + 1)
    live_rows = rows - rows // (LARGE + 1)
    return min(rows * wide, math.ceil(units * live_rows * LARGE / 2))


def block_kernel(n, s_count, rows, wide, ch, aligned, packed, *refs):
    (x_in, cot_in, live_in, gain1_in, shift1_in, gain2_in, shift2_in, w1_hbm, w2_hbm) = refs[:9]
    (out_block, out_input, out_wg1, out_wg2, out_gain1, out_shift1, out_gain2, out_shift2) = refs[9:17]
    (turned, wv, wf, x_t, pack, unpack, places, edge_send, edge_recv, cot_send, cot_recv, cotm, mask, masked,
     normed1, normed2, through, slope1, hid, hid2, pad, acc, hold, taken,
     part, psend, crecv, hsend, qrecv, wout, st_send, st_recv, row_send, row_recv, early, flat_block, flat_input,
     w_sem, wz_ssem, wz_rsem, wp_ssem, wp_rsem, e_ssem, e_rsem, ce_ssem, ce_rsem, ag_ssem, ag_rsem,
     st_ssem, st_rsem, row_ssem, row_rsem, c_ssem, c_rsem, q_ssem, q_rsem,
     f_ssem, f_rsem, h_ssem, h_rsem, o_sem, r_sem) = refs[17:]

    z = lax.axis_index("chan")
    s = lax.axis_index("space")
    cells = rows * wide
    total = cells + 2 * wide
    band = cells // HALVES
    core, chip, chips = s % 2, s // 2, s_count // 2
    before, after = (s + s_count - 1) % s_count, (s + 1) % s_count
    tap_rows = 9 * ch

    barrier = pltpu.get_barrier_semaphore()

    @pl.loop(1, s_count)
    def _(k):
        pl.semaphore_signal(barrier, inc=1, device_id=(z, (s + k) % s_count), device_id_type=MESH)

    @pl.loop(1, n)
    def _(k):
        pl.semaphore_signal(barrier, inc=1, device_id=((z + k) % n, s), device_id_type=MESH)

    w_copies = []
    for which, source in enumerate((w1_hbm, w2_hbm)):
        for d in range(n):
            block = source.at[:, d * ch:(d + 1) * ch] if aligned else source.at[d]
            w_copies.append(pltpu.make_async_copy(block, wv.at[which, d], w_sem.at[which, d]))
    for copy in w_copies:
        copy.start()

    def chunked(fn, init, first=0, count=cells):
        def step(i, carry):
            return fn(pl.multiple_of(first + i * CHUNK, CHUNK), CHUNK, carry)
        return lax.fori_loop(0, count // CHUNK, step, init, unroll=UNROLL)

    lanes = 128
    tiles = ch * wide // lanes

    def from_flat(flat, put):
        for i in range(tiles):
            turned[i * lanes:(i + 1) * lanes, 0:rows] = flat[:, i * lanes:(i + 1) * lanes].astype(F32).T
        for w in range(wide):
            put(pl.ds(w, rows, stride=wide), turned[pl.ds(w, ch, stride=wide), 0:rows].T)

    def to_flat(source, flat):
        for w in range(wide):
            turned[pl.ds(w, ch, stride=wide), 0:rows] = source[pl.ds(w, rows, stride=wide), :].T
        for i in range(tiles):
            flat[:, i * lanes:(i + 1) * lanes] = turned[i * lanes:(i + 1) * lanes, 0:rows].T.astype(flat.dtype)

    def put_masked(at, value):
        masked[at, :] = value

    from_flat(x_in, put_masked)

    cell = lax.broadcasted_iota(jnp.int32, (cells, rows), 0)
    pick = (cell // wide == lax.broadcasted_iota(jnp.int32, (cells, rows), 1)).astype(F32).astype(BF16)
    column_of = lax.broadcasted_iota(jnp.int32, (cells, wide), 0) % wide
    picked = lax.dot_general(pick, live_in[...].astype(BF16), (((1,), (1,)), ((), ())), preferred_element_type=F32)
    picked = jnp.where(column_of == lax.broadcasted_iota(jnp.int32, (cells, wide), 1), picked, 0.0)
    mask[0:cells, :] = dot(picked.astype(BF16), jnp.ones((wide, ch), BF16))

    def load_main(start, size, carry):
        at = pl.ds(start, size)
        lv = mask[at, :]
        masked[at, :] = masked[at, :] * lv
        return carry

    chunked(load_main, 0)
    for side, start in ((0, 0), (1, cells - wide)):
        edge_send[side, 0] = masked[start:start + wide, :].astype(BF16)
        edge_send[side, 1] = mask[start:start + wide, :].astype(BF16)

    acc[...] = jnp.zeros_like(acc)
    for block in range(n):
        for row in (rows // HALVES + 1, rows + 2):
            taken[block, row:row + 1, :, :] = jnp.zeros((1, wide, 3 * ch), BF16)
    st_send[...] = jnp.zeros_like(st_send)

    pl.semaphore_wait(barrier, s_count - 1 + n - 1)

    def edge_copy(side):
        return pltpu.make_async_remote_copy(
            src_ref=edge_send.at[side], dst_ref=edge_recv.at[1 - side],
            send_sem=e_ssem.at[side], recv_sem=e_rsem.at[1 - side],
            device_id=(z, before if side == 0 else after), device_id_type=MESH)

    for side in range(2):
        edge_copy(side).start()

    def cot_copy(side):
        return pltpu.make_async_remote_copy(
            src_ref=cot_send.at[side], dst_ref=cot_recv.at[1 - side],
            send_sem=ce_ssem.at[side], recv_sem=ce_rsem.at[1 - side],
            device_id=(z, before if side == 0 else after), device_id_type=MESH)

    def load_cotangent():
        def put(at, value):
            cotm[at, :] = value
        from_flat(cot_in, put)

        def live_only(start, size, carry):
            at = pl.ds(start, size)
            cotm[at, :] = cotm[at, :] * mask[at, :]
            return carry
        chunked(live_only, 0)
        for side, start in ((0, 0), (1, cells - wide)):
            cot_send[side] = cotm[start:start + wide, :].astype(BF16)
            cot_copy(side).start()

    def take_cotangent():
        for side in range(2):
            cot_copy(1 - side).wait_recv()
            at = slice(cells + side * wide, cells + (side + 1) * wide)
            cotm[at, :] = cot_recv[side].astype(F32) * mask[at, :]

    w_parts = math.gcd(tap_rows // 16, s_count)
    w_rows = tap_rows // w_parts
    w_mine = s % w_parts
    w_group = s - w_mine

    def wz_copy(which, k):
        at = pl.ds(w_mine * w_rows, w_rows)
        slot = n - k - 1
        return pltpu.make_async_remote_copy(
            src_ref=wv.at[which, (z + k) % n, at, :], dst_ref=wf.at[which, slot, at, :],
            send_sem=wz_ssem.at[which, slot], recv_sem=wz_rsem.at[which, slot],
            device_id=((z + k) % n, s), device_id_type=MESH)

    def wp_copy(which, slot, k, whose):
        at = pl.ds(whose * w_rows, w_rows)
        return pltpu.make_async_remote_copy(
            src_ref=wf.at[which, slot, at, :], dst_ref=wf.at[which, slot, at, :],
            send_sem=wp_ssem.at[which, slot, k], recv_sem=wp_rsem.at[which, slot, whose],
            device_id=(z, w_group + (w_mine + k) % w_parts), device_id_type=MESH)

    def weights_over_z(which):
        for copy in w_copies[which * n:(which + 1) * n]:
            copy.wait()

        @pl.loop(1, n)
        def _(k):
            wz_copy(which, k).start()

    def slot_of(block):
        return (block - z + n - 1) % n

    def weights_round(which):
        @pl.loop(1, n)
        def _(distance):
            for sign in (1, -1):
                block = z - distance * sign

                @pl.when((block >= 0) & (block < n))
                def _():
                    slot = slot_of(block)
                    wz_copy(which, n - 1 - slot).wait_recv()

                    @pl.loop(1, w_parts)
                    def _(k):
                        wp_copy(which, slot, k, w_mine).start()

    def weights_arrived(which, slot):
        @pl.loop(1, w_parts)
        def _(k):
            wp_copy(which, slot, k, (w_mine + k) % w_parts).wait_recv()

    def row_copy(slot, side):
        return pltpu.make_async_remote_copy(
            src_ref=row_send.at[slot, side], dst_ref=row_recv.at[slot, 1 - side],
            send_sem=row_ssem.at[slot, side], recv_sem=row_rsem.at[slot, 1 - side],
            device_id=(z, before if side == 0 else after), device_id_type=MESH)

    def send_row(slot, side):
        start = side * (cells - wide)
        row_send[slot, side] = acc[start:start + wide, :]
        row_copy(slot, side).start()

    settled = (rows // HALVES - 1) * wide

    def take_rows(slot, ref):
        for side in range(2):
            row_copy(slot, 1 - side).wait_recv()
            ref[cells + side * wide:cells + (side + 1) * wide, :] = row_recv[slot, side]

    def st_copy(slot, k, whose):
        return pltpu.make_async_remote_copy(
            src_ref=st_send.at[slot], dst_ref=st_recv.at[slot, whose],
            send_sem=st_ssem.at[slot, k], recv_sem=st_rsem.at[slot, whose],
            device_id=(z, (s + k) % s_count), device_id_type=MESH)

    def send_stats(slot, values):
        for i, v in enumerate(values):
            st_send[slot, i:i + 1, :] = v
        for k in range(1, s_count):
            st_copy(slot, k, s).start()
        st_recv[slot, s] = st_send[slot]

    def take_stats(slot):
        for k in range(1, s_count):
            st_copy(slot, k, (s + k) % s_count).wait_recv()

    strip = 8
    column = lax.broadcasted_iota(jnp.int32, (strip * wide, ch), 0) % wide

    def shift(target, first, count):
        size = count * wide
        where = column[:size]
        here = pad[pl.ds(8 + first * wide, size), :]
        left = jnp.where(where == 0, 0.0, pad[pl.ds(7 + first * wide, size), :])
        right = jnp.where(where == wide - 1, 0.0, pad[pl.ds(9 + first * wide, size), :])
        for b, v in enumerate((left, here, right)):
            target[pl.ds(first, count), :, b * ch:(b + 1) * ch] = v.astype(BF16).reshape(count, wide, ch)

    edge = 2 * wide
    ag_rows = ((0, edge + packed), (edge + packed, packed))
    band_rows = rows // HALVES

    def unpack_half(ph, block, q, target):
        if q == 0:
            pad[8:8 + wide, :] = hold[ph, block, 0:wide, :].astype(F32)
            pad[8 + wide + cells:8 + 2 * wide + cells, :] = hold[ph, block, wide:edge, :].astype(F32)
            shift(target, 0, 1)
            shift(target, rows + 1, 1)
        for j in range(2):
            start = edge + q * packed + j * (packed - unpack.shape[3])
            at = 8 + wide + q * band + j * (band // 2)
            pad[at:at + band // 2, :] = dot(unpack[q, j], hold[ph, block, start:start + unpack.shape[3], :])

        for i in range(band_rows // strip):
            shift(target, 1 + q * band_rows + i * strip, strip)

    def add_conv(q, field, taps, turned_taps=None):
        first, last = (0, band_rows - 1) if q == 0 else (band_rows - 1, rows)
        count = last - first
        size = (count + 2) * wide
        lhs = jnp.concatenate([
            field[first + i:last + 2 + i, :, :].reshape(size, 3 * ch) for i in range(2)], axis=1)
        if turned_taps is None:
            none = jnp.zeros((3 * ch, ch), BF16)
            rhs = jnp.concatenate([
                jnp.concatenate([taps(0), taps(2)], axis=1), jnp.concatenate([taps(1), none], axis=1)], axis=0)
            value = dot(lhs, rhs)
        else:
            def row_taps(a):
                return [turned_taps(3 * (2 - a) + 2 - b) for b in range(3)]
            none = jnp.zeros((ch, 3 * ch), BF16)
            rhs = jnp.concatenate([
                jnp.concatenate(row_taps(0) + row_taps(1), axis=1), jnp.concatenate(row_taps(2) + [none], axis=1)], axis=0)
            value = lax.dot_general(lhs, rhs, (((1,), (1,)), ((), ())), preferred_element_type=F32)
        at = pl.ds(first * wide, count * wide)
        acc[at, :] = acc[at, :] + value[0:count * wide, 0:ch] + value[2 * wide:size, ch:2 * ch]

    def ag_copy(ph, block, q, sign):
        at = pl.ds(*ag_rows[q])
        return pltpu.make_async_remote_copy(
            src_ref=hold.at[ph, block, at, :], dst_ref=hold.at[ph, block, at, :],
            send_sem=ag_ssem.at[ph, (1 - sign) // 2, block, q], recv_sem=ag_rsem.at[ph, block, q],
            device_id=(z + sign, s), device_id_type=MESH)

    def pack_field(ph, source, fill=None, first=None):
        if fill is not None:
            fill(cells, edge, 0)
        hold[ph, z, 0:edge, :] = source[cells:cells + edge, :].astype(BF16)
        for q in range(HALVES):
            if first is not None:
                first(q)
            if fill is not None:
                chunked(fill, 0, q * band, band)
            hold[ph, z, edge + q * packed:edge + (q + 1) * packed, :] = dot(
                pack[q], source[q * band:(q + 1) * band, :].astype(BF16)).astype(BF16)
            for sign in (1, -1):
                @pl.when((z + sign >= 0) & (z + sign < n))
                def _():
                    ag_copy(ph, z, q, sign).start()

    def inside(slice_at):
        return (slice_at >= 0) & (slice_at < n)

    def take_and_pass(ph, k, q, sign, passes=True, takes=True):
        block = z - k * sign

        @pl.when((k > 0) & inside(block))
        def _():
            if passes and takes:
                ag_copy(ph, block, q, sign).wait_recv()

            @pl.when(inside(z + sign))
            def _():
                if passes:
                    if not takes:
                        ag_copy(ph, block, q, sign).wait_recv()
                    ag_copy(ph, block, q, sign).start()

            if not passes:
                @pl.when(jnp.logical_not(inside(z + sign)))
                def _():
                    ag_copy(ph, block, q, sign).wait_recv()

    near = jnp.where(z < n - n // 2, 1, 0)

    def consume_way(k, q, way, consume):
        block = z - k * (1 - 2 * way)

        @pl.when((k >= 0) & (k < n) & inside(block) & ((k > 0) | (way == near)))
        def _():
            consume(k, block, q)

    def take_both(ph, k, q, **how):
        @pl.loop(0, 2)
        def _(i):
            way = (near + i) % 2
            take_and_pass(ph, k, q, 1 - 2 * way, **how)

    def gather(ph, consume, each):
        @pl.loop(0, n)
        def _(k):
            for q in range(HALVES):
                take_both(ph, k, q)
                if q:
                    consume_way(k, q - 1, 1 - near, consume)
                else:
                    consume_way(k - 1, HALVES - 1, 1 - near, consume)
                consume_way(k, q, near, consume)
            each(k)

    last_step = jnp.maximum(z, n - 1 - z)

    last_pass = jnp.maximum(jnp.where(z < n - 1, z, 0), jnp.where(z > 0, n - 1 - z, 0))

    def forward(ph, field):
        def consume(k, block, q):
            into = taken.at[block]
            unpack_half(ph, block, q, into)

            @pl.when(k == 0)
            def _():
                add_conv(q, into, lambda a: wv[ph, z, 3 * a * ch:3 * (a + 1) * ch, :])

            @pl.when(k > 0)
            def _():
                slot = slot_of(block)
                if q == 0:
                    weights_arrived(ph, slot)
                add_conv(q, into, lambda a: wf[ph, slot, 3 * a * ch:3 * (a + 1) * ch, :])

            if q == 0:
                pl.when(k == last_step)(lambda: early_moments(ph))

        def each(k):
            if ph == 0:
                @pl.when(k == 0)
                def _():
                    weights_round(0)

                @pl.when(k == 1)
                def _():
                    weights_over_z(1)

                @pl.when(k == last_pass)
                def _():
                    load_cotangent()
        gather(ph, consume, each)

    def turn_field(ph, field):
        main = [field[start:start + ch, :].T for start in range(0, cells, ch)]
        ends = field[cells:cells + edge, :]
        if edge < ch:
            ends = jnp.concatenate([ends, jnp.zeros((ch - edge, ch), F32)], axis=0)
        ends = ends.T
        for i, here in enumerate(main):
            left = jnp.concatenate(
                [ends[:, 0:wide] if i == 0 else main[i - 1][:, ch - wide:], here[:, 0:ch - wide]], axis=1)
            right = jnp.concatenate(
                [here[:, wide:], main[i + 1][:, 0:wide] if i + 1 < len(main) else ends[:, wide:edge]], axis=1)
            for a, v in enumerate((left, here, right)):
                x_t[ph, a * ch:(a + 1) * ch, i * ch:(i + 1) * ch] = v.astype(BF16)

    half_rows = tap_rows // 2
    owners = math.gcd(half_rows // 16, chips)
    piece = half_rows // owners

    def c_copy(ph, j):
        return pltpu.make_async_remote_copy(
            src_ref=psend.at[ph, j], dst_ref=crecv.at[ph, j],
            send_sem=c_ssem.at[ph, j], recv_sem=c_rsem.at[ph, j],
            device_id=(z, chip * 2 + 1 - core), device_id_type=MESH)

    def q_copy(ph, j, e, whose, owner):
        return pltpu.make_async_remote_copy(
            src_ref=hsend.at[ph, j, owner], dst_ref=qrecv.at[ph, j, whose],
            send_sem=q_ssem.at[ph, j, e], recv_sem=q_rsem.at[ph, j, whose],
            device_id=(z, ((chip + e) % chips) * 2 + core), device_id_type=MESH)

    def f_copy(ph, j, e, owner):
        return pltpu.make_async_remote_copy(
            src_ref=wout.at[ph, j, core, owner], dst_ref=wout.at[ph, j, core, owner],
            send_sem=f_ssem.at[ph, j, e], recv_sem=f_rsem.at[ph, j, owner],
            device_id=(z, ((chip + e) % chips) * 2 + core), device_id_type=MESH)

    def h_copy(ph, j, whose):
        return pltpu.make_async_remote_copy(
            src_ref=wout.at[ph, j, whose], dst_ref=wout.at[ph, j, whose],
            send_sem=h_ssem.at[ph, j], recv_sem=h_rsem.at[ph, j],
            device_id=(z, chip * 2 + 1 - core), device_id_type=MESH)

    def o_copy(ph, j):
        target = (out_wg1, out_wg2)[ph]
        if aligned:
            target = target.at[:, :, :, pl.ds(pl.multiple_of(j * ch, ch), ch)]
        else:
            target = target.at[j]
        return pltpu.make_async_copy(wout.at[ph, j], target, o_sem.at[ph, j])

    def sum_cores(ph, j):
        for o in range(owners):
            psend[ph, j, o] = part[ph, j, 1 - core, o].astype(BF16)
        c_copy(ph, j).start()

    def sum_chips(ph, j):
        c_copy(ph, j).wait_recv()
        for o in range(owners):
            v = part[ph, j, core, o] + crecv[ph, j, o].astype(F32)
            part[ph, j, core, o] = v
            hsend[ph, j, o] = v.astype(BF16)

        @pl.loop(1, chips)
        def _(e):
            peer = (chip + e) % chips

            @pl.when(peer < owners)
            def _():
                q_copy(ph, j, e, chip, peer).start()

    def spread_chips(ph, j):
        @pl.when(chip < owners)
        def _():
            @pl.loop(1, chips)
            def _(e):
                q_copy(ph, j, e, (chip + e) % chips, chip).wait_recv()
            v = part[ph, j, core, chip]
            for e in range(1, chips):
                v = v + qrecv[ph, j, (chip + e) % chips].astype(F32)
            wout[ph, j, core, chip] = v.astype(BF16)

            @pl.loop(1, chips)
            def _(e):
                f_copy(ph, j, e, chip).start()

    def spread_cores(ph, j):
        @pl.loop(1, chips)
        def _(e):
            peer = (chip + e) % chips

            @pl.when(peer < owners)
            def _():
                f_copy(ph, j, e, peer).wait_recv()
        h_copy(ph, j, core).start()

    def finish(ph, j):
        h_copy(ph, j, 1 - core).wait_recv()
        o_copy(ph, j).start()

    def put_part(ph, j, tap, value):
        start = tap * ch
        done = 0
        while done < ch:
            row = start + done
            side, o, at = row // half_rows, row % half_rows // piece, row % piece
            size = min(ch - done, piece - at)
            part[ph, j, side, o, at:at + size, :] = value[done:done + size, :]
            done += size

    stages = (sum_cores, sum_chips, spread_chips, spread_cores, finish)

    def of_step(k, fn):
        @pl.loop(0, 2)
        def _(way):
            block = z - k * (1 - 2 * way)

            @pl.when((k >= 0) & (k < n) & inside(block) & ((k > 0) | (way == 0)))
            def _():
                fn(block)

    passing = last_pass > 0

    def made_at(step):
        first = jnp.where(passing & (step > 0), jnp.where(step == last_pass, 1, step + 1), step)
        return first, step + 1

    def advance(ph, k):
        for age in range(1, len(stages)):
            step = k - age

            @pl.when((step >= 0) & (step < n))
            def _():
                @pl.loop(*made_at(step))
                def _(made):
                    of_step(made, functools.partial(stages[age], ph))

    def advance_all(ph, age):
        @pl.loop(0, n)
        def _(j):
            stages[age](ph, j)

    def field_grad(ph, block):
        grad = taken[block, 1:rows + 1, :, :].reshape(cells, 3 * ch)
        value = dot(x_t[ph], grad)
        for a in range(3):
            for b in range(3):
                put_part(ph, block, 3 * a + b, value[a * ch:(a + 1) * ch, (2 - b) * ch:(3 - b) * ch])

    def make_grad(ph, block):
        field_grad(ph, block)
        sum_cores(ph, block)

    def inner_sums(first, last, side):
        start = side * (cells - wide)
        row_send[2, side] = acc[start:start + wide, :]
        at = slice(first, last)
        v = acc[at, :] * slope1[at, :]
        slope1[at, :] = v
        acc[at, :] = jnp.zeros((last - first, ch), F32)
        return fold(v * normed1[at, :]), fold(v)

    def early_inner():
        for i, v in enumerate(inner_sums(0, settled, 0)):
            early[8 * i:8 * i + 8, :] = v
        row_copy(2, 0).start()

    def backward(ph):
        last = ph == 0

        def consume(k, block, q):
            into = taken.at[block]
            unpack_half(2 + ph, block, q, into)
            if last and q == HALVES - 1:
                @pl.when((k == 0) | (k >= last_pass))
                def _():
                    make_grad(ph, block)
            add_conv(q, into, None, lambda t: wv[ph, block, t * ch:(t + 1) * ch, :])
            if q == 0 and not last:
                pl.when(k == last_step)(early_inner)

        def each(k):
            first, end = made_at(k)
            if last:
                @pl.loop(first, end - 1)
                def _(step):
                    of_step(step, functools.partial(make_grad, ph))
                advance(ph, k)
                for age in range(2, len(stages)):
                    @pl.when(k == age - 2)
                    def _():
                        advance_all(1, age)
            else:
                @pl.loop(first, jnp.where(passing | (k < n - 1), end, first))
                def _(step):
                    of_step(step, functools.partial(make_grad, ph))
        gather(2 + ph, consume, each)

    def fold(v):
        return jnp.sum(v.reshape(v.shape[0] // 8, 8, ch), axis=0)

    def flatten(v):
        return jnp.sum(v, axis=0, keepdims=True)

    zero = jnp.zeros((8, ch), F32)

    def part_moments(first, last):
        m = mask[first:last, :]
        v = acc[first:last, :]
        number, added = flatten(fold(m)), flatten(fold(v * m))
        c = (v - added / jnp.maximum(number, 1.0)) * m
        return added, number, flatten(fold(c * c))

    def early_moments(slot):
        for i, v in enumerate(part_moments(0, settled)):
            early[i:i + 1, :] = v
        send_row(slot, 0)

    def combine(added, number, spread):
        total_added, total_number = sum(added), sum(number)
        mean = total_added / jnp.maximum(total_number, 1.0)
        about = 0.0
        for a, k, q in zip(added, number, spread):
            off = a / jnp.maximum(k, 1.0) - mean
            about = about + (q + k * off * off)
        return total_added, total_number, about

    def local_moments():
        late = part_moments(settled, cells)
        return combine(*([early[i:i + 1, :], v] for i, v in enumerate(late)))

    def moments(slot):
        take_stats(slot)
        added, number, about = (st_recv[slot, :, i, :] for i in range(3))
        count = flatten(number)
        mean = flatten(added) / count
        off = added / jnp.maximum(number, 1.0) - mean
        return mean, lax.rsqrt(flatten(about + number * off * off) / count + EPSILON), count

    def everywhere(fn):
        chunked(fn, 0)
        fn(cells, 2 * wide, 0)

    gain1, shift1, gain2, shift2 = (r[...] for r in (gain1_in, shift1_in, gain2_in, shift2_in))

    weights_over_z(0)

    quarter = band // 2
    kept = packed // 2
    window = unpack.shape[3]
    below = lax.broadcasted_iota(jnp.int32, (quarter, quarter), 1) < lax.broadcasted_iota(jnp.int32, (quarter, quarter), 0)
    below = below.astype(F32).astype(BF16)

    def make_pack(h):
        for j in range(2):
            lv = mask[h * band + j * quarter:h * band + (j + 1) * quarter, :]
            place = jnp.where(lv > 0.0, dot(below, lv.astype(BF16)) + j * kept, -1.0)
            places[h, j] = place
            across = place.T[0:1, :]
            spot = lax.broadcasted_iota(jnp.int32, (packed, quarter), 0).astype(F32)
            pack[h, :, j * quarter:(j + 1) * quarter] = jnp.where(spot == across, 1.0, 0.0).astype(BF16)

    def make_unpack(h):
        for j in range(2):
            for start in range(0, window, ch):
                size = min(ch, window - start)
                spot = start + j * (packed - window) + lax.broadcasted_iota(jnp.int32, (quarter, size), 1)
                unpack[h, j, :, start:start + size] = jnp.where(
                    places[h, j, :, :size] == spot.astype(F32), 1.0, 0.0).astype(BF16)

    for side in range(2):
        edge_copy(1 - side).wait_recv()
        there = jnp.where(s > 0, 1.0, 0.0) if side == 0 else jnp.where(s < s_count - 1, 1.0, 0.0)
        at = slice(cells + side * wide, cells + (side + 1) * wide)
        masked[at, :] = edge_recv[side, 0].astype(F32) * there
        mask[at, :] = edge_recv[side, 1].astype(F32) * there

    def stats_sent(slot):
        for k in range(1, s_count):
            st_copy(slot, k, s).wait_send()

    def row_sent(slot):
        for side in range(2):
            row_copy(slot, side).wait_send()

    def gathered_sent(ph):
        @pl.loop(0, n)
        def _(k):
            for sign in (1, -1):
                block = z - k * sign

                @pl.when(inside(block) & inside(z + sign))
                def _():
                    for q in range(HALVES):
                        ag_copy(ph, block, q, sign).wait_send()

    def weights_sent(which):
        for k in range(1, n):
            wz_copy(which, k).wait_send()

        @pl.loop(1, w_parts)
        def _(k):
            for slot in range(n - 1):
                wp_copy(which, slot, k, w_mine).wait_send()

    def grads_sent(ph):
        @pl.loop(0, n)
        def _(j):
            c_copy(ph, j).wait_send()
            h_copy(ph, j, core).wait_send()
            o_copy(ph, j).wait()
            for e in range(1, chips):
                peer = (chip + e) % chips

                @pl.when(peer < owners)
                def _():
                    q_copy(ph, j, e, chip, peer).wait_send()

                @pl.when(chip < owners)
                def _():
                    f_copy(ph, j, e, chip).wait_send()

    block_copy = pltpu.make_async_copy(flat_block, out_block, r_sem.at[0])

    pack_field(0, masked, first=make_pack)
    for h in range(HALVES):
        make_unpack(h)
    forward(0, masked)
    send_stats(0, local_moments())
    send_row(0, 1)
    weights_round(1)
    mean1, scale1, count = moments(0)

    def activate_one(start, size, carry):
        at = pl.ds(start, size)
        main = start is not cells
        nv = ((acc if main else normed1)[at, :] - mean1) * scale1
        normed1[at, :] = nv
        hid[at, :] = gelu_parts(nv * gain1 + shift1)[0] * mask[at, :]
        if main:
            acc[at, :] = jnp.zeros((size, ch), F32)
        return carry

    def slope_one(start, size, carry):
        at = pl.ds(start, size)
        slope1[at, :] = gelu_parts(normed1[at, :] * gain1 + shift1)[1] * mask[at, :]
        return carry

    take_rows(0, normed1)
    pack_field(1, hid, activate_one)
    everywhere(slope_one)
    forward(1, hid)
    send_stats(1, local_moments())
    send_row(1, 1)
    turn_field(0, masked)
    turn_field(1, hid)
    weights_sent(0)
    gathered_sent(0)
    stats_sent(0)
    row_sent(0)
    for side in range(2):
        edge_copy(side).wait_send()
        cot_copy(side).wait_send()
    mean2, scale2, _ = moments(1)

    def activate_two(source, start, size):
        at = pl.ds(start, size)
        nv = (source[at, :] - mean2) * scale2
        normed2[at, :] = nv
        value, slope = gelu_parts(nv * gain2 + shift2 + masked[at, :])
        t = cotm[at, :] * slope
        through[at, :] = t
        return value, nv, t

    def activate_main(start, size, carry):
        value, nv, t = activate_two(acc, start, size)
        at = pl.ds(start, size)
        hid2[at, :] = value * mask[at, :]
        acc[at, :] = jnp.zeros((size, ch), F32)
        return carry[0] + fold(t * nv), carry[1] + fold(t)

    send_stats(2, [flatten(v) for v in chunked(activate_main, (zero, zero))])
    take_rows(1, normed2)
    take_cotangent()
    activate_two(normed2, cells, edge)
    to_flat(hid2, flat_block)
    block_copy.start()
    weights_sent(1)
    gathered_sent(1)

    def gradient_sums(slot):
        take_stats(slot)
        return flatten(st_recv[slot, :, 0, :]), flatten(st_recv[slot, :, 1, :])

    def norm_back(upstream, normed, gain, scale, sums):
        gain_grad, shift_grad = sums
        factor = gain * scale
        level, tilt = shift_grad / count, gain_grad / count

        def fill(start, size, carry):
            at = pl.ds(start, size)
            v = upstream[at, :] - mask[at, :] * (level + normed[at, :] * tilt)
            hid[at, :] = factor * v
            return carry
        return fill

    sums2 = gradient_sums(2)
    pack_field(3, hid, norm_back(through, normed2, gain2, scale2, sums2))
    backward(1)

    parts = inner_sums(settled, cells, 1)
    send_stats(3, [flatten(early[8 * i:8 * i + 8, :] + v) for i, v in enumerate(parts)])
    row_copy(2, 1).start()

    @pl.when(jnp.logical_not(passing))
    def _():
        of_step(n - 1, functools.partial(make_grad, 1))
    for side in range(2):
        row_copy(2, 1 - side).wait_recv()
        at = slice(cells + side * wide, cells + (side + 1) * wide)
        slope1[at, :] = row_recv[2, side] * slope1[at, :]
    stats_sent(1)
    row_sent(1)
    stats_sent(2)
    gathered_sent(3)
    sums1 = gradient_sums(3)
    pack_field(2, hid, norm_back(slope1, normed1, gain1, scale1, sums1))
    advance_all(1, 1)
    backward(0)
    advance(0, n)

    def finish_input(start, size, carry):
        at = pl.ds(start, size)
        acc[at, :] = (acc[at, :] + through[at, :]) * mask[at, :]
        return carry

    chunked(finish_input, 0)
    to_flat(acc, flat_input)
    input_copy = pltpu.make_async_copy(flat_input, out_input, r_sem.at[1])
    input_copy.start()
    out_gain1[...], out_shift1[...] = sums1
    out_gain2[...], out_shift2[...] = sums2
    for extra in range(1, len(stages) - 1):
        advance(0, n + extra)

    stats_sent(3)
    row_sent(2)
    gathered_sent(2)
    grads_sent(1)
    grads_sent(0)
    block_copy.wait()
    input_copy.wait()


def finish_kernel(count, *refs):
    ins, outs = refs[:count], refs[count:2 * count]
    narrow, wide, in_sem, out_sem, take_sem, give_sem = refs[2 * count:2 * count + 6]
    held = refs[2 * count + 6:]
    rows = narrow.shape[1] // FINISH_PARTS
    parts = [(w, i, pl.ds(i * rows, rows)) for i in range(FINISH_PARTS) for w in range(2)]
    loads = [pltpu.make_async_copy(ins[w].at[at, :], narrow.at[w, at, :], in_sem.at[w, i]) for w, i, at in parts]
    stores = [pltpu.make_async_copy(wide.at[w, at, :], outs[w].at[at, :], out_sem.at[w, i]) for w, i, at in parts]
    takes = [pltpu.make_async_copy(ins[2 + k], v, take_sem.at[k]) for k, v in enumerate(held)]
    gives = [pltpu.make_async_copy(v, outs[2 + k], give_sem.at[k]) for k, v in enumerate(held)]
    for copy in loads + takes:
        copy.start()
    for load, store, (w, i, at) in zip(loads, stores, parts):
        load.wait()
        wide[w, at, :] = narrow[w, at, :].astype(F32)
        store.start()
    for take, give in zip(takes, gives):
        take.wait()
        give.start()
    for copy in stores + gives:
        copy.wait()


def per_device(n, s_count, blocks, weight_one, weight_two, gain_one, shift_one, gain_two, shift_two, cell_live, cotangent):
    rows, wide = cell_live.shape
    ch = blocks.shape[1] // wide
    cells = rows * wide
    total = cells + 2 * wide
    packed = 2 * -(-most_live(rows // HALVES // 2, wide) // 8) * 8
    aligned = ch % 128 == 0
    chips = s_count // 2
    tap_rows = 9 * ch
    half_rows = tap_rows // 2
    owners = math.gcd(half_rows // 16, chips)
    piece = half_rows // owners

    if aligned:
        weight_one, weight_two = (w.reshape(tap_rows, n * ch) for w in (weight_one, weight_two))
    else:
        weight_one, weight_two = (
            w.reshape(tap_rows, n, ch).transpose(1, 0, 2) for w in (weight_one, weight_two))
    grad_shape = (2, owners, piece, n * ch) if aligned else (n, 2, owners, piece, ch)
    vmem = pl.BlockSpec(memory_space=pltpu.VMEM)
    hbm = pl.BlockSpec(memory_space=pl.ANY)
    sem = pltpu.SemaphoreType.DMA
    field = pltpu.VMEM((total, ch), F32)
    scratch = [
        pltpu.VMEM((ch * wide, 128), F32),
        pltpu.VMEM((2, n, tap_rows, ch), BF16),
        pltpu.VMEM((2, n - 1, tap_rows, ch), BF16),
        pltpu.VMEM((2, 3 * ch, cells), BF16),
        pltpu.VMEM((HALVES, packed, cells // HALVES), BF16),
        pltpu.VMEM((HALVES, 2, cells // HALVES // 2, -(-packed // 2 // 16) * 16), BF16),
        pltpu.VMEM((HALVES, 2, cells // HALVES // 2, ch), F32),
        pltpu.VMEM((2, 2, wide, ch), BF16),
        pltpu.VMEM((2, 2, wide, ch), BF16),
        pltpu.VMEM((2, wide, ch), BF16),
        pltpu.VMEM((2, wide, ch), BF16),
        field, field, field, field, field, field, field, field, field,
        pltpu.VMEM((total + 16, ch), F32),
        pltpu.VMEM((cells, ch), F32),
        pltpu.VMEM((4, n, 2 * wide + HALVES * packed, ch), BF16),
        pltpu.VMEM((n, rows + 3, wide, 3 * ch), BF16),
        pltpu.VMEM((2, n, 2, owners, piece, ch), F32),
        pltpu.VMEM((2, n, owners, piece, ch), BF16),
        pltpu.VMEM((2, n, owners, piece, ch), BF16),
        pltpu.VMEM((2, n, owners, piece, ch), BF16),
        pltpu.VMEM((2, n, chips, piece, ch), BF16),
        pltpu.VMEM((2, n, 2, owners, piece, ch), BF16),
        pltpu.VMEM((4, 8, ch), F32),
        pltpu.VMEM((4, s_count, 8, ch), F32),
        pltpu.VMEM((3, 2, wide, ch), F32),
        pltpu.VMEM((3, 2, wide, ch), F32),
        pltpu.VMEM((16, ch), F32),
        pltpu.VMEM((rows, ch * wide), BF16),
        pltpu.VMEM((rows, ch * wide), F32),
        sem((2, n)),
        sem((2, n)), sem((2, n)),
        sem((2, n - 1, s_count)), sem((2, n - 1, s_count)),
        sem((2,)), sem((2,)),
        sem((2,)), sem((2,)),
        sem((4, 2, n, HALVES)), sem((4, n, HALVES)),
        sem((4, s_count)), sem((4, s_count)),
        sem((3, 2)), sem((3, 2)),
        sem((2, n)), sem((2, n)),
        sem((2, n, chips)), sem((2, n, chips)),
        sem((2, n, chips)), sem((2, n, chips)),
        sem((2, n)), sem((2, n)),
        sem((2, n)),
        sem((2,)),
    ]
    block_out, input_grad, wg1, wg2, *sums = pl.pallas_call(
        functools.partial(block_kernel, n, s_count, rows, wide, ch, aligned, packed),
        out_shape=(
            jax.ShapeDtypeStruct((rows, ch * wide), BF16),
            jax.ShapeDtypeStruct((rows, ch * wide), F32),
            jax.ShapeDtypeStruct(grad_shape, BF16),
            jax.ShapeDtypeStruct(grad_shape, BF16),
            *[jax.ShapeDtypeStruct((1, ch), F32)] * 4,
        ),
        in_specs=[vmem] * 7 + [hbm] * 2,
        out_specs=(hbm, hbm, hbm, hbm, vmem, vmem, vmem, vmem),
        scratch_shapes=scratch,
        compiler_params=pltpu.CompilerParams(
            collective_id=0, has_side_effects=True, vmem_limit_bytes=60 * 1024 * 1024),
    )(blocks, cotangent, cell_live.T,
      *(v.reshape(1, ch) for v in (gain_one, shift_one, gain_two, shift_two)), weight_one, weight_two)

    if not aligned:
        def whole(grad):
            grad = grad.reshape(n, tap_rows, ch).transpose(1, 0, 2)
            return grad.astype(F32).reshape(9, ch, n * ch)
        return (block_out, input_grad, whole(wg1), whole(wg2), *(v.reshape(ch) for v in sums))

    wg1, wg2 = (w.reshape(tap_rows, n * ch) for w in (wg1, wg2))
    wide_grad = jax.ShapeDtypeStruct((tap_rows, n * ch), F32)
    moved = (block_out, input_grad, *sums)
    grad1, grad2, *moved = pl.pallas_call(
        functools.partial(finish_kernel, 2 + len(moved)),
        out_shape=(wide_grad, wide_grad, *(jax.ShapeDtypeStruct(v.shape, v.dtype) for v in moved)),
        in_specs=[pl.BlockSpec(memory_space=pl.ANY)] * (2 + len(moved)),
        out_specs=[pl.BlockSpec(memory_space=pl.ANY)] * (2 + len(moved)),
        scratch_shapes=[
            pltpu.VMEM((2, tap_rows, n * ch), BF16), pltpu.VMEM((2, tap_rows, n * ch), F32),
            sem((2, FINISH_PARTS)), sem((2, FINISH_PARTS)), sem((len(moved),)), sem((len(moved),)),
            *(pltpu.VMEM(v.shape, v.dtype) for v in moved),
        ],
        compiler_params=pltpu.CompilerParams(vmem_limit_bytes=64 * 1024 * 1024),
    )(wg1, wg2, *moved)
    block_out, input_grad, *sums = moved
    grads = (g.reshape(9, ch, n * ch) for g in (grad1, grad2))
    return (block_out, input_grad, *grads, *(v.reshape(ch) for v in sums))


def solution(mesh):
    return jax.shard_map(
        functools.partial(per_device, mesh.shape["chan"], mesh.shape["space"]),
        mesh=mesh,
        in_specs=(
            P("space", "chan"),
            P(None, "chan", None),
            P(None, "chan", None),
            P("chan"),
            P("chan"),
            P("chan"),
            P("chan"),
            P("space", None),
            P("space", "chan"),
        ),
        out_specs=(
            P("space", "chan"),
            P("space", "chan"),
            P(None, "chan", None),
            P(None, "chan", None),
            P("chan"),
            P("chan"),
            P("chan"),
            P("chan"),
        ),
        check_vma=False,
    )
```
